32 devices in a mesh: pb: 4 (over z), pa: 8 (over y, x, core).
Axes of the slice: x: 2, y: 2, z: 4, core: 2. Of those that a mesh axis runs over, the one named last changes fastest.
Arguments:
- passages: bfloat16 [4, 8, 512, 768], P('pb', 'pa'), may hold values from -6 to 6
- lengths: int32 [4, 8], P('pb', 'pa'), may hold values from 250 to 500, as said below
- answers: bfloat16 [4, 20, 768], P('pb'), may hold values from -6 to 6
- cotangent: bfloat16 [4, 20, 768], P('pb'), may hold values from -6 to 6
- enc_gain1: float32 [768], replicated, may hold values from 0.1 to 1.9
- enc_qkv: bfloat16 [768, 2304], replicated, may hold values from -0.21875 to 0.21875
- enc_bias: float32 [32, 12], replicated, may hold values from -4 to 4
- enc_out: bfloat16 [768, 768], replicated, may hold values from -1.75 to 1.75
- enc_gain2: float32 [768], replicated, may hold values from 0.1 to 1.9
- enc_ffn_in: bfloat16 [768, 3072], replicated, may hold values from -0.21875 to 0.21875
- enc_ffn_out: bfloat16 [3072, 768], replicated, may hold values from -0.109375 to 0.109375
- enc_gain3: float32 [768], replicated, may hold values from 0.1 to 1.9
- cross_kv: bfloat16 [768, 1536], replicated, may hold values from -0.21875 to 0.21875
- dec_gain1: float32 [768], replicated, may hold values from 0.1 to 1.9
- dec_qkv: bfloat16 [768, 2304], replicated, may hold values from -0.21875 to 0.21875
- dec_bias: float32 [32, 12], replicated, may hold values from -4 to 4
- dec_out: bfloat16 [768, 768], replicated, may hold values from -0.4375 to 0.4375
- dec_gain2: float32 [768], replicated, may hold values from 0.1 to 1.9
- cross_query: bfloat16 [768, 768], replicated, may hold values from -0.21875 to 0.21875
- cross_out: bfloat16 [768, 768], replicated, may hold values from -3.5 to 3.5
- dec_gain3: float32 [768], replicated, may hold values from 0.1 to 1.9
- dec_ffn_in: bfloat16 [768, 3072], replicated, may hold values from -0.21875 to 0.21875
- dec_ffn_out: bfloat16 [3072, 768], replicated, may hold values from -0.109375 to 0.109375
Outputs:
- answer_out: bfloat16 [4, 20, 768], P('pb')
- grad_passages: float32 [4, 8, 512, 768], P('pb', 'pa')
- grad_answers: float32 [4, 20, 768], P('pb')
- grad_enc_gain1: float32 [768], P('pa')
- grad_enc_qkv: float32 [768, 2304], P('pa')
- grad_enc_bias: float32 [32, 12], replicated
- grad_enc_out: float32 [768, 768], P('pa')
- grad_enc_gain2: float32 [768], P('pa')
- grad_enc_ffn_in: float32 [768, 3072], P('pa')
- grad_enc_ffn_out: float32 [3072, 768], P('pa')
- grad_enc_gain3: float32 [768], P('pa')
- grad_cross_kv: float32 [768, 1536], P('pa')
- grad_dec_gain1: float32 [768], P('pb')
- grad_dec_qkv: float32 [768, 2304], P('pb')
- grad_dec_bias: float32 [32, 12], P('pb')
- grad_dec_out: float32 [768, 768], P('pb')
- grad_dec_gain2: float32 [768], P('pb')
- grad_cross_query: float32 [768, 768], P('pb')
- grad_cross_out: float32 [768, 768], P('pb')
- grad_dec_gain3: float32 [768], P('pb')
- grad_dec_ffn_in: float32 [768, 3072], P('pb')
- grad_dec_ffn_out: float32 [3072, 768], P('pb')
The draws below stay inside these ranges and needn't reach their ends.
Inputs may be any that keep to these rules, and one draw needn't show every extreme that they name: Every passage holds 250 or 500 tokens at the start of its slot; every question has passages of both lengths.
All inputs are finite; a program needn't handle non-finite values.
Results may differ from the reference program's by a relative error of at most 0.02.
Values may be sent and summed in bfloat16 or wider, within the bound.
No kernel may reach another device: no remote copies, remote signals or barrier semaphores. Data moves between devices by JAX's collectives and lax.ppermute only.
A program may use at most 256 MiB of HBM per device.

```python
import jax
import jax.numpy as jnp
from jax import lax

D = 768
H = 12
HD = 64
FF = 3072
BUCKETS = 32
ANS = 20
SLOT = 512
LONG = 500
QUESTIONS = 4
PASSAGES = 8


def draw_lengths(key, part):
    key = jax.random.fold_in(key, 3)
    first_key, second_key = jax.random.split(key)
    picks = jax.random.randint(first_key, (QUESTIONS, PASSAGES), 0, 2)
    leader = jax.random.randint(second_key, (QUESTIONS, 1), 0, PASSAGES)
    column = jnp.arange(PASSAGES, dtype=jnp.int32)[None, :]
    picks = jnp.where(column == leader, 1, jnp.where(column == (leader + 1) % PASSAGES, 0, picks))
    return jnp.where(picks == 1, LONG, LONG // 2).astype(jnp.int32)


def steps_of(own_key, shape, shards, low, high):
    def one(position, parts):
        heights = jax.random.uniform(jax.random.fold_in(jax.random.fold_in(own_key, 6), position), (parts,), jnp.float32, low / len(shards), high / len(shards))
        return jnp.repeat(jnp.exp(heights), shape[position] // parts).reshape((-1,) + (1,) * (len(shape) - position - 1))

    loudness = one(*shards[0])
    for cut in shards[1:]:
        loudness = loudness * one(*cut)
    return loudness


def noise(own_key, shape, scale, bound, cuts=(), kind=jnp.bfloat16):
    values = jax.random.normal(own_key, shape, jnp.float32) * scale
    if len(cuts) > 0:
        values = steps_of(own_key, shape, cuts, -0.22, 0.18) * values
    return jnp.clip(values, min=-bound, max=bound).astype(kind)


def setup_inputs(seed: int = 0) -> dict:
    key_of = jax.random.split(jax.random.key(seed), 24)
    passages = noise(key_of[0], (QUESTIONS, PASSAGES, SLOT, D), 1.0, 6.0, ((0, 4), (1, 8)))
    lengths = draw_lengths(jax.random.fold_in(key_of[23], 71), 0)
    answers = noise(key_of[2], (QUESTIONS, ANS, D), 1.0, 6.0, ((0, 4),))
    cotangent = noise(key_of[3], (QUESTIONS, ANS, D), 1.0, 6.0, ((0, 4),))
    enc_gain1 = jnp.clip(1.0 + 0.18 * jax.random.normal(key_of[4], (D,), jnp.float32), 0.1, 1.9)
    enc_qkv = noise(key_of[5], (D, 3 * D), D ** -0.5, 0.21875)
    enc_bias = noise(key_of[6], (BUCKETS, H), 1.0, 4.0, (), jnp.float32)
    enc_out = noise(key_of[7], (D, D), (max(D // 64, 1)) ** -0.5, 1.75)
    enc_gain2 = jnp.clip(1.0 + 0.18 * jax.random.normal(key_of[8], (D,), jnp.float32), 0.1, 1.9)
    enc_ffn_in = noise(key_of[9], (D, FF), D ** -0.5, 0.21875)
    enc_ffn_out = noise(key_of[10], (FF, D), FF ** -0.5, 0.109375)
    enc_gain3 = jnp.clip(1.0 + 0.18 * jax.random.normal(key_of[11], (D,), jnp.float32), 0.1, 1.9)
    cross_kv = noise(key_of[12], (D, 2 * D), D ** -0.5, 0.21875)
    dec_gain1 = jnp.clip(1.0 + 0.18 * jax.random.normal(key_of[13], (D,), jnp.float32), 0.1, 1.9)
    dec_qkv = noise(key_of[14], (D, 3 * D), D ** -0.5, 0.21875)
    dec_bias = noise(key_of[15], (BUCKETS, H), 1.0, 4.0, (), jnp.float32)
    dec_out = noise(key_of[16], (D, D), (max(D // 4, 1)) ** -0.5, 0.4375)
    dec_gain2 = jnp.clip(1.0 + 0.18 * jax.random.normal(key_of[17], (D,), jnp.float32), 0.1, 1.9)
    cross_query = noise(key_of[18], (D, D), D ** -0.5, 0.21875)
    cross_out = noise(key_of[19], (D, D), (max(D // 256, 1)) ** -0.5, 3.5)
    dec_gain3 = jnp.clip(1.0 + 0.18 * jax.random.normal(key_of[20], (D,), jnp.float32), 0.1, 1.9)
    dec_ffn_in = noise(key_of[21], (D, FF), D ** -0.5, 0.21875)
    dec_ffn_out = noise(key_of[22], (FF, D), FF ** -0.5, 0.109375)
    return {"passages": passages, "lengths": lengths, "answers": answers, "cotangent": cotangent, "enc_gain1": enc_gain1, "enc_qkv": enc_qkv, "enc_bias": enc_bias, "enc_out": enc_out, "enc_gain2": enc_gain2, "enc_ffn_in": enc_ffn_in, "enc_ffn_out": enc_ffn_out, "enc_gain3": enc_gain3, "cross_kv": cross_kv, "dec_gain1": dec_gain1, "dec_qkv": dec_qkv, "dec_bias": dec_bias, "dec_out": dec_out, "dec_gain2": dec_gain2, "cross_query": cross_query, "cross_out": cross_out, "dec_gain3": dec_gain3, "dec_ffn_in": dec_ffn_in, "dec_ffn_out": dec_ffn_out}


@jax.custom_vjp
def low(v):
    return lax.optimization_barrier(v.astype(jnp.bfloat16)).astype(jnp.float32)

@jax.custom_vjp
def low_back(v):
    return v

def low_keep(v):
    return (low(v), None)

def low_pass(kept, grad):
    return (grad,)

def back_keep(v):
    return (v, None)

def back_low(kept, grad):
    return (low(grad),)
low.defvjp(low_keep, low_pass)
low_back.defvjp(back_keep, back_low)
HIGH = lax.Precision.HIGHEST
EPS = 1e-06

def norm_rows(values, gain):
    return values * lax.rsqrt(lax.optimization_barrier(jnp.mean(values * values, axis=-1, keepdims=True)) + EPS) * gain

def matmul(left, right):
    return jnp.dot(left, right, precision=HIGH)

def attend(query, keys, values, bias, allowed):
    scores = jnp.einsum('qhd,khd->hqk', query, keys, precision=HIGH) * 0.125 + bias
    scores = low_back(jnp.where(allowed, scores, -1000000000.0))
    probs = low(jax.nn.softmax(scores, axis=-1))
    mixed = jnp.einsum('hqk,khd->qhd', probs, values, precision=HIGH)
    return low(low_back(mixed.reshape(mixed.shape[0], H * HD)))

def encode(rows, length, weights):
    gain_one, qkv_w, table, out_w, gain_two, ffn_in, ffn_out, gain_three, pair_w = weights
    places = jnp.arange(SLOT, dtype=jnp.int32)
    allowed = (places < length)[None, None, :]
    spots = jnp.clip(places[None, :] - places[:, None], -(BUCKETS // 2), BUCKETS // 2 - 1) + BUCKETS // 2
    bias = jnp.transpose(table[spots], (2, 0, 1))
    heads = low(low_back(matmul(low(norm_rows(rows, gain_one)), qkv_w))).reshape(SLOT, 3, H, HD)
    after = rows + low_back(matmul(attend(heads[:, 0], heads[:, 1], heads[:, 2], bias, allowed), out_w))
    hidden = low(jax.nn.gelu(low_back(matmul(low(norm_rows(after, gain_two)), ffn_in))))
    final = after + low_back(matmul(hidden, ffn_out))
    return low(low_back(matmul(low(norm_rows(final, gain_three)), pair_w)))

def decode(start, keys, values, allowed, weights):
    gain_one, qkv_w, table, self_w, gain_two, query_w, cross_w, gain_three, ffn_in, ffn_out = weights
    turns = jnp.arange(ANS, dtype=jnp.int32)
    back = turns[:, None] - turns[None, :]
    causal = (back >= 0)[None]
    bias = jnp.transpose(table[jnp.clip(back, 0, BUCKETS - 1)], (2, 0, 1))
    heads = low(low_back(matmul(low(norm_rows(start, gain_one)), qkv_w))).reshape(ANS, 3, H, HD)
    after = start + low_back(matmul(attend(heads[:, 0], heads[:, 1], heads[:, 2], bias, causal), self_w))
    query = low(low_back(matmul(low(norm_rows(after, gain_two)), query_w))).reshape(ANS, H, HD)
    middle = after + low_back(matmul(attend(query, keys, values, 0.0, allowed), cross_w))
    hidden = low(jax.nn.gelu(low_back(matmul(low(norm_rows(middle, gain_three)), ffn_in))))
    return middle + low_back(matmul(hidden, ffn_out))

def reference(passages, lengths, answers, cotangent, enc_gain1, enc_qkv, enc_bias, enc_out, enc_gain2, enc_ffn_in, enc_ffn_out, enc_gain3, cross_kv, dec_gain1, dec_qkv, dec_bias, dec_out, dec_gain2, cross_query, cross_out, dec_gain3, dec_ffn_in, dec_ffn_out):
    inputs = (passages, answers, enc_gain1, enc_qkv, enc_bias, enc_out, enc_gain2, enc_ffn_in, enc_ffn_out, enc_gain3, cross_kv, dec_gain1, dec_qkv, dec_bias, dec_out, dec_gain2, cross_query, cross_out, dec_gain3, dec_ffn_in, dec_ffn_out)
    floats = [item.astype(jnp.float32) for item in inputs]
    flat_lengths = lengths.reshape(QUESTIONS * PASSAGES).astype(jnp.int32)
    places = jnp.arange(SLOT, dtype=jnp.int32)
    allowed = (places[None, None, :] < lengths[:, :, None]).reshape(QUESTIONS, 1, 1, PASSAGES * SLOT)

    def forward(all_passages, all_answers, *weights):
        enc_weights = weights[:9]
        dec_weights = weights[9:]
        items = all_passages.reshape(QUESTIONS * PASSAGES, SLOT, D)

        def one_passage(item):
            return encode(item[0], item[1], enc_weights)
        pairs = lax.map(jax.checkpoint(one_passage), (items, flat_lengths))
        pairs = pairs.reshape(QUESTIONS, PASSAGES * SLOT, 2, H, HD)

        def one_question(start, question_pairs, mask):
            return decode(start, question_pairs[:, 0], question_pairs[:, 1], mask, dec_weights)
        return jax.vmap(one_question)(all_answers, pairs, allowed)
    result, pull = jax.vjp(forward, *floats)
    grads = pull(cotangent.astype(jnp.float32))
    return (result.astype(jnp.bfloat16), grads[0], grads[1], grads[2], grads[3], grads[4], grads[5], grads[6], grads[7], grads[8], grads[9], grads[10], grads[11], grads[12], grads[13], grads[14], grads[15], grads[16], grads[17], grads[18], grads[19], grads[20])
```

```python
import jax
import jax.numpy as jnp
import numpy as np
from jax import lax
from jax.experimental import pallas as pl
from jax.experimental.pallas import tpu as pltpu
from jax.sharding import PartitionSpec as P

D = 768
H = 12
HD = 64
FF = 3072
BUCKETS = 32
ANS = 20
SLOT = 512
PAIR = 2 * HD
PAIRS = H // 2
EDGE = 128
STRIP = 256
SPAN = 256
EPS = 1e-06
MASKED = -1000000000.0
LOWER = jnp.bfloat16
WIDER = jnp.float32
HIGH = lax.Precision.HIGHEST


def tile_classes(away):
    rows = [np.clip(EDGE * d - away, -(BUCKETS // 2), BUCKETS // 2 - 1) + BUCKETS // 2 for d in (-1, 0, 1)]
    return np.eye(BUCKETS, dtype=np.float32)[np.concatenate(rows)]


LANES = np.arange(SPAN)
PICK = tile_classes(np.where(LANES < EDGE, LANES, LANES - SPAN))
PICK_BACK = tile_classes(LANES - (EDGE - 1))


def norm_rows(values, gain):
    return values * lax.rsqrt(jnp.mean(values * values, axis=-1, keepdims=True) + EPS) * gain


def norm_back(values, gain, grad):
    unused, pull = jax.vjp(norm_rows, values, gain)
    return pull(grad)


def gelu_back(inner, grad):
    unused, pull = jax.vjp(jax.nn.gelu, inner)
    return pull(grad)[0]


def product(left, right):
    return jnp.dot(left, right, preferred_element_type=WIDER)


def left_product(left, right):
    return lax.dot_general(left, right, (((0,), (0,)), ((), ())), preferred_element_type=WIDER)


def right_product(left, right):
    return lax.dot_general(left, right, (((1,), (1,)), ((), ())), preferred_element_type=WIDER)


def scores_of(query, keys, bias, allowed):
    raw = jnp.einsum("bqhd,bkhd->bhqk", query, keys, preferred_element_type=WIDER) * 0.125 + bias
    return jnp.where(allowed, raw, MASKED)


def attend_local(query, keys, values, bias, allowed):
    probs = jax.nn.softmax(scores_of(query, keys, bias, allowed), axis=-1)
    return jnp.einsum("bhqk,bkhd->bqhd", probs.astype(LOWER), values, preferred_element_type=WIDER)


def attend_back(query, keys, values, bias, allowed, grad_mixed):
    probs = jax.nn.softmax(scores_of(query, keys, bias, allowed), axis=-1)
    grad_probs = jnp.einsum("bqhd,bkhd->bhqk", grad_mixed, values, preferred_element_type=WIDER)
    grad_scores = probs * (grad_probs - jnp.sum(grad_probs * probs, axis=-1, keepdims=True))
    rounded = grad_scores.astype(LOWER)
    grad_query = jnp.einsum("bhqk,bkhd->bqhd", rounded, keys, preferred_element_type=WIDER) * 0.125
    grad_keys = jnp.einsum("bhqk,bqhd->bkhd", rounded, query, preferred_element_type=WIDER) * 0.125
    grad_values = jnp.einsum(
        "bhqk,bqhd->bkhd", probs.astype(LOWER), grad_mixed, preferred_element_type=WIDER
    )
    return (grad_query, grad_keys, grad_values, rounded)


def bias_tiles(u_ref, h):
    tiles = []
    for d in range(3):
        row = u_ref[0, h, d : d + 1, :]
        wide = jnp.broadcast_to(row, (EDGE, SPAN))
        tiles.append(pltpu.roll(wide, 0, 1, stride=1, stride_axis=0)[:, :EDGE])
    return tiles


def bias_strip(tiles, low, high, first):
    columns = []
    for i in range(first, first + STRIP // EDGE):
        blocks = []
        for j in range(SLOT // EDGE):
            d = j - i
            if abs(d) <= 1:
                blocks.append(tiles[d + 1])
            else:
                blocks.append(jnp.full((EDGE, EDGE), low if d < 0 else high, WIDER))
        columns.append(jnp.concatenate(blocks, axis=0))
    return jnp.concatenate(columns, axis=1)


def strip_scores(n, keys, query, bias):
    raw = right_product(keys, query) + bias
    places = lax.broadcasted_iota(jnp.int32, (SLOT, STRIP), 0)
    return jnp.where(places < n, raw, MASKED)


def attn_fwd_kernel(n_ref, edge_ref, u_ref, q_ref, k_ref, v_ref, o_ref, st_ref):
    n = n_ref[0]
    step = pl.program_id(0)
    values = jnp.transpose(v_ref[...])
    mixed = []
    for h in range(2):
        low, high = edge_ref[2 * step + h, 0], edge_ref[2 * step + h, 1]
        tiles = bias_tiles(u_ref, h)
        cols = slice(HD * h, HD * h + HD)
        keys = k_ref[:, cols]
        strips = []
        for i in range(0, SLOT // EDGE, STRIP // EDGE):
            lanes = slice(EDGE * i, EDGE * i + STRIP)
            query = q_ref[lanes, cols] * 0.125
            scores = strip_scores(n, keys, query, bias_strip(tiles, low, high, i))
            top = jnp.max(scores, axis=0, keepdims=True)
            powers = jnp.exp(scores - top)
            share = 1.0 / jnp.sum(powers, axis=0, keepdims=True)
            st_ref[0, 2 * h : 2 * h + 1, lanes] = top
            st_ref[0, 2 * h + 1 : 2 * h + 2, lanes] = share
            probs = (powers * share).astype(LOWER)
            strips.append(product(values[cols], probs))
        mixed.append(jnp.concatenate(strips, axis=1))
    o_ref[...] = jnp.transpose(jnp.concatenate(mixed, axis=0)).astype(LOWER)


def attn_bwd_kernel(
    n_ref, edge_ref, u_ref, q_ref, k_ref, v_ref, g_ref, st_ref, gq_ref, gk_ref, gv_ref, gb_ref
):
    n = n_ref[0]
    step = pl.program_id(0)
    keys_t = jnp.transpose(k_ref[...])
    rows = lax.broadcasted_iota(jnp.int32, (EDGE, EDGE), 0)
    columns = lax.broadcasted_iota(jnp.int32, (EDGE, EDGE), 1)
    mirror = jnp.where(rows + columns == EDGE - 1, 1.0, 0.0).astype(LOWER)
    grad_queries = []
    for h in range(2):
        low, high = edge_ref[2 * step + h, 0], edge_ref[2 * step + h, 1]
        tiles = bias_tiles(u_ref, h)
        cols = slice(HD * h, HD * h + HD)
        keys = k_ref[:, cols]
        values = v_ref[:, cols]
        grad_keys = jnp.zeros((SLOT, HD), WIDER)
        grad_values = jnp.zeros((SLOT, HD), WIDER)
        strips = []
        sums = {}
        for i in range(0, SLOT // EDGE, STRIP // EDGE):
            lanes = slice(EDGE * i, EDGE * i + STRIP)
            query = q_ref[lanes, cols]
            grad = g_ref[lanes, cols]
            scores = strip_scores(n, keys, query * 0.125, bias_strip(tiles, low, high, i))
            top = st_ref[0, 2 * h : 2 * h + 1, lanes]
            share = st_ref[0, 2 * h + 1 : 2 * h + 2, lanes]
            probs = jnp.exp(scores - top) * share
            grad_probs = right_product(values, grad)
            weighted = jnp.sum(probs * grad_probs, axis=0, keepdims=True)
            rounded = (probs * (grad_probs - weighted)).astype(LOWER)
            strips.append(product(keys_t[cols], rounded))
            grad_keys += product(rounded, query)
            grad_values += product(probs.astype(LOWER), grad)
            wide = rounded.astype(WIDER)
            for c in range(STRIP // EDGE):
                for j in range(SLOT // EDGE):
                    d = min(max(j - i - c, -2), 2)
                    block = wide[EDGE * j : EDGE * j + EDGE, EDGE * c : EDGE * c + EDGE]
                    sums[d] = sums[d] + block if d in sums else block
        grad_queries.append(jnp.concatenate(strips, axis=1))
        gk_ref[:, cols] = (grad_keys * 0.125).astype(LOWER)
        gv_ref[:, cols] = grad_values.astype(LOWER)
        empty = jnp.zeros((EDGE, SPAN - EDGE), WIDER)
        band = jnp.concatenate([sums[-1], sums[0], sums[1]], axis=1)
        upper = band.astype(LOWER)
        lower = (band - upper.astype(WIDER)).astype(LOWER)
        mirrored = product(mirror, upper) + product(mirror, lower)
        for d in range(3):
            wide = jnp.concatenate([mirrored[:, EDGE * d : EDGE * d + EDGE], empty], axis=1)
            turned = pltpu.roll(wide, 0, 1, stride=1, stride_axis=0)
            gb_ref[0, h, d : d + 1, :] = jnp.sum(turned, axis=0, keepdims=True)
        for row, d in ((3, -2), (4, 2)):
            wide = jnp.concatenate([sums[d], empty], axis=1)
            gb_ref[0, h, row : row + 1, :] = jnp.sum(wide, axis=0, keepdims=True)
        gb_ref[0, h, 5:8, :] = jnp.zeros((3, SPAN), WIDER)
    gq_ref[...] = (jnp.transpose(jnp.concatenate(grad_queries, axis=0)) * 0.125).astype(LOWER)


def columns_at(first):
    return pl.BlockSpec((SLOT, PAIR), lambda s: (0, first + s))


SCALARS = pl.BlockSpec(memory_space=pltpu.SMEM)
TILE_ROWS = pl.BlockSpec((1, 2, 3, SPAN), lambda s: (s, 0, 0, 0))
STATS = pl.BlockSpec((1, 4, SLOT), lambda s: (s, 0, 0))
VMEM_BYTES = 48 * 1024 * 1024


def attention(count, edges, tile_rows, heads):
    return pl.pallas_call(
        attn_fwd_kernel,
        grid=(PAIRS,),
        out_shape=(
            jax.ShapeDtypeStruct((SLOT, D), LOWER),
            jax.ShapeDtypeStruct((PAIRS, 4, SLOT), WIDER),
        ),
        in_specs=[SCALARS, SCALARS, TILE_ROWS, columns_at(0), columns_at(PAIRS), columns_at(2 * PAIRS)],
        out_specs=(columns_at(0), STATS),
        compiler_params=pltpu.CompilerParams(vmem_limit_bytes=VMEM_BYTES),
        cost_estimate=pl.CostEstimate(flops=2 * 2 * H * SLOT * SLOT * HD * 4, bytes_accessed=4 * SLOT * D * 2, transcendentals=H * SLOT * SLOT),
        name="enc_attention",
    )(count, edges, tile_rows, heads, heads, heads)


def attention_back(count, edges, tile_rows, heads, grad_mixed, stats):
    return pl.pallas_call(
        attn_bwd_kernel,
        grid=(PAIRS,),
        out_shape=(
            jax.ShapeDtypeStruct((SLOT, D), LOWER),
            jax.ShapeDtypeStruct((SLOT, D), LOWER),
            jax.ShapeDtypeStruct((SLOT, D), LOWER),
            jax.ShapeDtypeStruct((PAIRS, 2, 8, SPAN), WIDER),
        ),
        in_specs=[SCALARS, SCALARS, TILE_ROWS, columns_at(0), columns_at(PAIRS), columns_at(2 * PAIRS), columns_at(0), STATS],
        out_specs=(columns_at(0), columns_at(0), columns_at(0), pl.BlockSpec((1, 2, 8, SPAN), lambda s: (s, 0, 0, 0))),
        compiler_params=pltpu.CompilerParams(vmem_limit_bytes=VMEM_BYTES),
        cost_estimate=pl.CostEstimate(flops=2 * 5 * H * SLOT * SLOT * HD * 4, bytes_accessed=8 * SLOT * D * 2, transcendentals=H * SLOT * SLOT),
        name="enc_attention_back",
    )(count, edges, tile_rows, heads, heads, heads, grad_mixed, stats)


def add_low(first, second):
    return (first.astype(WIDER) + second.astype(WIDER)).astype(LOWER)


def share_over_pa(grad, turn):
    size = lax.axis_size("pa")
    bits = size.bit_length() - 1
    me = lax.axis_index("pa")
    left = list(range(bits - 1, -1, -1))
    order = [0] + [1 + (k + turn) % max(bits - 1, 1) for k in range(bits - 1)] if bits else []
    here = grad.reshape((2,) * bits + (grad.shape[0] // size, grad.shape[1]))
    for bit in order:
        axis = left.index(bit)
        mine = (me >> bit) & 1
        send = lax.dynamic_index_in_dim(here, 1 - mine, axis, keepdims=False)
        keep = lax.dynamic_index_in_dim(here, mine, axis, keepdims=False)
        got = lax.ppermute(send, "pa", [(k, k ^ (1 << bit)) for k in range(size)])
        here = add_low(keep, got)
        left.pop(axis)
    return here


def total_over_pb(share):
    size = lax.axis_size("pb")
    me = lax.axis_index("pb")
    rows = share.shape[0] // size
    parts = share.reshape(size, rows, share.shape[1])
    total = lax.dynamic_index_in_dim(parts, me, 0, keepdims=False).astype(WIDER)
    for s in range(1, size):
        send = lax.dynamic_index_in_dim(parts, (me + s) % size, 0, keepdims=False)
        total += lax.ppermute(send, "pb", [(k, (k + s) % size) for k in range(size)]).astype(WIDER)
    total = total.astype(LOWER)
    got = [total]
    for s in range(1, size):
        got.append(lax.ppermute(total, "pb", [(k, (k + s) % size) for k in range(size)]))
    blocks = [lax.select_n((me - b) % size, *got) for b in range(size)]
    return jnp.concatenate(blocks, axis=0).astype(WIDER)


def local(
    passages,
    lengths,
    answers,
    cotangent,
    enc_gain1,
    enc_qkv,
    enc_bias,
    enc_out,
    enc_gain2,
    enc_ffn_in,
    enc_ffn_out,
    enc_gain3,
    cross_kv,
    dec_gain1,
    dec_qkv,
    dec_bias,
    dec_out,
    dec_gain2,
    cross_query,
    cross_out,
    dec_gain3,
    dec_ffn_in,
    dec_ffn_out,
):
    pa_size = lax.axis_size("pa")
    pb_size = lax.axis_size("pb")
    rows = passages.reshape(SLOT, D).astype(WIDER)
    count = lengths.reshape(1)
    keep = jnp.arange(SLOT, dtype=jnp.int32) < count[0]
    tile_rows = jnp.transpose(jnp.dot(jnp.asarray(PICK), enc_bias, precision=HIGH)).reshape(PAIRS, 2, 3, SPAN)
    edges = jnp.stack([enc_bias[0], enc_bias[BUCKETS - 1]], axis=1)

    first = norm_rows(rows, enc_gain1).astype(LOWER)
    heads = product(first, enc_qkv).astype(LOWER)
    mixed, stats = attention(count, edges, tile_rows, heads)
    after = rows + product(mixed, enc_out)
    second = norm_rows(after, enc_gain2).astype(LOWER)
    inner = product(second, enc_ffn_in)
    hidden = jax.nn.gelu(inner).astype(LOWER)
    final = after + product(hidden, enc_ffn_out)
    third = norm_rows(final, enc_gain3).astype(LOWER)
    pairs = product(third, cross_kv).astype(LOWER)

    keys = pairs[:, :D].reshape(SLOT, H, HD)
    values = pairs[:, D:].reshape(SLOT, H, HD)
    turns = jnp.arange(ANS, dtype=jnp.int32)
    back = turns[:, None] - turns[None, :]
    causal = (back >= 0)[None, None]
    dec_spots = jnp.clip(back, 0, BUCKETS - 1)
    dec_match = dec_spots[:, :, None] == jnp.arange(BUCKETS, dtype=jnp.int32)
    dec_onehot = dec_match.astype(LOWER)
    dec_bias_full = jnp.einsum("qkc,ch->hqk", dec_match.astype(WIDER), dec_bias, precision=HIGH)
    start = answers[0].astype(WIDER)
    dec_first = norm_rows(start, dec_gain1).astype(LOWER)
    dec_heads = product(dec_first, dec_qkv).astype(LOWER).reshape(1, ANS, 3, H, HD)
    own = attend_local(
        dec_heads[:, :, 0], dec_heads[:, :, 1], dec_heads[:, :, 2], dec_bias_full, causal
    )
    own = own.reshape(ANS, D).astype(LOWER)
    dec_after = start + product(own, dec_out)
    dec_second = norm_rows(dec_after, dec_gain2).astype(LOWER)
    query_flat = product(dec_second, cross_query).astype(LOWER)
    query = query_flat.reshape(ANS, H, HD)

    cross_scores = jnp.einsum("qhd,khd->hqk", query, keys, preferred_element_type=WIDER) * 0.125
    cross_scores = jnp.where(keep[None, None, :], cross_scores, MASKED)
    local_top = jnp.max(cross_scores, axis=-1)
    local_powers = jnp.exp(cross_scores - local_top[..., None])
    local_total = jnp.sum(local_powers, axis=-1)
    local_probs = (local_powers / local_total[..., None]).astype(LOWER)
    local_mix = jnp.einsum("hqk,khd->qhd", local_probs, values, preferred_element_type=WIDER)
    packed = jnp.concatenate(
        [local_mix.reshape(ANS, D), jnp.transpose(local_top), jnp.transpose(local_total), jnp.zeros((ANS, 128 - 2 * H), WIDER)],
        axis=1,
    )
    gathered = lax.all_gather(packed, "pa")
    tops = gathered[:, :, D : D + H]
    totals = gathered[:, :, D + H : D + 2 * H]
    top = jnp.max(tops, axis=0)
    weights = totals * jnp.exp(tops - top)
    total = jnp.sum(weights, axis=0)
    mix_wide = jnp.sum(
        gathered[:, :, :D].reshape(pa_size, ANS, H, HD) * (weights / total)[..., None], axis=0
    )
    cross_mix = mix_wide.reshape(ANS, D).astype(LOWER)
    middle = dec_after + product(cross_mix, cross_out)
    dec_third = norm_rows(middle, dec_gain3).astype(LOWER)
    dec_inner = product(dec_third, dec_ffn_in)
    dec_hidden = jax.nn.gelu(dec_inner).astype(LOWER)
    output = middle + product(dec_hidden, dec_ffn_out)
    out_low = cotangent[0]
    grad_out = out_low.astype(WIDER)
    g_dec_inner = gelu_back(dec_inner, right_product(out_low, dec_ffn_out)).astype(LOWER)
    g_middle_part, g_dec_gain3 = norm_back(
        middle, dec_gain3, right_product(g_dec_inner, dec_ffn_in)
    )
    g_middle = grad_out + g_middle_part
    middle_low = g_middle.astype(LOWER)
    g_mix = right_product(middle_low, cross_out).astype(LOWER).reshape(ANS, H, HD)
    weighted = jnp.transpose(jnp.sum(g_mix.astype(WIDER) * mix_wide, axis=-1))
    scale = jnp.transpose(jnp.exp(jnp.transpose(local_top) - top) / total)
    probs = local_powers * scale[..., None]
    probs_low = probs.astype(LOWER)
    g_probs = jnp.einsum("qhd,khd->hqk", g_mix, values, preferred_element_type=WIDER)
    g_scores = (probs * (g_probs - weighted[..., None])).astype(LOWER)
    g_keys = (
        jnp.einsum("hqk,qhd->khd", g_scores, query, preferred_element_type=WIDER) * 0.125
    ).astype(LOWER)
    g_values = jnp.einsum("hqk,qhd->khd", probs_low, g_mix, preferred_element_type=WIDER).astype(
        LOWER
    )
    g_pairs = jnp.concatenate([g_keys.reshape(SLOT, D), g_values.reshape(SLOT, D)], axis=1)
    partial_query = jnp.einsum("hqk,khd->qhd", g_scores, keys, preferred_element_type=WIDER) * 0.125

    share_kv = share_over_pa(left_product(third, g_pairs).astype(LOWER), 0)
    g_final, g_enc_gain3 = norm_back(final, enc_gain3, right_product(g_pairs, cross_kv))
    branch = g_final.astype(LOWER)
    share_ffn_out = share_over_pa(left_product(hidden, branch).astype(LOWER), 1)
    g_inner = gelu_back(inner, right_product(branch, enc_ffn_out)).astype(LOWER)
    share_ffn_in = share_over_pa(left_product(second, g_inner).astype(LOWER), 0)
    g_after_part, g_enc_gain2 = norm_back(after, enc_gain2, right_product(g_inner, enc_ffn_in))
    g_after = g_final + g_after_part
    branch = g_after.astype(LOWER)
    share_out = share_over_pa(left_product(mixed, branch).astype(LOWER), 1)
    g_mixed = right_product(branch, enc_out).astype(LOWER)
    enc_q, enc_k, enc_v, diagonals = attention_back(count, edges, tile_rows, heads, g_mixed, stats)
    g_heads = jnp.concatenate([enc_q, enc_k, enc_v], axis=1)
    bias_rows = jnp.dot(diagonals[:, :, :3].reshape(H, 3 * SPAN), jnp.asarray(PICK_BACK), precision=HIGH)
    bias_ends = jnp.sum(diagonals[:, :, 3:5], axis=-1).reshape(H, 2)
    bias_rows = jnp.concatenate(
        [bias_rows[:, :1] + bias_ends[:, :1], bias_rows[:, 1:-1], bias_rows[:, -1:] + bias_ends[:, 1:]],
        axis=1,
    )
    g_enc_bias = jnp.transpose(bias_rows)
    g_rows_part, g_enc_gain1 = norm_back(rows, enc_gain1, right_product(g_heads, enc_qkv))
    g_rows = g_after + g_rows_part

    part = D // pa_size
    table_columns = -(-BUCKETS * H // part)
    table = jnp.pad(g_enc_bias.reshape(-1), (0, table_columns * part - BUCKETS * H))
    small = jnp.concatenate(
        [
            g_enc_gain1[:, None],
            g_enc_gain2[:, None],
            g_enc_gain3[:, None],
            jnp.tile(table.reshape(part, table_columns), (pa_size, 1)),
        ],
        axis=1,
    )
    small = jnp.pad(small, ((0, 0), (0, -small.shape[1] % 128)))
    g_enc_qkv = left_product(first, g_heads)
    share_qkv = share_over_pa(jnp.concatenate([g_enc_qkv, small], axis=1).astype(LOWER), 1)

    total_kv = total_over_pb(share_kv)
    total_ffn_out = total_over_pb(share_ffn_out)
    total_ffn_in = total_over_pb(share_ffn_in)
    total_out = total_over_pb(share_out)
    total_qkv = total_over_pb(share_qkv)
    total_table = total_qkv[:, 3 * D + 3 : 3 * D + 3 + table_columns].reshape(-1)[: BUCKETS * H]

    g_query = jnp.sum(lax.all_gather(partial_query.reshape(ANS, D), "pa"), axis=0).astype(LOWER)
    g_after_part, g_dec_gain2 = norm_back(dec_after, dec_gain2, right_product(g_query, cross_query))
    g_dec_after = g_middle + g_after_part
    after_low = g_dec_after.astype(LOWER)
    g_own = right_product(after_low, dec_out).astype(LOWER).reshape(1, ANS, H, HD)
    own_q, own_k, own_v, own_scores = attend_back(
        dec_heads[:, :, 0], dec_heads[:, :, 1], dec_heads[:, :, 2], dec_bias_full, causal, g_own
    )
    g_dec_heads = jnp.stack([own_q, own_k, own_v], axis=2).reshape(ANS, 3 * D).astype(LOWER)
    g_dec_bias = jnp.einsum("bhqk,qkc->ch", own_scores, dec_onehot, preferred_element_type=WIDER)
    g_start_part, g_dec_gain1 = norm_back(start, dec_gain1, right_product(g_dec_heads, dec_qkv))
    g_start = g_dec_after + g_start_part

    factors = [
        dec_first,
        own,
        dec_second,
        cross_mix,
        dec_third,
        dec_hidden,
        g_dec_heads,
        after_low,
        g_query,
        middle_low,
        g_dec_inner,
        out_low,
    ]
    widths = np.cumsum([0] + [f.shape[1] for f in factors])
    vector = jnp.concatenate([g_dec_gain1, g_dec_gain2, g_dec_gain3, g_dec_bias.reshape(-1)]).astype(LOWER)
    vector = jnp.pad(vector, (0, int(widths[-1]) - vector.shape[0]))[None]
    every = lax.all_gather(jnp.concatenate([jnp.concatenate(factors, axis=1), vector], axis=0), "pb")
    sums = jnp.sum(every[:, ANS].astype(WIDER), axis=0)
    every = every[:, :ANS].reshape(pb_size * ANS, int(widths[-1]))
    me = lax.axis_index("pb")

    def outer(a, b):
        left = every[:, widths[a] : widths[a + 1]]
        height = left.shape[1] // pb_size
        left = lax.dynamic_slice_in_dim(left, me * height, height, axis=1)
        return left_product(left, every[:, widths[b] : widths[b + 1]])

    def own_part(vector):
        height = vector.shape[0] // pb_size
        return lax.dynamic_slice_in_dim(vector, me * height, height, axis=0)

    return (
        output.astype(LOWER)[None],
        g_rows.reshape(1, 1, SLOT, D),
        g_start[None],
        total_qkv[:, 3 * D],
        total_qkv[:, : 3 * D],
        total_table.reshape(BUCKETS, H),
        total_out,
        total_qkv[:, 3 * D + 1],
        total_ffn_in,
        total_ffn_out,
        total_qkv[:, 3 * D + 2],
        total_kv,
        own_part(sums[:D]),
        outer(0, 6),
        own_part(sums[3 * D : 3 * D + BUCKETS * H].reshape(BUCKETS, H)),
        outer(1, 7),
        own_part(sums[D : 2 * D]),
        outer(2, 8),
        outer(3, 9),
        own_part(sums[2 * D : 3 * D]),
        outer(4, 10),
        outer(5, 11),
    )


def solution(mesh):
    copied = P()
    in_specs = (
        P("pb", "pa", None, None),
        P("pb", "pa"),
        P("pb", None, None),
        P("pb", None, None),
    ) + (copied,) * 19
    by_pa, by_pa_rows = P("pa"), P("pa", None)
    by_pb, by_pb_rows = P("pb"), P("pb", None)
    out_specs = (
        P("pb", None, None),
        P("pb", "pa", None, None),
        P("pb", None, None),
        by_pa,
        by_pa_rows,
        copied,
        by_pa_rows,
        by_pa,
        by_pa_rows,
        by_pa_rows,
        by_pa,
        by_pa_rows,
        by_pb,
        by_pb_rows,
        by_pb_rows,
        by_pb_rows,
        by_pb,
        by_pb_rows,
        by_pb_rows,
        by_pb,
        by_pb_rows,
        by_pb_rows,
    )
    return jax.shard_map(local, mesh=mesh, in_specs=in_specs, out_specs=out_specs, check_vma=False)
```

```python
import jax
import jax.numpy as jnp
import numpy as np
from jax import lax
from jax.experimental import pallas as pl
from jax.experimental.pallas import tpu as pltpu
from jax.sharding import PartitionSpec as P

D = 768
H = 12
HD = 64
FF = 3072
BUCKETS = 32
ANS = 20
SLOT = 512
PAIR = 2 * HD
PAIRS = H // 2
EDGE = 128
STRIP = 256
SPAN = 256
EPS = 1e-06
MASKED = -1000000000.0
LOWER = jnp.bfloat16
WIDER = jnp.float32
HIGH = lax.Precision.HIGHEST


def tile_classes(away):
    rows = [np.clip(EDGE * d - away, -(BUCKETS // 2), BUCKETS // 2 - 1) + BUCKETS // 2 for d in (-1, 0, 1)]
    return np.eye(BUCKETS, dtype=np.float32)[np.concatenate(rows)]


LANES = np.arange(SPAN)
PICK = tile_classes(np.where(LANES < EDGE, LANES, LANES - SPAN))
PICK_BACK = tile_classes(LANES - (EDGE - 1))


def product(left, right):
    return jnp.dot(left, right, preferred_element_type=WIDER)


def left_product(left, right):
    return lax.dot_general(left, right, (((0,), (0,)), ((), ())), preferred_element_type=WIDER)


def right_product(left, right):
    return lax.dot_general(left, right, (((1,), (1,)), ((), ())), preferred_element_type=WIDER)


def bias_tiles(u_ref, h):
    tiles = []
    for d in range(3):
        row = u_ref[0, h, d : d + 1, :]
        wide = jnp.broadcast_to(row, (EDGE, SPAN))
        tiles.append(pltpu.roll(wide, 0, 1, stride=1, stride_axis=0)[:, :EDGE])
    return tiles


def bias_strip(tiles, low, high, first):
    columns = []
    for i in range(first, first + STRIP // EDGE):
        blocks = []
        for j in range(SLOT // EDGE):
            d = j - i
            if abs(d) <= 1:
                blocks.append(tiles[d + 1])
            else:
                blocks.append(jnp.full((EDGE, EDGE), low if d < 0 else high, WIDER))
        columns.append(jnp.concatenate(blocks, axis=0))
    return jnp.concatenate(columns, axis=1)


def strip_scores(n, keys, query, bias):
    raw = right_product(keys, query) + bias
    places = lax.broadcasted_iota(jnp.int32, (SLOT, STRIP), 0)
    return jnp.where(places < n, raw, MASKED)


def attn_fwd_kernel(n_ref, edge_ref, u_ref, q_ref, k_ref, v_ref, o_ref, st_ref):
    n = n_ref[0]
    step = pl.program_id(0)
    values = jnp.transpose(v_ref[...])
    mixed = []
    for h in range(2):
        low, high = edge_ref[2 * step + h, 0], edge_ref[2 * step + h, 1]
        tiles = bias_tiles(u_ref, h)
        cols = slice(HD * h, HD * h + HD)
        keys = k_ref[:, cols]
        strips = []
        for i in range(0, SLOT // EDGE, STRIP // EDGE):
            lanes = slice(EDGE * i, EDGE * i + STRIP)
            query = q_ref[lanes, cols] * 0.125
            scores = strip_scores(n, keys, query, bias_strip(tiles, low, high, i))
            top = jnp.max(scores, axis=0, keepdims=True)
            powers = jnp.exp(scores - top)
            share = 1.0 / jnp.sum(powers, axis=0, keepdims=True)
            st_ref[0, 2 * h : 2 * h + 1, lanes] = top
            st_ref[0, 2 * h + 1 : 2 * h + 2, lanes] = share
            probs = (powers * share).astype(LOWER)
            strips.append(product(values[cols], probs))
        mixed.append(jnp.concatenate(strips, axis=1))
    o_ref[...] = jnp.transpose(jnp.concatenate(mixed, axis=0)).astype(LOWER)


def attn_bwd_kernel(
    n_ref, edge_ref, u_ref, q_ref, k_ref, v_ref, g_ref, st_ref, gq_ref, gk_ref, gv_ref, gb_ref
):
    n = n_ref[0]
    step = pl.program_id(0)
    keys_t = jnp.transpose(k_ref[...])
    rows = lax.broadcasted_iota(jnp.int32, (EDGE, EDGE), 0)
    columns = lax.broadcasted_iota(jnp.int32, (EDGE, EDGE), 1)
    mirror = jnp.where(rows + columns == EDGE - 1, 1.0, 0.0).astype(LOWER)
    grad_queries = []
    for h in range(2):
        low, high = edge_ref[2 * step + h, 0], edge_ref[2 * step + h, 1]
        tiles = bias_tiles(u_ref, h)
        cols = slice(HD * h, HD * h + HD)
        keys = k_ref[:, cols]
        values = v_ref[:, cols]
        grad_keys = jnp.zeros((SLOT, HD), WIDER)
        grad_values = jnp.zeros((SLOT, HD), WIDER)
        strips = []
        sums = {}
        for i in range(0, SLOT // EDGE, STRIP // EDGE):
            lanes = slice(EDGE * i, EDGE * i + STRIP)
            query = q_ref[lanes, cols]
            grad = g_ref[lanes, cols]
            scores = strip_scores(n, keys, query * 0.125, bias_strip(tiles, low, high, i))
            top = st_ref[0, 2 * h : 2 * h + 1, lanes]
            share = st_ref[0, 2 * h + 1 : 2 * h + 2, lanes]
            probs = jnp.exp(scores - top) * share
            grad_probs = right_product(values, grad)
            weighted = jnp.sum(probs * grad_probs, axis=0, keepdims=True)
            rounded = (probs * (grad_probs - weighted)).astype(LOWER)
            strips.append(product(keys_t[cols], rounded))
            grad_keys += product(rounded, query)
            grad_values += product(probs.astype(LOWER), grad)
            wide = rounded.astype(WIDER)
            for c in range(STRIP // EDGE):
                for j in range(SLOT // EDGE):
                    d = min(max(j - i - c, -2), 2)
                    block = wide[EDGE * j : EDGE * j + EDGE, EDGE * c : EDGE * c + EDGE]
                    sums[d] = sums[d] + block if d in sums else block
        grad_queries.append(jnp.concatenate(strips, axis=1))
        gk_ref[:, cols] = (grad_keys * 0.125).astype(LOWER)
        gv_ref[:, cols] = grad_values.astype(LOWER)
        empty = jnp.zeros((EDGE, SPAN - EDGE), WIDER)
        band = jnp.concatenate([sums[-1], sums[0], sums[1]], axis=1)
        upper = band.astype(LOWER)
        lower = (band - upper.astype(WIDER)).astype(LOWER)
        mirrored = product(mirror, upper) + product(mirror, lower)
        for d in range(3):
            wide = jnp.concatenate([mirrored[:, EDGE * d : EDGE * d + EDGE], empty], axis=1)
            turned = pltpu.roll(wide, 0, 1, stride=1, stride_axis=0)
            gb_ref[0, h, d : d + 1, :] = jnp.sum(turned, axis=0, keepdims=True)
        for row, d in ((3, -2), (4, 2)):
            wide = jnp.concatenate([sums[d], empty], axis=1)
            gb_ref[0, h, row : row + 1, :] = jnp.sum(wide, axis=0, keepdims=True)
        gb_ref[0, h, 5:8, :] = jnp.zeros((3, SPAN), WIDER)
    gq_ref[...] = (jnp.transpose(jnp.concatenate(grad_queries, axis=0)) * 0.125).astype(LOWER)


def columns_at(first):
    return pl.BlockSpec((SLOT, PAIR), lambda s: (0, first + s))


SCALARS = pl.BlockSpec(memory_space=pltpu.SMEM)
TILE_ROWS = pl.BlockSpec((1, 2, 3, SPAN), lambda s: (s, 0, 0, 0))
STATS = pl.BlockSpec((1, 4, SLOT), lambda s: (s, 0, 0))
VMEM_BYTES = 48 * 1024 * 1024


def attention(count, edges, tile_rows, heads):
    return pl.pallas_call(
        attn_fwd_kernel,
        grid=(PAIRS,),
        out_shape=(
            jax.ShapeDtypeStruct((SLOT, D), LOWER),
            jax.ShapeDtypeStruct((PAIRS, 4, SLOT), WIDER),
        ),
        in_specs=[SCALARS, SCALARS, TILE_ROWS, columns_at(0), columns_at(PAIRS), columns_at(2 * PAIRS)],
        out_specs=(columns_at(0), STATS),
        compiler_params=pltpu.CompilerParams(vmem_limit_bytes=VMEM_BYTES),
        cost_estimate=pl.CostEstimate(flops=2 * 2 * H * SLOT * SLOT * HD * 4, bytes_accessed=4 * SLOT * D * 2, transcendentals=H * SLOT * SLOT),
        name="enc_attention",
    )(count, edges, tile_rows, heads, heads, heads)


def attention_back(count, edges, tile_rows, heads, grad_mixed, stats):
    return pl.pallas_call(
        attn_bwd_kernel,
        grid=(PAIRS,),
        out_shape=(
            jax.ShapeDtypeStruct((SLOT, D), LOWER),
            jax.ShapeDtypeStruct((SLOT, D), LOWER),
            jax.ShapeDtypeStruct((SLOT, D), LOWER),
            jax.ShapeDtypeStruct((PAIRS, 2, 8, SPAN), WIDER),
        ),
        in_specs=[SCALARS, SCALARS, TILE_ROWS, columns_at(0), columns_at(PAIRS), columns_at(2 * PAIRS), columns_at(0), STATS],
        out_specs=(columns_at(0), columns_at(0), columns_at(0), pl.BlockSpec((1, 2, 8, SPAN), lambda s: (s, 0, 0, 0))),
        compiler_params=pltpu.CompilerParams(vmem_limit_bytes=VMEM_BYTES),
        cost_estimate=pl.CostEstimate(flops=2 * 5 * H * SLOT * SLOT * HD * 4, bytes_accessed=8 * SLOT * D * 2, transcendentals=H * SLOT * SLOT),
        name="enc_attention_back",
    )(count, edges, tile_rows, heads, heads, heads, grad_mixed, stats)


GROUP = 24
STACK = H * GROUP
STAT = 128
C_GELU = 0.7978845608028654
ANY = pl.BlockSpec(memory_space=pl.ANY)


def silu_like(inner):
    tanh = jnp.tanh(C_GELU * (inner + 0.044715 * (inner * inner * inner)))
    value = 0.5 * inner * (1.0 + tanh)
    slope = 0.5 * (1.0 + tanh) + 0.5 * inner * (1.0 - tanh * tanh) * (
        C_GELU * (1.0 + 3.0 * 0.044715 * (inner * inner))
    )
    return value, slope


def scale_of(values):
    return lax.rsqrt(jnp.mean(values * values, axis=-1, keepdims=True) + EPS)


def norm_pull(values, gain, grad):
    scale = scale_of(values)
    lifted = grad * gain
    inside = jnp.sum(values * lifted, axis=-1, keepdims=True)
    back = scale * lifted - values * (scale * scale * scale * inside * (1.0 / D))
    return back, jnp.sum(grad * values * scale, axis=0, keepdims=True)


def head_lanes(h):
    lanes = lax.broadcasted_iota(jnp.int32, (GROUP, D), 1)
    return (lanes >= h * HD) & (lanes < (h + 1) * HD)


def stack_heads(flat):
    return jnp.concatenate([jnp.where(head_lanes(h), flat, 0.0) for h in range(H)], axis=0)


def merge_heads(stacked):
    total = jnp.zeros((GROUP, D), WIDER)
    for h in range(H):
        total = total + jnp.where(head_lanes(h), stacked[GROUP * h : GROUP * h + GROUP], 0.0)
    return total


def lanes_to_column(stat):
    lanes = lax.broadcasted_iota(jnp.int32, (GROUP, STAT), 1)
    parts = [jnp.sum(jnp.where(lanes == h, stat, 0.0), axis=1, keepdims=True) for h in range(H)]
    return jnp.concatenate(parts, axis=0)


def column_to_lanes(column, first):
    lanes = lax.broadcasted_iota(jnp.int32, (GROUP, STAT), 1)
    total = jnp.zeros((GROUP, STAT), WIDER)
    for h in range(H):
        total = total + jnp.where(lanes == first + h, column[GROUP * h : GROUP * h + GROUP], 0.0)
    return total


def spread_heads(stat):
    rows = lax.broadcasted_iota(jnp.int32, (STAT, D), 0) * HD
    lanes = lax.broadcasted_iota(jnp.int32, (STAT, D), 1)
    spread = jnp.where((lanes >= rows) & (lanes < rows + HD), 1.0, 0.0).astype(LOWER)
    upper = stat.astype(LOWER)
    lower = (stat - upper.astype(WIDER)).astype(LOWER)
    return product(upper, spread) + product(lower, spread)


def own_scores(query, keys, table_ref):
    raw = right_product(query, keys)
    rows = lax.broadcasted_iota(jnp.int32, (GROUP, GROUP), 0)
    columns = lax.broadcasted_iota(jnp.int32, (GROUP, GROUP), 1)
    away = rows - columns
    parts = []
    for h in range(H):
        bias = jnp.full((GROUP, GROUP), table_ref[0, h], WIDER)
        for d in range(1, GROUP):
            bias = jnp.where(away == d, table_ref[d, h], bias)
        part = raw[GROUP * h : GROUP * h + GROUP] + bias
        parts.append(jnp.where(away >= 0, part, MASKED))
    scores = jnp.concatenate(parts, axis=0)
    powers = jnp.exp(scores - jnp.max(scores, axis=1, keepdims=True))
    return powers / jnp.sum(powers, axis=1, keepdims=True)


def fetch(sources, targets, sems):
    copies = [pltpu.make_async_copy(s, t, sems.at[k]) for k, (s, t) in enumerate(zip(sources, targets))]
    for copy in copies:
        copy.start()
    return copies


def dec_self_kernel(
    table_ref, x_ref, g1_ref, g2_ref, qkv_any, out_any, query_any,
    after_ref, lefts_ref, heads_ref, query_ref, qkv_ref, out_ref, cross_ref, sems,
):
    copies = fetch((qkv_any, out_any, query_any), (qkv_ref, out_ref, cross_ref), sems)
    start = x_ref[...].astype(WIDER)
    first = (start * scale_of(start) * g1_ref[...]).astype(LOWER)
    copies[0].wait()
    heads = product(first, qkv_ref[...]).astype(LOWER)
    heads_ref[...] = heads
    wide = heads.astype(WIDER)
    query = stack_heads(wide[:, :D] * 0.125).astype(LOWER)
    probs = own_scores(query, heads[:, D : 2 * D], table_ref)
    own = merge_heads(product(probs.astype(LOWER), heads[:, 2 * D :])).astype(LOWER)
    copies[1].wait()
    after = start + product(own, out_ref[...])
    after_ref[...] = after
    second = (after * scale_of(after) * g2_ref[...]).astype(LOWER)
    copies[2].wait()
    query_ref[...] = product(second, cross_ref[...]).astype(LOWER)
    lefts_ref[:, :D] = first
    lefts_ref[:, D : 2 * D] = own
    lefts_ref[:, 2 * D :] = second


def cross_scores(n_ref, query_ref, pairs_ref):
    query = stack_heads(query_ref[...].astype(WIDER) * 0.125).astype(LOWER)
    raw = right_product(query, pairs_ref[:, :D])
    places = lax.broadcasted_iota(jnp.int32, (STACK, SLOT), 1)
    return query, jnp.where(places < n_ref[0], raw, MASKED)


def cross_kernel(n_ref, query_ref, pairs_ref, packed_ref):
    unused, scores = cross_scores(n_ref, query_ref, pairs_ref)
    top = jnp.max(scores, axis=1, keepdims=True)
    powers = jnp.exp(scores - top)
    total = jnp.sum(powers, axis=1, keepdims=True)
    probs = (powers / total).astype(LOWER)
    packed_ref[:, :D] = merge_heads(product(probs, pairs_ref[:, D:]))
    packed_ref[:, D:] = column_to_lanes(top, 0) + column_to_lanes(total, STAT // 2)


def dec_mid_kernel(
    parts_ref, after_ref, cot_ref, g3_ref, cross_any, in_any, out_any,
    answer_ref, mids_ref, mix_ref, gmix_ref, gmid_ref, stat_ref, gain_ref,
    cross_ref, in_ref, out_ref, sems,
):
    copies = fetch((cross_any, in_any, out_any), (cross_ref, in_ref, out_ref), sems)
    size = parts_ref.shape[0]
    lanes = lax.broadcasted_iota(jnp.int32, (GROUP, STAT), 1)
    used = lanes < H
    tops, totals = [], []
    for k in range(size):
        stat = parts_ref[k, :, D:]
        tops.append(stat)
        totals.append(pltpu.roll(stat, STAT // 2, 1))
    top = tops[0]
    for k in range(1, size):
        top = jnp.maximum(top, tops[k])
    weights = [jnp.where(used, totals[k] * jnp.exp(tops[k] - top), 0.0) for k in range(size)]
    total = weights[0]
    for k in range(1, size):
        total = total + weights[k]
    total = jnp.where(used, total, 1.0)
    mix = jnp.zeros((GROUP, D), WIDER)
    for k in range(size):
        mix = mix + parts_ref[k, :, :D] * spread_heads(weights[k] / total)
    mix_ref[...] = mix
    stat_ref[:, :STAT] = jnp.where(used, top, 0.0)
    stat_ref[:, STAT:] = total
    mix_low = mix.astype(LOWER)
    copies[0].wait()
    middle = after_ref[...] + product(mix_low, cross_ref[...])
    third = (middle * scale_of(middle) * g3_ref[...]).astype(LOWER)
    copies[1].wait()
    inner = product(third, in_ref[...])
    value, slope = silu_like(inner)
    hidden = value.astype(LOWER)
    copies[2].wait()
    answer_ref[...] = (middle + product(hidden, out_ref[...])).astype(LOWER)
    out_low = cot_ref[...]
    g_inner = (right_product(out_low, out_ref[...]) * slope).astype(LOWER)
    back, gain = norm_pull(middle, g3_ref[...], right_product(g_inner, in_ref[...]))
    gain_ref[...] = gain
    g_middle = out_low.astype(WIDER) + back
    gmid_ref[...] = g_middle
    middle_low = g_middle.astype(LOWER)
    gmix_ref[...] = right_product(middle_low, cross_ref[...]).astype(LOWER)
    mids_ref[:, :D] = mix_low
    mids_ref[:, D : 2 * D] = third
    mids_ref[:, 2 * D : 2 * D + FF] = hidden
    mids_ref[:, 2 * D + FF : 3 * D + FF] = middle_low
    mids_ref[:, 3 * D + FF :] = g_inner


def cross_back_kernel(n_ref, query_ref, pairs_ref, gmix_ref, mix_ref, stat_ref, gpairs_ref, partial_ref):
    query, scores = cross_scores(n_ref, query_ref, pairs_ref)
    top = lanes_to_column(stat_ref[:, :STAT])
    total = lanes_to_column(stat_ref[:, STAT:])
    probs = jnp.exp(scores - top) / total
    grad = stack_heads(gmix_ref[...].astype(WIDER))
    weighted = jnp.sum(grad * jnp.concatenate([mix_ref[...]] * H, axis=0), axis=1, keepdims=True)
    grad = grad.astype(LOWER)
    grad_probs = right_product(grad, pairs_ref[:, D:])
    rounded = (probs * (grad_probs - weighted)).astype(LOWER)
    gpairs_ref[:, :D] = left_product(rounded, query).astype(LOWER)
    gpairs_ref[:, D:] = left_product(probs.astype(LOWER), grad).astype(LOWER)
    partial_ref[...] = merge_heads(product(rounded, pairs_ref[:, :D])) * 0.125


def dec_back_kernel(
    table_ref, x_ref, gquery_ref, after_ref, gmid_ref, heads_ref, lefts_ref, mids_ref, cot_ref,
    g1_ref, g2_ref, gain3_ref, query_any, out_any, qkv_any,
    factors_ref, gstart_ref, cross_ref, out_ref, qkv_ref, sems,
):
    copies = fetch((query_any, out_any, qkv_any), (cross_ref, out_ref, qkv_ref), sems)
    g_query = gquery_ref[...].astype(LOWER)
    copies[0].wait()
    back, gain2 = norm_pull(after_ref[...], g2_ref[...], right_product(g_query, cross_ref[...]))
    g_after = gmid_ref[...] + back
    after_low = g_after.astype(LOWER)
    copies[1].wait()
    g_own = stack_heads(right_product(after_low, out_ref[...])).astype(LOWER)
    heads = heads_ref[...]
    wide = heads.astype(WIDER)
    query = stack_heads(wide[:, :D] * 0.125).astype(LOWER)
    probs = own_scores(query, heads[:, D : 2 * D], table_ref)
    grad_probs = right_product(g_own, heads[:, 2 * D :])
    rounded = (probs * (grad_probs - jnp.sum(probs * grad_probs, axis=1, keepdims=True))).astype(LOWER)
    g_q = (merge_heads(product(rounded, heads[:, D : 2 * D])) * 0.125).astype(LOWER)
    g_k = left_product(rounded, query).astype(LOWER)
    g_v = left_product(probs.astype(LOWER), g_own).astype(LOWER)
    g_heads = jnp.concatenate([g_q, g_k, g_v], axis=1)
    copies[2].wait()
    start = x_ref[...].astype(WIDER)
    back, gain1 = norm_pull(start, g1_ref[...], right_product(g_heads, qkv_ref[...]))
    gstart_ref[...] = g_after + back
    wide = rounded.astype(WIDER)
    rows = lax.broadcasted_iota(jnp.int32, (GROUP, GROUP), 0)
    columns = lax.broadcasted_iota(jnp.int32, (GROUP, GROUP), 1)
    mirror = jnp.where(rows + columns == GROUP - 1, 1.0, 0.0).astype(LOWER)
    empty = jnp.zeros((GROUP, STAT - GROUP), WIDER)
    tables = []
    for h in range(H):
        part = product(mirror, wide[GROUP * h : GROUP * h + GROUP].astype(LOWER))
        turned = pltpu.roll(jnp.concatenate([part, empty], axis=1), 0, 1, stride=1, stride_axis=0)
        tables.append(jnp.sum(turned, axis=0, keepdims=True))
    small = jnp.concatenate([gain1, gain2, gain3_ref[...]] + tables, axis=1)
    width = small.shape[1]
    places = lax.broadcasted_iota(jnp.int32, (GROUP, width), 0)
    lefts = jnp.concatenate([lefts_ref[...].astype(WIDER), mids_ref[:, : 2 * D].astype(WIDER)], axis=1)
    factors_ref[:, :width] = jnp.where(places == ANS, small, lefts).astype(LOWER)
    factors_ref[:, width : 5 * D + 2 * FF + D] = mids_ref[:, 2 * D :]
    base = 6 * D + 2 * FF
    factors_ref[:, base : base + 3 * D] = g_heads
    factors_ref[:, base + 3 * D : base + 4 * D] = after_low
    factors_ref[:, base + 4 * D : base + 5 * D] = g_query
    factors_ref[:, base + 5 * D :] = cot_ref[...]


FACTORS = 9 * D + 3 * D + 2 * FF
AT = {
    "first": 0,
    "own": D,
    "second": 2 * D,
    "mix": 3 * D,
    "third": 4 * D,
    "hidden": 5 * D,
    "g_middle": 5 * D + FF,
    "g_inner": 6 * D + FF,
    "g_heads": 6 * D + 2 * FF,
    "g_after": 9 * D + 2 * FF,
    "g_query": 10 * D + 2 * FF,
    "g_out": 11 * D + 2 * FF,
}
PARAMS = pltpu.CompilerParams(vmem_limit_bytes=VMEM_BYTES)
WHOLE = pl.BlockSpec(memory_space=pltpu.VMEM)


def wide(rows, columns):
    return jax.ShapeDtypeStruct((rows, columns), WIDER)


def narrow(rows, columns):
    return jax.ShapeDtypeStruct((rows, columns), LOWER)


def held(*shapes):
    return [pltpu.VMEM(shape, LOWER) for shape in shapes] + [pltpu.SemaphoreType.DMA((len(shapes),))]


def dec_self(table, answers, gain1, gain2, qkv, out, query):
    return pl.pallas_call(
        dec_self_kernel,
        out_shape=(wide(GROUP, D), narrow(GROUP, 3 * D), narrow(GROUP, 3 * D), narrow(GROUP, D)),
        in_specs=[SCALARS] + [WHOLE] * 3 + [ANY] * 3,
        scratch_shapes=held((D, 3 * D), (D, D), (D, D)),
        compiler_params=PARAMS,
        cost_estimate=pl.CostEstimate(flops=10**9, bytes_accessed=2 * 5 * D * D, transcendentals=STACK * STAT),
        name="dec_self",
    )(table, answers, gain1, gain2, qkv, out, query)


def cross(count, query, pairs):
    return pl.pallas_call(
        cross_kernel,
        out_shape=wide(GROUP, D + STAT),
        in_specs=[SCALARS, WHOLE, WHOLE],
        compiler_params=PARAMS,
        cost_estimate=pl.CostEstimate(flops=4 * STACK * SLOT * D, bytes_accessed=4 * SLOT * D, transcendentals=STACK * SLOT),
        name="cross",
    )(count, query, pairs)


def dec_mid(parts, after, cotangent, gain3, cross_out, ffn_in, ffn_out):
    return pl.pallas_call(
        dec_mid_kernel,
        out_shape=(
            narrow(GROUP, D),
            narrow(GROUP, 3 * D + 2 * FF),
            wide(GROUP, D),
            narrow(GROUP, D),
            wide(GROUP, D),
            wide(GROUP, 2 * STAT),
            wide(1, D),
        ),
        in_specs=[WHOLE] * 4 + [ANY] * 3,
        scratch_shapes=held((D, D), (D, FF), (FF, D)),
        compiler_params=PARAMS,
        cost_estimate=pl.CostEstimate(flops=4 * 10**9, bytes_accessed=2 * 9 * D * D, transcendentals=GROUP * FF),
        name="dec_mid",
    )(parts, after, cotangent, gain3, cross_out, ffn_in, ffn_out)


def cross_back(count, query, pairs, g_mix, mix, stat):
    return pl.pallas_call(
        cross_back_kernel,
        out_shape=(narrow(SLOT, 2 * D), wide(GROUP, D)),
        in_specs=[SCALARS] + [WHOLE] * 5,
        compiler_params=PARAMS,
        cost_estimate=pl.CostEstimate(flops=10 * STACK * SLOT * D, bytes_accessed=8 * SLOT * D, transcendentals=STACK * SLOT),
        name="cross_back",
    )(count, query, pairs, g_mix, mix, stat)


def dec_back(table, answers, g_query, after, g_middle, heads, lefts, mids, cotangent, gain1, gain2, g_gain3, query, out, qkv):
    return pl.pallas_call(
        dec_back_kernel,
        out_shape=(narrow(GROUP, FACTORS), wide(GROUP, D)),
        in_specs=[SCALARS] + [WHOLE] * 11 + [ANY] * 3,
        scratch_shapes=held((D, D), (D, D), (D, 3 * D)),
        compiler_params=PARAMS,
        cost_estimate=pl.CostEstimate(flops=10**9, bytes_accessed=2 * 5 * D * D, transcendentals=STACK * STAT),
        name="dec_back",
    )(table, answers, g_query, after, g_middle, heads, lefts, mids, cotangent, gain1, gain2, g_gain3, query, out, qkv)


def norm_rows(values, gain):
    return values * lax.rsqrt(jnp.mean(values * values, axis=-1, keepdims=True) + EPS) * gain


def norm_back(values, gain, grad):
    unused, pull = jax.vjp(norm_rows, values, gain)
    return pull(grad)


def gelu_back(inner, grad):
    unused, pull = jax.vjp(jax.nn.gelu, inner)
    return pull(grad)[0]


def partner(axis, bit):
    return [(k, k ^ (1 << bit)) for k in range(lax.axis_size(axis))]


def all_sum(value, axis):
    for bit in range(lax.axis_size(axis).bit_length() - 1):
        value = value + lax.ppermute(value, axis, partner(axis, bit))
    return value


def pa_order(turn):
    rest = lax.axis_size("pa").bit_length() - 2
    return [1 + (k + turn) % rest for k in range(rest)]


def both_cores(acts, turn):
    size = lax.axis_size("pa")
    me = lax.axis_index("pa")
    blocks = jnp.transpose(acts).reshape(size, acts.shape[1] // size, acts.shape[0])
    order = pa_order(turn)
    offsets = [
        sum(((k >> (len(order) - 1 - p)) & 1) << bit for p, bit in enumerate(order)) for k in range(size // 2)
    ]
    mine = jnp.concatenate([lax.dynamic_slice_in_dim(blocks, me ^ d, 1) for d in offsets])
    theirs = jnp.concatenate([lax.dynamic_slice_in_dim(blocks, me ^ d ^ 1, 1) for d in offsets])
    return mine, lax.ppermute(theirs, "pa", partner("pa", 0))


def weight_part(acts, grads, first, last):
    total = None
    for act, grad in zip(acts, grads):
        act = act[first:last]
        term = product(act.reshape(-1, act.shape[2]), grad)
        total = term if total is None else total + term
    height = acts[0].shape[1]
    return total.astype(LOWER).reshape(last - first, height, -1)


def add_up(parts):
    total = parts[0].astype(WIDER)
    for part in parts[1:]:
        total = total + part.astype(WIDER)
    return total.astype(LOWER)


def share_over_pa(acts, grads, turn):
    size = acts[0].shape[0]
    keep = [weight_part(acts, grads, 0, size // 2)]
    send = weight_part(acts, grads, size // 2, size)
    for bit in pa_order(turn):
        keep.append(lax.ppermute(send, "pa", partner("pa", bit)))
        size //= 2
        if size > 1:
            send = add_up([part[size // 2 : size] for part in keep])
            keep = [part[: size // 2] for part in keep]
    return add_up([part[0] for part in keep])


def total_over_pb(share):
    size = lax.axis_size("pb")
    if size != 4:
        return lax.psum(share, "pb").astype(WIDER)
    me = lax.axis_index("pb")
    inner = (me == 1) | (me == 2)
    share = add_up([share, lax.ppermute(share, "pb", [(0, 1), (3, 2)])])
    share = add_up([share, lax.ppermute(share, "pb", [(1, 2), (2, 1)])])
    got = lax.ppermute(share, "pb", [(1, 0), (2, 3)])
    return jnp.where(inner, share, got).astype(WIDER)


def local(
    passages,
    lengths,
    answers,
    cotangent,
    enc_gain1,
    enc_qkv,
    enc_bias,
    enc_out,
    enc_gain2,
    enc_ffn_in,
    enc_ffn_out,
    enc_gain3,
    cross_kv,
    dec_gain1,
    dec_qkv,
    dec_bias,
    dec_out,
    dec_gain2,
    cross_query,
    cross_out,
    dec_gain3,
    dec_ffn_in,
    dec_ffn_out,
):
    pa_size = lax.axis_size("pa")
    pb_size = lax.axis_size("pb")
    rows = passages.reshape(SLOT, D).astype(WIDER)
    count = lengths.reshape(1)
    tile_rows = jnp.transpose(jnp.dot(jnp.asarray(PICK), enc_bias, precision=HIGH)).reshape(PAIRS, 2, 3, SPAN)
    edges = jnp.stack([enc_bias[0], enc_bias[BUCKETS - 1]], axis=1)
    extra = ((0, GROUP - ANS), (0, 0))
    start = jnp.pad(answers[0], extra)
    out_low = jnp.pad(cotangent[0], extra)
    gains = [gain.reshape(1, D) for gain in (dec_gain1, dec_gain2, dec_gain3)]

    dec_after, lefts, dec_heads, query = dec_self(
        dec_bias, start, gains[0], gains[1], dec_qkv, dec_out, cross_query
    )
    first = norm_rows(rows, enc_gain1).astype(LOWER)
    heads = product(first, enc_qkv).astype(LOWER)
    mixed, stats = attention(count, edges, tile_rows, heads)
    after = rows + product(mixed, enc_out)
    second = norm_rows(after, enc_gain2).astype(LOWER)
    inner = product(second, enc_ffn_in)
    hidden = jax.nn.gelu(inner).astype(LOWER)
    final = after + product(hidden, enc_ffn_out)
    third = norm_rows(final, enc_gain3).astype(LOWER)
    pairs = product(third, cross_kv).astype(LOWER)
    acts_kv = both_cores(third, 0)
    acts_ffn_out = both_cores(hidden, 1)
    acts_ffn_in = both_cores(second, 0)
    acts_out = both_cores(mixed, 1)
    acts_qkv = both_cores(first, 0)
    acts_qkv_too = both_cores(first, 1)

    gathered = lax.all_gather(cross(count, query, pairs), "pa")
    answer, mids, mix, g_mix, g_middle, stat, g_gain3 = dec_mid(
        gathered, dec_after, out_low, gains[2], cross_out, dec_ffn_in, dec_ffn_out
    )
    g_pairs, partial_query = cross_back(count, query, pairs, g_mix, mix, stat)
    g_query = all_sum(partial_query, "pa")

    def across(value):
        return value, lax.ppermute(value, "pa", partner("pa", 0))

    share_kv = share_over_pa(acts_kv, across(g_pairs), 0)
    g_final, g_enc_gain3 = norm_back(final, enc_gain3, right_product(g_pairs, cross_kv))
    branch = g_final.astype(LOWER)
    share_ffn_out = share_over_pa(acts_ffn_out, across(branch), 1)
    g_inner = gelu_back(inner, right_product(branch, enc_ffn_out)).astype(LOWER)
    share_ffn_in = share_over_pa(acts_ffn_in, across(g_inner), 0)
    g_after_part, g_enc_gain2 = norm_back(after, enc_gain2, right_product(g_inner, enc_ffn_in))
    g_after = g_final + g_after_part
    branch = g_after.astype(LOWER)
    share_out = share_over_pa(acts_out, across(branch), 1)
    g_mixed = right_product(branch, enc_out).astype(LOWER)
    enc_q, enc_k, enc_v, diagonals = attention_back(count, edges, tile_rows, heads, g_mixed, stats)
    g_heads = jnp.concatenate([enc_q, enc_k, enc_v], axis=1)
    here, there = across(g_heads)
    cut = 3 * D // 2
    share_qkv = share_over_pa(acts_qkv, (here[:, :cut], there[:, :cut]), 0)
    share_qkv_too = share_over_pa(acts_qkv_too, (here[:, cut:], there[:, cut:]), 1)
    bias_rows = jnp.dot(diagonals[:, :, :3].reshape(H, 3 * SPAN), jnp.asarray(PICK_BACK), precision=HIGH)
    bias_ends = jnp.sum(diagonals[:, :, 3:5], axis=-1).reshape(H, 2)
    bias_rows = jnp.concatenate(
        [bias_rows[:, :1] + bias_ends[:, :1], bias_rows[:, 1:-1], bias_rows[:, -1:] + bias_ends[:, 1:]],
        axis=1,
    )
    g_rows_part, g_enc_gain1 = norm_back(rows, enc_gain1, right_product(g_heads, enc_qkv))
    g_rows = g_after + g_rows_part
    small = jnp.concatenate([g_enc_gain1, g_enc_gain2, g_enc_gain3, bias_rows.reshape(-1)])
    small = jnp.pad(small, (0, -small.shape[0] % 1024)).reshape(-1, 128)
    small = all_sum(all_sum(small, "pa"), "pb").reshape(-1)

    factors, g_start = dec_back(
        dec_bias, start, g_query, dec_after, g_middle, dec_heads, lefts, mids, out_low,
        gains[0], gains[1], g_gain3, cross_query, dec_out, dec_qkv,
    )
    every = lax.all_gather(factors, "pb")
    sums = jnp.sum(every[:, ANS, : 3 * D + H * STAT].astype(WIDER), axis=0)
    table = sums[3 * D :].reshape(H, STAT)[:, GROUP - ANS : GROUP]
    table = jnp.pad(jnp.transpose(table[:, ::-1]), ((0, BUCKETS - ANS), (0, 0)))
    every = every.reshape(pb_size * GROUP, FACTORS)
    me = lax.axis_index("pb")

    def outer(a, width_a, b, width_b):
        height = width_a // pb_size
        left = lax.dynamic_slice_in_dim(every[:, AT[a] : AT[a] + width_a], me * height, height, axis=1)
        return left_product(left, every[:, AT[b] : AT[b] + width_b])

    def own_part(vector, axis="pb"):
        height = vector.shape[0] // lax.axis_size(axis)
        return lax.dynamic_slice_in_dim(vector, lax.axis_index(axis) * height, height, axis=0)

    g_qkv = jnp.concatenate([total_over_pb(share_qkv), total_over_pb(share_qkv_too)], axis=1)
    return (
        answer[:ANS][None],
        g_rows.reshape(1, 1, SLOT, D),
        g_start[:ANS][None],
        own_part(small[:D], "pa"),
        g_qkv,
        jnp.transpose(small[3 * D : 3 * D + H * BUCKETS].reshape(H, BUCKETS)),
        total_over_pb(share_out),
        own_part(small[D : 2 * D], "pa"),
        total_over_pb(share_ffn_in),
        total_over_pb(share_ffn_out),
        own_part(small[2 * D : 3 * D], "pa"),
        total_over_pb(share_kv),
        own_part(sums[:D]),
        outer("first", D, "g_heads", 3 * D),
        own_part(table),
        outer("own", D, "g_after", D),
        own_part(sums[D : 2 * D]),
        outer("second", D, "g_query", D),
        outer("mix", D, "g_middle", D),
        own_part(sums[2 * D : 3 * D]),
        outer("third", D, "g_inner", FF),
        outer("hidden", FF, "g_out", D),
    )


def solution(mesh):
    copied = P()
    in_specs = (
        P("pb", "pa", None, None),
        P("pb", "pa"),
        P("pb", None, None),
        P("pb", None, None),
    ) + (copied,) * 19
    by_pa, by_pa_rows = P("pa"), P("pa", None)
    by_pb, by_pb_rows = P("pb"), P("pb", None)
    out_specs = (
        P("pb", None, None),
        P("pb", "pa", None, None),
        P("pb", None, None),
        by_pa,
        by_pa_rows,
        copied,
        by_pa_rows,
        by_pa,
        by_pa_rows,
        by_pa_rows,
        by_pa,
        by_pa_rows,
        by_pb,
        by_pb_rows,
        by_pb_rows,
        by_pb_rows,
        by_pb,
        by_pb_rows,
        by_pb_rows,
        by_pb,
        by_pb_rows,
        by_pb_rows,
    )
    return jax.shard_map(local, mesh=mesh, in_specs=in_specs, out_specs=out_specs, check_vma=False)
```

```python
import jax
import jax.numpy as jnp
import numpy as np
from jax import lax
from jax.experimental import pallas as pl
from jax.experimental.pallas import tpu as pltpu
from jax.sharding import PartitionSpec as P

D = 768
H = 12
HD = 64
FF = 3072
BUCKETS = 32
ANS = 20
SLOT = 512
PAIR = 2 * HD
PAIRS = H // 2
EDGE = 128
STRIP = 256
SPAN = 256
GROUP = 24
STACK = H * GROUP
STAT = 128
STEPS = 4
WIDTH = FF // STEPS
HALF = D // 2
EPS = 1e-06
MASKED = -1000000000.0
C_GELU = 0.7978845608028654
LOWER = jnp.bfloat16
WIDER = jnp.float32
VMEM_BYTES = 56 * 1024 * 1024
EARLY = 7 * D + 2 * FF
LATE = 5 * D
AT = {
    "first": 0,
    "own": D,
    "second": 2 * D,
    "mix": 3 * D,
    "third": 4 * D,
    "hidden": 5 * D,
    "g_middle": 5 * D + FF,
    "g_inner": 6 * D + FF,
    "g_out": 6 * D + 2 * FF,
    "g_heads": 0,
    "g_after": 3 * D,
    "g_query": 4 * D,
}


def tile_classes(away):
    rows = [np.clip(EDGE * d - away, -(BUCKETS // 2), BUCKETS // 2 - 1) + BUCKETS // 2 for d in (-1, 0, 1)]
    return np.eye(BUCKETS, dtype=np.float32)[np.concatenate(rows)]


LANES = np.arange(SPAN)
PICK = tile_classes(np.where(LANES < EDGE, LANES, LANES - SPAN)).T
ENDS = np.repeat(np.eye(BUCKETS, dtype=np.float32)[[0, BUCKETS - 1]], EDGE, axis=0)
PICK_BACK = np.pad(np.concatenate([tile_classes(LANES - (EDGE - 1)), ENDS]), ((0, 0), (0, STAT - BUCKETS)))

SCALARS = pl.BlockSpec(memory_space=pltpu.SMEM)
ANY = pl.BlockSpec(memory_space=pl.ANY)
WHOLE = pl.BlockSpec(memory_space=pltpu.VMEM)
TOKEN = (8, 128)


def wide(*shape):
    return jax.ShapeDtypeStruct(shape, WIDER)


def narrow(*shape):
    return jax.ShapeDtypeStruct(shape, LOWER)


def run(name, body, ins, in_specs, outs, out_specs=None, after=(), grid=(), scratch=(), flops=0, exps=0):
    count, extra, results = len(ins), len(after), len(outs)
    if out_specs is None:
        out_specs = [WHOLE] * results
    zeros = (lambda *s: (0, 0)) if grid else (lambda: (0, 0))

    def wrapped(*refs):
        refs[count + extra + results][...] = jnp.zeros(TOKEN, WIDER)
        body(*refs[:count], *refs[count + extra : count + extra + results], *refs[count + extra + results + 1 :])

    moved = sum(int(np.prod(a.shape)) * a.dtype.itemsize for a in list(ins) + list(outs))
    got = pl.pallas_call(
        wrapped,
        grid=grid,
        out_shape=tuple(outs) + (wide(*TOKEN),),
        in_specs=list(in_specs) + [ANY] * extra,
        out_specs=tuple(out_specs) + (pl.BlockSpec(TOKEN, zeros),),
        scratch_shapes=list(scratch),
        compiler_params=pltpu.CompilerParams(vmem_limit_bytes=VMEM_BYTES),
        cost_estimate=pl.CostEstimate(flops=flops, bytes_accessed=moved, transcendentals=exps),
        name=name,
    )(*ins, *after)
    return got


def product(left, right):
    return jnp.dot(left, right, preferred_element_type=WIDER)


def left_product(left, right):
    return lax.dot_general(left, right, (((0,), (0,)), ((), ())), preferred_element_type=WIDER)


def right_product(left, right):
    return lax.dot_general(left, right, (((1,), (1,)), ((), ())), preferred_element_type=WIDER)


def split_product(left, right, terms):
    total = None
    for k in range(terms):
        part = left.astype(LOWER)
        left = left - part.astype(WIDER)
        term = product(part, right)
        total = term if total is None else total + term
    return total


def silu_like(inner):
    square = inner * inner
    tanh = jnp.tanh(inner * (C_GELU + (C_GELU * 0.044715) * square))
    half = 0.5 + 0.5 * tanh
    value = inner * half
    slope = half + value * (1.0 - tanh) * (C_GELU + (3.0 * C_GELU * 0.044715) * square)
    return value, slope


def row_of(ref):
    return ref[...].reshape(1, D)


def scale_of(values):
    return lax.rsqrt(jnp.mean(values * values, axis=-1, keepdims=True) + EPS)


def norm_pull(values, gain, grad):
    scale = scale_of(values)
    lifted = grad * gain
    inside = jnp.sum(values * lifted, axis=-1, keepdims=True)
    back = scale * lifted - values * (scale * scale * scale * inside * (1.0 / D))
    return back, jnp.sum(grad * values * scale, axis=0, keepdims=True)


def fetch(pairs, sems):
    copies = [pltpu.make_async_copy(s, t, sems.at[k]) for k, (s, t) in enumerate(pairs)]
    for copy in copies:
        copy.start()
    return copies


def bias_tiles(u_ref, head):
    tiles = []
    for d in range(3):
        row = u_ref[pl.ds(head, 1), SPAN * d : SPAN * d + SPAN]
        spread = jnp.broadcast_to(row, (EDGE, SPAN))
        tiles.append(pltpu.roll(spread, 0, 1, stride=1, stride_axis=0)[:, :EDGE])
    return tiles


def bias_strip(tiles, low, high, first):
    columns = []
    for i in range(first, first + STRIP // EDGE):
        blocks = []
        for j in range(SLOT // EDGE):
            d = j - i
            if abs(d) <= 1:
                blocks.append(tiles[d + 1])
            else:
                blocks.append(jnp.full((EDGE, EDGE), low if d < 0 else high, WIDER))
        columns.append(jnp.concatenate(blocks, axis=0))
    return jnp.concatenate(columns, axis=1)


def strip_scores(n, keys, query, bias):
    raw = right_product(keys, query) + bias
    places = lax.broadcasted_iota(jnp.int32, (SLOT, STRIP), 0)
    return jnp.where(places < n, raw, MASKED)


def fill_rows(table_ref, pick_ref, u_ref):
    @pl.when(pl.program_id(0) == 0)
    def _():
        u_ref[...] = split_product(table_ref[...], pick_ref[...], 3)


def attn_fwd_kernel(n_ref, ends_ref, table_ref, pick_ref, q_ref, k_ref, v_ref, o_ref, st_ref, u_ref):
    fill_rows(table_ref, pick_ref, u_ref)
    n = n_ref[0]
    step = pl.program_id(0)
    values = jnp.transpose(v_ref[...])
    mixed = []
    for h in range(2):
        head = 2 * step + h
        low, high = ends_ref[head, 0], ends_ref[head, BUCKETS - 1]
        tiles = bias_tiles(u_ref, head)
        cols = slice(HD * h, HD * h + HD)
        keys = k_ref[:, cols]
        strips = []
        for i in range(0, SLOT // EDGE, STRIP // EDGE):
            lanes = slice(EDGE * i, EDGE * i + STRIP)
            query = q_ref[lanes, cols] * 0.125
            scores = strip_scores(n, keys, query, bias_strip(tiles, low, high, i))
            top = jnp.max(scores, axis=0, keepdims=True)
            powers = jnp.exp(scores - top)
            share = 1.0 / jnp.sum(powers, axis=0, keepdims=True)
            st_ref[0, 2 * h : 2 * h + 1, lanes] = top
            st_ref[0, 2 * h + 1 : 2 * h + 2, lanes] = share
            probs = (powers * share).astype(LOWER)
            strips.append(product(values[cols], probs))
        mixed.append(jnp.concatenate(strips, axis=1))
    o_ref[...] = jnp.transpose(jnp.concatenate(mixed, axis=0)).astype(LOWER)


def attn_bwd_kernel(base):
    def body(
        n_ref, ends_ref, table_ref, pick_ref, q_ref, k_ref, v_ref, g_ref, st_ref, gh_ref, gb_ref, u_ref
    ):
        fill_rows(table_ref, pick_ref, u_ref)
        n = n_ref[0]
        step = pl.program_id(0) + base
        keys_t = jnp.transpose(k_ref[...])
        rows = lax.broadcasted_iota(jnp.int32, (EDGE, EDGE), 0)
        columns = lax.broadcasted_iota(jnp.int32, (EDGE, EDGE), 1)
        mirror = jnp.where(rows + columns == EDGE - 1, 1.0, 0.0).astype(LOWER)
        grad_queries = []
        gb_ref[0, 2:8, :] = jnp.zeros((6, 4 * SPAN), WIDER)
        for h in range(2):
            head = 2 * step + h
            low, high = ends_ref[head, 0], ends_ref[head, BUCKETS - 1]
            tiles = bias_tiles(u_ref, head)
            cols = slice(HD * h, HD * h + HD)
            keys = k_ref[:, cols]
            values = v_ref[:, cols]
            grad_keys = jnp.zeros((SLOT, HD), WIDER)
            grad_values = jnp.zeros((SLOT, HD), WIDER)
            strips = []
            sums = {}
            for i in range(0, SLOT // EDGE, STRIP // EDGE):
                lanes = slice(EDGE * i, EDGE * i + STRIP)
                query = q_ref[lanes, cols]
                grad = g_ref[lanes, cols]
                scores = strip_scores(n, keys, query * 0.125, bias_strip(tiles, low, high, i))
                top = st_ref[0, 2 * h : 2 * h + 1, lanes]
                share = st_ref[0, 2 * h + 1 : 2 * h + 2, lanes]
                probs = jnp.exp(scores - top) * share
                grad_probs = right_product(values, grad)
                weighted = jnp.sum(probs * grad_probs, axis=0, keepdims=True)
                rounded = (probs * (grad_probs - weighted)).astype(LOWER)
                strips.append(product(keys_t[cols], rounded))
                grad_keys += product(rounded, query)
                grad_values += product(probs.astype(LOWER), grad)
                spread = rounded.astype(WIDER)
                for c in range(STRIP // EDGE):
                    for j in range(SLOT // EDGE):
                        d = min(max(j - i - c, -2), 2)
                        block = spread[EDGE * j : EDGE * j + EDGE, EDGE * c : EDGE * c + EDGE]
                        sums[d] = sums[d] + block if d in sums else block
            grad_queries.append(jnp.concatenate(strips, axis=1))
            gh_ref[1, :, cols] = (grad_keys * 0.125).astype(LOWER)
            gh_ref[2, :, cols] = grad_values.astype(LOWER)
            empty = jnp.zeros((EDGE, SPAN - EDGE), WIDER)
            band = jnp.concatenate([sums[-1], sums[0], sums[1]], axis=1)
            upper = band.astype(LOWER)
            lower = (band - upper.astype(WIDER)).astype(LOWER)
            mirrored = product(mirror, upper) + product(mirror, lower)
            for d in range(3):
                spread = jnp.concatenate([mirrored[:, EDGE * d : EDGE * d + EDGE], empty], axis=1)
                turned = pltpu.roll(spread, 0, 1, stride=1, stride_axis=0)
                gb_ref[0, h : h + 1, SPAN * d : SPAN * d + SPAN] = jnp.sum(turned, axis=0, keepdims=True)
            for place, d in ((3 * SPAN, -2), (3 * SPAN + EDGE, 2)):
                gb_ref[0, h : h + 1, place : place + EDGE] = jnp.sum(sums[d], axis=0, keepdims=True)
        gh_ref[0] = (jnp.transpose(jnp.concatenate(grad_queries, axis=0)) * 0.125).astype(LOWER)

    return body


def columns_at(first):
    return pl.BlockSpec((SLOT, PAIR), lambda s: (0, first + s))


def stats_at(first):
    return pl.BlockSpec((1, 4, SLOT), lambda s: (first + s, 0, 0))


def attention(count, table, pick, heads, after=()):
    return run(
        "enc_attention",
        attn_fwd_kernel,
        [count, table, table, pick, heads, heads, heads],
        [SCALARS, SCALARS, WHOLE, WHOLE, columns_at(0), columns_at(PAIRS), columns_at(2 * PAIRS)],
        [narrow(SLOT, D), wide(PAIRS, 4, SLOT)],
        [columns_at(0), stats_at(0)],
        after=after,
        grid=(PAIRS,),
        scratch=[pltpu.VMEM((H, 3 * SPAN), WIDER)],
        flops=2 * 2 * H * SLOT * SLOT * HD * 4,
        exps=H * SLOT * SLOT,
    )


def attention_back(count, table, pick, heads, grad_mixed, stats, base, after=()):
    half = PAIRS // 2
    return run(
        "enc_attention_back",
        attn_bwd_kernel(base),
        [count, table, table, pick, heads, heads, heads, grad_mixed, stats],
        [SCALARS, SCALARS, WHOLE, WHOLE]
        + [columns_at(base), columns_at(PAIRS + base), columns_at(2 * PAIRS + base), columns_at(base), stats_at(base)],
        [narrow(3, SLOT, HALF), wide(half, 8, 4 * SPAN)],
        [pl.BlockSpec((3, SLOT, PAIR), lambda s: (0, 0, s)), pl.BlockSpec((1, 8, 4 * SPAN), lambda s: (s, 0, 0))],
        after=after,
        grid=(half,),
        scratch=[pltpu.VMEM((H, 3 * SPAN), WIDER)],
        flops=2 * 5 * H * SLOT * SLOT * HD * 2,
        exps=H * SLOT * SLOT // 2,
    )


def ffn_kernel(
    x_ref, mixed_ref, wo_ref, g2_ref, in_ref, out_ref, g3_ref, kv_any,
    after_ref, second_ref, slope_ref, hidden_ref, final_ref, third_ref, pairs_ref,
    kv_ref, sems,
):
    step = pl.program_id(0)
    copy = pltpu.make_async_copy(kv_any, kv_ref, sems.at[0])

    @pl.when(step == 0)
    def _():
        copy.start()
        after = x_ref[...].astype(WIDER) + product(mixed_ref[...], wo_ref[...])
        after_ref[...] = after
        final_ref[...] = after
        second_ref[...] = (after * scale_of(after) * row_of(g2_ref)).astype(LOWER)

    value, slope = silu_like(product(second_ref[...], in_ref[...]))
    slope_ref[...] = slope.astype(LOWER)
    hidden = value.astype(LOWER)
    hidden_ref[...] = hidden
    final_ref[...] += product(hidden, out_ref[...])

    @pl.when(step == STEPS - 1)
    def _():
        final = final_ref[...]
        third = (final * scale_of(final) * row_of(g3_ref)).astype(LOWER)
        third_ref[...] = third
        copy.wait()
        pairs_ref[...] = product(third, kv_ref[...]).astype(LOWER)


def whole(*shape):
    return pl.BlockSpec(shape, lambda s: (0,) * len(shape))


def feed_forward(x, mixed, wo, gain2, ffn_in, ffn_out, gain3, kv):
    rows = whole(SLOT, D)
    by_columns = pl.BlockSpec((SLOT, WIDTH), lambda s: (0, s))
    return run(
        "enc_ffn",
        ffn_kernel,
        [x, mixed, wo, gain2, ffn_in, ffn_out, gain3, kv],
        [rows, rows, whole(D, D), whole(D), pl.BlockSpec((D, WIDTH), lambda s: (0, s))]
        + [pl.BlockSpec((WIDTH, D), lambda s: (s, 0)), whole(D), ANY],
        [wide(SLOT, D), narrow(SLOT, D), narrow(SLOT, FF), narrow(SLOT, FF), wide(SLOT, D), narrow(SLOT, D), narrow(SLOT, 2 * D)],
        [rows, rows, by_columns, by_columns, rows, rows, whole(SLOT, 2 * D)],
        grid=(STEPS,),
        scratch=[pltpu.VMEM((D, 2 * D), LOWER), pltpu.SemaphoreType.DMA((1,))],
        flops=2 * SLOT * D * (D + 2 * FF + 2 * D),
        exps=SLOT * FF,
    )


def kv_back_kernel(gp_ref, kv_ref, final_ref, g3_ref, gfinal_ref, branch_ref, gain_ref):
    back, gain = norm_pull(final_ref[...], row_of(g3_ref), right_product(gp_ref[...], kv_ref[...]))
    gfinal_ref[...] = back
    branch_ref[...] = back.astype(LOWER)
    gain_ref[...] = gain


def kv_back(g_pairs, kv, final, gain3, after=()):
    return run(
        "enc_kv_back",
        kv_back_kernel,
        [g_pairs, kv, final, gain3],
        [WHOLE] * 4,
        [wide(SLOT, D), narrow(SLOT, D), wide(1, D)],
        after=after,
        flops=4 * SLOT * D * D,
    )


def ffn_back_kernel(
    branch_ref, out_ref, slope_ref, in_ref, after_ref, g2_ref, gfinal_ref, wo_any,
    ginner_ref, gafter_ref, low_ref, gmixed_ref, gain_ref,
    total_ref, wo_ref, sems,
):
    step = pl.program_id(0)
    copy = pltpu.make_async_copy(wo_any, wo_ref, sems.at[0])

    @pl.when(step == 0)
    def _():
        copy.start()
        total_ref[...] = jnp.zeros((SLOT, D), WIDER)

    grad = right_product(branch_ref[...], out_ref[...])
    inner = (grad * slope_ref[...].astype(WIDER)).astype(LOWER)
    ginner_ref[...] = inner
    total_ref[...] += right_product(inner, in_ref[...])

    @pl.when(step == STEPS - 1)
    def _():
        back, gain = norm_pull(after_ref[...], row_of(g2_ref), total_ref[...])
        gain_ref[...] = gain
        g_after = gfinal_ref[...] + back
        gafter_ref[...] = g_after
        low = g_after.astype(LOWER)
        low_ref[...] = low
        copy.wait()
        gmixed_ref[...] = right_product(low, wo_ref[...]).astype(LOWER)


def ffn_back(branch, ffn_out, slope, ffn_in, after_rows, gain2, g_final, wo, after=()):
    rows = whole(SLOT, D)
    by_columns = pl.BlockSpec((SLOT, WIDTH), lambda s: (0, s))
    return run(
        "enc_ffn_back",
        ffn_back_kernel,
        [branch, ffn_out, slope, ffn_in, after_rows, gain2, g_final, wo],
        [rows, pl.BlockSpec((WIDTH, D), lambda s: (s, 0)), by_columns, pl.BlockSpec((D, WIDTH), lambda s: (0, s))]
        + [rows, whole(D), rows, ANY],
        [narrow(SLOT, FF), wide(SLOT, D), narrow(SLOT, D), narrow(SLOT, D), wide(1, D)],
        [by_columns, rows, rows, rows, whole(1, D)],
        after=after,
        grid=(STEPS,),
        scratch=[pltpu.VMEM((SLOT, D), WIDER), pltpu.VMEM((D, D), LOWER), pltpu.SemaphoreType.DMA((1,))],
        flops=2 * SLOT * D * (D + 2 * FF),
    )


def rows_back_kernel(
    ga_ref, gb_ref, w_ref, x_ref, g1_ref, gafter_ref, gain2_ref, gain3_ref, da_ref, db_ref, pick_ref,
    grows_ref, small_ref, total_ref,
):
    step = pl.program_id(0)

    @pl.when(step == 0)
    def _():
        total_ref[...] = jnp.zeros((SLOT, D), WIDER)

    total_ref[...] += right_product(ga_ref[0], w_ref[:, :HALF]) + right_product(gb_ref[0], w_ref[:, HALF:])

    @pl.when(step == 2)
    def _():
        back, gain = norm_pull(x_ref[...].astype(WIDER), row_of(g1_ref), total_ref[...])
        grows_ref[...] = gafter_ref[...] + back
        sums = [ref[k, :2] for ref in (da_ref, db_ref) for k in range(PAIRS // 2)]
        table = split_product(jnp.concatenate(sums, axis=0), pick_ref[...], 2)
        small_ref[...] = jnp.zeros((16, D), WIDER)
        small_ref[0:1] = gain
        small_ref[1:2] = gain2_ref[...]
        small_ref[2:3] = gain3_ref[...]
        small_ref[4:16, :STAT] = table


def rows_back(grads, qkv, x, gain1, g_after, gain2, gain3, diagonals, pick_back, after=()):
    rows = whole(SLOT, D)
    by_kind = pl.BlockSpec((1, SLOT, HALF), lambda s: (s, 0, 0))
    diagonal = whole(PAIRS // 2, 8, 4 * SPAN)
    return run(
        "enc_rows_back",
        rows_back_kernel,
        [grads[0], grads[1], qkv, x, gain1, g_after, gain2, gain3, diagonals[0], diagonals[1], pick_back],
        [by_kind, by_kind, pl.BlockSpec((D, D), lambda s: (0, s)), rows, whole(D), rows, whole(1, D), whole(1, D)]
        + [diagonal, diagonal, whole(4 * SPAN, STAT)],
        [wide(SLOT, D), wide(16, D)],
        [rows, whole(16, D)],
        after=after,
        grid=(3,),
        scratch=[pltpu.VMEM((SLOT, D), WIDER)],
        flops=2 * SLOT * D * 3 * D,
    )


def head_lanes(h):
    lanes = lax.broadcasted_iota(jnp.int32, (GROUP, D), 1)
    return (lanes >= h * HD) & (lanes < (h + 1) * HD)


def stack_heads(flat):
    return jnp.concatenate([jnp.where(head_lanes(h), flat, 0.0) for h in range(H)], axis=0)


def merge_heads(stacked):
    total = jnp.zeros((GROUP, D), WIDER)
    for h in range(H):
        total = total + jnp.where(head_lanes(h), stacked[GROUP * h : GROUP * h + GROUP], 0.0)
    return total


def lanes_to_column(stat):
    lanes = lax.broadcasted_iota(jnp.int32, (GROUP, STAT), 1)
    parts = [jnp.sum(jnp.where(lanes == h, stat, 0.0), axis=1, keepdims=True) for h in range(H)]
    return jnp.concatenate(parts, axis=0)


def column_to_lanes(column, first):
    lanes = lax.broadcasted_iota(jnp.int32, (GROUP, STAT), 1)
    total = jnp.zeros((GROUP, STAT), WIDER)
    for h in range(H):
        total = total + jnp.where(lanes == first + h, column[GROUP * h : GROUP * h + GROUP], 0.0)
    return total


def spread_heads(stat):
    rows = lax.broadcasted_iota(jnp.int32, (STAT, D), 0) * HD
    lanes = lax.broadcasted_iota(jnp.int32, (STAT, D), 1)
    spread = jnp.where((lanes >= rows) & (lanes < rows + HD), 1.0, 0.0).astype(LOWER)
    return split_product(stat, spread, 2)


def own_scores(query, keys, table_ref):
    raw = right_product(query, keys)
    rows = lax.broadcasted_iota(jnp.int32, (GROUP, GROUP), 0)
    columns = lax.broadcasted_iota(jnp.int32, (GROUP, GROUP), 1)
    away = rows - columns
    parts = []
    for h in range(H):
        bias = jnp.full((GROUP, GROUP), table_ref[h, 0], WIDER)
        for d in range(1, GROUP):
            bias = jnp.where(away == d, table_ref[h, d], bias)
        part = raw[GROUP * h : GROUP * h + GROUP] + bias
        parts.append(jnp.where(away >= 0, part, MASKED))
    scores = jnp.concatenate(parts, axis=0)
    powers = jnp.exp(scores - jnp.max(scores, axis=1, keepdims=True))
    return powers / jnp.sum(powers, axis=1, keepdims=True)


def padded(ref, pad_ref):
    pad_ref[...] = jnp.zeros((GROUP, D), WIDER)
    pad_ref[:ANS] = ref[...].astype(WIDER)
    return pad_ref[...]


def answer_rows(width):
    return lax.broadcasted_iota(jnp.int32, (GROUP, width), 0) < ANS


def dec_self_kernel(
    table_ref, x_ref, g1_ref, g2_ref, qkv_any, out_any, query_any,
    after_ref, lefts_ref, heads_ref, query_ref,
    qkv_ref, out_ref, cross_ref, pad_ref, sems,
):
    copies = fetch(((qkv_any, qkv_ref), (out_any, out_ref), (query_any, cross_ref)), sems)
    start = padded(x_ref, pad_ref)
    first = (start * scale_of(start) * row_of(g1_ref)).astype(LOWER)
    copies[0].wait()
    heads = product(first, qkv_ref[...]).astype(LOWER)
    heads_ref[...] = heads
    query = stack_heads(heads.astype(WIDER)[:, :D] * 0.125).astype(LOWER)
    probs = own_scores(query, heads[:, D : 2 * D], table_ref)
    own = merge_heads(product(probs.astype(LOWER), heads[:, 2 * D :]))
    own = jnp.where(answer_rows(D), own, 0.0).astype(LOWER)
    copies[1].wait()
    after = start + product(own, out_ref[...])
    after_ref[...] = after
    second = (after * scale_of(after) * row_of(g2_ref)).astype(LOWER)
    copies[2].wait()
    query_ref[...] = product(second, cross_ref[...]).astype(LOWER)
    lefts_ref[:, :D] = first
    lefts_ref[:, D : 2 * D] = own
    lefts_ref[:, 2 * D :] = second


def masked_cross(n_ref, query_ref, pairs_ref):
    query = stack_heads(query_ref[...].astype(WIDER) * 0.125).astype(LOWER)
    raw = right_product(query, pairs_ref[:, :D])
    places = lax.broadcasted_iota(jnp.int32, (STACK, SLOT), 1)
    return query, jnp.where(places < n_ref[0], raw, MASKED)


def cross_kernel(n_ref, query_ref, pairs_ref, packed_ref):
    unused, scores = masked_cross(n_ref, query_ref, pairs_ref)
    top = jnp.max(scores, axis=1, keepdims=True)
    powers = jnp.exp(scores - top)
    total = jnp.sum(powers, axis=1, keepdims=True)
    probs = (powers / total).astype(LOWER)
    packed_ref[:, :D] = merge_heads(product(probs, pairs_ref[:, D:]))
    packed_ref[:, D:] = column_to_lanes(top, 0) + column_to_lanes(total, STAT // 2)


def dec_mid_kernel(
    parts_ref, after_ref, cot_ref, g3_ref, lefts_ref, cross_any, in_any, out_any,
    answer_ref, early_ref, mix_ref, gmix_ref, gmid_ref, stat_ref, gain_ref,
    cross_ref, in_ref, out_ref, pad_ref, sems,
):
    copies = fetch(((cross_any, cross_ref), (in_any, in_ref), (out_any, out_ref)), sems)
    size = parts_ref.shape[0]
    used = lax.broadcasted_iota(jnp.int32, (GROUP, STAT), 1) < H
    tops = [parts_ref[k, :, D:] for k in range(size)]
    totals = [pltpu.roll(stat, STAT // 2, 1) for stat in tops]
    top = tops[0]
    for k in range(1, size):
        top = jnp.maximum(top, tops[k])
    weights = [jnp.where(used, totals[k] * jnp.exp(tops[k] - top), 0.0) for k in range(size)]
    total = weights[0]
    for k in range(1, size):
        total = total + weights[k]
    total = jnp.where(used, total, 1.0)
    mix = jnp.zeros((GROUP, D), WIDER)
    for k in range(size):
        mix = mix + parts_ref[k, :, :D] * spread_heads(weights[k] / total)
    mix_ref[...] = mix
    stat_ref[:, :STAT] = jnp.where(used, top, 0.0)
    stat_ref[:, STAT:] = total
    mix_low = mix.astype(LOWER)
    copies[0].wait()
    middle = after_ref[...] + product(mix_low, cross_ref[...])
    third = (middle * scale_of(middle) * row_of(g3_ref)).astype(LOWER)
    copies[1].wait()
    inner = product(third, in_ref[...])
    value, slope = silu_like(inner)
    hidden = value.astype(LOWER)
    copies[2].wait()
    answer = (middle + product(hidden, out_ref[...])).astype(LOWER)
    answer_ref[...] = answer[:ANS]
    grad = padded(cot_ref, pad_ref)
    out_low = grad.astype(LOWER)
    g_inner = (right_product(out_low, out_ref[...]) * slope).astype(LOWER)
    back, gain = norm_pull(middle, row_of(g3_ref), right_product(g_inner, in_ref[...]))
    gain_ref[...] = gain
    g_middle = grad + back
    gmid_ref[...] = g_middle
    middle_low = g_middle.astype(LOWER)
    gmix_ref[...] = right_product(middle_low, cross_ref[...]).astype(LOWER)

    def store(name, rows):
        early_ref[:, AT[name] : AT[name] + rows.shape[1]] = rows

    def kept(rows):
        return jnp.where(answer_rows(rows.shape[1]), rows.astype(WIDER), 0.0).astype(LOWER)

    early_ref[:, : 3 * D] = kept(lefts_ref[...])
    store("mix", kept(mix_low))
    store("third", kept(third))
    store("hidden", kept(hidden))
    store("g_middle", middle_low)
    store("g_inner", g_inner)
    store("g_out", out_low)


def cross_back_kernel(n_ref, query_ref, pairs_ref, gmix_ref, mix_ref, stat_ref, gpairs_ref, partial_ref):
    query, scores = masked_cross(n_ref, query_ref, pairs_ref)
    top = lanes_to_column(stat_ref[:, :STAT])
    total = lanes_to_column(stat_ref[:, STAT:])
    probs = jnp.exp(scores - top) / total
    grad = stack_heads(gmix_ref[...].astype(WIDER))
    weighted = jnp.sum(grad * jnp.concatenate([mix_ref[...]] * H, axis=0), axis=1, keepdims=True)
    grad = grad.astype(LOWER)
    grad_probs = right_product(grad, pairs_ref[:, D:])
    rounded = (probs * (grad_probs - weighted)).astype(LOWER)
    gpairs_ref[:, :D] = left_product(rounded, query).astype(LOWER)
    gpairs_ref[:, D:] = left_product(probs.astype(LOWER), grad).astype(LOWER)
    partial_ref[...] = merge_heads(product(rounded, pairs_ref[:, :D])) * 0.125


def dec_back_kernel(
    table_ref, x_ref, gquery_ref, after_ref, gmid_ref, heads_ref,
    g1_ref, g2_ref, gain3_ref, query_any, out_any, qkv_any,
    late_ref, gstart_ref,
    cross_ref, out_ref, qkv_ref, pad_ref, sems,
):
    copies = fetch(((query_any, cross_ref), (out_any, out_ref), (qkv_any, qkv_ref)), sems)
    g_query = gquery_ref[...].astype(LOWER)
    copies[0].wait()
    back, gain2 = norm_pull(after_ref[...], row_of(g2_ref), right_product(g_query, cross_ref[...]))
    g_after = gmid_ref[...] + back
    after_low = g_after.astype(LOWER)
    copies[1].wait()
    g_own = stack_heads(right_product(after_low, out_ref[...])).astype(LOWER)
    heads = heads_ref[...]
    query = stack_heads(heads.astype(WIDER)[:, :D] * 0.125).astype(LOWER)
    probs = own_scores(query, heads[:, D : 2 * D], table_ref)
    grad_probs = right_product(g_own, heads[:, 2 * D :])
    rounded = (probs * (grad_probs - jnp.sum(probs * grad_probs, axis=1, keepdims=True))).astype(LOWER)
    g_q = (merge_heads(product(rounded, heads[:, D : 2 * D])) * 0.125).astype(LOWER)
    g_k = left_product(rounded, query).astype(LOWER)
    g_v = left_product(probs.astype(LOWER), g_own).astype(LOWER)
    g_heads = jnp.concatenate([g_q, g_k, g_v], axis=1)
    copies[2].wait()
    start = padded(x_ref, pad_ref)
    back, gain1 = norm_pull(start, row_of(g1_ref), right_product(g_heads, qkv_ref[...]))
    gstart_ref[...] = (g_after + back)[:ANS]
    spread = rounded.astype(WIDER)
    rows = lax.broadcasted_iota(jnp.int32, (GROUP, GROUP), 0)
    columns = lax.broadcasted_iota(jnp.int32, (GROUP, GROUP), 1)
    mirror = jnp.where(rows + columns == GROUP - 1, 1.0, 0.0).astype(LOWER)
    empty = jnp.zeros((GROUP, STAT - GROUP), WIDER)
    tables = []
    for h in range(H):
        part = product(mirror, spread[GROUP * h : GROUP * h + GROUP].astype(LOWER))
        turned = pltpu.roll(jnp.concatenate([part, empty], axis=1), 0, 1, stride=1, stride_axis=0)
        tables.append(jnp.sum(turned, axis=0, keepdims=True))
    small = jnp.concatenate([gain1, gain2, gain3_ref[...]] + tables, axis=1)
    places = lax.broadcasted_iota(jnp.int32, (GROUP, LATE), 0)
    late = jnp.concatenate([g_heads, after_low, g_query], axis=1).astype(WIDER)
    late_ref[...] = jnp.where(places == ANS, small, late).astype(LOWER)


def dec_outer_kernel(size):
    part = D // size

    def body(me_ref, early_ref, late_ref, qkv_ref, out_ref, query_ref, cross_ref, in_ref, ffn_ref, small_ref):
        me = me_ref[0]
        rows = lax.broadcasted_iota(jnp.int32, (part, D), 0) + me * part
        lanes = lax.broadcasted_iota(jnp.int32, (part, D), 1)
        picked = jnp.where(rows == lanes, 1.0, 0.0).astype(LOWER)

        def outer(name, right):
            left = right_product(picked, early_ref[:, AT[name] : AT[name] + D]).astype(LOWER)
            return product(left, right)

        qkv_ref[...] = outer("first", late_ref[:, : 3 * D])
        out_ref[...] = outer("own", late_ref[:, AT["g_after"] : AT["g_after"] + D])
        query_ref[...] = outer("second", late_ref[:, AT["g_query"] : AT["g_query"] + D])
        cross_ref[...] = outer("mix", early_ref[:, AT["g_middle"] : AT["g_middle"] + D])
        in_ref[...] = outer("third", early_ref[:, AT["g_inner"] : AT["g_inner"] + FF])
        height = FF // size
        first = pl.multiple_of(AT["hidden"] + me * height, 128)
        ffn_ref[...] = left_product(early_ref[:, pl.ds(first, height)], early_ref[:, AT["g_out"] : AT["g_out"] + D])
        total = jnp.zeros((1, LATE), WIDER)
        for k in range(size):
            total = total + late_ref[GROUP * k : GROUP * k + GROUP].astype(WIDER)[ANS : ANS + 1]
        small_ref[...] = total

    return body


def held(*shapes):
    return [pltpu.VMEM(shape, LOWER) for shape in shapes] + [
        pltpu.VMEM((GROUP, D), WIDER),
        pltpu.SemaphoreType.DMA((len(shapes),)),
    ]


def dec_self(table, answers, gain1, gain2, qkv, out, query, after=()):
    return run(
        "dec_self",
        dec_self_kernel,
        [table, answers, gain1, gain2, qkv, out, query],
        [SCALARS] + [WHOLE] * 3 + [ANY] * 3,
        [wide(GROUP, D), narrow(GROUP, 3 * D), narrow(GROUP, 3 * D), narrow(GROUP, D)],
        after=after,
        scratch=held((D, 3 * D), (D, D), (D, D)),
        flops=10**9,
    )


def cross(count, query, pairs, after=()):
    return run(
        "cross",
        cross_kernel,
        [count, query, pairs],
        [SCALARS, WHOLE, WHOLE],
        [wide(GROUP, D + STAT)],
        after=after,
        flops=4 * STACK * SLOT * D,
        exps=STACK * SLOT,
    )


def dec_mid(parts, after_rows, cotangent, gain3, lefts, cross_out, ffn_in, ffn_out, after=()):
    return run(
        "dec_mid",
        dec_mid_kernel,
        [parts, after_rows, cotangent, gain3, lefts, cross_out, ffn_in, ffn_out],
        [WHOLE] * 5 + [ANY] * 3,
        [narrow(ANS, D), narrow(GROUP, EARLY), wide(GROUP, D), narrow(GROUP, D), wide(GROUP, D), wide(GROUP, 2 * STAT), wide(1, D)],
        after=after,
        scratch=held((D, D), (D, FF), (FF, D)),
        flops=4 * 10**9,
    )


def cross_back(count, query, pairs, g_mix, mix, stat, after=()):
    return run(
        "cross_back",
        cross_back_kernel,
        [count, query, pairs, g_mix, mix, stat],
        [SCALARS] + [WHOLE] * 5,
        [narrow(SLOT, 2 * D), wide(GROUP, D)],
        after=after,
        flops=10 * STACK * SLOT * D,
        exps=STACK * SLOT,
    )


def dec_back(table, answers, g_query, after_rows, g_middle, heads, gain1, gain2, g_gain3, query, out, qkv, after=()):
    return run(
        "dec_back",
        dec_back_kernel,
        [table, answers, g_query, after_rows, g_middle, heads, gain1, gain2, g_gain3, query, out, qkv],
        [SCALARS] + [WHOLE] * 8 + [ANY] * 3,
        [narrow(GROUP, LATE), wide(ANS, D)],
        after=after,
        scratch=held((D, D), (D, D), (D, 3 * D)),
        flops=10**9,
    )


def dec_outer(me, early, late, size, after=()):
    part = D // size
    return run(
        "dec_outer",
        dec_outer_kernel(size),
        [me, early, late],
        [SCALARS, WHOLE, WHOLE],
        [wide(part, 3 * D), wide(part, D), wide(part, D), wide(part, D), wide(part, FF), wide(FF // size, D), wide(1, LATE)],
        after=after,
        flops=10**9,
    )


PLACES = [(0, 0), (0, 1), (1, 0), (1, 1)]


def place_of(me, there):
    return me ^ (4 * there[0] + 2 * there[1])


def turned_rows(me, acts, block):
    lanes = lax.broadcasted_iota(jnp.int32, (block, D), 1)
    rows = lax.broadcasted_iota(jnp.int32, (block, D), 0)
    picked = [jnp.where(lanes - rows == place_of(me, t) * block, 1.0, 0.0).astype(LOWER) for t in PLACES]
    picked = jnp.concatenate(picked, axis=0)
    return jnp.concatenate([right_product(picked, act).astype(LOWER) for act in acts], axis=1)


def target(there, x_refs, y_refs):
    dy, dx = there
    return (x_refs[dx].at[dy], y_refs[dy].at[dx])


def one_kernel(me_ref, t_own, t_par, p_own, p_par, h_own, h_par, b_own, b_par, xk, xs, yk, ys, t, p, h, b, sems):
    me = me_ref[0]
    block = FF // 8
    pairs = [(t_own, t.at[0]), (t_par, t.at[1]), (p_own, p.at[:SLOT]), (p_par, p.at[SLOT:])]
    pairs += [(b_own, b.at[:SLOT]), (b_par, b.at[SLOT:])]
    for k, there in enumerate(PLACES):
        lanes = pl.ds(pl.multiple_of(place_of(me, there) * block, 128), block)
        pairs += [(h_own.at[:, lanes], h.at[k, :SLOT]), (h_par.at[:, lanes], h.at[k, SLOT:])]
    copies = fetch(pairs, sems)
    copies[0].wait()
    copies[1].wait()
    height = D // 8
    left = turned_rows(me, (t[0], t[1]), height)
    copies[2].wait()
    copies[3].wait()
    for c in range(2):
        grad = product(left, p[:, D * c : D * c + D]).astype(LOWER)
        for k, there in enumerate(PLACES):
            to, unused = target(there, (xk, xs), (yk, ys))
            to[height * c : height * c + height] = grad[height * k : height * k + height]
    copies[4].wait()
    copies[5].wait()
    for k, there in enumerate(PLACES):
        copies[6 + 2 * k].wait()
        copies[7 + 2 * k].wait()
        grad = left_product(h[k], b[...]).astype(LOWER)
        to_x, to_y = target(there, (xk, xs), (yk, ys))
        to_x[2 * height : 3 * height] = grad[:height]
        to_y[...] = grad[height:]


def two_kernel(me_ref, s_own, s_par, i_own, i_par, m_own, m_par, l_own, l_par, xk, xs, yk, ys, s, i, m, l, sems):
    me = me_ref[0]
    pairs = [(s_own, s.at[0]), (s_par, s.at[1])]
    for c in range(4):
        lanes = slice(D * c, D * c + D)
        pairs += [(i_own.at[:, lanes], i.at[c, :SLOT]), (i_par.at[:, lanes], i.at[c, SLOT:])]
    pairs += [(m_own, m.at[0]), (m_par, m.at[1]), (l_own, l.at[:SLOT]), (l_par, l.at[SLOT:])]
    copies = fetch(pairs, sems)
    copies[0].wait()
    copies[1].wait()
    height = D // 8
    half = height // 2
    left = turned_rows(me, (s[0], s[1]), height)
    for c in range(4):
        copies[2 + 2 * c].wait()
        copies[3 + 2 * c].wait()
        grad = product(left, i[c]).astype(LOWER)
        for k, there in enumerate(PLACES):
            to = target(there, (xk, xs), (yk, ys))[c // 2]
            to[height * (c % 2) : height * (c % 2) + height] = grad[height * k : height * k + height]
    for k in range(10, 14):
        copies[k].wait()
    left = turned_rows(me, (m[0], m[1]), height)
    grad = product(left, l[...]).astype(LOWER)
    for k, there in enumerate(PLACES):
        for to, first in zip(target(there, (xk, xs), (yk, ys)), (0, half)):
            to[2 * height : 2 * height + half] = grad[height * k + first : height * k + first + half]


def three_kernel(x_first):
    def body(me_ref, f_own, f_par, g_own, g_par, keep, send, f, g, sems):
        me = me_ref[0]
        pairs = [(f_own, f.at[0]), (f_par, f.at[1])]
        for c in range(3):
            pairs += [(g_own.at[c], g.at[c, :SLOT]), (g_par.at[c], g.at[c, SLOT:])]
        copies = fetch(pairs, sems)
        copies[0].wait()
        copies[1].wait()
        height = D // 8
        left = turned_rows(me, (f[0], f[1]), height)
        for c in range(3):
            copies[2 + 2 * c].wait()
            copies[3 + 2 * c].wait()
            grad = product(left, g[c]).astype(LOWER)
            for k, there in enumerate(PLACES):
                to = target(there, (keep, send), (keep, send))[0 if x_first else 1]
                to[:, HALF * c : HALF * c + HALF] = grad[height * k : height * k + height]

    return body


def weights_one(me, third, g_pairs, hidden, branch, after=()):
    out = narrow(2, 3 * D // 8, D)
    return run(
        "weights_one",
        one_kernel,
        [me, *third, *g_pairs, *hidden, *branch],
        [SCALARS] + [ANY] * 8,
        [out] * 4,
        after=after,
        scratch=[
            pltpu.VMEM((2, SLOT, D), LOWER),
            pltpu.VMEM((2 * SLOT, 2 * D), LOWER),
            pltpu.VMEM((4, 2 * SLOT, FF // 8), LOWER),
            pltpu.VMEM((2 * SLOT, D), LOWER),
            pltpu.SemaphoreType.DMA((14,)),
        ],
        flops=4 * 10**9,
    )


def weights_two(me, second, g_inner, mixed, low, after=()):
    out = narrow(2, 5 * D // 16, D)
    return run(
        "weights_two",
        two_kernel,
        [me, *second, *g_inner, *mixed, *low],
        [SCALARS] + [ANY] * 8,
        [out] * 4,
        after=after,
        scratch=[
            pltpu.VMEM((2, SLOT, D), LOWER),
            pltpu.VMEM((4, 2 * SLOT, D), LOWER),
            pltpu.VMEM((2, SLOT, D), LOWER),
            pltpu.VMEM((2 * SLOT, D), LOWER),
            pltpu.SemaphoreType.DMA((14,)),
        ],
        flops=4 * 10**9,
    )


def weights_three(me, first, grads, x_first, after=()):
    out = narrow(2, D // 8, 3 * HALF)
    return run(
        "weights_three",
        three_kernel(x_first),
        [me, *first, *grads],
        [SCALARS] + [ANY] * 4,
        [out] * 2,
        after=after,
        scratch=[
            pltpu.VMEM((2, SLOT, D), LOWER),
            pltpu.VMEM((3, 2 * SLOT, HALF), LOWER),
            pltpu.SemaphoreType.DMA((8,)),
        ],
        flops=2 * 10**9,
    )


def page(array, k):
    return pl.BlockSpec((1,) + array.shape[1:], lambda s: (k, 0, 0))


def add_first(parts, after=()):
    def body(*refs):
        for k in range(len(parts)):
            refs[2 * len(parts) + k][...] = (refs[2 * k][0].astype(WIDER) + refs[2 * k + 1][0].astype(WIDER)).astype(LOWER)

    flat = [a for pair in parts for a in pair]
    outs = [narrow(*keep.shape[1:]) for keep, unused in parts]
    return run("add_first", body, flat, [page(a, 1) for a in flat], outs, after=after, grid=(1,))


def add_second(parts, after=()):
    count = len(parts)
    heights = [keep.shape[1] for keep, unused, unused_too in parts]

    def body(*refs):
        for k in range(count):
            keep, got, last = refs[3 * k : 3 * k + 3]
            total = keep[0].astype(WIDER) + got[0].astype(WIDER) + last[...].astype(WIDER)
            first = sum(heights[:k])
            refs[3 * count][first : first + heights[k]] = total.astype(LOWER)

    flat = [a for trio in parts for a in trio]
    specs = [page(a, 0) if a.ndim == 3 else WHOLE for a in flat]
    return run("add_second", body, flat, specs, [narrow(sum(heights), parts[0][0].shape[2])], after=after, grid=(1,))


def add_pair(one, two, after=()):
    def body(one_ref, two_ref, out_ref):
        out_ref[...] = (one_ref[...].astype(WIDER) + two_ref[...].astype(WIDER)).astype(LOWER)

    return run("add_pair", body, [one, two], [WHOLE] * 2, [narrow(*one.shape)], after=after)


def partner(axis, bit):
    return [(k, k ^ (1 << bit)) for k in range(lax.axis_size(axis))]


def swap(value, axis, bit):
    return lax.ppermute(value, axis, partner(axis, bit))


def all_sum(value, axis):
    for bit in range(lax.axis_size(axis).bit_length() - 1):
        value = value + swap(value, axis, bit)
    return value


def pa_order(turn):
    rest = lax.axis_size("pa").bit_length() - 2
    return [1 + (k + turn) % rest for k in range(rest)]


def both_cores(acts, turn):
    size = lax.axis_size("pa")
    me = lax.axis_index("pa")
    blocks = jnp.transpose(acts).reshape(size, acts.shape[1] // size, acts.shape[0])
    order = pa_order(turn)
    offsets = [
        sum(((k >> (len(order) - 1 - p)) & 1) << bit for p, bit in enumerate(order)) for k in range(size // 2)
    ]
    mine = jnp.concatenate([lax.dynamic_slice_in_dim(blocks, me ^ d, 1) for d in offsets])
    theirs = jnp.concatenate([lax.dynamic_slice_in_dim(blocks, me ^ d ^ 1, 1) for d in offsets])
    return mine, swap(theirs, "pa", 0)


def weight_part(acts, grads, first, last):
    total = None
    for act, grad in zip(acts, grads):
        act = act[first:last]
        term = product(act.reshape(-1, act.shape[2]), grad)
        total = term if total is None else total + term
    height = acts[0].shape[1]
    return total.astype(LOWER).reshape(last - first, height, -1)


def add_up(parts):
    total = parts[0].astype(WIDER)
    for part in parts[1:]:
        total = total + part.astype(WIDER)
    return total.astype(LOWER)


def share_over_pa(acts, grads, turn):
    size = acts[0].shape[0]
    keep = [weight_part(acts, grads, 0, size // 2)]
    send = weight_part(acts, grads, size // 2, size)
    for bit in pa_order(turn):
        keep.append(swap(send, "pa", bit))
        size //= 2
        if size > 1:
            send = add_up([part[size // 2 : size] for part in keep])
            keep = [part[: size // 2] for part in keep]
    return add_up([part[0] for part in keep])


def total_over_pb(share, after=()):
    size = lax.axis_size("pb")
    if size != 4:
        return lax.psum(share, "pb")
    me = lax.axis_index("pb")
    share, token = add_pair(share, lax.ppermute(share, "pb", [(0, 1), (3, 2)]), after=after)
    share, token = add_pair(share, lax.ppermute(share, "pb", [(1, 2), (2, 1)]))
    got = lax.ppermute(share, "pb", [(1, 0), (2, 3)])
    return jnp.where((me == 1) | (me == 2), share, got)


def total_plain(share):
    return lax.psum(share, "pb").astype(WIDER)


def local(
    passages,
    lengths,
    answers,
    cotangent,
    enc_gain1,
    enc_qkv,
    enc_bias,
    enc_out,
    enc_gain2,
    enc_ffn_in,
    enc_ffn_out,
    enc_gain3,
    cross_kv,
    dec_gain1,
    dec_qkv,
    dec_bias,
    dec_out,
    dec_gain2,
    cross_query,
    cross_out,
    dec_gain3,
    dec_ffn_in,
    dec_ffn_out,
):
    pa_size = lax.axis_size("pa")
    pb_size = lax.axis_size("pb")
    fast = pa_size == 8
    me = lax.axis_index("pa").astype(jnp.int32).reshape(1)
    x = passages.reshape(SLOT, D)
    count = lengths.reshape(1)
    table = jnp.transpose(enc_bias)
    dec_table = jnp.transpose(dec_bias)
    pick = jnp.asarray(PICK, LOWER)
    pick_back = jnp.asarray(PICK_BACK, LOWER)

    def across(value):
        return value, swap(value, "pa", 0)

    rows = x.astype(WIDER)
    first = (rows * scale_of(rows) * enc_gain1).astype(LOWER)
    heads = product(first, enc_qkv).astype(LOWER)
    mixed, stats, token = attention(count, table, pick, heads)
    after, second, slope, hidden, final, third, pairs, token = feed_forward(
        x, mixed, enc_out, enc_gain2, enc_ffn_in, enc_ffn_out, enc_gain3, cross_kv
    )
    dec_after, lefts, dec_heads, query, token = dec_self(
        dec_table, answers[0], dec_gain1, dec_gain2, dec_qkv, dec_out, cross_query, after=[token]
    )
    packed, token = cross(count, query, pairs)
    if fast:
        acts = [across(value) for value in (first, mixed, second, hidden, third)]
    else:
        acts = [both_cores(v, k % 2) for k, v in enumerate((first, mixed, second, hidden, third))]
    gathered = lax.all_gather(packed, "pa")
    answer, early, mix, g_mix, g_middle, stat, g_gain3, token = dec_mid(
        gathered, dec_after, cotangent[0], dec_gain3, lefts, cross_out, dec_ffn_in, dec_ffn_out,
        after=[got for unused, got in acts[:4]],
    )
    g_pairs, partial_query, token = cross_back(count, query, pairs, g_mix, mix, stat)
    early_all = lax.all_gather(early, "pb")
    g_final, branch, g_enc_gain3, token = kv_back(g_pairs, cross_kv, final, enc_gain3)
    part = partial_query + swap(partial_query, "pa", 0)
    g_inner, g_after, low, g_mixed, g_enc_gain2, token = ffn_back(
        branch, enc_ffn_out, slope, enc_ffn_in, after, enc_gain2, g_final, enc_out
    )

    def back_of(base, after):
        return attention_back(count, table, pick, heads, g_mixed, stats, base, after=after)

    if fast:
        part = part + swap(part, "pa", 1)
        xk, xs, yk, ys, token = weights_one(me, acts[4], across(g_pairs), acts[3], across(branch), after=[token])
        one_x, one_y = swap(xs, "pa", 1), swap(ys, "pa", 2)
        one = ((xk, one_x), (yk, one_y))
        xk, xs, yk, ys, token = weights_two(me, acts[2], across(g_inner), acts[1], across(low), after=[token, part])
        two_x, two_y = swap(xs, "pa", 1), swap(ys, "pa", 2)
        two = ((xk, two_x), (yk, two_y))
        g_query = part + swap(part, "pa", 2)
        grads_a, diagonal_a, token = back_of(0, [token])
        send_x, send_y, token = add_first(one, after=[token])
        one_last = (swap(send_x, "pa", 2), swap(send_y, "pa", 1))
        grads_b, diagonal_b, token = back_of(PAIRS // 2, [token, g_query])
        there_a = swap(grads_a, "pa", 0)
        there_b = swap(grads_b, "pa", 0)
        send_x, send_y, token = add_first(two, after=[token])
        two_last = (swap(send_x, "pa", 2), swap(send_y, "pa", 1))
        late, g_start, token = dec_back(
            dec_table, answers[0], g_query, dec_after, g_middle, dec_heads,
            dec_gain1, dec_gain2, g_gain3, cross_query, dec_out, dec_qkv, after=[token],
        )
        keep_a, send_a, token = weights_three(me, acts[0], (grads_a, there_a), True, after=[token])
        got_a = swap(send_a, "pa", 1)
        share_one, token = add_second([one[0] + (one_last[0],), one[1] + (one_last[1],)], after=[token])
        keep_b, send_b, token = weights_three(me, acts[0], (grads_b, there_b), False, after=[token])
        got_b = swap(send_b, "pa", 2)
        g_rows, small, token = rows_back(
            (grads_a, grads_b), enc_qkv, x, enc_gain1, g_after, g_enc_gain2, g_enc_gain3,
            (diagonal_a, diagonal_b), pick_back, after=[token],
        )
        share_two, token = add_second([two[0] + (two_last[0],), two[1] + (two_last[1],)], after=[token])
        send_a, send_b, token = add_first([(keep_a, got_a), (keep_b, got_b)], after=[token])
        last_a, last_b = swap(send_a, "pa", 2), swap(send_b, "pa", 1)
        share_three, token = add_second([(keep_a, got_a, last_a), (keep_b, got_b, last_b)], after=[token])
        total_one = total_over_pb(share_one).astype(WIDER)
        total_two = total_over_pb(share_two).astype(WIDER)
        total_three = total_over_pb(share_three).astype(WIDER)
        block = D // pa_size
        total_kv = jnp.concatenate([total_one[:block], total_one[block : 2 * block]], axis=1)
        total_ffn_out = total_one[2 * block :]
        second_part = 2 * block + block // 2
        total_ffn_in = jnp.concatenate(
            [total_two[first : first + block] for first in (0, block, second_part, second_part + block)], axis=1
        )
        total_out = jnp.concatenate([total_two[2 * block : second_part], total_two[second_part + 2 * block :]], axis=0)
        total_qkv = jnp.concatenate(
            [total_three[block * (k % 2) : block * (k % 2) + block, HALF * (k // 2) : HALF * (k // 2) + HALF] for k in range(6)],
            axis=1,
        )
    else:
        g_query = all_sum(partial_query, "pa")
        grads_a, diagonal_a, token = back_of(0, [token])
        grads_b, diagonal_b, token = back_of(PAIRS // 2, [token])
        late, g_start, token = dec_back(
            dec_table, answers[0], g_query, dec_after, g_middle, dec_heads,
            dec_gain1, dec_gain2, g_gain3, cross_query, dec_out, dec_qkv, after=[token],
        )
        g_rows, small, token = rows_back(
            (grads_a, grads_b), enc_qkv, x, enc_gain1, g_after, g_enc_gain2, g_enc_gain3,
            (diagonal_a, diagonal_b), pick_back, after=[token],
        )
        g_heads = jnp.concatenate([g for k in range(3) for g in (grads_a[k], grads_b[k])], axis=1)
        total_kv = total_plain(share_over_pa(acts[4], across(g_pairs), 0))
        total_ffn_out = total_plain(share_over_pa(acts[3], across(branch), 1))
        total_ffn_in = total_plain(share_over_pa(acts[2], across(g_inner), 0))
        total_out = total_plain(share_over_pa(acts[1], across(low), 1))
        total_qkv = total_plain(share_over_pa(acts[0], across(g_heads), 0))

    small = all_sum(all_sum(small, "pa"), "pb")
    late_all = lax.all_gather(late, "pb")
    pb_me = lax.axis_index("pb").astype(jnp.int32).reshape(1)
    d_qkv, d_out, d_query, d_cross, d_in, d_ffn, dec_small, token = dec_outer(
        pb_me, early_all.reshape(pb_size * GROUP, EARLY), late_all.reshape(pb_size * GROUP, LATE), pb_size
    )
    dec_small = dec_small[0]
    dec_bias_rows = dec_small[3 * D :].reshape(H, STAT)[:, GROUP - ANS : GROUP]
    dec_bias_all = jnp.pad(jnp.transpose(dec_bias_rows[:, ::-1]), ((0, BUCKETS - ANS), (0, 0)))

    def own_part(vector, axis):
        height = vector.shape[0] // lax.axis_size(axis)
        return lax.dynamic_slice_in_dim(vector, lax.axis_index(axis) * height, height, axis=0)

    return (
        answer[None],
        g_rows.reshape(1, 1, SLOT, D),
        g_start[None],
        own_part(small[0], "pa"),
        total_qkv,
        jnp.transpose(small[4:16, :BUCKETS]),
        total_out,
        own_part(small[1], "pa"),
        total_ffn_in,
        total_ffn_out,
        own_part(small[2], "pa"),
        total_kv,
        own_part(dec_small[:D], "pb"),
        d_qkv,
        own_part(dec_bias_all, "pb"),
        d_out,
        own_part(dec_small[D : 2 * D], "pb"),
        d_query,
        d_cross,
        own_part(dec_small[2 * D : 3 * D], "pb"),
        d_in,
        d_ffn,
    )


def solution(mesh):
    copied = P()
    in_specs = (
        P("pb", "pa", None, None),
        P("pb", "pa"),
        P("pb", None, None),
        P("pb", None, None),
    ) + (copied,) * 19
    by_pa, by_pa_rows = P("pa"), P("pa", None)
    by_pb, by_pb_rows = P("pb"), P("pb", None)
    out_specs = (
        P("pb", None, None),
        P("pb", "pa", None, None),
        P("pb", None, None),
        by_pa,
        by_pa_rows,
        copied,
        by_pa_rows,
        by_pa,
        by_pa_rows,
        by_pa_rows,
        by_pa,
        by_pa_rows,
        by_pb,
        by_pb_rows,
        by_pb_rows,
        by_pb_rows,
        by_pb,
        by_pb_rows,
        by_pb_rows,
        by_pb,
        by_pb_rows,
        by_pb_rows,
    )
    return jax.shard_map(local, mesh=mesh, in_specs=in_specs, out_specs=out_specs, check_vma=False)
```

```python
import jax
import jax.numpy as jnp
import numpy as np
from jax import lax
from jax.experimental import pallas as pl
from jax.experimental.pallas import tpu as pltpu
from jax.sharding import PartitionSpec as P

D = 768
H = 12
HD = 64
FF = 3072
BUCKETS = 32
ANS = 20
SLOT = 512
PAIR = 2 * HD
PAIRS = H // 2
EDGE = 128
STRIP = 256
SPAN = 256
GROUP = 24
SENT = 40
STACK = H * GROUP
STAT = 128
STEPS = 4
WIDTH = FF // STEPS
FIRST = 4
WIDE_A = FIRST * PAIR
WIDE_B = D - WIDE_A
EPS = 1e-06
MASKED = -1000000000.0
C_GELU = 0.7978845608028654
LOWER = jnp.bfloat16
WIDER = jnp.float32
EARLY = 7 * D + 2 * FF
LATE = 5 * D
AT = {
    "first": 0,
    "own": D,
    "second": 2 * D,
    "mix": 3 * D,
    "third": 4 * D,
    "hidden": 5 * D,
    "g_middle": 5 * D + FF,
    "g_inner": 6 * D + FF,
    "g_out": 6 * D + 2 * FF,
    "g_heads": 0,
    "g_after": 3 * D,
    "g_query": 4 * D,
}


def tile_classes(away):
    rows = [np.clip(EDGE * d - away, -(BUCKETS // 2), BUCKETS // 2 - 1) + BUCKETS // 2 for d in (-1, 0, 1)]
    return np.eye(BUCKETS, dtype=np.float32)[np.concatenate(rows)]


LANES = np.arange(SPAN)
PICK = tile_classes(np.where(LANES < EDGE, LANES, LANES - SPAN)).T
ENDS = np.repeat(np.eye(BUCKETS, dtype=np.float32)[[0, BUCKETS - 1]], EDGE, axis=0)
PICK_BACK = np.pad(np.concatenate([tile_classes(LANES - (EDGE - 1)), ENDS]), ((0, 0), (0, STAT - BUCKETS)))

SCALARS = pl.BlockSpec(memory_space=pltpu.SMEM)
ANY = pl.BlockSpec(memory_space=pl.ANY)
WHOLE = pl.BlockSpec(memory_space=pltpu.VMEM)
TOKEN = (8, 128)


def wide(*shape):
    return jax.ShapeDtypeStruct(shape, WIDER)


def narrow(*shape):
    return jax.ShapeDtypeStruct(shape, LOWER)


def run(name, body, ins, in_specs, outs, out_specs=None, after=(), grid=(), scratch=(), flops=10**9, mib=24):
    count, extra, results = len(ins), len(after), len(outs)
    if out_specs is None:
        out_specs = [WHOLE] * results
    zeros = (lambda *s: (0, 0)) if grid else (lambda: (0, 0))

    def wrapped(*refs):
        refs[count + extra + results][...] = jnp.zeros(TOKEN, WIDER)
        body(*refs[:count], *refs[count + extra : count + extra + results], *refs[count + extra + results + 1 :])

    got = pl.pallas_call(
        wrapped,
        grid=grid,
        out_shape=tuple(outs) + (wide(*TOKEN),),
        in_specs=list(in_specs) + [ANY] * extra,
        out_specs=tuple(out_specs) + (pl.BlockSpec(TOKEN, zeros),),
        scratch_shapes=list(scratch),
        compiler_params=pltpu.CompilerParams(vmem_limit_bytes=mib * 2**20),
        cost_estimate=pl.CostEstimate(flops=10 * flops, bytes_accessed=1, transcendentals=0),
        name=name,
    )(*ins, *after)
    return got


def product(left, right):
    return jnp.dot(left, right, preferred_element_type=WIDER)


def left_product(left, right):
    return lax.dot_general(left, right, (((0,), (0,)), ((), ())), preferred_element_type=WIDER)


def right_product(left, right):
    return lax.dot_general(left, right, (((1,), (1,)), ((), ())), preferred_element_type=WIDER)


def split_product(left, right, terms):
    total = None
    for k in range(terms):
        part = left.astype(LOWER)
        left = left - part.astype(WIDER)
        term = product(part, right)
        total = term if total is None else total + term
    return total


def silu_like(inner):
    square = inner * inner
    tanh = jnp.tanh(inner * (C_GELU + (C_GELU * 0.044715) * square))
    half = 0.5 + 0.5 * tanh
    value = inner * half
    slope = half + value * (1.0 - tanh) * (C_GELU + (3.0 * C_GELU * 0.044715) * square)
    return value, slope


def row_of(ref):
    return ref[...].reshape(1, D)


def scale_of(values):
    return lax.rsqrt(jnp.mean(values * values, axis=-1, keepdims=True) + EPS)


def norm_pull(values, gain, grad):
    scale = scale_of(values)
    lifted = grad * gain
    inside = jnp.sum(values * lifted, axis=-1, keepdims=True)
    back = scale * lifted - values * (scale * scale * scale * inside * (1.0 / D))
    return back, jnp.sum(grad * values * scale, axis=0, keepdims=True)


def fetch(pairs, sems):
    copies = [pltpu.make_async_copy(s, t, sems.at[k]) for k, (s, t) in enumerate(pairs)]
    for copy in copies:
        copy.start()
    return copies


def bias_tiles(u_ref, head):
    tiles = []
    for d in range(3):
        row = u_ref[pl.ds(head, 1), SPAN * d : SPAN * d + SPAN]
        spread = jnp.broadcast_to(row, (EDGE, SPAN))
        tiles.append(pltpu.roll(spread, 0, 1, stride=1, stride_axis=0)[:, :EDGE])
    return tiles


def bias_strip(tiles, low, high, first):
    columns = []
    for i in range(first, first + STRIP // EDGE):
        blocks = []
        for j in range(SLOT // EDGE):
            d = j - i
            if abs(d) <= 1:
                blocks.append(tiles[d + 1])
            else:
                blocks.append(jnp.full((EDGE, EDGE), low if d < 0 else high, WIDER))
        columns.append(jnp.concatenate(blocks, axis=0))
    return jnp.concatenate(columns, axis=1)


def strip_scores(n, keys, query, bias):
    raw = right_product(keys, query) + bias
    places = lax.broadcasted_iota(jnp.int32, (SLOT, STRIP), 0)
    return jnp.where(places < n, raw, MASKED)


def fill_rows(table_ref, pick_ref, u_ref):
    @pl.when(pl.program_id(0) == 0)
    def _():
        u_ref[...] = split_product(table_ref[...], pick_ref[...], 3)


def attn_fwd_kernel(n_ref, ends_ref, table_ref, pick_ref, q_ref, k_ref, v_ref, o_ref, st_ref, u_ref):
    fill_rows(table_ref, pick_ref, u_ref)
    n = n_ref[0]
    step = pl.program_id(0)
    values = jnp.transpose(v_ref[...])
    mixed = []
    for h in range(2):
        head = 2 * step + h
        low, high = ends_ref[head, 0], ends_ref[head, BUCKETS - 1]
        tiles = bias_tiles(u_ref, head)
        cols = slice(HD * h, HD * h + HD)
        keys = k_ref[:, cols]
        strips = []
        for i in range(0, SLOT // EDGE, STRIP // EDGE):
            lanes = slice(EDGE * i, EDGE * i + STRIP)
            query = q_ref[lanes, cols] * 0.125
            scores = strip_scores(n, keys, query, bias_strip(tiles, low, high, i))
            top = jnp.max(scores, axis=0, keepdims=True)
            powers = jnp.exp(scores - top)
            share = 1.0 / jnp.sum(powers, axis=0, keepdims=True)
            st_ref[0, 2 * h : 2 * h + 1, lanes] = top
            st_ref[0, 2 * h + 1 : 2 * h + 2, lanes] = share
            probs = (powers * share).astype(LOWER)
            strips.append(product(values[cols], probs))
        mixed.append(jnp.concatenate(strips, axis=1))
    o_ref[...] = jnp.transpose(jnp.concatenate(mixed, axis=0)).astype(LOWER)


def attn_bwd_kernel(base):
    def body(
        n_ref, ends_ref, table_ref, pick_ref, q_ref, k_ref, v_ref, g_ref, st_ref, gh_ref, gb_ref, u_ref
    ):
        fill_rows(table_ref, pick_ref, u_ref)
        n = n_ref[0]
        step = pl.program_id(0) + base
        keys_t = jnp.transpose(k_ref[...])
        rows = lax.broadcasted_iota(jnp.int32, (EDGE, EDGE), 0)
        columns = lax.broadcasted_iota(jnp.int32, (EDGE, EDGE), 1)
        mirror = jnp.where(rows + columns == EDGE - 1, 1.0, 0.0).astype(LOWER)
        grad_queries = []
        gb_ref[0, 2:8, :] = jnp.zeros((6, 4 * SPAN), WIDER)
        for h in range(2):
            head = 2 * step + h
            low, high = ends_ref[head, 0], ends_ref[head, BUCKETS - 1]
            tiles = bias_tiles(u_ref, head)
            cols = slice(HD * h, HD * h + HD)
            keys = k_ref[:, cols]
            values = v_ref[:, cols]
            grad_keys = jnp.zeros((SLOT, HD), WIDER)
            grad_values = jnp.zeros((SLOT, HD), WIDER)
            strips = []
            sums = {}
            for i in range(0, SLOT // EDGE, STRIP // EDGE):
                lanes = slice(EDGE * i, EDGE * i + STRIP)
                query = q_ref[lanes, cols]
                grad = g_ref[lanes, cols]
                scores = strip_scores(n, keys, query * 0.125, bias_strip(tiles, low, high, i))
                top = st_ref[0, 2 * h : 2 * h + 1, lanes]
                share = st_ref[0, 2 * h + 1 : 2 * h + 2, lanes]
                probs = jnp.exp(scores - top) * share
                grad_probs = right_product(values, grad)
                weighted = jnp.sum(probs * grad_probs, axis=0, keepdims=True)
                rounded = (probs * (grad_probs - weighted)).astype(LOWER)
                strips.append(product(keys_t[cols], rounded))
                grad_keys += product(rounded, query)
                grad_values += product(probs.astype(LOWER), grad)
                spread = rounded.astype(WIDER)
                for c in range(STRIP // EDGE):
                    for j in range(SLOT // EDGE):
                        d = min(max(j - i - c, -2), 2)
                        block = spread[EDGE * j : EDGE * j + EDGE, EDGE * c : EDGE * c + EDGE]
                        sums[d] = sums[d] + block if d in sums else block
            grad_queries.append(jnp.concatenate(strips, axis=1))
            gh_ref[1, :, cols] = (grad_keys * 0.125).astype(LOWER)
            gh_ref[2, :, cols] = grad_values.astype(LOWER)
            empty = jnp.zeros((EDGE, SPAN - EDGE), WIDER)
            band = jnp.concatenate([sums[-1], sums[0], sums[1]], axis=1)
            upper = band.astype(LOWER)
            lower = (band - upper.astype(WIDER)).astype(LOWER)
            mirrored = product(mirror, upper) + product(mirror, lower)
            for d in range(3):
                spread = jnp.concatenate([mirrored[:, EDGE * d : EDGE * d + EDGE], empty], axis=1)
                turned = pltpu.roll(spread, 0, 1, stride=1, stride_axis=0)
                gb_ref[0, h : h + 1, SPAN * d : SPAN * d + SPAN] = jnp.sum(turned, axis=0, keepdims=True)
            for place, d in ((3 * SPAN, -2), (3 * SPAN + EDGE, 2)):
                gb_ref[0, h : h + 1, place : place + EDGE] = jnp.sum(sums[d], axis=0, keepdims=True)
        gh_ref[0] = (jnp.transpose(jnp.concatenate(grad_queries, axis=0)) * 0.125).astype(LOWER)

    return body


def columns_at(first):
    return pl.BlockSpec((SLOT, PAIR), lambda s: (0, first + s))


def stats_at(first):
    return pl.BlockSpec((1, 4, SLOT), lambda s: (first + s, 0, 0))


def attention(count, table, pick, heads, after=()):
    return run(
        "enc_attention",
        attn_fwd_kernel,
        [count, table, table, pick, heads, heads, heads],
        [SCALARS, SCALARS, WHOLE, WHOLE, columns_at(0), columns_at(PAIRS), columns_at(2 * PAIRS)],
        [narrow(SLOT, D), wide(PAIRS, 4, SLOT)],
        [columns_at(0), stats_at(0)],
        after=after,
        grid=(PAIRS,),
        scratch=[pltpu.VMEM((H, 3 * SPAN), WIDER)],
        flops=2 * 2 * H * SLOT * SLOT * HD * 4,
    )


def attention_back(count, table, pick, heads, grad_mixed, stats, base, half, after=()):
    return run(
        "enc_attention_back",
        attn_bwd_kernel(base),
        [count, table, table, pick, heads, heads, heads, grad_mixed, stats],
        [SCALARS, SCALARS, WHOLE, WHOLE]
        + [columns_at(base), columns_at(PAIRS + base), columns_at(2 * PAIRS + base), columns_at(base), stats_at(base)],
        [narrow(3, SLOT, half * PAIR), wide(half, 8, 4 * SPAN)],
        [pl.BlockSpec((3, SLOT, PAIR), lambda s: (0, 0, s)), pl.BlockSpec((1, 8, 4 * SPAN), lambda s: (s, 0, 0))],
        after=after,
        grid=(half,),
        scratch=[pltpu.VMEM((H, 3 * SPAN), WIDER)],
        flops=2 * 5 * H * SLOT * SLOT * HD * 4,
    )


def ffn_kernel(
    x_ref, mixed_ref, wo_ref, g2_ref, in_ref, out_ref, g3_ref, kv_any,
    after_ref, second_ref, slope_ref, hidden_ref, final_ref, third_ref, pairs_ref,
    kv_ref, sems,
):
    step = pl.program_id(0)
    copy = pltpu.make_async_copy(kv_any, kv_ref, sems.at[0])

    @pl.when(step == 0)
    def _():
        copy.start()
        after = x_ref[...].astype(WIDER) + product(mixed_ref[...], wo_ref[...])
        after_ref[...] = after
        final_ref[...] = after
        second_ref[...] = (after * scale_of(after) * row_of(g2_ref)).astype(LOWER)

    value, slope = silu_like(product(second_ref[...], in_ref[...]))
    slope_ref[...] = slope.astype(LOWER)
    hidden = value.astype(LOWER)
    hidden_ref[...] = hidden
    final_ref[...] += product(hidden, out_ref[...])

    @pl.when(step == STEPS - 1)
    def _():
        final = final_ref[...]
        third = (final * scale_of(final) * row_of(g3_ref)).astype(LOWER)
        third_ref[...] = third
        copy.wait()
        pairs_ref[...] = product(third, kv_ref[...]).astype(LOWER)


def whole(*shape):
    return pl.BlockSpec(shape, lambda s: (0,) * len(shape))


def feed_forward(x, mixed, wo, gain2, ffn_in, ffn_out, gain3, kv):
    rows = whole(SLOT, D)
    by_columns = pl.BlockSpec((SLOT, WIDTH), lambda s: (0, s))
    return run(
        "enc_ffn",
        ffn_kernel,
        [x, mixed, wo, gain2, ffn_in, ffn_out, gain3, kv],
        [rows, rows, whole(D, D), whole(D), pl.BlockSpec((D, WIDTH), lambda s: (0, s))]
        + [pl.BlockSpec((WIDTH, D), lambda s: (s, 0)), whole(D), ANY],
        [wide(SLOT, D), narrow(SLOT, D), narrow(SLOT, FF), narrow(SLOT, FF), wide(SLOT, D), narrow(SLOT, D), narrow(SLOT, 2 * D)],
        [rows, rows, by_columns, by_columns, rows, rows, whole(SLOT, 2 * D)],
        grid=(STEPS,),
        scratch=[pltpu.VMEM((D, 2 * D), LOWER), pltpu.SemaphoreType.DMA((1,))],
        flops=2 * SLOT * D * (D + 2 * FF + 2 * D),
        mib=44,
    )


def kv_back_kernel(gp_ref, kv_ref, final_ref, g3_ref, gfinal_ref, branch_ref, gain_ref):
    back, gain = norm_pull(final_ref[...], row_of(g3_ref), right_product(gp_ref[...], kv_ref[...]))
    gfinal_ref[...] = back
    branch_ref[...] = back.astype(LOWER)
    gain_ref[...] = gain


def kv_back(g_pairs, kv, final, gain3, after=()):
    return run(
        "enc_kv_back",
        kv_back_kernel,
        [g_pairs, kv, final, gain3],
        [WHOLE] * 4,
        [wide(SLOT, D), narrow(SLOT, D), wide(1, D)],
        after=after,
        flops=0,
    )


def ffn_back_kernel(
    branch_ref, out_ref, slope_ref, in_ref, after_ref, g2_ref, gfinal_ref, wo_any,
    ginner_ref, gafter_ref, low_ref, gmixed_ref, gain_ref,
    total_ref, wo_ref, sems,
):
    step = pl.program_id(0)
    copy = pltpu.make_async_copy(wo_any, wo_ref, sems.at[0])

    @pl.when(step == 0)
    def _():
        copy.start()
        total_ref[...] = jnp.zeros((SLOT, D), WIDER)

    grad = right_product(branch_ref[...], out_ref[...])
    inner = (grad * slope_ref[...].astype(WIDER)).astype(LOWER)
    ginner_ref[...] = inner
    total_ref[...] += right_product(inner, in_ref[...])

    @pl.when(step == STEPS - 1)
    def _():
        back, gain = norm_pull(after_ref[...], row_of(g2_ref), total_ref[...])
        gain_ref[...] = gain
        g_after = gfinal_ref[...] + back
        gafter_ref[...] = g_after
        low = g_after.astype(LOWER)
        low_ref[...] = low
        copy.wait()
        gmixed_ref[...] = right_product(low, wo_ref[...]).astype(LOWER)


def ffn_back(branch, ffn_out, slope, ffn_in, after_rows, gain2, g_final, wo, after=()):
    rows = whole(SLOT, D)
    by_columns = pl.BlockSpec((SLOT, WIDTH), lambda s: (0, s))
    return run(
        "enc_ffn_back",
        ffn_back_kernel,
        [branch, ffn_out, slope, ffn_in, after_rows, gain2, g_final, wo],
        [rows, pl.BlockSpec((WIDTH, D), lambda s: (s, 0)), by_columns, pl.BlockSpec((D, WIDTH), lambda s: (0, s))]
        + [rows, whole(D), rows, ANY],
        [narrow(SLOT, FF), wide(SLOT, D), narrow(SLOT, D), narrow(SLOT, D), wide(1, D)],
        [by_columns, rows, rows, rows, whole(1, D)],
        after=after,
        grid=(STEPS,),
        scratch=[pltpu.VMEM((SLOT, D), WIDER), pltpu.VMEM((D, D), LOWER), pltpu.SemaphoreType.DMA((1,))],
        flops=2 * SLOT * D * (D + 2 * FF),
        mib=44,
    )


def rows_back_kernel(
    ga_ref, gb_ref, w_ref, x_ref, g1_ref, gafter_ref, gain2_ref, gain3_ref, da_ref, db_ref, pick_ref,
    grows_ref, small_ref, total_ref,
):
    step = pl.program_id(0)

    @pl.when(step == 0)
    def _():
        total_ref[...] = jnp.zeros((SLOT, D), WIDER)

    total_ref[...] += right_product(ga_ref[0], w_ref[:, :WIDE_A]) + right_product(gb_ref[0], w_ref[:, WIDE_A:])

    @pl.when(step == 2)
    def _():
        back, gain = norm_pull(x_ref[...].astype(WIDER), row_of(g1_ref), total_ref[...])
        grows_ref[...] = gafter_ref[...] + back
        sums = [ref[k, :2] for ref in (da_ref, db_ref) for k in range(ref.shape[0])]
        table = split_product(jnp.concatenate(sums, axis=0), pick_ref[...], 2)
        small_ref[...] = jnp.zeros((16, D), WIDER)
        small_ref[0:1] = gain
        small_ref[1:2] = gain2_ref[...]
        small_ref[2:3] = gain3_ref[...]
        small_ref[4:16, :STAT] = table


def rows_back(grads, qkv, x, gain1, g_after, gain2, gain3, diagonals, pick_back, after=()):
    rows = whole(SLOT, D)
    by_kind = [pl.BlockSpec((1, SLOT, w), lambda s: (s, 0, 0)) for w in (WIDE_A, WIDE_B)]
    return run(
        "enc_rows_back",
        rows_back_kernel,
        [grads[0], grads[1], qkv, x, gain1, g_after, gain2, gain3, diagonals[0], diagonals[1], pick_back],
        by_kind
        + [pl.BlockSpec((D, D), lambda s: (0, s)), rows, whole(D), rows, whole(1, D), whole(1, D)]
        + [whole(*diagonals[0].shape), whole(*diagonals[1].shape), whole(4 * SPAN, STAT)],
        [wide(SLOT, D), wide(16, D)],
        [rows, whole(16, D)],
        after=after,
        grid=(3,),
        scratch=[pltpu.VMEM((SLOT, D), WIDER)],
        flops=2 * SLOT * D * 3 * D,
    )


def head_lanes(h):
    lanes = lax.broadcasted_iota(jnp.int32, (GROUP, D), 1)
    return (lanes >= h * HD) & (lanes < (h + 1) * HD)


def stack_heads(flat):
    return jnp.concatenate([jnp.where(head_lanes(h), flat, 0.0) for h in range(H)], axis=0)


def merge_heads(stacked):
    total = jnp.zeros((GROUP, D), WIDER)
    for h in range(H):
        total = total + jnp.where(head_lanes(h), stacked[GROUP * h : GROUP * h + GROUP], 0.0)
    return total


def lanes_to_column(stat):
    lanes = lax.broadcasted_iota(jnp.int32, (GROUP, STAT), 1)
    parts = [jnp.sum(jnp.where(lanes == h, stat, 0.0), axis=1, keepdims=True) for h in range(H)]
    return jnp.concatenate(parts, axis=0)


def column_to_lanes(column, first):
    lanes = lax.broadcasted_iota(jnp.int32, (GROUP, STAT), 1)
    total = jnp.zeros((GROUP, STAT), WIDER)
    for h in range(H):
        total = total + jnp.where(lanes == first + h, column[GROUP * h : GROUP * h + GROUP], 0.0)
    return total


def spread_heads(stat):
    rows = lax.broadcasted_iota(jnp.int32, (STAT, D), 0) * HD
    lanes = lax.broadcasted_iota(jnp.int32, (STAT, D), 1)
    spread = jnp.where((lanes >= rows) & (lanes < rows + HD), 1.0, 0.0).astype(LOWER)
    return split_product(stat, spread, 2)


def own_scores(query, keys, table_ref):
    raw = right_product(query, keys)
    rows = lax.broadcasted_iota(jnp.int32, (GROUP, GROUP), 0)
    columns = lax.broadcasted_iota(jnp.int32, (GROUP, GROUP), 1)
    away = rows - columns
    parts = []
    for h in range(H):
        bias = jnp.full((GROUP, GROUP), table_ref[h, 0], WIDER)
        for d in range(1, GROUP):
            bias = jnp.where(away == d, table_ref[h, d], bias)
        part = raw[GROUP * h : GROUP * h + GROUP] + bias
        parts.append(jnp.where(away >= 0, part, MASKED))
    scores = jnp.concatenate(parts, axis=0)
    powers = jnp.exp(scores - jnp.max(scores, axis=1, keepdims=True))
    return powers / jnp.sum(powers, axis=1, keepdims=True)


def padded(ref, pad_ref):
    pad_ref[...] = jnp.zeros((GROUP, D), WIDER)
    pad_ref[:ANS] = ref[...].astype(WIDER)
    return pad_ref[...]


def answer_rows(width):
    return lax.broadcasted_iota(jnp.int32, (GROUP, width), 0) < ANS


def dec_self_kernel(
    table_ref, x_ref, g1_ref, g2_ref, qkv_any, out_any, query_any,
    after_ref, lefts_ref, heads_ref, query_ref,
    qkv_ref, out_ref, cross_ref, pad_ref, sems,
):
    copies = fetch(((qkv_any, qkv_ref), (out_any, out_ref), (query_any, cross_ref)), sems)
    start = padded(x_ref, pad_ref)
    first = (start * scale_of(start) * row_of(g1_ref)).astype(LOWER)
    copies[0].wait()
    heads = product(first, qkv_ref[...]).astype(LOWER)
    heads_ref[...] = heads
    query = stack_heads(heads.astype(WIDER)[:, :D] * 0.125).astype(LOWER)
    probs = own_scores(query, heads[:, D : 2 * D], table_ref)
    own = merge_heads(product(probs.astype(LOWER), heads[:, 2 * D :]))
    own = jnp.where(answer_rows(D), own, 0.0).astype(LOWER)
    copies[1].wait()
    after = start + product(own, out_ref[...])
    after_ref[...] = after
    second = (after * scale_of(after) * row_of(g2_ref)).astype(LOWER)
    copies[2].wait()
    query_ref[...] = product(second, cross_ref[...]).astype(LOWER)
    lefts_ref[:, :D] = first
    lefts_ref[:, D : 2 * D] = own
    lefts_ref[:, 2 * D :] = second


def masked_cross(n_ref, query_ref, pairs_ref):
    query = stack_heads(query_ref[...].astype(WIDER) * 0.125).astype(LOWER)
    raw = right_product(query, pairs_ref[:, :D])
    places = lax.broadcasted_iota(jnp.int32, (STACK, SLOT), 1)
    return query, jnp.where(places < n_ref[0], raw, MASKED)


def cross_kernel(n_ref, query_ref, pairs_ref, packed_ref):
    unused, scores = masked_cross(n_ref, query_ref, pairs_ref)
    top = jnp.max(scores, axis=1, keepdims=True)
    powers = jnp.exp(scores - top)
    total = jnp.sum(powers, axis=1, keepdims=True)
    probs = (powers / total).astype(LOWER)
    packed_ref[:, :D] = merge_heads(product(probs, pairs_ref[:, D:]))
    packed_ref[:, D:] = column_to_lanes(top, 0) + column_to_lanes(total, STAT // 2)


def dec_mid_kernel(
    parts_ref, after_ref, cot_ref, g3_ref, lefts_ref, cross_any, in_any, out_any,
    answer_ref, early_ref, mix_ref, gmix_ref, gmid_ref, stat_ref, gain_ref,
    cross_ref, in_ref, out_ref, pad_ref, sems,
):
    copies = fetch(((cross_any, cross_ref), (in_any, in_ref), (out_any, out_ref)), sems)
    size = parts_ref.shape[0]
    used = lax.broadcasted_iota(jnp.int32, (GROUP, STAT), 1) < H
    tops = [parts_ref[k, :, D:] for k in range(size)]
    totals = [pltpu.roll(stat, STAT // 2, 1) for stat in tops]
    top = tops[0]
    for k in range(1, size):
        top = jnp.maximum(top, tops[k])
    weights = [jnp.where(used, totals[k] * jnp.exp(tops[k] - top), 0.0) for k in range(size)]
    total = weights[0]
    for k in range(1, size):
        total = total + weights[k]
    total = jnp.where(used, total, 1.0)
    mix = jnp.zeros((GROUP, D), WIDER)
    for k in range(size):
        mix = mix + parts_ref[k, :, :D] * spread_heads(weights[k] / total)
    mix_ref[...] = mix
    stat_ref[:, :STAT] = jnp.where(used, top, 0.0)
    stat_ref[:, STAT:] = total
    mix_low = mix.astype(LOWER)
    copies[0].wait()
    middle = after_ref[...] + product(mix_low, cross_ref[...])
    third = (middle * scale_of(middle) * row_of(g3_ref)).astype(LOWER)
    copies[1].wait()
    inner = product(third, in_ref[...])
    value, slope = silu_like(inner)
    hidden = value.astype(LOWER)
    copies[2].wait()
    answer = (middle + product(hidden, out_ref[...])).astype(LOWER)
    answer_ref[...] = answer[:ANS]
    grad = padded(cot_ref, pad_ref)
    out_low = grad.astype(LOWER)
    g_inner = (right_product(out_low, out_ref[...]) * slope).astype(LOWER)
    back, gain = norm_pull(middle, row_of(g3_ref), right_product(g_inner, in_ref[...]))
    gain_ref[...] = gain
    g_middle = grad + back
    gmid_ref[...] = g_middle
    middle_low = g_middle.astype(LOWER)
    gmix_ref[...] = right_product(middle_low, cross_ref[...]).astype(LOWER)

    def store(name, rows):
        early_ref[:, AT[name] : AT[name] + rows.shape[1]] = rows

    def kept(rows):
        return jnp.where(answer_rows(rows.shape[1]), rows.astype(WIDER), 0.0).astype(LOWER)

    early_ref[:, : 3 * D] = kept(lefts_ref[...])
    store("mix", kept(mix_low))
    store("third", kept(third))
    store("hidden", kept(hidden))
    store("g_middle", middle_low)
    store("g_inner", g_inner)
    store("g_out", out_low)


def cross_back_kernel(n_ref, query_ref, pairs_ref, gmix_ref, mix_ref, stat_ref, gpairs_ref, partial_ref):
    query, scores = masked_cross(n_ref, query_ref, pairs_ref)
    top = lanes_to_column(stat_ref[:, :STAT])
    total = lanes_to_column(stat_ref[:, STAT:])
    probs = jnp.exp(scores - top) / total
    grad = stack_heads(gmix_ref[...].astype(WIDER))
    weighted = jnp.sum(grad * jnp.concatenate([mix_ref[...]] * H, axis=0), axis=1, keepdims=True)
    grad = grad.astype(LOWER)
    grad_probs = right_product(grad, pairs_ref[:, D:])
    rounded = (probs * (grad_probs - weighted)).astype(LOWER)
    gpairs_ref[:, :D] = left_product(rounded, query).astype(LOWER)
    gpairs_ref[:, D:] = left_product(probs.astype(LOWER), grad).astype(LOWER)
    partial_ref[...] = merge_heads(product(rounded, pairs_ref[:, :D])) * 0.125


def dec_back_kernel(
    table_ref, x_ref, part_ref, got_ref, after_ref, gmid_ref, heads_ref,
    g1_ref, g2_ref, gain3_ref, query_any, out_any, qkv_any,
    late_ref, gstart_ref,
    cross_ref, out_ref, qkv_ref, pad_ref, sems,
):
    copies = fetch(((query_any, cross_ref), (out_any, out_ref), (qkv_any, qkv_ref)), sems)
    g_query = (part_ref[...] + got_ref[...]).astype(LOWER)
    copies[0].wait()
    back, gain2 = norm_pull(after_ref[...], row_of(g2_ref), right_product(g_query, cross_ref[...]))
    g_after = gmid_ref[...] + back
    after_low = g_after.astype(LOWER)
    copies[1].wait()
    g_own = stack_heads(right_product(after_low, out_ref[...])).astype(LOWER)
    heads = heads_ref[...]
    query = stack_heads(heads.astype(WIDER)[:, :D] * 0.125).astype(LOWER)
    probs = own_scores(query, heads[:, D : 2 * D], table_ref)
    grad_probs = right_product(g_own, heads[:, 2 * D :])
    rounded = (probs * (grad_probs - jnp.sum(probs * grad_probs, axis=1, keepdims=True))).astype(LOWER)
    g_q = (merge_heads(product(rounded, heads[:, D : 2 * D])) * 0.125).astype(LOWER)
    g_k = left_product(rounded, query).astype(LOWER)
    g_v = left_product(probs.astype(LOWER), g_own).astype(LOWER)
    g_heads = jnp.concatenate([g_q, g_k, g_v], axis=1)
    copies[2].wait()
    start = padded(x_ref, pad_ref)
    back, gain1 = norm_pull(start, row_of(g1_ref), right_product(g_heads, qkv_ref[...]))
    gstart_ref[...] = (g_after + back)[:ANS]
    spread = rounded.astype(WIDER)
    rows = lax.broadcasted_iota(jnp.int32, (GROUP, GROUP), 0)
    columns = lax.broadcasted_iota(jnp.int32, (GROUP, GROUP), 1)
    mirror = jnp.where(rows + columns == GROUP - 1, 1.0, 0.0).astype(LOWER)
    empty = jnp.zeros((GROUP, STAT - GROUP), WIDER)
    tables = []
    for h in range(H):
        part = product(mirror, spread[GROUP * h : GROUP * h + GROUP].astype(LOWER))
        turned = pltpu.roll(jnp.concatenate([part, empty], axis=1), 0, 1, stride=1, stride_axis=0)
        tables.append(jnp.sum(turned, axis=0, keepdims=True))
    small = jnp.concatenate([gain1, gain2, gain3_ref[...]] + tables, axis=1)
    places = lax.broadcasted_iota(jnp.int32, (GROUP, LATE), 0)
    late = jnp.concatenate([g_heads, after_low, g_query], axis=1).astype(WIDER)
    late = jnp.concatenate([jnp.where(places == ANS, small, late), jnp.zeros((SENT - GROUP, LATE), WIDER)], axis=0)
    late_ref[...] = late.astype(LOWER)


def dec_outer_kernel(size):
    part = D // size

    def body(me_ref, *refs):
        me = me_ref[0]
        qkv_ref, out_ref, query_ref, cross_ref, in_ref, ffn_ref, small_ref, early_ref, late_ref = refs[2:]
        early_ref[...] = jnp.concatenate([refs[0][s].astype(WIDER) for s in range(size)], axis=0).astype(LOWER)
        late = [refs[1][s].astype(WIDER)[:GROUP] for s in range(size)]
        late_ref[...] = jnp.concatenate(late, axis=0).astype(LOWER)
        rows = lax.broadcasted_iota(jnp.int32, (part, D), 0) + me * part
        lanes = lax.broadcasted_iota(jnp.int32, (part, D), 1)
        picked = jnp.where(rows == lanes, 1.0, 0.0).astype(LOWER)

        def outer(name, right):
            left = right_product(picked, early_ref[:, AT[name] : AT[name] + D]).astype(LOWER)
            return product(left, right)

        qkv_ref[...] = outer("first", late_ref[:, : 3 * D])
        out_ref[...] = outer("own", late_ref[:, AT["g_after"] : AT["g_after"] + D])
        query_ref[...] = outer("second", late_ref[:, AT["g_query"] : AT["g_query"] + D])
        cross_ref[...] = outer("mix", early_ref[:, AT["g_middle"] : AT["g_middle"] + D])
        in_ref[...] = outer("third", early_ref[:, AT["g_inner"] : AT["g_inner"] + FF])
        height = FF // size
        first = pl.multiple_of(AT["hidden"] + me * height, 128)
        ffn_ref[...] = left_product(early_ref[:, pl.ds(first, height)], early_ref[:, AT["g_out"] : AT["g_out"] + D])
        total = jnp.zeros((1, LATE), WIDER)
        for k in range(size):
            total = total + late[k][ANS : ANS + 1]
        small_ref[...] = total

    return body


def held(*shapes):
    return [pltpu.VMEM(shape, LOWER) for shape in shapes] + [
        pltpu.VMEM((GROUP, D), WIDER),
        pltpu.SemaphoreType.DMA((len(shapes),)),
    ]


def dec_self(table, answers, gain1, gain2, qkv, out, query, after=()):
    return run(
        "dec_self",
        dec_self_kernel,
        [table, answers, gain1, gain2, qkv, out, query],
        [SCALARS] + [WHOLE] * 3 + [ANY] * 3,
        [wide(GROUP, D), narrow(GROUP, 3 * D), narrow(GROUP, 3 * D), narrow(GROUP, D)],
        after=after,
        scratch=held((D, 3 * D), (D, D), (D, D)),
        flops=10**9,
    )


def cross(count, query, pairs, after=()):
    return run(
        "cross",
        cross_kernel,
        [count, query, pairs],
        [SCALARS, WHOLE, WHOLE],
        [wide(GROUP, D + STAT)],
        after=after,
        flops=4 * STACK * SLOT * D,
    )


def dec_mid(parts, after_rows, cotangent, gain3, lefts, cross_out, ffn_in, ffn_out, after=()):
    return run(
        "dec_mid",
        dec_mid_kernel,
        [parts, after_rows, cotangent, gain3, lefts, cross_out, ffn_in, ffn_out],
        [WHOLE] * 5 + [ANY] * 3,
        [narrow(ANS, D), narrow(GROUP, EARLY), wide(GROUP, D), narrow(GROUP, D), wide(GROUP, D), wide(GROUP, 2 * STAT), wide(1, D)],
        after=after,
        scratch=held((D, D), (D, FF), (FF, D)),
        flops=4 * 10**9,
    )


def cross_back(count, query, pairs, g_mix, mix, stat, after=()):
    return run(
        "cross_back",
        cross_back_kernel,
        [count, query, pairs, g_mix, mix, stat],
        [SCALARS] + [WHOLE] * 5,
        [narrow(SLOT, 2 * D), wide(GROUP, D)],
        after=after,
        flops=10 * STACK * SLOT * D,
    )


def dec_back(table, answers, part, got, after_rows, g_middle, heads, gain1, gain2, g_gain3, query, out, qkv, after=()):
    return run(
        "dec_back",
        dec_back_kernel,
        [table, answers, part, got, after_rows, g_middle, heads, gain1, gain2, g_gain3, query, out, qkv],
        [SCALARS] + [WHOLE] * 9 + [ANY] * 3,
        [narrow(SENT, LATE), wide(ANS, D)],
        after=after,
        scratch=held((D, D), (D, D), (D, 3 * D)),
        flops=0,
    )


def dec_outer(me, early, late, size, after=()):
    part = D // size
    return run(
        "dec_outer",
        dec_outer_kernel(size),
        [me, early, late],
        [SCALARS, WHOLE, WHOLE],
        [wide(part, 3 * D), wide(part, D), wide(part, D), wide(part, D), wide(part, FF), wide(FF // size, D), wide(1, LATE)],
        after=after,
        scratch=[pltpu.VMEM((size * GROUP, EARLY), LOWER), pltpu.VMEM((size * GROUP, LATE), LOWER)],
        flops=10**9,
        mib=40,
    )


PLACES = [(0, 0), (0, 1), (1, 0), (1, 1)]


def place_of(me, there):
    return me ^ (4 * there[0] + 2 * there[1])


def turned_rows(me, acts, block):
    lanes = lax.broadcasted_iota(jnp.int32, (block, D), 1)
    rows = lax.broadcasted_iota(jnp.int32, (block, D), 0)
    picked = [jnp.where(lanes - rows == place_of(me, t) * block, 1.0, 0.0).astype(LOWER) for t in PLACES]
    picked = jnp.concatenate(picked, axis=0)
    return jnp.concatenate([right_product(picked, act).astype(LOWER) for act in acts], axis=1)


def target(there, x_refs, y_refs):
    dy, dx = there
    return (x_refs[dx].at[dy], y_refs[dy].at[dx])


def one_kernel(me_ref, t_own, t_par, p_own, p_par, h_own, h_par, b_own, b_par, xk, xs, yk, ys, t, p, h, b, sems):
    me = me_ref[0]
    block = FF // 8
    pairs = [(t_own, t.at[0]), (t_par, t.at[1]), (p_own, p.at[:SLOT]), (p_par, p.at[SLOT:])]
    pairs += [(b_own, b.at[:SLOT]), (b_par, b.at[SLOT:])]
    for k, there in enumerate(PLACES):
        lanes = pl.ds(pl.multiple_of(place_of(me, there) * block, 128), block)
        pairs += [(h_own.at[:, lanes], h.at[k, :SLOT]), (h_par.at[:, lanes], h.at[k, SLOT:])]
    copies = fetch(pairs, sems)
    copies[0].wait()
    copies[1].wait()
    height = D // 8
    left = turned_rows(me, (t[0], t[1]), height)
    copies[2].wait()
    copies[3].wait()
    for c in range(2):
        grad = product(left, p[:, D * c : D * c + D]).astype(LOWER)
        for k, there in enumerate(PLACES):
            to, unused = target(there, (xk, xs), (yk, ys))
            to[height * c : height * c + height] = grad[height * k : height * k + height]
    copies[4].wait()
    copies[5].wait()
    for k, there in enumerate(PLACES):
        copies[6 + 2 * k].wait()
        copies[7 + 2 * k].wait()
        grad = left_product(h[k], b[...]).astype(LOWER)
        to_x, to_y = target(there, (xk, xs), (yk, ys))
        to_x[2 * height : 3 * height] = grad[:height]
        to_y[...] = grad[height:]


def two_kernel(me_ref, s_own, s_par, i_own, i_par, m_own, m_par, l_own, l_par, xk, xs, yk, ys, s, i, m, l, sems):
    me = me_ref[0]
    pairs = [(s_own, s.at[0]), (s_par, s.at[1])]
    for c in range(4):
        lanes = slice(D * c, D * c + D)
        pairs += [(i_own.at[:, lanes], i.at[c, :SLOT]), (i_par.at[:, lanes], i.at[c, SLOT:])]
    pairs += [(m_own, m.at[0]), (m_par, m.at[1]), (l_own, l.at[:SLOT]), (l_par, l.at[SLOT:])]
    copies = fetch(pairs, sems)
    copies[0].wait()
    copies[1].wait()
    height = D // 8
    half = height // 2
    left = turned_rows(me, (s[0], s[1]), height)
    for c in range(4):
        copies[2 + 2 * c].wait()
        copies[3 + 2 * c].wait()
        grad = product(left, i[c]).astype(LOWER)
        for k, there in enumerate(PLACES):
            to = target(there, (xk, xs), (yk, ys))[c // 2]
            to[height * (c % 2) : height * (c % 2) + height] = grad[height * k : height * k + height]
    for k in range(10, 14):
        copies[k].wait()
    left = turned_rows(me, (m[0], m[1]), height)
    grad = product(left, l[...]).astype(LOWER)
    for k, there in enumerate(PLACES):
        for to, first in zip(target(there, (xk, xs), (yk, ys)), (0, half)):
            to[2 * height : 2 * height + half] = grad[height * k + first : height * k + first + half]


def three_kernel(me_ref, f_own, f_par, a_own, a_par, b_own, b_par, xk, xs, yk, ys, f, ga, gb, sems):
    me = me_ref[0]
    pairs = [(f_own, f.at[0]), (f_par, f.at[1])]
    for own, par, held_here in ((a_own, a_par, ga), (b_own, b_par, gb)):
        for c in range(3):
            pairs += [(own.at[c], held_here.at[c, :SLOT]), (par.at[c], held_here.at[c, SLOT:])]
    copies = fetch(pairs, sems)
    copies[0].wait()
    copies[1].wait()
    height = D // 8
    left = turned_rows(me, (f[0], f[1]), height)
    jobs = [(ga, 0, 0, 0), (ga, 1, 0, WIDE_A), (ga, 2, 1, 0)] + [(gb, c, 1, WIDE_A + WIDE_B * c) for c in range(3)]
    for k, (grads, c, side, first) in enumerate(jobs):
        copies[2 + 2 * k].wait()
        copies[3 + 2 * k].wait()
        grad = product(left, grads[c]).astype(LOWER)
        for p, there in enumerate(PLACES):
            to = target(there, (xk, xs), (yk, ys))[side]
            to[:, first : first + grad.shape[1]] = grad[height * p : height * p + height]


def weights_one(me, third, g_pairs, hidden, branch, after=()):
    out = narrow(2, 3 * D // 8, D)
    return run(
        "weights_one",
        one_kernel,
        [me, *third, *g_pairs, *hidden, *branch],
        [SCALARS] + [ANY] * 8,
        [out] * 4,
        after=after,
        scratch=[
            pltpu.VMEM((2, SLOT, D), LOWER),
            pltpu.VMEM((2 * SLOT, 2 * D), LOWER),
            pltpu.VMEM((4, 2 * SLOT, FF // 8), LOWER),
            pltpu.VMEM((2 * SLOT, D), LOWER),
            pltpu.SemaphoreType.DMA((14,)),
        ],
        flops=4 * 10**9,
    )


def weights_two(me, second, g_inner, mixed, low, after=()):
    out = narrow(2, 5 * D // 16, D)
    return run(
        "weights_two",
        two_kernel,
        [me, *second, *g_inner, *mixed, *low],
        [SCALARS] + [ANY] * 8,
        [out] * 4,
        after=after,
        scratch=[
            pltpu.VMEM((2, SLOT, D), LOWER),
            pltpu.VMEM((4, 2 * SLOT, D), LOWER),
            pltpu.VMEM((2, SLOT, D), LOWER),
            pltpu.VMEM((2 * SLOT, D), LOWER),
            pltpu.SemaphoreType.DMA((14,)),
        ],
        flops=0,
    )


def weights_three(me, first, grads_a, grads_b, after=()):
    out_x = narrow(2, D // 8, 2 * WIDE_A)
    out_y = narrow(2, D // 8, WIDE_A + 3 * WIDE_B)
    return run(
        "weights_three",
        three_kernel,
        [me, *first, *grads_a, *grads_b],
        [SCALARS] + [ANY] * 6,
        [out_x, out_x, out_y, out_y],
        after=after,
        scratch=[
            pltpu.VMEM((2, SLOT, D), LOWER),
            pltpu.VMEM((3, 2 * SLOT, WIDE_A), LOWER),
            pltpu.VMEM((3, 2 * SLOT, WIDE_B), LOWER),
            pltpu.SemaphoreType.DMA((14,)),
        ],
        flops=0,
    )


def page(array, k):
    return pl.BlockSpec((1,) + array.shape[1:], lambda s: (k, 0, 0))


def add_first(parts, small=None, after=()):
    count = len(parts)

    def body(*refs):
        outs = refs[len(flat) :]
        for k in range(count):
            outs[k][...] = (refs[2 * k][0].astype(WIDER) + refs[2 * k + 1][0].astype(WIDER)).astype(LOWER)
        if small is not None:
            outs[count][...] = refs[2 * count][...] + refs[2 * count + 1][...]

    flat = [a for pair in parts for a in pair] + list(small or ())
    specs = [page(a, 1) if a.ndim == 3 else WHOLE for a in flat]
    outs = [narrow(*keep.shape[1:]) for keep, unused in parts]
    specs_out = [WHOLE] * count
    if small is not None:
        outs.append(wide(*small[0].shape))
        specs_out.append(WHOLE)
    return run("add_first", body, flat, specs, outs, specs_out, after=after, grid=(1,), mib=8, flops=0)


def add_second(parts, small=None, after=()):
    count = len(parts)
    shapes = [keep.shape[1:] for keep, unused, unused_too in parts]
    stacked = shapes[0][1] == shapes[-1][1]
    rows = sum(shape[0] for shape in shapes) if stacked else shapes[0][0]
    columns = shapes[0][1] if stacked else sum(shape[1] for shape in shapes)

    def body(*refs):
        out = refs[-1]
        first = 0
        for k, (high, across) in enumerate(shapes):
            keep, got, last = refs[3 * k : 3 * k + 3]
            total = (keep[0].astype(WIDER) + got[0].astype(WIDER) + last[...].astype(WIDER)).astype(LOWER)
            if stacked:
                out[first : first + high] = total
                first += high
            else:
                out[:rows, first : first + across] = total
                first += across
        if small is not None:
            out[rows:] = jnp.zeros((16, columns), LOWER)
            out[rows:, :D] = (refs[3 * count][...] + refs[3 * count + 1][...]).astype(LOWER)

    flat = [a for trio in parts for a in trio] + list(small or ())
    specs = [page(a, 0) if a.ndim == 3 else WHOLE for a in flat]
    height = rows + (16 if small is not None else 0)
    return run("add_second", body, flat, specs, [narrow(height, columns)], after=after, grid=(1,), mib=8, flops=0)


def add_pair(one, two, small=None, after=()):
    def body(*refs):
        outs = refs[len(flat) :]
        outs[0][...] = (refs[0][...].astype(WIDER) + refs[1][...].astype(WIDER)).astype(LOWER)
        if small is not None:
            outs[1][...] = refs[2][...] + refs[3][...]

    flat = [one, two] + list(small or ())
    outs = [narrow(*one.shape)] + [wide(*a.shape) for a in (small or ())[:1]]
    return run("add_pair", body, flat, [WHOLE] * len(flat), outs, after=after, mib=8, flops=0)


def add_rows(one, two, after=()):
    def body(one_ref, two_ref, out_ref):
        out_ref[...] = one_ref[...] + two_ref[...]

    return run("add_rows", body, [one, two], [WHOLE] * 2, [wide(*one.shape)], after=after, mib=4, flops=0)


def partner(axis, bit):
    return [(k, k ^ (1 << bit)) for k in range(lax.axis_size(axis))]


def swap(value, axis, bit):
    return lax.ppermute(value, axis, partner(axis, bit))


def all_sum(value, axis):
    for bit in range(lax.axis_size(axis).bit_length() - 1):
        value = value + swap(value, axis, bit)
    return value


def pa_order(turn):
    rest = lax.axis_size("pa").bit_length() - 2
    return [1 + (k + turn) % rest for k in range(rest)]


def both_cores(acts, turn):
    size = lax.axis_size("pa")
    me = lax.axis_index("pa")
    blocks = jnp.transpose(acts).reshape(size, acts.shape[1] // size, acts.shape[0])
    order = pa_order(turn)
    offsets = [
        sum(((k >> (len(order) - 1 - p)) & 1) << bit for p, bit in enumerate(order)) for k in range(size // 2)
    ]
    mine = jnp.concatenate([lax.dynamic_slice_in_dim(blocks, me ^ d, 1) for d in offsets])
    theirs = jnp.concatenate([lax.dynamic_slice_in_dim(blocks, me ^ d ^ 1, 1) for d in offsets])
    return mine, swap(theirs, "pa", 0)


def weight_part(acts, grads, first, last):
    total = None
    for act, grad in zip(acts, grads):
        act = act[first:last]
        term = product(act.reshape(-1, act.shape[2]), grad)
        total = term if total is None else total + term
    height = acts[0].shape[1]
    return total.astype(LOWER).reshape(last - first, height, -1)


def add_up(parts):
    total = parts[0].astype(WIDER)
    for part in parts[1:]:
        total = total + part.astype(WIDER)
    return total.astype(LOWER)


def share_over_pa(acts, grads, turn):
    size = acts[0].shape[0]
    keep = [weight_part(acts, grads, 0, size // 2)]
    send = weight_part(acts, grads, size // 2, size)
    for bit in pa_order(turn):
        keep.append(swap(send, "pa", bit))
        size //= 2
        if size > 1:
            send = add_up([part[size // 2 : size] for part in keep])
            keep = [part[: size // 2] for part in keep]
    return add_up([part[0] for part in keep])


def inward(share):
    return lax.ppermute(share, "pb", [(0, 1), (3, 2)])


def between(share):
    return lax.ppermute(share, "pb", [(1, 2), (2, 1)])


def outward(share):
    me = lax.axis_index("pb")
    got = lax.ppermute(share, "pb", [(1, 0), (2, 3)])
    return jnp.where((me == 1) | (me == 2), share, got).astype(WIDER)


def total_plain(share):
    return lax.psum(share, "pb").astype(WIDER)


def local(
    passages,
    lengths,
    answers,
    cotangent,
    enc_gain1,
    enc_qkv,
    enc_bias,
    enc_out,
    enc_gain2,
    enc_ffn_in,
    enc_ffn_out,
    enc_gain3,
    cross_kv,
    dec_gain1,
    dec_qkv,
    dec_bias,
    dec_out,
    dec_gain2,
    cross_query,
    cross_out,
    dec_gain3,
    dec_ffn_in,
    dec_ffn_out,
):
    pa_size = lax.axis_size("pa")
    pb_size = lax.axis_size("pb")
    fast = pa_size == 8 and pb_size == 4
    me = lax.axis_index("pa").astype(jnp.int32).reshape(1)
    x = passages.reshape(SLOT, D)
    count = lengths.reshape(1)
    table = jnp.transpose(enc_bias)
    dec_table = jnp.transpose(dec_bias)
    pick = jnp.asarray(PICK, LOWER)
    pick_back = jnp.asarray(PICK_BACK, LOWER)

    def across(value):
        return value, swap(value, "pa", 0)

    rows = x.astype(WIDER)
    first = (rows * scale_of(rows) * enc_gain1).astype(LOWER)
    heads = product(first, enc_qkv).astype(LOWER)
    mixed, stats, token = attention(count, table, pick, heads)
    after, second, slope, hidden, final, third, pairs, token = feed_forward(
        x, mixed, enc_out, enc_gain2, enc_ffn_in, enc_ffn_out, enc_gain3, cross_kv
    )
    dec_after, lefts, dec_heads, query, token = dec_self(
        dec_table, answers[0], dec_gain1, dec_gain2, dec_qkv, dec_out, cross_query, after=[token]
    )
    packed, token = cross(count, query, pairs)
    if fast:
        acts = [across(value) for value in (first, mixed, second, hidden, third)]
    else:
        acts = [both_cores(v, k % 2) for k, v in enumerate((first, mixed, second, hidden, third))]
    gathered = lax.all_gather(packed, "pa")
    answer, early, mix, g_mix, g_middle, stat, g_gain3, token = dec_mid(
        gathered, dec_after, cotangent[0], dec_gain3, lefts, cross_out, dec_ffn_in, dec_ffn_out,
        after=[got for unused, got in acts[:4]],
    )
    g_pairs, partial, token = cross_back(count, query, pairs, g_mix, mix, stat)
    early_all = lax.all_gather(early, "pb")
    g_final, branch, g_enc_gain3, token = kv_back(g_pairs, cross_kv, final, enc_gain3)
    if fast:
        partial, token = add_rows(partial, swap(partial, "pa", 0), after=[token])
    g_inner, g_after, low, g_mixed, g_enc_gain2, token = ffn_back(
        branch, enc_ffn_out, slope, enc_ffn_in, after, enc_gain2, g_final, enc_out, after=[token]
    )

    def back_of(base, pairs, after):
        return attention_back(count, table, pick, heads, g_mixed, stats, base, pairs, after=after)

    def dec_end(part, got, token, wait=()):
        return dec_back(
            dec_table, answers[0], part, got, dec_after, g_middle, dec_heads,
            dec_gain1, dec_gain2, g_gain3, cross_query, dec_out, dec_qkv, after=[token, *wait],
        )

    def rows_end(token):
        return rows_back(
            (grads_a, grads_b), enc_qkv, x, enc_gain1, g_after, g_enc_gain2, g_enc_gain3,
            (diagonal_a, diagonal_b), pick_back, after=[token],
        )

    pb_me = lax.axis_index("pb").astype(jnp.int32).reshape(1)

    def outer_end(token):
        *outer, token = dec_outer(pb_me, early_all, late_all, pb_size, after=[token])
        return outer, token

    if fast:
        got = swap(partial, "pa", 1)
        xk, xs, yk, ys, token = weights_one(me, acts[4], across(g_pairs), acts[3], across(branch), after=[token])
        one = ((xk, swap(xs, "pa", 1)), (yk, swap(ys, "pa", 2)))
        partial, token = add_rows(partial, got, after=[token])
        got = swap(partial, "pa", 2)
        xk, xs, yk, ys, token = weights_two(me, acts[2], across(g_inner), acts[1], across(low), after=[token])
        two = ((xk, swap(xs, "pa", 1)), (yk, swap(ys, "pa", 2)))
        grads_a, diagonal_a, token = back_of(0, FIRST, [token])
        there_a = swap(grads_a, "pa", 0)
        late, g_start, token = dec_end(partial, got, token, [early_all])
        late_all = lax.all_gather(late, "pb")
        send_x, send_y, token = add_first(one, after=[token])
        last = (swap(send_x, "pa", 2), swap(send_y, "pa", 1))
        send_x, send_y, token = add_first(two, after=[token])
        last_two = (swap(send_x, "pa", 2), swap(send_y, "pa", 1))
        grads_b, diagonal_b, token = back_of(FIRST, PAIRS - FIRST, [token])
        there_b = swap(grads_b, "pa", 0)
        share_one, token = add_second([one[0] + last[:1], one[1] + last[1:]], after=[token])
        got_one = inward(share_one)
        xk, xs, yk, ys, token = weights_three(me, acts[0], (grads_a, there_a), (grads_b, there_b), after=[token])
        three = ((xk, swap(xs, "pa", 1)), (yk, swap(ys, "pa", 2)))
        share_two, token = add_second([two[0] + last_two[:1], two[1] + last_two[1:]], after=[token])
        got_two = inward(share_two)
        g_rows, small, token = rows_end(token)
        got_small = swap(small, "pa", 0)
        send_x, send_y, token = add_first(three, after=[token])
        last = (swap(send_x, "pa", 2), swap(send_y, "pa", 1))
        share_one, small, token = add_pair(share_one, got_one, (small, got_small), after=[token])
        got_one = between(share_one)
        got_small = swap(small, "pa", 1)
        outer, token = outer_end(token)
        share_two, small, token = add_pair(share_two, got_two, (small, got_small), after=[token])
        got_two = between(share_two)
        got_small = swap(small, "pa", 2)
        share_three, token = add_second([three[0] + last[:1], three[1] + last[1:]], (small, got_small), after=[token])
        got_three = inward(share_three)
        share_one, token = add_pair(share_one, got_one, after=[token])
        total_one = outward(share_one)
        share_three, token = add_pair(share_three, got_three, after=[token])
        got_three = between(share_three)
        share_two, token = add_pair(share_two, got_two, after=[token])
        total_two = outward(share_two)
        share_three, token = add_pair(share_three, got_three, after=[token])
        total_three = outward(share_three)
        small = total_three[D // pa_size :, :D]
        block = D // pa_size
        total_kv = jnp.concatenate([total_one[:block], total_one[block : 2 * block]], axis=1)
        total_ffn_out = total_one[2 * block :]
        second_part = 2 * block + block // 2
        total_ffn_in = jnp.concatenate(
            [total_two[first : first + block] for first in (0, block, second_part, second_part + block)], axis=1
        )
        total_out = jnp.concatenate([total_two[2 * block : second_part], total_two[second_part + 2 * block :]], axis=0)
        pieces = []
        for k in range(3):
            first = 3 * WIDE_A + WIDE_B * k
            pieces += [total_three[:block, WIDE_A * k : WIDE_A * k + WIDE_A], total_three[:block, first : first + WIDE_B]]
        total_qkv = jnp.concatenate(pieces, axis=1)
    else:
        partial = all_sum(partial, "pa")
        late, g_start, token = dec_end(partial, jnp.zeros_like(partial), token)
        late_all = lax.all_gather(late, "pb")
        grads_a, diagonal_a, token = back_of(0, FIRST, [token])
        grads_b, diagonal_b, token = back_of(FIRST, PAIRS - FIRST, [token])
        g_rows, small, token = rows_end(token)
        outer, token = outer_end(token)
        small = all_sum(all_sum(small, "pa"), "pb")
        g_heads = jnp.concatenate([g for k in range(3) for g in (grads_a[k], grads_b[k])], axis=1)
        total_kv = total_plain(share_over_pa(acts[4], across(g_pairs), 0))
        total_ffn_out = total_plain(share_over_pa(acts[3], across(branch), 1))
        total_ffn_in = total_plain(share_over_pa(acts[2], across(g_inner), 0))
        total_out = total_plain(share_over_pa(acts[1], across(low), 1))
        total_qkv = total_plain(share_over_pa(acts[0], across(g_heads), 0))

    d_qkv, d_out, d_query, d_cross, d_in, d_ffn, dec_small = outer
    dec_small = dec_small[0]
    dec_bias_rows = dec_small[3 * D :].reshape(H, STAT)[:, GROUP - ANS : GROUP]
    dec_bias_all = jnp.pad(jnp.transpose(dec_bias_rows[:, ::-1]), ((0, BUCKETS - ANS), (0, 0)))

    def own_part(vector, axis):
        height = vector.shape[0] // lax.axis_size(axis)
        return lax.dynamic_slice_in_dim(vector, lax.axis_index(axis) * height, height, axis=0)

    return (
        answer[None],
        g_rows.reshape(1, 1, SLOT, D),
        g_start[None],
        own_part(small[0], "pa"),
        total_qkv,
        jnp.transpose(small[4:16, :BUCKETS]),
        total_out,
        own_part(small[1], "pa"),
        total_ffn_in,
        total_ffn_out,
        own_part(small[2], "pa"),
        total_kv,
        own_part(dec_small[:D], "pb"),
        d_qkv,
        own_part(dec_bias_all, "pb"),
        d_out,
        own_part(dec_small[D : 2 * D], "pb"),
        d_query,
        d_cross,
        own_part(dec_small[2 * D : 3 * D], "pb"),
        d_in,
        d_ffn,
    )


def solution(mesh):
    copied = P()
    in_specs = (
        P("pb", "pa", None, None),
        P("pb", "pa"),
        P("pb", None, None),
        P("pb", None, None),
    ) + (copied,) * 19
    by_pa, by_pa_rows = P("pa"), P("pa", None)
    by_pb, by_pb_rows = P("pb"), P("pb", None)
    out_specs = (
        P("pb", None, None),
        P("pb", "pa", None, None),
        P("pb", None, None),
        by_pa,
        by_pa_rows,
        copied,
        by_pa_rows,
        by_pa,
        by_pa_rows,
        by_pa_rows,
        by_pa,
        by_pa_rows,
        by_pb,
        by_pb_rows,
        by_pb_rows,
        by_pb_rows,
        by_pb,
        by_pb_rows,
        by_pb_rows,
        by_pb,
        by_pb_rows,
        by_pb_rows,
    )
    return jax.shard_map(local, mesh=mesh, in_specs=in_specs, out_specs=out_specs, check_vma=False)
```

```python
import jax
import jax.numpy as jnp
import numpy as np
from jax import lax
from jax.experimental import pallas as pl
from jax.experimental.pallas import tpu as pltpu
from jax.sharding import PartitionSpec as P

D = 768
H = 12
HD = 64
FF = 3072
BUCKETS = 32
ANS = 20
SLOT = 512
PAIR = 2 * HD
PAIRS = H // 2
EDGE = 128
STRIP = 256
SPAN = 256
GROUP = 24
SENT = 40
STACK = H * GROUP
STAT = 128
STEPS = 4
WIDTH = FF // STEPS
FIRST = 4
EPS = 1e-06
MASKED = -1000000000.0
C_GELU = 0.7978845608028654
LOWER = jnp.bfloat16
WIDER = jnp.float32
EARLY = 7 * D + 2 * FF
LATE = 5 * D
AT = {
    "first": 0,
    "own": D,
    "second": 2 * D,
    "mix": 3 * D,
    "third": 4 * D,
    "hidden": 5 * D,
    "g_middle": 5 * D + FF,
    "g_inner": 6 * D + FF,
    "g_out": 6 * D + 2 * FF,
    "g_heads": 0,
    "g_after": 3 * D,
    "g_query": 4 * D,
}


def tile_classes(away):
    rows = [np.clip(EDGE * d - away, -(BUCKETS // 2), BUCKETS // 2 - 1) + BUCKETS // 2 for d in (-1, 0, 1)]
    return np.eye(BUCKETS, dtype=np.float32)[np.concatenate(rows)]


LANES = np.arange(SPAN)
PICK = tile_classes(np.where(LANES < EDGE, LANES, LANES - SPAN)).T
ENDS = np.repeat(np.eye(BUCKETS, dtype=np.float32)[[0, BUCKETS - 1]], EDGE, axis=0)
PICK_BACK = np.pad(np.concatenate([tile_classes(LANES - (EDGE - 1)), ENDS]), ((0, 0), (0, STAT - BUCKETS)))

SCALARS = pl.BlockSpec(memory_space=pltpu.SMEM)
ANY = pl.BlockSpec(memory_space=pl.ANY)
WHOLE = pl.BlockSpec(memory_space=pltpu.VMEM)
TOKEN = (8, 128)


def wide(*shape):
    return jax.ShapeDtypeStruct(shape, WIDER)


def narrow(*shape):
    return jax.ShapeDtypeStruct(shape, LOWER)


def run(name, body, ins, in_specs, outs, out_specs=None, after=(), grid=(), scratch=(), flops=10**9, mib=56, alias=None):
    count, extra, results = len(ins), len(after), len(outs)
    if out_specs is None:
        out_specs = [WHOLE] * results
    zeros = (lambda *s: (0, 0)) if grid else (lambda: (0, 0))

    def wrapped(*refs):
        refs[count + extra + results][...] = jnp.zeros(TOKEN, WIDER)
        body(*refs[:count], *refs[count + extra : count + extra + results], *refs[count + extra + results + 1 :])

    got = pl.pallas_call(
        wrapped,
        grid=grid,
        out_shape=tuple(outs) + (wide(*TOKEN),),
        in_specs=list(in_specs) + [ANY] * extra,
        out_specs=tuple(out_specs) + (pl.BlockSpec(TOKEN, zeros),),
        scratch_shapes=list(scratch),
        input_output_aliases=alias or {},
        compiler_params=pltpu.CompilerParams(vmem_limit_bytes=mib * 2**20),
        cost_estimate=pl.CostEstimate(flops=10 * flops, bytes_accessed=1, transcendentals=0),
        name=name,
    )(*ins, *after)
    return got


def product(left, right):
    return jnp.dot(left, right, preferred_element_type=WIDER)


def left_product(left, right):
    return lax.dot_general(left, right, (((0,), (0,)), ((), ())), preferred_element_type=WIDER)


def right_product(left, right):
    return lax.dot_general(left, right, (((1,), (1,)), ((), ())), preferred_element_type=WIDER)


def split_product(left, right, terms):
    total = None
    for k in range(terms):
        part = left.astype(LOWER)
        left = left - part.astype(WIDER)
        term = product(part, right)
        total = term if total is None else total + term
    return total


def silu_like(inner):
    square = inner * inner
    tanh = jnp.tanh(inner * (C_GELU + (C_GELU * 0.044715) * square))
    half = 0.5 + 0.5 * tanh
    value = inner * half
    slope = half + value * (1.0 - tanh) * (C_GELU + (3.0 * C_GELU * 0.044715) * square)
    return value, slope


def row_of(ref):
    return ref[...].reshape(1, D)


def scale_of(values):
    return lax.rsqrt(jnp.mean(values * values, axis=-1, keepdims=True) + EPS)


def norm_pull(values, gain, grad):
    scale = scale_of(values)
    lifted = grad * gain
    inside = jnp.sum(values * lifted, axis=-1, keepdims=True)
    back = scale * lifted - values * (scale * scale * scale * inside * (1.0 / D))
    return back, jnp.sum(grad * values * scale, axis=0, keepdims=True)


def fetch(pairs, sems):
    copies = [pltpu.make_async_copy(s, t, sems.at[k]) for k, (s, t) in enumerate(pairs)]
    for copy in copies:
        copy.start()
    return copies


def bias_tiles(u_ref, head):
    tiles = []
    for d in range(3):
        row = u_ref[pl.ds(head, 1), SPAN * d : SPAN * d + SPAN]
        spread = jnp.broadcast_to(row, (EDGE, SPAN))
        tiles.append(pltpu.roll(spread, 0, 1, stride=1, stride_axis=0)[:, :EDGE])
    return tiles


def bias_strip(tiles, low, high, first):
    columns = []
    for i in range(first, first + STRIP // EDGE):
        blocks = []
        for j in range(SLOT // EDGE):
            d = j - i
            if abs(d) <= 1:
                blocks.append(tiles[d + 1])
            else:
                blocks.append(jnp.full((EDGE, EDGE), low if d < 0 else high, WIDER))
        columns.append(jnp.concatenate(blocks, axis=0))
    return jnp.concatenate(columns, axis=1)


def strip_scores(n, keys, query, bias):
    raw = right_product(keys, query) + bias
    places = lax.broadcasted_iota(jnp.int32, (SLOT, STRIP), 0)
    return jnp.where(places < n, raw, MASKED)


def fill_rows(table_ref, pick_ref, u_ref):
    @pl.when(pl.program_id(0) == 0)
    def _():
        u_ref[...] = split_product(table_ref[...], pick_ref[...], 3)


def attn_fwd_kernel(n_ref, ends_ref, table_ref, pick_ref, q_ref, k_ref, v_ref, o_ref, st_ref, u_ref):
    fill_rows(table_ref, pick_ref, u_ref)
    n = n_ref[0]
    step = pl.program_id(0)
    values = jnp.transpose(v_ref[...])
    mixed = []
    for h in range(2):
        head = 2 * step + h
        low, high = ends_ref[head, 0], ends_ref[head, BUCKETS - 1]
        tiles = bias_tiles(u_ref, head)
        cols = slice(HD * h, HD * h + HD)
        keys = k_ref[:, cols]
        strips = []
        for i in range(0, SLOT // EDGE, STRIP // EDGE):
            lanes = slice(EDGE * i, EDGE * i + STRIP)
            query = q_ref[lanes, cols] * 0.125
            scores = strip_scores(n, keys, query, bias_strip(tiles, low, high, i))
            top = jnp.max(scores, axis=0, keepdims=True)
            powers = jnp.exp(scores - top)
            share = 1.0 / jnp.sum(powers, axis=0, keepdims=True)
            st_ref[0, 2 * h : 2 * h + 1, lanes] = top
            st_ref[0, 2 * h + 1 : 2 * h + 2, lanes] = share
            probs = (powers * share).astype(LOWER)
            strips.append(product(values[cols], probs))
        mixed.append(jnp.concatenate(strips, axis=1))
    o_ref[...] = jnp.transpose(jnp.concatenate(mixed, axis=0)).astype(LOWER)


def attn_bwd_kernel(base):
    def body(
        n_ref, ends_ref, table_ref, pick_ref, q_ref, k_ref, v_ref, g_ref, st_ref, gh_ref, gb_ref, u_ref
    ):
        fill_rows(table_ref, pick_ref, u_ref)
        n = n_ref[0]
        step = pl.program_id(0) + base
        keys_t = jnp.transpose(k_ref[...])
        rows = lax.broadcasted_iota(jnp.int32, (EDGE, EDGE), 0)
        columns = lax.broadcasted_iota(jnp.int32, (EDGE, EDGE), 1)
        mirror = jnp.where(rows + columns == EDGE - 1, 1.0, 0.0).astype(LOWER)
        grad_queries = []
        gb_ref[0, 2:8, :] = jnp.zeros((6, 4 * SPAN), WIDER)
        for h in range(2):
            head = 2 * step + h
            low, high = ends_ref[head, 0], ends_ref[head, BUCKETS - 1]
            tiles = bias_tiles(u_ref, head)
            cols = slice(HD * h, HD * h + HD)
            keys = k_ref[:, cols]
            values = v_ref[:, cols]
            grad_keys = jnp.zeros((SLOT, HD), WIDER)
            grad_values = jnp.zeros((SLOT, HD), WIDER)
            strips = []
            sums = {}
            for i in range(0, SLOT // EDGE, STRIP // EDGE):
                lanes = slice(EDGE * i, EDGE * i + STRIP)
                query = q_ref[lanes, cols]
                grad = g_ref[lanes, cols]
                scores = strip_scores(n, keys, query * 0.125, bias_strip(tiles, low, high, i))
                top = st_ref[0, 2 * h : 2 * h + 1, lanes]
                share = st_ref[0, 2 * h + 1 : 2 * h + 2, lanes]
                probs = jnp.exp(scores - top) * share
                grad_probs = right_product(values, grad)
                weighted = jnp.sum(probs * grad_probs, axis=0, keepdims=True)
                rounded = (probs * (grad_probs - weighted)).astype(LOWER)
                strips.append(product(keys_t[cols], rounded))
                grad_keys += product(rounded, query)
                grad_values += product(probs.astype(LOWER), grad)
                spread = rounded.astype(WIDER)
                for c in range(STRIP // EDGE):
                    for j in range(SLOT // EDGE):
                        d = min(max(j - i - c, -2), 2)
                        block = spread[EDGE * j : EDGE * j + EDGE, EDGE * c : EDGE * c + EDGE]
                        sums[d] = sums[d] + block if d in sums else block
            grad_queries.append(jnp.concatenate(strips, axis=1))
            gh_ref[1, :, cols] = (grad_keys * 0.125).astype(LOWER)
            gh_ref[2, :, cols] = grad_values.astype(LOWER)
            empty = jnp.zeros((EDGE, SPAN - EDGE), WIDER)
            band = jnp.concatenate([sums[-1], sums[0], sums[1]], axis=1)
            upper = band.astype(LOWER)
            lower = (band - upper.astype(WIDER)).astype(LOWER)
            mirrored = product(mirror, upper) + product(mirror, lower)
            for d in range(3):
                spread = jnp.concatenate([mirrored[:, EDGE * d : EDGE * d + EDGE], empty], axis=1)
                turned = pltpu.roll(spread, 0, 1, stride=1, stride_axis=0)
                gb_ref[0, h : h + 1, SPAN * d : SPAN * d + SPAN] = jnp.sum(turned, axis=0, keepdims=True)
            for place, d in ((3 * SPAN, -2), (3 * SPAN + EDGE, 2)):
                gb_ref[0, h : h + 1, place : place + EDGE] = jnp.sum(sums[d], axis=0, keepdims=True)
        gh_ref[0] = (jnp.transpose(jnp.concatenate(grad_queries, axis=0)) * 0.125).astype(LOWER)

    return body


def columns_at(first):
    return pl.BlockSpec((SLOT, PAIR), lambda s: (0, first + s))


def stats_at(first):
    return pl.BlockSpec((1, 4, SLOT), lambda s: (first + s, 0, 0))


def attention(count, table, pick, heads, after=()):
    return run(
        "enc_attention",
        attn_fwd_kernel,
        [count, table, table, pick, heads, heads, heads],
        [SCALARS, SCALARS, WHOLE, WHOLE, columns_at(0), columns_at(PAIRS), columns_at(2 * PAIRS)],
        [narrow(SLOT, D), wide(PAIRS, 4, SLOT)],
        [columns_at(0), stats_at(0)],
        after=after,
        grid=(PAIRS,),
        scratch=[pltpu.VMEM((H, 3 * SPAN), WIDER)],
        flops=2 * 2 * H * SLOT * SLOT * HD * 4,
    )


def attention_back(count, table, pick, heads, grad_mixed, stats, base, half, begun=None, after=()):
    ins = [count, table, table, pick, heads, heads, heads, grad_mixed, stats]
    specs = [columns_at(base), columns_at(PAIRS + base), columns_at(2 * PAIRS + base), columns_at(base), stats_at(base)]
    body = attn_bwd_kernel(base)
    if begun is not None:
        ins.append(begun)
        specs.append(ANY)
        inner = body

        def body(*refs):
            inner(*refs[:9], *refs[10:])

    return run(
        "enc_attention_back",
        body,
        ins,
        [SCALARS, SCALARS, WHOLE, WHOLE] + specs,
        [narrow(3, SLOT, D), wide(half, 8, 4 * SPAN)],
        [pl.BlockSpec((3, SLOT, PAIR), lambda s: (0, 0, base + s)), pl.BlockSpec((1, 8, 4 * SPAN), lambda s: (s, 0, 0))],
        after=after,
        grid=(half,),
        scratch=[pltpu.VMEM((H, 3 * SPAN), WIDER)],
        flops=2 * 5 * H * SLOT * SLOT * HD * 4,
        alias={9: 0} if begun is not None else None,
    )


def ffn_kernel(
    x_ref, mixed_ref, wo_ref, g2_ref, in_ref, out_ref, g3_ref, kv_any,
    after_ref, second_ref, slope_ref, hidden_ref, final_ref, third_ref, pairs_ref,
    kv_ref, sems,
):
    step = pl.program_id(0)
    copy = pltpu.make_async_copy(kv_any, kv_ref, sems.at[0])

    @pl.when(step == 0)
    def _():
        copy.start()
        after = x_ref[...].astype(WIDER) + product(mixed_ref[...], wo_ref[...])
        after_ref[...] = after
        final_ref[...] = after
        second_ref[...] = (after * scale_of(after) * row_of(g2_ref)).astype(LOWER)

    value, slope = silu_like(product(second_ref[...], in_ref[...]))
    slope_ref[...] = slope.astype(LOWER)
    hidden = value.astype(LOWER)
    hidden_ref[...] = hidden
    final_ref[...] += product(hidden, out_ref[...])

    @pl.when(step == STEPS - 1)
    def _():
        final = final_ref[...]
        third = (final * scale_of(final) * row_of(g3_ref)).astype(LOWER)
        third_ref[...] = third
        copy.wait()
        pairs_ref[...] = product(third, kv_ref[...]).astype(LOWER)


def whole(*shape):
    return pl.BlockSpec(shape, lambda s: (0,) * len(shape))


def feed_forward(x, mixed, wo, gain2, ffn_in, ffn_out, gain3, kv):
    rows = whole(SLOT, D)
    by_columns = pl.BlockSpec((SLOT, WIDTH), lambda s: (0, s))
    return run(
        "enc_ffn",
        ffn_kernel,
        [x, mixed, wo, gain2, ffn_in, ffn_out, gain3, kv],
        [rows, rows, whole(D, D), whole(D), pl.BlockSpec((D, WIDTH), lambda s: (0, s))]
        + [pl.BlockSpec((WIDTH, D), lambda s: (s, 0)), whole(D), ANY],
        [wide(SLOT, D), narrow(SLOT, D), narrow(SLOT, FF), narrow(SLOT, FF), wide(SLOT, D), narrow(SLOT, D), narrow(SLOT, 2 * D)],
        [rows, rows, by_columns, by_columns, rows, rows, whole(SLOT, 2 * D)],
        grid=(STEPS,),
        scratch=[pltpu.VMEM((D, 2 * D), LOWER), pltpu.SemaphoreType.DMA((1,))],
        flops=2 * SLOT * D * (D + 2 * FF + 2 * D),
    )


def kv_back_kernel(gp_ref, kv_ref, final_ref, g3_ref, gfinal_ref, branch_ref, gain_ref):
    back, gain = norm_pull(final_ref[...], row_of(g3_ref), right_product(gp_ref[...], kv_ref[...]))
    gfinal_ref[...] = back
    branch_ref[...] = back.astype(LOWER)
    gain_ref[...] = gain


def kv_back(g_pairs, kv, final, gain3, after=()):
    return run(
        "enc_kv_back",
        kv_back_kernel,
        [g_pairs, kv, final, gain3],
        [WHOLE] * 4,
        [wide(SLOT, D), narrow(SLOT, D), wide(1, D)],
        after=after,
        flops=0,
    )


def ffn_back_kernel(
    branch_ref, out_ref, slope_ref, in_ref, after_ref, g2_ref, gfinal_ref, wo_any,
    ginner_ref, gafter_ref, low_ref, gmixed_ref, gain_ref,
    total_ref, wo_ref, sems,
):
    step = pl.program_id(0)
    copy = pltpu.make_async_copy(wo_any, wo_ref, sems.at[0])

    @pl.when(step == 0)
    def _():
        copy.start()
        total_ref[...] = jnp.zeros((SLOT, D), WIDER)

    grad = right_product(branch_ref[...], out_ref[...])
    inner = (grad * slope_ref[...].astype(WIDER)).astype(LOWER)
    ginner_ref[...] = inner
    total_ref[...] += right_product(inner, in_ref[...])

    @pl.when(step == STEPS - 1)
    def _():
        back, gain = norm_pull(after_ref[...], row_of(g2_ref), total_ref[...])
        gain_ref[...] = gain
        g_after = gfinal_ref[...] + back
        gafter_ref[...] = g_after
        low = g_after.astype(LOWER)
        low_ref[...] = low
        copy.wait()
        gmixed_ref[...] = right_product(low, wo_ref[...]).astype(LOWER)


def ffn_back(branch, ffn_out, slope, ffn_in, after_rows, gain2, g_final, wo, after=()):
    rows = whole(SLOT, D)
    by_columns = pl.BlockSpec((SLOT, WIDTH), lambda s: (0, s))
    return run(
        "enc_ffn_back",
        ffn_back_kernel,
        [branch, ffn_out, slope, ffn_in, after_rows, gain2, g_final, wo],
        [rows, pl.BlockSpec((WIDTH, D), lambda s: (s, 0)), by_columns, pl.BlockSpec((D, WIDTH), lambda s: (0, s))]
        + [rows, whole(D), rows, ANY],
        [narrow(SLOT, FF), wide(SLOT, D), narrow(SLOT, D), narrow(SLOT, D), wide(1, D)],
        [by_columns, rows, rows, rows, whole(1, D)],
        after=after,
        grid=(STEPS,),
        scratch=[pltpu.VMEM((SLOT, D), WIDER), pltpu.VMEM((D, D), LOWER), pltpu.SemaphoreType.DMA((1,))],
        flops=2 * SLOT * D * (D + 2 * FF),
    )


def rows_back_kernel(
    g_ref, w_ref, x_ref, g1_ref, gafter_ref, gain2_ref, gain3_ref, da_ref, db_ref, pick_ref,
    grows_ref, small_ref, total_ref,
):
    step = pl.program_id(0)

    @pl.when(step == 0)
    def _():
        total_ref[...] = jnp.zeros((SLOT, D), WIDER)

    total_ref[...] += right_product(g_ref[0], w_ref[...])

    @pl.when(step == 2)
    def _():
        back, gain = norm_pull(x_ref[...].astype(WIDER), row_of(g1_ref), total_ref[...])
        grows_ref[...] = gafter_ref[...] + back
        sums = [ref[k, :2] for ref in (da_ref, db_ref) for k in range(ref.shape[0])]
        table = split_product(jnp.concatenate(sums, axis=0), pick_ref[...], 2)
        small_ref[...] = jnp.zeros((16, D), WIDER)
        small_ref[0:1] = gain
        small_ref[1:2] = gain2_ref[...]
        small_ref[2:3] = gain3_ref[...]
        small_ref[4:16, :STAT] = table


def rows_back(grads, qkv, x, gain1, g_after, gain2, gain3, diagonals, pick_back, after=()):
    rows = whole(SLOT, D)
    return run(
        "enc_rows_back",
        rows_back_kernel,
        [grads, qkv, x, gain1, g_after, gain2, gain3, diagonals[0], diagonals[1], pick_back],
        [pl.BlockSpec((1, SLOT, D), lambda s: (s, 0, 0)), pl.BlockSpec((D, D), lambda s: (0, s)), rows, whole(D), rows]
        + [whole(1, D), whole(1, D), whole(*diagonals[0].shape), whole(*diagonals[1].shape), whole(4 * SPAN, STAT)],
        [wide(SLOT, D), wide(16, D)],
        [rows, whole(16, D)],
        after=after,
        grid=(3,),
        scratch=[pltpu.VMEM((SLOT, D), WIDER)],
        flops=0,
    )


def head_lanes(h):
    lanes = lax.broadcasted_iota(jnp.int32, (GROUP, D), 1)
    return (lanes >= h * HD) & (lanes < (h + 1) * HD)


def stack_heads(flat):
    return jnp.concatenate([jnp.where(head_lanes(h), flat, 0.0) for h in range(H)], axis=0)


def merge_heads(stacked):
    total = jnp.zeros((GROUP, D), WIDER)
    for h in range(H):
        total = total + jnp.where(head_lanes(h), stacked[GROUP * h : GROUP * h + GROUP], 0.0)
    return total


def lanes_to_column(stat):
    lanes = lax.broadcasted_iota(jnp.int32, (GROUP, STAT), 1)
    parts = [jnp.sum(jnp.where(lanes == h, stat, 0.0), axis=1, keepdims=True) for h in range(H)]
    return jnp.concatenate(parts, axis=0)


def column_to_lanes(column, first):
    lanes = lax.broadcasted_iota(jnp.int32, (GROUP, STAT), 1)
    total = jnp.zeros((GROUP, STAT), WIDER)
    for h in range(H):
        total = total + jnp.where(lanes == first + h, column[GROUP * h : GROUP * h + GROUP], 0.0)
    return total


def spread_heads(stat):
    rows = lax.broadcasted_iota(jnp.int32, (STAT, D), 0) * HD
    lanes = lax.broadcasted_iota(jnp.int32, (STAT, D), 1)
    spread = jnp.where((lanes >= rows) & (lanes < rows + HD), 1.0, 0.0).astype(LOWER)
    return split_product(stat, spread, 2)


def own_scores(query, keys, table_ref):
    raw = right_product(query, keys)
    rows = lax.broadcasted_iota(jnp.int32, (GROUP, GROUP), 0)
    columns = lax.broadcasted_iota(jnp.int32, (GROUP, GROUP), 1)
    away = rows - columns
    parts = []
    for h in range(H):
        bias = jnp.full((GROUP, GROUP), table_ref[h, 0], WIDER)
        for d in range(1, GROUP):
            bias = jnp.where(away == d, table_ref[h, d], bias)
        part = raw[GROUP * h : GROUP * h + GROUP] + bias
        parts.append(jnp.where(away >= 0, part, MASKED))
    scores = jnp.concatenate(parts, axis=0)
    powers = jnp.exp(scores - jnp.max(scores, axis=1, keepdims=True))
    return powers / jnp.sum(powers, axis=1, keepdims=True)


def padded(ref, pad_ref):
    pad_ref[...] = jnp.zeros((GROUP, D), WIDER)
    pad_ref[:ANS] = ref[...].astype(WIDER)
    return pad_ref[...]


def answer_rows(width):
    return lax.broadcasted_iota(jnp.int32, (GROUP, width), 0) < ANS


def dec_self_kernel(
    table_ref, x_ref, g1_ref, g2_ref, qkv_any, out_any, query_any,
    after_ref, lefts_ref, heads_ref, query_ref,
    qkv_ref, out_ref, cross_ref, pad_ref, sems,
):
    copies = fetch(((qkv_any, qkv_ref), (out_any, out_ref), (query_any, cross_ref)), sems)
    start = padded(x_ref, pad_ref)
    first = (start * scale_of(start) * row_of(g1_ref)).astype(LOWER)
    copies[0].wait()
    heads = product(first, qkv_ref[...]).astype(LOWER)
    heads_ref[...] = heads
    query = stack_heads(heads.astype(WIDER)[:, :D] * 0.125).astype(LOWER)
    probs = own_scores(query, heads[:, D : 2 * D], table_ref)
    own = merge_heads(product(probs.astype(LOWER), heads[:, 2 * D :]))
    own = jnp.where(answer_rows(D), own, 0.0).astype(LOWER)
    copies[1].wait()
    after = start + product(own, out_ref[...])
    after_ref[...] = after
    second = (after * scale_of(after) * row_of(g2_ref)).astype(LOWER)
    copies[2].wait()
    query_ref[...] = product(second, cross_ref[...]).astype(LOWER)
    lefts_ref[:, :D] = first
    lefts_ref[:, D : 2 * D] = own
    lefts_ref[:, 2 * D :] = second


def masked_cross(n_ref, query_ref, pairs_ref):
    query = stack_heads(query_ref[...].astype(WIDER) * 0.125).astype(LOWER)
    raw = right_product(query, pairs_ref[:, :D])
    places = lax.broadcasted_iota(jnp.int32, (STACK, SLOT), 1)
    return query, jnp.where(places < n_ref[0], raw, MASKED)


def cross_kernel(n_ref, query_ref, pairs_ref, packed_ref):
    unused, scores = masked_cross(n_ref, query_ref, pairs_ref)
    top = jnp.max(scores, axis=1, keepdims=True)
    powers = jnp.exp(scores - top)
    total = jnp.sum(powers, axis=1, keepdims=True)
    probs = (powers / total).astype(LOWER)
    packed_ref[:, :D] = merge_heads(product(probs, pairs_ref[:, D:]))
    packed_ref[:, D:] = column_to_lanes(top, 0) + column_to_lanes(total, STAT // 2)


def dec_mid_kernel(
    parts_ref, after_ref, cot_ref, g3_ref, lefts_ref, cross_any, in_any, out_any,
    answer_ref, early_ref, mix_ref, gmix_ref, gmid_ref, stat_ref, gain_ref,
    cross_ref, in_ref, out_ref, pad_ref, sems,
):
    copies = fetch(((cross_any, cross_ref), (in_any, in_ref), (out_any, out_ref)), sems)
    size = parts_ref.shape[0]
    used = lax.broadcasted_iota(jnp.int32, (GROUP, STAT), 1) < H
    tops = [parts_ref[k, :, D:] for k in range(size)]
    totals = [pltpu.roll(stat, STAT // 2, 1) for stat in tops]
    top = tops[0]
    for k in range(1, size):
        top = jnp.maximum(top, tops[k])
    weights = [jnp.where(used, totals[k] * jnp.exp(tops[k] - top), 0.0) for k in range(size)]
    total = weights[0]
    for k in range(1, size):
        total = total + weights[k]
    total = jnp.where(used, total, 1.0)
    mix = jnp.zeros((GROUP, D), WIDER)
    for k in range(size):
        mix = mix + parts_ref[k, :, :D] * spread_heads(weights[k] / total)
    mix_ref[...] = mix
    stat_ref[:, :STAT] = jnp.where(used, top, 0.0)
    stat_ref[:, STAT:] = total
    mix_low = mix.astype(LOWER)
    copies[0].wait()
    middle = after_ref[...] + product(mix_low, cross_ref[...])
    third = (middle * scale_of(middle) * row_of(g3_ref)).astype(LOWER)
    copies[1].wait()
    inner = product(third, in_ref[...])
    value, slope = silu_like(inner)
    hidden = value.astype(LOWER)
    copies[2].wait()
    answer = (middle + product(hidden, out_ref[...])).astype(LOWER)
    answer_ref[...] = answer[:ANS]
    grad = padded(cot_ref, pad_ref)
    out_low = grad.astype(LOWER)
    g_inner = (right_product(out_low, out_ref[...]) * slope).astype(LOWER)
    back, gain = norm_pull(middle, row_of(g3_ref), right_product(g_inner, in_ref[...]))
    gain_ref[...] = gain
    g_middle = grad + back
    gmid_ref[...] = g_middle
    middle_low = g_middle.astype(LOWER)
    gmix_ref[...] = right_product(middle_low, cross_ref[...]).astype(LOWER)

    def store(name, rows):
        early_ref[:, AT[name] : AT[name] + rows.shape[1]] = rows

    def kept(rows):
        return jnp.where(answer_rows(rows.shape[1]), rows.astype(WIDER), 0.0).astype(LOWER)

    early_ref[:, : 3 * D] = kept(lefts_ref[...])
    store("mix", kept(mix_low))
    store("third", kept(third))
    store("hidden", kept(hidden))
    store("g_middle", middle_low)
    store("g_inner", g_inner)
    store("g_out", out_low)


def cross_back_kernel(n_ref, query_ref, pairs_ref, gmix_ref, mix_ref, stat_ref, gpairs_ref, partial_ref):
    query, scores = masked_cross(n_ref, query_ref, pairs_ref)
    top = lanes_to_column(stat_ref[:, :STAT])
    total = lanes_to_column(stat_ref[:, STAT:])
    probs = jnp.exp(scores - top) / total
    grad = stack_heads(gmix_ref[...].astype(WIDER))
    weighted = jnp.sum(grad * jnp.concatenate([mix_ref[...]] * H, axis=0), axis=1, keepdims=True)
    grad = grad.astype(LOWER)
    grad_probs = right_product(grad, pairs_ref[:, D:])
    rounded = (probs * (grad_probs - weighted)).astype(LOWER)
    gpairs_ref[:, :D] = left_product(rounded, query).astype(LOWER)
    gpairs_ref[:, D:] = left_product(probs.astype(LOWER), grad).astype(LOWER)
    partial_ref[...] = merge_heads(product(rounded, pairs_ref[:, :D])) * 0.125


def dec_back_kernel(
    table_ref, x_ref, part_ref, got_ref, after_ref, gmid_ref, heads_ref,
    g1_ref, g2_ref, gain3_ref, query_any, out_any, qkv_any,
    late_ref, gstart_ref,
    cross_ref, out_ref, qkv_ref, pad_ref, sems,
):
    copies = fetch(((query_any, cross_ref), (out_any, out_ref), (qkv_any, qkv_ref)), sems)
    g_query = (part_ref[...] + got_ref[...]).astype(LOWER)
    copies[0].wait()
    back, gain2 = norm_pull(after_ref[...], row_of(g2_ref), right_product(g_query, cross_ref[...]))
    g_after = gmid_ref[...] + back
    after_low = g_after.astype(LOWER)
    copies[1].wait()
    g_own = stack_heads(right_product(after_low, out_ref[...])).astype(LOWER)
    heads = heads_ref[...]
    query = stack_heads(heads.astype(WIDER)[:, :D] * 0.125).astype(LOWER)
    probs = own_scores(query, heads[:, D : 2 * D], table_ref)
    grad_probs = right_product(g_own, heads[:, 2 * D :])
    rounded = (probs * (grad_probs - jnp.sum(probs * grad_probs, axis=1, keepdims=True))).astype(LOWER)
    g_q = (merge_heads(product(rounded, heads[:, D : 2 * D])) * 0.125).astype(LOWER)
    g_k = left_product(rounded, query).astype(LOWER)
    g_v = left_product(probs.astype(LOWER), g_own).astype(LOWER)
    g_heads = jnp.concatenate([g_q, g_k, g_v], axis=1)
    copies[2].wait()
    start = padded(x_ref, pad_ref)
    back, gain1 = norm_pull(start, row_of(g1_ref), right_product(g_heads, qkv_ref[...]))
    gstart_ref[...] = (g_after + back)[:ANS]
    spread = rounded.astype(WIDER)
    rows = lax.broadcasted_iota(jnp.int32, (GROUP, GROUP), 0)
    columns = lax.broadcasted_iota(jnp.int32, (GROUP, GROUP), 1)
    mirror = jnp.where(rows + columns == GROUP - 1, 1.0, 0.0).astype(LOWER)
    empty = jnp.zeros((GROUP, STAT - GROUP), WIDER)
    tables = []
    for h in range(H):
        part = product(mirror, spread[GROUP * h : GROUP * h + GROUP].astype(LOWER))
        turned = pltpu.roll(jnp.concatenate([part, empty], axis=1), 0, 1, stride=1, stride_axis=0)
        tables.append(jnp.sum(turned, axis=0, keepdims=True))
    small = jnp.concatenate([gain1, gain2, gain3_ref[...]] + tables, axis=1)
    places = lax.broadcasted_iota(jnp.int32, (GROUP, LATE), 0)
    late = jnp.concatenate([g_heads, after_low, g_query], axis=1).astype(WIDER)
    late = jnp.concatenate([jnp.where(places == ANS, small, late), jnp.zeros((SENT - GROUP, LATE), WIDER)], axis=0)
    late_ref[...] = late.astype(LOWER)


def dec_outer_kernel(size):
    part = D // size

    def body(me_ref, *refs):
        me = me_ref[0]
        qkv_ref, out_ref, query_ref, cross_ref, in_ref, ffn_ref, small_ref, early_ref, late_ref = refs[2:]
        early_ref[...] = jnp.concatenate([refs[0][s].astype(WIDER) for s in range(size)], axis=0).astype(LOWER)
        late = [refs[1][s].astype(WIDER)[:GROUP] for s in range(size)]
        late_ref[...] = jnp.concatenate(late, axis=0).astype(LOWER)
        rows = lax.broadcasted_iota(jnp.int32, (part, D), 0) + me * part
        lanes = lax.broadcasted_iota(jnp.int32, (part, D), 1)
        picked = jnp.where(rows == lanes, 1.0, 0.0).astype(LOWER)

        def outer(name, right):
            left = right_product(picked, early_ref[:, AT[name] : AT[name] + D]).astype(LOWER)
            return product(left, right)

        qkv_ref[...] = outer("first", late_ref[:, : 3 * D])
        out_ref[...] = outer("own", late_ref[:, AT["g_after"] : AT["g_after"] + D])
        query_ref[...] = outer("second", late_ref[:, AT["g_query"] : AT["g_query"] + D])
        cross_ref[...] = outer("mix", early_ref[:, AT["g_middle"] : AT["g_middle"] + D])
        in_ref[...] = outer("third", early_ref[:, AT["g_inner"] : AT["g_inner"] + FF])
        height = FF // size
        first = pl.multiple_of(AT["hidden"] + me * height, 128)
        ffn_ref[...] = left_product(early_ref[:, pl.ds(first, height)], early_ref[:, AT["g_out"] : AT["g_out"] + D])
        total = jnp.zeros((1, LATE), WIDER)
        for k in range(size):
            total = total + late[k][ANS : ANS + 1]
        small_ref[...] = total

    return body


def held(*shapes):
    return [pltpu.VMEM(shape, LOWER) for shape in shapes] + [
        pltpu.VMEM((GROUP, D), WIDER),
        pltpu.SemaphoreType.DMA((len(shapes),)),
    ]


def dec_self(table, answers, gain1, gain2, qkv, out, query, after=()):
    return run(
        "dec_self",
        dec_self_kernel,
        [table, answers, gain1, gain2, qkv, out, query],
        [SCALARS] + [WHOLE] * 3 + [ANY] * 3,
        [wide(GROUP, D), narrow(GROUP, 3 * D), narrow(GROUP, 3 * D), narrow(GROUP, D)],
        after=after,
        scratch=held((D, 3 * D), (D, D), (D, D)),
        flops=10**9,
    )


def cross(count, query, pairs, after=()):
    return run(
        "cross",
        cross_kernel,
        [count, query, pairs],
        [SCALARS, WHOLE, WHOLE],
        [wide(GROUP, D + STAT)],
        after=after,
        flops=4 * STACK * SLOT * D,
    )


def dec_mid(parts, after_rows, cotangent, gain3, lefts, cross_out, ffn_in, ffn_out, after=()):
    return run(
        "dec_mid",
        dec_mid_kernel,
        [parts, after_rows, cotangent, gain3, lefts, cross_out, ffn_in, ffn_out],
        [WHOLE] * 5 + [ANY] * 3,
        [narrow(ANS, D), narrow(GROUP, EARLY), wide(GROUP, D), narrow(GROUP, D), wide(GROUP, D), wide(GROUP, 2 * STAT), wide(1, D)],
        after=after,
        scratch=held((D, D), (D, FF), (FF, D)),
        flops=4 * 10**9,
    )


def cross_back(count, query, pairs, g_mix, mix, stat, after=()):
    return run(
        "cross_back",
        cross_back_kernel,
        [count, query, pairs, g_mix, mix, stat],
        [SCALARS] + [WHOLE] * 5,
        [narrow(SLOT, 2 * D), wide(GROUP, D)],
        after=after,
        flops=10 * STACK * SLOT * D,
    )


def dec_back(table, answers, part, got, after_rows, g_middle, heads, gain1, gain2, g_gain3, query, out, qkv, after=()):
    return run(
        "dec_back",
        dec_back_kernel,
        [table, answers, part, got, after_rows, g_middle, heads, gain1, gain2, g_gain3, query, out, qkv],
        [SCALARS] + [WHOLE] * 9 + [ANY] * 3,
        [narrow(SENT, LATE), wide(ANS, D)],
        after=after,
        scratch=held((D, D), (D, D), (D, 3 * D)),
        flops=0,
    )


def dec_outer(me, early, late, size, after=()):
    part = D // size
    return run(
        "dec_outer",
        dec_outer_kernel(size),
        [me, early, late],
        [SCALARS, WHOLE, WHOLE],
        [wide(part, 3 * D), wide(part, D), wide(part, D), wide(part, D), wide(part, FF), wide(FF // size, D), wide(1, LATE)],
        after=after,
        scratch=[pltpu.VMEM((size * GROUP, EARLY), LOWER), pltpu.VMEM((size * GROUP, LATE), LOWER)],
        flops=8 * 10**9,
    )


PLACES = [(0, 0), (0, 1), (1, 0), (1, 1)]


def place_of(me, there):
    return me ^ (4 * there[0] + 2 * there[1])


def turned_rows(me, acts, block):
    lanes = lax.broadcasted_iota(jnp.int32, (block, D), 1)
    rows = lax.broadcasted_iota(jnp.int32, (block, D), 0)
    picked = [jnp.where(lanes - rows == place_of(me, t) * block, 1.0, 0.0).astype(LOWER) for t in PLACES]
    picked = jnp.concatenate(picked, axis=0)
    return jnp.concatenate([right_product(picked, act).astype(LOWER) for act in acts], axis=1)


def target(there, x_refs, y_refs):
    dy, dx = there
    return (x_refs[dx].at[dy], y_refs[dy].at[dx])


def one_kernel(me_ref, t_own, t_par, p_own, p_par, h_own, h_par, b_own, b_par, xk, xs, yk, ys, t, p, h, b, sems):
    me = me_ref[0]
    block = FF // 8
    pairs = [(t_own, t.at[0]), (t_par, t.at[1]), (p_own, p.at[:SLOT]), (p_par, p.at[SLOT:])]
    pairs += [(b_own, b.at[:SLOT]), (b_par, b.at[SLOT:])]
    for k, there in enumerate(PLACES):
        lanes = pl.ds(pl.multiple_of(place_of(me, there) * block, 128), block)
        pairs += [(h_own.at[:, lanes], h.at[k, :SLOT]), (h_par.at[:, lanes], h.at[k, SLOT:])]
    copies = fetch(pairs, sems)
    copies[0].wait()
    copies[1].wait()
    height = D // 8
    left = turned_rows(me, (t[0], t[1]), height)
    copies[2].wait()
    copies[3].wait()
    for c in range(2):
        grad = product(left, p[:, D * c : D * c + D]).astype(LOWER)
        for k, there in enumerate(PLACES):
            to, unused = target(there, (xk, xs), (yk, ys))
            to[height * c : height * c + height] = grad[height * k : height * k + height]
    copies[4].wait()
    copies[5].wait()
    for k, there in enumerate(PLACES):
        copies[6 + 2 * k].wait()
        copies[7 + 2 * k].wait()
        grad = left_product(h[k], b[...]).astype(LOWER)
        to_x, to_y = target(there, (xk, xs), (yk, ys))
        to_x[2 * height : 3 * height] = grad[:height]
        to_y[...] = grad[height:]


def two_kernel(me_ref, s_own, s_par, i_own, i_par, m_own, m_par, l_own, l_par, xk, xs, yk, ys, s, i, m, l, sems):
    me = me_ref[0]
    pairs = [(s_own, s.at[0]), (s_par, s.at[1])]
    for c in range(4):
        lanes = slice(D * c, D * c + D)
        pairs += [(i_own.at[:, lanes], i.at[c, :SLOT]), (i_par.at[:, lanes], i.at[c, SLOT:])]
    pairs += [(m_own, m.at[0]), (m_par, m.at[1]), (l_own, l.at[:SLOT]), (l_par, l.at[SLOT:])]
    copies = fetch(pairs, sems)
    copies[0].wait()
    copies[1].wait()
    height = D // 8
    half = height // 2
    left = turned_rows(me, (s[0], s[1]), height)
    for c in range(4):
        copies[2 + 2 * c].wait()
        copies[3 + 2 * c].wait()
        grad = product(left, i[c]).astype(LOWER)
        for k, there in enumerate(PLACES):
            to = target(there, (xk, xs), (yk, ys))[c // 2]
            to[height * (c % 2) : height * (c % 2) + height] = grad[height * k : height * k + height]
    for k in range(10, 14):
        copies[k].wait()
    left = turned_rows(me, (m[0], m[1]), height)
    grad = product(left, l[...]).astype(LOWER)
    for k, there in enumerate(PLACES):
        for to, first in zip(target(there, (xk, xs), (yk, ys)), (0, half)):
            to[2 * height : 2 * height + half] = grad[height * k + first : height * k + first + half]


def three_kernel(me_ref, f_own, f_par, g_own, g_par, xk, xs, yk, ys, f, g, sems):
    me = me_ref[0]
    pairs = [(f_own, f.at[0]), (f_par, f.at[1])]
    for c in range(3):
        pairs += [(g_own.at[c], g.at[c, :SLOT]), (g_par.at[c], g.at[c, SLOT:])]
    copies = fetch(pairs, sems)
    copies[0].wait()
    copies[1].wait()
    height = D // 8
    half = D // 2
    left = turned_rows(me, (f[0], f[1]), height)
    for c in range(3):
        copies[2 + 2 * c].wait()
        copies[3 + 2 * c].wait()
        grad = product(left, g[c]).astype(LOWER)
        for k, there in enumerate(PLACES):
            to_x, to_y = target(there, (xk, xs), (yk, ys))
            block = grad[height * k : height * k + height]
            if c == 0:
                to_x[:, :D] = block
            elif c == 1:
                to_x[:, D:] = block[:, :half]
                to_y[:, :half] = block[:, half:]
            else:
                to_y[:, half:] = block


def weights_one(me, third, g_pairs, hidden, branch, after=()):
    out = narrow(2, 3 * D // 8, D)
    return run(
        "weights_one",
        one_kernel,
        [me, *third, *g_pairs, *hidden, *branch],
        [SCALARS] + [ANY] * 8,
        [out] * 4,
        after=after,
        scratch=[
            pltpu.VMEM((2, SLOT, D), LOWER),
            pltpu.VMEM((2 * SLOT, 2 * D), LOWER),
            pltpu.VMEM((4, 2 * SLOT, FF // 8), LOWER),
            pltpu.VMEM((2 * SLOT, D), LOWER),
            pltpu.SemaphoreType.DMA((14,)),
        ],
        flops=4 * 10**9,
    )


def weights_two(me, second, g_inner, mixed, low, after=()):
    out = narrow(2, 5 * D // 16, D)
    return run(
        "weights_two",
        two_kernel,
        [me, *second, *g_inner, *mixed, *low],
        [SCALARS] + [ANY] * 8,
        [out] * 4,
        after=after,
        scratch=[
            pltpu.VMEM((2, SLOT, D), LOWER),
            pltpu.VMEM((4, 2 * SLOT, D), LOWER),
            pltpu.VMEM((2, SLOT, D), LOWER),
            pltpu.VMEM((2 * SLOT, D), LOWER),
            pltpu.SemaphoreType.DMA((14,)),
        ],
        flops=0,
    )


def weights_three(me, first, grads, after=()):
    out = narrow(2, D // 8, 3 * D // 2)
    return run(
        "weights_three",
        three_kernel,
        [me, *first, *grads],
        [SCALARS] + [ANY] * 4,
        [out] * 4,
        after=after,
        scratch=[
            pltpu.VMEM((2, SLOT, D), LOWER),
            pltpu.VMEM((3, 2 * SLOT, D), LOWER),
            pltpu.SemaphoreType.DMA((8,)),
        ],
        flops=0,
    )


def page(array, k):
    return pl.BlockSpec((1,) + array.shape[1:], lambda s: (k, 0, 0))


def add_first(parts, small=None, after=()):
    count = len(parts)

    def body(*refs):
        outs = refs[len(flat) :]
        for k in range(count):
            outs[k][...] = (refs[2 * k][0].astype(WIDER) + refs[2 * k + 1][0].astype(WIDER)).astype(LOWER)
        if small is not None:
            outs[count][...] = refs[2 * count][...] + refs[2 * count + 1][...]

    flat = [a for pair in parts for a in pair] + list(small or ())
    specs = [page(a, 1) if a.ndim == 3 else WHOLE for a in flat]
    outs = [narrow(*keep.shape[1:]) for keep, unused in parts]
    specs_out = [WHOLE] * count
    if small is not None:
        outs.append(wide(*small[0].shape))
        specs_out.append(WHOLE)
    return run("add_first", body, flat, specs, outs, specs_out, after=after, grid=(1,), flops=0)


def add_second(parts, small=None, after=()):
    count = len(parts)
    shapes = [keep.shape[1:] for keep, unused, unused_too in parts]
    stacked = small is None
    rows = sum(shape[0] for shape in shapes) if stacked else shapes[0][0]
    columns = shapes[0][1] if stacked else sum(shape[1] for shape in shapes)

    def body(*refs):
        out = refs[-1]
        first = 0
        for k, (high, across) in enumerate(shapes):
            keep, got, last = refs[3 * k : 3 * k + 3]
            total = (keep[0].astype(WIDER) + got[0].astype(WIDER) + last[...].astype(WIDER)).astype(LOWER)
            if stacked:
                out[first : first + high] = total
                first += high
            else:
                out[:rows, first : first + across] = total
                first += across
        if small is not None:
            out[rows:] = jnp.zeros((16, columns), LOWER)
            out[rows:, :D] = (refs[3 * count][...] + refs[3 * count + 1][...]).astype(LOWER)

    flat = [a for trio in parts for a in trio] + list(small or ())
    specs = [page(a, 0) if a.ndim == 3 else WHOLE for a in flat]
    height = rows + (16 if small is not None else 0)
    return run("add_second", body, flat, specs, [narrow(height, columns)], after=after, grid=(1,), flops=0)


def add_pair(one, two, small=None, after=()):
    def body(*refs):
        outs = refs[len(flat) :]
        outs[0][...] = (refs[0][...].astype(WIDER) + refs[1][...].astype(WIDER)).astype(LOWER)
        if small is not None:
            outs[1][...] = refs[2][...] + refs[3][...]

    flat = [one, two] + list(small or ())
    outs = [narrow(*one.shape)] + [wide(*a.shape) for a in (small or ())[:1]]
    return run("add_pair", body, flat, [WHOLE] * len(flat), outs, after=after, flops=0)


def add_rows(one, two, after=()):
    def body(one_ref, two_ref, out_ref):
        out_ref[...] = one_ref[...] + two_ref[...]

    return run("add_rows", body, [one, two], [WHOLE] * 2, [wide(*one.shape)], after=after, flops=0)


def partner(axis, bit):
    return [(k, k ^ (1 << bit)) for k in range(lax.axis_size(axis))]


def swap(value, axis, bit):
    return lax.ppermute(value, axis, partner(axis, bit))


def all_sum(value, axis):
    for bit in range(lax.axis_size(axis).bit_length() - 1):
        value = value + swap(value, axis, bit)
    return value


def pa_order(turn):
    rest = lax.axis_size("pa").bit_length() - 2
    return [1 + (k + turn) % rest for k in range(rest)]


def both_cores(acts, turn):
    size = lax.axis_size("pa")
    me = lax.axis_index("pa")
    blocks = jnp.transpose(acts).reshape(size, acts.shape[1] // size, acts.shape[0])
    order = pa_order(turn)
    offsets = [
        sum(((k >> (len(order) - 1 - p)) & 1) << bit for p, bit in enumerate(order)) for k in range(size // 2)
    ]
    mine = jnp.concatenate([lax.dynamic_slice_in_dim(blocks, me ^ d, 1) for d in offsets])
    theirs = jnp.concatenate([lax.dynamic_slice_in_dim(blocks, me ^ d ^ 1, 1) for d in offsets])
    return mine, swap(theirs, "pa", 0)


def weight_part(acts, grads, first, last):
    total = None
    for act, grad in zip(acts, grads):
        act = act[first:last]
        term = product(act.reshape(-1, act.shape[2]), grad)
        total = term if total is None else total + term
    height = acts[0].shape[1]
    return total.astype(LOWER).reshape(last - first, height, -1)


def add_up(parts):
    total = parts[0].astype(WIDER)
    for part in parts[1:]:
        total = total + part.astype(WIDER)
    return total.astype(LOWER)


def share_over_pa(acts, grads, turn):
    size = acts[0].shape[0]
    keep = [weight_part(acts, grads, 0, size // 2)]
    send = weight_part(acts, grads, size // 2, size)
    for bit in pa_order(turn):
        keep.append(swap(send, "pa", bit))
        size //= 2
        if size > 1:
            send = add_up([part[size // 2 : size] for part in keep])
            keep = [part[: size // 2] for part in keep]
    return add_up([part[0] for part in keep])


def inward(share):
    return lax.ppermute(share, "pb", [(0, 1), (3, 2)])


def between(share):
    return lax.ppermute(share, "pb", [(1, 2), (2, 1)])


def outward(share):
    me = lax.axis_index("pb")
    got = lax.ppermute(share, "pb", [(1, 0), (2, 3)])
    return jnp.where((me == 1) | (me == 2), share, got).astype(WIDER)


def total_plain(share):
    return lax.psum(share, "pb").astype(WIDER)


def local(
    passages,
    lengths,
    answers,
    cotangent,
    enc_gain1,
    enc_qkv,
    enc_bias,
    enc_out,
    enc_gain2,
    enc_ffn_in,
    enc_ffn_out,
    enc_gain3,
    cross_kv,
    dec_gain1,
    dec_qkv,
    dec_bias,
    dec_out,
    dec_gain2,
    cross_query,
    cross_out,
    dec_gain3,
    dec_ffn_in,
    dec_ffn_out,
):
    pa_size = lax.axis_size("pa")
    pb_size = lax.axis_size("pb")
    fast = pa_size == 8 and pb_size == 4
    me = lax.axis_index("pa").astype(jnp.int32).reshape(1)
    x = passages.reshape(SLOT, D)
    count = lengths.reshape(1)
    table = jnp.transpose(enc_bias)
    dec_table = jnp.transpose(dec_bias)
    pick = jnp.asarray(PICK, LOWER)
    pick_back = jnp.asarray(PICK_BACK, LOWER)

    def across(value):
        return value, swap(value, "pa", 0)

    rows = x.astype(WIDER)
    first = (rows * scale_of(rows) * enc_gain1).astype(LOWER)
    heads = product(first, enc_qkv).astype(LOWER)
    mixed, stats, token = attention(count, table, pick, heads)
    after, second, slope, hidden, final, third, pairs, token = feed_forward(
        x, mixed, enc_out, enc_gain2, enc_ffn_in, enc_ffn_out, enc_gain3, cross_kv
    )
    dec_after, lefts, dec_heads, query, token = dec_self(
        dec_table, answers[0], dec_gain1, dec_gain2, dec_qkv, dec_out, cross_query, after=[token]
    )
    packed, token = cross(count, query, pairs)
    if fast:
        acts = [across(value) for value in (first, mixed, second, hidden, third)]
    else:
        acts = [both_cores(v, k % 2) for k, v in enumerate((first, mixed, second, hidden, third))]
    gathered = lax.all_gather(packed, "pa")
    answer, early, mix, g_mix, g_middle, stat, g_gain3, token = dec_mid(
        gathered, dec_after, cotangent[0], dec_gain3, lefts, cross_out, dec_ffn_in, dec_ffn_out,
        after=[got for unused, got in acts[:4]],
    )
    g_pairs, partial, token = cross_back(count, query, pairs, g_mix, mix, stat)
    early_all = lax.all_gather(early, "pb")
    g_final, branch, g_enc_gain3, token = kv_back(g_pairs, cross_kv, final, enc_gain3)
    if fast:
        partial, token = add_rows(partial, swap(partial, "pa", 0), after=[token])
    g_inner, g_after, low, g_mixed, g_enc_gain2, token = ffn_back(
        branch, enc_ffn_out, slope, enc_ffn_in, after, enc_gain2, g_final, enc_out, after=[token]
    )

    def back_of(base, pairs, after, begun=None):
        return attention_back(count, table, pick, heads, g_mixed, stats, base, pairs, begun, after=after)

    def dec_end(part, got, token, wait=()):
        return dec_back(
            dec_table, answers[0], part, got, dec_after, g_middle, dec_heads,
            dec_gain1, dec_gain2, g_gain3, cross_query, dec_out, dec_qkv, after=[token, *wait],
        )

    def rows_end(token):
        return rows_back(
            grads, enc_qkv, x, enc_gain1, g_after, g_enc_gain2, g_enc_gain3,
            (diagonal_a, diagonal_b), pick_back, after=[token],
        )

    pb_me = lax.axis_index("pb").astype(jnp.int32).reshape(1)

    def outer_end(token):
        *outer, token = dec_outer(pb_me, early_all, late_all, pb_size, after=[token])
        return outer, token

    if fast:
        partial, token = add_rows(partial, swap(partial, "pa", 1), after=[token])
        got = swap(partial, "pa", 2)
        xk, xs, yk, ys, token = weights_one(me, acts[4], across(g_pairs), acts[3], across(branch), after=[token])
        one = ((xk, swap(xs, "pa", 1)), (yk, swap(ys, "pa", 2)))
        late, g_start, token = dec_end(partial, got, token)
        late_all = lax.all_gather(late, "pb")
        grads, diagonal_a, token = back_of(0, FIRST, [token])
        send_x, send_y, token = add_first(one, after=[token, early_all])
        last = (swap(send_x, "pa", 2), swap(send_y, "pa", 1))
        xk, xs, yk, ys, token = weights_two(me, acts[2], across(g_inner), acts[1], across(low), after=[token])
        two = ((xk, swap(xs, "pa", 1)), (yk, swap(ys, "pa", 2)))
        share_one, token = add_second([one[0] + last[:1], one[1] + last[1:]], after=[token])
        got_one = inward(share_one)
        grads, diagonal_b, token = back_of(FIRST, PAIRS - FIRST, [token], grads)
        there = swap(grads, "pa", 0)
        g_rows, small, token = rows_end(token)
        got_small = swap(small, "pa", 0)
        send_x, send_y, token = add_first(two, after=[token, late_all])
        last = (swap(send_x, "pa", 2), swap(send_y, "pa", 1))
        share_one, small, token = add_pair(share_one, got_one, (small, got_small), after=[token])
        got_one = between(share_one)
        got_small = swap(small, "pa", 1)
        outer, token = outer_end(token)
        xk, xs, yk, ys, token = weights_three(me, acts[0], (grads, there), after=[token])
        three = ((xk, swap(xs, "pa", 1)), (yk, swap(ys, "pa", 2)))
        share_two, token = add_second([two[0] + last[:1], two[1] + last[1:]], after=[token])
        got_two = inward(share_two)
        send_x, send_y, small, token = add_first(three, (small, got_small), after=[token])
        last = (swap(send_x, "pa", 2), swap(send_y, "pa", 1))
        got_small = swap(small, "pa", 2)
        share_one, token = add_pair(share_one, got_one, after=[token])
        total_one = outward(share_one)
        share_two, token = add_pair(share_two, got_two, after=[token])
        got_two = between(share_two)
        share_three, token = add_second([three[0] + last[:1], three[1] + last[1:]], (small, got_small), after=[token])
        got_three = inward(share_three)
        share_three, token = add_pair(share_three, got_three, after=[token])
        got_three = between(share_three)
        share_two, token = add_pair(share_two, got_two, after=[token])
        total_two = outward(share_two)
        share_three, token = add_pair(share_three, got_three, after=[token])
        total_three = outward(share_three)
        small = total_three[D // pa_size :, :D]
        block = D // pa_size
        total_kv = jnp.concatenate([total_one[:block], total_one[block : 2 * block]], axis=1)
        total_ffn_out = total_one[2 * block :]
        second_part = 2 * block + block // 2
        total_ffn_in = jnp.concatenate(
            [total_two[first : first + block] for first in (0, block, second_part, second_part + block)], axis=1
        )
        total_out = jnp.concatenate([total_two[2 * block : second_part], total_two[second_part + 2 * block :]], axis=0)
        total_qkv = total_three[:block]
    else:
        partial = all_sum(partial, "pa")
        late, g_start, token = dec_end(partial, jnp.zeros_like(partial), token)
        late_all = lax.all_gather(late, "pb")
        grads, diagonal_a, token = back_of(0, FIRST, [token])
        grads, diagonal_b, token = back_of(FIRST, PAIRS - FIRST, [token], grads)
        g_rows, small, token = rows_end(token)
        outer, token = outer_end(token)
        small = all_sum(all_sum(small, "pa"), "pb")
        g_heads = jnp.concatenate([grads[0], grads[1], grads[2]], axis=1)
        total_kv = total_plain(share_over_pa(acts[4], across(g_pairs), 0))
        total_ffn_out = total_plain(share_over_pa(acts[3], across(branch), 1))
        total_ffn_in = total_plain(share_over_pa(acts[2], across(g_inner), 0))
        total_out = total_plain(share_over_pa(acts[1], across(low), 1))
        total_qkv = total_plain(share_over_pa(acts[0], across(g_heads), 0))

    d_qkv, d_out, d_query, d_cross, d_in, d_ffn, dec_small = outer
    dec_small = dec_small[0]
    dec_bias_rows = dec_small[3 * D :].reshape(H, STAT)[:, GROUP - ANS : GROUP]
    dec_bias_all = jnp.pad(jnp.transpose(dec_bias_rows[:, ::-1]), ((0, BUCKETS - ANS), (0, 0)))

    def own_part(vector, axis):
        height = vector.shape[0] // lax.axis_size(axis)
        return lax.dynamic_slice_in_dim(vector, lax.axis_index(axis) * height, height, axis=0)

    return (
        answer[None],
        g_rows.reshape(1, 1, SLOT, D),
        g_start[None],
        own_part(small[0], "pa"),
        total_qkv,
        jnp.transpose(small[4:16, :BUCKETS]),
        total_out,
        own_part(small[1], "pa"),
        total_ffn_in,
        total_ffn_out,
        own_part(small[2], "pa"),
        total_kv,
        own_part(dec_small[:D], "pb"),
        d_qkv,
        own_part(dec_bias_all, "pb"),
        d_out,
        own_part(dec_small[D : 2 * D], "pb"),
        d_query,
        d_cross,
        own_part(dec_small[2 * D : 3 * D], "pb"),
        d_in,
        d_ffn,
    )


def solution(mesh):
    copied = P()
    in_specs = (
        P("pb", "pa", None, None),
        P("pb", "pa"),
        P("pb", None, None),
        P("pb", None, None),
    ) + (copied,) * 19
    by_pa, by_pa_rows = P("pa"), P("pa", None)
    by_pb, by_pb_rows = P("pb"), P("pb", None)
    out_specs = (
        P("pb", None, None),
        P("pb", "pa", None, None),
        P("pb", None, None),
        by_pa,
        by_pa_rows,
        copied,
        by_pa_rows,
        by_pa,
        by_pa_rows,
        by_pa_rows,
        by_pa,
        by_pa_rows,
        by_pb,
        by_pb_rows,
        by_pb_rows,
        by_pb_rows,
        by_pb,
        by_pb_rows,
        by_pb_rows,
        by_pb,
        by_pb_rows,
        by_pb_rows,
    )
    return jax.shard_map(local, mesh=mesh, in_specs=in_specs, out_specs=out_specs, check_vma=False)
```

```python
import jax
import jax.numpy as jnp
import numpy as np
from jax import lax
from jax.experimental import pallas as pl
from jax.experimental.pallas import tpu as pltpu
from jax.sharding import PartitionSpec as P

D = 768
H = 12
HD = 64
FF = 3072
BUCKETS = 32
ANS = 20
SLOT = 512
PAIR = 2 * HD
PAIRS = H // 2
EDGE = 128
STRIP = 256
SPAN = 256
GROUP = 24
SENT = 40
STACK = H * GROUP
STAT = 128
STEPS = 4
WIDTH = FF // STEPS
FIRST = 4
EPS = 1e-06
MASKED = -1000000000.0
C_GELU = 0.7978845608028654
LOWER = jnp.bfloat16
WIDER = jnp.float32
EARLY = 7 * D + 2 * FF
LATE = 5 * D
AT = {
    "first": 0,
    "own": D,
    "second": 2 * D,
    "mix": 3 * D,
    "third": 4 * D,
    "hidden": 5 * D,
    "g_middle": 5 * D + FF,
    "g_inner": 6 * D + FF,
    "g_out": 6 * D + 2 * FF,
    "g_heads": 0,
    "g_after": 3 * D,
    "g_query": 4 * D,
}


def tile_classes(away):
    rows = [np.clip(EDGE * d - away, -(BUCKETS // 2), BUCKETS // 2 - 1) + BUCKETS // 2 for d in (-1, 0, 1)]
    return np.eye(BUCKETS, dtype=np.float32)[np.concatenate(rows)]


LANES = np.arange(SPAN)
PICK = tile_classes(np.where(LANES < EDGE, LANES, LANES - SPAN)).T
ENDS = np.repeat(np.eye(BUCKETS, dtype=np.float32)[[0, BUCKETS - 1]], EDGE, axis=0)
PICK_BACK = np.pad(np.concatenate([tile_classes(LANES - (EDGE - 1)), ENDS]), ((0, 0), (0, STAT - BUCKETS)))

SCALARS = pl.BlockSpec(memory_space=pltpu.SMEM)
ANY = pl.BlockSpec(memory_space=pl.ANY)
WHOLE = pl.BlockSpec(memory_space=pltpu.VMEM)
TOKEN = (8, 128)


def wide(*shape):
    return jax.ShapeDtypeStruct(shape, WIDER)


def narrow(*shape):
    return jax.ShapeDtypeStruct(shape, LOWER)


def run(name, body, ins, in_specs, outs, out_specs=None, after=(), grid=(), scratch=(), flops=10**9, mib=56, alias=None):
    count, extra, results = len(ins), len(after), len(outs)
    if out_specs is None:
        out_specs = [WHOLE] * results
    zeros = (lambda *s: (0, 0)) if grid else (lambda: (0, 0))

    def wrapped(*refs):
        refs[count + extra + results][...] = jnp.zeros(TOKEN, WIDER)
        body(*refs[:count], *refs[count + extra : count + extra + results], *refs[count + extra + results + 1 :])

    got = pl.pallas_call(
        wrapped,
        grid=grid,
        out_shape=tuple(outs) + (wide(*TOKEN),),
        in_specs=list(in_specs) + [ANY] * extra,
        out_specs=tuple(out_specs) + (pl.BlockSpec(TOKEN, zeros),),
        scratch_shapes=list(scratch),
        input_output_aliases=alias or {},
        compiler_params=pltpu.CompilerParams(vmem_limit_bytes=mib * 2**20),
        cost_estimate=pl.CostEstimate(flops=10 * flops, bytes_accessed=1, transcendentals=0),
        name=name,
    )(*ins, *after)
    return got


def product(left, right):
    return jnp.dot(left, right, preferred_element_type=WIDER)


def left_product(left, right):
    return lax.dot_general(left, right, (((0,), (0,)), ((), ())), preferred_element_type=WIDER)


def right_product(left, right):
    return lax.dot_general(left, right, (((1,), (1,)), ((), ())), preferred_element_type=WIDER)


def split_product(left, right, terms):
    total = None
    for k in range(terms):
        part = left.astype(LOWER)
        left = left - part.astype(WIDER)
        term = product(part, right)
        total = term if total is None else total + term
    return total


def silu_like(inner):
    square = inner * inner
    tanh = jnp.tanh(inner * (C_GELU + (C_GELU * 0.044715) * square))
    half = 0.5 + 0.5 * tanh
    value = inner * half
    slope = half + value * (1.0 - tanh) * (C_GELU + (3.0 * C_GELU * 0.044715) * square)
    return value, slope


def row_of(ref):
    return ref[...].reshape(1, D)


def scale_of(values):
    return lax.rsqrt(jnp.mean(values * values, axis=-1, keepdims=True) + EPS)


def norm_pull(values, gain, grad):
    scale = scale_of(values)
    lifted = grad * gain
    inside = jnp.sum(values * lifted, axis=-1, keepdims=True)
    back = scale * lifted - values * (scale * scale * scale * inside * (1.0 / D))
    return back, jnp.sum(grad * values * scale, axis=0, keepdims=True)


def fetch(pairs, sems):
    copies = [pltpu.make_async_copy(s, t, sems.at[k]) for k, (s, t) in enumerate(pairs)]
    for copy in copies:
        copy.start()
    return copies


def bias_tiles(u_ref, head):
    tiles = []
    for d in range(3):
        row = u_ref[pl.ds(head, 1), SPAN * d : SPAN * d + SPAN]
        spread = jnp.broadcast_to(row, (EDGE, SPAN))
        tiles.append(pltpu.roll(spread, 0, 1, stride=1, stride_axis=0)[:, :EDGE])
    return tiles


def key_masks(n):
    places = lax.broadcasted_iota(jnp.int32, (EDGE, EDGE), 0)
    return [jnp.where(places + EDGE * j < n, 0.0, MASKED) for j in range(SLOT // EDGE)]


def score_blocks(raw, tiles, masks, low, high, first):
    columns = []
    for c in range(STRIP // EDGE):
        blocks = []
        for j in range(SLOT // EDGE):
            block = raw[EDGE * j : EDGE * j + EDGE, EDGE * c : EDGE * c + EDGE]
            d = j - first - c
            block = block + (tiles[d + 1] if abs(d) <= 1 else (low if d < 0 else high))
            blocks.append(block + masks[j] if j > 0 else block)
        columns.append(blocks)
    return columns


def paved(columns, kind):
    return jnp.concatenate([jnp.concatenate([b.astype(kind) for b in blocks], axis=0) for blocks in columns], axis=1)


def fill_rows(table_ref, pick_ref, u_ref):
    @pl.when(pl.program_id(0) == 0)
    def _():
        u_ref[...] = split_product(table_ref[...], pick_ref[...], 3)


def attn_fwd_kernel(n_ref, ends_ref, table_ref, pick_ref, q_ref, k_ref, v_ref, o_ref, st_ref, u_ref):
    fill_rows(table_ref, pick_ref, u_ref)
    step = pl.program_id(0)
    masks = key_masks(n_ref[0])
    values = jnp.transpose(v_ref[...])
    ones = jnp.ones((16, SLOT), LOWER)
    mixed = []
    for h in range(2):
        head = 2 * step + h
        low, high = ends_ref[head, 0], ends_ref[head, BUCKETS - 1]
        tiles = bias_tiles(u_ref, head)
        cols = slice(HD * h, HD * h + HD)
        keys = k_ref[:, cols]
        left = jnp.concatenate([values[cols], ones], axis=0)
        strips = []
        for i in range(0, SLOT // EDGE, STRIP // EDGE):
            lanes = slice(EDGE * i, EDGE * i + STRIP)
            raw = right_product(keys, q_ref[lanes, cols] * 0.125)
            tops, powers = [], []
            for blocks in score_blocks(raw, tiles, masks, low, high, i):
                top = jnp.maximum(jnp.maximum(blocks[0], blocks[1]), jnp.maximum(blocks[2], blocks[3]))
                top = jnp.max(top, axis=0, keepdims=True)
                tops.append(top)
                powers.append([jnp.exp(block - top) for block in blocks])
            out = product(left, paved(powers, LOWER))
            total = out[HD : HD + 1]
            st_ref[0, h : h + 1, lanes] = jnp.concatenate(tops, axis=1) + jnp.log(total)
            strips.append(out[:HD] * (1.0 / total))
        mixed.append(jnp.concatenate(strips, axis=1))
    o_ref[...] = jnp.transpose(jnp.concatenate(mixed, axis=0)).astype(LOWER)


def attn_bwd_kernel(base):
    def body(
        n_ref, ends_ref, table_ref, pick_ref, q_ref, k_ref, v_ref, g_ref, o_ref, st_ref, gh_ref, gb_ref, u_ref
    ):
        fill_rows(table_ref, pick_ref, u_ref)
        step = pl.program_id(0) + base
        masks = key_masks(n_ref[0])
        keys_t = jnp.transpose(k_ref[...])
        rows = lax.broadcasted_iota(jnp.int32, (EDGE, EDGE), 0)
        columns = lax.broadcasted_iota(jnp.int32, (EDGE, EDGE), 1)
        mirror = jnp.where(rows + columns == EDGE - 1, 1.0, 0.0).astype(LOWER)
        rows = lax.broadcasted_iota(jnp.int32, (16, SLOT), 0) * EDGE
        columns = lax.broadcasted_iota(jnp.int32, (16, SLOT), 1)
        places = jnp.where((columns >= rows) & (columns < rows + EDGE), 1.0, 0.0).astype(LOWER)
        rows = lax.broadcasted_iota(jnp.int32, (16, PAIR), 0) * HD
        columns = lax.broadcasted_iota(jnp.int32, (16, PAIR), 1)
        halves = jnp.where((columns >= rows) & (columns < rows + HD), 1.0, 0.0).astype(LOWER)
        met = g_ref[...].astype(WIDER) * o_ref[...].astype(WIDER)
        upper = met.astype(LOWER)
        lower = (met - upper.astype(WIDER)).astype(LOWER)
        weighted = right_product(halves, upper) + right_product(halves, lower)
        grad_queries = []
        gb_ref[0, 2:8, :] = jnp.zeros((6, 4 * SPAN), WIDER)
        for h in range(2):
            head = 2 * step + h
            low, high = ends_ref[head, 0], ends_ref[head, BUCKETS - 1]
            tiles = bias_tiles(u_ref, head)
            cols = slice(HD * h, HD * h + HD)
            keys = k_ref[:, cols]
            values = v_ref[:, cols]
            left = jnp.concatenate([keys_t[cols], places], axis=0)
            grad_keys = jnp.zeros((SLOT, HD), WIDER)
            grad_values = jnp.zeros((SLOT, HD), WIDER)
            strips = []
            sums = {}

            def gather(d, block):
                sums[d] = sums[d] + block if d in sums else block

            for i in range(0, SLOT // EDGE, STRIP // EDGE):
                lanes = slice(EDGE * i, EDGE * i + STRIP)
                query = q_ref[lanes, cols]
                grad = g_ref[lanes, cols]
                raw = right_product(keys, query * 0.125)
                grad_probs = right_product(values, grad)
                probs, changes = [], []
                for c, blocks in enumerate(score_blocks(raw, tiles, masks, low, high, i)):
                    part = slice(EDGE * (i + c), EDGE * (i + c) + EDGE)
                    total = st_ref[0, h : h + 1, part]
                    mean = weighted[h : h + 1, part]
                    probs.append([jnp.exp(block - total) for block in blocks])
                    changes.append([])
                    for j in range(SLOT // EDGE):
                        gap = grad_probs[EDGE * j : EDGE * j + EDGE, EDGE * c : EDGE * c + EDGE] - mean
                        change = probs[c][j] * gap
                        changes[c].append(change)
                        if abs(j - i - c) <= 1:
                            gather(j - i - c, change)
                rounded = paved(changes, LOWER)
                out = product(left, rounded)
                strips.append(out[:HD])
                for c in range(STRIP // EDGE):
                    for j in range(SLOT // EDGE):
                        if abs(j - i - c) > 1:
                            gather(2 if j > i + c else -2, out[HD + j : HD + j + 1, EDGE * c : EDGE * c + EDGE])
                grad_keys += product(rounded, query)
                grad_values += product(paved(probs, LOWER), grad)
            grad_queries.append(jnp.concatenate(strips, axis=1))
            gh_ref[1, :, cols] = (grad_keys * 0.125).astype(LOWER)
            gh_ref[2, :, cols] = grad_values.astype(LOWER)
            empty = jnp.zeros((EDGE, SPAN - EDGE), WIDER)
            band = jnp.concatenate([sums[-1], sums[0], sums[1]], axis=1)
            upper = band.astype(LOWER)
            lower = (band - upper.astype(WIDER)).astype(LOWER)
            mirrored = product(mirror, upper) + product(mirror, lower)
            for d in range(3):
                spread = jnp.concatenate([mirrored[:, EDGE * d : EDGE * d + EDGE], empty], axis=1)
                turned = pltpu.roll(spread, 0, 1, stride=1, stride_axis=0)
                gb_ref[0, h : h + 1, SPAN * d : SPAN * d + SPAN] = jnp.sum(turned, axis=0, keepdims=True)
            for place, d in ((3 * SPAN, -2), (3 * SPAN + EDGE, 2)):
                gb_ref[0, h : h + 1, place : place + EDGE] = sums[d]
        gh_ref[0] = (jnp.transpose(jnp.concatenate(grad_queries, axis=0)) * 0.125).astype(LOWER)

    return body


def columns_at(first):
    return pl.BlockSpec((SLOT, PAIR), lambda s: (0, first + s))


def stats_at(first):
    return pl.BlockSpec((1, 2, SLOT), lambda s: (first + s, 0, 0))


def attention(count, table, pick, heads, after=()):
    return run(
        "enc_attention",
        attn_fwd_kernel,
        [count, table, table, pick, heads, heads, heads],
        [SCALARS, SCALARS, WHOLE, WHOLE, columns_at(0), columns_at(PAIRS), columns_at(2 * PAIRS)],
        [narrow(SLOT, D), wide(PAIRS, 2, SLOT)],
        [columns_at(0), stats_at(0)],
        after=after,
        grid=(PAIRS,),
        scratch=[pltpu.VMEM((H, 3 * SPAN), WIDER)],
        flops=2 * 2 * H * SLOT * SLOT * HD * 4,
    )


def attention_back(count, table, pick, heads, grad_mixed, mixed, stats, base, half, begun=None, after=()):
    ins = [count, table, table, pick, heads, heads, heads, grad_mixed, mixed, stats]
    specs = [columns_at(base), columns_at(PAIRS + base), columns_at(2 * PAIRS + base), columns_at(base), columns_at(base)]
    specs.append(stats_at(base))
    body = attn_bwd_kernel(base)
    if begun is not None:
        ins.append(begun)
        specs.append(ANY)
        inner = body

        def body(*refs):
            inner(*refs[:10], *refs[11:])

    return run(
        "enc_attention_back",
        body,
        ins,
        [SCALARS, SCALARS, WHOLE, WHOLE] + specs,
        [narrow(3, SLOT, D), wide(half, 8, 4 * SPAN)],
        [pl.BlockSpec((3, SLOT, PAIR), lambda s: (0, 0, base + s)), pl.BlockSpec((1, 8, 4 * SPAN), lambda s: (s, 0, 0))],
        after=after,
        grid=(half,),
        scratch=[pltpu.VMEM((H, 3 * SPAN), WIDER)],
        flops=2 * 5 * H * SLOT * SLOT * HD * 4,
        alias={10: 0} if begun is not None else None,
    )


def ffn_kernel(
    x_ref, mixed_ref, wo_ref, g2_ref, in_ref, out_ref, g3_ref, kv_any,
    after_ref, second_ref, slope_ref, hidden_ref, final_ref, third_ref, pairs_ref,
    kv_ref, sems,
):
    step = pl.program_id(0)
    copy = pltpu.make_async_copy(kv_any, kv_ref, sems.at[0])

    @pl.when(step == 0)
    def _():
        copy.start()
        after = x_ref[...].astype(WIDER) + product(mixed_ref[...], wo_ref[...])
        after_ref[...] = after
        final_ref[...] = after
        second_ref[...] = (after * scale_of(after) * row_of(g2_ref)).astype(LOWER)

    value, slope = silu_like(product(second_ref[...], in_ref[...]))
    slope_ref[...] = slope.astype(LOWER)
    hidden = value.astype(LOWER)
    hidden_ref[...] = hidden
    final_ref[...] += product(hidden, out_ref[...])

    @pl.when(step == STEPS - 1)
    def _():
        final = final_ref[...]
        third = (final * scale_of(final) * row_of(g3_ref)).astype(LOWER)
        third_ref[...] = third
        copy.wait()
        pairs_ref[...] = product(third, kv_ref[...]).astype(LOWER)


def whole(*shape):
    return pl.BlockSpec(shape, lambda s: (0,) * len(shape))


def feed_forward(x, mixed, wo, gain2, ffn_in, ffn_out, gain3, kv):
    rows = whole(SLOT, D)
    by_columns = pl.BlockSpec((SLOT, WIDTH), lambda s: (0, s))
    return run(
        "enc_ffn",
        ffn_kernel,
        [x, mixed, wo, gain2, ffn_in, ffn_out, gain3, kv],
        [rows, rows, whole(D, D), whole(D), pl.BlockSpec((D, WIDTH), lambda s: (0, s))]
        + [pl.BlockSpec((WIDTH, D), lambda s: (s, 0)), whole(D), ANY],
        [wide(SLOT, D), narrow(SLOT, D), narrow(SLOT, FF), narrow(SLOT, FF), wide(SLOT, D), narrow(SLOT, D), narrow(SLOT, 2 * D)],
        [rows, rows, by_columns, by_columns, rows, rows, whole(SLOT, 2 * D)],
        grid=(STEPS,),
        scratch=[pltpu.VMEM((D, 2 * D), LOWER), pltpu.SemaphoreType.DMA((1,))],
        flops=2 * SLOT * D * (D + 2 * FF + 2 * D),
    )


def kv_back_kernel(gp_ref, kv_ref, final_ref, g3_ref, gfinal_ref, branch_ref, gain_ref):
    back, gain = norm_pull(final_ref[...], row_of(g3_ref), right_product(gp_ref[...], kv_ref[...]))
    gfinal_ref[...] = back
    branch_ref[...] = back.astype(LOWER)
    gain_ref[...] = gain


def kv_back(g_pairs, kv, final, gain3, after=()):
    return run(
        "enc_kv_back",
        kv_back_kernel,
        [g_pairs, kv, final, gain3],
        [WHOLE] * 4,
        [wide(SLOT, D), narrow(SLOT, D), wide(1, D)],
        after=after,
        flops=0,
    )


def ffn_back_kernel(
    branch_ref, out_ref, slope_ref, in_ref, after_ref, g2_ref, gfinal_ref, wo_any,
    ginner_ref, gafter_ref, low_ref, gmixed_ref, gain_ref,
    total_ref, wo_ref, sems,
):
    step = pl.program_id(0)
    copy = pltpu.make_async_copy(wo_any, wo_ref, sems.at[0])

    @pl.when(step == 0)
    def _():
        copy.start()
        total_ref[...] = jnp.zeros((SLOT, D), WIDER)

    grad = right_product(branch_ref[...], out_ref[...])
    inner = (grad * slope_ref[...].astype(WIDER)).astype(LOWER)
    ginner_ref[...] = inner
    total_ref[...] += right_product(inner, in_ref[...])

    @pl.when(step == STEPS - 1)
    def _():
        back, gain = norm_pull(after_ref[...], row_of(g2_ref), total_ref[...])
        gain_ref[...] = gain
        g_after = gfinal_ref[...] + back
        gafter_ref[...] = g_after
        low = g_after.astype(LOWER)
        low_ref[...] = low
        copy.wait()
        gmixed_ref[...] = right_product(low, wo_ref[...]).astype(LOWER)


def ffn_back(branch, ffn_out, slope, ffn_in, after_rows, gain2, g_final, wo, after=()):
    rows = whole(SLOT, D)
    by_columns = pl.BlockSpec((SLOT, WIDTH), lambda s: (0, s))
    return run(
        "enc_ffn_back",
        ffn_back_kernel,
        [branch, ffn_out, slope, ffn_in, after_rows, gain2, g_final, wo],
        [rows, pl.BlockSpec((WIDTH, D), lambda s: (s, 0)), by_columns, pl.BlockSpec((D, WIDTH), lambda s: (0, s))]
        + [rows, whole(D), rows, ANY],
        [narrow(SLOT, FF), wide(SLOT, D), narrow(SLOT, D), narrow(SLOT, D), wide(1, D)],
        [by_columns, rows, rows, rows, whole(1, D)],
        after=after,
        grid=(STEPS,),
        scratch=[pltpu.VMEM((SLOT, D), WIDER), pltpu.VMEM((D, D), LOWER), pltpu.SemaphoreType.DMA((1,))],
        flops=2 * SLOT * D * (D + 2 * FF),
    )


def rows_back_kernel(
    g_ref, w_ref, x_ref, g1_ref, gafter_ref, gain2_ref, gain3_ref, da_ref, db_ref, pick_ref,
    grows_ref, small_ref, total_ref,
):
    step = pl.program_id(0)

    @pl.when(step == 0)
    def _():
        total_ref[...] = jnp.zeros((SLOT, D), WIDER)

    total_ref[...] += right_product(g_ref[0], w_ref[...])

    @pl.when(step == 2)
    def _():
        back, gain = norm_pull(x_ref[...].astype(WIDER), row_of(g1_ref), total_ref[...])
        grows_ref[...] = gafter_ref[...] + back
        sums = [ref[k, :2] for ref in (da_ref, db_ref) for k in range(ref.shape[0])]
        table = split_product(jnp.concatenate(sums, axis=0), pick_ref[...], 2)
        small_ref[...] = jnp.zeros((16, D), WIDER)
        small_ref[0:1] = gain
        small_ref[1:2] = gain2_ref[...]
        small_ref[2:3] = gain3_ref[...]
        small_ref[4:16, :STAT] = table


def rows_back(grads, qkv, x, gain1, g_after, gain2, gain3, diagonals, pick_back, after=()):
    rows = whole(SLOT, D)
    return run(
        "enc_rows_back",
        rows_back_kernel,
        [grads, qkv, x, gain1, g_after, gain2, gain3, diagonals[0], diagonals[1], pick_back],
        [pl.BlockSpec((1, SLOT, D), lambda s: (s, 0, 0)), pl.BlockSpec((D, D), lambda s: (0, s)), rows, whole(D), rows]
        + [whole(1, D), whole(1, D), whole(*diagonals[0].shape), whole(*diagonals[1].shape), whole(4 * SPAN, STAT)],
        [wide(SLOT, D), wide(16, D)],
        [rows, whole(16, D)],
        after=after,
        grid=(3,),
        scratch=[pltpu.VMEM((SLOT, D), WIDER)],
        flops=0,
    )


def head_lanes(h):
    lanes = lax.broadcasted_iota(jnp.int32, (GROUP, D), 1)
    return (lanes >= h * HD) & (lanes < (h + 1) * HD)


def stack_heads(flat):
    return jnp.concatenate([jnp.where(head_lanes(h), flat, 0.0) for h in range(H)], axis=0)


def merge_heads(stacked):
    total = jnp.zeros((GROUP, D), WIDER)
    for h in range(H):
        total = total + jnp.where(head_lanes(h), stacked[GROUP * h : GROUP * h + GROUP], 0.0)
    return total


def lanes_to_column(stat):
    lanes = lax.broadcasted_iota(jnp.int32, (GROUP, STAT), 1)
    parts = [jnp.sum(jnp.where(lanes == h, stat, 0.0), axis=1, keepdims=True) for h in range(H)]
    return jnp.concatenate(parts, axis=0)


def column_to_lanes(column, first):
    lanes = lax.broadcasted_iota(jnp.int32, (GROUP, STAT), 1)
    total = jnp.zeros((GROUP, STAT), WIDER)
    for h in range(H):
        total = total + jnp.where(lanes == first + h, column[GROUP * h : GROUP * h + GROUP], 0.0)
    return total


def spread_heads(stat):
    rows = lax.broadcasted_iota(jnp.int32, (STAT, D), 0) * HD
    lanes = lax.broadcasted_iota(jnp.int32, (STAT, D), 1)
    spread = jnp.where((lanes >= rows) & (lanes < rows + HD), 1.0, 0.0).astype(LOWER)
    return split_product(stat, spread, 2)


def own_scores(query, keys, table_ref):
    raw = right_product(query, keys)
    rows = lax.broadcasted_iota(jnp.int32, (GROUP, GROUP), 0)
    columns = lax.broadcasted_iota(jnp.int32, (GROUP, GROUP), 1)
    away = rows - columns
    parts = []
    for h in range(H):
        bias = jnp.full((GROUP, GROUP), table_ref[h, 0], WIDER)
        for d in range(1, GROUP):
            bias = jnp.where(away == d, table_ref[h, d], bias)
        part = raw[GROUP * h : GROUP * h + GROUP] + bias
        parts.append(jnp.where(away >= 0, part, MASKED))
    scores = jnp.concatenate(parts, axis=0)
    powers = jnp.exp(scores - jnp.max(scores, axis=1, keepdims=True))
    return powers / jnp.sum(powers, axis=1, keepdims=True)


def padded(ref, pad_ref):
    pad_ref[...] = jnp.zeros((GROUP, D), WIDER)
    pad_ref[:ANS] = ref[...].astype(WIDER)
    return pad_ref[...]


def answer_rows(width):
    return lax.broadcasted_iota(jnp.int32, (GROUP, width), 0) < ANS


def dec_self_kernel(
    table_ref, x_ref, g1_ref, g2_ref, qkv_any, out_any, query_any,
    after_ref, lefts_ref, heads_ref, query_ref,
    qkv_ref, out_ref, cross_ref, pad_ref, sems,
):
    copies = fetch(((qkv_any, qkv_ref), (out_any, out_ref), (query_any, cross_ref)), sems)
    start = padded(x_ref, pad_ref)
    first = (start * scale_of(start) * row_of(g1_ref)).astype(LOWER)
    copies[0].wait()
    heads = product(first, qkv_ref[...]).astype(LOWER)
    heads_ref[...] = heads
    query = stack_heads(heads.astype(WIDER)[:, :D] * 0.125).astype(LOWER)
    probs = own_scores(query, heads[:, D : 2 * D], table_ref)
    own = merge_heads(product(probs.astype(LOWER), heads[:, 2 * D :]))
    own = jnp.where(answer_rows(D), own, 0.0).astype(LOWER)
    copies[1].wait()
    after = start + product(own, out_ref[...])
    after_ref[...] = after
    second = (after * scale_of(after) * row_of(g2_ref)).astype(LOWER)
    copies[2].wait()
    query_ref[...] = product(second, cross_ref[...]).astype(LOWER)
    lefts_ref[:, :D] = first
    lefts_ref[:, D : 2 * D] = own
    lefts_ref[:, 2 * D :] = second


def masked_cross(n_ref, query_ref, pairs_ref):
    query = stack_heads(query_ref[...].astype(WIDER) * 0.125).astype(LOWER)
    raw = right_product(query, pairs_ref[:, :D])
    places = lax.broadcasted_iota(jnp.int32, (STACK, SLOT), 1)
    return query, jnp.where(places < n_ref[0], raw, MASKED)


def cross_kernel(n_ref, query_ref, pairs_ref, packed_ref):
    unused, scores = masked_cross(n_ref, query_ref, pairs_ref)
    top = jnp.max(scores, axis=1, keepdims=True)
    powers = jnp.exp(scores - top)
    total = jnp.sum(powers, axis=1, keepdims=True)
    probs = (powers / total).astype(LOWER)
    packed_ref[:, :D] = merge_heads(product(probs, pairs_ref[:, D:]))
    packed_ref[:, D:] = column_to_lanes(top, 0) + column_to_lanes(total, STAT // 2)


def dec_mid_kernel(
    parts_ref, after_ref, cot_ref, g3_ref, lefts_ref, cross_any, in_any, out_any,
    answer_ref, early_ref, mix_ref, gmix_ref, gmid_ref, stat_ref, gain_ref,
    cross_ref, in_ref, out_ref, pad_ref, sems,
):
    copies = fetch(((cross_any, cross_ref), (in_any, in_ref), (out_any, out_ref)), sems)
    size = parts_ref.shape[0]
    used = lax.broadcasted_iota(jnp.int32, (GROUP, STAT), 1) < H
    tops = [parts_ref[k, :, D:] for k in range(size)]
    totals = [pltpu.roll(stat, STAT // 2, 1) for stat in tops]
    top = tops[0]
    for k in range(1, size):
        top = jnp.maximum(top, tops[k])
    weights = [jnp.where(used, totals[k] * jnp.exp(tops[k] - top), 0.0) for k in range(size)]
    total = weights[0]
    for k in range(1, size):
        total = total + weights[k]
    total = jnp.where(used, total, 1.0)
    mix = jnp.zeros((GROUP, D), WIDER)
    for k in range(size):
        mix = mix + parts_ref[k, :, :D] * spread_heads(weights[k] / total)
    mix_ref[...] = mix
    stat_ref[:, :STAT] = jnp.where(used, top, 0.0)
    stat_ref[:, STAT:] = total
    mix_low = mix.astype(LOWER)
    copies[0].wait()
    middle = after_ref[...] + product(mix_low, cross_ref[...])
    third = (middle * scale_of(middle) * row_of(g3_ref)).astype(LOWER)
    copies[1].wait()
    inner = product(third, in_ref[...])
    value, slope = silu_like(inner)
    hidden = value.astype(LOWER)
    copies[2].wait()
    answer = (middle + product(hidden, out_ref[...])).astype(LOWER)
    answer_ref[...] = answer[:ANS]
    grad = padded(cot_ref, pad_ref)
    out_low = grad.astype(LOWER)
    g_inner = (right_product(out_low, out_ref[...]) * slope).astype(LOWER)
    back, gain = norm_pull(middle, row_of(g3_ref), right_product(g_inner, in_ref[...]))
    gain_ref[...] = gain
    g_middle = grad + back
    gmid_ref[...] = g_middle
    middle_low = g_middle.astype(LOWER)
    gmix_ref[...] = right_product(middle_low, cross_ref[...]).astype(LOWER)

    def store(name, rows):
        early_ref[:, AT[name] : AT[name] + rows.shape[1]] = rows

    def kept(rows):
        return jnp.where(answer_rows(rows.shape[1]), rows.astype(WIDER), 0.0).astype(LOWER)

    early_ref[:, : 3 * D] = kept(lefts_ref[...])
    store("mix", kept(mix_low))
    store("third", kept(third))
    store("hidden", kept(hidden))
    store("g_middle", middle_low)
    store("g_inner", g_inner)
    store("g_out", out_low)


def cross_back_kernel(n_ref, query_ref, pairs_ref, gmix_ref, mix_ref, stat_ref, gpairs_ref, partial_ref):
    query, scores = masked_cross(n_ref, query_ref, pairs_ref)
    top = lanes_to_column(stat_ref[:, :STAT])
    total = lanes_to_column(stat_ref[:, STAT:])
    probs = jnp.exp(scores - top) / total
    grad = stack_heads(gmix_ref[...].astype(WIDER))
    weighted = jnp.sum(grad * jnp.concatenate([mix_ref[...]] * H, axis=0), axis=1, keepdims=True)
    grad = grad.astype(LOWER)
    grad_probs = right_product(grad, pairs_ref[:, D:])
    rounded = (probs * (grad_probs - weighted)).astype(LOWER)
    gpairs_ref[:, :D] = left_product(rounded, query).astype(LOWER)
    gpairs_ref[:, D:] = left_product(probs.astype(LOWER), grad).astype(LOWER)
    partial_ref[...] = merge_heads(product(rounded, pairs_ref[:, :D])) * 0.125


def dec_back_kernel(
    table_ref, x_ref, part_ref, got_ref, after_ref, gmid_ref, heads_ref,
    g1_ref, g2_ref, gain3_ref, query_any, out_any, qkv_any,
    late_ref, gstart_ref,
    cross_ref, out_ref, qkv_ref, pad_ref, sems,
):
    copies = fetch(((query_any, cross_ref), (out_any, out_ref), (qkv_any, qkv_ref)), sems)
    g_query = (part_ref[...] + got_ref[...]).astype(LOWER)
    copies[0].wait()
    back, gain2 = norm_pull(after_ref[...], row_of(g2_ref), right_product(g_query, cross_ref[...]))
    g_after = gmid_ref[...] + back
    after_low = g_after.astype(LOWER)
    copies[1].wait()
    g_own = stack_heads(right_product(after_low, out_ref[...])).astype(LOWER)
    heads = heads_ref[...]
    query = stack_heads(heads.astype(WIDER)[:, :D] * 0.125).astype(LOWER)
    probs = own_scores(query, heads[:, D : 2 * D], table_ref)
    grad_probs = right_product(g_own, heads[:, 2 * D :])
    rounded = (probs * (grad_probs - jnp.sum(probs * grad_probs, axis=1, keepdims=True))).astype(LOWER)
    g_q = (merge_heads(product(rounded, heads[:, D : 2 * D])) * 0.125).astype(LOWER)
    g_k = left_product(rounded, query).astype(LOWER)
    g_v = left_product(probs.astype(LOWER), g_own).astype(LOWER)
    g_heads = jnp.concatenate([g_q, g_k, g_v], axis=1)
    copies[2].wait()
    start = padded(x_ref, pad_ref)
    back, gain1 = norm_pull(start, row_of(g1_ref), right_product(g_heads, qkv_ref[...]))
    gstart_ref[...] = (g_after + back)[:ANS]
    spread = rounded.astype(WIDER)
    rows = lax.broadcasted_iota(jnp.int32, (GROUP, GROUP), 0)
    columns = lax.broadcasted_iota(jnp.int32, (GROUP, GROUP), 1)
    mirror = jnp.where(rows + columns == GROUP - 1, 1.0, 0.0).astype(LOWER)
    empty = jnp.zeros((GROUP, STAT - GROUP), WIDER)
    tables = []
    for h in range(H):
        part = product(mirror, spread[GROUP * h : GROUP * h + GROUP].astype(LOWER))
        turned = pltpu.roll(jnp.concatenate([part, empty], axis=1), 0, 1, stride=1, stride_axis=0)
        tables.append(jnp.sum(turned, axis=0, keepdims=True))
    small = jnp.concatenate([gain1, gain2, gain3_ref[...]] + tables, axis=1)
    places = lax.broadcasted_iota(jnp.int32, (GROUP, LATE), 0)
    late = jnp.concatenate([g_heads, after_low, g_query], axis=1).astype(WIDER)
    late = jnp.concatenate([jnp.where(places == ANS, small, late), jnp.zeros((SENT - GROUP, LATE), WIDER)], axis=0)
    late_ref[...] = late.astype(LOWER)


def dec_outer_kernel(size):
    part = D // size

    def body(me_ref, *refs):
        me = me_ref[0]
        qkv_ref, out_ref, query_ref, cross_ref, in_ref, ffn_ref, small_ref, early_ref, late_ref = refs[2:]
        early_ref[...] = jnp.concatenate([refs[0][s].astype(WIDER) for s in range(size)], axis=0).astype(LOWER)
        late = [refs[1][s].astype(WIDER)[:GROUP] for s in range(size)]
        late_ref[...] = jnp.concatenate(late, axis=0).astype(LOWER)
        rows = lax.broadcasted_iota(jnp.int32, (part, D), 0) + me * part
        lanes = lax.broadcasted_iota(jnp.int32, (part, D), 1)
        picked = jnp.where(rows == lanes, 1.0, 0.0).astype(LOWER)

        def outer(name, right):
            left = right_product(picked, early_ref[:, AT[name] : AT[name] + D]).astype(LOWER)
            return product(left, right)

        qkv_ref[...] = outer("first", late_ref[:, : 3 * D])
        out_ref[...] = outer("own", late_ref[:, AT["g_after"] : AT["g_after"] + D])
        query_ref[...] = outer("second", late_ref[:, AT["g_query"] : AT["g_query"] + D])
        cross_ref[...] = outer("mix", early_ref[:, AT["g_middle"] : AT["g_middle"] + D])
        in_ref[...] = outer("third", early_ref[:, AT["g_inner"] : AT["g_inner"] + FF])
        height = FF // size
        first = pl.multiple_of(AT["hidden"] + me * height, 128)
        ffn_ref[...] = left_product(early_ref[:, pl.ds(first, height)], early_ref[:, AT["g_out"] : AT["g_out"] + D])
        total = jnp.zeros((1, LATE), WIDER)
        for k in range(size):
            total = total + late[k][ANS : ANS + 1]
        small_ref[...] = total

    return body


def held(*shapes):
    return [pltpu.VMEM(shape, LOWER) for shape in shapes] + [
        pltpu.VMEM((GROUP, D), WIDER),
        pltpu.SemaphoreType.DMA((len(shapes),)),
    ]


def dec_self(table, answers, gain1, gain2, qkv, out, query, after=()):
    return run(
        "dec_self",
        dec_self_kernel,
        [table, answers, gain1, gain2, qkv, out, query],
        [SCALARS] + [WHOLE] * 3 + [ANY] * 3,
        [wide(GROUP, D), narrow(GROUP, 3 * D), narrow(GROUP, 3 * D), narrow(GROUP, D)],
        after=after,
        scratch=held((D, 3 * D), (D, D), (D, D)),
        flops=10**9,
    )


def cross(count, query, pairs, after=()):
    return run(
        "cross",
        cross_kernel,
        [count, query, pairs],
        [SCALARS, WHOLE, WHOLE],
        [wide(GROUP, D + STAT)],
        after=after,
        flops=4 * STACK * SLOT * D,
    )


def dec_mid(parts, after_rows, cotangent, gain3, lefts, cross_out, ffn_in, ffn_out, after=()):
    return run(
        "dec_mid",
        dec_mid_kernel,
        [parts, after_rows, cotangent, gain3, lefts, cross_out, ffn_in, ffn_out],
        [WHOLE] * 5 + [ANY] * 3,
        [narrow(ANS, D), narrow(GROUP, EARLY), wide(GROUP, D), narrow(GROUP, D), wide(GROUP, D), wide(GROUP, 2 * STAT), wide(1, D)],
        after=after,
        scratch=held((D, D), (D, FF), (FF, D)),
        flops=4 * 10**9,
    )


def cross_back(count, query, pairs, g_mix, mix, stat, after=()):
    return run(
        "cross_back",
        cross_back_kernel,
        [count, query, pairs, g_mix, mix, stat],
        [SCALARS] + [WHOLE] * 5,
        [narrow(SLOT, 2 * D), wide(GROUP, D)],
        after=after,
        flops=10 * STACK * SLOT * D,
    )


def dec_back(table, answers, part, got, after_rows, g_middle, heads, gain1, gain2, g_gain3, query, out, qkv, after=()):
    return run(
        "dec_back",
        dec_back_kernel,
        [table, answers, part, got, after_rows, g_middle, heads, gain1, gain2, g_gain3, query, out, qkv],
        [SCALARS] + [WHOLE] * 9 + [ANY] * 3,
        [narrow(SENT, LATE), wide(ANS, D)],
        after=after,
        scratch=held((D, D), (D, D), (D, 3 * D)),
        flops=0,
    )


def dec_outer(me, early, late, size, after=()):
    part = D // size
    return run(
        "dec_outer",
        dec_outer_kernel(size),
        [me, early, late],
        [SCALARS, WHOLE, WHOLE],
        [wide(part, 3 * D), wide(part, D), wide(part, D), wide(part, D), wide(part, FF), wide(FF // size, D), wide(1, LATE)],
        after=after,
        scratch=[pltpu.VMEM((size * GROUP, EARLY), LOWER), pltpu.VMEM((size * GROUP, LATE), LOWER)],
        flops=8 * 10**9,
    )


PLACES = [(0, 0), (0, 1), (1, 0), (1, 1)]


def place_of(me, there):
    return me ^ (4 * there[0] + 2 * there[1])


def turned_rows(me, acts, block):
    lanes = lax.broadcasted_iota(jnp.int32, (block, D), 1)
    rows = lax.broadcasted_iota(jnp.int32, (block, D), 0)
    picked = [jnp.where(lanes - rows == place_of(me, t) * block, 1.0, 0.0).astype(LOWER) for t in PLACES]
    picked = jnp.concatenate(picked, axis=0)
    return jnp.concatenate([right_product(picked, act).astype(LOWER) for act in acts], axis=1)


def target(there, x_refs, y_refs):
    dy, dx = there
    return (x_refs[dx].at[dy], y_refs[dy].at[dx])


def one_kernel(me_ref, t_own, t_par, p_own, p_par, h_own, h_par, b_own, b_par, xk, xs, yk, ys, t, p, h, b, sems):
    me = me_ref[0]
    block = FF // 8
    pairs = [(t_own, t.at[0]), (t_par, t.at[1]), (p_own, p.at[:SLOT]), (p_par, p.at[SLOT:])]
    pairs += [(b_own, b.at[:SLOT]), (b_par, b.at[SLOT:])]
    for k, there in enumerate(PLACES):
        lanes = pl.ds(pl.multiple_of(place_of(me, there) * block, 128), block)
        pairs += [(h_own.at[:, lanes], h.at[k, :SLOT]), (h_par.at[:, lanes], h.at[k, SLOT:])]
    copies = fetch(pairs, sems)
    copies[0].wait()
    copies[1].wait()
    height = D // 8
    left = turned_rows(me, (t[0], t[1]), height)
    copies[2].wait()
    copies[3].wait()
    for c in range(2):
        grad = product(left, p[:, D * c : D * c + D]).astype(LOWER)
        for k, there in enumerate(PLACES):
            to, unused = target(there, (xk, xs), (yk, ys))
            to[height * c : height * c + height] = grad[height * k : height * k + height]
    copies[4].wait()
    copies[5].wait()
    for k, there in enumerate(PLACES):
        copies[6 + 2 * k].wait()
        copies[7 + 2 * k].wait()
        grad = left_product(h[k], b[...]).astype(LOWER)
        to_x, to_y = target(there, (xk, xs), (yk, ys))
        to_x[2 * height : 3 * height] = grad[:height]
        to_y[...] = grad[height:]


def two_kernel(me_ref, s_own, s_par, i_own, i_par, m_own, m_par, l_own, l_par, xk, xs, yk, ys, s, i, m, l, sems):
    me = me_ref[0]
    pairs = [(s_own, s.at[0]), (s_par, s.at[1])]
    for c in range(4):
        lanes = slice(D * c, D * c + D)
        pairs += [(i_own.at[:, lanes], i.at[c, :SLOT]), (i_par.at[:, lanes], i.at[c, SLOT:])]
    pairs += [(m_own, m.at[0]), (m_par, m.at[1]), (l_own, l.at[:SLOT]), (l_par, l.at[SLOT:])]
    copies = fetch(pairs, sems)
    copies[0].wait()
    copies[1].wait()
    height = D // 8
    half = height // 2
    left = turned_rows(me, (s[0], s[1]), height)
    for c in range(4):
        copies[2 + 2 * c].wait()
        copies[3 + 2 * c].wait()
        grad = product(left, i[c]).astype(LOWER)
        for k, there in enumerate(PLACES):
            to = target(there, (xk, xs), (yk, ys))[c // 2]
            to[height * (c % 2) : height * (c % 2) + height] = grad[height * k : height * k + height]
    for k in range(10, 14):
        copies[k].wait()
    left = turned_rows(me, (m[0], m[1]), height)
    grad = product(left, l[...]).astype(LOWER)
    for k, there in enumerate(PLACES):
        for to, first in zip(target(there, (xk, xs), (yk, ys)), (0, half)):
            to[2 * height : 2 * height + half] = grad[height * k + first : height * k + first + half]


def three_kernel(me_ref, f_own, f_par, g_own, g_par, xk, xs, yk, ys, f, g, sems):
    me = me_ref[0]
    pairs = [(f_own, f.at[0]), (f_par, f.at[1])]
    for c in range(3):
        pairs += [(g_own.at[c], g.at[c, :SLOT]), (g_par.at[c], g.at[c, SLOT:])]
    copies = fetch(pairs, sems)
    copies[0].wait()
    copies[1].wait()
    height = D // 8
    half = D // 2
    left = turned_rows(me, (f[0], f[1]), height)
    for c in range(3):
        copies[2 + 2 * c].wait()
        copies[3 + 2 * c].wait()
        grad = product(left, g[c]).astype(LOWER)
        for k, there in enumerate(PLACES):
            to_x, to_y = target(there, (xk, xs), (yk, ys))
            block = grad[height * k : height * k + height]
            if c == 0:
                to_x[:, :D] = block
            elif c == 1:
                to_x[:, D:] = block[:, :half]
                to_y[:, :half] = block[:, half:]
            else:
                to_y[:, half:] = block


def weights_one(me, third, g_pairs, hidden, branch, after=()):
    out = narrow(2, 3 * D // 8, D)
    return run(
        "weights_one",
        one_kernel,
        [me, *third, *g_pairs, *hidden, *branch],
        [SCALARS] + [ANY] * 8,
        [out] * 4,
        after=after,
        scratch=[
            pltpu.VMEM((2, SLOT, D), LOWER),
            pltpu.VMEM((2 * SLOT, 2 * D), LOWER),
            pltpu.VMEM((4, 2 * SLOT, FF // 8), LOWER),
            pltpu.VMEM((2 * SLOT, D), LOWER),
            pltpu.SemaphoreType.DMA((14,)),
        ],
        flops=4 * 10**9,
    )


def weights_two(me, second, g_inner, mixed, low, after=()):
    out = narrow(2, 5 * D // 16, D)
    return run(
        "weights_two",
        two_kernel,
        [me, *second, *g_inner, *mixed, *low],
        [SCALARS] + [ANY] * 8,
        [out] * 4,
        after=after,
        scratch=[
            pltpu.VMEM((2, SLOT, D), LOWER),
            pltpu.VMEM((4, 2 * SLOT, D), LOWER),
            pltpu.VMEM((2, SLOT, D), LOWER),
            pltpu.VMEM((2 * SLOT, D), LOWER),
            pltpu.SemaphoreType.DMA((14,)),
        ],
        flops=0,
    )


def weights_three(me, first, grads, after=()):
    out = narrow(2, D // 8, 3 * D // 2)
    return run(
        "weights_three",
        three_kernel,
        [me, *first, *grads],
        [SCALARS] + [ANY] * 4,
        [out] * 4,
        after=after,
        scratch=[
            pltpu.VMEM((2, SLOT, D), LOWER),
            pltpu.VMEM((3, 2 * SLOT, D), LOWER),
            pltpu.SemaphoreType.DMA((8,)),
        ],
        flops=0,
    )


def page(array, k):
    return pl.BlockSpec((1,) + array.shape[1:], lambda s: (k, 0, 0))


def add_first(parts, small=None, after=()):
    count = len(parts)

    def body(*refs):
        outs = refs[len(flat) :]
        for k in range(count):
            outs[k][...] = (refs[2 * k][0].astype(WIDER) + refs[2 * k + 1][0].astype(WIDER)).astype(LOWER)
        if small is not None:
            outs[count][...] = refs[2 * count][...] + refs[2 * count + 1][...]

    flat = [a for pair in parts for a in pair] + list(small or ())
    specs = [page(a, 1) if a.ndim == 3 else WHOLE for a in flat]
    outs = [narrow(*keep.shape[1:]) for keep, unused in parts]
    specs_out = [WHOLE] * count
    if small is not None:
        outs.append(wide(*small[0].shape))
        specs_out.append(WHOLE)
    return run("add_first", body, flat, specs, outs, specs_out, after=after, grid=(1,), flops=0)


def add_second(parts, small=None, after=()):
    count = len(parts)
    shapes = [keep.shape[1:] for keep, unused, unused_too in parts]
    stacked = small is None
    rows = sum(shape[0] for shape in shapes) if stacked else shapes[0][0]
    columns = shapes[0][1] if stacked else sum(shape[1] for shape in shapes)

    def body(*refs):
        out = refs[-1]
        first = 0
        for k, (high, across) in enumerate(shapes):
            keep, got, last = refs[3 * k : 3 * k + 3]
            total = (keep[0].astype(WIDER) + got[0].astype(WIDER) + last[...].astype(WIDER)).astype(LOWER)
            if stacked:
                out[first : first + high] = total
                first += high
            else:
                out[:rows, first : first + across] = total
                first += across
        if small is not None:
            out[rows:] = jnp.zeros((32, columns), LOWER)
            out[rows : rows + 16, :D] = (refs[3 * count][...] + refs[3 * count + 1][...]).astype(LOWER)

    flat = [a for trio in parts for a in trio] + list(small or ())
    specs = [page(a, 0) if a.ndim == 3 else WHOLE for a in flat]
    height = rows + (32 if small is not None else 0)
    return run("add_second", body, flat, specs, [narrow(height, columns)], after=after, grid=(1,), flops=0)


def add_pair(one, two, small=None, after=()):
    def body(*refs):
        outs = refs[len(flat) :]
        outs[0][...] = (refs[0][...].astype(WIDER) + refs[1][...].astype(WIDER)).astype(LOWER)
        if small is not None:
            outs[1][...] = refs[2][...] + refs[3][...]

    flat = [one, two] + list(small or ())
    outs = [narrow(*one.shape)] + [wide(*a.shape) for a in (small or ())[:1]]
    return run("add_pair", body, flat, [WHOLE] * len(flat), outs, after=after, flops=0)


def add_parts(share, parts, me, after=()):
    rows, columns = parts[0].shape

    def body(me_ref, share_ref, one_ref, two_ref, three_ref, out_ref):
        first = pl.multiple_of(me_ref[0] * rows, 16)
        total = share_ref[pl.ds(first, rows), :].astype(WIDER) + one_ref[...].astype(WIDER)
        out_ref[...] = (total + two_ref[...].astype(WIDER) + three_ref[...].astype(WIDER)).astype(LOWER)

    return run("add_parts", body, [me, share, *parts], [SCALARS] + [WHOLE] * 4, [narrow(rows, columns)], after=after, flops=0)


def add_rows(one, two, after=()):
    def body(one_ref, two_ref, out_ref):
        out_ref[...] = one_ref[...] + two_ref[...]

    return run("add_rows", body, [one, two], [WHOLE] * 2, [wide(*one.shape)], after=after, flops=0)


def partner(axis, bit):
    return [(k, k ^ (1 << bit)) for k in range(lax.axis_size(axis))]


def swap(value, axis, bit):
    return lax.ppermute(value, axis, partner(axis, bit))


def all_sum(value, axis):
    for bit in range(lax.axis_size(axis).bit_length() - 1):
        value = value + swap(value, axis, bit)
    return value


def pa_order(turn):
    rest = lax.axis_size("pa").bit_length() - 2
    return [1 + (k + turn) % rest for k in range(rest)]


def both_cores(acts, turn):
    size = lax.axis_size("pa")
    me = lax.axis_index("pa")
    blocks = jnp.transpose(acts).reshape(size, acts.shape[1] // size, acts.shape[0])
    order = pa_order(turn)
    offsets = [
        sum(((k >> (len(order) - 1 - p)) & 1) << bit for p, bit in enumerate(order)) for k in range(size // 2)
    ]
    mine = jnp.concatenate([lax.dynamic_slice_in_dim(blocks, me ^ d, 1) for d in offsets])
    theirs = jnp.concatenate([lax.dynamic_slice_in_dim(blocks, me ^ d ^ 1, 1) for d in offsets])
    return mine, swap(theirs, "pa", 0)


def weight_part(acts, grads, first, last):
    total = None
    for act, grad in zip(acts, grads):
        act = act[first:last]
        term = product(act.reshape(-1, act.shape[2]), grad)
        total = term if total is None else total + term
    height = acts[0].shape[1]
    return total.astype(LOWER).reshape(last - first, height, -1)


def add_up(parts):
    total = parts[0].astype(WIDER)
    for part in parts[1:]:
        total = total + part.astype(WIDER)
    return total.astype(LOWER)


def share_over_pa(acts, grads, turn):
    size = acts[0].shape[0]
    keep = [weight_part(acts, grads, 0, size // 2)]
    send = weight_part(acts, grads, size // 2, size)
    for bit in pa_order(turn):
        keep.append(swap(send, "pa", bit))
        size //= 2
        if size > 1:
            send = add_up([part[size // 2 : size] for part in keep])
            keep = [part[: size // 2] for part in keep]
    return add_up([part[0] for part in keep])


def inward(share):
    return lax.ppermute(share, "pb", [(0, 1), (3, 2)])


def between(share):
    return lax.ppermute(share, "pb", [(1, 2), (2, 1)])


def outward(share):
    me = lax.axis_index("pb")
    got = lax.ppermute(share, "pb", [(1, 0), (2, 3)])
    return jnp.where((me == 1) | (me == 2), share, got).astype(WIDER)


def swap_parts(share):
    me = lax.axis_index("pb")
    quarters = share.reshape(4, share.shape[0] // 4, share.shape[1])
    return [
        lax.ppermute(lax.dynamic_index_in_dim(quarters, me ^ s, 0, False), "pb", [(k, k ^ s) for k in range(4)])
        for s in range(1, 4)
    ]


def spread_parts(total, token):
    me = lax.axis_index("pb")
    got = [total] + [lax.ppermute(total, "pb", [(k, k ^ s) for k in range(4)]) for s in range(1, 4)]
    return jnp.concatenate([lax.select_n(me ^ b, *got) for b in range(4)], axis=0).astype(WIDER)


def total_plain(share):
    return lax.psum(share, "pb").astype(WIDER)


def local(
    passages,
    lengths,
    answers,
    cotangent,
    enc_gain1,
    enc_qkv,
    enc_bias,
    enc_out,
    enc_gain2,
    enc_ffn_in,
    enc_ffn_out,
    enc_gain3,
    cross_kv,
    dec_gain1,
    dec_qkv,
    dec_bias,
    dec_out,
    dec_gain2,
    cross_query,
    cross_out,
    dec_gain3,
    dec_ffn_in,
    dec_ffn_out,
):
    pa_size = lax.axis_size("pa")
    pb_size = lax.axis_size("pb")
    fast = pa_size == 8 and pb_size == 4
    me = lax.axis_index("pa").astype(jnp.int32).reshape(1)
    x = passages.reshape(SLOT, D)
    count = lengths.reshape(1)
    table = jnp.transpose(enc_bias)
    dec_table = jnp.transpose(dec_bias)
    pick = jnp.asarray(PICK, LOWER)
    pick_back = jnp.asarray(PICK_BACK, LOWER)

    def across(value):
        return value, swap(value, "pa", 0)

    rows = x.astype(WIDER)
    first = (rows * scale_of(rows) * enc_gain1).astype(LOWER)
    heads = product(first, enc_qkv).astype(LOWER)
    mixed, stats, token = attention(count, table, pick, heads)
    after, second, slope, hidden, final, third, pairs, token = feed_forward(
        x, mixed, enc_out, enc_gain2, enc_ffn_in, enc_ffn_out, enc_gain3, cross_kv
    )
    dec_after, lefts, dec_heads, query, token = dec_self(
        dec_table, answers[0], dec_gain1, dec_gain2, dec_qkv, dec_out, cross_query, after=[token]
    )
    packed, token = cross(count, query, pairs)
    if fast:
        acts = [across(value) for value in (first, mixed, second, hidden, third)]
    else:
        acts = [both_cores(v, k % 2) for k, v in enumerate((first, mixed, second, hidden, third))]
    gathered = lax.all_gather(packed, "pa")
    answer, early, mix, g_mix, g_middle, stat, g_gain3, token = dec_mid(
        gathered, dec_after, cotangent[0], dec_gain3, lefts, cross_out, dec_ffn_in, dec_ffn_out,
        after=[got for unused, got in acts[:4]],
    )
    g_pairs, partial, token = cross_back(count, query, pairs, g_mix, mix, stat)
    early_all = lax.all_gather(early, "pb")
    g_final, branch, g_enc_gain3, token = kv_back(g_pairs, cross_kv, final, enc_gain3)
    if fast:
        partial, token = add_rows(partial, swap(partial, "pa", 0), after=[token])
    g_inner, g_after, low, g_mixed, g_enc_gain2, token = ffn_back(
        branch, enc_ffn_out, slope, enc_ffn_in, after, enc_gain2, g_final, enc_out, after=[token]
    )

    def back_of(base, pairs, after, begun=None):
        return attention_back(count, table, pick, heads, g_mixed, mixed, stats, base, pairs, begun, after=after)

    def dec_end(part, got, token, wait=()):
        return dec_back(
            dec_table, answers[0], part, got, dec_after, g_middle, dec_heads,
            dec_gain1, dec_gain2, g_gain3, cross_query, dec_out, dec_qkv, after=[token, *wait],
        )

    def rows_end(token):
        return rows_back(
            grads, enc_qkv, x, enc_gain1, g_after, g_enc_gain2, g_enc_gain3,
            (diagonal_a, diagonal_b), pick_back, after=[token],
        )

    pb_me = lax.axis_index("pb").astype(jnp.int32).reshape(1)

    def outer_end(token):
        *outer, token = dec_outer(pb_me, early_all, late_all, pb_size, after=[token])
        return outer, token

    if fast:
        partial, token = add_rows(partial, swap(partial, "pa", 1), after=[token])
        got = swap(partial, "pa", 2)
        xk, xs, yk, ys, token = weights_one(me, acts[4], across(g_pairs), acts[3], across(branch), after=[token])
        one = ((xk, swap(xs, "pa", 1)), (yk, swap(ys, "pa", 2)))
        late, g_start, token = dec_end(partial, got, token)
        late_all = lax.all_gather(late, "pb")
        grads, diagonal_a, token = back_of(0, FIRST, [token])
        send_x, send_y, token = add_first(one, after=[token, early_all])
        last = (swap(send_x, "pa", 2), swap(send_y, "pa", 1))
        xk, xs, yk, ys, token = weights_two(me, acts[2], across(g_inner), acts[1], across(low), after=[token])
        two = ((xk, swap(xs, "pa", 1)), (yk, swap(ys, "pa", 2)))
        share_one, token = add_second([one[0] + last[:1], one[1] + last[1:]], after=[token])
        got_one = inward(share_one)
        grads, diagonal_b, token = back_of(FIRST, PAIRS - FIRST, [token], grads)
        there = swap(grads, "pa", 0)
        g_rows, small, token = rows_end(token)
        got_small = swap(small, "pa", 0)
        send_x, send_y, token = add_first(two, after=[token, late_all])
        last = (swap(send_x, "pa", 2), swap(send_y, "pa", 1))
        share_one, small, token = add_pair(share_one, got_one, (small, got_small), after=[token])
        got_one = between(share_one)
        got_small = swap(small, "pa", 1)
        outer, token = outer_end(token)
        xk, xs, yk, ys, token = weights_three(me, acts[0], (grads, there), after=[token])
        three = ((xk, swap(xs, "pa", 1)), (yk, swap(ys, "pa", 2)))
        share_two, token = add_second([two[0] + last[:1], two[1] + last[1:]], after=[token])
        got_two = inward(share_two)
        send_x, send_y, small, token = add_first(three, (small, got_small), after=[token])
        last = (swap(send_x, "pa", 2), swap(send_y, "pa", 1))
        got_small = swap(small, "pa", 2)
        share_one, token = add_pair(share_one, got_one, after=[token])
        total_one = outward(share_one)
        share_two, token = add_pair(share_two, got_two, after=[token])
        got_two = between(share_two)
        share_three, token = add_second([three[0] + last[:1], three[1] + last[1:]], (small, got_small), after=[token])
        parts = swap_parts(share_three)
        share_two, token = add_pair(share_two, got_two, after=[token])
        total_two = outward(share_two)
        total_three = spread_parts(*add_parts(share_three, parts, pb_me, after=[token]))
        small = total_three[D // pa_size :, :D]
        block = D // pa_size
        total_kv = jnp.concatenate([total_one[:block], total_one[block : 2 * block]], axis=1)
        total_ffn_out = total_one[2 * block :]
        second_part = 2 * block + block // 2
        total_ffn_in = jnp.concatenate(
            [total_two[first : first + block] for first in (0, block, second_part, second_part + block)], axis=1
        )
        total_out = jnp.concatenate([total_two[2 * block : second_part], total_two[second_part + 2 * block :]], axis=0)
        total_qkv = total_three[:block]
    else:
        partial = all_sum(partial, "pa")
        late, g_start, token = dec_end(partial, jnp.zeros_like(partial), token)
        late_all = lax.all_gather(late, "pb")
        grads, diagonal_a, token = back_of(0, FIRST, [token])
        grads, diagonal_b, token = back_of(FIRST, PAIRS - FIRST, [token], grads)
        g_rows, small, token = rows_end(token)
        outer, token = outer_end(token)
        small = all_sum(all_sum(small, "pa"), "pb")
        g_heads = jnp.concatenate([grads[0], grads[1], grads[2]], axis=1)
        total_kv = total_plain(share_over_pa(acts[4], across(g_pairs), 0))
        total_ffn_out = total_plain(share_over_pa(acts[3], across(branch), 1))
        total_ffn_in = total_plain(share_over_pa(acts[2], across(g_inner), 0))
        total_out = total_plain(share_over_pa(acts[1], across(low), 1))
        total_qkv = total_plain(share_over_pa(acts[0], across(g_heads), 0))

    d_qkv, d_out, d_query, d_cross, d_in, d_ffn, dec_small = outer
    dec_small = dec_small[0]
    dec_bias_rows = dec_small[3 * D :].reshape(H, STAT)[:, GROUP - ANS : GROUP]
    dec_bias_all = jnp.pad(jnp.transpose(dec_bias_rows[:, ::-1]), ((0, BUCKETS - ANS), (0, 0)))

    def own_part(vector, axis):
        height = vector.shape[0] // lax.axis_size(axis)
        return lax.dynamic_slice_in_dim(vector, lax.axis_index(axis) * height, height, axis=0)

    return (
        answer[None],
        g_rows.reshape(1, 1, SLOT, D),
        g_start[None],
        own_part(small[0], "pa"),
        total_qkv,
        jnp.transpose(small[4:16, :BUCKETS]),
        total_out,
        own_part(small[1], "pa"),
        total_ffn_in,
        total_ffn_out,
        own_part(small[2], "pa"),
        total_kv,
        own_part(dec_small[:D], "pb"),
        d_qkv,
        own_part(dec_bias_all, "pb"),
        d_out,
        own_part(dec_small[D : 2 * D], "pb"),
        d_query,
        d_cross,
        own_part(dec_small[2 * D : 3 * D], "pb"),
        d_in,
        d_ffn,
    )


def solution(mesh):
    copied = P()
    in_specs = (
        P("pb", "pa", None, None),
        P("pb", "pa"),
        P("pb", None, None),
        P("pb", None, None),
    ) + (copied,) * 19
    by_pa, by_pa_rows = P("pa"), P("pa", None)
    by_pb, by_pb_rows = P("pb"), P("pb", None)
    out_specs = (
        P("pb", None, None),
        P("pb", "pa", None, None),
        P("pb", None, None),
        by_pa,
        by_pa_rows,
        copied,
        by_pa_rows,
        by_pa,
        by_pa_rows,
        by_pa_rows,
        by_pa,
        by_pa_rows,
        by_pb,
        by_pb_rows,
        by_pb_rows,
        by_pb_rows,
        by_pb,
        by_pb_rows,
        by_pb_rows,
        by_pb,
        by_pb_rows,
        by_pb_rows,
    )
    return jax.shard_map(local, mesh=mesh, in_specs=in_specs, out_specs=out_specs, check_vma=False)
```

```python
import jax
import jax.numpy as jnp
import numpy as np
from jax import lax
from jax.experimental import pallas as pl
from jax.experimental.pallas import tpu as pltpu
from jax.sharding import PartitionSpec as P

D = 768
H = 12
HD = 64
FF = 3072
BUCKETS = 32
ANS = 20
SLOT = 512
PAIR = 2 * HD
PAIRS = H // 2
EDGE = 128
STRIP = 256
SPAN = 256
GROUP = 24
SENT = 40
STACK = H * GROUP
STAT = 128
STEPS = 4
WIDTH = FF // STEPS
FIRST = 4
EPS = 1e-06
MASKED = -1000000000.0
C_GELU = 0.7978845608028654
LOWER = jnp.bfloat16
WIDER = jnp.float32
EARLY = 7 * D + 2 * FF
LATE = 5 * D
AT = {
    "first": 0,
    "own": D,
    "second": 2 * D,
    "mix": 3 * D,
    "third": 4 * D,
    "hidden": 5 * D,
    "g_middle": 5 * D + FF,
    "g_inner": 6 * D + FF,
    "g_out": 6 * D + 2 * FF,
    "g_heads": 0,
    "g_after": 3 * D,
    "g_query": 4 * D,
}


def tile_classes(away):
    rows = [np.clip(EDGE * d - away, -(BUCKETS // 2), BUCKETS // 2 - 1) + BUCKETS // 2 for d in (-1, 0, 1)]
    return np.eye(BUCKETS, dtype=np.float32)[np.concatenate(rows)]


LANES = np.arange(SPAN)
PICK = tile_classes(np.where(LANES < EDGE, LANES, LANES - SPAN)).T
ENDS = np.repeat(np.eye(BUCKETS, dtype=np.float32)[[0, BUCKETS - 1]], EDGE, axis=0)
PICK_BACK = np.pad(np.concatenate([tile_classes(LANES - (EDGE - 1)), ENDS]), ((0, 0), (0, STAT - BUCKETS)))

SCALARS = pl.BlockSpec(memory_space=pltpu.SMEM)
ANY = pl.BlockSpec(memory_space=pl.ANY)
WHOLE = pl.BlockSpec(memory_space=pltpu.VMEM)
TOKEN = (8, 128)


def wide(*shape):
    return jax.ShapeDtypeStruct(shape, WIDER)


def narrow(*shape):
    return jax.ShapeDtypeStruct(shape, LOWER)


def run(name, body, ins, in_specs, outs, out_specs=None, after=(), grid=(), scratch=(), flops=10**9, mib=56, alias=None):
    count, extra, results = len(ins), len(after), len(outs)
    if out_specs is None:
        out_specs = [WHOLE] * results
    zeros = (lambda *s: (0, 0)) if grid else (lambda: (0, 0))

    def wrapped(*refs):
        refs[count + extra + results][...] = jnp.zeros(TOKEN, WIDER)
        body(*refs[:count], *refs[count + extra : count + extra + results], *refs[count + extra + results + 1 :])

    got = pl.pallas_call(
        wrapped,
        grid=grid,
        out_shape=tuple(outs) + (wide(*TOKEN),),
        in_specs=list(in_specs) + [ANY] * extra,
        out_specs=tuple(out_specs) + (pl.BlockSpec(TOKEN, zeros),),
        scratch_shapes=list(scratch),
        input_output_aliases=alias or {},
        compiler_params=pltpu.CompilerParams(vmem_limit_bytes=mib * 2**20),
        cost_estimate=pl.CostEstimate(flops=10 * flops, bytes_accessed=1, transcendentals=0),
        name=name,
    )(*ins, *after)
    return got


def product(left, right):
    return jnp.dot(left, right, preferred_element_type=WIDER)


def left_product(left, right):
    return lax.dot_general(left, right, (((0,), (0,)), ((), ())), preferred_element_type=WIDER)


def right_product(left, right):
    return lax.dot_general(left, right, (((1,), (1,)), ((), ())), preferred_element_type=WIDER)


def split_product(left, right, terms):
    total = None
    for k in range(terms):
        part = left.astype(LOWER)
        left = left - part.astype(WIDER)
        term = product(part, right)
        total = term if total is None else total + term
    return total


def silu_like(inner):
    square = inner * inner
    tanh = jnp.tanh(inner * (C_GELU + (C_GELU * 0.044715) * square))
    half = 0.5 + 0.5 * tanh
    value = inner * half
    slope = half + value * (1.0 - tanh) * (C_GELU + (3.0 * C_GELU * 0.044715) * square)
    return value, slope


def row_of(ref):
    return ref[...].reshape(1, D)


def scale_of(values):
    return lax.rsqrt(jnp.mean(values * values, axis=-1, keepdims=True) + EPS)


def norm_pull(values, gain, grad):
    scale = scale_of(values)
    lifted = grad * gain
    inside = jnp.sum(values * lifted, axis=-1, keepdims=True)
    back = scale * lifted - values * (scale * scale * scale * inside * (1.0 / D))
    return back, jnp.sum(grad * values * scale, axis=0, keepdims=True)


def fetch(pairs, sems):
    copies = [pltpu.make_async_copy(s, t, sems.at[k]) for k, (s, t) in enumerate(pairs)]
    for copy in copies:
        copy.start()
    return copies


def bias_tiles(u_ref, head):
    tiles = []
    for d in range(3):
        row = u_ref[pl.ds(head, 1), SPAN * d : SPAN * d + SPAN]
        spread = jnp.broadcast_to(row, (EDGE, SPAN))
        tiles.append(pltpu.roll(spread, 0, 1, stride=1, stride_axis=0)[:, :EDGE])
    return tiles


def key_masks(n):
    places = lax.broadcasted_iota(jnp.int32, (EDGE, EDGE), 0)
    return [jnp.where(places + EDGE * j < n, 0.0, MASKED) for j in range(SLOT // EDGE)]


def score_blocks(raw, tiles, masks, low, high, first):
    columns = []
    for c in range(STRIP // EDGE):
        blocks = []
        for j in range(SLOT // EDGE):
            block = raw[EDGE * j : EDGE * j + EDGE, EDGE * c : EDGE * c + EDGE]
            d = j - first - c
            block = block + (tiles[d + 1] if abs(d) <= 1 else (low if d < 0 else high))
            blocks.append(block + masks[j] if j > 0 else block)
        columns.append(blocks)
    return columns


def paved(columns, kind):
    return jnp.concatenate([jnp.concatenate([b.astype(kind) for b in blocks], axis=0) for blocks in columns], axis=1)


def fill_rows(table_ref, pick_ref, u_ref):
    @pl.when(pl.program_id(0) == 0)
    def _():
        u_ref[...] = split_product(table_ref[...], pick_ref[...], 3)


def attn_fwd_kernel(
    n_ref, ends_ref, table_ref, pick_ref, x_ref, g1_ref, wq_ref, wk_ref, wv_ref,
    first_ref, heads_ref, o_ref, st_ref, u_ref,
):
    fill_rows(table_ref, pick_ref, u_ref)
    step = pl.program_id(0)

    @pl.when(step == 0)
    def _():
        rows = x_ref[...].astype(WIDER)
        first_ref[...] = (rows * scale_of(rows) * row_of(g1_ref)).astype(LOWER)

    masks = key_masks(n_ref[0])
    first = first_ref[...]
    for k, w_ref in enumerate((wq_ref, wk_ref, wv_ref)):
        heads_ref[k] = product(first, w_ref[...]).astype(LOWER)
    q_ref, k_ref = heads_ref.at[0], heads_ref.at[1]
    values = jnp.transpose(heads_ref[2])
    ones = jnp.ones((16, SLOT), LOWER)
    mixed = []
    for h in range(2):
        head = 2 * step + h
        low, high = ends_ref[head, 0], ends_ref[head, BUCKETS - 1]
        tiles = bias_tiles(u_ref, head)
        cols = slice(HD * h, HD * h + HD)
        keys = k_ref[:, cols]
        left = jnp.concatenate([values[cols], ones], axis=0)
        strips = []
        for i in range(0, SLOT // EDGE, STRIP // EDGE):
            lanes = slice(EDGE * i, EDGE * i + STRIP)
            raw = right_product(keys, q_ref[lanes, cols] * 0.125)
            tops, powers = [], []
            for blocks in score_blocks(raw, tiles, masks, low, high, i):
                top = jnp.maximum(jnp.maximum(blocks[0], blocks[1]), jnp.maximum(blocks[2], blocks[3]))
                top = jnp.max(top, axis=0, keepdims=True)
                tops.append(top)
                powers.append([jnp.exp(block - top) for block in blocks])
            out = product(left, paved(powers, LOWER))
            total = out[HD : HD + 1]
            st_ref[0, h : h + 1, lanes] = jnp.concatenate(tops, axis=1) + jnp.log(total)
            strips.append(out[:HD] * (1.0 / total))
        mixed.append(jnp.concatenate(strips, axis=1))
    o_ref[...] = jnp.transpose(jnp.concatenate(mixed, axis=0)).astype(LOWER)


def attn_bwd_kernel(base):
    def body(
        n_ref, ends_ref, table_ref, pick_ref, h_ref, g_ref, o_ref, st_ref, gh_ref, gb_ref, u_ref
    ):
        q_ref, k_ref, v_ref = h_ref.at[0], h_ref.at[1], h_ref.at[2]
        fill_rows(table_ref, pick_ref, u_ref)
        step = pl.program_id(0) + base
        masks = key_masks(n_ref[0])
        keys_t = jnp.transpose(k_ref[...])
        rows = lax.broadcasted_iota(jnp.int32, (EDGE, EDGE), 0)
        columns = lax.broadcasted_iota(jnp.int32, (EDGE, EDGE), 1)
        mirror = jnp.where(rows + columns == EDGE - 1, 1.0, 0.0).astype(LOWER)
        rows = lax.broadcasted_iota(jnp.int32, (16, SLOT), 0) * EDGE
        columns = lax.broadcasted_iota(jnp.int32, (16, SLOT), 1)
        places = jnp.where((columns >= rows) & (columns < rows + EDGE), 1.0, 0.0).astype(LOWER)
        rows = lax.broadcasted_iota(jnp.int32, (16, PAIR), 0) * HD
        columns = lax.broadcasted_iota(jnp.int32, (16, PAIR), 1)
        halves = jnp.where((columns >= rows) & (columns < rows + HD), 1.0, 0.0).astype(LOWER)
        met = g_ref[...].astype(WIDER) * o_ref[...].astype(WIDER)
        upper = met.astype(LOWER)
        lower = (met - upper.astype(WIDER)).astype(LOWER)
        weighted = right_product(halves, upper) + right_product(halves, lower)
        grad_queries = []
        gb_ref[0, 2:8, :] = jnp.zeros((6, 4 * SPAN), WIDER)
        for h in range(2):
            head = 2 * step + h
            low, high = ends_ref[head, 0], ends_ref[head, BUCKETS - 1]
            tiles = bias_tiles(u_ref, head)
            cols = slice(HD * h, HD * h + HD)
            keys = k_ref[:, cols]
            values = v_ref[:, cols]
            left = jnp.concatenate([keys_t[cols], places], axis=0)
            grad_keys = jnp.zeros((SLOT, HD), WIDER)
            grad_values = jnp.zeros((SLOT, HD), WIDER)
            strips = []
            sums = {}

            def gather(d, block):
                sums[d] = sums[d] + block if d in sums else block

            for i in range(0, SLOT // EDGE, STRIP // EDGE):
                lanes = slice(EDGE * i, EDGE * i + STRIP)
                query = q_ref[lanes, cols]
                grad = g_ref[lanes, cols]
                raw = right_product(keys, query * 0.125)
                grad_probs = right_product(values, grad)
                probs, changes = [], []
                for c, blocks in enumerate(score_blocks(raw, tiles, masks, low, high, i)):
                    part = slice(EDGE * (i + c), EDGE * (i + c) + EDGE)
                    total = st_ref[0, h : h + 1, part]
                    mean = weighted[h : h + 1, part]
                    probs.append([jnp.exp(block - total) for block in blocks])
                    changes.append([])
                    for j in range(SLOT // EDGE):
                        gap = grad_probs[EDGE * j : EDGE * j + EDGE, EDGE * c : EDGE * c + EDGE] - mean
                        change = probs[c][j] * gap
                        changes[c].append(change)
                        if abs(j - i - c) <= 1:
                            gather(j - i - c, change)
                rounded = paved(changes, LOWER)
                out = product(left, rounded)
                strips.append(out[:HD])
                for c in range(STRIP // EDGE):
                    for j in range(SLOT // EDGE):
                        if abs(j - i - c) > 1:
                            gather(2 if j > i + c else -2, out[HD + j : HD + j + 1, EDGE * c : EDGE * c + EDGE])
                grad_keys += product(rounded, query)
                grad_values += product(paved(probs, LOWER), grad)
            grad_queries.append(jnp.concatenate(strips, axis=1))
            gh_ref[1, :, cols] = (grad_keys * 0.125).astype(LOWER)
            gh_ref[2, :, cols] = grad_values.astype(LOWER)
            empty = jnp.zeros((EDGE, SPAN - EDGE), WIDER)
            band = jnp.concatenate([sums[-1], sums[0], sums[1]], axis=1)
            upper = band.astype(LOWER)
            lower = (band - upper.astype(WIDER)).astype(LOWER)
            mirrored = product(mirror, upper) + product(mirror, lower)
            for d in range(3):
                spread = jnp.concatenate([mirrored[:, EDGE * d : EDGE * d + EDGE], empty], axis=1)
                turned = pltpu.roll(spread, 0, 1, stride=1, stride_axis=0)
                gb_ref[0, h : h + 1, SPAN * d : SPAN * d + SPAN] = jnp.sum(turned, axis=0, keepdims=True)
            for place, d in ((3 * SPAN, -2), (3 * SPAN + EDGE, 2)):
                gb_ref[0, h : h + 1, place : place + EDGE] = sums[d]
        gh_ref[0] = (jnp.transpose(jnp.concatenate(grad_queries, axis=0)) * 0.125).astype(LOWER)

    return body


def columns_at(first):
    return pl.BlockSpec((SLOT, PAIR), lambda s: (0, first + s))


def stats_at(first):
    return pl.BlockSpec((1, 2, SLOT), lambda s: (first + s, 0, 0))


def pair_of_all(base):
    return pl.BlockSpec((3, SLOT, PAIR), lambda s: (0, 0, base + s))


def attention(count, table, pick, x, gain1, qkv, after=()):
    def weights_at(first):
        return pl.BlockSpec((D, PAIR), lambda s: (0, first + s))

    return run(
        "enc_attention",
        attn_fwd_kernel,
        [count, table, table, pick, x, gain1, qkv, qkv, qkv],
        [SCALARS, SCALARS, WHOLE, WHOLE, whole(SLOT, D), whole(D), weights_at(0), weights_at(PAIRS), weights_at(2 * PAIRS)],
        [narrow(SLOT, D), narrow(3, SLOT, D), narrow(SLOT, D), wide(PAIRS, 2, SLOT)],
        [whole(SLOT, D), pair_of_all(0), columns_at(0), stats_at(0)],
        after=after,
        grid=(PAIRS,),
        scratch=[pltpu.VMEM((H, 3 * SPAN), WIDER)],
        flops=2 * 2 * H * SLOT * SLOT * HD * 4,
    )


def attention_back(count, table, pick, heads, grad_mixed, mixed, stats, base, half, begun=None, after=()):
    ins = [count, table, table, pick, heads, grad_mixed, mixed, stats]
    specs = [pair_of_all(base), columns_at(base), columns_at(base), stats_at(base)]
    body = attn_bwd_kernel(base)
    if begun is not None:
        ins.append(begun)
        specs.append(ANY)
        inner = body

        def body(*refs):
            inner(*refs[:8], *refs[9:])

    return run(
        "enc_attention_back",
        body,
        ins,
        [SCALARS, SCALARS, WHOLE, WHOLE] + specs,
        [narrow(3, SLOT, D), wide(half, 8, 4 * SPAN)],
        [pair_of_all(base), pl.BlockSpec((1, 8, 4 * SPAN), lambda s: (s, 0, 0))],
        after=after,
        grid=(half,),
        scratch=[pltpu.VMEM((H, 3 * SPAN), WIDER)],
        flops=2 * 5 * H * SLOT * SLOT * HD * 4,
        alias={8: 0} if begun is not None else None,
    )


def send_out(pairs, sems, first):
    copies = [pltpu.make_async_copy(s, t, sems.at[first + k]) for k, (s, t) in enumerate(pairs)]
    for copy in copies:
        copy.start()
    return copies


def chunk(k):
    return slice(WIDTH * k, WIDTH * k + WIDTH)


def ffn_kernel(
    x_ref, mixed_ref, g2_ref, g3_ref, wo_any, in_any, out_any, kv_any,
    after_any, second_any, slope_any, hidden_any, final_any, third_any, pairs_any,
    wo_ref, in_ref, out_ref, kv_ref, after_ref, second_ref, slope_ref, hidden_ref, final_ref, third_ref, pairs_ref,
    sems, out_sems,
):
    pairs = [(wo_any, wo_ref)]
    for k in range(STEPS):
        pairs += [(in_any.at[:, chunk(k)], in_ref.at[k]), (out_any.at[chunk(k)], out_ref.at[k])]
    copies = fetch(pairs + [(kv_any, kv_ref)], sems)
    copies[0].wait()
    copies[1].wait()
    after = x_ref[...].astype(WIDER) + product(mixed_ref[...], wo_ref[...])
    after_ref[...] = after
    second = (after * scale_of(after) * row_of(g2_ref)).astype(LOWER)
    second_ref[...] = second
    inner = product(second, in_ref[0])
    sent = send_out([(after_ref, after_any), (second_ref, second_any)], out_sems, 0)
    total = after
    for k in range(STEPS):
        copies[2 + 2 * k].wait()
        copies[3 + 2 * k].wait()
        following = product(second, in_ref[k + 1]) if k + 1 < STEPS else None
        value, slope = silu_like(inner)
        slope_ref[:, chunk(k)] = slope.astype(LOWER)
        hidden = value.astype(LOWER)
        hidden_ref[:, chunk(k)] = hidden
        total = total + product(hidden, out_ref[k])
        inner = following
        if k % 2:
            half = slice(WIDTH * (k - 1), WIDTH * (k + 1))
            sent += send_out(
                [(slope_ref.at[:, half], slope_any.at[:, half]), (hidden_ref.at[:, half], hidden_any.at[:, half])],
                out_sems, len(sent),
            )
    final_ref[...] = total
    third = (total * scale_of(total) * row_of(g3_ref)).astype(LOWER)
    third_ref[...] = third
    sent += send_out([(final_ref, final_any), (third_ref, third_any)], out_sems, len(sent))
    for k in range(2):
        half = slice(D * k, D * k + D)
        pairs_ref[:, half] = product(third, kv_ref[:, half]).astype(LOWER)
        sent += send_out([(pairs_ref.at[:, half], pairs_any.at[:, half])], out_sems, len(sent))
    for copy in sent:
        copy.wait()


def whole(*shape):
    return pl.BlockSpec(shape, lambda s: (0,) * len(shape))


def feed_forward(x, mixed, wo, gain2, ffn_in, ffn_out, gain3, kv):
    outs = [wide(SLOT, D), narrow(SLOT, D), narrow(SLOT, FF), narrow(SLOT, FF), wide(SLOT, D), narrow(SLOT, D), narrow(SLOT, 2 * D)]
    return run(
        "enc_ffn",
        ffn_kernel,
        [x, mixed, gain2, gain3, wo, ffn_in, ffn_out, kv],
        [WHOLE] * 4 + [ANY] * 4,
        outs,
        [ANY] * 7,
        scratch=[
            pltpu.VMEM((D, D), LOWER),
            pltpu.VMEM((STEPS, D, WIDTH), LOWER),
            pltpu.VMEM((STEPS, WIDTH, D), LOWER),
            pltpu.VMEM((D, 2 * D), LOWER),
        ]
        + [pltpu.VMEM(out.shape, out.dtype) for out in outs]
        + [pltpu.SemaphoreType.DMA((2 * STEPS + 2,)), pltpu.SemaphoreType.DMA((10,))],
        flops=2 * SLOT * D * (D + 2 * FF + 2 * D),
    )


def kv_back_kernel(gp_ref, kv_ref, final_ref, g3_ref, gfinal_ref, branch_ref, gain_ref):
    back, gain = norm_pull(final_ref[...], row_of(g3_ref), right_product(gp_ref[...], kv_ref[...]))
    gfinal_ref[...] = back
    branch_ref[...] = back.astype(LOWER)
    gain_ref[...] = gain


def kv_back(g_pairs, kv, final, gain3, after=()):
    return run(
        "enc_kv_back",
        kv_back_kernel,
        [g_pairs, kv, final, gain3],
        [WHOLE] * 4,
        [wide(SLOT, D), narrow(SLOT, D), wide(1, D)],
        after=after,
        flops=0,
    )


def ffn_back_kernel(
    branch_ref, g2_ref, gfinal_any, after_any, slope_any, out_any, in_any, wo_any,
    ginner_any, gafter_any, low_any, gmixed_any, gain_ref,
    gfinal_ref, after_ref, slope_ref, out_ref, in_ref, wo_ref, ginner_ref, gafter_ref, low_ref, gmixed_ref,
    sems, out_sems,
):
    pairs = []
    for k in range(STEPS):
        pairs += [(out_any.at[chunk(k)], out_ref.at[k]), (slope_any.at[:, chunk(k)], slope_ref.at[k])]
        pairs += [(in_any.at[:, chunk(k)], in_ref.at[k])]
    copies = fetch(pairs + [(after_any, after_ref), (gfinal_any, gfinal_ref), (wo_any, wo_ref)], sems)
    branch = branch_ref[...]
    copies[0].wait()
    grad = right_product(branch, out_ref[0])
    total = None
    sent = []
    for k in range(STEPS):
        copies[3 * k + 1].wait()
        copies[3 * k + 2].wait()
        copies[3 * k + 3].wait()
        following = right_product(branch, out_ref[k + 1]) if k + 1 < STEPS else None
        inner = (grad * slope_ref[k].astype(WIDER)).astype(LOWER)
        ginner_ref[:, chunk(k)] = inner
        term = right_product(inner, in_ref[k])
        total = term if total is None else total + term
        grad = following
        sent += send_out([(ginner_ref.at[:, chunk(k)], ginner_any.at[:, chunk(k)])], out_sems, len(sent))
    copies[3 * STEPS + 1].wait()
    copies[3 * STEPS + 2].wait()
    back, gain = norm_pull(after_ref[...], row_of(g2_ref), total)
    gain_ref[...] = gain
    g_after = gfinal_ref[...] + back
    gafter_ref[...] = g_after
    low = g_after.astype(LOWER)
    low_ref[...] = low
    sent += send_out([(gafter_ref, gafter_any), (low_ref, low_any)], out_sems, len(sent))
    gmixed_ref[...] = right_product(low, wo_ref[...]).astype(LOWER)
    sent += send_out([(gmixed_ref, gmixed_any)], out_sems, len(sent))
    for copy in sent:
        copy.wait()


def ffn_back(branch, ffn_out, slope, ffn_in, after_rows, gain2, g_final, wo, after=()):
    outs = [narrow(SLOT, FF), wide(SLOT, D), narrow(SLOT, D), narrow(SLOT, D)]
    return run(
        "enc_ffn_back",
        ffn_back_kernel,
        [branch, gain2, g_final, after_rows, slope, ffn_out, ffn_in, wo],
        [WHOLE] * 2 + [ANY] * 6,
        outs + [wide(1, D)],
        [ANY] * 4 + [WHOLE],
        after=after,
        scratch=[
            pltpu.VMEM((SLOT, D), WIDER),
            pltpu.VMEM((SLOT, D), WIDER),
            pltpu.VMEM((STEPS, SLOT, WIDTH), LOWER),
            pltpu.VMEM((STEPS, WIDTH, D), LOWER),
            pltpu.VMEM((STEPS, D, WIDTH), LOWER),
            pltpu.VMEM((D, D), LOWER),
        ]
        + [pltpu.VMEM(out.shape, out.dtype) for out in outs]
        + [pltpu.SemaphoreType.DMA((3 * STEPS + 3,)), pltpu.SemaphoreType.DMA((STEPS + 3,))],
        flops=2 * SLOT * D * (D + 2 * FF),
    )


def rows_back_kernel(
    g_ref, w_ref, x_ref, g1_ref, gafter_ref, gain2_ref, gain3_ref, da_ref, db_ref, pick_ref,
    grows_ref, small_ref, total_ref,
):
    step = pl.program_id(0)

    @pl.when(step == 0)
    def _():
        total_ref[...] = jnp.zeros((SLOT, D), WIDER)

    total_ref[...] += right_product(g_ref[0], w_ref[...])

    @pl.when(step == 2)
    def _():
        back, gain = norm_pull(x_ref[...].astype(WIDER), row_of(g1_ref), total_ref[...])
        grows_ref[...] = gafter_ref[...] + back
        sums = [ref[k, :2] for ref in (da_ref, db_ref) for k in range(ref.shape[0])]
        table = split_product(jnp.concatenate(sums, axis=0), pick_ref[...], 2)
        small_ref[...] = jnp.zeros((16, D), WIDER)
        small_ref[0:1] = gain
        small_ref[1:2] = gain2_ref[...]
        small_ref[2:3] = gain3_ref[...]
        small_ref[4:16, :STAT] = table


def rows_back(grads, qkv, x, gain1, g_after, gain2, gain3, diagonals, pick_back, after=()):
    rows = whole(SLOT, D)
    return run(
        "enc_rows_back",
        rows_back_kernel,
        [grads, qkv, x, gain1, g_after, gain2, gain3, diagonals[0], diagonals[1], pick_back],
        [pl.BlockSpec((1, SLOT, D), lambda s: (s, 0, 0)), pl.BlockSpec((D, D), lambda s: (0, s)), rows, whole(D), rows]
        + [whole(1, D), whole(1, D), whole(*diagonals[0].shape), whole(*diagonals[1].shape), whole(4 * SPAN, STAT)],
        [wide(SLOT, D), wide(16, D)],
        [rows, whole(16, D)],
        after=after,
        grid=(3,),
        scratch=[pltpu.VMEM((SLOT, D), WIDER)],
        flops=0,
    )


def head_lanes(h):
    lanes = lax.broadcasted_iota(jnp.int32, (GROUP, D), 1)
    return (lanes >= h * HD) & (lanes < (h + 1) * HD)


def stack_heads(flat):
    return jnp.concatenate([jnp.where(head_lanes(h), flat, 0.0) for h in range(H)], axis=0)


def merge_heads(stacked):
    total = jnp.zeros((GROUP, D), WIDER)
    for h in range(H):
        total = total + jnp.where(head_lanes(h), stacked[GROUP * h : GROUP * h + GROUP], 0.0)
    return total


def lanes_to_column(stat):
    lanes = lax.broadcasted_iota(jnp.int32, (GROUP, STAT), 1)
    parts = [jnp.sum(jnp.where(lanes == h, stat, 0.0), axis=1, keepdims=True) for h in range(H)]
    return jnp.concatenate(parts, axis=0)


def column_to_lanes(column, first):
    lanes = lax.broadcasted_iota(jnp.int32, (GROUP, STAT), 1)
    total = jnp.zeros((GROUP, STAT), WIDER)
    for h in range(H):
        total = total + jnp.where(lanes == first + h, column[GROUP * h : GROUP * h + GROUP], 0.0)
    return total


def spread_heads(stat):
    rows = lax.broadcasted_iota(jnp.int32, (STAT, D), 0) * HD
    lanes = lax.broadcasted_iota(jnp.int32, (STAT, D), 1)
    spread = jnp.where((lanes >= rows) & (lanes < rows + HD), 1.0, 0.0).astype(LOWER)
    return split_product(stat, spread, 2)


def own_scores(query, keys, table_ref):
    raw = right_product(query, keys)
    rows = lax.broadcasted_iota(jnp.int32, (GROUP, GROUP), 0)
    columns = lax.broadcasted_iota(jnp.int32, (GROUP, GROUP), 1)
    away = rows - columns
    parts = []
    for h in range(H):
        bias = jnp.full((GROUP, GROUP), table_ref[h, 0], WIDER)
        for d in range(1, GROUP):
            bias = jnp.where(away == d, table_ref[h, d], bias)
        part = raw[GROUP * h : GROUP * h + GROUP] + bias
        parts.append(jnp.where(away >= 0, part, MASKED))
    scores = jnp.concatenate(parts, axis=0)
    powers = jnp.exp(scores - jnp.max(scores, axis=1, keepdims=True))
    return powers / jnp.sum(powers, axis=1, keepdims=True)


def padded(ref, pad_ref):
    pad_ref[...] = jnp.zeros((GROUP, D), WIDER)
    pad_ref[:ANS] = ref[...].astype(WIDER)
    return pad_ref[...]


def answer_rows(width):
    return lax.broadcasted_iota(jnp.int32, (GROUP, width), 0) < ANS


def dec_self_kernel(
    table_ref, x_ref, g1_ref, g2_ref, qkv_any, out_any, query_any,
    after_ref, lefts_ref, heads_ref, query_ref,
    qkv_ref, out_ref, cross_ref, pad_ref, sems,
):
    copies = fetch(((qkv_any, qkv_ref), (out_any, out_ref), (query_any, cross_ref)), sems)
    start = padded(x_ref, pad_ref)
    first = (start * scale_of(start) * row_of(g1_ref)).astype(LOWER)
    copies[0].wait()
    heads = product(first, qkv_ref[...]).astype(LOWER)
    heads_ref[...] = heads
    query = stack_heads(heads.astype(WIDER)[:, :D] * 0.125).astype(LOWER)
    probs = own_scores(query, heads[:, D : 2 * D], table_ref)
    own = merge_heads(product(probs.astype(LOWER), heads[:, 2 * D :]))
    own = jnp.where(answer_rows(D), own, 0.0).astype(LOWER)
    copies[1].wait()
    after = start + product(own, out_ref[...])
    after_ref[...] = after
    second = (after * scale_of(after) * row_of(g2_ref)).astype(LOWER)
    copies[2].wait()
    query_ref[...] = product(second, cross_ref[...]).astype(LOWER)
    lefts_ref[:, :D] = first
    lefts_ref[:, D : 2 * D] = own
    lefts_ref[:, 2 * D :] = second


def masked_cross(n_ref, query_ref, pairs_ref):
    query = stack_heads(query_ref[...].astype(WIDER) * 0.125).astype(LOWER)
    raw = right_product(query, pairs_ref[:, :D])
    places = lax.broadcasted_iota(jnp.int32, (STACK, SLOT), 1)
    return query, jnp.where(places < n_ref[0], raw, MASKED)


def cross_kernel(n_ref, query_ref, pairs_ref, packed_ref):
    unused, scores = masked_cross(n_ref, query_ref, pairs_ref)
    top = jnp.max(scores, axis=1, keepdims=True)
    powers = jnp.exp(scores - top)
    total = jnp.sum(powers, axis=1, keepdims=True)
    probs = (powers / total).astype(LOWER)
    packed_ref[:, :D] = merge_heads(product(probs, pairs_ref[:, D:]))
    packed_ref[:, D:] = column_to_lanes(top, 0) + column_to_lanes(total, STAT // 2)


def dec_mid_kernel(
    parts_ref, after_ref, cot_ref, g3_ref, lefts_ref, cross_any, in_any, out_any,
    answer_ref, early_ref, mix_ref, gmix_ref, gmid_ref, stat_ref, gain_ref,
    cross_ref, in_ref, out_ref, pad_ref, sems,
):
    copies = fetch(((cross_any, cross_ref), (in_any, in_ref), (out_any, out_ref)), sems)
    size = parts_ref.shape[0]
    used = lax.broadcasted_iota(jnp.int32, (GROUP, STAT), 1) < H
    tops = [parts_ref[k, :, D:] for k in range(size)]
    totals = [pltpu.roll(stat, STAT // 2, 1) for stat in tops]
    top = tops[0]
    for k in range(1, size):
        top = jnp.maximum(top, tops[k])
    weights = [jnp.where(used, totals[k] * jnp.exp(tops[k] - top), 0.0) for k in range(size)]
    total = weights[0]
    for k in range(1, size):
        total = total + weights[k]
    total = jnp.where(used, total, 1.0)
    mix = jnp.zeros((GROUP, D), WIDER)
    for k in range(size):
        mix = mix + parts_ref[k, :, :D] * spread_heads(weights[k] / total)
    mix_ref[...] = mix
    stat_ref[:, :STAT] = jnp.where(used, top, 0.0)
    stat_ref[:, STAT:] = total
    mix_low = mix.astype(LOWER)
    copies[0].wait()
    middle = after_ref[...] + product(mix_low, cross_ref[...])
    third = (middle * scale_of(middle) * row_of(g3_ref)).astype(LOWER)
    copies[1].wait()
    inner = product(third, in_ref[...])
    value, slope = silu_like(inner)
    hidden = value.astype(LOWER)
    copies[2].wait()
    answer = (middle + product(hidden, out_ref[...])).astype(LOWER)
    answer_ref[...] = answer[:ANS]
    grad = padded(cot_ref, pad_ref)
    out_low = grad.astype(LOWER)
    g_inner = (right_product(out_low, out_ref[...]) * slope).astype(LOWER)
    back, gain = norm_pull(middle, row_of(g3_ref), right_product(g_inner, in_ref[...]))
    gain_ref[...] = gain
    g_middle = grad + back
    gmid_ref[...] = g_middle
    middle_low = g_middle.astype(LOWER)
    gmix_ref[...] = right_product(middle_low, cross_ref[...]).astype(LOWER)

    def store(name, rows):
        early_ref[:, AT[name] : AT[name] + rows.shape[1]] = rows

    def kept(rows):
        return jnp.where(answer_rows(rows.shape[1]), rows.astype(WIDER), 0.0).astype(LOWER)

    early_ref[:, : 3 * D] = kept(lefts_ref[...])
    store("mix", kept(mix_low))
    store("third", kept(third))
    store("hidden", kept(hidden))
    store("g_middle", middle_low)
    store("g_inner", g_inner)
    store("g_out", out_low)


def cross_back_kernel(n_ref, query_ref, pairs_ref, gmix_ref, mix_ref, stat_ref, gpairs_ref, partial_ref):
    query, scores = masked_cross(n_ref, query_ref, pairs_ref)
    top = lanes_to_column(stat_ref[:, :STAT])
    total = lanes_to_column(stat_ref[:, STAT:])
    probs = jnp.exp(scores - top) / total
    grad = stack_heads(gmix_ref[...].astype(WIDER))
    weighted = jnp.sum(grad * jnp.concatenate([mix_ref[...]] * H, axis=0), axis=1, keepdims=True)
    grad = grad.astype(LOWER)
    grad_probs = right_product(grad, pairs_ref[:, D:])
    rounded = (probs * (grad_probs - weighted)).astype(LOWER)
    gpairs_ref[:, :D] = left_product(rounded, query).astype(LOWER)
    gpairs_ref[:, D:] = left_product(probs.astype(LOWER), grad).astype(LOWER)
    partial_ref[...] = merge_heads(product(rounded, pairs_ref[:, :D])) * 0.125


def dec_back_kernel(
    table_ref, x_ref, part_ref, got_ref, after_ref, gmid_ref, heads_ref,
    g1_ref, g2_ref, gain3_ref, query_any, out_any, qkv_any,
    late_ref, gstart_ref,
    cross_ref, out_ref, qkv_ref, pad_ref, sems,
):
    copies = fetch(((query_any, cross_ref), (out_any, out_ref), (qkv_any, qkv_ref)), sems)
    g_query = (part_ref[...] + got_ref[...]).astype(LOWER)
    copies[0].wait()
    back, gain2 = norm_pull(after_ref[...], row_of(g2_ref), right_product(g_query, cross_ref[...]))
    g_after = gmid_ref[...] + back
    after_low = g_after.astype(LOWER)
    copies[1].wait()
    g_own = stack_heads(right_product(after_low, out_ref[...])).astype(LOWER)
    heads = heads_ref[...]
    query = stack_heads(heads.astype(WIDER)[:, :D] * 0.125).astype(LOWER)
    probs = own_scores(query, heads[:, D : 2 * D], table_ref)
    grad_probs = right_product(g_own, heads[:, 2 * D :])
    rounded = (probs * (grad_probs - jnp.sum(probs * grad_probs, axis=1, keepdims=True))).astype(LOWER)
    g_q = (merge_heads(product(rounded, heads[:, D : 2 * D])) * 0.125).astype(LOWER)
    g_k = left_product(rounded, query).astype(LOWER)
    g_v = left_product(probs.astype(LOWER), g_own).astype(LOWER)
    g_heads = jnp.concatenate([g_q, g_k, g_v], axis=1)
    copies[2].wait()
    start = padded(x_ref, pad_ref)
    back, gain1 = norm_pull(start, row_of(g1_ref), right_product(g_heads, qkv_ref[...]))
    gstart_ref[...] = (g_after + back)[:ANS]
    spread = rounded.astype(WIDER)
    rows = lax.broadcasted_iota(jnp.int32, (GROUP, GROUP), 0)
    columns = lax.broadcasted_iota(jnp.int32, (GROUP, GROUP), 1)
    mirror = jnp.where(rows + columns == GROUP - 1, 1.0, 0.0).astype(LOWER)
    empty = jnp.zeros((GROUP, STAT - GROUP), WIDER)
    tables = []
    for h in range(H):
        part = product(mirror, spread[GROUP * h : GROUP * h + GROUP].astype(LOWER))
        turned = pltpu.roll(jnp.concatenate([part, empty], axis=1), 0, 1, stride=1, stride_axis=0)
        tables.append(jnp.sum(turned, axis=0, keepdims=True))
    small = jnp.concatenate([gain1, gain2, gain3_ref[...]] + tables, axis=1)
    places = lax.broadcasted_iota(jnp.int32, (GROUP, LATE), 0)
    late = jnp.concatenate([g_heads, after_low, g_query], axis=1).astype(WIDER)
    late = jnp.concatenate([jnp.where(places == ANS, small, late), jnp.zeros((SENT - GROUP, LATE), WIDER)], axis=0)
    late_ref[...] = late.astype(LOWER)


def dec_outer_kernel(size):
    part = D // size

    def body(me_ref, *refs):
        me = me_ref[0]
        small_ref = refs[8]
        there, here = refs[2:8], refs[9:15]
        early_ref, late_ref, sems = refs[15:]
        sent = []
        early_ref[...] = jnp.concatenate([refs[0][s].astype(WIDER) for s in range(size)], axis=0).astype(LOWER)
        late = [refs[1][s].astype(WIDER)[:GROUP] for s in range(size)]
        late_ref[...] = jnp.concatenate(late, axis=0).astype(LOWER)
        rows = lax.broadcasted_iota(jnp.int32, (part, D), 0) + me * part
        lanes = lax.broadcasted_iota(jnp.int32, (part, D), 1)
        picked = jnp.where(rows == lanes, 1.0, 0.0).astype(LOWER)
        height = FF // size
        first = pl.multiple_of(AT["hidden"] + me * height, 128)

        def outer(k, name, right):
            left = right_product(picked, early_ref[:, AT[name] : AT[name] + D]).astype(LOWER)
            here[k][...] = product(left, right)
            sent.extend(send_out([(here[k], there[k])], sems, len(sent)))

        outer(4, "third", early_ref[:, AT["g_inner"] : AT["g_inner"] + FF])
        outer(0, "first", late_ref[:, : 3 * D])
        here[5][...] = left_product(early_ref[:, pl.ds(first, height)], early_ref[:, AT["g_out"] : AT["g_out"] + D])
        sent.extend(send_out([(here[5], there[5])], sems, len(sent)))
        outer(1, "own", late_ref[:, AT["g_after"] : AT["g_after"] + D])
        outer(2, "second", late_ref[:, AT["g_query"] : AT["g_query"] + D])
        outer(3, "mix", early_ref[:, AT["g_middle"] : AT["g_middle"] + D])
        total = jnp.zeros((1, LATE), WIDER)
        for k in range(size):
            total = total + late[k][ANS : ANS + 1]
        small_ref[...] = total
        for copy in sent:
            copy.wait()

    return body


def held(*shapes):
    return [pltpu.VMEM(shape, LOWER) for shape in shapes] + [
        pltpu.VMEM((GROUP, D), WIDER),
        pltpu.SemaphoreType.DMA((len(shapes),)),
    ]


def dec_self(table, answers, gain1, gain2, qkv, out, query, after=()):
    return run(
        "dec_self",
        dec_self_kernel,
        [table, answers, gain1, gain2, qkv, out, query],
        [SCALARS] + [WHOLE] * 3 + [ANY] * 3,
        [wide(GROUP, D), narrow(GROUP, 3 * D), narrow(GROUP, 3 * D), narrow(GROUP, D)],
        after=after,
        scratch=held((D, 3 * D), (D, D), (D, D)),
        flops=10**9,
    )


def cross(count, query, pairs, after=()):
    return run(
        "cross",
        cross_kernel,
        [count, query, pairs],
        [SCALARS, WHOLE, WHOLE],
        [wide(GROUP, D + STAT)],
        after=after,
        flops=4 * STACK * SLOT * D,
    )


def dec_mid(parts, after_rows, cotangent, gain3, lefts, cross_out, ffn_in, ffn_out, after=()):
    return run(
        "dec_mid",
        dec_mid_kernel,
        [parts, after_rows, cotangent, gain3, lefts, cross_out, ffn_in, ffn_out],
        [WHOLE] * 5 + [ANY] * 3,
        [narrow(ANS, D), narrow(GROUP, EARLY), wide(GROUP, D), narrow(GROUP, D), wide(GROUP, D), wide(GROUP, 2 * STAT), wide(1, D)],
        after=after,
        scratch=held((D, D), (D, FF), (FF, D)),
        flops=4 * 10**9,
    )


def cross_back(count, query, pairs, g_mix, mix, stat, after=()):
    return run(
        "cross_back",
        cross_back_kernel,
        [count, query, pairs, g_mix, mix, stat],
        [SCALARS] + [WHOLE] * 5,
        [narrow(SLOT, 2 * D), wide(GROUP, D)],
        after=after,
        flops=10 * STACK * SLOT * D,
    )


def dec_back(table, answers, part, got, after_rows, g_middle, heads, gain1, gain2, g_gain3, query, out, qkv, after=()):
    return run(
        "dec_back",
        dec_back_kernel,
        [table, answers, part, got, after_rows, g_middle, heads, gain1, gain2, g_gain3, query, out, qkv],
        [SCALARS] + [WHOLE] * 9 + [ANY] * 3,
        [narrow(SENT, LATE), wide(ANS, D)],
        after=after,
        scratch=held((D, D), (D, D), (D, 3 * D)),
        flops=0,
    )


def dec_outer(me, early, late, size, after=()):
    part = D // size
    outs = [wide(part, 3 * D), wide(part, D), wide(part, D), wide(part, D), wide(part, FF), wide(FF // size, D)]
    return run(
        "dec_outer",
        dec_outer_kernel(size),
        [me, early, late],
        [SCALARS, WHOLE, WHOLE],
        outs + [wide(1, LATE)],
        [ANY] * 6 + [WHOLE],
        after=after,
        scratch=[pltpu.VMEM(out.shape, WIDER) for out in outs]
        + [pltpu.VMEM((size * GROUP, EARLY), LOWER), pltpu.VMEM((size * GROUP, LATE), LOWER), pltpu.SemaphoreType.DMA((6,))],
        flops=8 * 10**9,
    )


PLACES = [(0, 0), (0, 1), (1, 0), (1, 1)]


def place_of(me, there):
    return me ^ (4 * there[0] + 2 * there[1])


def turned_rows(me, acts, block):
    lanes = lax.broadcasted_iota(jnp.int32, (block, D), 1)
    rows = lax.broadcasted_iota(jnp.int32, (block, D), 0)
    picked = [jnp.where(lanes - rows == place_of(me, t) * block, 1.0, 0.0).astype(LOWER) for t in PLACES]
    picked = jnp.concatenate(picked, axis=0)
    return jnp.concatenate([right_product(picked, act).astype(LOWER) for act in acts], axis=1)


def target(there, x_refs, y_refs):
    dy, dx = there
    return (x_refs[dx].at[dy], y_refs[dy].at[dx])


def pages_out(pairs, sems, first):
    return send_out([(here.at[k], there.at[k]) for here, there in pairs for k in range(2)], sems, first)


def one_kernel(
    me_ref, t_own, t_par, p_own, p_par, h_own, h_par, b_own, b_par, xk_any, xs_any, yk_any, ys_any,
    xk, xs, yk, ys, t, p, h, b, sems, out_sems,
):
    me = me_ref[0]
    block = FF // 8
    pairs = [(t_own, t.at[0]), (t_par, t.at[1]), (p_own, p.at[:SLOT]), (p_par, p.at[SLOT:])]
    pairs += [(b_own, b.at[:SLOT]), (b_par, b.at[SLOT:])]
    for k, there in enumerate(PLACES):
        lanes = pl.ds(pl.multiple_of(place_of(me, there) * block, 128), block)
        pairs += [(h_own.at[:, lanes], h.at[k, :SLOT]), (h_par.at[:, lanes], h.at[k, SLOT:])]
    copies = fetch(pairs, sems)
    copies[0].wait()
    copies[1].wait()
    height = D // 8
    left = turned_rows(me, (t[0], t[1]), height)
    for k in range(2, 8):
        copies[k].wait()
    for c in range(2):
        grad = product(left, p[:, D * c : D * c + D]).astype(LOWER)
        for k, there in enumerate(PLACES):
            to, unused = target(there, (xk, xs), (yk, ys))
            to[height * c : height * c + height] = grad[height * k : height * k + height]
    sent = []
    for k, there in enumerate(PLACES):
        grad = left_product(h[k], b[...]).astype(LOWER)
        to_x, to_y = target(there, (xk, xs), (yk, ys))
        to_x[2 * height : 3 * height] = grad[:height]
        to_y[...] = grad[height:]
        out_x, out_y = target(there, (xk_any, xs_any), (yk_any, ys_any))
        if k + 1 < len(PLACES):
            copies[8 + 2 * k].wait()
            copies[9 + 2 * k].wait()
        sent += send_out([(to_x, out_x), (to_y, out_y)], out_sems, len(sent))
    for copy in sent:
        copy.wait()


def two_kernel(
    me_ref, s_own, s_par, i_own, i_par, m_own, m_par, l_own, l_par, xk_any, xs_any, yk_any, ys_any,
    xk, xs, yk, ys, s, i, m, l, sems, out_sems,
):
    me = me_ref[0]
    pairs = [(s_own, s.at[0]), (s_par, s.at[1]), (m_own, m.at[0]), (m_par, m.at[1])]
    pairs += [(l_own, l.at[:SLOT]), (l_par, l.at[SLOT:])]
    for c in range(4):
        lanes = slice(D * c, D * c + D)
        pairs += [(i_own.at[:, lanes], i.at[c, :SLOT]), (i_par.at[:, lanes], i.at[c, SLOT:])]
    copies = fetch(pairs, sems)
    for k in range(6):
        copies[k].wait()
    height = D // 8
    half = height // 2
    left = turned_rows(me, (m[0], m[1]), height)
    turned = turned_rows(me, (s[0], s[1]), height)
    grad = product(left, l[...]).astype(LOWER)
    for k, there in enumerate(PLACES):
        for to, first in zip(target(there, (xk, xs), (yk, ys)), (0, half)):
            to[2 * height : 2 * height + half] = grad[height * k + first : height * k + first + half]
    sent = []
    for c in range(4):
        if c % 2 == 0:
            for k in range(6 + 2 * c, 10 + 2 * c):
                copies[k].wait()
        grad = product(turned, i[c]).astype(LOWER)
        for k, there in enumerate(PLACES):
            to = target(there, (xk, xs), (yk, ys))[c // 2]
            to[height * (c % 2) : height * (c % 2) + height] = grad[height * k : height * k + height]
        if c % 2:
            done = ((xk, xk_any), (xs, xs_any)) if c == 1 else ((yk, yk_any), (ys, ys_any))
            sent += pages_out(done, out_sems, len(sent))
    for copy in sent:
        copy.wait()


def three_kernel(
    me_ref, f_own, f_par, g_own, g_par, xk_any, xs_any, yk_any, ys_any, xk, xs, yk, ys, f, g, sems, out_sems
):
    me = me_ref[0]
    pairs = [(f_own, f.at[0]), (f_par, f.at[1])]
    for c in range(3):
        pairs += [(g_own.at[c], g.at[c, :SLOT]), (g_par.at[c], g.at[c, SLOT:])]
    copies = fetch(pairs, sems)
    copies[0].wait()
    copies[1].wait()
    height = D // 8
    half = D // 2
    left = turned_rows(me, (f[0], f[1]), height)
    for k in range(2, 8):
        copies[k].wait()
    sent = []
    for c in range(3):
        grad = product(left, g[c]).astype(LOWER)
        for k, there in enumerate(PLACES):
            to_x, to_y = target(there, (xk, xs), (yk, ys))
            block = grad[height * k : height * k + height]
            if c == 0:
                to_x[:, :D] = block
            elif c == 1:
                to_x[:, D:] = block[:, :half]
                to_y[:, :half] = block[:, half:]
            else:
                to_y[:, half:] = block
        if c:
            done = ((xk, xk_any), (xs, xs_any)) if c == 1 else ((yk, yk_any), (ys, ys_any))
            sent += pages_out(done, out_sems, len(sent))
    for copy in sent:
        copy.wait()


def weight_call(name, body, me, ins, rows, columns, held_shapes, flops, after):
    out = narrow(2, rows, columns)
    copies = {"weights_one": 14, "weights_two": 14, "weights_three": 8}[name]
    return run(
        name,
        body,
        [me, *ins],
        [SCALARS] + [ANY] * len(ins),
        [out] * 4,
        [ANY] * 4,
        after=after,
        scratch=[pltpu.VMEM(out.shape, LOWER)] * 4
        + [pltpu.VMEM(shape, LOWER) for shape in held_shapes]
        + [pltpu.SemaphoreType.DMA((copies,)), pltpu.SemaphoreType.DMA((8,))],
        flops=flops,
    )


def weights_one(me, third, g_pairs, hidden, branch, after=()):
    shapes = [(2, SLOT, D), (2 * SLOT, 2 * D), (4, 2 * SLOT, FF // 8), (2 * SLOT, D)]
    ins = (*third, *g_pairs, *hidden, *branch)
    return weight_call("weights_one", one_kernel, me, ins, 3 * D // 8, D, shapes, 4 * 10**9, after)


def weights_two(me, second, g_inner, mixed, low, after=()):
    shapes = [(2, SLOT, D), (4, 2 * SLOT, D), (2, SLOT, D), (2 * SLOT, D)]
    ins = (*second, *g_inner, *mixed, *low)
    return weight_call("weights_two", two_kernel, me, ins, 5 * D // 16, D, shapes, 0, after)


def weights_three(me, first, grads, after=()):
    shapes = [(2, SLOT, D), (3, 2 * SLOT, D)]
    return weight_call("weights_three", three_kernel, me, (*first, *grads), D // 8, 3 * D // 2, shapes, 0, after)


def page(array, k):
    return pl.BlockSpec((1,) + array.shape[1:], lambda s: (k, 0, 0))


def add_first(parts, small=None, after=()):
    count = len(parts)

    def body(*refs):
        outs = refs[len(flat) :]
        for k in range(count):
            outs[k][...] = (refs[2 * k][0].astype(WIDER) + refs[2 * k + 1][0].astype(WIDER)).astype(LOWER)
        if small is not None:
            outs[count][...] = refs[2 * count][...] + refs[2 * count + 1][...]

    flat = [a for pair in parts for a in pair] + list(small or ())
    specs = [page(a, 1) if a.ndim == 3 else WHOLE for a in flat]
    outs = [narrow(*keep.shape[1:]) for keep, unused in parts]
    specs_out = [WHOLE] * count
    if small is not None:
        outs.append(wide(*small[0].shape))
        specs_out.append(WHOLE)
    return run("add_first", body, flat, specs, outs, specs_out, after=after, grid=(1,), flops=0)


def add_second(parts, small=None, after=()):
    count = len(parts)
    shapes = [keep.shape[1:] for keep, unused, unused_too in parts]
    stacked = small is None
    rows = sum(shape[0] for shape in shapes) if stacked else shapes[0][0]
    columns = shapes[0][1] if stacked else sum(shape[1] for shape in shapes)

    def body(*refs):
        out = refs[-1]
        first = 0
        for k, (high, across) in enumerate(shapes):
            keep, got, last = refs[3 * k : 3 * k + 3]
            total = (keep[0].astype(WIDER) + got[0].astype(WIDER) + last[...].astype(WIDER)).astype(LOWER)
            if stacked:
                out[first : first + high] = total
                first += high
            else:
                out[:rows, first : first + across] = total
                first += across
        if small is not None:
            out[rows:] = jnp.zeros((32, columns), LOWER)
            out[rows : rows + 16, :D] = (refs[3 * count][...] + refs[3 * count + 1][...]).astype(LOWER)

    flat = [a for trio in parts for a in trio] + list(small or ())
    specs = [page(a, 0) if a.ndim == 3 else WHOLE for a in flat]
    height = rows + (32 if small is not None else 0)
    return run("add_second", body, flat, specs, [narrow(height, columns)], after=after, grid=(1,), flops=0)


def add_pair(one, two, small=None, after=()):
    def body(*refs):
        outs = refs[len(flat) :]
        outs[0][...] = (refs[0][...].astype(WIDER) + refs[1][...].astype(WIDER)).astype(LOWER)
        if small is not None:
            outs[1][...] = refs[2][...] + refs[3][...]

    flat = [one, two] + list(small or ())
    outs = [narrow(*one.shape)] + [wide(*a.shape) for a in (small or ())[:1]]
    return run("add_pair", body, flat, [WHOLE] * len(flat), outs, after=after, flops=0)


def add_parts(share, parts, me, after=()):
    rows, columns = parts[0].shape

    def body(me_ref, share_ref, one_ref, two_ref, three_ref, out_ref):
        first = pl.multiple_of(me_ref[0] * rows, 16)
        total = share_ref[pl.ds(first, rows), :].astype(WIDER) + one_ref[...].astype(WIDER)
        out_ref[...] = (total + two_ref[...].astype(WIDER) + three_ref[...].astype(WIDER)).astype(LOWER)

    return run("add_parts", body, [me, share, *parts], [SCALARS] + [WHOLE] * 4, [narrow(rows, columns)], after=after, flops=0)


def add_rows(one, two, after=()):
    def body(one_ref, two_ref, out_ref):
        out_ref[...] = one_ref[...] + two_ref[...]

    return run("add_rows", body, [one, two], [WHOLE] * 2, [wide(*one.shape)], after=after, flops=0)


def partner(axis, bit):
    return [(k, k ^ (1 << bit)) for k in range(lax.axis_size(axis))]


def swap(value, axis, bit):
    return lax.ppermute(value, axis, partner(axis, bit))


def all_sum(value, axis):
    for bit in range(lax.axis_size(axis).bit_length() - 1):
        value = value + swap(value, axis, bit)
    return value


def pa_order(turn):
    rest = lax.axis_size("pa").bit_length() - 2
    return [1 + (k + turn) % rest for k in range(rest)]


def both_cores(acts, turn):
    size = lax.axis_size("pa")
    me = lax.axis_index("pa")
    blocks = jnp.transpose(acts).reshape(size, acts.shape[1] // size, acts.shape[0])
    order = pa_order(turn)
    offsets = [
        sum(((k >> (len(order) - 1 - p)) & 1) << bit for p, bit in enumerate(order)) for k in range(size // 2)
    ]
    mine = jnp.concatenate([lax.dynamic_slice_in_dim(blocks, me ^ d, 1) for d in offsets])
    theirs = jnp.concatenate([lax.dynamic_slice_in_dim(blocks, me ^ d ^ 1, 1) for d in offsets])
    return mine, swap(theirs, "pa", 0)


def weight_part(acts, grads, first, last):
    total = None
    for act, grad in zip(acts, grads):
        act = act[first:last]
        term = product(act.reshape(-1, act.shape[2]), grad)
        total = term if total is None else total + term
    height = acts[0].shape[1]
    return total.astype(LOWER).reshape(last - first, height, -1)


def add_up(parts):
    total = parts[0].astype(WIDER)
    for part in parts[1:]:
        total = total + part.astype(WIDER)
    return total.astype(LOWER)


def share_over_pa(acts, grads, turn):
    size = acts[0].shape[0]
    keep = [weight_part(acts, grads, 0, size // 2)]
    send = weight_part(acts, grads, size // 2, size)
    for bit in pa_order(turn):
        keep.append(swap(send, "pa", bit))
        size //= 2
        if size > 1:
            send = add_up([part[size // 2 : size] for part in keep])
            keep = [part[: size // 2] for part in keep]
    return add_up([part[0] for part in keep])


def inward(share):
    return lax.ppermute(share, "pb", [(0, 1), (3, 2)])


def between(share):
    return lax.ppermute(share, "pb", [(1, 2), (2, 1)])


def outward(share):
    me = lax.axis_index("pb")
    got = lax.ppermute(share, "pb", [(1, 0), (2, 3)])
    return jnp.where((me == 1) | (me == 2), share, got).astype(WIDER)


def swap_parts(share):
    me = lax.axis_index("pb")
    quarters = share.reshape(4, share.shape[0] // 4, share.shape[1])
    return [
        lax.ppermute(lax.dynamic_index_in_dim(quarters, me ^ s, 0, False), "pb", [(k, k ^ s) for k in range(4)])
        for s in range(1, 4)
    ]


def spread_parts(total, token):
    me = lax.axis_index("pb")
    got = [total] + [lax.ppermute(total, "pb", [(k, k ^ s) for k in range(4)]) for s in range(1, 4)]
    return jnp.concatenate([lax.select_n(me ^ b, *got) for b in range(4)], axis=0).astype(WIDER)


def total_plain(share):
    return lax.psum(share, "pb").astype(WIDER)


def local(
    passages,
    lengths,
    answers,
    cotangent,
    enc_gain1,
    enc_qkv,
    enc_bias,
    enc_out,
    enc_gain2,
    enc_ffn_in,
    enc_ffn_out,
    enc_gain3,
    cross_kv,
    dec_gain1,
    dec_qkv,
    dec_bias,
    dec_out,
    dec_gain2,
    cross_query,
    cross_out,
    dec_gain3,
    dec_ffn_in,
    dec_ffn_out,
):
    pa_size = lax.axis_size("pa")
    pb_size = lax.axis_size("pb")
    fast = pa_size == 8 and pb_size == 4
    me = lax.axis_index("pa").astype(jnp.int32).reshape(1)
    x = passages.reshape(SLOT, D)
    count = lengths.reshape(1)
    table = jnp.transpose(enc_bias)
    dec_table = jnp.transpose(dec_bias)
    pick = jnp.asarray(PICK, LOWER)
    pick_back = jnp.asarray(PICK_BACK, LOWER)

    def across(value):
        return value, swap(value, "pa", 0)

    first, heads, mixed, stats, token = attention(count, table, pick, x, enc_gain1, enc_qkv)
    after, second, slope, hidden, final, third, pairs, token = feed_forward(
        x, mixed, enc_out, enc_gain2, enc_ffn_in, enc_ffn_out, enc_gain3, cross_kv
    )
    dec_after, lefts, dec_heads, query, token = dec_self(
        dec_table, answers[0], dec_gain1, dec_gain2, dec_qkv, dec_out, cross_query, after=[token]
    )
    packed, token = cross(count, query, pairs)
    if fast:
        acts = [across(value) for value in (first, mixed, second, hidden, third)]
    else:
        acts = [both_cores(v, k % 2) for k, v in enumerate((first, mixed, second, hidden, third))]
    gathered = lax.all_gather(packed, "pa")
    answer, early, mix, g_mix, g_middle, stat, g_gain3, token = dec_mid(
        gathered, dec_after, cotangent[0], dec_gain3, lefts, cross_out, dec_ffn_in, dec_ffn_out,
        after=[got for unused, got in acts[:4]],
    )
    g_pairs, partial, token = cross_back(count, query, pairs, g_mix, mix, stat)
    early_all = lax.all_gather(early, "pb")
    g_final, branch, g_enc_gain3, token = kv_back(g_pairs, cross_kv, final, enc_gain3)
    if fast:
        partial, token = add_rows(partial, swap(partial, "pa", 0), after=[token])
    g_inner, g_after, low, g_mixed, g_enc_gain2, token = ffn_back(
        branch, enc_ffn_out, slope, enc_ffn_in, after, enc_gain2, g_final, enc_out, after=[token]
    )

    def back_of(base, pairs, after, begun=None):
        return attention_back(count, table, pick, heads, g_mixed, mixed, stats, base, pairs, begun, after=after)

    def dec_end(part, got, token, wait=()):
        return dec_back(
            dec_table, answers[0], part, got, dec_after, g_middle, dec_heads,
            dec_gain1, dec_gain2, g_gain3, cross_query, dec_out, dec_qkv, after=[token, *wait],
        )

    def rows_end(token):
        return rows_back(
            grads, enc_qkv, x, enc_gain1, g_after, g_enc_gain2, g_enc_gain3,
            (diagonal_a, diagonal_b), pick_back, after=[token],
        )

    pb_me = lax.axis_index("pb").astype(jnp.int32).reshape(1)

    def outer_end(token):
        *outer, token = dec_outer(pb_me, early_all, late_all, pb_size, after=[token])
        return outer, token

    if fast:
        partial, token = add_rows(partial, swap(partial, "pa", 1), after=[token])
        got = swap(partial, "pa", 2)
        xk, xs, yk, ys, token = weights_one(me, acts[4], across(g_pairs), acts[3], across(branch), after=[token])
        one = ((xk, swap(xs, "pa", 1)), (yk, swap(ys, "pa", 2)))
        late, g_start, token = dec_end(partial, got, token)
        late_all = lax.all_gather(late, "pb")
        grads, diagonal_a, token = back_of(0, FIRST, [token])
        send_x, send_y, token = add_first(one, after=[token, early_all])
        last = (swap(send_x, "pa", 2), swap(send_y, "pa", 1))
        xk, xs, yk, ys, token = weights_two(me, acts[2], across(g_inner), acts[1], across(low), after=[token])
        two = ((xk, swap(xs, "pa", 1)), (yk, swap(ys, "pa", 2)))
        share_one, token = add_second([one[0] + last[:1], one[1] + last[1:]], after=[token])
        got_one = inward(share_one)
        grads, diagonal_b, token = back_of(FIRST, PAIRS - FIRST, [token], grads)
        there = swap(grads, "pa", 0)
        g_rows, small, token = rows_end(token)
        got_small = swap(small, "pa", 0)
        send_x, send_y, token = add_first(two, after=[token, late_all])
        last = (swap(send_x, "pa", 2), swap(send_y, "pa", 1))
        share_one, small, token = add_pair(share_one, got_one, (small, got_small), after=[token])
        got_one = between(share_one)
        got_small = swap(small, "pa", 1)
        outer, token = outer_end(token)
        xk, xs, yk, ys, token = weights_three(me, acts[0], (grads, there), after=[token])
        three = ((xk, swap(xs, "pa", 1)), (yk, swap(ys, "pa", 2)))
        share_two, token = add_second([two[0] + last[:1], two[1] + last[1:]], after=[token])
        got_two = inward(share_two)
        send_x, send_y, small, token = add_first(three, (small, got_small), after=[token])
        last = (swap(send_x, "pa", 2), swap(send_y, "pa", 1))
        got_small = swap(small, "pa", 2)
        share_one, token = add_pair(share_one, got_one, after=[token])
        total_one = outward(share_one)
        share_two, token = add_pair(share_two, got_two, after=[token])
        got_two = between(share_two)
        share_three, token = add_second([three[0] + last[:1], three[1] + last[1:]], (small, got_small), after=[token])
        parts = swap_parts(share_three)
        share_two, token = add_pair(share_two, got_two, after=[token])
        total_two = outward(share_two)
        total_three = spread_parts(*add_parts(share_three, parts, pb_me, after=[token]))
        small = total_three[D // pa_size :, :D]
        block = D // pa_size
        total_kv = jnp.concatenate([total_one[:block], total_one[block : 2 * block]], axis=1)
        total_ffn_out = total_one[2 * block :]
        second_part = 2 * block + block // 2
        total_ffn_in = jnp.concatenate(
            [total_two[first : first + block] for first in (0, block, second_part, second_part + block)], axis=1
        )
        total_out = jnp.concatenate([total_two[2 * block : second_part], total_two[second_part + 2 * block :]], axis=0)
        total_qkv = total_three[:block]
    else:
        partial = all_sum(partial, "pa")
        late, g_start, token = dec_end(partial, jnp.zeros_like(partial), token)
        late_all = lax.all_gather(late, "pb")
        grads, diagonal_a, token = back_of(0, FIRST, [token])
        grads, diagonal_b, token = back_of(FIRST, PAIRS - FIRST, [token], grads)
        g_rows, small, token = rows_end(token)
        outer, token = outer_end(token)
        small = all_sum(all_sum(small, "pa"), "pb")
        g_heads = jnp.concatenate([grads[0], grads[1], grads[2]], axis=1)
        total_kv = total_plain(share_over_pa(acts[4], across(g_pairs), 0))
        total_ffn_out = total_plain(share_over_pa(acts[3], across(branch), 1))
        total_ffn_in = total_plain(share_over_pa(acts[2], across(g_inner), 0))
        total_out = total_plain(share_over_pa(acts[1], across(low), 1))
        total_qkv = total_plain(share_over_pa(acts[0], across(g_heads), 0))

    d_qkv, d_out, d_query, d_cross, d_in, d_ffn, dec_small = outer
    dec_small = dec_small[0]
    dec_bias_rows = dec_small[3 * D :].reshape(H, STAT)[:, GROUP - ANS : GROUP]
    dec_bias_all = jnp.pad(jnp.transpose(dec_bias_rows[:, ::-1]), ((0, BUCKETS - ANS), (0, 0)))

    def own_part(vector, axis):
        height = vector.shape[0] // lax.axis_size(axis)
        return lax.dynamic_slice_in_dim(vector, lax.axis_index(axis) * height, height, axis=0)

    return (
        answer[None],
        g_rows.reshape(1, 1, SLOT, D),
        g_start[None],
        own_part(small[0], "pa"),
        total_qkv,
        jnp.transpose(small[4:16, :BUCKETS]),
        total_out,
        own_part(small[1], "pa"),
        total_ffn_in,
        total_ffn_out,
        own_part(small[2], "pa"),
        total_kv,
        own_part(dec_small[:D], "pb"),
        d_qkv,
        own_part(dec_bias_all, "pb"),
        d_out,
        own_part(dec_small[D : 2 * D], "pb"),
        d_query,
        d_cross,
        own_part(dec_small[2 * D : 3 * D], "pb"),
        d_in,
        d_ffn,
    )


def solution(mesh):
    copied = P()
    in_specs = (
        P("pb", "pa", None, None),
        P("pb", "pa"),
        P("pb", None, None),
        P("pb", None, None),
    ) + (copied,) * 19
    by_pa, by_pa_rows = P("pa"), P("pa", None)
    by_pb, by_pb_rows = P("pb"), P("pb", None)
    out_specs = (
        P("pb", None, None),
        P("pb", "pa", None, None),
        P("pb", None, None),
        by_pa,
        by_pa_rows,
        copied,
        by_pa_rows,
        by_pa,
        by_pa_rows,
        by_pa_rows,
        by_pa,
        by_pa_rows,
        by_pb,
        by_pb_rows,
        by_pb_rows,
        by_pb_rows,
        by_pb,
        by_pb_rows,
        by_pb_rows,
        by_pb,
        by_pb_rows,
        by_pb_rows,
    )
    return jax.shard_map(local, mesh=mesh, in_specs=in_specs, out_specs=out_specs, check_vma=False)
```

```python
import jax
import jax.numpy as jnp
import numpy as np
from jax import lax
from jax.experimental import pallas as pl
from jax.experimental.pallas import tpu as pltpu
from jax.sharding import PartitionSpec as P

D = 768
H = 12
HD = 64
FF = 3072
BUCKETS = 32
ANS = 20
SLOT = 512
PAIR = 2 * HD
PAIRS = H // 2
EDGE = 128
STRIP = 256
SPAN = 256
GROUP = 24
SENT = 40
STACK = H * GROUP
STAT = 128
STEPS = 4
WIDTH = FF // STEPS
FIRST = 4
EPS = 1e-06
MASKED = -1000000000.0
C_GELU = 0.7978845608028654
LOWER = jnp.bfloat16
WIDER = jnp.float32
EARLY = 7 * D + 2 * FF
LATE = 5 * D
AT = {
    "first": 0,
    "own": D,
    "second": 2 * D,
    "mix": 3 * D,
    "third": 4 * D,
    "hidden": 5 * D,
    "g_middle": 5 * D + FF,
    "g_inner": 6 * D + FF,
    "g_out": 6 * D + 2 * FF,
    "g_heads": 0,
    "g_after": 3 * D,
    "g_query": 4 * D,
}


def tile_classes(away):
    rows = [np.clip(EDGE * d - away, -(BUCKETS // 2), BUCKETS // 2 - 1) + BUCKETS // 2 for d in (-1, 0, 1)]
    return np.eye(BUCKETS, dtype=np.float32)[np.concatenate(rows)]


LANES = np.arange(SPAN)
PICK = tile_classes(np.where(LANES < EDGE, LANES, LANES - SPAN)).T
ENDS = np.repeat(np.eye(BUCKETS, dtype=np.float32)[[0, BUCKETS - 1]], EDGE, axis=0)
PICK_BACK = np.pad(np.concatenate([tile_classes(LANES - (EDGE - 1)), ENDS]), ((0, 0), (0, STAT - BUCKETS)))

SCALARS = pl.BlockSpec(memory_space=pltpu.SMEM)
ANY = pl.BlockSpec(memory_space=pl.ANY)
WHOLE = pl.BlockSpec(memory_space=pltpu.VMEM)
TOKEN = (8, 128)


def wide(*shape):
    return jax.ShapeDtypeStruct(shape, WIDER)


def narrow(*shape):
    return jax.ShapeDtypeStruct(shape, LOWER)


def run(name, body, ins, in_specs, outs, out_specs=None, after=(), grid=(), scratch=(), flops=10**9, mib=63, alias=None):
    count, extra, results = len(ins), len(after), len(outs)
    if out_specs is None:
        out_specs = [WHOLE] * results
    zeros = (lambda *s: (0, 0)) if grid else (lambda: (0, 0))

    def wrapped(*refs):
        refs[count + extra + results][...] = jnp.zeros(TOKEN, WIDER)
        body(*refs[:count], *refs[count + extra : count + extra + results], *refs[count + extra + results + 1 :])

    got = pl.pallas_call(
        wrapped,
        grid=grid,
        out_shape=tuple(outs) + (wide(*TOKEN),),
        in_specs=list(in_specs) + [ANY] * extra,
        out_specs=tuple(out_specs) + (pl.BlockSpec(TOKEN, zeros),),
        scratch_shapes=list(scratch),
        input_output_aliases=alias or {},
        compiler_params=pltpu.CompilerParams(vmem_limit_bytes=mib * 2**20),
        cost_estimate=pl.CostEstimate(flops=10 * flops, bytes_accessed=1, transcendentals=0),
        name=name,
    )(*ins, *after)
    return got


def product(left, right):
    return jnp.dot(left, right, preferred_element_type=WIDER)


def left_product(left, right):
    return lax.dot_general(left, right, (((0,), (0,)), ((), ())), preferred_element_type=WIDER)


def right_product(left, right):
    return lax.dot_general(left, right, (((1,), (1,)), ((), ())), preferred_element_type=WIDER)


def split_product(left, right, terms):
    total = None
    for k in range(terms):
        part = left.astype(LOWER)
        left = left - part.astype(WIDER)
        term = product(part, right)
        total = term if total is None else total + term
    return total


def silu_like(inner):
    square = inner * inner
    tanh = jnp.tanh(inner * (C_GELU + (C_GELU * 0.044715) * square))
    half = 0.5 + 0.5 * tanh
    value = inner * half
    slope = half + value * (1.0 - tanh) * (C_GELU + (3.0 * C_GELU * 0.044715) * square)
    return value, slope


def row_of(ref):
    return ref[...].reshape(1, D)


def scale_of(values):
    return lax.rsqrt(jnp.mean(values * values, axis=-1, keepdims=True) + EPS)


def norm_pull(values, gain, grad):
    scale = scale_of(values)
    lifted = grad * gain
    inside = jnp.sum(values * lifted, axis=-1, keepdims=True)
    back = scale * lifted - values * (scale * scale * scale * inside * (1.0 / D))
    return back, jnp.sum(grad * values * scale, axis=0, keepdims=True)


def fetch(pairs, sems):
    copies = [pltpu.make_async_copy(s, t, sems.at[k]) for k, (s, t) in enumerate(pairs)]
    for copy in copies:
        copy.start()
    return copies


def bias_tiles(u_ref, head):
    tiles = []
    for d in range(3):
        row = u_ref[pl.ds(head, 1), SPAN * d : SPAN * d + SPAN]
        spread = jnp.broadcast_to(row, (EDGE, SPAN))
        tiles.append(pltpu.roll(spread, 0, 1, stride=1, stride_axis=0)[:, :EDGE])
    return tiles


def key_masks(n):
    places = lax.broadcasted_iota(jnp.int32, (EDGE, EDGE), 0)
    return [jnp.where(places + EDGE * j < n, 0.0, MASKED) for j in range(SLOT // EDGE)]


def score_blocks(raw, tiles, masks, low, high, first):
    columns = []
    for c in range(STRIP // EDGE):
        blocks = []
        for j in range(SLOT // EDGE):
            block = raw[EDGE * j : EDGE * j + EDGE, EDGE * c : EDGE * c + EDGE]
            d = j - first - c
            block = block + (tiles[d + 1] if abs(d) <= 1 else (low if d < 0 else high))
            blocks.append(block + masks[j] if j > 0 else block)
        columns.append(blocks)
    return columns


def paved(columns, kind):
    return jnp.concatenate([jnp.concatenate([b.astype(kind) for b in blocks], axis=0) for blocks in columns], axis=1)


def fill_rows(table_ref, pick_ref, u_ref):
    @pl.when(pl.program_id(0) == 0)
    def _():
        u_ref[...] = split_product(table_ref[...], pick_ref[...], 3)


def attn_fwd_kernel(n_ref, ends_ref, table_ref, pick_ref, x_ref, g1_ref, wq_ref, wk_ref, wv_ref, first_ref, heads_ref, o_ref, st_ref, u_ref):
    fill_rows(table_ref, pick_ref, u_ref)
    step = pl.program_id(0)

    @pl.when(step == 0)
    def _():
        rows = x_ref[...].astype(WIDER)
        first_ref[...] = (rows * scale_of(rows) * row_of(g1_ref)).astype(LOWER)

    masks = key_masks(n_ref[0])
    first = first_ref[...]
    for k, w_ref in enumerate((wq_ref, wk_ref, wv_ref)):
        heads_ref[k] = product(first, w_ref[...]).astype(LOWER)
    q_ref, k_ref = heads_ref.at[0], heads_ref.at[1]
    values = jnp.transpose(heads_ref[2])
    ones = jnp.ones((16, SLOT), LOWER)
    mixed = []
    for h in range(2):
        head = 2 * step + h
        low, high = ends_ref[head, 0], ends_ref[head, BUCKETS - 1]
        tiles = bias_tiles(u_ref, head)
        cols = slice(HD * h, HD * h + HD)
        keys = k_ref[:, cols]
        left = jnp.concatenate([values[cols], ones], axis=0)
        strips = []
        for i in range(0, SLOT // EDGE, STRIP // EDGE):
            lanes = slice(EDGE * i, EDGE * i + STRIP)
            raw = right_product(keys, q_ref[lanes, cols] * 0.125)
            tops, powers = [], []
            for blocks in score_blocks(raw, tiles, masks, low, high, i):
                top = jnp.maximum(jnp.maximum(blocks[0], blocks[1]), jnp.maximum(blocks[2], blocks[3]))
                top = jnp.max(top, axis=0, keepdims=True)
                tops.append(top)
                powers.append([jnp.exp(block - top) for block in blocks])
            out = product(left, paved(powers, LOWER))
            total = out[HD : HD + 1]
            st_ref[0, h : h + 1, lanes] = jnp.concatenate(tops, axis=1) + jnp.log(total)
            strips.append(out[:HD] * (1.0 / total))
        mixed.append(jnp.concatenate(strips, axis=1))
    lanes = pl.ds(pl.multiple_of(step * PAIR, PAIR), PAIR)
    o_ref[:, lanes] = jnp.transpose(jnp.concatenate(mixed, axis=0)).astype(LOWER)


def attn_bwd_kernel(base):
    def body(
        n_ref, ends_ref, table_ref, pick_ref, h_ref, g_ref, o_ref, st_ref, gh_ref, gb_ref, u_ref
    ):
        q_ref, k_ref, v_ref = h_ref.at[0], h_ref.at[1], h_ref.at[2]
        fill_rows(table_ref, pick_ref, u_ref)
        step = pl.program_id(0) + base
        masks = key_masks(n_ref[0])
        keys_t = jnp.transpose(k_ref[...])
        rows = lax.broadcasted_iota(jnp.int32, (EDGE, EDGE), 0)
        columns = lax.broadcasted_iota(jnp.int32, (EDGE, EDGE), 1)
        mirror = jnp.where(rows + columns == EDGE - 1, 1.0, 0.0).astype(LOWER)
        rows = lax.broadcasted_iota(jnp.int32, (16, SLOT), 0) * EDGE
        columns = lax.broadcasted_iota(jnp.int32, (16, SLOT), 1)
        places = jnp.where((columns >= rows) & (columns < rows + EDGE), 1.0, 0.0).astype(LOWER)
        rows = lax.broadcasted_iota(jnp.int32, (16, PAIR), 0) * HD
        columns = lax.broadcasted_iota(jnp.int32, (16, PAIR), 1)
        halves = jnp.where((columns >= rows) & (columns < rows + HD), 1.0, 0.0).astype(LOWER)
        met = g_ref[...].astype(WIDER) * o_ref[...].astype(WIDER)
        upper = met.astype(LOWER)
        lower = (met - upper.astype(WIDER)).astype(LOWER)
        weighted = right_product(halves, upper) + right_product(halves, lower)
        grad_queries = []
        gb_ref[0, 2:8, :] = jnp.zeros((6, 4 * SPAN), WIDER)
        for h in range(2):
            head = 2 * step + h
            low, high = ends_ref[head, 0], ends_ref[head, BUCKETS - 1]
            tiles = bias_tiles(u_ref, head)
            cols = slice(HD * h, HD * h + HD)
            keys = k_ref[:, cols]
            values = v_ref[:, cols]
            left = jnp.concatenate([keys_t[cols], places], axis=0)
            grad_keys = jnp.zeros((SLOT, HD), WIDER)
            grad_values = jnp.zeros((SLOT, HD), WIDER)
            strips = []
            sums = {}

            def gather(d, block):
                sums[d] = sums[d] + block if d in sums else block

            for i in range(0, SLOT // EDGE, STRIP // EDGE):
                lanes = slice(EDGE * i, EDGE * i + STRIP)
                query = q_ref[lanes, cols]
                grad = g_ref[lanes, cols]
                raw = right_product(keys, query * 0.125)
                grad_probs = right_product(values, grad)
                probs, changes = [], []
                for c, blocks in enumerate(score_blocks(raw, tiles, masks, low, high, i)):
                    part = slice(EDGE * (i + c), EDGE * (i + c) + EDGE)
                    total = st_ref[0, h : h + 1, part]
                    mean = weighted[h : h + 1, part]
                    probs.append([jnp.exp(block - total) for block in blocks])
                    changes.append([])
                    for j in range(SLOT // EDGE):
                        gap = grad_probs[EDGE * j : EDGE * j + EDGE, EDGE * c : EDGE * c + EDGE] - mean
                        change = probs[c][j] * gap
                        changes[c].append(change)
                        if abs(j - i - c) <= 1:
                            gather(j - i - c, change)
                rounded = paved(changes, LOWER)
                out = product(left, rounded)
                strips.append(out[:HD])
                for c in range(STRIP // EDGE):
                    for j in range(SLOT // EDGE):
                        if abs(j - i - c) > 1:
                            gather(2 if j > i + c else -2, out[HD + j : HD + j + 1, EDGE * c : EDGE * c + EDGE])
                grad_keys += product(rounded, query)
                grad_values += product(paved(probs, LOWER), grad)
            grad_queries.append(jnp.concatenate(strips, axis=1))
            gh_ref[1, :, cols] = (grad_keys * 0.125).astype(LOWER)
            gh_ref[2, :, cols] = grad_values.astype(LOWER)
            empty = jnp.zeros((EDGE, SPAN - EDGE), WIDER)
            band = jnp.concatenate([sums[-1], sums[0], sums[1]], axis=1)
            upper = band.astype(LOWER)
            lower = (band - upper.astype(WIDER)).astype(LOWER)
            mirrored = product(mirror, upper) + product(mirror, lower)
            for d in range(3):
                spread = jnp.concatenate([mirrored[:, EDGE * d : EDGE * d + EDGE], empty], axis=1)
                turned = pltpu.roll(spread, 0, 1, stride=1, stride_axis=0)
                gb_ref[0, h : h + 1, SPAN * d : SPAN * d + SPAN] = jnp.sum(turned, axis=0, keepdims=True)
            for place, d in ((3 * SPAN, -2), (3 * SPAN + EDGE, 2)):
                gb_ref[0, h : h + 1, place : place + EDGE] = sums[d]
        gh_ref[0] = (jnp.transpose(jnp.concatenate(grad_queries, axis=0)) * 0.125).astype(LOWER)

    return body


def columns_at(first):
    return pl.BlockSpec((SLOT, PAIR), lambda s: (0, first + s))


def stats_at(first):
    return pl.BlockSpec((1, 2, SLOT), lambda s: (first + s, 0, 0))


def pair_of_all(base):
    return pl.BlockSpec((3, SLOT, PAIR), lambda s: (0, 0, base + s))


def attention_back(count, table, pick, heads, grad_mixed, mixed, stats, base, half, begun=None, after=()):
    ins = [count, table, table, pick, heads, grad_mixed, mixed, stats]
    specs = [pair_of_all(base), columns_at(base), columns_at(base), stats_at(base)]
    body = attn_bwd_kernel(base)
    if begun is not None:
        ins.append(begun)
        specs.append(ANY)
        inner = body

        def body(*refs):
            inner(*refs[:8], *refs[9:])

    return run(
        "enc_attention_back",
        body,
        ins,
        [SCALARS, SCALARS, WHOLE, WHOLE] + specs,
        [narrow(3, SLOT, D), wide(half, 8, 4 * SPAN)],
        [pair_of_all(base), pl.BlockSpec((1, 8, 4 * SPAN), lambda s: (s, 0, 0))],
        after=after,
        grid=(half,),
        scratch=[pltpu.VMEM((H, 3 * SPAN), WIDER)],
        flops=2 * 5 * H * SLOT * SLOT * HD * 4,
        alias={8: 0} if begun is not None else None,
    )


def send_out(pairs, sems, first):
    copies = [pltpu.make_async_copy(s, t, sems.at[first + k]) for k, (s, t) in enumerate(pairs)]
    for copy in copies:
        copy.start()
    return copies


def chunk(k):
    return slice(WIDTH * k, WIDTH * k + WIDTH)


def copy_all(pairs, sems):
    return [pltpu.make_async_copy(s, t, sems.at[k]) for k, (s, t) in enumerate(pairs)]


def forward_kernel(
    n_ref, ends_ref, table_ref, pick_ref, x_ref, g1_ref, wq_ref, wk_ref, wv_ref,
    g2_ref, g3_ref, query_ref, wo_any, in_any, out_any, kv_any,
    first_ref, heads_ref, mixed_ref, st_ref, packed_ref,
    after_any, second_any, slope_any, hidden_any, final_any, third_any, pairs_any,
    u_ref, wo_ref, in_ref, out_ref, kv_ref,
    after_ref, second_ref, slope_ref, hidden_ref, final_ref, third_ref, pairs_ref,
    sems, out_sems,
):
    step = pl.program_id(0)
    pairs = [(wo_any, wo_ref)]
    for k in range(STEPS):
        pairs += [(in_any.at[:, chunk(k)], in_ref.at[k]), (out_any.at[chunk(k)], out_ref.at[k])]
    copies = copy_all(pairs + [(kv_any, kv_ref)], sems)

    @pl.when(step == 0)
    def _():
        for copy in copies:
            copy.start()

    attn_fwd_kernel(
        n_ref, ends_ref, table_ref, pick_ref, x_ref, g1_ref, wq_ref, wk_ref, wv_ref,
        first_ref, heads_ref, mixed_ref, st_ref, u_ref,
    )

    @pl.when(step == PAIRS - 1)
    def _():
        for copy in copies:
            copy.wait()
        after = x_ref[...].astype(WIDER) + product(mixed_ref[...], wo_ref[...])
        after_ref[...] = after
        second = (after * scale_of(after) * row_of(g2_ref)).astype(LOWER)
        second_ref[...] = second
        inner = product(second, in_ref[0])
        sent = send_out([(after_ref, after_any), (second_ref, second_any)], out_sems, 0)
        total = after
        for k in range(STEPS):
            following = product(second, in_ref[k + 1]) if k + 1 < STEPS else None
            value, slope = silu_like(inner)
            slope_ref[:, chunk(k)] = slope.astype(LOWER)
            hidden = value.astype(LOWER)
            hidden_ref[:, chunk(k)] = hidden
            total = total + product(hidden, out_ref[k])
            inner = following
            if k % 2:
                half = slice(WIDTH * (k - 1), WIDTH * (k + 1))
                sent += send_out(
                    [(slope_ref.at[:, half], slope_any.at[:, half]), (hidden_ref.at[:, half], hidden_any.at[:, half])],
                    out_sems, len(sent),
                )
        final_ref[...] = total
        third = (total * scale_of(total) * row_of(g3_ref)).astype(LOWER)
        third_ref[...] = third
        sent += send_out([(final_ref, final_any), (third_ref, third_any)], out_sems, len(sent))
        for k in range(2):
            half = slice(D * k, D * k + D)
            pairs_ref[:, half] = product(third, kv_ref[:, half]).astype(LOWER)
        sent += send_out([(pairs_ref, pairs_any)], out_sems, len(sent))
        cross_kernel(n_ref, query_ref, pairs_ref, packed_ref)
        for copy in sent:
            copy.wait()


def whole(*shape):
    return pl.BlockSpec(shape, lambda s: (0,) * len(shape))


def forward(count, table, pick, x, gain1, qkv, gain2, gain3, query, wo, ffn_in, ffn_out, kv, after=()):
    def weights_at(first):
        return pl.BlockSpec((D, PAIR), lambda s: (0, first + s))

    kept = [wide(SLOT, D), narrow(SLOT, D), narrow(SLOT, FF), narrow(SLOT, FF), wide(SLOT, D), narrow(SLOT, D), narrow(SLOT, 2 * D)]
    return run(
        "enc_forward",
        forward_kernel,
        [count, table, table, pick, x, gain1, qkv, qkv, qkv, gain2, gain3, query, wo, ffn_in, ffn_out, kv],
        [SCALARS, SCALARS, WHOLE, WHOLE, whole(SLOT, D), whole(D), weights_at(0), weights_at(PAIRS), weights_at(2 * PAIRS)]
        + [whole(D), whole(D), whole(GROUP, D)] + [ANY] * 4,
        [narrow(SLOT, D), narrow(3, SLOT, D), narrow(SLOT, D), wide(PAIRS, 2, SLOT), wide(GROUP, D + STAT)] + kept,
        [whole(SLOT, D), pair_of_all(0), whole(SLOT, D), stats_at(0), whole(GROUP, D + STAT)] + [ANY] * 7,
        after=after,
        grid=(PAIRS,),
        scratch=[
            pltpu.VMEM((H, 3 * SPAN), WIDER),
            pltpu.VMEM((D, D), LOWER),
            pltpu.VMEM((STEPS, D, WIDTH), LOWER),
            pltpu.VMEM((STEPS, WIDTH, D), LOWER),
            pltpu.VMEM((D, 2 * D), LOWER),
        ]
        + [pltpu.VMEM(out.shape, out.dtype) for out in kept]
        + [pltpu.SemaphoreType.DMA((2 * STEPS + 2,)), pltpu.SemaphoreType.DMA((9,))],
        flops=2 * SLOT * D * (D + 2 * FF + 2 * D),
    )


def ffn_back_kernel(
    branch_ref, g2_ref, gfinal_any, after_any, slope_any, out_any, in_any, wo_any,
    ginner_any, gafter_any, low_any, gmixed_any, gain_ref,
    gfinal_ref, after_ref, slope_ref, out_ref, in_ref, wo_ref, ginner_ref, gafter_ref, low_ref, gmixed_ref,
    sems, out_sems,
):
    pairs = []
    for k in range(STEPS):
        pairs += [(out_any.at[chunk(k)], out_ref.at[k]), (slope_any.at[:, chunk(k)], slope_ref.at[k])]
        pairs += [(in_any.at[:, chunk(k)], in_ref.at[k])]
    copies = fetch(pairs + [(after_any, after_ref), (gfinal_any, gfinal_ref), (wo_any, wo_ref)], sems)
    branch = branch_ref[...]
    copies[0].wait()
    grad = right_product(branch, out_ref[0])
    total = None
    sent = []
    for k in range(STEPS):
        copies[3 * k + 1].wait()
        copies[3 * k + 2].wait()
        copies[3 * k + 3].wait()
        following = right_product(branch, out_ref[k + 1]) if k + 1 < STEPS else None
        inner = (grad * slope_ref[k].astype(WIDER)).astype(LOWER)
        ginner_ref[:, chunk(k)] = inner
        term = right_product(inner, in_ref[k])
        total = term if total is None else total + term
        grad = following
        sent += send_out([(ginner_ref.at[:, chunk(k)], ginner_any.at[:, chunk(k)])], out_sems, len(sent))
    copies[3 * STEPS + 1].wait()
    copies[3 * STEPS + 2].wait()
    back, gain = norm_pull(after_ref[...], row_of(g2_ref), total)
    gain_ref[...] = gain
    g_after = gfinal_ref[...] + back
    gafter_ref[...] = g_after
    low = g_after.astype(LOWER)
    low_ref[...] = low
    sent += send_out([(gafter_ref, gafter_any), (low_ref, low_any)], out_sems, len(sent))
    gmixed_ref[...] = right_product(low, wo_ref[...]).astype(LOWER)
    sent += send_out([(gmixed_ref, gmixed_any)], out_sems, len(sent))
    for copy in sent:
        copy.wait()


def ffn_back(branch, ffn_out, slope, ffn_in, after_rows, gain2, g_final, wo, after=()):
    outs = [narrow(SLOT, FF), wide(SLOT, D), narrow(SLOT, D), narrow(SLOT, D)]
    return run(
        "enc_ffn_back",
        ffn_back_kernel,
        [branch, gain2, g_final, after_rows, slope, ffn_out, ffn_in, wo],
        [WHOLE] * 2 + [ANY] * 6,
        outs + [wide(1, D)],
        [ANY] * 4 + [WHOLE],
        after=after,
        scratch=[
            pltpu.VMEM((SLOT, D), WIDER),
            pltpu.VMEM((SLOT, D), WIDER),
            pltpu.VMEM((STEPS, SLOT, WIDTH), LOWER),
            pltpu.VMEM((STEPS, WIDTH, D), LOWER),
            pltpu.VMEM((STEPS, D, WIDTH), LOWER),
            pltpu.VMEM((D, D), LOWER),
        ]
        + [pltpu.VMEM(out.shape, out.dtype) for out in outs]
        + [pltpu.SemaphoreType.DMA((3 * STEPS + 3,)), pltpu.SemaphoreType.DMA((STEPS + 3,))],
        flops=2 * SLOT * D * (D + 2 * FF),
    )


def rows_back_kernel(
    g_ref, w_ref, x_ref, g1_ref, gafter_ref, gain2_ref, gain3_ref, da_ref, db_ref, pick_ref,
    grows_ref, small_ref, total_ref,
):
    step = pl.program_id(0)

    @pl.when(step == 0)
    def _():
        total_ref[...] = jnp.zeros((SLOT, D), WIDER)

    total_ref[...] += right_product(g_ref[0], w_ref[...])

    @pl.when(step == 2)
    def _():
        back, gain = norm_pull(x_ref[...].astype(WIDER), row_of(g1_ref), total_ref[...])
        grows_ref[...] = gafter_ref[...] + back
        sums = [ref[k, :2] for ref in (da_ref, db_ref) for k in range(ref.shape[0])]
        table = split_product(jnp.concatenate(sums, axis=0), pick_ref[...], 2)
        small_ref[...] = jnp.zeros((16, D), WIDER)
        small_ref[0:1] = gain
        small_ref[1:2] = gain2_ref[...]
        small_ref[2:3] = gain3_ref[...]
        small_ref[4:16, :STAT] = table


def rows_back(grads, qkv, x, gain1, g_after, gain2, gain3, diagonals, pick_back, after=()):
    rows = whole(SLOT, D)
    return run(
        "enc_rows_back",
        rows_back_kernel,
        [grads, qkv, x, gain1, g_after, gain2, gain3, diagonals[0], diagonals[1], pick_back],
        [pl.BlockSpec((1, SLOT, D), lambda s: (s, 0, 0)), pl.BlockSpec((D, D), lambda s: (0, s)), rows, whole(D), rows]
        + [whole(1, D), whole(1, D), whole(*diagonals[0].shape), whole(*diagonals[1].shape), whole(4 * SPAN, STAT)],
        [wide(SLOT, D), wide(16, D)],
        [rows, whole(16, D)],
        after=after,
        grid=(3,),
        scratch=[pltpu.VMEM((SLOT, D), WIDER)],
        flops=0,
    )


def head_lanes(h):
    lanes = lax.broadcasted_iota(jnp.int32, (GROUP, D), 1)
    return (lanes >= h * HD) & (lanes < (h + 1) * HD)


def stack_heads(flat):
    return jnp.concatenate([jnp.where(head_lanes(h), flat, 0.0) for h in range(H)], axis=0)


def merge_heads(stacked):
    total = jnp.zeros((GROUP, D), WIDER)
    for h in range(H):
        total = total + jnp.where(head_lanes(h), stacked[GROUP * h : GROUP * h + GROUP], 0.0)
    return total


def lanes_to_column(stat):
    lanes = lax.broadcasted_iota(jnp.int32, (GROUP, STAT), 1)
    parts = [jnp.sum(jnp.where(lanes == h, stat, 0.0), axis=1, keepdims=True) for h in range(H)]
    return jnp.concatenate(parts, axis=0)


def column_to_lanes(column, first):
    lanes = lax.broadcasted_iota(jnp.int32, (GROUP, STAT), 1)
    total = jnp.zeros((GROUP, STAT), WIDER)
    for h in range(H):
        total = total + jnp.where(lanes == first + h, column[GROUP * h : GROUP * h + GROUP], 0.0)
    return total


def spread_heads(stat):
    rows = lax.broadcasted_iota(jnp.int32, (STAT, D), 0) * HD
    lanes = lax.broadcasted_iota(jnp.int32, (STAT, D), 1)
    spread = jnp.where((lanes >= rows) & (lanes < rows + HD), 1.0, 0.0).astype(LOWER)
    return split_product(stat, spread, 2)


def own_scores(query, keys, table_ref):
    raw = right_product(query, keys)
    rows = lax.broadcasted_iota(jnp.int32, (GROUP, GROUP), 0)
    columns = lax.broadcasted_iota(jnp.int32, (GROUP, GROUP), 1)
    away = rows - columns
    parts = []
    for h in range(H):
        bias = jnp.full((GROUP, GROUP), table_ref[h, 0], WIDER)
        for d in range(1, GROUP):
            bias = jnp.where(away == d, table_ref[h, d], bias)
        part = raw[GROUP * h : GROUP * h + GROUP] + bias
        parts.append(jnp.where(away >= 0, part, MASKED))
    scores = jnp.concatenate(parts, axis=0)
    powers = jnp.exp(scores - jnp.max(scores, axis=1, keepdims=True))
    return powers / jnp.sum(powers, axis=1, keepdims=True)


def padded(ref, pad_ref):
    pad_ref[...] = jnp.zeros((GROUP, D), WIDER)
    pad_ref[:ANS] = ref[...].astype(WIDER)
    return pad_ref[...]


def answer_rows(width):
    return lax.broadcasted_iota(jnp.int32, (GROUP, width), 0) < ANS


def dec_self_kernel(
    table_ref, x_ref, g1_ref, g2_ref, qkv_any, out_any, query_any,
    after_ref, lefts_ref, heads_ref, query_ref,
    qkv_ref, out_ref, cross_ref, pad_ref, sems,
):
    copies = fetch(((qkv_any, qkv_ref), (out_any, out_ref), (query_any, cross_ref)), sems)
    start = padded(x_ref, pad_ref)
    first = (start * scale_of(start) * row_of(g1_ref)).astype(LOWER)
    copies[0].wait()
    heads = product(first, qkv_ref[...]).astype(LOWER)
    heads_ref[...] = heads
    query = stack_heads(heads.astype(WIDER)[:, :D] * 0.125).astype(LOWER)
    probs = own_scores(query, heads[:, D : 2 * D], table_ref)
    own = merge_heads(product(probs.astype(LOWER), heads[:, 2 * D :]))
    own = jnp.where(answer_rows(D), own, 0.0).astype(LOWER)
    copies[1].wait()
    after = start + product(own, out_ref[...])
    after_ref[...] = after
    second = (after * scale_of(after) * row_of(g2_ref)).astype(LOWER)
    copies[2].wait()
    query_ref[...] = product(second, cross_ref[...]).astype(LOWER)
    lefts_ref[:, :D] = first
    lefts_ref[:, D : 2 * D] = own
    lefts_ref[:, 2 * D :] = second


def masked_cross(n_ref, query_ref, pairs_ref):
    query = stack_heads(query_ref[...].astype(WIDER) * 0.125).astype(LOWER)
    raw = right_product(query, pairs_ref[:, :D])
    places = lax.broadcasted_iota(jnp.int32, (STACK, SLOT), 1)
    return query, jnp.where(places < n_ref[0], raw, MASKED)


def cross_kernel(n_ref, query_ref, pairs_ref, packed_ref):
    unused, scores = masked_cross(n_ref, query_ref, pairs_ref)
    top = jnp.max(scores, axis=1, keepdims=True)
    powers = jnp.exp(scores - top)
    total = jnp.sum(powers, axis=1, keepdims=True)
    probs = (powers / total).astype(LOWER)
    packed_ref[:, :D] = merge_heads(product(probs, pairs_ref[:, D:]))
    packed_ref[:, D:] = column_to_lanes(top, 0) + column_to_lanes(total, STAT // 2)


def dec_mid_kernel(
    n_ref, parts_ref, after_ref, cot_ref, g3_ref, lefts_ref, query_ref, e3_ref,
    pairs_any, cross_any, in_any, out_any, kv_any, final_any,
    answer_ref, early_ref, gmid_ref, gain_ref, partial_ref, gain_enc_ref, gpairs_any, gfinal_any, branch_any,
    pairs_ref, cross_ref, in_ref, out_ref, kv_ref, final_ref, gpairs_ref, gfinal_ref, branch_ref, pad_ref,
    sems, out_sems,
):
    held_pairs = ((cross_any, cross_ref), (in_any, in_ref), (out_any, out_ref), (pairs_any, pairs_ref))
    copies = fetch(held_pairs + ((kv_any, kv_ref), (final_any, final_ref)), sems)
    size = parts_ref.shape[0]
    used = lax.broadcasted_iota(jnp.int32, (GROUP, STAT), 1) < H
    tops = [parts_ref[k, :, D:] for k in range(size)]
    totals = [pltpu.roll(stat, STAT // 2, 1) for stat in tops]
    top = tops[0]
    for k in range(1, size):
        top = jnp.maximum(top, tops[k])
    weights = [jnp.where(used, totals[k] * jnp.exp(tops[k] - top), 0.0) for k in range(size)]
    total = weights[0]
    for k in range(1, size):
        total = total + weights[k]
    total = jnp.where(used, total, 1.0)
    mix = jnp.zeros((GROUP, D), WIDER)
    for k in range(size):
        mix = mix + parts_ref[k, :, :D] * spread_heads(weights[k] / total)
    mix_low = mix.astype(LOWER)
    copies[0].wait()
    middle = after_ref[...] + product(mix_low, cross_ref[...])
    third = (middle * scale_of(middle) * row_of(g3_ref)).astype(LOWER)
    copies[1].wait()
    inner = product(third, in_ref[...])
    value, slope = silu_like(inner)
    hidden = value.astype(LOWER)
    copies[2].wait()
    answer = (middle + product(hidden, out_ref[...])).astype(LOWER)
    answer_ref[...] = answer[:ANS]
    grad = padded(cot_ref, pad_ref)
    out_low = grad.astype(LOWER)
    g_inner = (right_product(out_low, out_ref[...]) * slope).astype(LOWER)
    back, gain = norm_pull(middle, row_of(g3_ref), right_product(g_inner, in_ref[...]))
    gain_ref[...] = gain
    g_middle = grad + back
    gmid_ref[...] = g_middle
    middle_low = g_middle.astype(LOWER)
    g_mix = right_product(middle_low, cross_ref[...]).astype(LOWER)

    def store(name, rows):
        early_ref[:, AT[name] : AT[name] + rows.shape[1]] = rows

    def kept(rows):
        return jnp.where(answer_rows(rows.shape[1]), rows.astype(WIDER), 0.0).astype(LOWER)

    early_ref[:, : 3 * D] = kept(lefts_ref[...])
    store("mix", kept(mix_low))
    store("third", kept(third))
    store("hidden", kept(hidden))
    store("g_middle", middle_low)
    store("g_inner", g_inner)
    store("g_out", out_low)
    copies[3].wait()
    copies[4].wait()
    copies[5].wait()
    query, scores = masked_cross(n_ref, query_ref, pairs_ref)
    probs = jnp.exp(scores - lanes_to_column(jnp.where(used, top, 0.0))) / lanes_to_column(total)
    grad = stack_heads(g_mix.astype(WIDER))
    weighted = jnp.sum(grad * jnp.concatenate([mix] * H, axis=0), axis=1, keepdims=True)
    grad = grad.astype(LOWER)
    grad_probs = right_product(grad, pairs_ref[:, D:])
    rounded = (probs * (grad_probs - weighted)).astype(LOWER)
    g_keys = left_product(rounded, query).astype(LOWER)
    g_values = left_product(probs.astype(LOWER), grad).astype(LOWER)
    gpairs_ref[:, :D] = g_keys
    gpairs_ref[:, D:] = g_values
    sent = send_out([(gpairs_ref, gpairs_any)], out_sems, 0)
    partial_ref[...] = merge_heads(product(rounded, pairs_ref[:, :D])) * 0.125
    g_third = right_product(g_keys, kv_ref[:, :D]) + right_product(g_values, kv_ref[:, D:])
    back, gain = norm_pull(final_ref[...], row_of(e3_ref), g_third)
    gain_enc_ref[...] = gain
    gfinal_ref[...] = back
    branch_ref[...] = back.astype(LOWER)
    sent += send_out([(gfinal_ref, gfinal_any), (branch_ref, branch_any)], out_sems, 1)
    for copy in sent:
        copy.wait()


def dec_back_kernel(
    table_ref, x_ref, part_ref, got_ref, after_ref, gmid_ref, heads_ref,
    g1_ref, g2_ref, gain3_ref, query_any, out_any, qkv_any,
    late_ref, gstart_ref,
    cross_ref, out_ref, qkv_ref, pad_ref, sems,
):
    copies = fetch(((query_any, cross_ref), (out_any, out_ref), (qkv_any, qkv_ref)), sems)
    g_query = (part_ref[...] + got_ref[...]).astype(LOWER)
    copies[0].wait()
    back, gain2 = norm_pull(after_ref[...], row_of(g2_ref), right_product(g_query, cross_ref[...]))
    g_after = gmid_ref[...] + back
    after_low = g_after.astype(LOWER)
    copies[1].wait()
    g_own = stack_heads(right_product(after_low, out_ref[...])).astype(LOWER)
    heads = heads_ref[...]
    query = stack_heads(heads.astype(WIDER)[:, :D] * 0.125).astype(LOWER)
    probs = own_scores(query, heads[:, D : 2 * D], table_ref)
    grad_probs = right_product(g_own, heads[:, 2 * D :])
    rounded = (probs * (grad_probs - jnp.sum(probs * grad_probs, axis=1, keepdims=True))).astype(LOWER)
    g_q = (merge_heads(product(rounded, heads[:, D : 2 * D])) * 0.125).astype(LOWER)
    g_k = left_product(rounded, query).astype(LOWER)
    g_v = left_product(probs.astype(LOWER), g_own).astype(LOWER)
    g_heads = jnp.concatenate([g_q, g_k, g_v], axis=1)
    copies[2].wait()
    start = padded(x_ref, pad_ref)
    back, gain1 = norm_pull(start, row_of(g1_ref), right_product(g_heads, qkv_ref[...]))
    gstart_ref[...] = (g_after + back)[:ANS]
    spread = rounded.astype(WIDER)
    rows = lax.broadcasted_iota(jnp.int32, (GROUP, GROUP), 0)
    columns = lax.broadcasted_iota(jnp.int32, (GROUP, GROUP), 1)
    mirror = jnp.where(rows + columns == GROUP - 1, 1.0, 0.0).astype(LOWER)
    empty = jnp.zeros((GROUP, STAT - GROUP), WIDER)
    tables = []
    for h in range(H):
        part = product(mirror, spread[GROUP * h : GROUP * h + GROUP].astype(LOWER))
        turned = pltpu.roll(jnp.concatenate([part, empty], axis=1), 0, 1, stride=1, stride_axis=0)
        tables.append(jnp.sum(turned, axis=0, keepdims=True))
    small = jnp.concatenate([gain1, gain2, gain3_ref[...]] + tables, axis=1)
    places = lax.broadcasted_iota(jnp.int32, (GROUP, LATE), 0)
    late = jnp.concatenate([g_heads, after_low, g_query], axis=1).astype(WIDER)
    late = jnp.concatenate([jnp.where(places == ANS, small, late), jnp.zeros((SENT - GROUP, LATE), WIDER)], axis=0)
    late_ref[...] = late.astype(LOWER)


def dec_outer_kernel(size):
    part = D // size

    def body(me_ref, *refs):
        me = me_ref[0]
        small_ref = refs[8]
        there, here = refs[2:8], refs[9:15]
        early_ref, late_ref, sems = refs[15:]
        sent = []
        early_ref[...] = jnp.concatenate([refs[0][s].astype(WIDER) for s in range(size)], axis=0).astype(LOWER)
        late = [refs[1][s].astype(WIDER)[:GROUP] for s in range(size)]
        late_ref[...] = jnp.concatenate(late, axis=0).astype(LOWER)
        rows = lax.broadcasted_iota(jnp.int32, (part, D), 0) + me * part
        lanes = lax.broadcasted_iota(jnp.int32, (part, D), 1)
        picked = jnp.where(rows == lanes, 1.0, 0.0).astype(LOWER)
        height = FF // size
        first = pl.multiple_of(AT["hidden"] + me * height, 128)

        def outer(k, name, right):
            left = right_product(picked, early_ref[:, AT[name] : AT[name] + D]).astype(LOWER)
            here[k][...] = product(left, right)
            sent.extend(send_out([(here[k], there[k])], sems, len(sent)))

        outer(4, "third", early_ref[:, AT["g_inner"] : AT["g_inner"] + FF])
        outer(0, "first", late_ref[:, : 3 * D])
        here[5][...] = left_product(early_ref[:, pl.ds(first, height)], early_ref[:, AT["g_out"] : AT["g_out"] + D])
        sent.extend(send_out([(here[5], there[5])], sems, len(sent)))
        outer(1, "own", late_ref[:, AT["g_after"] : AT["g_after"] + D])
        outer(2, "second", late_ref[:, AT["g_query"] : AT["g_query"] + D])
        outer(3, "mix", early_ref[:, AT["g_middle"] : AT["g_middle"] + D])
        total = jnp.zeros((1, LATE), WIDER)
        for k in range(size):
            total = total + late[k][ANS : ANS + 1]
        small_ref[...] = total
        for copy in sent:
            copy.wait()

    return body


def held(*shapes):
    return [pltpu.VMEM(shape, LOWER) for shape in shapes] + [
        pltpu.VMEM((GROUP, D), WIDER),
        pltpu.SemaphoreType.DMA((len(shapes),)),
    ]


def dec_self(table, answers, gain1, gain2, qkv, out, query, after=()):
    return run(
        "dec_self",
        dec_self_kernel,
        [table, answers, gain1, gain2, qkv, out, query],
        [SCALARS] + [WHOLE] * 3 + [ANY] * 3,
        [wide(GROUP, D), narrow(GROUP, 3 * D), narrow(GROUP, 3 * D), narrow(GROUP, D)],
        after=after,
        scratch=held((D, 3 * D), (D, D), (D, D)),
        flops=10**9,
    )


def dec_mid(count, parts, after_rows, cotangent, gain3, lefts, query, enc_gain3, pairs, cross_out, ffn_in, ffn_out, kv, final, after=()):
    outs = [narrow(SLOT, 2 * D), wide(SLOT, D), narrow(SLOT, D)]
    shapes = [(SLOT, 2 * D), (D, D), (D, FF), (FF, D), (D, 2 * D)]
    return run(
        "dec_mid",
        dec_mid_kernel,
        [count, parts, after_rows, cotangent, gain3, lefts, query, enc_gain3, pairs, cross_out, ffn_in, ffn_out, kv, final],
        [SCALARS] + [WHOLE] * 7 + [ANY] * 6,
        [narrow(ANS, D), narrow(GROUP, EARLY), wide(GROUP, D), wide(1, D), wide(GROUP, D), wide(1, D)] + outs,
        [WHOLE] * 6 + [ANY] * 3,
        after=after,
        scratch=[pltpu.VMEM(shape, LOWER) for shape in shapes]
        + [pltpu.VMEM((SLOT, D), WIDER)]
        + [pltpu.VMEM(out.shape, out.dtype) for out in outs]
        + [pltpu.VMEM((GROUP, D), WIDER), pltpu.SemaphoreType.DMA((6,)), pltpu.SemaphoreType.DMA((3,))],
        flops=4 * 10**9,
    )


def dec_back(table, answers, part, got, after_rows, g_middle, heads, gain1, gain2, g_gain3, query, out, qkv, after=()):
    return run(
        "dec_back",
        dec_back_kernel,
        [table, answers, part, got, after_rows, g_middle, heads, gain1, gain2, g_gain3, query, out, qkv],
        [SCALARS] + [WHOLE] * 9 + [ANY] * 3,
        [narrow(SENT, LATE), wide(ANS, D)],
        after=after,
        scratch=held((D, D), (D, D), (D, 3 * D)),
        flops=0,
    )


def dec_outer(me, early, late, size, after=()):
    part = D // size
    outs = [wide(part, 3 * D), wide(part, D), wide(part, D), wide(part, D), wide(part, FF), wide(FF // size, D)]
    return run(
        "dec_outer",
        dec_outer_kernel(size),
        [me, early, late],
        [SCALARS, WHOLE, WHOLE],
        outs + [wide(1, LATE)],
        [ANY] * 6 + [WHOLE],
        after=after,
        scratch=[pltpu.VMEM(out.shape, WIDER) for out in outs]
        + [pltpu.VMEM((size * GROUP, EARLY), LOWER), pltpu.VMEM((size * GROUP, LATE), LOWER), pltpu.SemaphoreType.DMA((6,))],
        flops=8 * 10**9,
    )


PLACES = [(0, 0), (0, 1), (1, 0), (1, 1)]


def place_of(me, there):
    return me ^ (4 * there[0] + 2 * there[1])


def turned_rows(me, acts, block):
    lanes = lax.broadcasted_iota(jnp.int32, (block, D), 1)
    rows = lax.broadcasted_iota(jnp.int32, (block, D), 0)
    picked = [jnp.where(lanes - rows == place_of(me, t) * block, 1.0, 0.0).astype(LOWER) for t in PLACES]
    picked = jnp.concatenate(picked, axis=0)
    return jnp.concatenate([right_product(picked, act).astype(LOWER) for act in acts], axis=1)


def target(there, x_refs, y_refs):
    dy, dx = there
    return (x_refs[dx].at[dy], y_refs[dy].at[dx])


def pages_out(pairs, sems, first):
    return send_out([(here.at[k], there.at[k]) for here, there in pairs for k in range(2)], sems, first)


def one_kernel(
    me_ref, t_own, t_par, p_own, p_par, h_own, h_par, b_own, b_par, xk_any, xs_any, yk_any, ys_any,
    xk, xs, yk, ys, t, p, h, b, sems, out_sems,
):
    me = me_ref[0]
    block = FF // 8
    pairs = [(t_own, t.at[0]), (t_par, t.at[1]), (p_own, p.at[:SLOT]), (p_par, p.at[SLOT:])]
    pairs += [(b_own, b.at[:SLOT]), (b_par, b.at[SLOT:])]
    for k, there in enumerate(PLACES):
        lanes = pl.ds(pl.multiple_of(place_of(me, there) * block, 128), block)
        pairs += [(h_own.at[:, lanes], h.at[k, :SLOT]), (h_par.at[:, lanes], h.at[k, SLOT:])]
    copies = fetch(pairs, sems)
    copies[0].wait()
    copies[1].wait()
    height = D // 8
    left = turned_rows(me, (t[0], t[1]), height)
    for k in range(2, 8):
        copies[k].wait()
    for c in range(2):
        grad = product(left, p[:, D * c : D * c + D]).astype(LOWER)
        for k, there in enumerate(PLACES):
            to, unused = target(there, (xk, xs), (yk, ys))
            to[height * c : height * c + height] = grad[height * k : height * k + height]
    sent = []
    for k, there in enumerate(PLACES):
        grad = left_product(h[k], b[...]).astype(LOWER)
        to_x, to_y = target(there, (xk, xs), (yk, ys))
        to_x[2 * height : 3 * height] = grad[:height]
        to_y[...] = grad[height:]
        out_x, out_y = target(there, (xk_any, xs_any), (yk_any, ys_any))
        if k + 1 < len(PLACES):
            copies[8 + 2 * k].wait()
            copies[9 + 2 * k].wait()
        sent += send_out([(to_x, out_x), (to_y, out_y)], out_sems, len(sent))
    for copy in sent:
        copy.wait()


def two_kernel(
    me_ref, s_own, s_par, i_own, i_par, m_own, m_par, l_own, l_par, xk_any, xs_any, yk_any, ys_any,
    xk, xs, yk, ys, s, i, m, l, sems, out_sems,
):
    me = me_ref[0]
    pairs = [(s_own, s.at[0]), (s_par, s.at[1]), (m_own, m.at[0]), (m_par, m.at[1])]
    pairs += [(l_own, l.at[:SLOT]), (l_par, l.at[SLOT:])]
    for c in range(4):
        lanes = slice(D * c, D * c + D)
        pairs += [(i_own.at[:, lanes], i.at[c, :SLOT]), (i_par.at[:, lanes], i.at[c, SLOT:])]
    copies = fetch(pairs, sems)
    for k in range(6):
        copies[k].wait()
    height = D // 8
    half = height // 2
    left = turned_rows(me, (m[0], m[1]), height)
    turned = turned_rows(me, (s[0], s[1]), height)
    grad = product(left, l[...]).astype(LOWER)
    for k, there in enumerate(PLACES):
        for to, first in zip(target(there, (xk, xs), (yk, ys)), (0, half)):
            to[2 * height : 2 * height + half] = grad[height * k + first : height * k + first + half]
    sent = []
    for c in range(4):
        if c % 2 == 0:
            for k in range(6 + 2 * c, 10 + 2 * c):
                copies[k].wait()
        grad = product(turned, i[c]).astype(LOWER)
        for k, there in enumerate(PLACES):
            to = target(there, (xk, xs), (yk, ys))[c // 2]
            to[height * (c % 2) : height * (c % 2) + height] = grad[height * k : height * k + height]
        if c % 2:
            done = ((xk, xk_any), (xs, xs_any)) if c == 1 else ((yk, yk_any), (ys, ys_any))
            sent += pages_out(done, out_sems, len(sent))
    for copy in sent:
        copy.wait()


def three_kernel(
    me_ref, f_own, f_par, g_own, g_par, xk_any, xs_any, yk_any, ys_any, xk, xs, yk, ys, f, g, sems, out_sems
):
    me = me_ref[0]
    pairs = [(f_own, f.at[0]), (f_par, f.at[1])]
    for c in range(3):
        pairs += [(g_own.at[c], g.at[c, :SLOT]), (g_par.at[c], g.at[c, SLOT:])]
    copies = fetch(pairs, sems)
    copies[0].wait()
    copies[1].wait()
    height = D // 8
    half = D // 2
    left = turned_rows(me, (f[0], f[1]), height)
    for k in range(2, 8):
        copies[k].wait()
    sent = []
    for c in range(3):
        grad = product(left, g[c]).astype(LOWER)
        for k, there in enumerate(PLACES):
            to_x, to_y = target(there, (xk, xs), (yk, ys))
            block = grad[height * k : height * k + height]
            if c == 0:
                to_x[:, :D] = block
            elif c == 1:
                to_x[:, D:] = block[:, :half]
                to_y[:, :half] = block[:, half:]
            else:
                to_y[:, half:] = block
        if c:
            done = ((xk, xk_any), (xs, xs_any)) if c == 1 else ((yk, yk_any), (ys, ys_any))
            sent += pages_out(done, out_sems, len(sent))
    for copy in sent:
        copy.wait()


def weight_call(name, body, me, ins, rows, columns, held_shapes, flops, after):
    out = narrow(2, rows, columns)
    copies = {"weights_one": 14, "weights_two": 14, "weights_three": 8}[name]
    return run(
        name,
        body,
        [me, *ins],
        [SCALARS] + [ANY] * len(ins),
        [out] * 4,
        [ANY] * 4,
        after=after,
        scratch=[pltpu.VMEM(out.shape, LOWER)] * 4
        + [pltpu.VMEM(shape, LOWER) for shape in held_shapes]
        + [pltpu.SemaphoreType.DMA((copies,)), pltpu.SemaphoreType.DMA((8,))],
        flops=flops,
    )


def weights_one(me, third, g_pairs, hidden, branch, after=()):
    shapes = [(2, SLOT, D), (2 * SLOT, 2 * D), (4, 2 * SLOT, FF // 8), (2 * SLOT, D)]
    ins = (*third, *g_pairs, *hidden, *branch)
    return weight_call("weights_one", one_kernel, me, ins, 3 * D // 8, D, shapes, 4 * 10**9, after)


def weights_two(me, second, g_inner, mixed, low, after=()):
    shapes = [(2, SLOT, D), (4, 2 * SLOT, D), (2, SLOT, D), (2 * SLOT, D)]
    ins = (*second, *g_inner, *mixed, *low)
    return weight_call("weights_two", two_kernel, me, ins, 5 * D // 16, D, shapes, 0, after)


def weights_three(me, first, grads, after=()):
    shapes = [(2, SLOT, D), (3, 2 * SLOT, D)]
    return weight_call("weights_three", three_kernel, me, (*first, *grads), D // 8, 3 * D // 2, shapes, 0, after)


def page(array, k):
    return pl.BlockSpec((1,) + array.shape[1:], lambda s: (k, 0, 0))


def add_first(parts, small=None, after=()):
    count = len(parts)

    def body(*refs):
        outs = refs[len(flat) :]
        for k in range(count):
            outs[k][...] = (refs[2 * k][0].astype(WIDER) + refs[2 * k + 1][0].astype(WIDER)).astype(LOWER)
        if small is not None:
            outs[count][...] = refs[2 * count][...] + refs[2 * count + 1][...]

    flat = [a for pair in parts for a in pair] + list(small or ())
    specs = [page(a, 1) if a.ndim == 3 else WHOLE for a in flat]
    outs = [narrow(*keep.shape[1:]) for keep, unused in parts]
    specs_out = [WHOLE] * count
    if small is not None:
        outs.append(wide(*small[0].shape))
        specs_out.append(WHOLE)
    return run("add_first", body, flat, specs, outs, specs_out, after=after, grid=(1,), flops=0)


def add_second(parts, small=None, after=()):
    count = len(parts)
    shapes = [keep.shape[1:] for keep, unused, unused_too in parts]
    stacked = small is None
    rows = sum(shape[0] for shape in shapes) if stacked else shapes[0][0]
    columns = shapes[0][1] if stacked else sum(shape[1] for shape in shapes)

    def body(*refs):
        out = refs[-1]
        first = 0
        for k, (high, across) in enumerate(shapes):
            keep, got, last = refs[3 * k : 3 * k + 3]
            total = (keep[0].astype(WIDER) + got[0].astype(WIDER) + last[...].astype(WIDER)).astype(LOWER)
            if stacked:
                out[first : first + high] = total
                first += high
            else:
                out[:rows, first : first + across] = total
                first += across
        if small is not None:
            out[rows:] = jnp.zeros((32, columns), LOWER)
            out[rows : rows + 16, :D] = (refs[3 * count][...] + refs[3 * count + 1][...]).astype(LOWER)

    flat = [a for trio in parts for a in trio] + list(small or ())
    specs = [page(a, 0) if a.ndim == 3 else WHOLE for a in flat]
    height = rows + (32 if small is not None else 0)
    return run("add_second", body, flat, specs, [narrow(height, columns)], after=after, grid=(1,), flops=0)


def add_pair(one, two, small=None, after=()):
    def body(*refs):
        outs = refs[len(flat) :]
        outs[0][...] = (refs[0][...].astype(WIDER) + refs[1][...].astype(WIDER)).astype(LOWER)
        if small is not None:
            outs[1][...] = refs[2][...] + refs[3][...]

    flat = [one, two] + list(small or ())
    outs = [narrow(*one.shape)] + [wide(*a.shape) for a in (small or ())[:1]]
    return run("add_pair", body, flat, [WHOLE] * len(flat), outs, after=after, flops=0)


def add_parts(share, parts, me, after=()):
    rows, columns = parts[0].shape

    def body(me_ref, share_ref, one_ref, two_ref, three_ref, out_ref):
        first = pl.multiple_of(me_ref[0] * rows, 16)
        total = share_ref[pl.ds(first, rows), :].astype(WIDER) + one_ref[...].astype(WIDER)
        out_ref[...] = (total + two_ref[...].astype(WIDER) + three_ref[...].astype(WIDER)).astype(LOWER)

    return run("add_parts", body, [me, share, *parts], [SCALARS] + [WHOLE] * 4, [narrow(rows, columns)], after=after, flops=0)


def add_rows(one, two, after=()):
    def body(one_ref, two_ref, out_ref):
        out_ref[...] = one_ref[...] + two_ref[...]

    return run("add_rows", body, [one, two], [WHOLE] * 2, [wide(*one.shape)], after=after, flops=0)


def partner(axis, bit):
    return [(k, k ^ (1 << bit)) for k in range(lax.axis_size(axis))]


def swap(value, axis, bit):
    return lax.ppermute(value, axis, partner(axis, bit))


def all_sum(value, axis):
    for bit in range(lax.axis_size(axis).bit_length() - 1):
        value = value + swap(value, axis, bit)
    return value


def pa_order(turn):
    rest = lax.axis_size("pa").bit_length() - 2
    return [1 + (k + turn) % rest for k in range(rest)]


def both_cores(acts, turn):
    size = lax.axis_size("pa")
    me = lax.axis_index("pa")
    blocks = jnp.transpose(acts).reshape(size, acts.shape[1] // size, acts.shape[0])
    order = pa_order(turn)
    offsets = [
        sum(((k >> (len(order) - 1 - p)) & 1) << bit for p, bit in enumerate(order)) for k in range(size // 2)
    ]
    mine = jnp.concatenate([lax.dynamic_slice_in_dim(blocks, me ^ d, 1) for d in offsets])
    theirs = jnp.concatenate([lax.dynamic_slice_in_dim(blocks, me ^ d ^ 1, 1) for d in offsets])
    return mine, swap(theirs, "pa", 0)


def weight_part(acts, grads, first, last):
    total = None
    for act, grad in zip(acts, grads):
        act = act[first:last]
        term = product(act.reshape(-1, act.shape[2]), grad)
        total = term if total is None else total + term
    height = acts[0].shape[1]
    return total.astype(LOWER).reshape(last - first, height, -1)


def add_up(parts):
    total = parts[0].astype(WIDER)
    for part in parts[1:]:
        total = total + part.astype(WIDER)
    return total.astype(LOWER)


def share_over_pa(acts, grads, turn):
    size = acts[0].shape[0]
    keep = [weight_part(acts, grads, 0, size // 2)]
    send = weight_part(acts, grads, size // 2, size)
    for bit in pa_order(turn):
        keep.append(swap(send, "pa", bit))
        size //= 2
        if size > 1:
            send = add_up([part[size // 2 : size] for part in keep])
            keep = [part[: size // 2] for part in keep]
    return add_up([part[0] for part in keep])


def inward(share):
    return lax.ppermute(share, "pb", [(0, 1), (3, 2)])


def between(share):
    return lax.ppermute(share, "pb", [(1, 2), (2, 1)])


def outward(share):
    me = lax.axis_index("pb")
    got = lax.ppermute(share, "pb", [(1, 0), (2, 3)])
    return jnp.where((me == 1) | (me == 2), share, got).astype(WIDER)


def swap_parts(share):
    me = lax.axis_index("pb")
    quarters = share.reshape(4, share.shape[0] // 4, share.shape[1])
    return [
        lax.ppermute(lax.dynamic_index_in_dim(quarters, me ^ s, 0, False), "pb", [(k, k ^ s) for k in range(4)])
        for s in range(1, 4)
    ]


def spread_parts(total, token):
    me = lax.axis_index("pb")
    got = [total] + [lax.ppermute(total, "pb", [(k, k ^ s) for k in range(4)]) for s in range(1, 4)]
    return jnp.concatenate([lax.select_n(me ^ b, *got) for b in range(4)], axis=0).astype(WIDER)


def total_plain(share):
    return lax.psum(share, "pb").astype(WIDER)


def local(
    passages,
    lengths,
    answers,
    cotangent,
    enc_gain1,
    enc_qkv,
    enc_bias,
    enc_out,
    enc_gain2,
    enc_ffn_in,
    enc_ffn_out,
    enc_gain3,
    cross_kv,
    dec_gain1,
    dec_qkv,
    dec_bias,
    dec_out,
    dec_gain2,
    cross_query,
    cross_out,
    dec_gain3,
    dec_ffn_in,
    dec_ffn_out,
):
    pa_size = lax.axis_size("pa")
    pb_size = lax.axis_size("pb")
    fast = pa_size == 8 and pb_size == 4
    me = lax.axis_index("pa").astype(jnp.int32).reshape(1)
    x = passages.reshape(SLOT, D)
    count = lengths.reshape(1)
    table = jnp.transpose(enc_bias)
    dec_table = jnp.transpose(dec_bias)
    pick = jnp.asarray(PICK, LOWER)
    pick_back = jnp.asarray(PICK_BACK, LOWER)

    def across(value):
        return value, swap(value, "pa", 0)

    dec_after, lefts, dec_heads, query, token = dec_self(
        dec_table, answers[0], dec_gain1, dec_gain2, dec_qkv, dec_out, cross_query
    )
    first, heads, mixed, stats, packed, after, second, slope, hidden, final, third, pairs, token = forward(
        count, table, pick, x, enc_gain1, enc_qkv, enc_gain2, enc_gain3, query, enc_out, enc_ffn_in, enc_ffn_out, cross_kv,
        after=[token],
    )
    if fast:
        acts = [across(value) for value in (first, mixed, second, hidden, third)]
    else:
        acts = [both_cores(v, k % 2) for k, v in enumerate((first, mixed, second, hidden, third))]
    gathered = lax.all_gather(packed, "pa")
    answer, early, g_middle, g_gain3, partial, g_enc_gain3, g_pairs, g_final, branch, token = dec_mid(
        count, gathered, dec_after, cotangent[0], dec_gain3, lefts, query, enc_gain3, pairs,
        cross_out, dec_ffn_in, dec_ffn_out, cross_kv, final,
        after=[got for unused, got in acts[:4]],
    )
    early_all = lax.all_gather(early, "pb")
    g_inner, g_after, low, g_mixed, g_enc_gain2, token = ffn_back(
        branch, enc_ffn_out, slope, enc_ffn_in, after, enc_gain2, g_final, enc_out, after=[token]
    )

    def back_of(base, pairs, after, begun=None):
        return attention_back(count, table, pick, heads, g_mixed, mixed, stats, base, pairs, begun, after=after)

    def dec_end(part, got, token, wait=()):
        return dec_back(
            dec_table, answers[0], part, got, dec_after, g_middle, dec_heads,
            dec_gain1, dec_gain2, g_gain3, cross_query, dec_out, dec_qkv, after=[token, *wait],
        )

    def rows_end(token):
        return rows_back(
            grads, enc_qkv, x, enc_gain1, g_after, g_enc_gain2, g_enc_gain3,
            (diagonal_a, diagonal_b), pick_back, after=[token],
        )

    pb_me = lax.axis_index("pb").astype(jnp.int32).reshape(1)

    def outer_end(token):
        *outer, token = dec_outer(pb_me, early_all, late_all, pb_size, after=[token])
        return outer, token

    if fast:
        partial, token = add_rows(partial, swap(partial, "pa", 0), after=[token])
        got = swap(partial, "pa", 1)
        xk, xs, yk, ys, token = weights_one(me, acts[4], across(g_pairs), acts[3], across(branch), after=[token])
        one = ((xk, swap(xs, "pa", 1)), (yk, swap(ys, "pa", 2)))
        partial, token = add_rows(partial, got, after=[token])
        got = swap(partial, "pa", 2)
        grads, diagonal_a, token = back_of(0, FIRST, [token])
        late, g_start, token = dec_end(partial, got, token)
        late_all = lax.all_gather(late, "pb")
        send_x, send_y, token = add_first(one, after=[token, early_all])
        last = (swap(send_x, "pa", 2), swap(send_y, "pa", 1))
        xk, xs, yk, ys, token = weights_two(me, acts[2], across(g_inner), acts[1], across(low), after=[token])
        two = ((xk, swap(xs, "pa", 1)), (yk, swap(ys, "pa", 2)))
        share_one, token = add_second([one[0] + last[:1], one[1] + last[1:]], after=[token])
        got_one = inward(share_one)
        grads, diagonal_b, token = back_of(FIRST, PAIRS - FIRST, [token], grads)
        there = swap(grads, "pa", 0)
        g_rows, small, token = rows_end(token)
        got_small = swap(small, "pa", 0)
        send_x, send_y, token = add_first(two, after=[token])
        last = (swap(send_x, "pa", 2), swap(send_y, "pa", 1))
        share_one, small, token = add_pair(share_one, got_one, (small, got_small), after=[token])
        got_one = between(share_one)
        got_small = swap(small, "pa", 1)
        outer, token = outer_end(token)
        share_two, token = add_second([two[0] + last[:1], two[1] + last[1:]], after=[token])
        got_two = inward(share_two)
        xk, xs, yk, ys, token = weights_three(me, acts[0], (grads, there), after=[token])
        three = ((xk, swap(xs, "pa", 1)), (yk, swap(ys, "pa", 2)))
        send_x, send_y, small, token = add_first(three, (small, got_small), after=[token])
        last = (swap(send_x, "pa", 2), swap(send_y, "pa", 1))
        got_small = swap(small, "pa", 2)
        share_one, token = add_pair(share_one, got_one, after=[token])
        total_one = outward(share_one)
        share_two, token = add_pair(share_two, got_two, after=[token])
        got_two = between(share_two)
        share_three, token = add_second([three[0] + last[:1], three[1] + last[1:]], (small, got_small), after=[token])
        parts = swap_parts(share_three)
        share_two, token = add_pair(share_two, got_two, after=[token])
        total_two = outward(share_two)
        total_three = spread_parts(*add_parts(share_three, parts, pb_me, after=[token, total_two]))
        small = total_three[D // pa_size :, :D]
        block = D // pa_size
        total_kv = jnp.concatenate([total_one[:block], total_one[block : 2 * block]], axis=1)
        total_ffn_out = total_one[2 * block :]
        second_part = 2 * block + block // 2
        total_ffn_in = jnp.concatenate(
            [total_two[first : first + block] for first in (0, block, second_part, second_part + block)], axis=1
        )
        total_out = jnp.concatenate([total_two[2 * block : second_part], total_two[second_part + 2 * block :]], axis=0)
        total_qkv = total_three[:block]
    else:
        partial = all_sum(partial, "pa")
        late, g_start, token = dec_end(partial, jnp.zeros_like(partial), token)
        late_all = lax.all_gather(late, "pb")
        grads, diagonal_a, token = back_of(0, FIRST, [token])
        grads, diagonal_b, token = back_of(FIRST, PAIRS - FIRST, [token], grads)
        g_rows, small, token = rows_end(token)
        outer, token = outer_end(token)
        small = all_sum(all_sum(small, "pa"), "pb")
        g_heads = jnp.concatenate([grads[0], grads[1], grads[2]], axis=1)
        total_kv = total_plain(share_over_pa(acts[4], across(g_pairs), 0))
        total_ffn_out = total_plain(share_over_pa(acts[3], across(branch), 1))
        total_ffn_in = total_plain(share_over_pa(acts[2], across(g_inner), 0))
        total_out = total_plain(share_over_pa(acts[1], across(low), 1))
        total_qkv = total_plain(share_over_pa(acts[0], across(g_heads), 0))

    d_qkv, d_out, d_query, d_cross, d_in, d_ffn, dec_small = outer
    dec_small = dec_small[0]
    dec_bias_rows = dec_small[3 * D :].reshape(H, STAT)[:, GROUP - ANS : GROUP]
    dec_bias_all = jnp.pad(jnp.transpose(dec_bias_rows[:, ::-1]), ((0, BUCKETS - ANS), (0, 0)))

    def own_part(vector, axis):
        height = vector.shape[0] // lax.axis_size(axis)
        return lax.dynamic_slice_in_dim(vector, lax.axis_index(axis) * height, height, axis=0)

    return (
        answer[None],
        g_rows.reshape(1, 1, SLOT, D),
        g_start[None],
        own_part(small[0], "pa"),
        total_qkv,
        jnp.transpose(small[4:16, :BUCKETS]),
        total_out,
        own_part(small[1], "pa"),
        total_ffn_in,
        total_ffn_out,
        own_part(small[2], "pa"),
        total_kv,
        own_part(dec_small[:D], "pb"),
        d_qkv,
        own_part(dec_bias_all, "pb"),
        d_out,
        own_part(dec_small[D : 2 * D], "pb"),
        d_query,
        d_cross,
        own_part(dec_small[2 * D : 3 * D], "pb"),
        d_in,
        d_ffn,
    )


def solution(mesh):
    copied = P()
    in_specs = (
        P("pb", "pa", None, None),
        P("pb", "pa"),
        P("pb", None, None),
        P("pb", None, None),
    ) + (copied,) * 19
    by_pa, by_pa_rows = P("pa"), P("pa", None)
    by_pb, by_pb_rows = P("pb"), P("pb", None)
    out_specs = (
        P("pb", None, None),
        P("pb", "pa", None, None),
        P("pb", None, None),
        by_pa,
        by_pa_rows,
        copied,
        by_pa_rows,
        by_pa,
        by_pa_rows,
        by_pa_rows,
        by_pa,
        by_pa_rows,
        by_pb,
        by_pb_rows,
        by_pb_rows,
        by_pb_rows,
        by_pb,
        by_pb_rows,
        by_pb_rows,
        by_pb,
        by_pb_rows,
        by_pb_rows,
    )
    return jax.shard_map(local, mesh=mesh, in_specs=in_specs, out_specs=out_specs, check_vma=False)
```

```python
import jax
import jax.numpy as jnp
import numpy as np
from jax import lax
from jax.experimental import pallas as pl
from jax.experimental.pallas import tpu as pltpu
from jax.sharding import PartitionSpec as P

D = 768
H = 12
HD = 64
FF = 3072
BUCKETS = 32
ANS = 20
SLOT = 512
PAIR = 2 * HD
PAIRS = H // 2
EDGE = 128
STRIP = 256
SPAN = 256
GROUP = 24
STACK = H * GROUP
STAT = 128
STEPS = 4
WIDTH = FF // STEPS
FIRST = 4
EPS = 1e-06
MASKED = -1000000000.0
C_GELU = 0.7978845608028654
LOWER = jnp.bfloat16
WIDER = jnp.float32
EARLY = 7 * D + 2 * FF
LATE = 5 * D
AT = {
    "first": 0,
    "own": D,
    "second": 2 * D,
    "mix": 3 * D,
    "third": 4 * D,
    "hidden": 5 * D,
    "g_middle": 5 * D + FF,
    "g_inner": 6 * D + FF,
    "g_out": 6 * D + 2 * FF,
    "g_heads": 0,
    "g_after": 3 * D,
    "g_query": 4 * D,
}


def tile_classes(away):
    rows = [np.clip(EDGE * d - away, -(BUCKETS // 2), BUCKETS // 2 - 1) + BUCKETS // 2 for d in (-1, 0, 1)]
    return np.eye(BUCKETS, dtype=np.float32)[np.concatenate(rows)]


LANES = np.arange(SPAN)
PICK = tile_classes(np.where(LANES < EDGE, LANES, LANES - SPAN)).T
ENDS = np.repeat(np.eye(BUCKETS, dtype=np.float32)[[0, BUCKETS - 1]], EDGE, axis=0)
PICK_BACK = np.pad(np.concatenate([tile_classes(LANES - (EDGE - 1)), ENDS]), ((0, 0), (0, STAT - BUCKETS)))

SCALARS = pl.BlockSpec(memory_space=pltpu.SMEM)
ANY = pl.BlockSpec(memory_space=pl.ANY)
WHOLE = pl.BlockSpec(memory_space=pltpu.VMEM)
TOKEN = (8, 128)


def wide(*shape):
    return jax.ShapeDtypeStruct(shape, WIDER)


def narrow(*shape):
    return jax.ShapeDtypeStruct(shape, LOWER)


def run(name, body, ins, in_specs, outs, out_specs=None, after=(), grid=(), scratch=(), flops=10**9, mib=63, alias=None):
    count, extra, results = len(ins), len(after), len(outs)
    if out_specs is None:
        out_specs = [WHOLE] * results
    zeros = (lambda *s: (0, 0)) if grid else (lambda: (0, 0))

    def wrapped(*refs):
        refs[count + extra + results][...] = jnp.zeros(TOKEN, WIDER)
        body(*refs[:count], *refs[count + extra : count + extra + results], *refs[count + extra + results + 1 :])

    got = pl.pallas_call(
        wrapped,
        grid=grid,
        out_shape=tuple(outs) + (wide(*TOKEN),),
        in_specs=list(in_specs) + [ANY] * extra,
        out_specs=tuple(out_specs) + (pl.BlockSpec(TOKEN, zeros),),
        scratch_shapes=list(scratch),
        input_output_aliases=alias or {},
        compiler_params=pltpu.CompilerParams(vmem_limit_bytes=mib * 2**20),
        cost_estimate=pl.CostEstimate(flops=10 * flops, bytes_accessed=1, transcendentals=0),
        name=name,
    )(*ins, *after)
    return got


def product(left, right):
    return jnp.dot(left, right, preferred_element_type=WIDER)


def left_product(left, right):
    return lax.dot_general(left, right, (((0,), (0,)), ((), ())), preferred_element_type=WIDER)


def right_product(left, right):
    return lax.dot_general(left, right, (((1,), (1,)), ((), ())), preferred_element_type=WIDER)


def split_product(left, right, terms):
    total = None
    for k in range(terms):
        part = left.astype(LOWER)
        left = left - part.astype(WIDER)
        term = product(part, right)
        total = term if total is None else total + term
    return total


def silu_like(inner):
    square = inner * inner
    tanh = jnp.tanh(inner * (C_GELU + (C_GELU * 0.044715) * square))
    half = 0.5 + 0.5 * tanh
    value = inner * half
    slope = half + value * (1.0 - tanh) * (C_GELU + (3.0 * C_GELU * 0.044715) * square)
    return value, slope


def row_of(ref):
    return ref[...].reshape(1, D)


def scale_of(values):
    return lax.rsqrt(jnp.mean(values * values, axis=-1, keepdims=True) + EPS)


def norm_pull(values, gain, grad):
    scale = scale_of(values)
    lifted = grad * gain
    inside = jnp.sum(values * lifted, axis=-1, keepdims=True)
    back = scale * lifted - values * (scale * scale * scale * inside * (1.0 / D))
    return back, jnp.sum(grad * values * scale, axis=0, keepdims=True)


def fetch(pairs, sems):
    copies = [pltpu.make_async_copy(s, t, sems.at[k]) for k, (s, t) in enumerate(pairs)]
    for copy in copies:
        copy.start()
    return copies


def bias_tiles(u_ref, head):
    tiles = []
    for d in range(3):
        row = u_ref[pl.ds(head, 1), SPAN * d : SPAN * d + SPAN]
        spread = jnp.broadcast_to(row, (EDGE, SPAN))
        tiles.append(pltpu.roll(spread, 0, 1, stride=1, stride_axis=0)[:, :EDGE])
    return tiles


def key_masks(n):
    places = lax.broadcasted_iota(jnp.int32, (EDGE, EDGE), 0)
    return [jnp.where(places + EDGE * j < n, 0.0, MASKED) for j in range(SLOT // EDGE)]


def score_blocks(raw, tiles, masks, low, high, first):
    columns = []
    for c in range(STRIP // EDGE):
        blocks = []
        for j in range(SLOT // EDGE):
            block = raw[EDGE * j : EDGE * j + EDGE, EDGE * c : EDGE * c + EDGE]
            d = j - first - c
            block = block + (tiles[d + 1] if abs(d) <= 1 else (low if d < 0 else high))
            blocks.append(block + masks[j] if j > 0 else block)
        columns.append(blocks)
    return columns


def paved(columns, kind):
    return jnp.concatenate([jnp.concatenate([b.astype(kind) for b in blocks], axis=0) for blocks in columns], axis=1)


def fill_rows(table_ref, pick_ref, u_ref):
    @pl.when(pl.program_id(0) == 0)
    def _():
        u_ref[...] = split_product(table_ref[...], pick_ref[...], 3)


def attn_fwd_kernel(n_ref, ends_ref, table_ref, pick_ref, x_ref, g1_ref, wq_ref, wk_ref, wv_ref, first_ref, heads_ref, o_ref, st_ref, u_ref):
    fill_rows(table_ref, pick_ref, u_ref)
    step = pl.program_id(0)

    @pl.when(step == 0)
    def _():
        rows = x_ref[...].astype(WIDER)
        first_ref[...] = (rows * scale_of(rows) * row_of(g1_ref)).astype(LOWER)

    masks = key_masks(n_ref[0])
    first = first_ref[...]
    for k, w_ref in enumerate((wq_ref, wk_ref, wv_ref)):
        heads_ref[k] = product(first, w_ref[...]).astype(LOWER)
    q_ref, k_ref = heads_ref.at[0], heads_ref.at[1]
    values = jnp.transpose(heads_ref[2])
    ones = jnp.ones((16, SLOT), LOWER)
    mixed = []
    for h in range(2):
        head = 2 * step + h
        low, high = ends_ref[head, 0], ends_ref[head, BUCKETS - 1]
        tiles = bias_tiles(u_ref, head)
        cols = slice(HD * h, HD * h + HD)
        keys = k_ref[:, cols]
        left = jnp.concatenate([values[cols], ones], axis=0)
        strips = []
        for i in range(0, SLOT // EDGE, STRIP // EDGE):
            lanes = slice(EDGE * i, EDGE * i + STRIP)
            raw = right_product(keys, q_ref[lanes, cols] * 0.125)
            tops, powers = [], []
            for blocks in score_blocks(raw, tiles, masks, low, high, i):
                top = jnp.maximum(jnp.maximum(blocks[0], blocks[1]), jnp.maximum(blocks[2], blocks[3]))
                top = jnp.max(top, axis=0, keepdims=True)
                tops.append(top)
                powers.append([jnp.exp(block - top) for block in blocks])
            out = product(left, paved(powers, LOWER))
            total = out[HD : HD + 1]
            st_ref[0, h : h + 1, lanes] = jnp.concatenate(tops, axis=1) + jnp.log(total)
            strips.append(out[:HD] * (1.0 / total))
        mixed.append(jnp.concatenate(strips, axis=1))
    lanes = pl.ds(pl.multiple_of(step * PAIR, PAIR), PAIR)
    o_ref[:, lanes] = jnp.transpose(jnp.concatenate(mixed, axis=0)).astype(LOWER)


def attn_bwd_kernel(base):
    def body(
        n_ref, ends_ref, table_ref, pick_ref, h_ref, g_ref, o_ref, st_ref, gh_ref, gb_ref, u_ref
    ):
        q_ref, k_ref, v_ref = h_ref.at[0], h_ref.at[1], h_ref.at[2]
        fill_rows(table_ref, pick_ref, u_ref)
        step = pl.program_id(0) + base
        masks = key_masks(n_ref[0])
        keys_t = jnp.transpose(k_ref[...])
        rows = lax.broadcasted_iota(jnp.int32, (EDGE, EDGE), 0)
        columns = lax.broadcasted_iota(jnp.int32, (EDGE, EDGE), 1)
        mirror = jnp.where(rows + columns == EDGE - 1, 1.0, 0.0).astype(LOWER)
        rows = lax.broadcasted_iota(jnp.int32, (16, SLOT), 0) * EDGE
        columns = lax.broadcasted_iota(jnp.int32, (16, SLOT), 1)
        places = jnp.where((columns >= rows) & (columns < rows + EDGE), 1.0, 0.0).astype(LOWER)
        rows = lax.broadcasted_iota(jnp.int32, (16, PAIR), 0) * HD
        columns = lax.broadcasted_iota(jnp.int32, (16, PAIR), 1)
        halves = jnp.where((columns >= rows) & (columns < rows + HD), 1.0, 0.0).astype(LOWER)
        met = g_ref[...].astype(WIDER) * o_ref[...].astype(WIDER)
        upper = met.astype(LOWER)
        lower = (met - upper.astype(WIDER)).astype(LOWER)
        weighted = right_product(halves, upper) + right_product(halves, lower)
        grad_queries = []
        gb_ref[0, 2:8, :] = jnp.zeros((6, 4 * SPAN), WIDER)
        for h in range(2):
            head = 2 * step + h
            low, high = ends_ref[head, 0], ends_ref[head, BUCKETS - 1]
            tiles = bias_tiles(u_ref, head)
            cols = slice(HD * h, HD * h + HD)
            keys = k_ref[:, cols]
            values = v_ref[:, cols]
            left = jnp.concatenate([keys_t[cols], places], axis=0)
            grad_keys = jnp.zeros((SLOT, HD), WIDER)
            grad_values = jnp.zeros((SLOT, HD), WIDER)
            strips = []
            sums = {}

            def gather(d, block):
                sums[d] = sums[d] + block if d in sums else block

            for i in range(0, SLOT // EDGE, STRIP // EDGE):
                lanes = slice(EDGE * i, EDGE * i + STRIP)
                query = q_ref[lanes, cols]
                grad = g_ref[lanes, cols]
                raw = right_product(keys, query * 0.125)
                grad_probs = right_product(values, grad)
                probs, changes = [], []
                for c, blocks in enumerate(score_blocks(raw, tiles, masks, low, high, i)):
                    part = slice(EDGE * (i + c), EDGE * (i + c) + EDGE)
                    total = st_ref[0, h : h + 1, part]
                    mean = weighted[h : h + 1, part]
                    probs.append([jnp.exp(block - total) for block in blocks])
                    changes.append([])
                    for j in range(SLOT // EDGE):
                        gap = grad_probs[EDGE * j : EDGE * j + EDGE, EDGE * c : EDGE * c + EDGE] - mean
                        change = probs[c][j] * gap
                        changes[c].append(change)
                        if abs(j - i - c) <= 1:
                            gather(j - i - c, change)
                rounded = paved(changes, LOWER)
                out = product(left, rounded)
                strips.append(out[:HD])
                for c in range(STRIP // EDGE):
                    for j in range(SLOT // EDGE):
                        if abs(j - i - c) > 1:
                            gather(2 if j > i + c else -2, out[HD + j : HD + j + 1, EDGE * c : EDGE * c + EDGE])
                grad_keys += product(rounded, query)
                grad_values += product(paved(probs, LOWER), grad)
            grad_queries.append(jnp.concatenate(strips, axis=1))
            gh_ref[1, :, cols] = (grad_keys * 0.125).astype(LOWER)
            gh_ref[2, :, cols] = grad_values.astype(LOWER)
            empty = jnp.zeros((EDGE, SPAN - EDGE), WIDER)
            band = jnp.concatenate([sums[-1], sums[0], sums[1]], axis=1)
            upper = band.astype(LOWER)
            lower = (band - upper.astype(WIDER)).astype(LOWER)
            mirrored = product(mirror, upper) + product(mirror, lower)
            for d in range(3):
                spread = jnp.concatenate([mirrored[:, EDGE * d : EDGE * d + EDGE], empty], axis=1)
                turned = pltpu.roll(spread, 0, 1, stride=1, stride_axis=0)
                gb_ref[0, h : h + 1, SPAN * d : SPAN * d + SPAN] = jnp.sum(turned, axis=0, keepdims=True)
            for place, d in ((3 * SPAN, -2), (3 * SPAN + EDGE, 2)):
                gb_ref[0, h : h + 1, place : place + EDGE] = sums[d]
        gh_ref[0] = (jnp.transpose(jnp.concatenate(grad_queries, axis=0)) * 0.125).astype(LOWER)

    return body


def columns_at(first):
    return pl.BlockSpec((SLOT, PAIR), lambda s: (0, first + s))


def stats_at(first):
    return pl.BlockSpec((1, 2, SLOT), lambda s: (first + s, 0, 0))


def pair_of_all(base):
    return pl.BlockSpec((3, SLOT, PAIR), lambda s: (0, 0, base + s))


def attention_back(count, table, pick, heads, grad_mixed, mixed, stats, base, half, begun=None, after=()):
    ins = [count, table, table, pick, heads, grad_mixed, mixed, stats]
    specs = [pair_of_all(base), columns_at(base), columns_at(base), stats_at(base)]
    body = attn_bwd_kernel(base)
    if begun is not None:
        ins.append(begun)
        specs.append(ANY)
        inner = body

        def body(*refs):
            inner(*refs[:8], *refs[9:])

    return run(
        "enc_attention_back",
        body,
        ins,
        [SCALARS, SCALARS, WHOLE, WHOLE] + specs,
        [narrow(3, SLOT, D), wide(half, 8, 4 * SPAN)],
        [pair_of_all(base), pl.BlockSpec((1, 8, 4 * SPAN), lambda s: (s, 0, 0))],
        after=after,
        grid=(half,),
        scratch=[pltpu.VMEM((H, 3 * SPAN), WIDER)],
        flops=2 * 5 * H * SLOT * SLOT * HD * 4,
        alias={8: 0} if begun is not None else None,
    )


def send_out(pairs, sems, first):
    copies = [pltpu.make_async_copy(s, t, sems.at[first + k]) for k, (s, t) in enumerate(pairs)]
    for copy in copies:
        copy.start()
    return copies


def chunk(k):
    return slice(WIDTH * k, WIDTH * k + WIDTH)


def copy_all(pairs, sems):
    return [pltpu.make_async_copy(s, t, sems.at[k]) for k, (s, t) in enumerate(pairs)]


def forward_kernel(
    n_ref, ends_ref, table_ref, pick_ref, x_ref, g1_ref, wq_ref, wk_ref, wv_ref,
    g2_ref, g3_ref, query_ref, wo_any, in_any, out_any, kv_any,
    first_ref, heads_ref, mixed_ref, st_ref, packed_ref,
    after_any, second_any, slope_any, hidden_any, final_any, third_any, pairs_any,
    u_ref, wo_ref, in_ref, out_ref, kv_ref,
    after_ref, second_ref, slope_ref, hidden_ref, final_ref, third_ref, pairs_ref,
    sems, out_sems,
):
    step = pl.program_id(0)
    pairs = [(wo_any, wo_ref)]
    for k in range(STEPS):
        pairs += [(in_any.at[:, chunk(k)], in_ref.at[k]), (out_any.at[chunk(k)], out_ref.at[k])]
    copies = copy_all(pairs + [(kv_any, kv_ref)], sems)

    @pl.when(step == 0)
    def _():
        for copy in copies:
            copy.start()

    attn_fwd_kernel(
        n_ref, ends_ref, table_ref, pick_ref, x_ref, g1_ref, wq_ref, wk_ref, wv_ref,
        first_ref, heads_ref, mixed_ref, st_ref, u_ref,
    )

    @pl.when(step == PAIRS - 1)
    def _():
        for copy in copies:
            copy.wait()
        after = x_ref[...].astype(WIDER) + product(mixed_ref[...], wo_ref[...])
        after_ref[...] = after
        second = (after * scale_of(after) * row_of(g2_ref)).astype(LOWER)
        second_ref[...] = second
        inner = product(second, in_ref[0])
        sent = send_out([(after_ref, after_any), (second_ref, second_any)], out_sems, 0)
        total = after
        for k in range(STEPS):
            following = product(second, in_ref[k + 1]) if k + 1 < STEPS else None
            value, slope = silu_like(inner)
            slope_ref[:, chunk(k)] = slope.astype(LOWER)
            hidden = value.astype(LOWER)
            hidden_ref[:, chunk(k)] = hidden
            total = total + product(hidden, out_ref[k])
            inner = following
            if k % 2:
                half = slice(WIDTH * (k - 1), WIDTH * (k + 1))
                sent += send_out(
                    [(slope_ref.at[:, half], slope_any.at[:, half]), (hidden_ref.at[:, half], hidden_any.at[:, half])],
                    out_sems, len(sent),
                )
        final_ref[...] = total
        third = (total * scale_of(total) * row_of(g3_ref)).astype(LOWER)
        third_ref[...] = third
        sent += send_out([(final_ref, final_any), (third_ref, third_any)], out_sems, len(sent))
        for k in range(2):
            half = slice(D * k, D * k + D)
            pairs_ref[:, half] = product(third, kv_ref[:, half]).astype(LOWER)
        sent += send_out([(pairs_ref, pairs_any)], out_sems, len(sent))
        cross_kernel(n_ref, query_ref, pairs_ref, packed_ref)
        for copy in sent:
            copy.wait()


def whole(*shape):
    return pl.BlockSpec(shape, lambda s: (0,) * len(shape))


def forward(count, table, pick, x, gain1, qkv, gain2, gain3, query, wo, ffn_in, ffn_out, kv, after=()):
    def weights_at(first):
        return pl.BlockSpec((D, PAIR), lambda s: (0, first + s))

    kept = [wide(SLOT, D), narrow(SLOT, D), narrow(SLOT, FF), narrow(SLOT, FF), wide(SLOT, D), narrow(SLOT, D), narrow(SLOT, 2 * D)]
    return run(
        "enc_forward",
        forward_kernel,
        [count, table, table, pick, x, gain1, qkv, qkv, qkv, gain2, gain3, query, wo, ffn_in, ffn_out, kv],
        [SCALARS, SCALARS, WHOLE, WHOLE, whole(SLOT, D), whole(D), weights_at(0), weights_at(PAIRS), weights_at(2 * PAIRS)]
        + [whole(D), whole(D), whole(GROUP, D)] + [ANY] * 4,
        [narrow(SLOT, D), narrow(3, SLOT, D), narrow(SLOT, D), wide(PAIRS, 2, SLOT), wide(GROUP, D + STAT)] + kept,
        [whole(SLOT, D), pair_of_all(0), whole(SLOT, D), stats_at(0), whole(GROUP, D + STAT)] + [ANY] * 7,
        after=after,
        grid=(PAIRS,),
        scratch=[
            pltpu.VMEM((H, 3 * SPAN), WIDER),
            pltpu.VMEM((D, D), LOWER),
            pltpu.VMEM((STEPS, D, WIDTH), LOWER),
            pltpu.VMEM((STEPS, WIDTH, D), LOWER),
            pltpu.VMEM((D, 2 * D), LOWER),
        ]
        + [pltpu.VMEM(out.shape, out.dtype) for out in kept]
        + [pltpu.SemaphoreType.DMA((2 * STEPS + 2,)), pltpu.SemaphoreType.DMA((9,))],
        flops=2 * SLOT * D * (D + 2 * FF + 2 * D),
    )


def ffn_back_kernel(
    branch_ref, g2_ref, gfinal_any, after_any, slope_any, out_any, in_any, wo_any,
    ginner_any, gafter_any, low_any, gmixed_any, gain_ref,
    gfinal_ref, after_ref, slope_ref, out_ref, in_ref, wo_ref, ginner_ref, gafter_ref, low_ref, gmixed_ref,
    sems, out_sems,
):
    pairs = []
    for k in range(STEPS):
        pairs += [(out_any.at[chunk(k)], out_ref.at[k]), (slope_any.at[:, chunk(k)], slope_ref.at[k])]
        pairs += [(in_any.at[:, chunk(k)], in_ref.at[k])]
    copies = fetch(pairs + [(after_any, after_ref), (gfinal_any, gfinal_ref), (wo_any, wo_ref)], sems)
    branch = branch_ref[...]
    copies[0].wait()
    grad = right_product(branch, out_ref[0])
    total = None
    sent = []
    for k in range(STEPS):
        copies[3 * k + 1].wait()
        copies[3 * k + 2].wait()
        copies[3 * k + 3].wait()
        following = right_product(branch, out_ref[k + 1]) if k + 1 < STEPS else None
        inner = (grad * slope_ref[k].astype(WIDER)).astype(LOWER)
        ginner_ref[:, chunk(k)] = inner
        term = right_product(inner, in_ref[k])
        total = term if total is None else total + term
        grad = following
        sent += send_out([(ginner_ref.at[:, chunk(k)], ginner_any.at[:, chunk(k)])], out_sems, len(sent))
    copies[3 * STEPS + 1].wait()
    copies[3 * STEPS + 2].wait()
    back, gain = norm_pull(after_ref[...], row_of(g2_ref), total)
    gain_ref[...] = gain
    g_after = gfinal_ref[...] + back
    gafter_ref[...] = g_after
    low = g_after.astype(LOWER)
    low_ref[...] = low
    sent += send_out([(gafter_ref, gafter_any), (low_ref, low_any)], out_sems, len(sent))
    gmixed_ref[...] = right_product(low, wo_ref[...]).astype(LOWER)
    sent += send_out([(gmixed_ref, gmixed_any)], out_sems, len(sent))
    for copy in sent:
        copy.wait()


def ffn_back(branch, ffn_out, slope, ffn_in, after_rows, gain2, g_final, wo, after=()):
    outs = [narrow(SLOT, FF), wide(SLOT, D), narrow(SLOT, D), narrow(SLOT, D)]
    return run(
        "enc_ffn_back",
        ffn_back_kernel,
        [branch, gain2, g_final, after_rows, slope, ffn_out, ffn_in, wo],
        [WHOLE] * 2 + [ANY] * 6,
        outs + [wide(1, D)],
        [ANY] * 4 + [WHOLE],
        after=after,
        scratch=[
            pltpu.VMEM((SLOT, D), WIDER),
            pltpu.VMEM((SLOT, D), WIDER),
            pltpu.VMEM((STEPS, SLOT, WIDTH), LOWER),
            pltpu.VMEM((STEPS, WIDTH, D), LOWER),
            pltpu.VMEM((STEPS, D, WIDTH), LOWER),
            pltpu.VMEM((D, D), LOWER),
        ]
        + [pltpu.VMEM(out.shape, out.dtype) for out in outs]
        + [pltpu.SemaphoreType.DMA((3 * STEPS + 3,)), pltpu.SemaphoreType.DMA((STEPS + 3,))],
        flops=2 * SLOT * D * (D + 2 * FF),
    )


def rows_back_kernel(
    g_ref, w_ref, x_ref, g1_ref, gafter_ref, gain2_ref, gain3_ref, da_ref, db_ref, pick_ref,
    grows_ref, small_ref, total_ref,
):
    step = pl.program_id(0)

    @pl.when(step == 0)
    def _():
        total_ref[...] = jnp.zeros((SLOT, D), WIDER)

    total_ref[...] += right_product(g_ref[0], w_ref[...])

    @pl.when(step == 2)
    def _():
        back, gain = norm_pull(x_ref[...].astype(WIDER), row_of(g1_ref), total_ref[...])
        grows_ref[...] = gafter_ref[...] + back
        sums = [ref[k, :2] for ref in (da_ref, db_ref) for k in range(ref.shape[0])]
        table = split_product(jnp.concatenate(sums, axis=0), pick_ref[...], 2)
        small_ref[...] = jnp.zeros((16, D), WIDER)
        small_ref[0:1] = gain
        small_ref[1:2] = gain2_ref[...]
        small_ref[2:3] = gain3_ref[...]
        small_ref[4:16, :STAT] = table


def rows_back(grads, qkv, x, gain1, g_after, gain2, gain3, diagonals, pick_back, after=()):
    rows = whole(SLOT, D)
    return run(
        "enc_rows_back",
        rows_back_kernel,
        [grads, qkv, x, gain1, g_after, gain2, gain3, diagonals[0], diagonals[1], pick_back],
        [pl.BlockSpec((1, SLOT, D), lambda s: (s, 0, 0)), pl.BlockSpec((D, D), lambda s: (0, s)), rows, whole(D), rows]
        + [whole(1, D), whole(1, D), whole(*diagonals[0].shape), whole(*diagonals[1].shape), whole(4 * SPAN, STAT)],
        [wide(SLOT, D), wide(16, D)],
        [rows, whole(16, D)],
        after=after,
        grid=(3,),
        scratch=[pltpu.VMEM((SLOT, D), WIDER)],
        flops=0,
    )


def head_lanes(h):
    lanes = lax.broadcasted_iota(jnp.int32, (GROUP, D), 1)
    return (lanes >= h * HD) & (lanes < (h + 1) * HD)


def stack_heads(flat):
    return jnp.concatenate([jnp.where(head_lanes(h), flat, 0.0) for h in range(H)], axis=0)


def merge_heads(stacked):
    total = jnp.zeros((GROUP, D), WIDER)
    for h in range(H):
        total = total + jnp.where(head_lanes(h), stacked[GROUP * h : GROUP * h + GROUP], 0.0)
    return total


def lanes_to_column(stat):
    lanes = lax.broadcasted_iota(jnp.int32, (GROUP, STAT), 1)
    parts = [jnp.sum(jnp.where(lanes == h, stat, 0.0), axis=1, keepdims=True) for h in range(H)]
    return jnp.concatenate(parts, axis=0)


def column_to_lanes(column, first):
    lanes = lax.broadcasted_iota(jnp.int32, (GROUP, STAT), 1)
    total = jnp.zeros((GROUP, STAT), WIDER)
    for h in range(H):
        total = total + jnp.where(lanes == first + h, column[GROUP * h : GROUP * h + GROUP], 0.0)
    return total


def spread_heads(stat):
    rows = lax.broadcasted_iota(jnp.int32, (STAT, D), 0) * HD
    lanes = lax.broadcasted_iota(jnp.int32, (STAT, D), 1)
    spread = jnp.where((lanes >= rows) & (lanes < rows + HD), 1.0, 0.0).astype(LOWER)
    return split_product(stat, spread, 2)


def own_scores(query, keys, table_ref):
    raw = right_product(query, keys)
    rows = lax.broadcasted_iota(jnp.int32, (GROUP, GROUP), 0)
    columns = lax.broadcasted_iota(jnp.int32, (GROUP, GROUP), 1)
    away = rows - columns
    parts = []
    for h in range(H):
        bias = jnp.full((GROUP, GROUP), table_ref[h, 0], WIDER)
        for d in range(1, GROUP):
            bias = jnp.where(away == d, table_ref[h, d], bias)
        part = raw[GROUP * h : GROUP * h + GROUP] + bias
        parts.append(jnp.where(away >= 0, part, MASKED))
    scores = jnp.concatenate(parts, axis=0)
    powers = jnp.exp(scores - jnp.max(scores, axis=1, keepdims=True))
    return powers / jnp.sum(powers, axis=1, keepdims=True)


def padded(ref, pad_ref):
    pad_ref[...] = jnp.zeros((GROUP, D), WIDER)
    pad_ref[:ANS] = ref[...].astype(WIDER)
    return pad_ref[...]


def answer_rows(width):
    return lax.broadcasted_iota(jnp.int32, (GROUP, width), 0) < ANS


def dec_self_kernel(
    table_ref, x_ref, g1_ref, g2_ref, qkv_any, out_any, query_any,
    after_ref, lefts_ref, heads_ref, query_ref,
    qkv_ref, out_ref, cross_ref, pad_ref, sems,
):
    copies = fetch(((qkv_any, qkv_ref), (out_any, out_ref), (query_any, cross_ref)), sems)
    start = padded(x_ref, pad_ref)
    first = (start * scale_of(start) * row_of(g1_ref)).astype(LOWER)
    copies[0].wait()
    heads = product(first, qkv_ref[...]).astype(LOWER)
    heads_ref[...] = heads
    query = stack_heads(heads.astype(WIDER)[:, :D] * 0.125).astype(LOWER)
    probs = own_scores(query, heads[:, D : 2 * D], table_ref)
    own = merge_heads(product(probs.astype(LOWER), heads[:, 2 * D :]))
    own = jnp.where(answer_rows(D), own, 0.0).astype(LOWER)
    copies[1].wait()
    after = start + product(own, out_ref[...])
    after_ref[...] = after
    second = (after * scale_of(after) * row_of(g2_ref)).astype(LOWER)
    copies[2].wait()
    query_ref[...] = product(second, cross_ref[...]).astype(LOWER)
    lefts_ref[:, :D] = first
    lefts_ref[:, D : 2 * D] = own
    lefts_ref[:, 2 * D :] = second


def masked_cross(n_ref, query_ref, pairs_ref):
    query = stack_heads(query_ref[...].astype(WIDER) * 0.125).astype(LOWER)
    raw = right_product(query, pairs_ref[:, :D])
    places = lax.broadcasted_iota(jnp.int32, (STACK, SLOT), 1)
    return query, jnp.where(places < n_ref[0], raw, MASKED)


def cross_kernel(n_ref, query_ref, pairs_ref, packed_ref):
    unused, scores = masked_cross(n_ref, query_ref, pairs_ref)
    top = jnp.max(scores, axis=1, keepdims=True)
    powers = jnp.exp(scores - top)
    total = jnp.sum(powers, axis=1, keepdims=True)
    probs = (powers / total).astype(LOWER)
    packed_ref[:, :D] = merge_heads(product(probs, pairs_ref[:, D:]))
    packed_ref[:, D:] = column_to_lanes(top, 0) + column_to_lanes(total, STAT // 2)


def dec_mid_kernel(
    n_ref, parts_ref, after_ref, cot_ref, g3_ref, lefts_ref, query_ref, e3_ref,
    pairs_any, cross_any, in_any, out_any, kv_any, final_any,
    answer_ref, early_ref, gmid_ref, gain_ref, partial_ref, gain_enc_ref, gpairs_any, gfinal_any, branch_any,
    pairs_ref, cross_ref, in_ref, out_ref, kv_ref, final_ref, gpairs_ref, gfinal_ref, branch_ref, pad_ref,
    sems, out_sems,
):
    held_pairs = ((cross_any, cross_ref), (in_any, in_ref), (out_any, out_ref), (pairs_any, pairs_ref))
    copies = fetch(held_pairs + ((kv_any, kv_ref), (final_any, final_ref)), sems)
    size = parts_ref.shape[0]
    used = lax.broadcasted_iota(jnp.int32, (GROUP, STAT), 1) < H
    tops = [parts_ref[k, :, D:] for k in range(size)]
    totals = [pltpu.roll(stat, STAT // 2, 1) for stat in tops]
    top = tops[0]
    for k in range(1, size):
        top = jnp.maximum(top, tops[k])
    weights = [jnp.where(used, totals[k] * jnp.exp(tops[k] - top), 0.0) for k in range(size)]
    total = weights[0]
    for k in range(1, size):
        total = total + weights[k]
    total = jnp.where(used, total, 1.0)
    mix = jnp.zeros((GROUP, D), WIDER)
    for k in range(size):
        mix = mix + parts_ref[k, :, :D] * spread_heads(weights[k] / total)
    mix_low = mix.astype(LOWER)
    copies[0].wait()
    middle = after_ref[...] + product(mix_low, cross_ref[...])
    third = (middle * scale_of(middle) * row_of(g3_ref)).astype(LOWER)
    copies[1].wait()
    inner = product(third, in_ref[...])
    value, slope = silu_like(inner)
    hidden = value.astype(LOWER)
    copies[2].wait()
    answer = (middle + product(hidden, out_ref[...])).astype(LOWER)
    answer_ref[...] = answer[:ANS]
    grad = padded(cot_ref, pad_ref)
    out_low = grad.astype(LOWER)
    g_inner = (right_product(out_low, out_ref[...]) * slope).astype(LOWER)
    back, gain = norm_pull(middle, row_of(g3_ref), right_product(g_inner, in_ref[...]))
    gain_ref[...] = gain
    g_middle = grad + back
    gmid_ref[...] = g_middle
    middle_low = g_middle.astype(LOWER)
    g_mix = right_product(middle_low, cross_ref[...]).astype(LOWER)

    def store(name, rows):
        early_ref[:, AT[name] : AT[name] + rows.shape[1]] = rows

    def kept(rows):
        return jnp.where(answer_rows(rows.shape[1]), rows.astype(WIDER), 0.0).astype(LOWER)

    early_ref[:, : 3 * D] = kept(lefts_ref[...])
    store("mix", kept(mix_low))
    store("third", kept(third))
    store("hidden", kept(hidden))
    store("g_middle", middle_low)
    store("g_inner", g_inner)
    store("g_out", out_low)
    copies[3].wait()
    copies[4].wait()
    copies[5].wait()
    query, scores = masked_cross(n_ref, query_ref, pairs_ref)
    probs = jnp.exp(scores - lanes_to_column(jnp.where(used, top, 0.0))) / lanes_to_column(total)
    grad = stack_heads(g_mix.astype(WIDER))
    weighted = jnp.sum(grad * jnp.concatenate([mix] * H, axis=0), axis=1, keepdims=True)
    grad = grad.astype(LOWER)
    grad_probs = right_product(grad, pairs_ref[:, D:])
    rounded = (probs * (grad_probs - weighted)).astype(LOWER)
    g_keys = left_product(rounded, query).astype(LOWER)
    g_values = left_product(probs.astype(LOWER), grad).astype(LOWER)
    gpairs_ref[:, :D] = g_keys
    gpairs_ref[:, D:] = g_values
    sent = send_out([(gpairs_ref, gpairs_any)], out_sems, 0)
    partial_ref[...] = merge_heads(product(rounded, pairs_ref[:, :D])) * 0.125
    g_third = right_product(g_keys, kv_ref[:, :D]) + right_product(g_values, kv_ref[:, D:])
    back, gain = norm_pull(final_ref[...], row_of(e3_ref), g_third)
    gain_enc_ref[...] = gain
    gfinal_ref[...] = back
    branch_ref[...] = back.astype(LOWER)
    sent += send_out([(gfinal_ref, gfinal_any), (branch_ref, branch_any)], out_sems, 1)
    for copy in sent:
        copy.wait()


def dec_back_kernel(
    table_ref, x_ref, part_ref, got_ref, after_ref, gmid_ref, heads_ref,
    g1_ref, g2_ref, gain3_ref, query_any, out_any, qkv_any,
    late_ref, gstart_ref,
    cross_ref, out_ref, qkv_ref, pad_ref, sems,
):
    copies = fetch(((query_any, cross_ref), (out_any, out_ref), (qkv_any, qkv_ref)), sems)
    g_query = (part_ref[...] + got_ref[...]).astype(LOWER)
    copies[0].wait()
    back, gain2 = norm_pull(after_ref[...], row_of(g2_ref), right_product(g_query, cross_ref[...]))
    g_after = gmid_ref[...] + back
    after_low = g_after.astype(LOWER)
    copies[1].wait()
    g_own = stack_heads(right_product(after_low, out_ref[...])).astype(LOWER)
    heads = heads_ref[...]
    query = stack_heads(heads.astype(WIDER)[:, :D] * 0.125).astype(LOWER)
    probs = own_scores(query, heads[:, D : 2 * D], table_ref)
    grad_probs = right_product(g_own, heads[:, 2 * D :])
    rounded = (probs * (grad_probs - jnp.sum(probs * grad_probs, axis=1, keepdims=True))).astype(LOWER)
    g_q = (merge_heads(product(rounded, heads[:, D : 2 * D])) * 0.125).astype(LOWER)
    g_k = left_product(rounded, query).astype(LOWER)
    g_v = left_product(probs.astype(LOWER), g_own).astype(LOWER)
    g_heads = jnp.concatenate([g_q, g_k, g_v], axis=1)
    copies[2].wait()
    start = padded(x_ref, pad_ref)
    back, gain1 = norm_pull(start, row_of(g1_ref), right_product(g_heads, qkv_ref[...]))
    gstart_ref[...] = (g_after + back)[:ANS]
    spread = rounded.astype(WIDER)
    rows = lax.broadcasted_iota(jnp.int32, (GROUP, GROUP), 0)
    columns = lax.broadcasted_iota(jnp.int32, (GROUP, GROUP), 1)
    mirror = jnp.where(rows + columns == GROUP - 1, 1.0, 0.0).astype(LOWER)
    empty = jnp.zeros((GROUP, STAT - GROUP), WIDER)
    tables = []
    for h in range(H):
        part = product(mirror, spread[GROUP * h : GROUP * h + GROUP].astype(LOWER))
        turned = pltpu.roll(jnp.concatenate([part, empty], axis=1), 0, 1, stride=1, stride_axis=0)
        tables.append(jnp.sum(turned, axis=0, keepdims=True))
    small = jnp.concatenate([gain1, gain2, gain3_ref[...]] + tables, axis=1)
    places = lax.broadcasted_iota(jnp.int32, (GROUP, LATE), 0)
    late = jnp.concatenate([g_heads, after_low, g_query], axis=1).astype(WIDER)
    late_ref[...] = jnp.where(places == ANS, small, late).astype(LOWER)


def dec_outer_kernel(size):
    part = D // size

    def body(me_ref, *refs):
        me = me_ref[0]
        small_ref = refs[9]
        there, here = refs[3:9], refs[10:16]
        early_ref, late_ref, sems = refs[16:]
        sent = []
        early_ref[...] = jnp.concatenate([refs[0][me ^ s].astype(WIDER) for s in range(size)], axis=0).astype(LOWER)
        late = [ref[...].astype(WIDER) for ref in refs[1:3]]
        late_ref[...] = jnp.concatenate(late, axis=0).astype(LOWER)
        rows = lax.broadcasted_iota(jnp.int32, (part, D), 0) + me * part
        lanes = lax.broadcasted_iota(jnp.int32, (part, D), 1)
        picked = jnp.where(rows == lanes, 1.0, 0.0).astype(LOWER)
        height = FF // size
        first = pl.multiple_of(AT["hidden"] + me * height, 128)

        def outer(k, name, right):
            left = right_product(picked, early_ref[:, AT[name] : AT[name] + D]).astype(LOWER)
            here[k][...] = product(left, right)
            sent.extend(send_out([(here[k], there[k])], sems, len(sent)))

        outer(4, "third", early_ref[:, AT["g_inner"] : AT["g_inner"] + FF])
        outer(0, "first", late_ref[:, : 3 * D])
        here[5][...] = left_product(early_ref[:, pl.ds(first, height)], early_ref[:, AT["g_out"] : AT["g_out"] + D])
        sent.extend(send_out([(here[5], there[5])], sems, len(sent)))
        outer(1, "own", late_ref[:, AT["g_after"] : AT["g_after"] + D])
        outer(2, "second", late_ref[:, AT["g_query"] : AT["g_query"] + D])
        outer(3, "mix", early_ref[:, AT["g_middle"] : AT["g_middle"] + D])
        total = jnp.zeros((1, LATE), WIDER)
        for part_late in late:
            for k in (0, GROUP):
                total = total + part_late[k + ANS : k + ANS + 1]
        small_ref[...] = total
        for copy in sent:
            copy.wait()

    return body


def held(*shapes):
    return [pltpu.VMEM(shape, LOWER) for shape in shapes] + [
        pltpu.VMEM((GROUP, D), WIDER),
        pltpu.SemaphoreType.DMA((len(shapes),)),
    ]


def dec_self(table, answers, gain1, gain2, qkv, out, query, after=()):
    return run(
        "dec_self",
        dec_self_kernel,
        [table, answers, gain1, gain2, qkv, out, query],
        [SCALARS] + [WHOLE] * 3 + [ANY] * 3,
        [wide(GROUP, D), narrow(GROUP, 3 * D), narrow(GROUP, 3 * D), narrow(GROUP, D)],
        after=after,
        scratch=held((D, 3 * D), (D, D), (D, D)),
        flops=10**9,
    )


def dec_mid(count, parts, after_rows, cotangent, gain3, lefts, query, enc_gain3, pairs, cross_out, ffn_in, ffn_out, kv, final, after=()):
    outs = [narrow(SLOT, 2 * D), wide(SLOT, D), narrow(SLOT, D)]
    shapes = [(SLOT, 2 * D), (D, D), (D, FF), (FF, D), (D, 2 * D)]
    return run(
        "dec_mid",
        dec_mid_kernel,
        [count, parts, after_rows, cotangent, gain3, lefts, query, enc_gain3, pairs, cross_out, ffn_in, ffn_out, kv, final],
        [SCALARS] + [WHOLE] * 7 + [ANY] * 6,
        [narrow(ANS, D), narrow(GROUP, EARLY), wide(GROUP, D), wide(1, D), wide(GROUP, D), wide(1, D)] + outs,
        [WHOLE] * 6 + [ANY] * 3,
        after=after,
        scratch=[pltpu.VMEM(shape, LOWER) for shape in shapes]
        + [pltpu.VMEM((SLOT, D), WIDER)]
        + [pltpu.VMEM(out.shape, out.dtype) for out in outs]
        + [pltpu.VMEM((GROUP, D), WIDER), pltpu.SemaphoreType.DMA((6,)), pltpu.SemaphoreType.DMA((3,))],
        flops=4 * 10**9,
    )


def dec_back(table, answers, part, got, after_rows, g_middle, heads, gain1, gain2, g_gain3, query, out, qkv, after=()):
    return run(
        "dec_back",
        dec_back_kernel,
        [table, answers, part, got, after_rows, g_middle, heads, gain1, gain2, g_gain3, query, out, qkv],
        [SCALARS] + [WHOLE] * 9 + [ANY] * 3,
        [narrow(GROUP, LATE), wide(ANS, D)],
        after=after,
        scratch=held((D, D), (D, D), (D, 3 * D)),
        flops=0,
    )


def dec_outer(me, early, late_one, late_two, size, after=()):
    part = D // size
    outs = [wide(part, 3 * D), wide(part, D), wide(part, D), wide(part, D), wide(part, FF), wide(FF // size, D)]
    return run(
        "dec_outer",
        dec_outer_kernel(size),
        [me, early, late_one, late_two],
        [SCALARS, WHOLE, WHOLE, WHOLE],
        outs + [wide(1, LATE)],
        [ANY] * 6 + [WHOLE],
        after=after,
        scratch=[pltpu.VMEM(out.shape, WIDER) for out in outs]
        + [pltpu.VMEM((size * GROUP, EARLY), LOWER), pltpu.VMEM((size * GROUP, LATE), LOWER), pltpu.SemaphoreType.DMA((6,))],
        flops=8 * 10**9,
    )


def stack_late(one, two, after=()):
    def body(one_ref, two_ref, out_ref):
        out_ref[...] = jnp.concatenate([one_ref[...].astype(WIDER), two_ref[...].astype(WIDER)], axis=0).astype(LOWER)

    return run("stack_late", body, [one, two], [WHOLE] * 2, [narrow(2 * GROUP, LATE)], after=after, flops=0)


PLACES = [(0, 0), (0, 1), (1, 0), (1, 1)]


def place_of(me, there):
    return me ^ (4 * there[0] + 2 * there[1])


def turned_rows(me, acts, block):
    lanes = lax.broadcasted_iota(jnp.int32, (block, D), 1)
    rows = lax.broadcasted_iota(jnp.int32, (block, D), 0)
    picked = [jnp.where(lanes - rows == place_of(me, t) * block, 1.0, 0.0).astype(LOWER) for t in PLACES]
    picked = jnp.concatenate(picked, axis=0)
    return jnp.concatenate([right_product(picked, act).astype(LOWER) for act in acts], axis=1)


def target(there, x_refs, y_refs):
    dy, dx = there
    return (x_refs[dx].at[dy], y_refs[dy].at[dx])


def pages_out(pairs, sems, first):
    return send_out([(here.at[k], there.at[k]) for here, there in pairs for k in range(2)], sems, first)


def one_kernel(
    me_ref, t_own, t_par, p_own, p_par, h_own, h_par, b_own, b_par, xk_any, xs_any, yk_any, ys_any,
    xk, xs, yk, ys, t, p, h, b, sems, out_sems,
):
    me = me_ref[0]
    block = FF // 8
    pairs = [(t_own, t.at[0]), (t_par, t.at[1]), (p_own, p.at[:SLOT]), (p_par, p.at[SLOT:])]
    pairs += [(b_own, b.at[:SLOT]), (b_par, b.at[SLOT:])]
    for k, there in enumerate(PLACES):
        lanes = pl.ds(pl.multiple_of(place_of(me, there) * block, 128), block)
        pairs += [(h_own.at[:, lanes], h.at[k, :SLOT]), (h_par.at[:, lanes], h.at[k, SLOT:])]
    copies = fetch(pairs, sems)
    copies[0].wait()
    copies[1].wait()
    height = D // 8
    left = turned_rows(me, (t[0], t[1]), height)
    for k in range(2, 8):
        copies[k].wait()
    for c in range(2):
        grad = product(left, p[:, D * c : D * c + D]).astype(LOWER)
        for k, there in enumerate(PLACES):
            to, unused = target(there, (xk, xs), (yk, ys))
            to[height * c : height * c + height] = grad[height * k : height * k + height]
    sent = []
    for k, there in enumerate(PLACES):
        grad = left_product(h[k], b[...]).astype(LOWER)
        to_x, to_y = target(there, (xk, xs), (yk, ys))
        to_x[2 * height : 3 * height] = grad[:height]
        to_y[...] = grad[height:]
        out_x, out_y = target(there, (xk_any, xs_any), (yk_any, ys_any))
        if k + 1 < len(PLACES):
            copies[8 + 2 * k].wait()
            copies[9 + 2 * k].wait()
        sent += send_out([(to_x, out_x), (to_y, out_y)], out_sems, len(sent))
    for copy in sent:
        copy.wait()


def two_kernel(
    me_ref, s_own, s_par, i_own, i_par, m_own, m_par, l_own, l_par, xk_any, xs_any, yk_any, ys_any,
    xk, xs, yk, ys, s, i, m, l, sems, out_sems,
):
    me = me_ref[0]
    pairs = [(s_own, s.at[0]), (s_par, s.at[1]), (m_own, m.at[0]), (m_par, m.at[1])]
    pairs += [(l_own, l.at[:SLOT]), (l_par, l.at[SLOT:])]
    for c in range(4):
        lanes = slice(D * c, D * c + D)
        pairs += [(i_own.at[:, lanes], i.at[c, :SLOT]), (i_par.at[:, lanes], i.at[c, SLOT:])]
    copies = fetch(pairs, sems)
    for k in range(6):
        copies[k].wait()
    height = D // 8
    half = height // 2
    left = turned_rows(me, (m[0], m[1]), height)
    turned = turned_rows(me, (s[0], s[1]), height)
    grad = product(left, l[...]).astype(LOWER)
    for k, there in enumerate(PLACES):
        for to, first in zip(target(there, (xk, xs), (yk, ys)), (0, half)):
            to[2 * height : 2 * height + half] = grad[height * k + first : height * k + first + half]
    sent = []
    for c in range(4):
        if c % 2 == 0:
            for k in range(6 + 2 * c, 10 + 2 * c):
                copies[k].wait()
        grad = product(turned, i[c]).astype(LOWER)
        for k, there in enumerate(PLACES):
            to = target(there, (xk, xs), (yk, ys))[c // 2]
            to[height * (c % 2) : height * (c % 2) + height] = grad[height * k : height * k + height]
        if c % 2:
            done = ((xk, xk_any), (xs, xs_any)) if c == 1 else ((yk, yk_any), (ys, ys_any))
            sent += pages_out(done, out_sems, len(sent))
    for copy in sent:
        copy.wait()


def three_kernel(
    me_ref, f_own, f_par, g_own, g_par, small_ref, got_ref, xk_any, xs_any, yk_any, ys_any,
    xk, xs, yk, ys, f, g, sems, out_sems,
):
    me = me_ref[0]
    small = (small_ref[...] + got_ref[...]).astype(LOWER)
    pairs = [(f_own, f.at[0]), (f_par, f.at[1])]
    for c in range(3):
        pairs += [(g_own.at[c], g.at[c, :SLOT]), (g_par.at[c], g.at[c, SLOT:])]
    copies = fetch(pairs, sems)
    copies[0].wait()
    copies[1].wait()
    height = D // 8
    half = D // 2
    left = turned_rows(me, (f[0], f[1]), height)
    for ref in (xk, xs, yk, ys):
        for k in range(2):
            ref[k, height:] = jnp.zeros((16, 3 * half), LOWER)
            if ref is xk or ref is xs:
                ref[k, height:, :D] = small
    for k in range(2, 8):
        copies[k].wait()
    sent = []
    for c in range(3):
        grad = product(left, g[c]).astype(LOWER)
        for k, there in enumerate(PLACES):
            to_x, to_y = target(there, (xk, xs), (yk, ys))
            block = grad[height * k : height * k + height]
            if c == 0:
                to_x[:height, :D] = block
            elif c == 1:
                to_x[:height, D:] = block[:, :half]
                to_y[:height, :half] = block[:, half:]
            else:
                to_y[:height, half:] = block
        if c:
            done = ((xk, xk_any), (xs, xs_any)) if c == 1 else ((yk, yk_any), (ys, ys_any))
            sent += pages_out(done, out_sems, len(sent))
    for copy in sent:
        copy.wait()


def weight_call(name, body, me, ins, rows, columns, held_shapes, flops, after, extra=()):
    out = narrow(2, rows, columns)
    copies = {"weights_one": 14, "weights_two": 14, "weights_three": 8}[name]
    return run(
        name,
        body,
        [me, *ins, *extra],
        [SCALARS] + [ANY] * len(ins) + [WHOLE] * len(extra),
        [out] * 4,
        [ANY] * 4,
        after=after,
        scratch=[pltpu.VMEM(out.shape, LOWER)] * 4
        + [pltpu.VMEM(shape, LOWER) for shape in held_shapes]
        + [pltpu.SemaphoreType.DMA((copies,)), pltpu.SemaphoreType.DMA((8,))],
        flops=flops,
    )


def weights_one(me, third, g_pairs, hidden, branch, after=()):
    shapes = [(2, SLOT, D), (2 * SLOT, 2 * D), (4, 2 * SLOT, FF // 8), (2 * SLOT, D)]
    ins = (*third, *g_pairs, *hidden, *branch)
    return weight_call("weights_one", one_kernel, me, ins, 3 * D // 8, D, shapes, 4 * 10**9, after)


def weights_two(me, second, g_inner, mixed, low, after=()):
    shapes = [(2, SLOT, D), (4, 2 * SLOT, D), (2, SLOT, D), (2 * SLOT, D)]
    ins = (*second, *g_inner, *mixed, *low)
    return weight_call("weights_two", two_kernel, me, ins, 5 * D // 16, D, shapes, 0, after)


def weights_three(me, first, grads, small, after=()):
    shapes = [(2, SLOT, D), (3, 2 * SLOT, D)]
    ins = (*first, *grads)
    return weight_call("weights_three", three_kernel, me, ins, D // 8 + 16, 3 * D // 2, shapes, 0, after, small)


def page(array, k):
    return pl.BlockSpec((1,) + array.shape[1:], lambda s: (k, 0, 0))


def add_first(parts, after=()):
    count = len(parts)

    def body(*refs):
        for k in range(count):
            refs[2 * count + k][...] = (refs[2 * k][0].astype(WIDER) + refs[2 * k + 1][0].astype(WIDER)).astype(LOWER)

    flat = [a for pair in parts for a in pair]
    outs = [narrow(*keep.shape[1:]) for keep, unused in parts]
    return run("add_first", body, flat, [page(a, 1) for a in flat], outs, after=after, grid=(1,), flops=0)


def add_second(parts, side=False, after=()):
    shapes = [keep.shape[1:] for keep, unused, unused_too in parts]
    rows = shapes[0][0] + 16 if side else sum(shape[0] for shape in shapes)
    columns = sum(shape[1] for shape in shapes) if side else shapes[0][1]

    def body(*refs):
        out = refs[-1]
        first = 0
        for k, (high, across) in enumerate(shapes):
            keep, got, last = refs[3 * k : 3 * k + 3]
            total = (keep[0].astype(WIDER) + got[0].astype(WIDER) + last[...].astype(WIDER)).astype(LOWER)
            if side:
                out[:high, first : first + across] = total
                first += across
            else:
                out[first : first + high] = total
                first += high
        if side:
            out[rows - 16 :] = jnp.zeros((16, columns), LOWER)

    flat = [a for trio in parts for a in trio]
    specs = [page(a, 0) if a.ndim == 3 else WHOLE for a in flat]
    return run("add_second", body, flat, specs, [narrow(rows, columns)], after=after, grid=(1,), flops=0)


def add_pair(one, two, after=()):
    def body(one_ref, two_ref, out_ref):
        out_ref[...] = (one_ref[...].astype(WIDER) + two_ref[...].astype(WIDER)).astype(LOWER)

    return run("add_pair", body, [one, two], [WHOLE] * 2, [narrow(*one.shape)], after=after, flops=0)


def add_parts(share, parts, me, after=()):
    rows, columns = parts[0].shape

    def body(me_ref, share_ref, one_ref, two_ref, three_ref, out_ref):
        first = pl.multiple_of(me_ref[0] * rows, 16)
        total = share_ref[pl.ds(first, rows), :].astype(WIDER) + one_ref[...].astype(WIDER)
        out_ref[...] = (total + two_ref[...].astype(WIDER) + three_ref[...].astype(WIDER)).astype(LOWER)

    return run("add_parts", body, [me, share, *parts], [SCALARS] + [WHOLE] * 4, [narrow(rows, columns)], after=after, flops=0)


def add_rows(one, two, after=()):
    def body(one_ref, two_ref, out_ref):
        out_ref[...] = one_ref[...] + two_ref[...]

    return run("add_rows", body, [one, two], [WHOLE] * 2, [wide(*one.shape)], after=after, flops=0)


def partner(axis, bit):
    return [(k, k ^ (1 << bit)) for k in range(lax.axis_size(axis))]


def swap(value, axis, bit):
    return lax.ppermute(value, axis, partner(axis, bit))


def all_sum(value, axis):
    for bit in range(lax.axis_size(axis).bit_length() - 1):
        value = value + swap(value, axis, bit)
    return value


def pa_order(turn):
    rest = lax.axis_size("pa").bit_length() - 2
    return [1 + (k + turn) % rest for k in range(rest)]


def both_cores(acts, turn):
    size = lax.axis_size("pa")
    me = lax.axis_index("pa")
    blocks = jnp.transpose(acts).reshape(size, acts.shape[1] // size, acts.shape[0])
    order = pa_order(turn)
    offsets = [
        sum(((k >> (len(order) - 1 - p)) & 1) << bit for p, bit in enumerate(order)) for k in range(size // 2)
    ]
    mine = jnp.concatenate([lax.dynamic_slice_in_dim(blocks, me ^ d, 1) for d in offsets])
    theirs = jnp.concatenate([lax.dynamic_slice_in_dim(blocks, me ^ d ^ 1, 1) for d in offsets])
    return mine, swap(theirs, "pa", 0)


def weight_part(acts, grads, first, last):
    total = None
    for act, grad in zip(acts, grads):
        act = act[first:last]
        term = product(act.reshape(-1, act.shape[2]), grad)
        total = term if total is None else total + term
    height = acts[0].shape[1]
    return total.astype(LOWER).reshape(last - first, height, -1)


def add_up(parts):
    total = parts[0].astype(WIDER)
    for part in parts[1:]:
        total = total + part.astype(WIDER)
    return total.astype(LOWER)


def share_over_pa(acts, grads, turn):
    size = acts[0].shape[0]
    keep = [weight_part(acts, grads, 0, size // 2)]
    send = weight_part(acts, grads, size // 2, size)
    for bit in pa_order(turn):
        keep.append(swap(send, "pa", bit))
        size //= 2
        if size > 1:
            send = add_up([part[size // 2 : size] for part in keep])
            keep = [part[: size // 2] for part in keep]
    return add_up([part[0] for part in keep])


def inward(share):
    return lax.ppermute(share, "pb", [(0, 1), (3, 2)])


def between(share):
    return lax.ppermute(share, "pb", [(1, 2), (2, 1)])


def outward(share):
    me = lax.axis_index("pb")
    got = lax.ppermute(share, "pb", [(1, 0), (2, 3)])
    return jnp.where((me == 1) | (me == 2), share, got).astype(WIDER)


def swap_parts(share):
    me = lax.axis_index("pb")
    quarters = share.reshape(4, share.shape[0] // 4, share.shape[1])
    return [
        lax.ppermute(lax.dynamic_index_in_dim(quarters, me ^ s, 0, False), "pb", [(k, k ^ s) for k in range(4)])
        for s in range(1, 4)
    ]


def spread_parts(total, token):
    me = lax.axis_index("pb")
    got = [total] + [lax.ppermute(total, "pb", [(k, k ^ s) for k in range(4)]) for s in range(1, 4)]
    return jnp.concatenate([lax.select_n(me ^ b, *got) for b in range(4)], axis=0).astype(WIDER)


def total_plain(share):
    return lax.psum(share, "pb").astype(WIDER)


def local(
    passages,
    lengths,
    answers,
    cotangent,
    enc_gain1,
    enc_qkv,
    enc_bias,
    enc_out,
    enc_gain2,
    enc_ffn_in,
    enc_ffn_out,
    enc_gain3,
    cross_kv,
    dec_gain1,
    dec_qkv,
    dec_bias,
    dec_out,
    dec_gain2,
    cross_query,
    cross_out,
    dec_gain3,
    dec_ffn_in,
    dec_ffn_out,
):
    pa_size = lax.axis_size("pa")
    pb_size = lax.axis_size("pb")
    fast = pa_size == 8 and pb_size == 4
    me = lax.axis_index("pa").astype(jnp.int32).reshape(1)
    x = passages.reshape(SLOT, D)
    count = lengths.reshape(1)
    table = jnp.transpose(enc_bias)
    dec_table = jnp.transpose(dec_bias)
    pick = jnp.asarray(PICK, LOWER)
    pick_back = jnp.asarray(PICK_BACK, LOWER)

    def across(value):
        return value, swap(value, "pa", 0)

    dec_after, lefts, dec_heads, query, token = dec_self(
        dec_table, answers[0], dec_gain1, dec_gain2, dec_qkv, dec_out, cross_query
    )
    first, heads, mixed, stats, packed, after, second, slope, hidden, final, third, pairs, token = forward(
        count, table, pick, x, enc_gain1, enc_qkv, enc_gain2, enc_gain3, query, enc_out, enc_ffn_in, enc_ffn_out, cross_kv,
        after=[token],
    )
    if fast:
        acts = [across(value) for value in (first, mixed, second, hidden, third)]
    else:
        acts = [both_cores(v, k % 2) for k, v in enumerate((first, mixed, second, hidden, third))]
    gathered = lax.all_gather(packed, "pa")
    answer, early, g_middle, g_gain3, partial, g_enc_gain3, g_pairs, g_final, branch, token = dec_mid(
        count, gathered, dec_after, cotangent[0], dec_gain3, lefts, query, enc_gain3, pairs,
        cross_out, dec_ffn_in, dec_ffn_out, cross_kv, final,
        after=[got for unused, got in acts[:4]],
    )
    early_all = lax.all_gather(early, "pb")
    g_inner, g_after, low, g_mixed, g_enc_gain2, token = ffn_back(
        branch, enc_ffn_out, slope, enc_ffn_in, after, enc_gain2, g_final, enc_out, after=[token]
    )

    def back_of(base, pairs, after, begun=None):
        return attention_back(count, table, pick, heads, g_mixed, mixed, stats, base, pairs, begun, after=after)

    def dec_end(part, got, token, wait=()):
        return dec_back(
            dec_table, answers[0], part, got, dec_after, g_middle, dec_heads,
            dec_gain1, dec_gain2, g_gain3, cross_query, dec_out, dec_qkv, after=[token, *wait],
        )

    def rows_end(token):
        return rows_back(
            grads, enc_qkv, x, enc_gain1, g_after, g_enc_gain2, g_enc_gain3,
            (diagonal_a, diagonal_b), pick_back, after=[token],
        )

    pb_me = lax.axis_index("pb").astype(jnp.int32).reshape(1)

    def outer_end(token, late_one, late_two):
        *outer, token = dec_outer(pb_me, early_all, late_one, late_two, pb_size, after=[token])
        return outer, token

    if fast:
        partial, token = add_rows(partial, swap(partial, "pa", 0), after=[token])
        got = swap(partial, "pa", 1)
        xk, xs, yk, ys, token = weights_one(me, acts[4], across(g_pairs), acts[3], across(branch), after=[token])
        one = ((xk, swap(xs, "pa", 1)), (yk, swap(ys, "pa", 2)))
        partial, token = add_rows(partial, got, after=[token])
        got = swap(partial, "pa", 2)
        grads, diagonal_a, token = back_of(0, FIRST, [token])
        late, g_start, token = dec_end(partial, got, token)
        late_near = swap(late, "pb", 0)
        send_x, send_y, token = add_first(one, after=[token, early_all])
        last = (swap(send_x, "pa", 2), swap(send_y, "pa", 1))
        xk, xs, yk, ys, token = weights_two(me, acts[2], across(g_inner), acts[1], across(low), after=[token])
        two = ((xk, swap(xs, "pa", 1)), (yk, swap(ys, "pa", 2)))
        share_one, token = add_second([one[0] + last[:1], one[1] + last[1:]], after=[token])
        got_one = inward(share_one)
        late, token = stack_late(late, late_near, after=[token])
        late_far = swap(late, "pb", 1)
        grads, diagonal_b, token = back_of(FIRST, PAIRS - FIRST, [token], grads)
        there = swap(grads, "pa", 0)
        g_rows, small, token = rows_end(token)
        got_small = swap(small, "pa", 0)
        send_x, send_y, token = add_first(two, after=[token])
        last = (swap(send_x, "pa", 2), swap(send_y, "pa", 1))
        share_one, token = add_pair(share_one, got_one, after=[token])
        got_one = between(share_one)
        outer, token = outer_end(token, late, late_far)
        share_two, token = add_second([two[0] + last[:1], two[1] + last[1:]], after=[token])
        got_two = inward(share_two)
        xk, xs, yk, ys, token = weights_three(me, acts[0], (grads, there), (small, got_small), after=[token])
        three = ((xk, swap(xs, "pa", 1)), (yk, swap(ys, "pa", 2)))
        send_x, send_y, token = add_first(three, after=[token])
        last = (swap(send_x, "pa", 2), swap(send_y, "pa", 1))
        share_one, token = add_pair(share_one, got_one, after=[token])
        total_one = outward(share_one)
        share_two, token = add_pair(share_two, got_two, after=[token])
        got_two = between(share_two)
        share_three, token = add_second([three[0] + last[:1], three[1] + last[1:]], side=True, after=[token])
        parts = swap_parts(share_three)
        share_two, token = add_pair(share_two, got_two, after=[token])
        total_two = outward(share_two)
        total_three = spread_parts(*add_parts(share_three, parts, pb_me, after=[token, total_one]))
        small = total_three[D // pa_size :, :D]
        block = D // pa_size
        total_kv = jnp.concatenate([total_one[:block], total_one[block : 2 * block]], axis=1)
        total_ffn_out = total_one[2 * block :]
        second_part = 2 * block + block // 2
        total_ffn_in = jnp.concatenate(
            [total_two[first : first + block] for first in (0, block, second_part, second_part + block)], axis=1
        )
        total_out = jnp.concatenate([total_two[2 * block : second_part], total_two[second_part + 2 * block :]], axis=0)
        total_qkv = total_three[:block]
    else:
        partial = all_sum(partial, "pa")
        late, g_start, token = dec_end(partial, jnp.zeros_like(partial), token)
        late, token = stack_late(late, swap(late, "pb", 0), after=[token])
        late_far = swap(late, "pb", 1)
        grads, diagonal_a, token = back_of(0, FIRST, [token])
        grads, diagonal_b, token = back_of(FIRST, PAIRS - FIRST, [token], grads)
        g_rows, small, token = rows_end(token)
        outer, token = outer_end(token, late, late_far)
        small = all_sum(all_sum(small, "pa"), "pb")
        g_heads = jnp.concatenate([grads[0], grads[1], grads[2]], axis=1)
        total_kv = total_plain(share_over_pa(acts[4], across(g_pairs), 0))
        total_ffn_out = total_plain(share_over_pa(acts[3], across(branch), 1))
        total_ffn_in = total_plain(share_over_pa(acts[2], across(g_inner), 0))
        total_out = total_plain(share_over_pa(acts[1], across(low), 1))
        total_qkv = total_plain(share_over_pa(acts[0], across(g_heads), 0))

    d_qkv, d_out, d_query, d_cross, d_in, d_ffn, dec_small = outer
    dec_small = dec_small[0]
    dec_bias_rows = dec_small[3 * D :].reshape(H, STAT)[:, GROUP - ANS : GROUP]
    dec_bias_all = jnp.pad(jnp.transpose(dec_bias_rows[:, ::-1]), ((0, BUCKETS - ANS), (0, 0)))

    def own_part(vector, axis):
        height = vector.shape[0] // lax.axis_size(axis)
        return lax.dynamic_slice_in_dim(vector, lax.axis_index(axis) * height, height, axis=0)

    return (
        answer[None],
        g_rows.reshape(1, 1, SLOT, D),
        g_start[None],
        own_part(small[0], "pa"),
        total_qkv,
        jnp.transpose(small[4:16, :BUCKETS]),
        total_out,
        own_part(small[1], "pa"),
        total_ffn_in,
        total_ffn_out,
        own_part(small[2], "pa"),
        total_kv,
        own_part(dec_small[:D], "pb"),
        d_qkv,
        own_part(dec_bias_all, "pb"),
        d_out,
        own_part(dec_small[D : 2 * D], "pb"),
        d_query,
        d_cross,
        own_part(dec_small[2 * D : 3 * D], "pb"),
        d_in,
        d_ffn,
    )


def solution(mesh):
    copied = P()
    in_specs = (
        P("pb", "pa", None, None),
        P("pb", "pa"),
        P("pb", None, None),
        P("pb", None, None),
    ) + (copied,) * 19
    by_pa, by_pa_rows = P("pa"), P("pa", None)
    by_pb, by_pb_rows = P("pb"), P("pb", None)
    out_specs = (
        P("pb", None, None),
        P("pb", "pa", None, None),
        P("pb", None, None),
        by_pa,
        by_pa_rows,
        copied,
        by_pa_rows,
        by_pa,
        by_pa_rows,
        by_pa_rows,
        by_pa,
        by_pa_rows,
        by_pb,
        by_pb_rows,
        by_pb_rows,
        by_pb_rows,
        by_pb,
        by_pb_rows,
        by_pb_rows,
        by_pb,
        by_pb_rows,
        by_pb_rows,
    )
    return jax.shard_map(local, mesh=mesh, in_specs=in_specs, out_specs=out_specs, check_vma=False)
```

```python
import jax
import jax.numpy as jnp
import numpy as np
from jax import lax
from jax.experimental import pallas as pl
from jax.experimental.pallas import tpu as pltpu
from jax.sharding import PartitionSpec as P

D = 768
H = 12
HD = 64
FF = 3072
BUCKETS = 32
ANS = 20
SLOT = 512
PAIR = 2 * HD
PAIRS = H // 2
EDGE = 128
STRIP = 256
SPAN = 256
GROUP = 24
COST = (4 * 10**9, 0, 4 * 10**9, 0, 4 * 10**9)
STACK = H * GROUP
STAT = 128
STEPS = 4
WIDTH = FF // STEPS
FIRST = 4
EPS = 1e-06
MASKED = -1000000000.0
C_GELU = 0.7978845608028654
LOWER = jnp.bfloat16
WIDER = jnp.float32
EARLY = 7 * D + 2 * FF
LATE = 5 * D
AT = {
    "first": 0,
    "own": D,
    "second": 2 * D,
    "mix": 3 * D,
    "third": 4 * D,
    "hidden": 5 * D,
    "g_middle": 5 * D + FF,
    "g_inner": 6 * D + FF,
    "g_out": 6 * D + 2 * FF,
    "g_heads": 0,
    "g_after": 3 * D,
    "g_query": 4 * D,
}


def tile_classes(away):
    rows = [np.clip(EDGE * d - away, -(BUCKETS // 2), BUCKETS // 2 - 1) + BUCKETS // 2 for d in (-1, 0, 1)]
    return np.eye(BUCKETS, dtype=np.float32)[np.concatenate(rows)]


LANES = np.arange(SPAN)
PICK = tile_classes(np.where(LANES < EDGE, LANES, LANES - SPAN)).T
ENDS = np.repeat(np.eye(BUCKETS, dtype=np.float32)[[0, BUCKETS - 1]], EDGE, axis=0)
PICK_BACK = np.pad(np.concatenate([tile_classes(LANES - (EDGE - 1)), ENDS]), ((0, 0), (0, STAT - BUCKETS)))

SCALARS = pl.BlockSpec(memory_space=pltpu.SMEM)
ANY = pl.BlockSpec(memory_space=pl.ANY)
WHOLE = pl.BlockSpec(memory_space=pltpu.VMEM)
TOKEN = (8, 128)


def wide(*shape):
    return jax.ShapeDtypeStruct(shape, WIDER)


def narrow(*shape):
    return jax.ShapeDtypeStruct(shape, LOWER)


def run(name, body, ins, in_specs, outs, out_specs=None, after=(), grid=(), scratch=(), flops=10**9, mib=63, alias=None):
    count, extra, results = len(ins), len(after), len(outs)
    if out_specs is None:
        out_specs = [WHOLE] * results
    zeros = (lambda *s: (0, 0)) if grid else (lambda: (0, 0))

    def wrapped(*refs):
        refs[count + extra + results][...] = jnp.zeros(TOKEN, WIDER)
        body(*refs[:count], *refs[count + extra : count + extra + results], *refs[count + extra + results + 1 :])

    got = pl.pallas_call(
        wrapped,
        grid=grid,
        out_shape=tuple(outs) + (wide(*TOKEN),),
        in_specs=list(in_specs) + [ANY] * extra,
        out_specs=tuple(out_specs) + (pl.BlockSpec(TOKEN, zeros),),
        scratch_shapes=list(scratch),
        input_output_aliases=alias or {},
        compiler_params=pltpu.CompilerParams(vmem_limit_bytes=mib * 2**20),
        cost_estimate=pl.CostEstimate(flops=10 * flops, bytes_accessed=1, transcendentals=0),
        name=name,
    )(*ins, *after)
    return got


def product(left, right):
    return jnp.dot(left, right, preferred_element_type=WIDER)


def left_product(left, right):
    return lax.dot_general(left, right, (((0,), (0,)), ((), ())), preferred_element_type=WIDER)


def right_product(left, right):
    return lax.dot_general(left, right, (((1,), (1,)), ((), ())), preferred_element_type=WIDER)


def split_product(left, right, terms):
    total = None
    for k in range(terms):
        part = left.astype(LOWER)
        left = left - part.astype(WIDER)
        term = product(part, right)
        total = term if total is None else total + term
    return total


def silu_like(inner):
    square = inner * inner
    tanh = jnp.tanh(inner * (C_GELU + (C_GELU * 0.044715) * square))
    half = 0.5 + 0.5 * tanh
    value = inner * half
    slope = half + value * (1.0 - tanh) * (C_GELU + (3.0 * C_GELU * 0.044715) * square)
    return value, slope


def row_of(ref):
    return ref[...].reshape(1, D)


def scale_of(values):
    return lax.rsqrt(jnp.mean(values * values, axis=-1, keepdims=True) + EPS)


def norm_pull(values, gain, grad):
    scale = scale_of(values)
    lifted = grad * gain
    inside = jnp.sum(values * lifted, axis=-1, keepdims=True)
    back = scale * lifted - values * (scale * scale * scale * inside * (1.0 / D))
    return back, jnp.sum(grad * values * scale, axis=0, keepdims=True)


def fetch(pairs, sems):
    copies = [pltpu.make_async_copy(s, t, sems.at[k]) for k, (s, t) in enumerate(pairs)]
    for copy in copies:
        copy.start()
    return copies


def bias_tiles(u_ref, head):
    tiles = []
    for d in range(3):
        row = u_ref[pl.ds(head, 1), SPAN * d : SPAN * d + SPAN]
        spread = jnp.broadcast_to(row, (EDGE, SPAN))
        tiles.append(pltpu.roll(spread, 0, 1, stride=1, stride_axis=0)[:, :EDGE])
    return tiles


def key_masks(n):
    places = lax.broadcasted_iota(jnp.int32, (EDGE, EDGE), 0)
    return [jnp.where(places + EDGE * j < n, 0.0, MASKED) for j in range(SLOT // EDGE)]


def score_blocks(raw, tiles, masks, low, high, first):
    columns = []
    for c in range(STRIP // EDGE):
        blocks = []
        for j in range(SLOT // EDGE):
            block = raw[EDGE * j : EDGE * j + EDGE, EDGE * c : EDGE * c + EDGE]
            d = j - first - c
            block = block + (tiles[d + 1] if abs(d) <= 1 else (low if d < 0 else high))
            blocks.append(block + masks[j] if j > 0 else block)
        columns.append(blocks)
    return columns


def paved(columns, kind):
    return jnp.concatenate([jnp.concatenate([b.astype(kind) for b in blocks], axis=0) for blocks in columns], axis=1)


def fill_rows(table_ref, pick_ref, u_ref):
    @pl.when(pl.program_id(0) == 0)
    def _():
        u_ref[...] = split_product(table_ref[...], pick_ref[...], 3)


def attn_fwd_kernel(n_ref, ends_ref, table_ref, pick_ref, x_ref, g1_ref, wq_ref, wk_ref, wv_ref, first_ref, heads_ref, o_ref, st_ref, u_ref):
    fill_rows(table_ref, pick_ref, u_ref)
    step = pl.program_id(0)

    @pl.when(step == 0)
    def _():
        rows = x_ref[...].astype(WIDER)
        first_ref[...] = (rows * scale_of(rows) * row_of(g1_ref)).astype(LOWER)

    masks = key_masks(n_ref[0])
    first = first_ref[...]
    for k, w_ref in enumerate((wq_ref, wk_ref, wv_ref)):
        heads_ref[k] = product(first, w_ref[...]).astype(LOWER)
    q_ref, k_ref = heads_ref.at[0], heads_ref.at[1]
    values = jnp.transpose(heads_ref[2])
    ones = jnp.ones((16, SLOT), LOWER)
    mixed = []
    for h in range(2):
        head = 2 * step + h
        low, high = ends_ref[head, 0], ends_ref[head, BUCKETS - 1]
        tiles = bias_tiles(u_ref, head)
        cols = slice(HD * h, HD * h + HD)
        keys = k_ref[:, cols]
        left = jnp.concatenate([values[cols], ones], axis=0)
        strips = []
        for i in range(0, SLOT // EDGE, STRIP // EDGE):
            lanes = slice(EDGE * i, EDGE * i + STRIP)
            raw = right_product(keys, q_ref[lanes, cols] * 0.125)
            tops, powers = [], []
            for blocks in score_blocks(raw, tiles, masks, low, high, i):
                top = jnp.maximum(jnp.maximum(blocks[0], blocks[1]), jnp.maximum(blocks[2], blocks[3]))
                top = jnp.max(top, axis=0, keepdims=True)
                tops.append(top)
                powers.append([jnp.exp(block - top) for block in blocks])
            out = product(left, paved(powers, LOWER))
            total = out[HD : HD + 1]
            st_ref[0, h : h + 1, lanes] = jnp.concatenate(tops, axis=1) + jnp.log(total)
            strips.append(out[:HD] * (1.0 / total))
        mixed.append(jnp.concatenate(strips, axis=1))
    lanes = pl.ds(pl.multiple_of(step * PAIR, PAIR), PAIR)
    o_ref[:, lanes] = jnp.transpose(jnp.concatenate(mixed, axis=0)).astype(LOWER)


def attn_bwd_kernel(base):
    def body(
        n_ref, ends_ref, table_ref, pick_ref, h_ref, g_ref, o_ref, st_ref, gh_ref, gb_ref, u_ref
    ):
        q_ref, k_ref, v_ref = h_ref.at[0], h_ref.at[1], h_ref.at[2]
        fill_rows(table_ref, pick_ref, u_ref)
        step = pl.program_id(0) + base
        masks = key_masks(n_ref[0])
        keys_t = jnp.transpose(k_ref[...])
        rows = lax.broadcasted_iota(jnp.int32, (EDGE, EDGE), 0)
        columns = lax.broadcasted_iota(jnp.int32, (EDGE, EDGE), 1)
        mirror = jnp.where(rows + columns == EDGE - 1, 1.0, 0.0).astype(LOWER)
        rows = lax.broadcasted_iota(jnp.int32, (16, SLOT), 0) * EDGE
        columns = lax.broadcasted_iota(jnp.int32, (16, SLOT), 1)
        places = jnp.where((columns >= rows) & (columns < rows + EDGE), 1.0, 0.0).astype(LOWER)
        rows = lax.broadcasted_iota(jnp.int32, (16, PAIR), 0) * HD
        columns = lax.broadcasted_iota(jnp.int32, (16, PAIR), 1)
        halves = jnp.where((columns >= rows) & (columns < rows + HD), 1.0, 0.0).astype(LOWER)
        met = g_ref[...].astype(WIDER) * o_ref[...].astype(WIDER)
        upper = met.astype(LOWER)
        lower = (met - upper.astype(WIDER)).astype(LOWER)
        weighted = right_product(halves, upper) + right_product(halves, lower)
        grad_queries = []
        gb_ref[0, 2:8, :] = jnp.zeros((6, 4 * SPAN), WIDER)
        for h in range(2):
            head = 2 * step + h
            low, high = ends_ref[head, 0], ends_ref[head, BUCKETS - 1]
            tiles = bias_tiles(u_ref, head)
            cols = slice(HD * h, HD * h + HD)
            keys = k_ref[:, cols]
            values = v_ref[:, cols]
            left = jnp.concatenate([keys_t[cols], places], axis=0)
            grad_keys = jnp.zeros((SLOT, HD), WIDER)
            grad_values = jnp.zeros((SLOT, HD), WIDER)
            strips = []
            sums = {}

            def gather(d, block):
                sums[d] = sums[d] + block if d in sums else block

            for i in range(0, SLOT // EDGE, STRIP // EDGE):
                lanes = slice(EDGE * i, EDGE * i + STRIP)
                query = q_ref[lanes, cols]
                grad = g_ref[lanes, cols]
                raw = right_product(keys, query * 0.125)
                grad_probs = right_product(values, grad)
                probs, changes = [], []
                for c, blocks in enumerate(score_blocks(raw, tiles, masks, low, high, i)):
                    part = slice(EDGE * (i + c), EDGE * (i + c) + EDGE)
                    total = st_ref[0, h : h + 1, part]
                    mean = weighted[h : h + 1, part]
                    probs.append([jnp.exp(block - total) for block in blocks])
                    changes.append([])
                    for j in range(SLOT // EDGE):
                        gap = grad_probs[EDGE * j : EDGE * j + EDGE, EDGE * c : EDGE * c + EDGE] - mean
                        change = probs[c][j] * gap
                        changes[c].append(change)
                        if abs(j - i - c) <= 1:
                            gather(j - i - c, change)
                rounded = paved(changes, LOWER)
                out = product(left, rounded)
                strips.append(out[:HD])
                for c in range(STRIP // EDGE):
                    for j in range(SLOT // EDGE):
                        if abs(j - i - c) > 1:
                            gather(2 if j > i + c else -2, out[HD + j : HD + j + 1, EDGE * c : EDGE * c + EDGE])
                grad_keys += product(rounded, query)
                grad_values += product(paved(probs, LOWER), grad)
            grad_queries.append(jnp.concatenate(strips, axis=1))
            gh_ref[1, :, cols] = (grad_keys * 0.125).astype(LOWER)
            gh_ref[2, :, cols] = grad_values.astype(LOWER)
            empty = jnp.zeros((EDGE, SPAN - EDGE), WIDER)
            band = jnp.concatenate([sums[-1], sums[0], sums[1]], axis=1)
            upper = band.astype(LOWER)
            lower = (band - upper.astype(WIDER)).astype(LOWER)
            mirrored = product(mirror, upper) + product(mirror, lower)
            for d in range(3):
                spread = jnp.concatenate([mirrored[:, EDGE * d : EDGE * d + EDGE], empty], axis=1)
                turned = pltpu.roll(spread, 0, 1, stride=1, stride_axis=0)
                gb_ref[0, h : h + 1, SPAN * d : SPAN * d + SPAN] = jnp.sum(turned, axis=0, keepdims=True)
            for place, d in ((3 * SPAN, -2), (3 * SPAN + EDGE, 2)):
                gb_ref[0, h : h + 1, place : place + EDGE] = sums[d]
        gh_ref[0] = (jnp.transpose(jnp.concatenate(grad_queries, axis=0)) * 0.125).astype(LOWER)

    return body


def columns_at(first):
    return pl.BlockSpec((SLOT, PAIR), lambda s: (0, first + s))


def stats_at(first):
    return pl.BlockSpec((1, 2, SLOT), lambda s: (first + s, 0, 0))


def pair_of_all(base):
    return pl.BlockSpec((3, SLOT, PAIR), lambda s: (0, 0, base + s))


def attention_back(count, table, pick, heads, grad_mixed, mixed, stats, base, half, after=()):
    return run(
        "enc_attention_back",
        attn_bwd_kernel(base),
        [count, table, table, pick, heads, grad_mixed, mixed, stats],
        [SCALARS, SCALARS, WHOLE, WHOLE, pair_of_all(base), columns_at(base), columns_at(base), stats_at(base)],
        [narrow(3, SLOT, D), wide(half, 8, 4 * SPAN)],
        [pair_of_all(base), pl.BlockSpec((1, 8, 4 * SPAN), lambda s: (s, 0, 0))],
        after=after,
        grid=(half,),
        scratch=[pltpu.VMEM((H, 3 * SPAN), WIDER)],
        flops=2 * 5 * H * SLOT * SLOT * HD * 4,
    )


def send_out(pairs, sems, first):
    copies = [pltpu.make_async_copy(s, t, sems.at[first + k]) for k, (s, t) in enumerate(pairs)]
    for copy in copies:
        copy.start()
    return copies


def chunk(k):
    return slice(WIDTH * k, WIDTH * k + WIDTH)


def copy_all(pairs, sems):
    return [pltpu.make_async_copy(s, t, sems.at[k]) for k, (s, t) in enumerate(pairs)]


def forward_kernel(
    n_ref, ends_ref, table_ref, pick_ref, x_ref, g1_ref, wq_ref, wk_ref, wv_ref,
    g2_ref, g3_ref, query_ref, wo_any, in_any, out_any, kv_any,
    first_ref, heads_ref, mixed_ref, st_ref, packed_ref,
    after_any, second_any, slope_any, hidden_any, final_any, third_any, pairs_any,
    u_ref, wo_ref, in_ref, out_ref, kv_ref,
    after_ref, second_ref, slope_ref, hidden_ref, final_ref, third_ref, pairs_ref,
    sems, out_sems,
):
    step = pl.program_id(0)
    pairs = [(wo_any, wo_ref)]
    for k in range(STEPS):
        pairs += [(in_any.at[:, chunk(k)], in_ref.at[k]), (out_any.at[chunk(k)], out_ref.at[k])]
    copies = copy_all(pairs + [(kv_any, kv_ref)], sems)

    @pl.when(step == 0)
    def _():
        for copy in copies:
            copy.start()

    attn_fwd_kernel(
        n_ref, ends_ref, table_ref, pick_ref, x_ref, g1_ref, wq_ref, wk_ref, wv_ref,
        first_ref, heads_ref, mixed_ref, st_ref, u_ref,
    )

    @pl.when(step == PAIRS - 1)
    def _():
        for copy in copies:
            copy.wait()
        after = x_ref[...].astype(WIDER) + product(mixed_ref[...], wo_ref[...])
        after_ref[...] = after
        second = (after * scale_of(after) * row_of(g2_ref)).astype(LOWER)
        second_ref[...] = second
        inner = product(second, in_ref[0])
        sent = send_out([(after_ref, after_any), (second_ref, second_any)], out_sems, 0)
        total = after
        for k in range(STEPS):
            following = product(second, in_ref[k + 1]) if k + 1 < STEPS else None
            value, slope = silu_like(inner)
            slope_ref[:, chunk(k)] = slope.astype(LOWER)
            hidden = value.astype(LOWER)
            hidden_ref[:, chunk(k)] = hidden
            total = total + product(hidden, out_ref[k])
            inner = following
            if k % 2:
                half = slice(WIDTH * (k - 1), WIDTH * (k + 1))
                sent += send_out(
                    [(slope_ref.at[:, half], slope_any.at[:, half]), (hidden_ref.at[:, half], hidden_any.at[:, half])],
                    out_sems, len(sent),
                )
        final_ref[...] = total
        third = (total * scale_of(total) * row_of(g3_ref)).astype(LOWER)
        third_ref[...] = third
        sent += send_out([(final_ref, final_any), (third_ref, third_any)], out_sems, len(sent))
        for k in range(2):
            half = slice(D * k, D * k + D)
            pairs_ref[:, half] = product(third, kv_ref[:, half]).astype(LOWER)
        sent += send_out([(pairs_ref, pairs_any)], out_sems, len(sent))
        cross_kernel(n_ref, query_ref, pairs_ref, packed_ref)
        for copy in sent:
            copy.wait()


def whole(*shape):
    return pl.BlockSpec(shape, lambda s: (0,) * len(shape))


def forward(count, table, pick, x, gain1, qkv, gain2, gain3, query, wo, ffn_in, ffn_out, kv, after=()):
    def weights_at(first):
        return pl.BlockSpec((D, PAIR), lambda s: (0, first + s))

    kept = [wide(SLOT, D), narrow(SLOT, D), narrow(SLOT, FF), narrow(SLOT, FF), wide(SLOT, D), narrow(SLOT, D), narrow(SLOT, 2 * D)]
    return run(
        "enc_forward",
        forward_kernel,
        [count, table, table, pick, x, gain1, qkv, qkv, qkv, gain2, gain3, query, wo, ffn_in, ffn_out, kv],
        [SCALARS, SCALARS, WHOLE, WHOLE, whole(SLOT, D), whole(D), weights_at(0), weights_at(PAIRS), weights_at(2 * PAIRS)]
        + [whole(D), whole(D), whole(GROUP, D)] + [ANY] * 4,
        [narrow(SLOT, D), narrow(3, SLOT, D), narrow(SLOT, D), wide(PAIRS, 2, SLOT), wide(GROUP, D + STAT)] + kept,
        [whole(SLOT, D), pair_of_all(0), whole(SLOT, D), stats_at(0), whole(GROUP, D + STAT)] + [ANY] * 7,
        after=after,
        grid=(PAIRS,),
        scratch=[
            pltpu.VMEM((H, 3 * SPAN), WIDER),
            pltpu.VMEM((D, D), LOWER),
            pltpu.VMEM((STEPS, D, WIDTH), LOWER),
            pltpu.VMEM((STEPS, WIDTH, D), LOWER),
            pltpu.VMEM((D, 2 * D), LOWER),
        ]
        + [pltpu.VMEM(out.shape, out.dtype) for out in kept]
        + [pltpu.SemaphoreType.DMA((2 * STEPS + 2,)), pltpu.SemaphoreType.DMA((9,))],
        flops=2 * SLOT * D * (D + 2 * FF + 2 * D),
    )


def ffn_back_kernel(
    branch_ref, g2_ref, gfinal_any, after_any, slope_any, out_any, in_any, wo_any,
    ginner_any, gafter_any, low_any, gmixed_any, gain_ref,
    gfinal_ref, after_ref, slope_ref, out_ref, in_ref, wo_ref, ginner_ref, gafter_ref, low_ref, gmixed_ref,
    sems, out_sems,
):
    pairs = []
    for k in range(STEPS):
        pairs += [(out_any.at[chunk(k)], out_ref.at[k]), (slope_any.at[:, chunk(k)], slope_ref.at[k])]
        pairs += [(in_any.at[:, chunk(k)], in_ref.at[k])]
    copies = fetch(pairs + [(after_any, after_ref), (gfinal_any, gfinal_ref), (wo_any, wo_ref)], sems)
    branch = branch_ref[...]
    copies[0].wait()
    grad = right_product(branch, out_ref[0])
    total = None
    sent = []
    for k in range(STEPS):
        copies[3 * k + 1].wait()
        copies[3 * k + 2].wait()
        copies[3 * k + 3].wait()
        following = right_product(branch, out_ref[k + 1]) if k + 1 < STEPS else None
        inner = (grad * slope_ref[k].astype(WIDER)).astype(LOWER)
        ginner_ref[:, chunk(k)] = inner
        term = right_product(inner, in_ref[k])
        total = term if total is None else total + term
        grad = following
        sent += send_out([(ginner_ref.at[:, chunk(k)], ginner_any.at[:, chunk(k)])], out_sems, len(sent))
    copies[3 * STEPS + 1].wait()
    copies[3 * STEPS + 2].wait()
    back, gain = norm_pull(after_ref[...], row_of(g2_ref), total)
    gain_ref[...] = gain
    g_after = gfinal_ref[...] + back
    gafter_ref[...] = g_after
    low = g_after.astype(LOWER)
    low_ref[...] = low
    sent += send_out([(gafter_ref, gafter_any), (low_ref, low_any)], out_sems, len(sent))
    gmixed_ref[...] = right_product(low, wo_ref[...]).astype(LOWER)
    sent += send_out([(gmixed_ref, gmixed_any)], out_sems, len(sent))
    for copy in sent:
        copy.wait()


def ffn_back(branch, ffn_out, slope, ffn_in, after_rows, gain2, g_final, wo, after=()):
    outs = [narrow(SLOT, FF), wide(SLOT, D), narrow(SLOT, D), narrow(SLOT, D)]
    return run(
        "enc_ffn_back",
        ffn_back_kernel,
        [branch, gain2, g_final, after_rows, slope, ffn_out, ffn_in, wo],
        [WHOLE] * 2 + [ANY] * 6,
        outs + [wide(1, D)],
        [ANY] * 4 + [WHOLE],
        after=after,
        scratch=[
            pltpu.VMEM((SLOT, D), WIDER),
            pltpu.VMEM((SLOT, D), WIDER),
            pltpu.VMEM((STEPS, SLOT, WIDTH), LOWER),
            pltpu.VMEM((STEPS, WIDTH, D), LOWER),
            pltpu.VMEM((STEPS, D, WIDTH), LOWER),
            pltpu.VMEM((D, D), LOWER),
        ]
        + [pltpu.VMEM(out.shape, out.dtype) for out in outs]
        + [pltpu.SemaphoreType.DMA((3 * STEPS + 3,)), pltpu.SemaphoreType.DMA((STEPS + 3,))],
        flops=2 * SLOT * D * (D + 2 * FF),
    )


def attention_end(
    count, table, pick, heads, grad_mixed, mixed, stats, begun, diagonal, qkv, x, gain1,
    g_after, gain2, gain3, pick_back, after=(),
):
    base = FIRST
    half = PAIRS - FIRST
    inner = attn_bwd_kernel(base)

    def body(
        n_ref, ends_ref, table_ref, pick_ref, h_ref, g_ref, o_ref, st_ref, begun_any,
        da_ref, x_ref, g1_ref, gain2_ref, gain3_ref, back_ref, qkv_any, gafter_any,
        gh_any, small_ref, gb_ref, grows_any,
        u_ref, gh_ref, gall_ref, w_ref, gafter_ref, grows_ref, sems, out_sems,
    ):
        step = pl.program_id(0)
        old = slice(0, base * PAIR)
        loads = copy_all([(begun_any.at[:, :, old], gall_ref.at[:, :, old]), (qkv_any, w_ref), (gafter_any, gafter_ref)], sems)

        @pl.when(step == 0)
        def _():
            for load in loads:
                load.start()

        inner(n_ref, ends_ref, table_ref, pick_ref, h_ref, g_ref, o_ref, st_ref, gh_ref, gb_ref, u_ref)
        for k in range(half):

            @pl.when(step == k)
            def _():
                place = slice((base + k) * PAIR, (base + k + 1) * PAIR)
                gall_ref[:, :, place] = gh_ref[...]
                sums_ref = gb_ref.at[0]
                small_ref[2 * k : 2 * k + 2] = sums_ref[:2]

        @pl.when(step == half - 1)
        def _():
            new = slice(base * PAIR, D)
            sent = send_out([(gall_ref.at[:, :, new], gh_any.at[:, :, new])], out_sems, 0)
            for load in loads:
                load.wait()
            total = right_product(gall_ref[0], w_ref[:, :D])
            total = total + right_product(gall_ref[1], w_ref[:, D : 2 * D])
            total = total + right_product(gall_ref[2], w_ref[:, 2 * D :])
            back, gain = norm_pull(x_ref[...].astype(WIDER), row_of(g1_ref), total)
            grows_ref[...] = gafter_ref[...] + back
            sent += send_out([(grows_ref, grows_any)], out_sems, 1)
            sums = [da_ref[k, :2] for k in range(base)]
            sums += [small_ref[2 * k : 2 * k + 2] for k in range(half)]
            found = split_product(jnp.concatenate(sums, axis=0), back_ref[...], 2)
            small_ref[...] = jnp.zeros((16, D + 2 * EDGE), WIDER)
            small_ref[0:1, :D] = gain
            small_ref[1:2, :D] = gain2_ref[...]
            small_ref[2:3, :D] = gain3_ref[...]
            small_ref[4:16, :STAT] = found
            for copy in sent:
                copy.wait()

    rows = whole(SLOT, D)
    grads, small, unused, g_rows, token = run(
        "enc_attention_end",
        body,
        [count, table, table, pick, heads, grad_mixed, mixed, stats, begun]
        + [diagonal, x, gain1, gain2, gain3, pick_back, qkv, g_after],
        [SCALARS, SCALARS, WHOLE, WHOLE, pair_of_all(base), columns_at(base), columns_at(base), stats_at(base), ANY]
        + [whole(*diagonal.shape), rows, whole(D), whole(1, D), whole(1, D), whole(4 * SPAN, STAT), ANY, ANY],
        [narrow(3, SLOT, D), wide(16, D + 2 * EDGE), wide(half, 8, 4 * SPAN), wide(SLOT, D)],
        [ANY, whole(16, D + 2 * EDGE), pl.BlockSpec((1, 8, 4 * SPAN), lambda s: (s, 0, 0)), ANY],
        after=after,
        grid=(half,),
        scratch=[
            pltpu.VMEM((H, 3 * SPAN), WIDER),
            pltpu.VMEM((3, SLOT, PAIR), LOWER),
            pltpu.VMEM((3, SLOT, D), LOWER),
            pltpu.VMEM((D, 3 * D), LOWER),
            pltpu.VMEM((SLOT, D), WIDER),
            pltpu.VMEM((SLOT, D), WIDER),
            pltpu.SemaphoreType.DMA((3,)),
            pltpu.SemaphoreType.DMA((2,)),
        ],
        flops=2 * 5 * H * SLOT * SLOT * HD * 4,
        alias={8: 0},
    )
    return g_rows, small, unused, grads, token


def head_lanes(h):
    lanes = lax.broadcasted_iota(jnp.int32, (GROUP, D), 1)
    return (lanes >= h * HD) & (lanes < (h + 1) * HD)


def stack_heads(flat):
    return jnp.concatenate([jnp.where(head_lanes(h), flat, 0.0) for h in range(H)], axis=0)


def merge_heads(stacked):
    total = jnp.zeros((GROUP, D), WIDER)
    for h in range(H):
        total = total + jnp.where(head_lanes(h), stacked[GROUP * h : GROUP * h + GROUP], 0.0)
    return total


def lanes_to_column(stat):
    lanes = lax.broadcasted_iota(jnp.int32, (GROUP, STAT), 1)
    parts = [jnp.sum(jnp.where(lanes == h, stat, 0.0), axis=1, keepdims=True) for h in range(H)]
    return jnp.concatenate(parts, axis=0)


def column_to_lanes(column, first):
    lanes = lax.broadcasted_iota(jnp.int32, (GROUP, STAT), 1)
    total = jnp.zeros((GROUP, STAT), WIDER)
    for h in range(H):
        total = total + jnp.where(lanes == first + h, column[GROUP * h : GROUP * h + GROUP], 0.0)
    return total


def spread_heads(stat):
    rows = lax.broadcasted_iota(jnp.int32, (STAT, D), 0) * HD
    lanes = lax.broadcasted_iota(jnp.int32, (STAT, D), 1)
    spread = jnp.where((lanes >= rows) & (lanes < rows + HD), 1.0, 0.0).astype(LOWER)
    return split_product(stat, spread, 2)


def own_scores(query, keys, table_ref):
    raw = right_product(query, keys)
    rows = lax.broadcasted_iota(jnp.int32, (GROUP, GROUP), 0)
    columns = lax.broadcasted_iota(jnp.int32, (GROUP, GROUP), 1)
    away = rows - columns
    parts = []
    for h in range(H):
        bias = jnp.full((GROUP, GROUP), table_ref[h, 0], WIDER)
        for d in range(1, GROUP):
            bias = jnp.where(away == d, table_ref[h, d], bias)
        part = raw[GROUP * h : GROUP * h + GROUP] + bias
        parts.append(jnp.where(away >= 0, part, MASKED))
    scores = jnp.concatenate(parts, axis=0)
    powers = jnp.exp(scores - jnp.max(scores, axis=1, keepdims=True))
    return powers / jnp.sum(powers, axis=1, keepdims=True)


def padded(ref, pad_ref):
    pad_ref[...] = jnp.zeros((GROUP, D), WIDER)
    pad_ref[:ANS] = ref[...].astype(WIDER)
    return pad_ref[...]


def answer_rows(width):
    return lax.broadcasted_iota(jnp.int32, (GROUP, width), 0) < ANS


def dec_self_kernel(
    table_ref, x_ref, g1_ref, g2_ref, qkv_any, out_any, query_any,
    after_ref, lefts_ref, heads_ref, query_ref,
    qkv_ref, out_ref, cross_ref, pad_ref, sems,
):
    copies = fetch(((qkv_any, qkv_ref), (out_any, out_ref), (query_any, cross_ref)), sems)
    start = padded(x_ref, pad_ref)
    first = (start * scale_of(start) * row_of(g1_ref)).astype(LOWER)
    copies[0].wait()
    heads = product(first, qkv_ref[...]).astype(LOWER)
    heads_ref[...] = heads
    query = stack_heads(heads.astype(WIDER)[:, :D] * 0.125).astype(LOWER)
    probs = own_scores(query, heads[:, D : 2 * D], table_ref)
    own = merge_heads(product(probs.astype(LOWER), heads[:, 2 * D :]))
    own = jnp.where(answer_rows(D), own, 0.0).astype(LOWER)
    copies[1].wait()
    after = start + product(own, out_ref[...])
    after_ref[...] = after
    second = (after * scale_of(after) * row_of(g2_ref)).astype(LOWER)
    copies[2].wait()
    query_ref[...] = product(second, cross_ref[...]).astype(LOWER)
    lefts_ref[:, :D] = first
    lefts_ref[:, D : 2 * D] = own
    lefts_ref[:, 2 * D :] = second


def masked_cross(n_ref, query_ref, pairs_ref):
    query = stack_heads(query_ref[...].astype(WIDER) * 0.125).astype(LOWER)
    raw = right_product(query, pairs_ref[:, :D])
    places = lax.broadcasted_iota(jnp.int32, (STACK, SLOT), 1)
    return query, jnp.where(places < n_ref[0], raw, MASKED)


def cross_kernel(n_ref, query_ref, pairs_ref, packed_ref):
    unused, scores = masked_cross(n_ref, query_ref, pairs_ref)
    top = jnp.max(scores, axis=1, keepdims=True)
    powers = jnp.exp(scores - top)
    total = jnp.sum(powers, axis=1, keepdims=True)
    probs = (powers / total).astype(LOWER)
    packed_ref[:, :D] = merge_heads(product(probs, pairs_ref[:, D:]))
    packed_ref[:, D:] = column_to_lanes(top, 0) + column_to_lanes(total, STAT // 2)


def dec_mid_kernel(
    n_ref, parts_ref, after_ref, cot_ref, g3_ref, lefts_ref, query_ref, e3_ref,
    pairs_any, cross_any, in_any, out_any, kv_any, final_any,
    answer_ref, early_ref, gmid_ref, gain_ref, partial_ref, gain_enc_ref, gpairs_any, gfinal_any, branch_any,
    pairs_ref, cross_ref, in_ref, out_ref, kv_ref, final_ref, gpairs_ref, gfinal_ref, branch_ref, pad_ref,
    sems, out_sems,
):
    held_pairs = ((cross_any, cross_ref), (in_any, in_ref), (out_any, out_ref), (pairs_any, pairs_ref))
    copies = fetch(held_pairs + ((kv_any, kv_ref), (final_any, final_ref)), sems)
    size = parts_ref.shape[0]
    used = lax.broadcasted_iota(jnp.int32, (GROUP, STAT), 1) < H
    tops = [parts_ref[k, :, D:] for k in range(size)]
    totals = [pltpu.roll(stat, STAT // 2, 1) for stat in tops]
    top = tops[0]
    for k in range(1, size):
        top = jnp.maximum(top, tops[k])
    weights = [jnp.where(used, totals[k] * jnp.exp(tops[k] - top), 0.0) for k in range(size)]
    total = weights[0]
    for k in range(1, size):
        total = total + weights[k]
    total = jnp.where(used, total, 1.0)
    mix = jnp.zeros((GROUP, D), WIDER)
    for k in range(size):
        mix = mix + parts_ref[k, :, :D] * spread_heads(weights[k] / total)
    mix_low = mix.astype(LOWER)
    copies[0].wait()
    middle = after_ref[...] + product(mix_low, cross_ref[...])
    third = (middle * scale_of(middle) * row_of(g3_ref)).astype(LOWER)
    copies[1].wait()
    inner = product(third, in_ref[...])
    value, slope = silu_like(inner)
    hidden = value.astype(LOWER)
    copies[2].wait()
    answer = (middle + product(hidden, out_ref[...])).astype(LOWER)
    answer_ref[...] = answer[:ANS]
    grad = padded(cot_ref, pad_ref)
    out_low = grad.astype(LOWER)
    g_inner = (right_product(out_low, out_ref[...]) * slope).astype(LOWER)
    back, gain = norm_pull(middle, row_of(g3_ref), right_product(g_inner, in_ref[...]))
    gain_ref[...] = gain
    g_middle = grad + back
    gmid_ref[...] = g_middle
    middle_low = g_middle.astype(LOWER)
    g_mix = right_product(middle_low, cross_ref[...]).astype(LOWER)

    def store(name, rows):
        early_ref[:, AT[name] : AT[name] + rows.shape[1]] = rows

    def kept(rows):
        return jnp.where(answer_rows(rows.shape[1]), rows.astype(WIDER), 0.0).astype(LOWER)

    early_ref[:, : 3 * D] = kept(lefts_ref[...])
    store("mix", kept(mix_low))
    store("third", kept(third))
    store("hidden", kept(hidden))
    store("g_middle", middle_low)
    store("g_inner", g_inner)
    store("g_out", out_low)
    copies[3].wait()
    copies[4].wait()
    copies[5].wait()
    query, scores = masked_cross(n_ref, query_ref, pairs_ref)
    probs = jnp.exp(scores - lanes_to_column(jnp.where(used, top, 0.0))) / lanes_to_column(total)
    grad = stack_heads(g_mix.astype(WIDER))
    weighted = jnp.sum(grad * jnp.concatenate([mix] * H, axis=0), axis=1, keepdims=True)
    grad = grad.astype(LOWER)
    grad_probs = right_product(grad, pairs_ref[:, D:])
    rounded = (probs * (grad_probs - weighted)).astype(LOWER)
    g_keys = left_product(rounded, query).astype(LOWER)
    g_values = left_product(probs.astype(LOWER), grad).astype(LOWER)
    gpairs_ref[:, :D] = g_keys
    gpairs_ref[:, D:] = g_values
    sent = send_out([(gpairs_ref, gpairs_any)], out_sems, 0)
    partial_ref[...] = merge_heads(product(rounded, pairs_ref[:, :D])) * 0.125
    g_third = right_product(g_keys, kv_ref[:, :D]) + right_product(g_values, kv_ref[:, D:])
    back, gain = norm_pull(final_ref[...], row_of(e3_ref), g_third)
    gain_enc_ref[...] = gain
    gfinal_ref[...] = back
    branch_ref[...] = back.astype(LOWER)
    sent += send_out([(gfinal_ref, gfinal_any), (branch_ref, branch_any)], out_sems, 1)
    for copy in sent:
        copy.wait()


def dec_back_kernel(
    table_ref, x_ref, part_ref, got_ref, after_ref, gmid_ref, heads_ref,
    g1_ref, g2_ref, gain3_ref, query_any, out_any, qkv_any,
    late_ref, gstart_ref,
    cross_ref, out_ref, qkv_ref, pad_ref, sems,
):
    copies = fetch(((query_any, cross_ref), (out_any, out_ref), (qkv_any, qkv_ref)), sems)
    g_query = (part_ref[...] + got_ref[...]).astype(LOWER)
    copies[0].wait()
    back, gain2 = norm_pull(after_ref[...], row_of(g2_ref), right_product(g_query, cross_ref[...]))
    g_after = gmid_ref[...] + back
    after_low = g_after.astype(LOWER)
    copies[1].wait()
    g_own = stack_heads(right_product(after_low, out_ref[...])).astype(LOWER)
    heads = heads_ref[...]
    query = stack_heads(heads.astype(WIDER)[:, :D] * 0.125).astype(LOWER)
    probs = own_scores(query, heads[:, D : 2 * D], table_ref)
    grad_probs = right_product(g_own, heads[:, 2 * D :])
    rounded = (probs * (grad_probs - jnp.sum(probs * grad_probs, axis=1, keepdims=True))).astype(LOWER)
    g_q = (merge_heads(product(rounded, heads[:, D : 2 * D])) * 0.125).astype(LOWER)
    g_k = left_product(rounded, query).astype(LOWER)
    g_v = left_product(probs.astype(LOWER), g_own).astype(LOWER)
    g_heads = jnp.concatenate([g_q, g_k, g_v], axis=1)
    copies[2].wait()
    start = padded(x_ref, pad_ref)
    back, gain1 = norm_pull(start, row_of(g1_ref), right_product(g_heads, qkv_ref[...]))
    gstart_ref[...] = (g_after + back)[:ANS]
    spread = rounded.astype(WIDER)
    rows = lax.broadcasted_iota(jnp.int32, (GROUP, GROUP), 0)
    columns = lax.broadcasted_iota(jnp.int32, (GROUP, GROUP), 1)
    mirror = jnp.where(rows + columns == GROUP - 1, 1.0, 0.0).astype(LOWER)
    empty = jnp.zeros((GROUP, STAT - GROUP), WIDER)
    tables = []
    for h in range(H):
        part = product(mirror, spread[GROUP * h : GROUP * h + GROUP].astype(LOWER))
        turned = pltpu.roll(jnp.concatenate([part, empty], axis=1), 0, 1, stride=1, stride_axis=0)
        tables.append(jnp.sum(turned, axis=0, keepdims=True))
    small = jnp.concatenate([gain1, gain2, gain3_ref[...]] + tables, axis=1)
    places = lax.broadcasted_iota(jnp.int32, (GROUP, LATE), 0)
    late = jnp.concatenate([g_heads, after_low, g_query], axis=1).astype(WIDER)
    late_ref[...] = jnp.where(places == ANS, small, late).astype(LOWER)


def dec_outer_kernel(size):
    part = D // size

    def body(me_ref, *refs):
        me = me_ref[0]
        small_ref = refs[9]
        there, here = refs[3:9], refs[10:16]
        early_ref, late_ref, sems = refs[16:]
        sent = []
        early_ref[...] = jnp.concatenate([refs[0][me ^ s].astype(WIDER) for s in range(size)], axis=0).astype(LOWER)
        late = [ref[...].astype(WIDER) for ref in refs[1:3]]
        late_ref[...] = jnp.concatenate(late, axis=0).astype(LOWER)
        rows = lax.broadcasted_iota(jnp.int32, (part, D), 0) + me * part
        lanes = lax.broadcasted_iota(jnp.int32, (part, D), 1)
        picked = jnp.where(rows == lanes, 1.0, 0.0).astype(LOWER)
        height = FF // size
        first = pl.multiple_of(AT["hidden"] + me * height, 128)

        def outer(k, name, right):
            left = right_product(picked, early_ref[:, AT[name] : AT[name] + D]).astype(LOWER)
            here[k][...] = product(left, right)
            sent.extend(send_out([(here[k], there[k])], sems, len(sent)))

        outer(4, "third", early_ref[:, AT["g_inner"] : AT["g_inner"] + FF])
        outer(0, "first", late_ref[:, : 3 * D])
        here[5][...] = left_product(early_ref[:, pl.ds(first, height)], early_ref[:, AT["g_out"] : AT["g_out"] + D])
        sent.extend(send_out([(here[5], there[5])], sems, len(sent)))
        outer(1, "own", late_ref[:, AT["g_after"] : AT["g_after"] + D])
        outer(2, "second", late_ref[:, AT["g_query"] : AT["g_query"] + D])
        outer(3, "mix", early_ref[:, AT["g_middle"] : AT["g_middle"] + D])
        total = jnp.zeros((1, LATE), WIDER)
        for part_late in late:
            for k in (0, GROUP):
                total = total + part_late[k + ANS : k + ANS + 1]
        small_ref[...] = total
        for copy in sent:
            copy.wait()

    return body


def held(*shapes):
    return [pltpu.VMEM(shape, LOWER) for shape in shapes] + [
        pltpu.VMEM((GROUP, D), WIDER),
        pltpu.SemaphoreType.DMA((len(shapes),)),
    ]


def dec_self(table, answers, gain1, gain2, qkv, out, query, after=()):
    return run(
        "dec_self",
        dec_self_kernel,
        [table, answers, gain1, gain2, qkv, out, query],
        [SCALARS] + [WHOLE] * 3 + [ANY] * 3,
        [wide(GROUP, D), narrow(GROUP, 3 * D), narrow(GROUP, 3 * D), narrow(GROUP, D)],
        after=after,
        scratch=held((D, 3 * D), (D, D), (D, D)),
        flops=10**9,
    )


def dec_mid(count, parts, after_rows, cotangent, gain3, lefts, query, enc_gain3, pairs, cross_out, ffn_in, ffn_out, kv, final, after=()):
    outs = [narrow(SLOT, 2 * D), wide(SLOT, D), narrow(SLOT, D)]
    shapes = [(SLOT, 2 * D), (D, D), (D, FF), (FF, D), (D, 2 * D)]
    return run(
        "dec_mid",
        dec_mid_kernel,
        [count, parts, after_rows, cotangent, gain3, lefts, query, enc_gain3, pairs, cross_out, ffn_in, ffn_out, kv, final],
        [SCALARS] + [WHOLE] * 7 + [ANY] * 6,
        [narrow(ANS, D), narrow(GROUP, EARLY), wide(GROUP, D), wide(1, D), wide(GROUP, D), wide(1, D)] + outs,
        [WHOLE] * 6 + [ANY] * 3,
        after=after,
        scratch=[pltpu.VMEM(shape, LOWER) for shape in shapes]
        + [pltpu.VMEM((SLOT, D), WIDER)]
        + [pltpu.VMEM(out.shape, out.dtype) for out in outs]
        + [pltpu.VMEM((GROUP, D), WIDER), pltpu.SemaphoreType.DMA((6,)), pltpu.SemaphoreType.DMA((3,))],
        flops=4 * 10**9,
    )


def dec_back(table, answers, part, got, after_rows, g_middle, heads, gain1, gain2, g_gain3, query, out, qkv, after=()):
    return run(
        "dec_back",
        dec_back_kernel,
        [table, answers, part, got, after_rows, g_middle, heads, gain1, gain2, g_gain3, query, out, qkv],
        [SCALARS] + [WHOLE] * 9 + [ANY] * 3,
        [narrow(GROUP, LATE), wide(ANS, D)],
        after=after,
        scratch=held((D, D), (D, D), (D, 3 * D)),
        flops=0,
    )


def dec_outer(me, early, late_one, late_two, size, after=()):
    part = D // size
    outs = [wide(part, 3 * D), wide(part, D), wide(part, D), wide(part, D), wide(part, FF), wide(FF // size, D)]
    return run(
        "dec_outer",
        dec_outer_kernel(size),
        [me, early, late_one, late_two],
        [SCALARS, WHOLE, WHOLE, WHOLE],
        outs + [wide(1, LATE)],
        [ANY] * 6 + [WHOLE],
        after=after,
        scratch=[pltpu.VMEM(out.shape, WIDER) for out in outs]
        + [pltpu.VMEM((size * GROUP, EARLY), LOWER), pltpu.VMEM((size * GROUP, LATE), LOWER), pltpu.SemaphoreType.DMA((6,))],
        flops=8 * 10**9,
    )


def stack_late(one, two, after=()):
    def body(one_ref, two_ref, out_ref):
        out_ref[...] = jnp.concatenate([one_ref[...].astype(WIDER), two_ref[...].astype(WIDER)], axis=0).astype(LOWER)

    return run("stack_late", body, [one, two], [WHOLE] * 2, [narrow(2 * GROUP, LATE)], after=after, flops=0)


PLACES = [(0, 0), (0, 1), (1, 0), (1, 1)]


def place_of(me, there):
    return me ^ (4 * there[0] + 2 * there[1])


def turned_rows(me, acts, block):
    lanes = lax.broadcasted_iota(jnp.int32, (block, D), 1)
    rows = lax.broadcasted_iota(jnp.int32, (block, D), 0)
    picked = [jnp.where(lanes - rows == place_of(me, t) * block, 1.0, 0.0).astype(LOWER) for t in PLACES]
    picked = jnp.concatenate(picked, axis=0)
    return jnp.concatenate([right_product(picked, act).astype(LOWER) for act in acts], axis=1)


def target(there, x_refs, y_refs):
    dy, dx = there
    return (x_refs[dx].at[dy], y_refs[dy].at[dx])


def pages_out(pairs, sems, first):
    return send_out([(here.at[k], there.at[k]) for here, there in pairs for k in range(2)], sems, first)


def one_kernel(
    me_ref, t_own, t_par, p_own, p_par, h_own, h_par, b_own, b_par, xk_any, xs_any, yk_any, ys_any,
    xk, xs, yk, ys, t, p, h, b, sems, out_sems,
):
    me = me_ref[0]
    block = FF // 8
    pairs = [(t_own, t.at[0]), (t_par, t.at[1]), (p_own, p.at[:SLOT]), (p_par, p.at[SLOT:])]
    pairs += [(b_own, b.at[:SLOT]), (b_par, b.at[SLOT:])]
    for k, there in enumerate(PLACES):
        lanes = pl.ds(pl.multiple_of(place_of(me, there) * block, 128), block)
        pairs += [(h_own.at[:, lanes], h.at[k, :SLOT]), (h_par.at[:, lanes], h.at[k, SLOT:])]
    copies = fetch(pairs, sems)
    copies[0].wait()
    copies[1].wait()
    height = D // 8
    left = turned_rows(me, (t[0], t[1]), height)
    for k in range(2, 8):
        copies[k].wait()
    for c in range(2):
        grad = product(left, p[:, D * c : D * c + D]).astype(LOWER)
        for k, there in enumerate(PLACES):
            to, unused = target(there, (xk, xs), (yk, ys))
            to[height * c : height * c + height] = grad[height * k : height * k + height]
    sent = []
    for k, there in enumerate(PLACES):
        grad = left_product(h[k], b[...]).astype(LOWER)
        to_x, to_y = target(there, (xk, xs), (yk, ys))
        to_x[2 * height : 3 * height] = grad[:height]
        to_y[...] = grad[height:]
        out_x, out_y = target(there, (xk_any, xs_any), (yk_any, ys_any))
        if k + 1 < len(PLACES):
            copies[8 + 2 * k].wait()
            copies[9 + 2 * k].wait()
        sent += send_out([(to_x, out_x), (to_y, out_y)], out_sems, len(sent))
    for copy in sent:
        copy.wait()


def two_kernel(
    me_ref, s_own, s_par, i_own, i_par, m_own, m_par, l_own, l_par, xk_any, xs_any, yk_any, ys_any,
    xk, xs, yk, ys, s, i, m, l, sems, out_sems,
):
    me = me_ref[0]
    pairs = [(s_own, s.at[0]), (s_par, s.at[1]), (m_own, m.at[0]), (m_par, m.at[1])]
    pairs += [(l_own, l.at[:SLOT]), (l_par, l.at[SLOT:])]
    for c in range(4):
        lanes = slice(D * c, D * c + D)
        pairs += [(i_own.at[:, lanes], i.at[c, :SLOT]), (i_par.at[:, lanes], i.at[c, SLOT:])]
    copies = fetch(pairs, sems)
    for k in range(6):
        copies[k].wait()
    height = D // 8
    half = height // 2
    left = turned_rows(me, (m[0], m[1]), height)
    turned = turned_rows(me, (s[0], s[1]), height)
    grad = product(left, l[...]).astype(LOWER)
    for k, there in enumerate(PLACES):
        for to, first in zip(target(there, (xk, xs), (yk, ys)), (0, half)):
            to[2 * height : 2 * height + half] = grad[height * k + first : height * k + first + half]
    sent = []
    for c in range(4):
        if c % 2 == 0:
            for k in range(6 + 2 * c, 10 + 2 * c):
                copies[k].wait()
        grad = product(turned, i[c]).astype(LOWER)
        for k, there in enumerate(PLACES):
            to = target(there, (xk, xs), (yk, ys))[c // 2]
            to[height * (c % 2) : height * (c % 2) + height] = grad[height * k : height * k + height]
        if c % 2:
            done = ((xk, xk_any), (xs, xs_any)) if c == 1 else ((yk, yk_any), (ys, ys_any))
            sent += pages_out(done, out_sems, len(sent))
    for copy in sent:
        copy.wait()


def three_kernel(
    me_ref, f_own, f_par, g_own, g_par, small_ref, got_ref, xk_any, xs_any, yk_any, ys_any,
    xk, xs, yk, ys, f, g, sems, out_sems,
):
    me = me_ref[0]
    small = (small_ref[:, :D] + got_ref[:, :D]).astype(LOWER)
    pairs = [(f_own, f.at[0]), (f_par, f.at[1])]
    for c in range(3):
        pairs += [(g_own.at[c], g.at[c, :SLOT]), (g_par.at[c], g.at[c, SLOT:])]
    copies = fetch(pairs, sems)
    copies[0].wait()
    copies[1].wait()
    height = D // 8
    half = D // 2
    left = turned_rows(me, (f[0], f[1]), height)
    for ref in (xk, xs, yk, ys):
        for k in range(2):
            ref[k, height:] = jnp.zeros((16, 3 * half), LOWER)
            if ref is xk or ref is xs:
                ref[k, height:, :D] = small
    for k in range(2, 8):
        copies[k].wait()
    sent = []
    for c in range(3):
        grad = product(left, g[c]).astype(LOWER)
        for k, there in enumerate(PLACES):
            to_x, to_y = target(there, (xk, xs), (yk, ys))
            block = grad[height * k : height * k + height]
            if c == 0:
                to_x[:height, :D] = block
            elif c == 1:
                to_x[:height, D:] = block[:, :half]
                to_y[:height, :half] = block[:, half:]
            else:
                to_y[:height, half:] = block
        if c:
            done = ((xk, xk_any), (xs, xs_any)) if c == 1 else ((yk, yk_any), (ys, ys_any))
            sent += pages_out(done, out_sems, len(sent))
    for copy in sent:
        copy.wait()


def weight_call(name, body, me, ins, rows, columns, held_shapes, flops, after, extra=()):
    out = narrow(2, rows, columns)
    copies = {"weights_one": 14, "weights_two": 14, "weights_three": 8}[name]
    return run(
        name,
        body,
        [me, *ins, *extra],
        [SCALARS] + [ANY] * len(ins) + [WHOLE] * len(extra),
        [out] * 4,
        [ANY] * 4,
        after=after,
        scratch=[pltpu.VMEM(out.shape, LOWER)] * 4
        + [pltpu.VMEM(shape, LOWER) for shape in held_shapes]
        + [pltpu.SemaphoreType.DMA((copies,)), pltpu.SemaphoreType.DMA((8,))],
        flops=flops,
    )


def weights_one(me, third, g_pairs, hidden, branch, after=()):
    shapes = [(2, SLOT, D), (2 * SLOT, 2 * D), (4, 2 * SLOT, FF // 8), (2 * SLOT, D)]
    ins = (*third, *g_pairs, *hidden, *branch)
    return weight_call("weights_one", one_kernel, me, ins, 3 * D // 8, D, shapes, 4 * 10**9, after)


def weights_two(me, second, g_inner, mixed, low, after=()):
    shapes = [(2, SLOT, D), (4, 2 * SLOT, D), (2, SLOT, D), (2 * SLOT, D)]
    ins = (*second, *g_inner, *mixed, *low)
    return weight_call("weights_two", two_kernel, me, ins, 5 * D // 16, D, shapes, 0, after)


def weights_three(me, first, grads, small, after=()):
    shapes = [(2, SLOT, D), (3, 2 * SLOT, D)]
    ins = (*first, *grads)
    return weight_call("weights_three", three_kernel, me, ins, D // 8 + 16, 3 * D // 2, shapes, COST[4], after, small)


def page(array, k):
    return pl.BlockSpec((1,) + array.shape[1:], lambda s: (k, 0, 0))


def add_first(parts, flops=0, after=()):
    count = len(parts)

    def body(*refs):
        for k in range(count):
            refs[2 * count + k][...] = (refs[2 * k][0].astype(WIDER) + refs[2 * k + 1][0].astype(WIDER)).astype(LOWER)

    flat = [a for pair in parts for a in pair]
    outs = [narrow(*keep.shape[1:]) for keep, unused in parts]
    return run("add_first", body, flat, [page(a, 1) for a in flat], outs, after=after, grid=(1,), flops=flops)


def add_second(parts, side=False, after=()):
    shapes = [keep.shape[1:] for keep, unused, unused_too in parts]
    rows = shapes[0][0] + 16 if side else sum(shape[0] for shape in shapes)
    columns = sum(shape[1] for shape in shapes) if side else shapes[0][1]

    def body(*refs):
        out = refs[-1]
        first = 0
        for k, (high, across) in enumerate(shapes):
            keep, got, last = refs[3 * k : 3 * k + 3]
            total = (keep[0].astype(WIDER) + got[0].astype(WIDER) + last[...].astype(WIDER)).astype(LOWER)
            if side:
                out[:high, first : first + across] = total
                first += across
            else:
                out[first : first + high] = total
                first += high
        if side:
            out[rows - 16 :] = jnp.zeros((16, columns), LOWER)

    flat = [a for trio in parts for a in trio]
    specs = [page(a, 0) if a.ndim == 3 else WHOLE for a in flat]
    return run("add_second", body, flat, specs, [narrow(rows, columns)], after=after, grid=(1,), flops=0)


def add_pair(one, two, flops=0, after=()):
    def body(one_ref, two_ref, out_ref):
        out_ref[...] = (one_ref[...].astype(WIDER) + two_ref[...].astype(WIDER)).astype(LOWER)

    return run("add_pair", body, [one, two], [WHOLE] * 2, [narrow(*one.shape)], after=after, flops=flops)


def add_parts(share, parts, me, after=()):
    rows, columns = parts[0].shape

    def body(me_ref, share_ref, one_ref, two_ref, three_ref, out_ref):
        first = pl.multiple_of(me_ref[0] * rows, 16)
        total = share_ref[pl.ds(first, rows), :].astype(WIDER) + one_ref[...].astype(WIDER)
        out_ref[...] = (total + two_ref[...].astype(WIDER) + three_ref[...].astype(WIDER)).astype(LOWER)

    return run("add_parts", body, [me, share, *parts], [SCALARS] + [WHOLE] * 4, [narrow(rows, columns)], after=after, flops=0)


def add_rows(one, two, after=()):
    def body(one_ref, two_ref, out_ref):
        out_ref[...] = one_ref[...] + two_ref[...]

    return run("add_rows", body, [one, two], [WHOLE] * 2, [wide(*one.shape)], after=after, flops=0)


def partner(axis, bit):
    return [(k, k ^ (1 << bit)) for k in range(lax.axis_size(axis))]


def swap(value, axis, bit):
    return lax.ppermute(value, axis, partner(axis, bit))


def all_sum(value, axis):
    for bit in range(lax.axis_size(axis).bit_length() - 1):
        value = value + swap(value, axis, bit)
    return value


def pa_order(turn):
    rest = lax.axis_size("pa").bit_length() - 2
    return [1 + (k + turn) % rest for k in range(rest)]


def both_cores(acts, turn):
    size = lax.axis_size("pa")
    me = lax.axis_index("pa")
    blocks = jnp.transpose(acts).reshape(size, acts.shape[1] // size, acts.shape[0])
    order = pa_order(turn)
    offsets = [
        sum(((k >> (len(order) - 1 - p)) & 1) << bit for p, bit in enumerate(order)) for k in range(size // 2)
    ]
    mine = jnp.concatenate([lax.dynamic_slice_in_dim(blocks, me ^ d, 1) for d in offsets])
    theirs = jnp.concatenate([lax.dynamic_slice_in_dim(blocks, me ^ d ^ 1, 1) for d in offsets])
    return mine, swap(theirs, "pa", 0)


def weight_part(acts, grads, first, last):
    total = None
    for act, grad in zip(acts, grads):
        act = act[first:last]
        term = product(act.reshape(-1, act.shape[2]), grad)
        total = term if total is None else total + term
    height = acts[0].shape[1]
    return total.astype(LOWER).reshape(last - first, height, -1)


def add_up(parts):
    total = parts[0].astype(WIDER)
    for part in parts[1:]:
        total = total + part.astype(WIDER)
    return total.astype(LOWER)


def share_over_pa(acts, grads, turn):
    size = acts[0].shape[0]
    keep = [weight_part(acts, grads, 0, size // 2)]
    send = weight_part(acts, grads, size // 2, size)
    for bit in pa_order(turn):
        keep.append(swap(send, "pa", bit))
        size //= 2
        if size > 1:
            send = add_up([part[size // 2 : size] for part in keep])
            keep = [part[: size // 2] for part in keep]
    return add_up([part[0] for part in keep])


def inward(share):
    return lax.ppermute(share, "pb", [(0, 1), (3, 2)])


def between(share):
    return lax.ppermute(share, "pb", [(1, 2), (2, 1)])


def outward(share):
    me = lax.axis_index("pb")
    got = lax.ppermute(share, "pb", [(1, 0), (2, 3)])
    return jnp.where((me == 1) | (me == 2), share, got).astype(WIDER)


def swap_parts(share):
    me = lax.axis_index("pb")
    quarters = share.reshape(4, share.shape[0] // 4, share.shape[1])
    return [
        lax.ppermute(lax.dynamic_index_in_dim(quarters, me ^ s, 0, False), "pb", [(k, k ^ s) for k in range(4)])
        for s in range(1, 4)
    ]


def spread_parts(total, token):
    me = lax.axis_index("pb")
    got = [total] + [lax.ppermute(total, "pb", [(k, k ^ s) for k in range(4)]) for s in range(1, 4)]
    return jnp.concatenate([lax.select_n(me ^ b, *got) for b in range(4)], axis=0).astype(WIDER)


def total_plain(share):
    return lax.psum(share, "pb").astype(WIDER)


def local(
    passages,
    lengths,
    answers,
    cotangent,
    enc_gain1,
    enc_qkv,
    enc_bias,
    enc_out,
    enc_gain2,
    enc_ffn_in,
    enc_ffn_out,
    enc_gain3,
    cross_kv,
    dec_gain1,
    dec_qkv,
    dec_bias,
    dec_out,
    dec_gain2,
    cross_query,
    cross_out,
    dec_gain3,
    dec_ffn_in,
    dec_ffn_out,
):
    pa_size = lax.axis_size("pa")
    pb_size = lax.axis_size("pb")
    fast = pa_size == 8 and pb_size == 4
    me = lax.axis_index("pa").astype(jnp.int32).reshape(1)
    x = passages.reshape(SLOT, D)
    count = lengths.reshape(1)
    table = jnp.transpose(enc_bias)
    dec_table = jnp.transpose(dec_bias)
    pick = jnp.asarray(PICK, LOWER)
    pick_back = jnp.asarray(PICK_BACK, LOWER)

    def across(value):
        return value, swap(value, "pa", 0)

    dec_after, lefts, dec_heads, query, token = dec_self(
        dec_table, answers[0], dec_gain1, dec_gain2, dec_qkv, dec_out, cross_query
    )
    first, heads, mixed, stats, packed, after, second, slope, hidden, final, third, pairs, token = forward(
        count, table, pick, x, enc_gain1, enc_qkv, enc_gain2, enc_gain3, query, enc_out, enc_ffn_in, enc_ffn_out, cross_kv,
        after=[token],
    )
    if fast:
        acts = [across(value) for value in (first, mixed, second, hidden, third)]
    else:
        acts = [both_cores(v, k % 2) for k, v in enumerate((first, mixed, second, hidden, third))]
    gathered = lax.all_gather(packed, "pa")
    answer, early, g_middle, g_gain3, partial, g_enc_gain3, g_pairs, g_final, branch, token = dec_mid(
        count, gathered, dec_after, cotangent[0], dec_gain3, lefts, query, enc_gain3, pairs,
        cross_out, dec_ffn_in, dec_ffn_out, cross_kv, final,
        after=[got for unused, got in acts[:4]],
    )
    early_all = lax.all_gather(early, "pb")
    g_inner, g_after, low, g_mixed, g_enc_gain2, token = ffn_back(
        branch, enc_ffn_out, slope, enc_ffn_in, after, enc_gain2, g_final, enc_out, after=[token]
    )

    def back_of(base, pairs, after):
        return attention_back(count, table, pick, heads, g_mixed, mixed, stats, base, pairs, after=after)

    def dec_end(part, got, token, wait=()):
        return dec_back(
            dec_table, answers[0], part, got, dec_after, g_middle, dec_heads,
            dec_gain1, dec_gain2, g_gain3, cross_query, dec_out, dec_qkv, after=[token, *wait],
        )

    def rows_end(grads, diagonal, token):
        return attention_end(
            count, table, pick, heads, g_mixed, mixed, stats, grads, diagonal, enc_qkv, x, enc_gain1,
            g_after, g_enc_gain2, g_enc_gain3, pick_back, after=[token],
        )

    pb_me = lax.axis_index("pb").astype(jnp.int32).reshape(1)

    def outer_end(token, late_one, late_two):
        *outer, token = dec_outer(pb_me, early_all, late_one, late_two, pb_size, after=[token])
        return outer, token

    if fast:
        partial, token = add_rows(partial, swap(partial, "pa", 0), after=[token])
        got = swap(partial, "pa", 1)
        xk, xs, yk, ys, token = weights_one(me, acts[4], across(g_pairs), acts[3], across(branch), after=[token])
        one = ((xk, swap(xs, "pa", 1)), (yk, swap(ys, "pa", 2)))
        partial, token = add_rows(partial, got, after=[token])
        got = swap(partial, "pa", 2)
        grads, diagonal_a, token = back_of(0, FIRST, [token])
        late, g_start, token = dec_end(partial, got, token)
        late_near = swap(late, "pb", 0)
        send_x, send_y, token = add_first(one, after=[token, early_all])
        last = (swap(send_x, "pa", 2), swap(send_y, "pa", 1))
        xk, xs, yk, ys, token = weights_two(me, acts[2], across(g_inner), acts[1], across(low), after=[token])
        two = ((xk, swap(xs, "pa", 1)), (yk, swap(ys, "pa", 2)))
        share_one, token = add_second([one[0] + last[:1], one[1] + last[1:]], after=[token])
        got_one = inward(share_one)
        late, token = stack_late(late, late_near, after=[token])
        late_far = swap(late, "pb", 1)
        g_rows, small, diagonal_a, grads, token = rows_end(grads, diagonal_a, token)
        there, got_small = swap(grads, "pa", 0), swap(small, "pa", 0)
        send_x, send_y, token = add_first(two, flops=COST[0], after=[token, late_far])
        last = (swap(send_x, "pa", 2), swap(send_y, "pa", 1))
        share_one, token = add_pair(share_one, got_one, flops=COST[1], after=[token])
        got_one = between(share_one)
        xk, xs, yk, ys, token = weights_three(me, acts[0], (grads, there), (small, got_small), after=[token])
        three = ((xk, swap(xs, "pa", 1)), (yk, swap(ys, "pa", 2)))
        share_two, token = add_second([two[0] + last[:1], two[1] + last[1:]], after=[token])
        got_two = inward(share_two)
        share_one, token = add_pair(share_one, got_one, flops=COST[2], after=[token])
        total_one = outward(share_one)
        send_x, send_y, token = add_first(three, after=[token])
        last = (swap(send_x, "pa", 2), swap(send_y, "pa", 1))
        share_two, token = add_pair(share_two, got_two, flops=COST[3], after=[token])
        got_two = between(share_two)
        share_three, token = add_second([three[0] + last[:1], three[1] + last[1:]], side=True, after=[token])
        parts = swap_parts(share_three)
        outer, token = outer_end(token, late, late_far)
        share_two, token = add_pair(share_two, got_two, after=[token])
        total_two = outward(share_two)
        total_three = spread_parts(*add_parts(share_three, parts, pb_me, after=[token, total_one]))
        small = total_three[D // pa_size :, :D]
        block = D // pa_size
        total_kv = jnp.concatenate([total_one[:block], total_one[block : 2 * block]], axis=1)
        total_ffn_out = total_one[2 * block :]
        second_part = 2 * block + block // 2
        total_ffn_in = jnp.concatenate(
            [total_two[first : first + block] for first in (0, block, second_part, second_part + block)], axis=1
        )
        total_out = jnp.concatenate([total_two[2 * block : second_part], total_two[second_part + 2 * block :]], axis=0)
        total_qkv = total_three[:block]
    else:
        partial = all_sum(partial, "pa")
        late, g_start, token = dec_end(partial, jnp.zeros_like(partial), token)
        late, token = stack_late(late, swap(late, "pb", 0), after=[token])
        late_far = swap(late, "pb", 1)
        grads, diagonal_a, token = back_of(0, FIRST, [token])
        g_rows, small, diagonal_a, grads, token = rows_end(grads, diagonal_a, token)
        outer, token = outer_end(token, late, late_far)
        small = all_sum(all_sum(small[:, :D], "pa"), "pb")
        g_heads = jnp.concatenate([grads[0], grads[1], grads[2]], axis=1)
        total_kv = total_plain(share_over_pa(acts[4], across(g_pairs), 0))
        total_ffn_out = total_plain(share_over_pa(acts[3], across(branch), 1))
        total_ffn_in = total_plain(share_over_pa(acts[2], across(g_inner), 0))
        total_out = total_plain(share_over_pa(acts[1], across(low), 1))
        total_qkv = total_plain(share_over_pa(acts[0], across(g_heads), 0))

    d_qkv, d_out, d_query, d_cross, d_in, d_ffn, dec_small = outer
    dec_small = dec_small[0]
    dec_bias_rows = dec_small[3 * D :].reshape(H, STAT)[:, GROUP - ANS : GROUP]
    dec_bias_all = jnp.pad(jnp.transpose(dec_bias_rows[:, ::-1]), ((0, BUCKETS - ANS), (0, 0)))

    def own_part(vector, axis):
        height = vector.shape[0] // lax.axis_size(axis)
        return lax.dynamic_slice_in_dim(vector, lax.axis_index(axis) * height, height, axis=0)

    return (
        answer[None],
        g_rows.reshape(1, 1, SLOT, D),
        g_start[None],
        own_part(small[0], "pa"),
        total_qkv,
        jnp.transpose(small[4:16, :BUCKETS]),
        total_out,
        own_part(small[1], "pa"),
        total_ffn_in,
        total_ffn_out,
        own_part(small[2], "pa"),
        total_kv,
        own_part(dec_small[:D], "pb"),
        d_qkv,
        own_part(dec_bias_all, "pb"),
        d_out,
        own_part(dec_small[D : 2 * D], "pb"),
        d_query,
        d_cross,
        own_part(dec_small[2 * D : 3 * D], "pb"),
        d_in,
        d_ffn,
    )


def solution(mesh):
    copied = P()
    in_specs = (
        P("pb", "pa", None, None),
        P("pb", "pa"),
        P("pb", None, None),
        P("pb", None, None),
    ) + (copied,) * 19
    by_pa, by_pa_rows = P("pa"), P("pa", None)
    by_pb, by_pb_rows = P("pb"), P("pb", None)
    out_specs = (
        P("pb", None, None),
        P("pb", "pa", None, None),
        P("pb", None, None),
        by_pa,
        by_pa_rows,
        copied,
        by_pa_rows,
        by_pa,
        by_pa_rows,
        by_pa_rows,
        by_pa,
        by_pa_rows,
        by_pb,
        by_pb_rows,
        by_pb_rows,
        by_pb_rows,
        by_pb,
        by_pb_rows,
        by_pb_rows,
        by_pb,
        by_pb_rows,
        by_pb_rows,
    )
    return jax.shard_map(local, mesh=mesh, in_specs=in_specs, out_specs=out_specs, check_vma=False)
```

```python
import jax
import jax.numpy as jnp
import numpy as np
from jax import lax
from jax.experimental import pallas as pl
from jax.experimental.pallas import tpu as pltpu
from jax.sharding import PartitionSpec as P

D = 768
H = 12
HD = 64
FF = 3072
BUCKETS = 32
ANS = 20
SLOT = 512
PAIR = 2 * HD
PAIRS = H // 2
EDGE = 128
STRIP = 256
SPAN = 256
GROUP = 24
COST = (4 * 10**9, 0, 4 * 10**9, 0, 4 * 10**9, 4 * 10**9, 4 * 10**9)
STACK = H * GROUP
STAT = 128
STEPS = 4
WIDTH = FF // STEPS
FIRST = 4
EPS = 1e-06
MASKED = -1000000000.0
C_GELU = 0.7978845608028654
LOWER = jnp.bfloat16
WIDER = jnp.float32
EARLY = 7 * D + 2 * FF
LATE = 5 * D
AT = {
    "first": 0,
    "own": D,
    "second": 2 * D,
    "mix": 3 * D,
    "third": 4 * D,
    "hidden": 5 * D,
    "g_middle": 5 * D + FF,
    "g_inner": 6 * D + FF,
    "g_out": 6 * D + 2 * FF,
    "g_heads": 0,
    "g_after": 3 * D,
    "g_query": 4 * D,
}


def tile_classes(away):
    rows = [np.clip(EDGE * d - away, -(BUCKETS // 2), BUCKETS // 2 - 1) + BUCKETS // 2 for d in (-1, 0, 1)]
    return np.eye(BUCKETS, dtype=np.float32)[np.concatenate(rows)]


LANES = np.arange(SPAN)
PICK = tile_classes(np.where(LANES < EDGE, LANES, LANES - SPAN)).T
ENDS = np.repeat(np.eye(BUCKETS, dtype=np.float32)[[0, BUCKETS - 1]], EDGE, axis=0)
PICK_BACK = np.pad(np.concatenate([tile_classes(LANES - (EDGE - 1)), ENDS]), ((0, 0), (0, STAT - BUCKETS)))

SCALARS = pl.BlockSpec(memory_space=pltpu.SMEM)
ANY = pl.BlockSpec(memory_space=pl.ANY)
WHOLE = pl.BlockSpec(memory_space=pltpu.VMEM)
TOKEN = (8, 128)


def wide(*shape):
    return jax.ShapeDtypeStruct(shape, WIDER)


def narrow(*shape):
    return jax.ShapeDtypeStruct(shape, LOWER)


def run(name, body, ins, in_specs, outs, out_specs=None, after=(), grid=(), scratch=(), flops=10**9, mib=63, alias=None):
    count, extra, results = len(ins), len(after), len(outs)
    if out_specs is None:
        out_specs = [WHOLE] * results
    zeros = (lambda *s: (0, 0)) if grid else (lambda: (0, 0))

    def wrapped(*refs):
        refs[count + extra + results][...] = jnp.zeros(TOKEN, WIDER)
        body(*refs[:count], *refs[count + extra : count + extra + results], *refs[count + extra + results + 1 :])

    got = pl.pallas_call(
        wrapped,
        grid=grid,
        out_shape=tuple(outs) + (wide(*TOKEN),),
        in_specs=list(in_specs) + [ANY] * extra,
        out_specs=tuple(out_specs) + (pl.BlockSpec(TOKEN, zeros),),
        scratch_shapes=list(scratch),
        input_output_aliases=alias or {},
        compiler_params=pltpu.CompilerParams(vmem_limit_bytes=mib * 2**20),
        cost_estimate=pl.CostEstimate(flops=10 * flops, bytes_accessed=1, transcendentals=0),
        name=name,
    )(*ins, *after)
    return got


def product(left, right):
    return jnp.dot(left, right, preferred_element_type=WIDER)


def left_product(left, right):
    return lax.dot_general(left, right, (((0,), (0,)), ((), ())), preferred_element_type=WIDER)


def right_product(left, right):
    return lax.dot_general(left, right, (((1,), (1,)), ((), ())), preferred_element_type=WIDER)


def split_product(left, right, terms):
    total = None
    for k in range(terms):
        part = left.astype(LOWER)
        left = left - part.astype(WIDER)
        term = product(part, right)
        total = term if total is None else total + term
    return total


def silu_like(inner):
    square = inner * inner
    tanh = jnp.tanh(inner * (C_GELU + (C_GELU * 0.044715) * square))
    half = 0.5 + 0.5 * tanh
    value = inner * half
    slope = half + value * (1.0 - tanh) * (C_GELU + (3.0 * C_GELU * 0.044715) * square)
    return value, slope


def row_of(ref):
    return ref[...].reshape(1, D)


def scale_of(values):
    return lax.rsqrt(jnp.mean(values * values, axis=-1, keepdims=True) + EPS)


def norm_pull(values, gain, grad):
    scale = scale_of(values)
    lifted = grad * gain
    inside = jnp.sum(values * lifted, axis=-1, keepdims=True)
    back = scale * lifted - values * (scale * scale * scale * inside * (1.0 / D))
    return back, jnp.sum(grad * values * scale, axis=0, keepdims=True)


def fetch(pairs, sems):
    copies = [pltpu.make_async_copy(s, t, sems.at[k]) for k, (s, t) in enumerate(pairs)]
    for copy in copies:
        copy.start()
    return copies


def bias_tiles(u_ref, head):
    tiles = []
    for d in range(3):
        row = u_ref[pl.ds(head, 1), SPAN * d : SPAN * d + SPAN]
        spread = jnp.broadcast_to(row, (EDGE, SPAN))
        tiles.append(pltpu.roll(spread, 0, 1, stride=1, stride_axis=0)[:, :EDGE])
    return tiles


def key_masks(n):
    places = lax.broadcasted_iota(jnp.int32, (EDGE, EDGE), 0)
    return [jnp.where(places + EDGE * j < n, 0.0, MASKED) for j in range(SLOT // EDGE)]


def score_blocks(raw, tiles, masks, low, high, first):
    columns = []
    for c in range(STRIP // EDGE):
        blocks = []
        for j in range(SLOT // EDGE):
            block = raw[EDGE * j : EDGE * j + EDGE, EDGE * c : EDGE * c + EDGE]
            d = j - first - c
            block = block + (tiles[d + 1] if abs(d) <= 1 else (low if d < 0 else high))
            blocks.append(block + masks[j] if j > 0 else block)
        columns.append(blocks)
    return columns


def paved(columns, kind):
    return jnp.concatenate([jnp.concatenate([b.astype(kind) for b in blocks], axis=0) for blocks in columns], axis=1)


def fill_rows(table_ref, pick_ref, u_ref):
    @pl.when(pl.program_id(0) == 0)
    def _():
        u_ref[...] = split_product(table_ref[...], pick_ref[...], 3)


def attn_fwd_kernel(n_ref, ends_ref, table_ref, pick_ref, x_ref, g1_ref, wq_ref, wk_ref, wv_ref, first_ref, heads_ref, o_ref, st_ref, u_ref):
    fill_rows(table_ref, pick_ref, u_ref)
    step = pl.program_id(0)

    @pl.when(step == 0)
    def _():
        rows = x_ref[...].astype(WIDER)
        first_ref[...] = (rows * scale_of(rows) * row_of(g1_ref)).astype(LOWER)

    masks = key_masks(n_ref[0])
    first = first_ref[...]
    for k, w_ref in enumerate((wq_ref, wk_ref, wv_ref)):
        heads_ref[k] = product(first, w_ref[...]).astype(LOWER)
    q_ref, k_ref = heads_ref.at[0], heads_ref.at[1]
    values = jnp.transpose(heads_ref[2])
    ones = jnp.ones((16, SLOT), LOWER)
    mixed = []
    for h in range(2):
        head = 2 * step + h
        low, high = ends_ref[head, 0], ends_ref[head, BUCKETS - 1]
        tiles = bias_tiles(u_ref, head)
        cols = slice(HD * h, HD * h + HD)
        keys = k_ref[:, cols]
        left = jnp.concatenate([values[cols], ones], axis=0)
        strips = []
        for i in range(0, SLOT // EDGE, STRIP // EDGE):
            lanes = slice(EDGE * i, EDGE * i + STRIP)
            raw = right_product(keys, q_ref[lanes, cols] * 0.125)
            tops, powers = [], []
            for blocks in score_blocks(raw, tiles, masks, low, high, i):
                top = jnp.maximum(jnp.maximum(blocks[0], blocks[1]), jnp.maximum(blocks[2], blocks[3]))
                top = jnp.max(top, axis=0, keepdims=True)
                tops.append(top)
                powers.append([jnp.exp(block - top) for block in blocks])
            out = product(left, paved(powers, LOWER))
            total = out[HD : HD + 1]
            st_ref[0, h : h + 1, lanes] = jnp.concatenate(tops, axis=1) + jnp.log(total)
            strips.append(out[:HD] * (1.0 / total))
        mixed.append(jnp.concatenate(strips, axis=1))
    lanes = pl.ds(pl.multiple_of(step * PAIR, PAIR), PAIR)
    o_ref[:, lanes] = jnp.transpose(jnp.concatenate(mixed, axis=0)).astype(LOWER)


def attn_bwd_kernel(base):
    def body(
        n_ref, ends_ref, table_ref, pick_ref, h_ref, g_ref, o_ref, st_ref, gh_ref, gb_ref, u_ref
    ):
        q_ref, k_ref, v_ref = h_ref.at[0], h_ref.at[1], h_ref.at[2]
        fill_rows(table_ref, pick_ref, u_ref)
        step = pl.program_id(0) + base
        masks = key_masks(n_ref[0])
        keys_t = jnp.transpose(k_ref[...])
        rows = lax.broadcasted_iota(jnp.int32, (EDGE, EDGE), 0)
        columns = lax.broadcasted_iota(jnp.int32, (EDGE, EDGE), 1)
        mirror = jnp.where(rows + columns == EDGE - 1, 1.0, 0.0).astype(LOWER)
        rows = lax.broadcasted_iota(jnp.int32, (16, SLOT), 0) * EDGE
        columns = lax.broadcasted_iota(jnp.int32, (16, SLOT), 1)
        places = jnp.where((columns >= rows) & (columns < rows + EDGE), 1.0, 0.0).astype(LOWER)
        rows = lax.broadcasted_iota(jnp.int32, (16, PAIR), 0) * HD
        columns = lax.broadcasted_iota(jnp.int32, (16, PAIR), 1)
        halves = jnp.where((columns >= rows) & (columns < rows + HD), 1.0, 0.0).astype(LOWER)
        met = g_ref[...].astype(WIDER) * o_ref[...].astype(WIDER)
        upper = met.astype(LOWER)
        lower = (met - upper.astype(WIDER)).astype(LOWER)
        weighted = right_product(halves, upper) + right_product(halves, lower)
        grad_queries = []
        gb_ref[0, 2:8, :] = jnp.zeros((6, 4 * SPAN), WIDER)
        for h in range(2):
            head = 2 * step + h
            low, high = ends_ref[head, 0], ends_ref[head, BUCKETS - 1]
            tiles = bias_tiles(u_ref, head)
            cols = slice(HD * h, HD * h + HD)
            keys = k_ref[:, cols]
            values = v_ref[:, cols]
            left = jnp.concatenate([keys_t[cols], places], axis=0)
            grad_keys = jnp.zeros((SLOT, HD), WIDER)
            grad_values = jnp.zeros((SLOT, HD), WIDER)
            strips = []
            sums = {}

            def gather(d, block):
                sums[d] = sums[d] + block if d in sums else block

            for i in range(0, SLOT // EDGE, STRIP // EDGE):
                lanes = slice(EDGE * i, EDGE * i + STRIP)
                query = q_ref[lanes, cols]
                grad = g_ref[lanes, cols]
                raw = right_product(keys, query * 0.125)
                grad_probs = right_product(values, grad)
                probs, changes = [], []
                for c, blocks in enumerate(score_blocks(raw, tiles, masks, low, high, i)):
                    part = slice(EDGE * (i + c), EDGE * (i + c) + EDGE)
                    total = st_ref[0, h : h + 1, part]
                    mean = weighted[h : h + 1, part]
                    probs.append([jnp.exp(block - total) for block in blocks])
                    changes.append([])
                    for j in range(SLOT // EDGE):
                        gap = grad_probs[EDGE * j : EDGE * j + EDGE, EDGE * c : EDGE * c + EDGE] - mean
                        change = probs[c][j] * gap
                        changes[c].append(change)
                        if abs(j - i - c) <= 1:
                            gather(j - i - c, change)
                rounded = paved(changes, LOWER)
                out = product(left, rounded)
                strips.append(out[:HD])
                for c in range(STRIP // EDGE):
                    for j in range(SLOT // EDGE):
                        if abs(j - i - c) > 1:
                            gather(2 if j > i + c else -2, out[HD + j : HD + j + 1, EDGE * c : EDGE * c + EDGE])
                grad_keys += product(rounded, query)
                grad_values += product(paved(probs, LOWER), grad)
            grad_queries.append(jnp.concatenate(strips, axis=1))
            gh_ref[1, :, cols] = (grad_keys * 0.125).astype(LOWER)
            gh_ref[2, :, cols] = grad_values.astype(LOWER)
            empty = jnp.zeros((EDGE, SPAN - EDGE), WIDER)
            band = jnp.concatenate([sums[-1], sums[0], sums[1]], axis=1)
            upper = band.astype(LOWER)
            lower = (band - upper.astype(WIDER)).astype(LOWER)
            mirrored = product(mirror, upper) + product(mirror, lower)
            for d in range(3):
                spread = jnp.concatenate([mirrored[:, EDGE * d : EDGE * d + EDGE], empty], axis=1)
                turned = pltpu.roll(spread, 0, 1, stride=1, stride_axis=0)
                gb_ref[0, h : h + 1, SPAN * d : SPAN * d + SPAN] = jnp.sum(turned, axis=0, keepdims=True)
            for place, d in ((3 * SPAN, -2), (3 * SPAN + EDGE, 2)):
                gb_ref[0, h : h + 1, place : place + EDGE] = sums[d]
        gh_ref[0] = (jnp.transpose(jnp.concatenate(grad_queries, axis=0)) * 0.125).astype(LOWER)

    return body


def columns_at(first):
    return pl.BlockSpec((SLOT, PAIR), lambda s: (0, first + s))


def stats_at(first):
    return pl.BlockSpec((1, 2, SLOT), lambda s: (first + s, 0, 0))


def pair_of_all(base):
    return pl.BlockSpec((3, SLOT, PAIR), lambda s: (0, 0, base + s))


def attention_back(count, table, pick, heads, grad_mixed, mixed, stats, base, half, after=()):
    return run(
        "enc_attention_back",
        attn_bwd_kernel(base),
        [count, table, table, pick, heads, grad_mixed, mixed, stats],
        [SCALARS, SCALARS, WHOLE, WHOLE, pair_of_all(base), columns_at(base), columns_at(base), stats_at(base)],
        [narrow(3, SLOT, D), wide(half, 8, 4 * SPAN)],
        [pair_of_all(base), pl.BlockSpec((1, 8, 4 * SPAN), lambda s: (s, 0, 0))],
        after=after,
        grid=(half,),
        scratch=[pltpu.VMEM((H, 3 * SPAN), WIDER)],
        flops=2 * 5 * H * SLOT * SLOT * HD * 4,
    )


def send_out(pairs, sems, first):
    copies = [pltpu.make_async_copy(s, t, sems.at[first + k]) for k, (s, t) in enumerate(pairs)]
    for copy in copies:
        copy.start()
    return copies


def chunk(k):
    return slice(WIDTH * k, WIDTH * k + WIDTH)


def copy_all(pairs, sems):
    return [pltpu.make_async_copy(s, t, sems.at[k]) for k, (s, t) in enumerate(pairs)]


def forward_kernel(
    n_ref, ends_ref, table_ref, pick_ref, x_ref, g1_ref, wq_ref, wk_ref, wv_ref,
    g2_ref, g3_ref, query_ref, wo_any, in_any, out_any, kv_any,
    first_ref, heads_ref, mixed_ref, st_ref, packed_ref,
    after_any, second_any, slope_any, hidden_any, final_any, third_any, pairs_any,
    u_ref, wo_ref, in_ref, out_ref, kv_ref,
    after_ref, second_ref, slope_ref, hidden_ref, final_ref, third_ref, pairs_ref,
    sems, out_sems,
):
    step = pl.program_id(0)
    pairs = [(wo_any, wo_ref)]
    for k in range(STEPS):
        pairs += [(in_any.at[:, chunk(k)], in_ref.at[k]), (out_any.at[chunk(k)], out_ref.at[k])]
    copies = copy_all(pairs + [(kv_any, kv_ref)], sems)

    @pl.when(step == 0)
    def _():
        for copy in copies:
            copy.start()

    attn_fwd_kernel(
        n_ref, ends_ref, table_ref, pick_ref, x_ref, g1_ref, wq_ref, wk_ref, wv_ref,
        first_ref, heads_ref, mixed_ref, st_ref, u_ref,
    )

    @pl.when(step == PAIRS - 1)
    def _():
        for copy in copies:
            copy.wait()
        after = x_ref[...].astype(WIDER) + product(mixed_ref[...], wo_ref[...])
        after_ref[...] = after
        second = (after * scale_of(after) * row_of(g2_ref)).astype(LOWER)
        second_ref[...] = second
        inner = product(second, in_ref[0])
        sent = send_out([(after_ref, after_any), (second_ref, second_any)], out_sems, 0)
        total = after
        for k in range(STEPS):
            following = product(second, in_ref[k + 1]) if k + 1 < STEPS else None
            value, slope = silu_like(inner)
            slope_ref[:, chunk(k)] = slope.astype(LOWER)
            hidden = value.astype(LOWER)
            hidden_ref[:, chunk(k)] = hidden
            total = total + product(hidden, out_ref[k])
            inner = following
            if k % 2:
                half = slice(WIDTH * (k - 1), WIDTH * (k + 1))
                sent += send_out(
                    [(slope_ref.at[:, half], slope_any.at[:, half]), (hidden_ref.at[:, half], hidden_any.at[:, half])],
                    out_sems, len(sent),
                )
        final_ref[...] = total
        third = (total * scale_of(total) * row_of(g3_ref)).astype(LOWER)
        third_ref[...] = third
        sent += send_out([(final_ref, final_any), (third_ref, third_any)], out_sems, len(sent))
        for k in range(2):
            half = slice(D * k, D * k + D)
            pairs_ref[:, half] = product(third, kv_ref[:, half]).astype(LOWER)
        sent += send_out([(pairs_ref, pairs_any)], out_sems, len(sent))
        cross_kernel(n_ref, query_ref, pairs_ref, packed_ref)
        for copy in sent:
            copy.wait()


def whole(*shape):
    return pl.BlockSpec(shape, lambda s: (0,) * len(shape))


def forward(count, table, pick, x, gain1, qkv, gain2, gain3, query, wo, ffn_in, ffn_out, kv, after=()):
    def weights_at(first):
        return pl.BlockSpec((D, PAIR), lambda s: (0, first + s))

    kept = [wide(SLOT, D), narrow(SLOT, D), narrow(SLOT, FF), narrow(SLOT, FF), wide(SLOT, D), narrow(SLOT, D), narrow(SLOT, 2 * D)]
    return run(
        "enc_forward",
        forward_kernel,
        [count, table, table, pick, x, gain1, qkv, qkv, qkv, gain2, gain3, query, wo, ffn_in, ffn_out, kv],
        [SCALARS, SCALARS, WHOLE, WHOLE, whole(SLOT, D), whole(D), weights_at(0), weights_at(PAIRS), weights_at(2 * PAIRS)]
        + [whole(D), whole(D), whole(GROUP, D)] + [ANY] * 4,
        [narrow(SLOT, D), narrow(3, SLOT, D), narrow(SLOT, D), wide(PAIRS, 2, SLOT), wide(GROUP, D + STAT)] + kept,
        [whole(SLOT, D), pair_of_all(0), whole(SLOT, D), stats_at(0), whole(GROUP, D + STAT)] + [ANY] * 7,
        after=after,
        grid=(PAIRS,),
        scratch=[
            pltpu.VMEM((H, 3 * SPAN), WIDER),
            pltpu.VMEM((D, D), LOWER),
            pltpu.VMEM((STEPS, D, WIDTH), LOWER),
            pltpu.VMEM((STEPS, WIDTH, D), LOWER),
            pltpu.VMEM((D, 2 * D), LOWER),
        ]
        + [pltpu.VMEM(out.shape, out.dtype) for out in kept]
        + [pltpu.SemaphoreType.DMA((2 * STEPS + 2,)), pltpu.SemaphoreType.DMA((9,))],
        flops=2 * SLOT * D * (D + 2 * FF + 2 * D),
    )


def ffn_back_kernel(
    branch_ref, g2_ref, gfinal_any, after_any, slope_any, out_any, in_any, wo_any,
    ginner_any, gafter_any, low_any, gmixed_any, gain_ref,
    gfinal_ref, after_ref, slope_ref, out_ref, in_ref, wo_ref, ginner_ref, gafter_ref, low_ref, gmixed_ref,
    sems, out_sems,
):
    pairs = []
    for k in range(STEPS):
        pairs += [(out_any.at[chunk(k)], out_ref.at[k]), (slope_any.at[:, chunk(k)], slope_ref.at[k])]
        pairs += [(in_any.at[:, chunk(k)], in_ref.at[k])]
    copies = fetch(pairs + [(after_any, after_ref), (gfinal_any, gfinal_ref), (wo_any, wo_ref)], sems)
    branch = branch_ref[...]
    copies[0].wait()
    grad = right_product(branch, out_ref[0])
    total = None
    sent = []
    for k in range(STEPS):
        copies[3 * k + 1].wait()
        copies[3 * k + 2].wait()
        copies[3 * k + 3].wait()
        following = right_product(branch, out_ref[k + 1]) if k + 1 < STEPS else None
        inner = (grad * slope_ref[k].astype(WIDER)).astype(LOWER)
        ginner_ref[:, chunk(k)] = inner
        term = right_product(inner, in_ref[k])
        total = term if total is None else total + term
        grad = following
        sent += send_out([(ginner_ref.at[:, chunk(k)], ginner_any.at[:, chunk(k)])], out_sems, len(sent))
    copies[3 * STEPS + 1].wait()
    copies[3 * STEPS + 2].wait()
    back, gain = norm_pull(after_ref[...], row_of(g2_ref), total)
    gain_ref[...] = gain
    g_after = gfinal_ref[...] + back
    gafter_ref[...] = g_after
    low = g_after.astype(LOWER)
    low_ref[...] = low
    sent += send_out([(gafter_ref, gafter_any), (low_ref, low_any)], out_sems, len(sent))
    gmixed_ref[...] = right_product(low, wo_ref[...]).astype(LOWER)
    sent += send_out([(gmixed_ref, gmixed_any)], out_sems, len(sent))
    for copy in sent:
        copy.wait()


def ffn_back(branch, ffn_out, slope, ffn_in, after_rows, gain2, g_final, wo, after=()):
    outs = [narrow(SLOT, FF), wide(SLOT, D), narrow(SLOT, D), narrow(SLOT, D)]
    return run(
        "enc_ffn_back",
        ffn_back_kernel,
        [branch, gain2, g_final, after_rows, slope, ffn_out, ffn_in, wo],
        [WHOLE] * 2 + [ANY] * 6,
        outs + [wide(1, D)],
        [ANY] * 4 + [WHOLE],
        after=after,
        scratch=[
            pltpu.VMEM((SLOT, D), WIDER),
            pltpu.VMEM((SLOT, D), WIDER),
            pltpu.VMEM((STEPS, SLOT, WIDTH), LOWER),
            pltpu.VMEM((STEPS, WIDTH, D), LOWER),
            pltpu.VMEM((STEPS, D, WIDTH), LOWER),
            pltpu.VMEM((D, D), LOWER),
        ]
        + [pltpu.VMEM(out.shape, out.dtype) for out in outs]
        + [pltpu.SemaphoreType.DMA((3 * STEPS + 3,)), pltpu.SemaphoreType.DMA((STEPS + 3,))],
        flops=2 * SLOT * D * (D + 2 * FF),
    )


def attention_end(
    count, table, pick, heads, grad_mixed, mixed, stats, begun, diagonal, qkv, x, gain1,
    g_after, gain2, gain3, pick_back, after=(),
):
    base = FIRST
    half = PAIRS - FIRST
    inner = attn_bwd_kernel(base)

    def body(
        n_ref, ends_ref, table_ref, pick_ref, h_ref, g_ref, o_ref, st_ref, begun_any,
        da_ref, x_ref, g1_ref, gain2_ref, gain3_ref, back_ref, qkv_any, gafter_any,
        gh_any, small_ref, gb_ref, grows_any,
        u_ref, gh_ref, gall_ref, w_ref, gafter_ref, grows_ref, sems, out_sems,
    ):
        step = pl.program_id(0)
        old = slice(0, base * PAIR)
        loads = copy_all([(begun_any.at[:, :, old], gall_ref.at[:, :, old]), (qkv_any, w_ref), (gafter_any, gafter_ref)], sems)

        @pl.when(step == 0)
        def _():
            for load in loads:
                load.start()

        inner(n_ref, ends_ref, table_ref, pick_ref, h_ref, g_ref, o_ref, st_ref, gh_ref, gb_ref, u_ref)
        for k in range(half):

            @pl.when(step == k)
            def _():
                place = slice((base + k) * PAIR, (base + k + 1) * PAIR)
                gall_ref[:, :, place] = gh_ref[...]
                sums_ref = gb_ref.at[0]
                small_ref[2 * k : 2 * k + 2] = sums_ref[:2]

        @pl.when(step == half - 1)
        def _():
            new = slice(base * PAIR, D)
            sent = send_out([(gall_ref.at[:, :, new], gh_any.at[:, :, new])], out_sems, 0)
            for load in loads:
                load.wait()
            total = right_product(gall_ref[0], w_ref[:, :D])
            total = total + right_product(gall_ref[1], w_ref[:, D : 2 * D])
            total = total + right_product(gall_ref[2], w_ref[:, 2 * D :])
            back, gain = norm_pull(x_ref[...].astype(WIDER), row_of(g1_ref), total)
            grows_ref[...] = gafter_ref[...] + back
            sent += send_out([(grows_ref, grows_any)], out_sems, 1)
            sums = [da_ref[k, :2] for k in range(base)]
            sums += [small_ref[2 * k : 2 * k + 2] for k in range(half)]
            found = split_product(jnp.concatenate(sums, axis=0), back_ref[...], 2)
            small_ref[...] = jnp.zeros((16, D + 2 * EDGE), WIDER)
            small_ref[0:1, :D] = gain
            small_ref[1:2, :D] = gain2_ref[...]
            small_ref[2:3, :D] = gain3_ref[...]
            small_ref[4:16, :STAT] = found
            for copy in sent:
                copy.wait()

    rows = whole(SLOT, D)
    grads, small, unused, g_rows, token = run(
        "enc_attention_end",
        body,
        [count, table, table, pick, heads, grad_mixed, mixed, stats, begun]
        + [diagonal, x, gain1, gain2, gain3, pick_back, qkv, g_after],
        [SCALARS, SCALARS, WHOLE, WHOLE, pair_of_all(base), columns_at(base), columns_at(base), stats_at(base), ANY]
        + [whole(*diagonal.shape), rows, whole(D), whole(1, D), whole(1, D), whole(4 * SPAN, STAT), ANY, ANY],
        [narrow(3, SLOT, D), wide(16, D + 2 * EDGE), wide(half, 8, 4 * SPAN), wide(SLOT, D)],
        [ANY, whole(16, D + 2 * EDGE), pl.BlockSpec((1, 8, 4 * SPAN), lambda s: (s, 0, 0)), ANY],
        after=after,
        grid=(half,),
        scratch=[
            pltpu.VMEM((H, 3 * SPAN), WIDER),
            pltpu.VMEM((3, SLOT, PAIR), LOWER),
            pltpu.VMEM((3, SLOT, D), LOWER),
            pltpu.VMEM((D, 3 * D), LOWER),
            pltpu.VMEM((SLOT, D), WIDER),
            pltpu.VMEM((SLOT, D), WIDER),
            pltpu.SemaphoreType.DMA((3,)),
            pltpu.SemaphoreType.DMA((2,)),
        ],
        flops=2 * 5 * H * SLOT * SLOT * HD * 4,
        alias={8: 0},
    )
    return g_rows, small, unused, grads, token


def head_lanes(h):
    lanes = lax.broadcasted_iota(jnp.int32, (GROUP, D), 1)
    return (lanes >= h * HD) & (lanes < (h + 1) * HD)


def stack_heads(flat):
    return jnp.concatenate([jnp.where(head_lanes(h), flat, 0.0) for h in range(H)], axis=0)


def merge_heads(stacked):
    total = jnp.zeros((GROUP, D), WIDER)
    for h in range(H):
        total = total + jnp.where(head_lanes(h), stacked[GROUP * h : GROUP * h + GROUP], 0.0)
    return total


def lanes_to_column(stat):
    lanes = lax.broadcasted_iota(jnp.int32, (GROUP, STAT), 1)
    parts = [jnp.sum(jnp.where(lanes == h, stat, 0.0), axis=1, keepdims=True) for h in range(H)]
    return jnp.concatenate(parts, axis=0)


def column_to_lanes(column, first):
    lanes = lax.broadcasted_iota(jnp.int32, (GROUP, STAT), 1)
    total = jnp.zeros((GROUP, STAT), WIDER)
    for h in range(H):
        total = total + jnp.where(lanes == first + h, column[GROUP * h : GROUP * h + GROUP], 0.0)
    return total


def spread_heads(stat):
    rows = lax.broadcasted_iota(jnp.int32, (STAT, D), 0) * HD
    lanes = lax.broadcasted_iota(jnp.int32, (STAT, D), 1)
    spread = jnp.where((lanes >= rows) & (lanes < rows + HD), 1.0, 0.0).astype(LOWER)
    return split_product(stat, spread, 2)


def own_scores(query, keys, table_ref):
    raw = right_product(query, keys)
    rows = lax.broadcasted_iota(jnp.int32, (GROUP, GROUP), 0)
    columns = lax.broadcasted_iota(jnp.int32, (GROUP, GROUP), 1)
    away = rows - columns
    parts = []
    for h in range(H):
        bias = jnp.full((GROUP, GROUP), table_ref[h, 0], WIDER)
        for d in range(1, GROUP):
            bias = jnp.where(away == d, table_ref[h, d], bias)
        part = raw[GROUP * h : GROUP * h + GROUP] + bias
        parts.append(jnp.where(away >= 0, part, MASKED))
    scores = jnp.concatenate(parts, axis=0)
    powers = jnp.exp(scores - jnp.max(scores, axis=1, keepdims=True))
    return powers / jnp.sum(powers, axis=1, keepdims=True)


def padded(ref, pad_ref):
    pad_ref[...] = jnp.zeros((GROUP, D), WIDER)
    pad_ref[:ANS] = ref[...].astype(WIDER)
    return pad_ref[...]


def answer_rows(width):
    return lax.broadcasted_iota(jnp.int32, (GROUP, width), 0) < ANS


def dec_self_kernel(
    table_ref, x_ref, g1_ref, g2_ref, qkv_any, out_any, query_any,
    after_ref, lefts_ref, heads_ref, query_ref,
    qkv_ref, out_ref, cross_ref, pad_ref, sems,
):
    copies = fetch(((qkv_any, qkv_ref), (out_any, out_ref), (query_any, cross_ref)), sems)
    start = padded(x_ref, pad_ref)
    first = (start * scale_of(start) * row_of(g1_ref)).astype(LOWER)
    copies[0].wait()
    heads = product(first, qkv_ref[...]).astype(LOWER)
    heads_ref[...] = heads
    query = stack_heads(heads.astype(WIDER)[:, :D] * 0.125).astype(LOWER)
    probs = own_scores(query, heads[:, D : 2 * D], table_ref)
    own = merge_heads(product(probs.astype(LOWER), heads[:, 2 * D :]))
    own = jnp.where(answer_rows(D), own, 0.0).astype(LOWER)
    copies[1].wait()
    after = start + product(own, out_ref[...])
    after_ref[...] = after
    second = (after * scale_of(after) * row_of(g2_ref)).astype(LOWER)
    copies[2].wait()
    query_ref[...] = product(second, cross_ref[...]).astype(LOWER)
    lefts_ref[:, :D] = first
    lefts_ref[:, D : 2 * D] = own
    lefts_ref[:, 2 * D :] = second


def masked_cross(n_ref, query_ref, pairs_ref):
    query = stack_heads(query_ref[...].astype(WIDER) * 0.125).astype(LOWER)
    raw = right_product(query, pairs_ref[:, :D])
    places = lax.broadcasted_iota(jnp.int32, (STACK, SLOT), 1)
    return query, jnp.where(places < n_ref[0], raw, MASKED)


def cross_kernel(n_ref, query_ref, pairs_ref, packed_ref):
    unused, scores = masked_cross(n_ref, query_ref, pairs_ref)
    top = jnp.max(scores, axis=1, keepdims=True)
    powers = jnp.exp(scores - top)
    total = jnp.sum(powers, axis=1, keepdims=True)
    probs = (powers / total).astype(LOWER)
    packed_ref[:, :D] = merge_heads(product(probs, pairs_ref[:, D:]))
    packed_ref[:, D:] = column_to_lanes(top, 0) + column_to_lanes(total, STAT // 2)


def dec_mid_kernel(
    n_ref, parts_ref, after_ref, cot_ref, g3_ref, lefts_ref, query_ref, e3_ref,
    pairs_any, cross_any, in_any, out_any, kv_any, final_any,
    answer_ref, early_ref, gmid_ref, gain_ref, partial_ref, gain_enc_ref, gpairs_any, gfinal_any, branch_any,
    pairs_ref, cross_ref, in_ref, out_ref, kv_ref, final_ref, gpairs_ref, gfinal_ref, branch_ref, pad_ref,
    sems, out_sems,
):
    held_pairs = ((cross_any, cross_ref), (in_any, in_ref), (out_any, out_ref), (pairs_any, pairs_ref))
    copies = fetch(held_pairs + ((kv_any, kv_ref), (final_any, final_ref)), sems)
    size = parts_ref.shape[0]
    used = lax.broadcasted_iota(jnp.int32, (GROUP, STAT), 1) < H
    tops = [parts_ref[k, :, D:] for k in range(size)]
    totals = [pltpu.roll(stat, STAT // 2, 1) for stat in tops]
    top = tops[0]
    for k in range(1, size):
        top = jnp.maximum(top, tops[k])
    weights = [jnp.where(used, totals[k] * jnp.exp(tops[k] - top), 0.0) for k in range(size)]
    total = weights[0]
    for k in range(1, size):
        total = total + weights[k]
    total = jnp.where(used, total, 1.0)
    mix = jnp.zeros((GROUP, D), WIDER)
    for k in range(size):
        mix = mix + parts_ref[k, :, :D] * spread_heads(weights[k] / total)
    mix_low = mix.astype(LOWER)
    copies[0].wait()
    middle = after_ref[...] + product(mix_low, cross_ref[...])
    third = (middle * scale_of(middle) * row_of(g3_ref)).astype(LOWER)
    copies[1].wait()
    inner = product(third, in_ref[...])
    value, slope = silu_like(inner)
    hidden = value.astype(LOWER)
    copies[2].wait()
    answer = (middle + product(hidden, out_ref[...])).astype(LOWER)
    answer_ref[...] = answer[:ANS]
    grad = padded(cot_ref, pad_ref)
    out_low = grad.astype(LOWER)
    g_inner = (right_product(out_low, out_ref[...]) * slope).astype(LOWER)
    back, gain = norm_pull(middle, row_of(g3_ref), right_product(g_inner, in_ref[...]))
    gain_ref[...] = gain
    g_middle = grad + back
    gmid_ref[...] = g_middle
    middle_low = g_middle.astype(LOWER)
    g_mix = right_product(middle_low, cross_ref[...]).astype(LOWER)

    def store(name, rows):
        early_ref[:, AT[name] : AT[name] + rows.shape[1]] = rows

    def kept(rows):
        return jnp.where(answer_rows(rows.shape[1]), rows.astype(WIDER), 0.0).astype(LOWER)

    early_ref[:, : 3 * D] = kept(lefts_ref[...])
    store("mix", kept(mix_low))
    store("third", kept(third))
    store("hidden", kept(hidden))
    store("g_middle", middle_low)
    store("g_inner", g_inner)
    store("g_out", out_low)
    copies[3].wait()
    copies[4].wait()
    copies[5].wait()
    query, scores = masked_cross(n_ref, query_ref, pairs_ref)
    probs = jnp.exp(scores - lanes_to_column(jnp.where(used, top, 0.0))) / lanes_to_column(total)
    grad = stack_heads(g_mix.astype(WIDER))
    weighted = jnp.sum(grad * jnp.concatenate([mix] * H, axis=0), axis=1, keepdims=True)
    grad = grad.astype(LOWER)
    grad_probs = right_product(grad, pairs_ref[:, D:])
    rounded = (probs * (grad_probs - weighted)).astype(LOWER)
    g_keys = left_product(rounded, query).astype(LOWER)
    g_values = left_product(probs.astype(LOWER), grad).astype(LOWER)
    gpairs_ref[:, :D] = g_keys
    gpairs_ref[:, D:] = g_values
    sent = send_out([(gpairs_ref, gpairs_any)], out_sems, 0)
    partial_ref[...] = merge_heads(product(rounded, pairs_ref[:, :D])) * 0.125
    g_third = right_product(g_keys, kv_ref[:, :D]) + right_product(g_values, kv_ref[:, D:])
    back, gain = norm_pull(final_ref[...], row_of(e3_ref), g_third)
    gain_enc_ref[...] = gain
    gfinal_ref[...] = back
    branch_ref[...] = back.astype(LOWER)
    sent += send_out([(gfinal_ref, gfinal_any), (branch_ref, branch_any)], out_sems, 1)
    for copy in sent:
        copy.wait()


def dec_back_kernel(
    table_ref, x_ref, part_ref, got_ref, after_ref, gmid_ref, heads_ref,
    g1_ref, g2_ref, gain3_ref, query_any, out_any, qkv_any,
    late_ref, gstart_ref,
    cross_ref, out_ref, qkv_ref, pad_ref, sems,
):
    copies = fetch(((query_any, cross_ref), (out_any, out_ref), (qkv_any, qkv_ref)), sems)
    g_query = (part_ref[...] + got_ref[...]).astype(LOWER)
    copies[0].wait()
    back, gain2 = norm_pull(after_ref[...], row_of(g2_ref), right_product(g_query, cross_ref[...]))
    g_after = gmid_ref[...] + back
    after_low = g_after.astype(LOWER)
    copies[1].wait()
    g_own = stack_heads(right_product(after_low, out_ref[...])).astype(LOWER)
    heads = heads_ref[...]
    query = stack_heads(heads.astype(WIDER)[:, :D] * 0.125).astype(LOWER)
    probs = own_scores(query, heads[:, D : 2 * D], table_ref)
    grad_probs = right_product(g_own, heads[:, 2 * D :])
    rounded = (probs * (grad_probs - jnp.sum(probs * grad_probs, axis=1, keepdims=True))).astype(LOWER)
    g_q = (merge_heads(product(rounded, heads[:, D : 2 * D])) * 0.125).astype(LOWER)
    g_k = left_product(rounded, query).astype(LOWER)
    g_v = left_product(probs.astype(LOWER), g_own).astype(LOWER)
    g_heads = jnp.concatenate([g_q, g_k, g_v], axis=1)
    copies[2].wait()
    start = padded(x_ref, pad_ref)
    back, gain1 = norm_pull(start, row_of(g1_ref), right_product(g_heads, qkv_ref[...]))
    gstart_ref[...] = (g_after + back)[:ANS]
    spread = rounded.astype(WIDER)
    rows = lax.broadcasted_iota(jnp.int32, (GROUP, GROUP), 0)
    columns = lax.broadcasted_iota(jnp.int32, (GROUP, GROUP), 1)
    mirror = jnp.where(rows + columns == GROUP - 1, 1.0, 0.0).astype(LOWER)
    empty = jnp.zeros((GROUP, STAT - GROUP), WIDER)
    tables = []
    for h in range(H):
        part = product(mirror, spread[GROUP * h : GROUP * h + GROUP].astype(LOWER))
        turned = pltpu.roll(jnp.concatenate([part, empty], axis=1), 0, 1, stride=1, stride_axis=0)
        tables.append(jnp.sum(turned, axis=0, keepdims=True))
    small = jnp.concatenate([gain1, gain2, gain3_ref[...]] + tables, axis=1)
    places = lax.broadcasted_iota(jnp.int32, (GROUP, LATE), 0)
    late = jnp.concatenate([g_heads, after_low, g_query], axis=1).astype(WIDER)
    late_ref[...] = jnp.where(places == ANS, small, late).astype(LOWER)


def dec_outer_kernel(size):
    part = D // size

    def body(me_ref, *refs):
        me = me_ref[0]
        small_ref = refs[9]
        there, here = refs[3:9], refs[10:16]
        early_ref, late_ref, sems = refs[16:]
        sent = []
        early_ref[...] = jnp.concatenate([refs[0][me ^ s].astype(WIDER) for s in range(size)], axis=0).astype(LOWER)
        late = [ref[...].astype(WIDER) for ref in refs[1:3]]
        late_ref[...] = jnp.concatenate(late, axis=0).astype(LOWER)
        rows = lax.broadcasted_iota(jnp.int32, (part, D), 0) + me * part
        lanes = lax.broadcasted_iota(jnp.int32, (part, D), 1)
        picked = jnp.where(rows == lanes, 1.0, 0.0).astype(LOWER)
        height = FF // size
        first = pl.multiple_of(AT["hidden"] + me * height, 128)

        def outer(k, name, right):
            left = right_product(picked, early_ref[:, AT[name] : AT[name] + D]).astype(LOWER)
            here[k][...] = product(left, right)
            sent.extend(send_out([(here[k], there[k])], sems, len(sent)))

        outer(4, "third", early_ref[:, AT["g_inner"] : AT["g_inner"] + FF])
        outer(0, "first", late_ref[:, : 3 * D])
        here[5][...] = left_product(early_ref[:, pl.ds(first, height)], early_ref[:, AT["g_out"] : AT["g_out"] + D])
        sent.extend(send_out([(here[5], there[5])], sems, len(sent)))
        outer(1, "own", late_ref[:, AT["g_after"] : AT["g_after"] + D])
        outer(2, "second", late_ref[:, AT["g_query"] : AT["g_query"] + D])
        outer(3, "mix", early_ref[:, AT["g_middle"] : AT["g_middle"] + D])
        total = jnp.zeros((1, LATE), WIDER)
        for part_late in late:
            for k in (0, GROUP):
                total = total + part_late[k + ANS : k + ANS + 1]
        small_ref[...] = total
        for copy in sent:
            copy.wait()

    return body


def held(*shapes):
    return [pltpu.VMEM(shape, LOWER) for shape in shapes] + [
        pltpu.VMEM((GROUP, D), WIDER),
        pltpu.SemaphoreType.DMA((len(shapes),)),
    ]


def dec_self(table, answers, gain1, gain2, qkv, out, query, after=()):
    return run(
        "dec_self",
        dec_self_kernel,
        [table, answers, gain1, gain2, qkv, out, query],
        [SCALARS] + [WHOLE] * 3 + [ANY] * 3,
        [wide(GROUP, D), narrow(GROUP, 3 * D), narrow(GROUP, 3 * D), narrow(GROUP, D)],
        after=after,
        scratch=held((D, 3 * D), (D, D), (D, D)),
        flops=10**9,
    )


def dec_mid(count, parts, after_rows, cotangent, gain3, lefts, query, enc_gain3, pairs, cross_out, ffn_in, ffn_out, kv, final, after=()):
    outs = [narrow(SLOT, 2 * D), wide(SLOT, D), narrow(SLOT, D)]
    shapes = [(SLOT, 2 * D), (D, D), (D, FF), (FF, D), (D, 2 * D)]
    return run(
        "dec_mid",
        dec_mid_kernel,
        [count, parts, after_rows, cotangent, gain3, lefts, query, enc_gain3, pairs, cross_out, ffn_in, ffn_out, kv, final],
        [SCALARS] + [WHOLE] * 7 + [ANY] * 6,
        [narrow(ANS, D), narrow(GROUP, EARLY), wide(GROUP, D), wide(1, D), wide(GROUP, D), wide(1, D)] + outs,
        [WHOLE] * 6 + [ANY] * 3,
        after=after,
        scratch=[pltpu.VMEM(shape, LOWER) for shape in shapes]
        + [pltpu.VMEM((SLOT, D), WIDER)]
        + [pltpu.VMEM(out.shape, out.dtype) for out in outs]
        + [pltpu.VMEM((GROUP, D), WIDER), pltpu.SemaphoreType.DMA((6,)), pltpu.SemaphoreType.DMA((3,))],
        flops=4 * 10**9,
    )


def dec_back(table, answers, part, got, after_rows, g_middle, heads, gain1, gain2, g_gain3, query, out, qkv, after=()):
    return run(
        "dec_back",
        dec_back_kernel,
        [table, answers, part, got, after_rows, g_middle, heads, gain1, gain2, g_gain3, query, out, qkv],
        [SCALARS] + [WHOLE] * 9 + [ANY] * 3,
        [narrow(GROUP, LATE), wide(ANS, D)],
        after=after,
        scratch=held((D, D), (D, D), (D, 3 * D)),
        flops=0,
    )


def dec_outer(me, early, late_one, late_two, size, after=()):
    part = D // size
    outs = [wide(part, 3 * D), wide(part, D), wide(part, D), wide(part, D), wide(part, FF), wide(FF // size, D)]
    return run(
        "dec_outer",
        dec_outer_kernel(size),
        [me, early, late_one, late_two],
        [SCALARS, WHOLE, WHOLE, WHOLE],
        outs + [wide(1, LATE)],
        [ANY] * 6 + [WHOLE],
        after=after,
        scratch=[pltpu.VMEM(out.shape, WIDER) for out in outs]
        + [pltpu.VMEM((size * GROUP, EARLY), LOWER), pltpu.VMEM((size * GROUP, LATE), LOWER), pltpu.SemaphoreType.DMA((6,))],
        flops=8 * 10**9,
    )


def stack_late(one, two, after=()):
    def body(one_ref, two_ref, out_ref):
        out_ref[...] = jnp.concatenate([one_ref[...].astype(WIDER), two_ref[...].astype(WIDER)], axis=0).astype(LOWER)

    return run("stack_late", body, [one, two], [WHOLE] * 2, [narrow(2 * GROUP, LATE)], after=after, flops=0)


PLACES = [(0, 0), (0, 1), (1, 0), (1, 1)]


def place_of(me, there):
    return me ^ (4 * there[0] + 2 * there[1])


def turned_rows(me, acts, block):
    lanes = lax.broadcasted_iota(jnp.int32, (block, D), 1)
    rows = lax.broadcasted_iota(jnp.int32, (block, D), 0)
    picked = [jnp.where(lanes - rows == place_of(me, t) * block, 1.0, 0.0).astype(LOWER) for t in PLACES]
    picked = jnp.concatenate(picked, axis=0)
    return jnp.concatenate([right_product(picked, act).astype(LOWER) for act in acts], axis=1)


def target(there, x_refs, y_refs):
    dy, dx = there
    return (x_refs[dx].at[dy], y_refs[dy].at[dx])


def pages_out(pairs, sems, first):
    return send_out([(here.at[k], there.at[k]) for here, there in pairs for k in range(2)], sems, first)


def one_kernel(
    me_ref, t_own, t_par, p_own, p_par, h_own, h_par, b_own, b_par, xk_any, xs_any, yk_any, ys_any,
    xk, xs, yk, ys, t, p, h, b, sems, out_sems,
):
    me = me_ref[0]
    block = FF // 8
    pairs = [(t_own, t.at[0]), (t_par, t.at[1]), (p_own, p.at[:SLOT]), (p_par, p.at[SLOT:])]
    pairs += [(b_own, b.at[:SLOT]), (b_par, b.at[SLOT:])]
    for k, there in enumerate(PLACES):
        lanes = pl.ds(pl.multiple_of(place_of(me, there) * block, 128), block)
        pairs += [(h_own.at[:, lanes], h.at[k, :SLOT]), (h_par.at[:, lanes], h.at[k, SLOT:])]
    copies = fetch(pairs, sems)
    copies[0].wait()
    copies[1].wait()
    height = D // 8
    left = turned_rows(me, (t[0], t[1]), height)
    for k in range(2, 8):
        copies[k].wait()
    for c in range(2):
        grad = product(left, p[:, D * c : D * c + D]).astype(LOWER)
        for k, there in enumerate(PLACES):
            to, unused = target(there, (xk, xs), (yk, ys))
            to[height * c : height * c + height] = grad[height * k : height * k + height]
    sent = []
    for k, there in enumerate(PLACES):
        grad = left_product(h[k], b[...]).astype(LOWER)
        to_x, to_y = target(there, (xk, xs), (yk, ys))
        to_x[2 * height : 3 * height] = grad[:height]
        to_y[...] = grad[height:]
        out_x, out_y = target(there, (xk_any, xs_any), (yk_any, ys_any))
        if k + 1 < len(PLACES):
            copies[8 + 2 * k].wait()
            copies[9 + 2 * k].wait()
        sent += send_out([(to_x, out_x), (to_y, out_y)], out_sems, len(sent))
    for copy in sent:
        copy.wait()


def two_kernel(
    me_ref, s_own, s_par, i_own, i_par, m_own, m_par, l_own, l_par, xk_any, xs_any, yk_any, ys_any,
    xk, xs, yk, ys, s, i, m, l, sems, out_sems,
):
    me = me_ref[0]
    pairs = [(s_own, s.at[0]), (s_par, s.at[1]), (m_own, m.at[0]), (m_par, m.at[1])]
    pairs += [(l_own, l.at[:SLOT]), (l_par, l.at[SLOT:])]
    for c in range(4):
        lanes = slice(D * c, D * c + D)
        pairs += [(i_own.at[:, lanes], i.at[c, :SLOT]), (i_par.at[:, lanes], i.at[c, SLOT:])]
    copies = fetch(pairs, sems)
    for k in range(6):
        copies[k].wait()
    height = D // 8
    half = height // 2
    left = turned_rows(me, (m[0], m[1]), height)
    turned = turned_rows(me, (s[0], s[1]), height)
    grad = product(left, l[...]).astype(LOWER)
    for k, there in enumerate(PLACES):
        for to, first in zip(target(there, (xk, xs), (yk, ys)), (0, half)):
            to[2 * height : 2 * height + half] = grad[height * k + first : height * k + first + half]
    sent = []
    for c in range(4):
        if c % 2 == 0:
            for k in range(6 + 2 * c, 10 + 2 * c):
                copies[k].wait()
        grad = product(turned, i[c]).astype(LOWER)
        for k, there in enumerate(PLACES):
            to = target(there, (xk, xs), (yk, ys))[c // 2]
            to[height * (c % 2) : height * (c % 2) + height] = grad[height * k : height * k + height]
        if c % 2:
            done = ((xk, xk_any), (xs, xs_any)) if c == 1 else ((yk, yk_any), (ys, ys_any))
            sent += pages_out(done, out_sems, len(sent))
    for copy in sent:
        copy.wait()


def three_kernel(
    me_ref, f_own, f_par, g_own, g_par, small_ref, got_ref, xk_any, xs_any, yk_any, ys_any,
    xk, xs, yk, ys, f, g, sems, out_sems,
):
    me = me_ref[0]
    small = (small_ref[:, :D] + got_ref[:, :D]).astype(LOWER)
    pairs = [(f_own, f.at[0]), (f_par, f.at[1])]
    for c in range(3):
        pairs += [(g_own.at[c], g.at[c, :SLOT]), (g_par.at[c], g.at[c, SLOT:])]
    copies = fetch(pairs, sems)
    copies[0].wait()
    copies[1].wait()
    height = D // 8
    half = D // 2
    left = turned_rows(me, (f[0], f[1]), height)
    for ref in (xk, xs, yk, ys):
        for k in range(2):
            ref[k, height:] = jnp.zeros((16, 3 * half), LOWER)
            if ref is xk or ref is xs:
                ref[k, height:, :D] = small
    for k in range(2, 8):
        copies[k].wait()
    sent = []
    for c in range(3):
        grad = product(left, g[c]).astype(LOWER)
        for k, there in enumerate(PLACES):
            to_x, to_y = target(there, (xk, xs), (yk, ys))
            block = grad[height * k : height * k + height]
            if c == 0:
                to_x[:height, :D] = block
            elif c == 1:
                to_x[:height, D:] = block[:, :half]
                to_y[:height, :half] = block[:, half:]
            else:
                to_y[:height, half:] = block
        if c:
            done = ((xk, xk_any), (xs, xs_any)) if c == 1 else ((yk, yk_any), (ys, ys_any))
            sent += pages_out(done, out_sems, len(sent))
    for copy in sent:
        copy.wait()


def weight_call(name, body, me, ins, rows, columns, held_shapes, flops, after, extra=()):
    out = narrow(2, rows, columns)
    copies = {"weights_one": 14, "weights_two": 14, "weights_three": 8}[name]
    return run(
        name,
        body,
        [me, *ins, *extra],
        [SCALARS] + [ANY] * len(ins) + [WHOLE] * len(extra),
        [out] * 4,
        [ANY] * 4,
        after=after,
        scratch=[pltpu.VMEM(out.shape, LOWER)] * 4
        + [pltpu.VMEM(shape, LOWER) for shape in held_shapes]
        + [pltpu.SemaphoreType.DMA((copies,)), pltpu.SemaphoreType.DMA((8,))],
        flops=flops,
    )


def weights_one(me, third, g_pairs, hidden, branch, after=()):
    shapes = [(2, SLOT, D), (2 * SLOT, 2 * D), (4, 2 * SLOT, FF // 8), (2 * SLOT, D)]
    ins = (*third, *g_pairs, *hidden, *branch)
    return weight_call("weights_one", one_kernel, me, ins, 3 * D // 8, D, shapes, 4 * 10**9, after)


def weights_two(me, second, g_inner, mixed, low, after=()):
    shapes = [(2, SLOT, D), (4, 2 * SLOT, D), (2, SLOT, D), (2 * SLOT, D)]
    ins = (*second, *g_inner, *mixed, *low)
    return weight_call("weights_two", two_kernel, me, ins, 5 * D // 16, D, shapes, COST[6], after)


def weights_three(me, first, grads, small, after=()):
    shapes = [(2, SLOT, D), (3, 2 * SLOT, D)]
    ins = (*first, *grads)
    return weight_call("weights_three", three_kernel, me, ins, D // 8 + 16, 3 * D // 2, shapes, COST[4], after, small)


def page(array, k):
    return pl.BlockSpec((1,) + array.shape[1:], lambda s: (k, 0, 0))


def add_first(parts, flops=0, after=()):
    count = len(parts)

    def body(*refs):
        for k in range(count):
            refs[2 * count + k][...] = (refs[2 * k][0].astype(WIDER) + refs[2 * k + 1][0].astype(WIDER)).astype(LOWER)

    flat = [a for pair in parts for a in pair]
    outs = [narrow(*keep.shape[1:]) for keep, unused in parts]
    return run("add_first", body, flat, [page(a, 1) for a in flat], outs, after=after, grid=(1,), flops=flops)


def add_second(parts, side=False, after=()):
    shapes = [keep.shape[1:] for keep, unused, unused_too in parts]
    rows = shapes[0][0] + 16 if side else sum(shape[0] for shape in shapes)
    columns = sum(shape[1] for shape in shapes) if side else shapes[0][1]

    def body(*refs):
        out = refs[-1]
        first = 0
        for k, (high, across) in enumerate(shapes):
            keep, got, last = refs[3 * k : 3 * k + 3]
            total = (keep[0].astype(WIDER) + got[0].astype(WIDER) + last[...].astype(WIDER)).astype(LOWER)
            if side:
                out[:high, first : first + across] = total
                first += across
            else:
                out[first : first + high] = total
                first += high
        if side:
            out[rows - 16 :] = jnp.zeros((16, columns), LOWER)

    flat = [a for trio in parts for a in trio]
    specs = [page(a, 0) if a.ndim == 3 else WHOLE for a in flat]
    return run("add_second", body, flat, specs, [narrow(rows, columns)], after=after, grid=(1,), flops=0)


def add_pair(one, two, flops=0, after=()):
    def body(one_ref, two_ref, out_ref):
        out_ref[...] = (one_ref[...].astype(WIDER) + two_ref[...].astype(WIDER)).astype(LOWER)

    return run("add_pair", body, [one, two], [WHOLE] * 2, [narrow(*one.shape)], after=after, flops=flops)


def add_parts(share, parts, me, after=()):
    rows, columns = parts[0].shape

    def body(me_ref, share_ref, one_ref, two_ref, three_ref, out_ref):
        first = pl.multiple_of(me_ref[0] * rows, 16)
        total = share_ref[pl.ds(first, rows), :].astype(WIDER) + one_ref[...].astype(WIDER)
        out_ref[...] = (total + two_ref[...].astype(WIDER) + three_ref[...].astype(WIDER)).astype(LOWER)

    return run("add_parts", body, [me, share, *parts], [SCALARS] + [WHOLE] * 4, [narrow(rows, columns)], after=after, flops=0)


def add_rows(one, two, after=()):
    def body(one_ref, two_ref, out_ref):
        out_ref[...] = one_ref[...] + two_ref[...]

    return run("add_rows", body, [one, two], [WHOLE] * 2, [wide(*one.shape)], after=after, flops=0)


def partner(axis, bit):
    return [(k, k ^ (1 << bit)) for k in range(lax.axis_size(axis))]


def swap(value, axis, bit):
    return lax.ppermute(value, axis, partner(axis, bit))


def all_sum(value, axis):
    for bit in range(lax.axis_size(axis).bit_length() - 1):
        value = value + swap(value, axis, bit)
    return value


def pa_order(turn):
    rest = lax.axis_size("pa").bit_length() - 2
    return [1 + (k + turn) % rest for k in range(rest)]


def both_cores(acts, turn):
    size = lax.axis_size("pa")
    me = lax.axis_index("pa")
    blocks = jnp.transpose(acts).reshape(size, acts.shape[1] // size, acts.shape[0])
    order = pa_order(turn)
    offsets = [
        sum(((k >> (len(order) - 1 - p)) & 1) << bit for p, bit in enumerate(order)) for k in range(size // 2)
    ]
    mine = jnp.concatenate([lax.dynamic_slice_in_dim(blocks, me ^ d, 1) for d in offsets])
    theirs = jnp.concatenate([lax.dynamic_slice_in_dim(blocks, me ^ d ^ 1, 1) for d in offsets])
    return mine, swap(theirs, "pa", 0)


def weight_part(acts, grads, first, last):
    total = None
    for act, grad in zip(acts, grads):
        act = act[first:last]
        term = product(act.reshape(-1, act.shape[2]), grad)
        total = term if total is None else total + term
    height = acts[0].shape[1]
    return total.astype(LOWER).reshape(last - first, height, -1)


def add_up(parts):
    total = parts[0].astype(WIDER)
    for part in parts[1:]:
        total = total + part.astype(WIDER)
    return total.astype(LOWER)


def share_over_pa(acts, grads, turn):
    size = acts[0].shape[0]
    keep = [weight_part(acts, grads, 0, size // 2)]
    send = weight_part(acts, grads, size // 2, size)
    for bit in pa_order(turn):
        keep.append(swap(send, "pa", bit))
        size //= 2
        if size > 1:
            send = add_up([part[size // 2 : size] for part in keep])
            keep = [part[: size // 2] for part in keep]
    return add_up([part[0] for part in keep])


def inward(share):
    return lax.ppermute(share, "pb", [(0, 1), (3, 2)])


def between(share):
    return lax.ppermute(share, "pb", [(1, 2), (2, 1)])


def outward(share):
    me = lax.axis_index("pb")
    got = lax.ppermute(share, "pb", [(1, 0), (2, 3)])
    return jnp.where((me == 1) | (me == 2), share, got).astype(WIDER)


def swap_parts(share):
    me = lax.axis_index("pb")
    quarters = share.reshape(4, share.shape[0] // 4, share.shape[1])
    return [
        lax.ppermute(lax.dynamic_index_in_dim(quarters, me ^ s, 0, False), "pb", [(k, k ^ s) for k in range(4)])
        for s in range(1, 4)
    ]


def spread_parts(total, token):
    me = lax.axis_index("pb")
    got = [total] + [lax.ppermute(total, "pb", [(k, k ^ s) for k in range(4)]) for s in range(1, 4)]
    return jnp.concatenate([lax.select_n(me ^ b, *got) for b in range(4)], axis=0).astype(WIDER)


def total_plain(share):
    return lax.psum(share, "pb").astype(WIDER)


def local(
    passages,
    lengths,
    answers,
    cotangent,
    enc_gain1,
    enc_qkv,
    enc_bias,
    enc_out,
    enc_gain2,
    enc_ffn_in,
    enc_ffn_out,
    enc_gain3,
    cross_kv,
    dec_gain1,
    dec_qkv,
    dec_bias,
    dec_out,
    dec_gain2,
    cross_query,
    cross_out,
    dec_gain3,
    dec_ffn_in,
    dec_ffn_out,
):
    pa_size = lax.axis_size("pa")
    pb_size = lax.axis_size("pb")
    fast = pa_size == 8 and pb_size == 4
    me = lax.axis_index("pa").astype(jnp.int32).reshape(1)
    x = passages.reshape(SLOT, D)
    count = lengths.reshape(1)
    table = jnp.transpose(enc_bias)
    dec_table = jnp.transpose(dec_bias)
    pick = jnp.asarray(PICK, LOWER)
    pick_back = jnp.asarray(PICK_BACK, LOWER)

    def across(value):
        return value, swap(value, "pa", 0)

    dec_after, lefts, dec_heads, query, token = dec_self(
        dec_table, answers[0], dec_gain1, dec_gain2, dec_qkv, dec_out, cross_query
    )
    first, heads, mixed, stats, packed, after, second, slope, hidden, final, third, pairs, token = forward(
        count, table, pick, x, enc_gain1, enc_qkv, enc_gain2, enc_gain3, query, enc_out, enc_ffn_in, enc_ffn_out, cross_kv,
        after=[token],
    )
    if fast:
        acts = [across(value) for value in (first, mixed, second, hidden, third)]
    else:
        acts = [both_cores(v, k % 2) for k, v in enumerate((first, mixed, second, hidden, third))]
    gathered = lax.all_gather(packed, "pa")
    answer, early, g_middle, g_gain3, partial, g_enc_gain3, g_pairs, g_final, branch, token = dec_mid(
        count, gathered, dec_after, cotangent[0], dec_gain3, lefts, query, enc_gain3, pairs,
        cross_out, dec_ffn_in, dec_ffn_out, cross_kv, final,
        after=[got for unused, got in acts[:4]],
    )
    early_all = lax.all_gather(early, "pb")
    g_inner, g_after, low, g_mixed, g_enc_gain2, token = ffn_back(
        branch, enc_ffn_out, slope, enc_ffn_in, after, enc_gain2, g_final, enc_out, after=[token]
    )

    def back_of(base, pairs, after):
        return attention_back(count, table, pick, heads, g_mixed, mixed, stats, base, pairs, after=after)

    def dec_end(part, got, token, wait=()):
        return dec_back(
            dec_table, answers[0], part, got, dec_after, g_middle, dec_heads,
            dec_gain1, dec_gain2, g_gain3, cross_query, dec_out, dec_qkv, after=[token, *wait],
        )

    def rows_end(grads, diagonal, token, wait=()):
        return attention_end(
            count, table, pick, heads, g_mixed, mixed, stats, grads, diagonal, enc_qkv, x, enc_gain1,
            g_after, g_enc_gain2, g_enc_gain3, pick_back, after=[token, *wait],
        )

    pb_me = lax.axis_index("pb").astype(jnp.int32).reshape(1)

    def outer_end(token, late_one, late_two):
        *outer, token = dec_outer(pb_me, early_all, late_one, late_two, pb_size, after=[token])
        return outer, token

    if fast:
        partial, token = add_rows(partial, swap(partial, "pa", 0), after=[token])
        got = swap(partial, "pa", 1)
        xk, xs, yk, ys, token = weights_one(me, acts[4], across(g_pairs), acts[3], across(branch), after=[token])
        one = ((xk, swap(xs, "pa", 1)), (yk, swap(ys, "pa", 2)))
        partial, token = add_rows(partial, got, after=[token])
        got = swap(partial, "pa", 2)
        grads, diagonal_a, token = back_of(0, FIRST, [token])
        late, g_start, token = dec_end(partial, got, token)
        late_near = swap(late, "pb", 0)
        send_x, send_y, token = add_first(one, flops=COST[5], after=[token, early_all])
        last = (swap(send_x, "pa", 2), swap(send_y, "pa", 1))
        late, token = stack_late(late, late_near, after=[token])
        late_far = swap(late, "pb", 1)
        xk, xs, yk, ys, token = weights_two(me, acts[2], across(g_inner), acts[1], across(low), after=[token])
        two = ((xk, swap(xs, "pa", 1)), (yk, swap(ys, "pa", 2)))
        share_one, token = add_second([one[0] + last[:1], one[1] + last[1:]], after=[token])
        got_one = inward(share_one)
        g_rows, small, diagonal_a, grads, token = rows_end(grads, diagonal_a, token, [late_far])
        there, got_small = swap(grads, "pa", 0), swap(small, "pa", 0)
        send_x, send_y, token = add_first(two, flops=COST[0], after=[token])
        last = (swap(send_x, "pa", 2), swap(send_y, "pa", 1))
        share_one, token = add_pair(share_one, got_one, flops=COST[1], after=[token])
        got_one = between(share_one)
        xk, xs, yk, ys, token = weights_three(me, acts[0], (grads, there), (small, got_small), after=[token])
        three = ((xk, swap(xs, "pa", 1)), (yk, swap(ys, "pa", 2)))
        share_two, token = add_second([two[0] + last[:1], two[1] + last[1:]], after=[token])
        got_two = inward(share_two)
        share_one, token = add_pair(share_one, got_one, flops=COST[2], after=[token])
        total_one = outward(share_one)
        send_x, send_y, token = add_first(three, after=[token])
        last = (swap(send_x, "pa", 2), swap(send_y, "pa", 1))
        share_two, token = add_pair(share_two, got_two, flops=COST[3], after=[token])
        got_two = between(share_two)
        share_three, token = add_second([three[0] + last[:1], three[1] + last[1:]], side=True, after=[token])
        parts = swap_parts(share_three)
        outer, token = outer_end(token, late, late_far)
        share_two, token = add_pair(share_two, got_two, after=[token])
        total_two = outward(share_two)
        total_three = spread_parts(*add_parts(share_three, parts, pb_me, after=[token, total_one]))
        small = total_three[D // pa_size :, :D]
        block = D // pa_size
        total_kv = jnp.concatenate([total_one[:block], total_one[block : 2 * block]], axis=1)
        total_ffn_out = total_one[2 * block :]
        second_part = 2 * block + block // 2
        total_ffn_in = jnp.concatenate(
            [total_two[first : first + block] for first in (0, block, second_part, second_part + block)], axis=1
        )
        total_out = jnp.concatenate([total_two[2 * block : second_part], total_two[second_part + 2 * block :]], axis=0)
        total_qkv = total_three[:block]
    else:
        partial = all_sum(partial, "pa")
        late, g_start, token = dec_end(partial, jnp.zeros_like(partial), token)
        late, token = stack_late(late, swap(late, "pb", 0), after=[token])
        late_far = swap(late, "pb", 1)
        grads, diagonal_a, token = back_of(0, FIRST, [token])
        g_rows, small, diagonal_a, grads, token = rows_end(grads, diagonal_a, token)
        outer, token = outer_end(token, late, late_far)
        small = all_sum(all_sum(small[:, :D], "pa"), "pb")
        g_heads = jnp.concatenate([grads[0], grads[1], grads[2]], axis=1)
        total_kv = total_plain(share_over_pa(acts[4], across(g_pairs), 0))
        total_ffn_out = total_plain(share_over_pa(acts[3], across(branch), 1))
        total_ffn_in = total_plain(share_over_pa(acts[2], across(g_inner), 0))
        total_out = total_plain(share_over_pa(acts[1], across(low), 1))
        total_qkv = total_plain(share_over_pa(acts[0], across(g_heads), 0))

    d_qkv, d_out, d_query, d_cross, d_in, d_ffn, dec_small = outer
    dec_small = dec_small[0]
    dec_bias_rows = dec_small[3 * D :].reshape(H, STAT)[:, GROUP - ANS : GROUP]
    dec_bias_all = jnp.pad(jnp.transpose(dec_bias_rows[:, ::-1]), ((0, BUCKETS - ANS), (0, 0)))

    def own_part(vector, axis):
        height = vector.shape[0] // lax.axis_size(axis)
        return lax.dynamic_slice_in_dim(vector, lax.axis_index(axis) * height, height, axis=0)

    return (
        answer[None],
        g_rows.reshape(1, 1, SLOT, D),
        g_start[None],
        own_part(small[0], "pa"),
        total_qkv,
        jnp.transpose(small[4:16, :BUCKETS]),
        total_out,
        own_part(small[1], "pa"),
        total_ffn_in,
        total_ffn_out,
        own_part(small[2], "pa"),
        total_kv,
        own_part(dec_small[:D], "pb"),
        d_qkv,
        own_part(dec_bias_all, "pb"),
        d_out,
        own_part(dec_small[D : 2 * D], "pb"),
        d_query,
        d_cross,
        own_part(dec_small[2 * D : 3 * D], "pb"),
        d_in,
        d_ffn,
    )


def solution(mesh):
    copied = P()
    in_specs = (
        P("pb", "pa", None, None),
        P("pb", "pa"),
        P("pb", None, None),
        P("pb", None, None),
    ) + (copied,) * 19
    by_pa, by_pa_rows = P("pa"), P("pa", None)
    by_pb, by_pb_rows = P("pb"), P("pb", None)
    out_specs = (
        P("pb", None, None),
        P("pb", "pa", None, None),
        P("pb", None, None),
        by_pa,
        by_pa_rows,
        copied,
        by_pa_rows,
        by_pa,
        by_pa_rows,
        by_pa_rows,
        by_pa,
        by_pa_rows,
        by_pb,
        by_pb_rows,
        by_pb_rows,
        by_pb_rows,
        by_pb,
        by_pb_rows,
        by_pb_rows,
        by_pb,
        by_pb_rows,
        by_pb_rows,
    )
    return jax.shard_map(local, mesh=mesh, in_specs=in_specs, out_specs=out_specs, check_vma=False)
```

```python
import jax
import jax.numpy as jnp
import numpy as np
from jax import lax
from jax.experimental import pallas as pl
from jax.experimental.pallas import tpu as pltpu
from jax.sharding import PartitionSpec as P

D = 768
H = 12
HD = 64
FF = 3072
BUCKETS = 32
ANS = 20
SLOT = 512
PAIR = 2 * HD
PAIRS = H // 2
EDGE = 128
STRIP = 256
SPAN = 256
GROUP = 24
COST = (4 * 10**9, 0, 4 * 10**9, 0, 4 * 10**9, 4 * 10**9, 4 * 10**9)
STACK = H * GROUP
STAT = 128
STEPS = 4
WIDTH = FF // STEPS
FIRST = 4
EPS = 1e-06
MASKED = -1000000000.0
C_GELU = 0.7978845608028654
LOWER = jnp.bfloat16
WIDER = jnp.float32
EARLY = 7 * D + 2 * FF
LATE = 5 * D
AT = {
    "first": 0,
    "own": D,
    "second": 2 * D,
    "mix": 3 * D,
    "third": 4 * D,
    "hidden": 5 * D,
    "g_middle": 5 * D + FF,
    "g_inner": 6 * D + FF,
    "g_out": 6 * D + 2 * FF,
    "g_heads": 0,
    "g_after": 3 * D,
    "g_query": 4 * D,
}


def tile_classes(away):
    rows = [np.clip(EDGE * d - away, -(BUCKETS // 2), BUCKETS // 2 - 1) + BUCKETS // 2 for d in (-1, 0, 1)]
    return np.eye(BUCKETS, dtype=np.float32)[np.concatenate(rows)]


LANES = np.arange(SPAN)
PICK = tile_classes(np.where(LANES < EDGE, LANES, LANES - SPAN)).T
ENDS = np.repeat(np.eye(BUCKETS, dtype=np.float32)[[0, BUCKETS - 1]], EDGE, axis=0)
PICK_BACK = np.pad(np.concatenate([tile_classes(LANES - (EDGE - 1)), ENDS]), ((0, 0), (0, STAT - BUCKETS)))

SCALARS = pl.BlockSpec(memory_space=pltpu.SMEM)
ANY = pl.BlockSpec(memory_space=pl.ANY)
WHOLE = pl.BlockSpec(memory_space=pltpu.VMEM)
TOKEN = (8, 128)


def wide(*shape):
    return jax.ShapeDtypeStruct(shape, WIDER)


def narrow(*shape):
    return jax.ShapeDtypeStruct(shape, LOWER)


def run(name, body, ins, in_specs, outs, out_specs=None, after=(), grid=(), scratch=(), flops=10**9, mib=63, alias=None):
    count, extra, results = len(ins), len(after), len(outs)
    if out_specs is None:
        out_specs = [WHOLE] * results
    zeros = (lambda *s: (0, 0)) if grid else (lambda: (0, 0))

    def wrapped(*refs):
        refs[count + extra + results][...] = jnp.zeros(TOKEN, WIDER)
        body(*refs[:count], *refs[count + extra : count + extra + results], *refs[count + extra + results + 1 :])

    got = pl.pallas_call(
        wrapped,
        grid=grid,
        out_shape=tuple(outs) + (wide(*TOKEN),),
        in_specs=list(in_specs) + [ANY] * extra,
        out_specs=tuple(out_specs) + (pl.BlockSpec(TOKEN, zeros),),
        scratch_shapes=list(scratch),
        input_output_aliases=alias or {},
        compiler_params=pltpu.CompilerParams(vmem_limit_bytes=mib * 2**20),
        cost_estimate=pl.CostEstimate(flops=10 * flops, bytes_accessed=1, transcendentals=0),
        name=name,
    )(*ins, *after)
    return got


def product(left, right):
    return jnp.dot(left, right, preferred_element_type=WIDER)


def left_product(left, right):
    return lax.dot_general(left, right, (((0,), (0,)), ((), ())), preferred_element_type=WIDER)


def right_product(left, right):
    return lax.dot_general(left, right, (((1,), (1,)), ((), ())), preferred_element_type=WIDER)


def split_product(left, right, terms):
    total = None
    for k in range(terms):
        part = left.astype(LOWER)
        left = left - part.astype(WIDER)
        term = product(part, right)
        total = term if total is None else total + term
    return total


def silu_like(inner):
    square = inner * inner
    tanh = jnp.tanh(inner * (C_GELU + (C_GELU * 0.044715) * square))
    half = 0.5 + 0.5 * tanh
    value = inner * half
    slope = half + value * (1.0 - tanh) * (C_GELU + (3.0 * C_GELU * 0.044715) * square)
    return value, slope


def row_of(ref):
    return ref[...].reshape(1, D)


def scale_of(values):
    return lax.rsqrt(jnp.mean(values * values, axis=-1, keepdims=True) + EPS)


def norm_pull(values, gain, grad):
    scale = scale_of(values)
    lifted = grad * gain
    inside = jnp.sum(values * lifted, axis=-1, keepdims=True)
    back = scale * lifted - values * (scale * scale * scale * inside * (1.0 / D))
    return back, jnp.sum(grad * values * scale, axis=0, keepdims=True)


def fetch(pairs, sems):
    copies = [pltpu.make_async_copy(s, t, sems.at[k]) for k, (s, t) in enumerate(pairs)]
    for copy in copies:
        copy.start()
    return copies


def copy_all(pairs, sems):
    return [pltpu.make_async_copy(s, t, sems.at[k]) for k, (s, t) in enumerate(pairs)]


def begin(copies):
    for copy in copies:
        copy.start()


def bias_tiles(u_ref, head):
    tiles = []
    for d in range(3):
        row = u_ref[pl.ds(head, 1), SPAN * d : SPAN * d + SPAN]
        spread = jnp.broadcast_to(row, (EDGE, SPAN))
        tiles.append(pltpu.roll(spread, 0, 1, stride=1, stride_axis=0)[:, :EDGE])
    return tiles


def key_masks(n):
    places = lax.broadcasted_iota(jnp.int32, (EDGE, EDGE), 0)
    return [jnp.where(places + EDGE * j < n, 0.0, MASKED) for j in range(SLOT // EDGE)]


def score_blocks(raw, tiles, masks, low, high, first):
    columns = []
    for c in range(STRIP // EDGE):
        blocks = []
        for j in range(SLOT // EDGE):
            block = raw[EDGE * j : EDGE * j + EDGE, EDGE * c : EDGE * c + EDGE]
            d = j - first - c
            block = block + (tiles[d + 1] if abs(d) <= 1 else (low if d < 0 else high))
            blocks.append(block + masks[j] if j > 0 else block)
        columns.append(blocks)
    return columns


def paved(columns, kind):
    return jnp.concatenate([jnp.concatenate([b.astype(kind) for b in blocks], axis=0) for blocks in columns], axis=1)


def fill_rows(table_ref, pick_ref, u_ref):
    @pl.when(pl.program_id(0) == 0)
    def _():
        u_ref[...] = split_product(table_ref[...], pick_ref[...], 3)


def attn_fwd_kernel(n_ref, ends_ref, table_ref, pick_ref, x_ref, g1_ref, wq_ref, wk_ref, wv_ref, first_ref, heads_ref, o_ref, st_ref, u_ref):
    fill_rows(table_ref, pick_ref, u_ref)
    step = pl.program_id(0)

    @pl.when(step == 0)
    def _():
        rows = x_ref[...].astype(WIDER)
        first_ref[...] = (rows * scale_of(rows) * row_of(g1_ref)).astype(LOWER)

    masks = key_masks(n_ref[0])
    first = first_ref[...]
    for k, w_ref in enumerate((wq_ref, wk_ref, wv_ref)):
        heads_ref[k] = product(first, w_ref[...]).astype(LOWER)
    q_ref, k_ref = heads_ref.at[0], heads_ref.at[1]
    values = jnp.transpose(heads_ref[2])
    ones = jnp.ones((16, SLOT), LOWER)
    mixed = []
    for h in range(2):
        head = 2 * step + h
        low, high = ends_ref[head, 0], ends_ref[head, BUCKETS - 1]
        tiles = bias_tiles(u_ref, head)
        cols = slice(HD * h, HD * h + HD)
        keys = k_ref[:, cols]
        left = jnp.concatenate([values[cols], ones], axis=0)
        strips = []
        for i in range(0, SLOT // EDGE, STRIP // EDGE):
            lanes = slice(EDGE * i, EDGE * i + STRIP)
            raw = right_product(keys, q_ref[lanes, cols] * 0.125)
            tops, powers = [], []
            for blocks in score_blocks(raw, tiles, masks, low, high, i):
                top = jnp.maximum(jnp.maximum(blocks[0], blocks[1]), jnp.maximum(blocks[2], blocks[3]))
                top = jnp.max(top, axis=0, keepdims=True)
                tops.append(top)
                powers.append([jnp.exp(block - top) for block in blocks])
            out = product(left, paved(powers, LOWER))
            total = out[HD : HD + 1]
            st_ref[0, h : h + 1, lanes] = jnp.concatenate(tops, axis=1) + jnp.log(total)
            strips.append(out[:HD] * (1.0 / total))
        mixed.append(jnp.concatenate(strips, axis=1))
    lanes = pl.ds(pl.multiple_of(step * PAIR, PAIR), PAIR)
    o_ref[:, lanes] = jnp.transpose(jnp.concatenate(mixed, axis=0)).astype(LOWER)


def attn_bwd_kernel(base):
    def body(
        n_ref, ends_ref, table_ref, pick_ref, h_ref, g_ref, o_ref, st_ref, gh_ref, gb_ref, u_ref
    ):
        q_ref, k_ref, v_ref = h_ref.at[0], h_ref.at[1], h_ref.at[2]
        fill_rows(table_ref, pick_ref, u_ref)
        step = pl.program_id(0) + base
        masks = key_masks(n_ref[0])
        keys_t = jnp.transpose(k_ref[...])
        rows = lax.broadcasted_iota(jnp.int32, (EDGE, EDGE), 0)
        columns = lax.broadcasted_iota(jnp.int32, (EDGE, EDGE), 1)
        mirror = jnp.where(rows + columns == EDGE - 1, 1.0, 0.0).astype(LOWER)
        rows = lax.broadcasted_iota(jnp.int32, (16, SLOT), 0) * EDGE
        columns = lax.broadcasted_iota(jnp.int32, (16, SLOT), 1)
        places = jnp.where((columns >= rows) & (columns < rows + EDGE), 1.0, 0.0).astype(LOWER)
        rows = lax.broadcasted_iota(jnp.int32, (16, PAIR), 0) * HD
        columns = lax.broadcasted_iota(jnp.int32, (16, PAIR), 1)
        halves = jnp.where((columns >= rows) & (columns < rows + HD), 1.0, 0.0).astype(LOWER)
        met = g_ref[...].astype(WIDER) * o_ref[...].astype(WIDER)
        upper = met.astype(LOWER)
        lower = (met - upper.astype(WIDER)).astype(LOWER)
        weighted = right_product(halves, upper) + right_product(halves, lower)
        grad_queries = []
        gb_ref[0, 2:8, :] = jnp.zeros((6, 4 * SPAN), WIDER)
        for h in range(2):
            head = 2 * step + h
            low, high = ends_ref[head, 0], ends_ref[head, BUCKETS - 1]
            tiles = bias_tiles(u_ref, head)
            cols = slice(HD * h, HD * h + HD)
            keys = k_ref[:, cols]
            values = v_ref[:, cols]
            left = jnp.concatenate([keys_t[cols], places], axis=0)
            grad_keys = jnp.zeros((SLOT, HD), WIDER)
            grad_values = jnp.zeros((SLOT, HD), WIDER)
            strips = []
            sums = {}

            def gather(d, block):
                sums[d] = sums[d] + block if d in sums else block

            for i in range(0, SLOT // EDGE, STRIP // EDGE):
                lanes = slice(EDGE * i, EDGE * i + STRIP)
                query = q_ref[lanes, cols]
                grad = g_ref[lanes, cols]
                raw = right_product(keys, query * 0.125)
                grad_probs = right_product(values, grad)
                probs, changes = [], []
                for c, blocks in enumerate(score_blocks(raw, tiles, masks, low, high, i)):
                    part = slice(EDGE * (i + c), EDGE * (i + c) + EDGE)
                    total = st_ref[0, h : h + 1, part]
                    mean = weighted[h : h + 1, part]
                    probs.append([jnp.exp(block - total) for block in blocks])
                    changes.append([])
                    for j in range(SLOT // EDGE):
                        gap = grad_probs[EDGE * j : EDGE * j + EDGE, EDGE * c : EDGE * c + EDGE] - mean
                        change = probs[c][j] * gap
                        changes[c].append(change)
                        if abs(j - i - c) <= 1:
                            gather(j - i - c, change)
                rounded = paved(changes, LOWER)
                out = product(left, rounded)
                strips.append(out[:HD])
                for c in range(STRIP // EDGE):
                    for j in range(SLOT // EDGE):
                        if abs(j - i - c) > 1:
                            gather(2 if j > i + c else -2, out[HD + j : HD + j + 1, EDGE * c : EDGE * c + EDGE])
                grad_keys += product(rounded, query)
                grad_values += product(paved(probs, LOWER), grad)
            grad_queries.append(jnp.concatenate(strips, axis=1))
            gh_ref[1, :, cols] = (grad_keys * 0.125).astype(LOWER)
            gh_ref[2, :, cols] = grad_values.astype(LOWER)
            empty = jnp.zeros((EDGE, SPAN - EDGE), WIDER)
            band = jnp.concatenate([sums[-1], sums[0], sums[1]], axis=1)
            upper = band.astype(LOWER)
            lower = (band - upper.astype(WIDER)).astype(LOWER)
            mirrored = product(mirror, upper) + product(mirror, lower)
            for d in range(3):
                spread = jnp.concatenate([mirrored[:, EDGE * d : EDGE * d + EDGE], empty], axis=1)
                turned = pltpu.roll(spread, 0, 1, stride=1, stride_axis=0)
                gb_ref[0, h : h + 1, SPAN * d : SPAN * d + SPAN] = jnp.sum(turned, axis=0, keepdims=True)
            for place, d in ((3 * SPAN, -2), (3 * SPAN + EDGE, 2)):
                gb_ref[0, h : h + 1, place : place + EDGE] = sums[d]
        gh_ref[0] = (jnp.transpose(jnp.concatenate(grad_queries, axis=0)) * 0.125).astype(LOWER)

    return body


def columns_at(first):
    return pl.BlockSpec((SLOT, PAIR), lambda s: (0, first + s))


def stats_at(first):
    return pl.BlockSpec((1, 2, SLOT), lambda s: (first + s, 0, 0))


def pair_of_all(base):
    return pl.BlockSpec((3, SLOT, PAIR), lambda s: (0, 0, base + s))


def attention_back(count, table, pick, heads, grad_mixed, mixed, stats, base, half, after=()):
    return run(
        "enc_attention_back",
        attn_bwd_kernel(base),
        [count, table, table, pick, heads, grad_mixed, mixed, stats],
        [SCALARS, SCALARS, WHOLE, WHOLE, pair_of_all(base), columns_at(base), columns_at(base), stats_at(base)],
        [narrow(3, SLOT, D), wide(half, 8, 4 * SPAN)],
        [pair_of_all(base), pl.BlockSpec((1, 8, 4 * SPAN), lambda s: (s, 0, 0))],
        after=after,
        grid=(half,),
        scratch=[pltpu.VMEM((H, 3 * SPAN), WIDER)],
        flops=2 * 5 * H * SLOT * SLOT * HD * 4,
    )


def send_out(pairs, sems, first):
    copies = [pltpu.make_async_copy(s, t, sems.at[first + k]) for k, (s, t) in enumerate(pairs)]
    for copy in copies:
        copy.start()
    return copies


def chunk(k):
    return slice(WIDTH * k, WIDTH * k + WIDTH)


def forward_kernel(
    n_ref, ends_ref, table_ref, pick_ref, x_ref, g1_ref, wq_ref, wk_ref, wv_ref,
    g2_ref, g3_ref, query_ref, wo_any, in_any, out_any, kv_any,
    first_ref, heads_ref, mixed_ref, st_ref, packed_ref,
    after_any, second_any, slope_any, hidden_any, final_any, third_any, pairs_any,
    u_ref, wo_ref, in_ref, out_ref, kv_ref,
    after_ref, second_ref, slope_ref, hidden_ref, final_ref, third_ref, pairs_ref,
    sems, out_sems,
):
    step = pl.program_id(0)
    pairs = [(wo_any, wo_ref)]
    for k in range(STEPS):
        pairs += [(in_any.at[:, chunk(k)], in_ref.at[k]), (out_any.at[chunk(k)], out_ref.at[k])]
    copies = copy_all(pairs + [(kv_any, kv_ref)], sems)

    @pl.when(step == 0)
    def _():
        for copy in copies:
            copy.start()

    attn_fwd_kernel(
        n_ref, ends_ref, table_ref, pick_ref, x_ref, g1_ref, wq_ref, wk_ref, wv_ref,
        first_ref, heads_ref, mixed_ref, st_ref, u_ref,
    )

    @pl.when(step == PAIRS - 1)
    def _():
        for copy in copies:
            copy.wait()
        after = x_ref[...].astype(WIDER) + product(mixed_ref[...], wo_ref[...])
        after_ref[...] = after
        second = (after * scale_of(after) * row_of(g2_ref)).astype(LOWER)
        second_ref[...] = second
        inner = product(second, in_ref[0])
        sent = send_out([(after_ref, after_any), (second_ref, second_any)], out_sems, 0)
        total = after
        for k in range(STEPS):
            following = product(second, in_ref[k + 1]) if k + 1 < STEPS else None
            value, slope = silu_like(inner)
            slope_ref[:, chunk(k)] = slope.astype(LOWER)
            hidden = value.astype(LOWER)
            hidden_ref[:, chunk(k)] = hidden
            total = total + product(hidden, out_ref[k])
            inner = following
            if k % 2:
                half = slice(WIDTH * (k - 1), WIDTH * (k + 1))
                sent += send_out(
                    [(slope_ref.at[:, half], slope_any.at[:, half]), (hidden_ref.at[:, half], hidden_any.at[:, half])],
                    out_sems, len(sent),
                )
        final_ref[...] = total
        third = (total * scale_of(total) * row_of(g3_ref)).astype(LOWER)
        third_ref[...] = third
        sent += send_out([(final_ref, final_any), (third_ref, third_any)], out_sems, len(sent))
        for k in range(2):
            half = slice(D * k, D * k + D)
            pairs_ref[:, half] = product(third, kv_ref[:, half]).astype(LOWER)
        sent += send_out([(pairs_ref, pairs_any)], out_sems, len(sent))
        cross_kernel(n_ref, query_ref, pairs_ref, packed_ref)
        for copy in sent:
            copy.wait()


def whole(*shape):
    return pl.BlockSpec(shape, lambda s: (0,) * len(shape))


def forward(count, table, pick, x, gain1, qkv, gain2, gain3, query, wo, ffn_in, ffn_out, kv, after=()):
    def weights_at(first):
        return pl.BlockSpec((D, PAIR), lambda s: (0, first + s))

    kept = [wide(SLOT, D), narrow(SLOT, D), narrow(SLOT, FF), narrow(SLOT, FF), wide(SLOT, D), narrow(SLOT, D), narrow(SLOT, 2 * D)]
    return run(
        "enc_forward",
        forward_kernel,
        [count, table, table, pick, x, gain1, qkv, qkv, qkv, gain2, gain3, query, wo, ffn_in, ffn_out, kv],
        [SCALARS, SCALARS, WHOLE, WHOLE, whole(SLOT, D), whole(D), weights_at(0), weights_at(PAIRS), weights_at(2 * PAIRS)]
        + [whole(D), whole(D), whole(GROUP, D)] + [ANY] * 4,
        [narrow(SLOT, D), narrow(3, SLOT, D), narrow(SLOT, D), wide(PAIRS, 2, SLOT), wide(GROUP, D + STAT)] + kept,
        [whole(SLOT, D), pair_of_all(0), whole(SLOT, D), stats_at(0), whole(GROUP, D + STAT)] + [ANY] * 7,
        after=after,
        grid=(PAIRS,),
        scratch=[
            pltpu.VMEM((H, 3 * SPAN), WIDER),
            pltpu.VMEM((D, D), LOWER),
            pltpu.VMEM((STEPS, D, WIDTH), LOWER),
            pltpu.VMEM((STEPS, WIDTH, D), LOWER),
            pltpu.VMEM((D, 2 * D), LOWER),
        ]
        + [pltpu.VMEM(out.shape, out.dtype) for out in kept]
        + [pltpu.SemaphoreType.DMA((2 * STEPS + 2,)), pltpu.SemaphoreType.DMA((9,))],
        flops=2 * SLOT * D * (D + 2 * FF + 2 * D),
    )


def ffn_back_kernel(
    branch_ref, g2_ref, gfinal_any, after_any, slope_any, out_any, in_any, wo_any,
    ginner_any, gafter_any, low_any, gmixed_any, gain_ref,
    gfinal_ref, after_ref, slope_ref, out_ref, in_ref, wo_ref, ginner_ref, gafter_ref, low_ref, gmixed_ref,
    sems, out_sems,
):
    pairs = []
    for k in range(STEPS):
        pairs += [(out_any.at[chunk(k)], out_ref.at[k]), (slope_any.at[:, chunk(k)], slope_ref.at[k])]
        pairs += [(in_any.at[:, chunk(k)], in_ref.at[k])]
    copies = copy_all(pairs + [(after_any, after_ref), (gfinal_any, gfinal_ref), (wo_any, wo_ref)], sems)
    begin(copies[:4])
    branch = branch_ref[...]
    copies[0].wait()
    begin(copies[4:7])
    grad = right_product(branch, out_ref[0])
    total = None
    sent = []
    for k in range(STEPS):
        copies[3 * k + 1].wait()
        copies[3 * k + 2].wait()
        copies[3 * k + 3].wait()
        begin(copies[3 * k + 7 : 3 * k + 10])
        following = right_product(branch, out_ref[k + 1]) if k + 1 < STEPS else None
        inner = (grad * slope_ref[k].astype(WIDER)).astype(LOWER)
        ginner_ref[:, chunk(k)] = inner
        term = right_product(inner, in_ref[k])
        total = term if total is None else total + term
        grad = following
        sent += send_out([(ginner_ref.at[:, chunk(k)], ginner_any.at[:, chunk(k)])], out_sems, len(sent))
    copies[3 * STEPS + 1].wait()
    copies[3 * STEPS + 2].wait()
    back, gain = norm_pull(after_ref[...], row_of(g2_ref), total)
    gain_ref[...] = gain
    g_after = gfinal_ref[...] + back
    gafter_ref[...] = g_after
    low = g_after.astype(LOWER)
    low_ref[...] = low
    sent += send_out([(gafter_ref, gafter_any), (low_ref, low_any)], out_sems, len(sent))
    gmixed_ref[...] = right_product(low, wo_ref[...]).astype(LOWER)
    sent += send_out([(gmixed_ref, gmixed_any)], out_sems, len(sent))
    for copy in sent:
        copy.wait()


def ffn_back(branch, ffn_out, slope, ffn_in, after_rows, gain2, g_final, wo, after=()):
    outs = [narrow(SLOT, FF), wide(SLOT, D), narrow(SLOT, D), narrow(SLOT, D)]
    return run(
        "enc_ffn_back",
        ffn_back_kernel,
        [branch, gain2, g_final, after_rows, slope, ffn_out, ffn_in, wo],
        [WHOLE] * 2 + [ANY] * 6,
        outs + [wide(1, D)],
        [ANY] * 4 + [WHOLE],
        after=after,
        scratch=[
            pltpu.VMEM((SLOT, D), WIDER),
            pltpu.VMEM((SLOT, D), WIDER),
            pltpu.VMEM((STEPS, SLOT, WIDTH), LOWER),
            pltpu.VMEM((STEPS, WIDTH, D), LOWER),
            pltpu.VMEM((STEPS, D, WIDTH), LOWER),
            pltpu.VMEM((D, D), LOWER),
        ]
        + [pltpu.VMEM(out.shape, out.dtype) for out in outs]
        + [pltpu.SemaphoreType.DMA((3 * STEPS + 3,)), pltpu.SemaphoreType.DMA((STEPS + 3,))],
        flops=2 * SLOT * D * (D + 2 * FF),
    )


def attention_end(
    count, table, pick, heads, grad_mixed, mixed, stats, begun, diagonal, qkv, x, gain1,
    g_after, gain2, gain3, pick_back, after=(),
):
    base = FIRST
    half = PAIRS - FIRST
    inner = attn_bwd_kernel(base)

    def body(
        n_ref, ends_ref, table_ref, pick_ref, h_ref, g_ref, o_ref, st_ref, begun_any,
        da_ref, x_ref, g1_ref, gain2_ref, gain3_ref, back_ref, qkv_any, gafter_any,
        gh_any, small_ref, gb_ref, grows_any,
        u_ref, gh_ref, gall_ref, w_ref, gafter_ref, grows_ref, sems, out_sems,
    ):
        step = pl.program_id(0)
        old = slice(0, base * PAIR)
        loads = copy_all([(begun_any.at[:, :, old], gall_ref.at[:, :, old]), (qkv_any, w_ref), (gafter_any, gafter_ref)], sems)

        @pl.when(step == 0)
        def _():
            for load in loads:
                load.start()

        inner(n_ref, ends_ref, table_ref, pick_ref, h_ref, g_ref, o_ref, st_ref, gh_ref, gb_ref, u_ref)
        for k in range(half):

            @pl.when(step == k)
            def _():
                place = slice((base + k) * PAIR, (base + k + 1) * PAIR)
                gall_ref[:, :, place] = gh_ref[...]
                sums_ref = gb_ref.at[0]
                small_ref[2 * k : 2 * k + 2] = sums_ref[:2]

        @pl.when(step == half - 1)
        def _():
            new = slice(base * PAIR, D)
            sent = send_out([(gall_ref.at[:, :, new], gh_any.at[:, :, new])], out_sems, 0)
            for load in loads:
                load.wait()
            total = right_product(gall_ref[0], w_ref[:, :D])
            total = total + right_product(gall_ref[1], w_ref[:, D : 2 * D])
            total = total + right_product(gall_ref[2], w_ref[:, 2 * D :])
            back, gain = norm_pull(x_ref[...].astype(WIDER), row_of(g1_ref), total)
            grows_ref[...] = gafter_ref[...] + back
            sent += send_out([(grows_ref, grows_any)], out_sems, 1)
            sums = [da_ref[k, :2] for k in range(base)]
            sums += [small_ref[2 * k : 2 * k + 2] for k in range(half)]
            found = split_product(jnp.concatenate(sums, axis=0), back_ref[...], 2)
            small_ref[...] = jnp.zeros((16, D + 2 * EDGE), WIDER)
            small_ref[0:1, :D] = gain
            small_ref[1:2, :D] = gain2_ref[...]
            small_ref[2:3, :D] = gain3_ref[...]
            small_ref[4:16, :STAT] = found
            for copy in sent:
                copy.wait()

    rows = whole(SLOT, D)
    grads, small, unused, g_rows, token = run(
        "enc_attention_end",
        body,
        [count, table, table, pick, heads, grad_mixed, mixed, stats, begun]
        + [diagonal, x, gain1, gain2, gain3, pick_back, qkv, g_after],
        [SCALARS, SCALARS, WHOLE, WHOLE, pair_of_all(base), columns_at(base), columns_at(base), stats_at(base), ANY]
        + [whole(*diagonal.shape), rows, whole(D), whole(1, D), whole(1, D), whole(4 * SPAN, STAT), ANY, ANY],
        [narrow(3, SLOT, D), wide(16, D + 2 * EDGE), wide(half, 8, 4 * SPAN), wide(SLOT, D)],
        [ANY, whole(16, D + 2 * EDGE), pl.BlockSpec((1, 8, 4 * SPAN), lambda s: (s, 0, 0)), ANY],
        after=after,
        grid=(half,),
        scratch=[
            pltpu.VMEM((H, 3 * SPAN), WIDER),
            pltpu.VMEM((3, SLOT, PAIR), LOWER),
            pltpu.VMEM((3, SLOT, D), LOWER),
            pltpu.VMEM((D, 3 * D), LOWER),
            pltpu.VMEM((SLOT, D), WIDER),
            pltpu.VMEM((SLOT, D), WIDER),
            pltpu.SemaphoreType.DMA((3,)),
            pltpu.SemaphoreType.DMA((2,)),
        ],
        flops=2 * 5 * H * SLOT * SLOT * HD * 4,
        alias={8: 0},
    )
    return g_rows, small, unused, grads, token


def head_lanes(h):
    lanes = lax.broadcasted_iota(jnp.int32, (GROUP, D), 1)
    return (lanes >= h * HD) & (lanes < (h + 1) * HD)


def stack_heads(flat):
    return jnp.concatenate([jnp.where(head_lanes(h), flat, 0.0) for h in range(H)], axis=0)


def merge_heads(stacked):
    total = jnp.zeros((GROUP, D), WIDER)
    for h in range(H):
        total = total + jnp.where(head_lanes(h), stacked[GROUP * h : GROUP * h + GROUP], 0.0)
    return total


def lanes_to_column(stat):
    lanes = lax.broadcasted_iota(jnp.int32, (GROUP, STAT), 1)
    parts = [jnp.sum(jnp.where(lanes == h, stat, 0.0), axis=1, keepdims=True) for h in range(H)]
    return jnp.concatenate(parts, axis=0)


def column_to_lanes(column, first):
    lanes = lax.broadcasted_iota(jnp.int32, (GROUP, STAT), 1)
    total = jnp.zeros((GROUP, STAT), WIDER)
    for h in range(H):
        total = total + jnp.where(lanes == first + h, column[GROUP * h : GROUP * h + GROUP], 0.0)
    return total


def spread_heads(stat):
    rows = lax.broadcasted_iota(jnp.int32, (STAT, D), 0) * HD
    lanes = lax.broadcasted_iota(jnp.int32, (STAT, D), 1)
    spread = jnp.where((lanes >= rows) & (lanes < rows + HD), 1.0, 0.0).astype(LOWER)
    return split_product(stat, spread, 2)


def own_scores(query, keys, table_ref):
    raw = right_product(query, keys)
    rows = lax.broadcasted_iota(jnp.int32, (GROUP, GROUP), 0)
    columns = lax.broadcasted_iota(jnp.int32, (GROUP, GROUP), 1)
    away = rows - columns
    parts = []
    for h in range(H):
        bias = jnp.full((GROUP, GROUP), table_ref[h, 0], WIDER)
        for d in range(1, GROUP):
            bias = jnp.where(away == d, table_ref[h, d], bias)
        part = raw[GROUP * h : GROUP * h + GROUP] + bias
        parts.append(jnp.where(away >= 0, part, MASKED))
    scores = jnp.concatenate(parts, axis=0)
    powers = jnp.exp(scores - jnp.max(scores, axis=1, keepdims=True))
    return powers / jnp.sum(powers, axis=1, keepdims=True)


def padded(ref, pad_ref):
    pad_ref[...] = jnp.zeros((GROUP, D), WIDER)
    pad_ref[:ANS] = ref[...].astype(WIDER)
    return pad_ref[...]


def answer_rows(width):
    return lax.broadcasted_iota(jnp.int32, (GROUP, width), 0) < ANS


def dec_self_kernel(
    table_ref, x_ref, g1_ref, g2_ref, qkv_any, out_any, query_any,
    after_ref, lefts_ref, heads_ref, query_ref,
    qkv_ref, out_ref, cross_ref, pad_ref, sems,
):
    copies = copy_all(((qkv_any, qkv_ref), (out_any, out_ref), (query_any, cross_ref)), sems)
    begin(copies[:2])
    start = padded(x_ref, pad_ref)
    first = (start * scale_of(start) * row_of(g1_ref)).astype(LOWER)
    copies[0].wait()
    begin(copies[2:])
    heads = product(first, qkv_ref[...]).astype(LOWER)
    heads_ref[...] = heads
    query = stack_heads(heads.astype(WIDER)[:, :D] * 0.125).astype(LOWER)
    probs = own_scores(query, heads[:, D : 2 * D], table_ref)
    own = merge_heads(product(probs.astype(LOWER), heads[:, 2 * D :]))
    own = jnp.where(answer_rows(D), own, 0.0).astype(LOWER)
    copies[1].wait()
    after = start + product(own, out_ref[...])
    after_ref[...] = after
    second = (after * scale_of(after) * row_of(g2_ref)).astype(LOWER)
    copies[2].wait()
    query_ref[...] = product(second, cross_ref[...]).astype(LOWER)
    lefts_ref[:, :D] = first
    lefts_ref[:, D : 2 * D] = own
    lefts_ref[:, 2 * D :] = second


def masked_cross(n_ref, query_ref, pairs_ref):
    query = stack_heads(query_ref[...].astype(WIDER) * 0.125).astype(LOWER)
    raw = right_product(query, pairs_ref[:, :D])
    places = lax.broadcasted_iota(jnp.int32, (STACK, SLOT), 1)
    return query, jnp.where(places < n_ref[0], raw, MASKED)


def cross_kernel(n_ref, query_ref, pairs_ref, packed_ref):
    unused, scores = masked_cross(n_ref, query_ref, pairs_ref)
    top = jnp.max(scores, axis=1, keepdims=True)
    powers = jnp.exp(scores - top)
    total = jnp.sum(powers, axis=1, keepdims=True)
    probs = (powers / total).astype(LOWER)
    packed_ref[:, :D] = merge_heads(product(probs, pairs_ref[:, D:]))
    packed_ref[:, D:] = column_to_lanes(top, 0) + column_to_lanes(total, STAT // 2)


def dec_mid_kernel(
    n_ref, parts_ref, after_ref, cot_ref, g3_ref, lefts_ref, query_ref, e3_ref,
    pairs_any, cross_any, in_any, out_any, kv_any, final_any,
    answer_ref, early_ref, gmid_ref, gain_ref, partial_ref, gain_enc_ref, gpairs_any, gfinal_any, branch_any,
    pairs_ref, cross_ref, in_ref, out_ref, kv_ref, final_ref, gpairs_ref, gfinal_ref, branch_ref, pad_ref,
    sems, out_sems,
):
    held_pairs = ((cross_any, cross_ref), (in_any, in_ref), (out_any, out_ref), (pairs_any, pairs_ref))
    copies = copy_all(held_pairs + ((kv_any, kv_ref), (final_any, final_ref)), sems)
    begin(copies[:2])
    size = parts_ref.shape[0]
    used = lax.broadcasted_iota(jnp.int32, (GROUP, STAT), 1) < H
    tops = [parts_ref[k, :, D:] for k in range(size)]
    totals = [pltpu.roll(stat, STAT // 2, 1) for stat in tops]
    top = tops[0]
    for k in range(1, size):
        top = jnp.maximum(top, tops[k])
    weights = [jnp.where(used, totals[k] * jnp.exp(tops[k] - top), 0.0) for k in range(size)]
    total = weights[0]
    for k in range(1, size):
        total = total + weights[k]
    total = jnp.where(used, total, 1.0)
    mix = jnp.zeros((GROUP, D), WIDER)
    for k in range(size):
        mix = mix + parts_ref[k, :, :D] * spread_heads(weights[k] / total)
    mix_low = mix.astype(LOWER)
    copies[0].wait()
    begin(copies[2:3])
    middle = after_ref[...] + product(mix_low, cross_ref[...])
    third = (middle * scale_of(middle) * row_of(g3_ref)).astype(LOWER)
    copies[1].wait()
    begin(copies[3:])
    inner = product(third, in_ref[...])
    value, slope = silu_like(inner)
    hidden = value.astype(LOWER)
    copies[2].wait()
    answer = (middle + product(hidden, out_ref[...])).astype(LOWER)
    answer_ref[...] = answer[:ANS]
    grad = padded(cot_ref, pad_ref)
    out_low = grad.astype(LOWER)
    g_inner = (right_product(out_low, out_ref[...]) * slope).astype(LOWER)
    back, gain = norm_pull(middle, row_of(g3_ref), right_product(g_inner, in_ref[...]))
    gain_ref[...] = gain
    g_middle = grad + back
    gmid_ref[...] = g_middle
    middle_low = g_middle.astype(LOWER)
    g_mix = right_product(middle_low, cross_ref[...]).astype(LOWER)

    def store(name, rows):
        early_ref[:, AT[name] : AT[name] + rows.shape[1]] = rows

    def kept(rows):
        return jnp.where(answer_rows(rows.shape[1]), rows.astype(WIDER), 0.0).astype(LOWER)

    early_ref[:, : 3 * D] = kept(lefts_ref[...])
    store("mix", kept(mix_low))
    store("third", kept(third))
    store("hidden", kept(hidden))
    store("g_middle", middle_low)
    store("g_inner", g_inner)
    store("g_out", out_low)
    copies[3].wait()
    copies[4].wait()
    copies[5].wait()
    query, scores = masked_cross(n_ref, query_ref, pairs_ref)
    probs = jnp.exp(scores - lanes_to_column(jnp.where(used, top, 0.0))) / lanes_to_column(total)
    grad = stack_heads(g_mix.astype(WIDER))
    weighted = jnp.sum(grad * jnp.concatenate([mix] * H, axis=0), axis=1, keepdims=True)
    grad = grad.astype(LOWER)
    grad_probs = right_product(grad, pairs_ref[:, D:])
    rounded = (probs * (grad_probs - weighted)).astype(LOWER)
    g_keys = left_product(rounded, query).astype(LOWER)
    g_values = left_product(probs.astype(LOWER), grad).astype(LOWER)
    gpairs_ref[:, :D] = g_keys
    gpairs_ref[:, D:] = g_values
    sent = send_out([(gpairs_ref, gpairs_any)], out_sems, 0)
    partial_ref[...] = merge_heads(product(rounded, pairs_ref[:, :D])) * 0.125
    g_third = right_product(g_keys, kv_ref[:, :D]) + right_product(g_values, kv_ref[:, D:])
    back, gain = norm_pull(final_ref[...], row_of(e3_ref), g_third)
    gain_enc_ref[...] = gain
    gfinal_ref[...] = back
    branch_ref[...] = back.astype(LOWER)
    sent += send_out([(gfinal_ref, gfinal_any), (branch_ref, branch_any)], out_sems, 1)
    for copy in sent:
        copy.wait()


def dec_back_kernel(
    table_ref, x_ref, part_ref, got_ref, after_ref, gmid_ref, heads_ref,
    g1_ref, g2_ref, gain3_ref, query_any, out_any, qkv_any,
    late_ref, gstart_ref,
    cross_ref, out_ref, qkv_ref, pad_ref, sems,
):
    copies = copy_all(((query_any, cross_ref), (out_any, out_ref), (qkv_any, qkv_ref)), sems)
    begin(copies[:2])
    g_query = (part_ref[...] + got_ref[...]).astype(LOWER)
    copies[0].wait()
    begin(copies[2:])
    back, gain2 = norm_pull(after_ref[...], row_of(g2_ref), right_product(g_query, cross_ref[...]))
    g_after = gmid_ref[...] + back
    after_low = g_after.astype(LOWER)
    copies[1].wait()
    g_own = stack_heads(right_product(after_low, out_ref[...])).astype(LOWER)
    heads = heads_ref[...]
    query = stack_heads(heads.astype(WIDER)[:, :D] * 0.125).astype(LOWER)
    probs = own_scores(query, heads[:, D : 2 * D], table_ref)
    grad_probs = right_product(g_own, heads[:, 2 * D :])
    rounded = (probs * (grad_probs - jnp.sum(probs * grad_probs, axis=1, keepdims=True))).astype(LOWER)
    g_q = (merge_heads(product(rounded, heads[:, D : 2 * D])) * 0.125).astype(LOWER)
    g_k = left_product(rounded, query).astype(LOWER)
    g_v = left_product(probs.astype(LOWER), g_own).astype(LOWER)
    g_heads = jnp.concatenate([g_q, g_k, g_v], axis=1)
    copies[2].wait()
    start = padded(x_ref, pad_ref)
    back, gain1 = norm_pull(start, row_of(g1_ref), right_product(g_heads, qkv_ref[...]))
    gstart_ref[...] = (g_after + back)[:ANS]
    spread = rounded.astype(WIDER)
    rows = lax.broadcasted_iota(jnp.int32, (GROUP, GROUP), 0)
    columns = lax.broadcasted_iota(jnp.int32, (GROUP, GROUP), 1)
    mirror = jnp.where(rows + columns == GROUP - 1, 1.0, 0.0).astype(LOWER)
    empty = jnp.zeros((GROUP, STAT - GROUP), WIDER)
    tables = []
    for h in range(H):
        part = product(mirror, spread[GROUP * h : GROUP * h + GROUP].astype(LOWER))
        turned = pltpu.roll(jnp.concatenate([part, empty], axis=1), 0, 1, stride=1, stride_axis=0)
        tables.append(jnp.sum(turned, axis=0, keepdims=True))
    small = jnp.concatenate([gain1, gain2, gain3_ref[...]] + tables, axis=1)
    places = lax.broadcasted_iota(jnp.int32, (GROUP, LATE), 0)
    late = jnp.concatenate([g_heads, after_low, g_query], axis=1).astype(WIDER)
    late_ref[...] = jnp.where(places == ANS, small, late).astype(LOWER)


def dec_outer_kernel(size):
    part = D // size

    def body(me_ref, *refs):
        me = me_ref[0]
        small_ref = refs[9]
        there, here = refs[3:9], refs[10:16]
        early_ref, late_ref, sems = refs[16:]
        sent = []
        early_ref[...] = jnp.concatenate([refs[0][me ^ s].astype(WIDER) for s in range(size)], axis=0).astype(LOWER)
        late = [ref[...].astype(WIDER) for ref in refs[1:3]]
        late_ref[...] = jnp.concatenate(late, axis=0).astype(LOWER)
        rows = lax.broadcasted_iota(jnp.int32, (part, D), 0) + me * part
        lanes = lax.broadcasted_iota(jnp.int32, (part, D), 1)
        picked = jnp.where(rows == lanes, 1.0, 0.0).astype(LOWER)
        height = FF // size
        first = pl.multiple_of(AT["hidden"] + me * height, 128)

        def outer(k, name, right):
            left = right_product(picked, early_ref[:, AT[name] : AT[name] + D]).astype(LOWER)
            here[k][...] = product(left, right)
            sent.extend(send_out([(here[k], there[k])], sems, len(sent)))

        outer(4, "third", early_ref[:, AT["g_inner"] : AT["g_inner"] + FF])
        outer(0, "first", late_ref[:, : 3 * D])
        here[5][...] = left_product(early_ref[:, pl.ds(first, height)], early_ref[:, AT["g_out"] : AT["g_out"] + D])
        sent.extend(send_out([(here[5], there[5])], sems, len(sent)))
        outer(1, "own", late_ref[:, AT["g_after"] : AT["g_after"] + D])
        outer(2, "second", late_ref[:, AT["g_query"] : AT["g_query"] + D])
        outer(3, "mix", early_ref[:, AT["g_middle"] : AT["g_middle"] + D])
        total = jnp.zeros((1, LATE), WIDER)
        for part_late in late:
            for k in (0, GROUP):
                total = total + part_late[k + ANS : k + ANS + 1]
        small_ref[...] = total
        for copy in sent:
            copy.wait()

    return body


def held(*shapes):
    return [pltpu.VMEM(shape, LOWER) for shape in shapes] + [
        pltpu.VMEM((GROUP, D), WIDER),
        pltpu.SemaphoreType.DMA((len(shapes),)),
    ]


def dec_self(table, answers, gain1, gain2, qkv, out, query, after=()):
    return run(
        "dec_self",
        dec_self_kernel,
        [table, answers, gain1, gain2, qkv, out, query],
        [SCALARS] + [WHOLE] * 3 + [ANY] * 3,
        [wide(GROUP, D), narrow(GROUP, 3 * D), narrow(GROUP, 3 * D), narrow(GROUP, D)],
        after=after,
        scratch=held((D, 3 * D), (D, D), (D, D)),
        flops=10**9,
    )


def dec_mid(count, parts, after_rows, cotangent, gain3, lefts, query, enc_gain3, pairs, cross_out, ffn_in, ffn_out, kv, final, after=()):
    outs = [narrow(SLOT, 2 * D), wide(SLOT, D), narrow(SLOT, D)]
    shapes = [(SLOT, 2 * D), (D, D), (D, FF), (FF, D), (D, 2 * D)]
    return run(
        "dec_mid",
        dec_mid_kernel,
        [count, parts, after_rows, cotangent, gain3, lefts, query, enc_gain3, pairs, cross_out, ffn_in, ffn_out, kv, final],
        [SCALARS] + [WHOLE] * 7 + [ANY] * 6,
        [narrow(ANS, D), narrow(GROUP, EARLY), wide(GROUP, D), wide(1, D), wide(GROUP, D), wide(1, D)] + outs,
        [WHOLE] * 6 + [ANY] * 3,
        after=after,
        scratch=[pltpu.VMEM(shape, LOWER) for shape in shapes]
        + [pltpu.VMEM((SLOT, D), WIDER)]
        + [pltpu.VMEM(out.shape, out.dtype) for out in outs]
        + [pltpu.VMEM((GROUP, D), WIDER), pltpu.SemaphoreType.DMA((6,)), pltpu.SemaphoreType.DMA((3,))],
        flops=4 * 10**9,
    )


def dec_back(table, answers, part, got, after_rows, g_middle, heads, gain1, gain2, g_gain3, query, out, qkv, after=()):
    return run(
        "dec_back",
        dec_back_kernel,
        [table, answers, part, got, after_rows, g_middle, heads, gain1, gain2, g_gain3, query, out, qkv],
        [SCALARS] + [WHOLE] * 9 + [ANY] * 3,
        [narrow(GROUP, LATE), wide(ANS, D)],
        after=after,
        scratch=held((D, D), (D, D), (D, 3 * D)),
        flops=0,
    )


def dec_outer(me, early, late_one, late_two, size, after=()):
    part = D // size
    outs = [wide(part, 3 * D), wide(part, D), wide(part, D), wide(part, D), wide(part, FF), wide(FF // size, D)]
    return run(
        "dec_outer",
        dec_outer_kernel(size),
        [me, early, late_one, late_two],
        [SCALARS, WHOLE, WHOLE, WHOLE],
        outs + [wide(1, LATE)],
        [ANY] * 6 + [WHOLE],
        after=after,
        scratch=[pltpu.VMEM(out.shape, WIDER) for out in outs]
        + [pltpu.VMEM((size * GROUP, EARLY), LOWER), pltpu.VMEM((size * GROUP, LATE), LOWER), pltpu.SemaphoreType.DMA((6,))],
        flops=8 * 10**9,
    )


def stack_late(one, two, after=()):
    def body(one_ref, two_ref, out_ref):
        out_ref[...] = jnp.concatenate([one_ref[...].astype(WIDER), two_ref[...].astype(WIDER)], axis=0).astype(LOWER)

    return run("stack_late", body, [one, two], [WHOLE] * 2, [narrow(2 * GROUP, LATE)], after=after, flops=0)


PLACES = [(0, 0), (0, 1), (1, 0), (1, 1)]


def place_of(me, there):
    return me ^ (4 * there[0] + 2 * there[1])


def turned_rows(me, acts, block):
    lanes = lax.broadcasted_iota(jnp.int32, (block, D), 1)
    rows = lax.broadcasted_iota(jnp.int32, (block, D), 0)
    picked = [jnp.where(lanes - rows == place_of(me, t) * block, 1.0, 0.0).astype(LOWER) for t in PLACES]
    picked = jnp.concatenate(picked, axis=0)
    return jnp.concatenate([right_product(picked, act).astype(LOWER) for act in acts], axis=1)


def target(there, x_refs, y_refs):
    dy, dx = there
    return (x_refs[dx].at[dy], y_refs[dy].at[dx])


def pages_out(pairs, sems, first):
    return send_out([(here.at[k], there.at[k]) for here, there in pairs for k in range(2)], sems, first)


def one_kernel(
    me_ref, t_own, t_par, p_own, p_par, h_own, h_par, b_own, b_par, xk_any, xs_any, yk_any, ys_any,
    xk, xs, yk, ys, t, p, h, b, sems, out_sems,
):
    me = me_ref[0]
    block = FF // 8
    pairs = [(t_own, t.at[0]), (t_par, t.at[1]), (p_own, p.at[:SLOT]), (p_par, p.at[SLOT:])]
    pairs += [(b_own, b.at[:SLOT]), (b_par, b.at[SLOT:])]
    for k, there in enumerate(PLACES):
        lanes = pl.ds(pl.multiple_of(place_of(me, there) * block, 128), block)
        pairs += [(h_own.at[:, lanes], h.at[k, :SLOT]), (h_par.at[:, lanes], h.at[k, SLOT:])]
    copies = copy_all(pairs, sems)
    begin(copies[:4])
    copies[0].wait()
    copies[1].wait()
    begin(copies[4:8])
    height = D // 8
    left = turned_rows(me, (t[0], t[1]), height)
    copies[2].wait()
    copies[3].wait()
    begin(copies[8:])
    for c in range(2):
        grad = product(left, p[:, D * c : D * c + D]).astype(LOWER)
        for k, there in enumerate(PLACES):
            to, unused = target(there, (xk, xs), (yk, ys))
            to[height * c : height * c + height] = grad[height * k : height * k + height]
    for k in range(4, 8):
        copies[k].wait()
    sent = []
    for k, there in enumerate(PLACES):
        grad = left_product(h[k], b[...]).astype(LOWER)
        to_x, to_y = target(there, (xk, xs), (yk, ys))
        to_x[2 * height : 3 * height] = grad[:height]
        to_y[...] = grad[height:]
        out_x, out_y = target(there, (xk_any, xs_any), (yk_any, ys_any))
        if k + 1 < len(PLACES):
            copies[8 + 2 * k].wait()
            copies[9 + 2 * k].wait()
        sent += send_out([(to_x, out_x), (to_y, out_y)], out_sems, len(sent))
    for copy in sent:
        copy.wait()


def two_kernel(
    me_ref, s_own, s_par, i_own, i_par, m_own, m_par, l_own, l_par, xk_any, xs_any, yk_any, ys_any,
    xk, xs, yk, ys, s, i, m, l, sems, out_sems,
):
    me = me_ref[0]
    pairs = [(s_own, s.at[0]), (s_par, s.at[1]), (m_own, m.at[0]), (m_par, m.at[1])]
    pairs += [(l_own, l.at[:SLOT]), (l_par, l.at[SLOT:])]
    for c in range(4):
        lanes = slice(D * c, D * c + D)
        pairs += [(i_own.at[:, lanes], i.at[c, :SLOT]), (i_par.at[:, lanes], i.at[c, SLOT:])]
    copies = copy_all(pairs, sems)
    begin(copies[:6])
    for k in range(4):
        copies[k].wait()
    begin(copies[6:10])
    height = D // 8
    half = height // 2
    left = turned_rows(me, (m[0], m[1]), height)
    turned = turned_rows(me, (s[0], s[1]), height)
    copies[4].wait()
    copies[5].wait()
    begin(copies[10:])
    grad = product(left, l[...]).astype(LOWER)
    for k, there in enumerate(PLACES):
        for to, first in zip(target(there, (xk, xs), (yk, ys)), (0, half)):
            to[2 * height : 2 * height + half] = grad[height * k + first : height * k + first + half]
    sent = []
    for c in range(4):
        if c % 2 == 0:
            for k in range(6 + 2 * c, 10 + 2 * c):
                copies[k].wait()
        grad = product(turned, i[c]).astype(LOWER)
        for k, there in enumerate(PLACES):
            to = target(there, (xk, xs), (yk, ys))[c // 2]
            to[height * (c % 2) : height * (c % 2) + height] = grad[height * k : height * k + height]
        if c % 2:
            done = ((xk, xk_any), (xs, xs_any)) if c == 1 else ((yk, yk_any), (ys, ys_any))
            sent += pages_out(done, out_sems, len(sent))
    for copy in sent:
        copy.wait()


def three_kernel(
    me_ref, f_own, f_par, g_own, g_par, small_ref, got_ref, xk_any, xs_any, yk_any, ys_any,
    xk, xs, yk, ys, f, g, sems, out_sems,
):
    me = me_ref[0]
    small = (small_ref[:, :D] + got_ref[:, :D]).astype(LOWER)
    pairs = [(f_own, f.at[0]), (f_par, f.at[1])]
    for c in range(3):
        pairs += [(g_own.at[c], g.at[c, :SLOT]), (g_par.at[c], g.at[c, SLOT:])]
    copies = copy_all(pairs, sems)
    begin(copies[:4])
    copies[0].wait()
    copies[1].wait()
    begin(copies[4:])
    height = D // 8
    half = D // 2
    left = turned_rows(me, (f[0], f[1]), height)
    for ref in (xk, xs, yk, ys):
        for k in range(2):
            ref[k, height:] = jnp.zeros((16, 3 * half), LOWER)
            if ref is xk or ref is xs:
                ref[k, height:, :D] = small
    copies[2].wait()
    copies[3].wait()
    sent = []
    for c in range(3):
        if c == 1:
            for k in range(4, 8):
                copies[k].wait()
        grad = product(left, g[c]).astype(LOWER)
        for k, there in enumerate(PLACES):
            to_x, to_y = target(there, (xk, xs), (yk, ys))
            block = grad[height * k : height * k + height]
            if c == 0:
                to_x[:height, :D] = block
            elif c == 1:
                to_x[:height, D:] = block[:, :half]
                to_y[:height, :half] = block[:, half:]
            else:
                to_y[:height, half:] = block
        if c:
            done = ((xk, xk_any), (xs, xs_any)) if c == 1 else ((yk, yk_any), (ys, ys_any))
            sent += pages_out(done, out_sems, len(sent))
    for copy in sent:
        copy.wait()


def weight_call(name, body, me, ins, rows, columns, held_shapes, flops, after, extra=()):
    out = narrow(2, rows, columns)
    copies = {"weights_one": 14, "weights_two": 14, "weights_three": 8}[name]
    return run(
        name,
        body,
        [me, *ins, *extra],
        [SCALARS] + [ANY] * len(ins) + [WHOLE] * len(extra),
        [out] * 4,
        [ANY] * 4,
        after=after,
        scratch=[pltpu.VMEM(out.shape, LOWER)] * 4
        + [pltpu.VMEM(shape, LOWER) for shape in held_shapes]
        + [pltpu.SemaphoreType.DMA((copies,)), pltpu.SemaphoreType.DMA((8,))],
        flops=flops,
    )


def weights_one(me, third, g_pairs, hidden, branch, after=()):
    shapes = [(2, SLOT, D), (2 * SLOT, 2 * D), (4, 2 * SLOT, FF // 8), (2 * SLOT, D)]
    ins = (*third, *g_pairs, *hidden, *branch)
    return weight_call("weights_one", one_kernel, me, ins, 3 * D // 8, D, shapes, 4 * 10**9, after)


def weights_two(me, second, g_inner, mixed, low, after=()):
    shapes = [(2, SLOT, D), (4, 2 * SLOT, D), (2, SLOT, D), (2 * SLOT, D)]
    ins = (*second, *g_inner, *mixed, *low)
    return weight_call("weights_two", two_kernel, me, ins, 5 * D // 16, D, shapes, COST[6], after)


def weights_three(me, first, grads, small, after=()):
    shapes = [(2, SLOT, D), (3, 2 * SLOT, D)]
    ins = (*first, *grads)
    return weight_call("weights_three", three_kernel, me, ins, D // 8 + 16, 3 * D // 2, shapes, COST[4], after, small)


def page(array, k):
    return pl.BlockSpec((1,) + array.shape[1:], lambda s: (k, 0, 0))


def add_first(parts, flops=0, after=()):
    count = len(parts)

    def body(*refs):
        for k in range(count):
            refs[2 * count + k][...] = (refs[2 * k][0].astype(WIDER) + refs[2 * k + 1][0].astype(WIDER)).astype(LOWER)

    flat = [a for pair in parts for a in pair]
    outs = [narrow(*keep.shape[1:]) for keep, unused in parts]
    return run("add_first", body, flat, [page(a, 1) for a in flat], outs, after=after, grid=(1,), flops=flops)


def add_second(parts, side=False, after=()):
    shapes = [keep.shape[1:] for keep, unused, unused_too in parts]
    rows = shapes[0][0] + 16 if side else sum(shape[0] for shape in shapes)
    columns = sum(shape[1] for shape in shapes) if side else shapes[0][1]

    def body(*refs):
        out = refs[-1]
        first = 0
        for k, (high, across) in enumerate(shapes):
            keep, got, last = refs[3 * k : 3 * k + 3]
            total = (keep[0].astype(WIDER) + got[0].astype(WIDER) + last[...].astype(WIDER)).astype(LOWER)
            if side:
                out[:high, first : first + across] = total
                first += across
            else:
                out[first : first + high] = total
                first += high
        if side:
            out[rows - 16 :] = jnp.zeros((16, columns), LOWER)

    flat = [a for trio in parts for a in trio]
    specs = [page(a, 0) if a.ndim == 3 else WHOLE for a in flat]
    return run("add_second", body, flat, specs, [narrow(rows, columns)], after=after, grid=(1,), flops=0)


def add_pair(one, two, flops=0, after=()):
    def body(one_ref, two_ref, out_ref):
        out_ref[...] = (one_ref[...].astype(WIDER) + two_ref[...].astype(WIDER)).astype(LOWER)

    return run("add_pair", body, [one, two], [WHOLE] * 2, [narrow(*one.shape)], after=after, flops=flops)


def add_parts(share, parts, me, after=()):
    rows, columns = parts[0].shape

    def body(me_ref, share_ref, one_ref, two_ref, three_ref, out_ref):
        first = pl.multiple_of(me_ref[0] * rows, 16)
        total = share_ref[pl.ds(first, rows), :].astype(WIDER) + one_ref[...].astype(WIDER)
        out_ref[...] = (total + two_ref[...].astype(WIDER) + three_ref[...].astype(WIDER)).astype(LOWER)

    return run("add_parts", body, [me, share, *parts], [SCALARS] + [WHOLE] * 4, [narrow(rows, columns)], after=after, flops=0)


def add_rows(one, two, after=()):
    def body(one_ref, two_ref, out_ref):
        out_ref[...] = one_ref[...] + two_ref[...]

    return run("add_rows", body, [one, two], [WHOLE] * 2, [wide(*one.shape)], after=after, flops=0)


def partner(axis, bit):
    return [(k, k ^ (1 << bit)) for k in range(lax.axis_size(axis))]


def swap(value, axis, bit):
    return lax.ppermute(value, axis, partner(axis, bit))


def all_sum(value, axis):
    for bit in range(lax.axis_size(axis).bit_length() - 1):
        value = value + swap(value, axis, bit)
    return value


def pa_order(turn):
    rest = lax.axis_size("pa").bit_length() - 2
    return [1 + (k + turn) % rest for k in range(rest)]


def both_cores(acts, turn):
    size = lax.axis_size("pa")
    me = lax.axis_index("pa")
    blocks = jnp.transpose(acts).reshape(size, acts.shape[1] // size, acts.shape[0])
    order = pa_order(turn)
    offsets = [
        sum(((k >> (len(order) - 1 - p)) & 1) << bit for p, bit in enumerate(order)) for k in range(size // 2)
    ]
    mine = jnp.concatenate([lax.dynamic_slice_in_dim(blocks, me ^ d, 1) for d in offsets])
    theirs = jnp.concatenate([lax.dynamic_slice_in_dim(blocks, me ^ d ^ 1, 1) for d in offsets])
    return mine, swap(theirs, "pa", 0)


def weight_part(acts, grads, first, last):
    total = None
    for act, grad in zip(acts, grads):
        act = act[first:last]
        term = product(act.reshape(-1, act.shape[2]), grad)
        total = term if total is None else total + term
    height = acts[0].shape[1]
    return total.astype(LOWER).reshape(last - first, height, -1)


def add_up(parts):
    total = parts[0].astype(WIDER)
    for part in parts[1:]:
        total = total + part.astype(WIDER)
    return total.astype(LOWER)


def share_over_pa(acts, grads, turn):
    size = acts[0].shape[0]
    keep = [weight_part(acts, grads, 0, size // 2)]
    send = weight_part(acts, grads, size // 2, size)
    for bit in pa_order(turn):
        keep.append(swap(send, "pa", bit))
        size //= 2
        if size > 1:
            send = add_up([part[size // 2 : size] for part in keep])
            keep = [part[: size // 2] for part in keep]
    return add_up([part[0] for part in keep])


def inward(share):
    return lax.ppermute(share, "pb", [(0, 1), (3, 2)])


def between(share):
    return lax.ppermute(share, "pb", [(1, 2), (2, 1)])


def outward(share):
    me = lax.axis_index("pb")
    got = lax.ppermute(share, "pb", [(1, 0), (2, 3)])
    return jnp.where((me == 1) | (me == 2), share, got).astype(WIDER)


def swap_parts(share):
    me = lax.axis_index("pb")
    quarters = share.reshape(4, share.shape[0] // 4, share.shape[1])
    return [
        lax.ppermute(lax.dynamic_index_in_dim(quarters, me ^ s, 0, False), "pb", [(k, k ^ s) for k in range(4)])
        for s in range(1, 4)
    ]


def spread_parts(total, token):
    me = lax.axis_index("pb")
    got = [total] + [lax.ppermute(total, "pb", [(k, k ^ s) for k in range(4)]) for s in range(1, 4)]
    return jnp.concatenate([lax.select_n(me ^ b, *got) for b in range(4)], axis=0).astype(WIDER)


def total_plain(share):
    return lax.psum(share, "pb").astype(WIDER)


def local(
    passages,
    lengths,
    answers,
    cotangent,
    enc_gain1,
    enc_qkv,
    enc_bias,
    enc_out,
    enc_gain2,
    enc_ffn_in,
    enc_ffn_out,
    enc_gain3,
    cross_kv,
    dec_gain1,
    dec_qkv,
    dec_bias,
    dec_out,
    dec_gain2,
    cross_query,
    cross_out,
    dec_gain3,
    dec_ffn_in,
    dec_ffn_out,
):
    pa_size = lax.axis_size("pa")
    pb_size = lax.axis_size("pb")
    fast = pa_size == 8 and pb_size == 4
    me = lax.axis_index("pa").astype(jnp.int32).reshape(1)
    x = passages.reshape(SLOT, D)
    count = lengths.reshape(1)
    table = jnp.transpose(enc_bias)
    dec_table = jnp.transpose(dec_bias)
    pick = jnp.asarray(PICK, LOWER)
    pick_back = jnp.asarray(PICK_BACK, LOWER)

    def across(value):
        return value, swap(value, "pa", 0)

    dec_after, lefts, dec_heads, query, token = dec_self(
        dec_table, answers[0], dec_gain1, dec_gain2, dec_qkv, dec_out, cross_query
    )
    first, heads, mixed, stats, packed, after, second, slope, hidden, final, third, pairs, token = forward(
        count, table, pick, x, enc_gain1, enc_qkv, enc_gain2, enc_gain3, query, enc_out, enc_ffn_in, enc_ffn_out, cross_kv,
        after=[token],
    )
    if fast:
        acts = [across(value) for value in (first, mixed, second, hidden, third)]
    else:
        acts = [both_cores(v, k % 2) for k, v in enumerate((first, mixed, second, hidden, third))]
    gathered = lax.all_gather(packed, "pa")
    answer, early, g_middle, g_gain3, partial, g_enc_gain3, g_pairs, g_final, branch, token = dec_mid(
        count, gathered, dec_after, cotangent[0], dec_gain3, lefts, query, enc_gain3, pairs,
        cross_out, dec_ffn_in, dec_ffn_out, cross_kv, final,
        after=[got for unused, got in acts[:4]],
    )
    early_all = lax.all_gather(early, "pb")
    g_inner, g_after, low, g_mixed, g_enc_gain2, token = ffn_back(
        branch, enc_ffn_out, slope, enc_ffn_in, after, enc_gain2, g_final, enc_out, after=[token]
    )

    def back_of(base, pairs, after):
        return attention_back(count, table, pick, heads, g_mixed, mixed, stats, base, pairs, after=after)

    def dec_end(part, got, token, wait=()):
        return dec_back(
            dec_table, answers[0], part, got, dec_after, g_middle, dec_heads,
            dec_gain1, dec_gain2, g_gain3, cross_query, dec_out, dec_qkv, after=[token, *wait],
        )

    def rows_end(grads, diagonal, token, wait=()):
        return attention_end(
            count, table, pick, heads, g_mixed, mixed, stats, grads, diagonal, enc_qkv, x, enc_gain1,
            g_after, g_enc_gain2, g_enc_gain3, pick_back, after=[token, *wait],
        )

    pb_me = lax.axis_index("pb").astype(jnp.int32).reshape(1)

    def outer_end(token, late_one, late_two):
        *outer, token = dec_outer(pb_me, early_all, late_one, late_two, pb_size, after=[token])
        return outer, token

    if fast:
        partial, token = add_rows(partial, swap(partial, "pa", 0), after=[token])
        got = swap(partial, "pa", 1)
        xk, xs, yk, ys, token = weights_one(me, acts[4], across(g_pairs), acts[3], across(branch), after=[token])
        one = ((xk, swap(xs, "pa", 1)), (yk, swap(ys, "pa", 2)))
        partial, token = add_rows(partial, got, after=[token])
        got = swap(partial, "pa", 2)
        grads, diagonal_a, token = back_of(0, FIRST, [token])
        late, g_start, token = dec_end(partial, got, token)
        late_near = swap(late, "pb", 0)
        send_x, send_y, token = add_first(one, flops=COST[5], after=[token, early_all])
        last = (swap(send_x, "pa", 2), swap(send_y, "pa", 1))
        late, token = stack_late(late, late_near, after=[token])
        late_far = swap(late, "pb", 1)
        xk, xs, yk, ys, token = weights_two(me, acts[2], across(g_inner), acts[1], across(low), after=[token])
        two = ((xk, swap(xs, "pa", 1)), (yk, swap(ys, "pa", 2)))
        share_one, token = add_second([one[0] + last[:1], one[1] + last[1:]], after=[token])
        got_one = inward(share_one)
        g_rows, small, diagonal_a, grads, token = rows_end(grads, diagonal_a, token, [late_far])
        there, got_small = swap(grads, "pa", 0), swap(small, "pa", 0)
        send_x, send_y, token = add_first(two, flops=COST[0], after=[token])
        last = (swap(send_x, "pa", 2), swap(send_y, "pa", 1))
        share_one, token = add_pair(share_one, got_one, flops=COST[1], after=[token])
        got_one = between(share_one)
        xk, xs, yk, ys, token = weights_three(me, acts[0], (grads, there), (small, got_small), after=[token])
        three = ((xk, swap(xs, "pa", 1)), (yk, swap(ys, "pa", 2)))
        share_two, token = add_second([two[0] + last[:1], two[1] + last[1:]], after=[token])
        got_two = inward(share_two)
        share_one, token = add_pair(share_one, got_one, flops=COST[2], after=[token])
        total_one = outward(share_one)
        send_x, send_y, token = add_first(three, after=[token])
        last = (swap(send_x, "pa", 2), swap(send_y, "pa", 1))
        share_two, token = add_pair(share_two, got_two, flops=COST[3], after=[token])
        got_two = between(share_two)
        share_three, token = add_second([three[0] + last[:1], three[1] + last[1:]], side=True, after=[token])
        parts = swap_parts(share_three)
        outer, token = outer_end(token, late, late_far)
        share_two, token = add_pair(share_two, got_two, after=[token])
        total_two = outward(share_two)
        total_three = spread_parts(*add_parts(share_three, parts, pb_me, after=[token, total_one]))
        small = total_three[D // pa_size :, :D]
        block = D // pa_size
        total_kv = jnp.concatenate([total_one[:block], total_one[block : 2 * block]], axis=1)
        total_ffn_out = total_one[2 * block :]
        second_part = 2 * block + block // 2
        total_ffn_in = jnp.concatenate(
            [total_two[first : first + block] for first in (0, block, second_part, second_part + block)], axis=1
        )
        total_out = jnp.concatenate([total_two[2 * block : second_part], total_two[second_part + 2 * block :]], axis=0)
        total_qkv = total_three[:block]
    else:
        partial = all_sum(partial, "pa")
        late, g_start, token = dec_end(partial, jnp.zeros_like(partial), token)
        late, token = stack_late(late, swap(late, "pb", 0), after=[token])
        late_far = swap(late, "pb", 1)
        grads, diagonal_a, token = back_of(0, FIRST, [token])
        g_rows, small, diagonal_a, grads, token = rows_end(grads, diagonal_a, token)
        outer, token = outer_end(token, late, late_far)
        small = all_sum(all_sum(small[:, :D], "pa"), "pb")
        g_heads = jnp.concatenate([grads[0], grads[1], grads[2]], axis=1)
        total_kv = total_plain(share_over_pa(acts[4], across(g_pairs), 0))
        total_ffn_out = total_plain(share_over_pa(acts[3], across(branch), 1))
        total_ffn_in = total_plain(share_over_pa(acts[2], across(g_inner), 0))
        total_out = total_plain(share_over_pa(acts[1], across(low), 1))
        total_qkv = total_plain(share_over_pa(acts[0], across(g_heads), 0))

    d_qkv, d_out, d_query, d_cross, d_in, d_ffn, dec_small = outer
    dec_small = dec_small[0]
    dec_bias_rows = dec_small[3 * D :].reshape(H, STAT)[:, GROUP - ANS : GROUP]
    dec_bias_all = jnp.pad(jnp.transpose(dec_bias_rows[:, ::-1]), ((0, BUCKETS - ANS), (0, 0)))

    def own_part(vector, axis):
        height = vector.shape[0] // lax.axis_size(axis)
        return lax.dynamic_slice_in_dim(vector, lax.axis_index(axis) * height, height, axis=0)

    return (
        answer[None],
        g_rows.reshape(1, 1, SLOT, D),
        g_start[None],
        own_part(small[0], "pa"),
        total_qkv,
        jnp.transpose(small[4:16, :BUCKETS]),
        total_out,
        own_part(small[1], "pa"),
        total_ffn_in,
        total_ffn_out,
        own_part(small[2], "pa"),
        total_kv,
        own_part(dec_small[:D], "pb"),
        d_qkv,
        own_part(dec_bias_all, "pb"),
        d_out,
        own_part(dec_small[D : 2 * D], "pb"),
        d_query,
        d_cross,
        own_part(dec_small[2 * D : 3 * D], "pb"),
        d_in,
        d_ffn,
    )


def solution(mesh):
    copied = P()
    in_specs = (
        P("pb", "pa", None, None),
        P("pb", "pa"),
        P("pb", None, None),
        P("pb", None, None),
    ) + (copied,) * 19
    by_pa, by_pa_rows = P("pa"), P("pa", None)
    by_pb, by_pb_rows = P("pb"), P("pb", None)
    out_specs = (
        P("pb", None, None),
        P("pb", "pa", None, None),
        P("pb", None, None),
        by_pa,
        by_pa_rows,
        copied,
        by_pa_rows,
        by_pa,
        by_pa_rows,
        by_pa_rows,
        by_pa,
        by_pa_rows,
        by_pb,
        by_pb_rows,
        by_pb_rows,
        by_pb_rows,
        by_pb,
        by_pb_rows,
        by_pb_rows,
        by_pb,
        by_pb_rows,
        by_pb_rows,
    )
    return jax.shard_map(local, mesh=mesh, in_specs=in_specs, out_specs=out_specs, check_vma=False)
```

```python
import jax
import jax.numpy as jnp
import numpy as np
from jax import lax
from jax.experimental import pallas as pl
from jax.experimental.pallas import tpu as pltpu
from jax.sharding import PartitionSpec as P

D = 768
H = 12
HD = 64
FF = 3072
BUCKETS = 32
ANS = 20
SLOT = 512
PAIR = 2 * HD
PAIRS = H // 2
EDGE = 128
STRIP = 256
SPAN = 256
GROUP = 24
COST = (4 * 10**9, 0, 4 * 10**9, 0, 4 * 10**9, 4 * 10**9, 4 * 10**9)
STACK = H * GROUP
STAT = 128
STEPS = 4
WIDTH = FF // STEPS
FIRST = 4
EPS = 1e-06
MASKED = -1000000000.0
C_GELU = 0.7978845608028654
LOWER = jnp.bfloat16
WIDER = jnp.float32
EARLY = 7 * D + 2 * FF
LATE = 5 * D
AT = {
    "first": 0,
    "own": D,
    "second": 2 * D,
    "mix": 3 * D,
    "third": 4 * D,
    "hidden": 5 * D,
    "g_middle": 5 * D + FF,
    "g_inner": 6 * D + FF,
    "g_out": 6 * D + 2 * FF,
    "g_heads": 0,
    "g_after": 3 * D,
    "g_query": 4 * D,
}


def tile_classes(away):
    rows = [np.clip(EDGE * d - away, -(BUCKETS // 2), BUCKETS // 2 - 1) + BUCKETS // 2 for d in (-1, 0, 1)]
    return np.eye(BUCKETS, dtype=np.float32)[np.concatenate(rows)]


LANES = np.arange(SPAN)
PICK = tile_classes(np.where(LANES < EDGE, LANES, LANES - SPAN)).T
ENDS = np.repeat(np.eye(BUCKETS, dtype=np.float32)[[0, BUCKETS - 1]], EDGE, axis=0)
PICK_BACK = np.pad(np.concatenate([tile_classes(LANES - (EDGE - 1)), ENDS]), ((0, 0), (0, STAT - BUCKETS)))

SCALARS = pl.BlockSpec(memory_space=pltpu.SMEM)
ANY = pl.BlockSpec(memory_space=pl.ANY)
WHOLE = pl.BlockSpec(memory_space=pltpu.VMEM)
TOKEN = (8, 128)


def wide(*shape):
    return jax.ShapeDtypeStruct(shape, WIDER)


def narrow(*shape):
    return jax.ShapeDtypeStruct(shape, LOWER)


def run(name, body, ins, in_specs, outs, out_specs=None, after=(), grid=(), scratch=(), flops=10**9, mib=63, alias=None):
    count, extra, results = len(ins), len(after), len(outs)
    if out_specs is None:
        out_specs = [WHOLE] * results
    zeros = (lambda *s: (0, 0)) if grid else (lambda: (0, 0))

    def wrapped(*refs):
        refs[count + extra + results][...] = jnp.zeros(TOKEN, WIDER)
        body(*refs[:count], *refs[count + extra : count + extra + results], *refs[count + extra + results + 1 :])

    got = pl.pallas_call(
        wrapped,
        grid=grid,
        out_shape=tuple(outs) + (wide(*TOKEN),),
        in_specs=list(in_specs) + [ANY] * extra,
        out_specs=tuple(out_specs) + (pl.BlockSpec(TOKEN, zeros),),
        scratch_shapes=list(scratch),
        input_output_aliases=alias or {},
        compiler_params=pltpu.CompilerParams(vmem_limit_bytes=mib * 2**20),
        cost_estimate=pl.CostEstimate(flops=10 * flops, bytes_accessed=1, transcendentals=0),
        name=name,
    )(*ins, *after)
    return got


def product(left, right):
    return jnp.dot(left, right, preferred_element_type=WIDER)


def left_product(left, right):
    return lax.dot_general(left, right, (((0,), (0,)), ((), ())), preferred_element_type=WIDER)


def right_product(left, right):
    return lax.dot_general(left, right, (((1,), (1,)), ((), ())), preferred_element_type=WIDER)


def split_product(left, right, terms):
    total = None
    for k in range(terms):
        part = left.astype(LOWER)
        left = left - part.astype(WIDER)
        term = product(part, right)
        total = term if total is None else total + term
    return total


def silu_like(inner):
    square = inner * inner
    tanh = jnp.tanh(inner * (C_GELU + (C_GELU * 0.044715) * square))
    half = 0.5 + 0.5 * tanh
    value = inner * half
    slope = half + value * (1.0 - tanh) * (C_GELU + (3.0 * C_GELU * 0.044715) * square)
    return value, slope


def row_of(ref):
    return ref[...].reshape(1, D)


def scale_of(values):
    return lax.rsqrt(jnp.mean(values * values, axis=-1, keepdims=True) + EPS)


def norm_pull(values, gain, grad):
    scale = scale_of(values)
    lifted = grad * gain
    inside = jnp.sum(values * lifted, axis=-1, keepdims=True)
    back = scale * lifted - values * (scale * scale * scale * inside * (1.0 / D))
    return back, jnp.sum(grad * values * scale, axis=0, keepdims=True)


def fetch(pairs, sems):
    copies = [pltpu.make_async_copy(s, t, sems.at[k]) for k, (s, t) in enumerate(pairs)]
    for copy in copies:
        copy.start()
    return copies


def copy_all(pairs, sems):
    return [pltpu.make_async_copy(s, t, sems.at[k]) for k, (s, t) in enumerate(pairs)]


def begin(copies):
    for copy in copies:
        copy.start()


def bias_tiles(u_ref, head):
    tiles = []
    for d in range(3):
        row = u_ref[pl.ds(head, 1), SPAN * d : SPAN * d + SPAN]
        spread = jnp.broadcast_to(row, (EDGE, SPAN))
        tiles.append(pltpu.roll(spread, 0, 1, stride=1, stride_axis=0)[:, :EDGE])
    return tiles


def key_masks(n):
    places = lax.broadcasted_iota(jnp.int32, (EDGE, EDGE), 0)
    return [jnp.where(places + EDGE * j < n, 0.0, MASKED) for j in range(SLOT // EDGE)]


def score_blocks(raw, tiles, masks, low, high, first):
    columns = []
    for c in range(STRIP // EDGE):
        blocks = []
        for j in range(SLOT // EDGE):
            block = raw[EDGE * j : EDGE * j + EDGE, EDGE * c : EDGE * c + EDGE]
            d = j - first - c
            block = block + (tiles[d + 1] if abs(d) <= 1 else (low if d < 0 else high))
            blocks.append(block + masks[j] if j > 0 else block)
        columns.append(blocks)
    return columns


def paved(columns, kind):
    return jnp.concatenate([jnp.concatenate([b.astype(kind) for b in blocks], axis=0) for blocks in columns], axis=1)


def fill_rows(table_ref, pick_ref, u_ref):
    @pl.when(pl.program_id(0) == 0)
    def _():
        u_ref[...] = split_product(table_ref[...], pick_ref[...], 3)


def attn_fwd_kernel(n_ref, ends_ref, table_ref, pick_ref, x_ref, g1_ref, wq_ref, wk_ref, wv_ref, first_ref, heads_ref, o_ref, st_ref, u_ref):
    fill_rows(table_ref, pick_ref, u_ref)
    step = pl.program_id(0)

    @pl.when(step == 0)
    def _():
        rows = x_ref[...].astype(WIDER)
        first_ref[...] = (rows * scale_of(rows) * row_of(g1_ref)).astype(LOWER)

    masks = key_masks(n_ref[0])
    first = first_ref[...]
    for k, w_ref in enumerate((wq_ref, wk_ref, wv_ref)):
        heads_ref[k] = product(first, w_ref[...]).astype(LOWER)
    q_ref, k_ref = heads_ref.at[0], heads_ref.at[1]
    values = jnp.transpose(heads_ref[2])
    ones = jnp.ones((16, SLOT), LOWER)
    mixed = []
    for h in range(2):
        head = 2 * step + h
        low, high = ends_ref[head, 0], ends_ref[head, BUCKETS - 1]
        tiles = bias_tiles(u_ref, head)
        cols = slice(HD * h, HD * h + HD)
        keys = k_ref[:, cols]
        left = jnp.concatenate([values[cols], ones], axis=0)
        strips = []
        for i in range(0, SLOT // EDGE, STRIP // EDGE):
            lanes = slice(EDGE * i, EDGE * i + STRIP)
            raw = right_product(keys, q_ref[lanes, cols] * 0.125)
            tops, powers = [], []
            for blocks in score_blocks(raw, tiles, masks, low, high, i):
                top = jnp.maximum(jnp.maximum(blocks[0], blocks[1]), jnp.maximum(blocks[2], blocks[3]))
                top = jnp.max(top, axis=0, keepdims=True)
                tops.append(top)
                powers.append([jnp.exp(block - top) for block in blocks])
            out = product(left, paved(powers, LOWER))
            total = out[HD : HD + 1]
            st_ref[0, h : h + 1, lanes] = jnp.concatenate(tops, axis=1) + jnp.log(total)
            strips.append(out[:HD] * (1.0 / total))
        mixed.append(jnp.concatenate(strips, axis=1))
    lanes = pl.ds(pl.multiple_of(step * PAIR, PAIR), PAIR)
    o_ref[:, lanes] = jnp.transpose(jnp.concatenate(mixed, axis=0)).astype(LOWER)


def attn_bwd_kernel(base):
    def body(
        n_ref, ends_ref, table_ref, pick_ref, h_ref, g_ref, o_ref, st_ref, gh_ref, gb_ref, u_ref
    ):
        q_ref, k_ref, v_ref = h_ref.at[0], h_ref.at[1], h_ref.at[2]
        fill_rows(table_ref, pick_ref, u_ref)
        step = pl.program_id(0) + base
        masks = key_masks(n_ref[0])
        keys_t = jnp.transpose(k_ref[...])
        rows = lax.broadcasted_iota(jnp.int32, (EDGE, EDGE), 0)
        columns = lax.broadcasted_iota(jnp.int32, (EDGE, EDGE), 1)
        mirror = jnp.where(rows + columns == EDGE - 1, 1.0, 0.0).astype(LOWER)
        rows = lax.broadcasted_iota(jnp.int32, (16, SLOT), 0) * EDGE
        columns = lax.broadcasted_iota(jnp.int32, (16, SLOT), 1)
        places = jnp.where((columns >= rows) & (columns < rows + EDGE), 1.0, 0.0).astype(LOWER)
        rows = lax.broadcasted_iota(jnp.int32, (16, PAIR), 0) * HD
        columns = lax.broadcasted_iota(jnp.int32, (16, PAIR), 1)
        halves = jnp.where((columns >= rows) & (columns < rows + HD), 1.0, 0.0).astype(LOWER)
        met = g_ref[...].astype(WIDER) * o_ref[...].astype(WIDER)
        upper = met.astype(LOWER)
        lower = (met - upper.astype(WIDER)).astype(LOWER)
        weighted = right_product(halves, upper) + right_product(halves, lower)
        grad_queries = []
        gb_ref[0, 2:8, :] = jnp.zeros((6, 4 * SPAN), WIDER)
        for h in range(2):
            head = 2 * step + h
            low, high = ends_ref[head, 0], ends_ref[head, BUCKETS - 1]
            tiles = bias_tiles(u_ref, head)
            cols = slice(HD * h, HD * h + HD)
            keys = k_ref[:, cols]
            values = v_ref[:, cols]
            left = jnp.concatenate([keys_t[cols], places], axis=0)
            grad_keys = jnp.zeros((SLOT, HD), WIDER)
            grad_values = jnp.zeros((SLOT, HD), WIDER)
            strips = []
            sums = {}

            def gather(d, block):
                sums[d] = sums[d] + block if d in sums else block

            for i in range(0, SLOT // EDGE, STRIP // EDGE):
                lanes = slice(EDGE * i, EDGE * i + STRIP)
                query = q_ref[lanes, cols]
                grad = g_ref[lanes, cols]
                raw = right_product(keys, query * 0.125)
                grad_probs = right_product(values, grad)
                probs, changes = [], []
                for c, blocks in enumerate(score_blocks(raw, tiles, masks, low, high, i)):
                    part = slice(EDGE * (i + c), EDGE * (i + c) + EDGE)
                    total = st_ref[0, h : h + 1, part]
                    mean = weighted[h : h + 1, part]
                    probs.append([jnp.exp(block - total) for block in blocks])
                    changes.append([])
                    for j in range(SLOT // EDGE):
                        gap = grad_probs[EDGE * j : EDGE * j + EDGE, EDGE * c : EDGE * c + EDGE] - mean
                        change = probs[c][j] * gap
                        changes[c].append(change)
                        if abs(j - i - c) <= 1:
                            gather(j - i - c, change)
                rounded = paved(changes, LOWER)
                out = product(left, rounded)
                strips.append(out[:HD])
                for c in range(STRIP // EDGE):
                    for j in range(SLOT // EDGE):
                        if abs(j - i - c) > 1:
                            gather(2 if j > i + c else -2, out[HD + j : HD + j + 1, EDGE * c : EDGE * c + EDGE])
                grad_keys += product(rounded, query)
                grad_values += product(paved(probs, LOWER), grad)
            grad_queries.append(jnp.concatenate(strips, axis=1))
            gh_ref[1, :, cols] = (grad_keys * 0.125).astype(LOWER)
            gh_ref[2, :, cols] = grad_values.astype(LOWER)
            empty = jnp.zeros((EDGE, SPAN - EDGE), WIDER)
            band = jnp.concatenate([sums[-1], sums[0], sums[1]], axis=1)
            upper = band.astype(LOWER)
            lower = (band - upper.astype(WIDER)).astype(LOWER)
            mirrored = product(mirror, upper) + product(mirror, lower)
            for d in range(3):
                spread = jnp.concatenate([mirrored[:, EDGE * d : EDGE * d + EDGE], empty], axis=1)
                turned = pltpu.roll(spread, 0, 1, stride=1, stride_axis=0)
                gb_ref[0, h : h + 1, SPAN * d : SPAN * d + SPAN] = jnp.sum(turned, axis=0, keepdims=True)
            for place, d in ((3 * SPAN, -2), (3 * SPAN + EDGE, 2)):
                gb_ref[0, h : h + 1, place : place + EDGE] = sums[d]
        gh_ref[0] = (jnp.transpose(jnp.concatenate(grad_queries, axis=0)) * 0.125).astype(LOWER)

    return body


def columns_at(first):
    return pl.BlockSpec((SLOT, PAIR), lambda s: (0, first + s))


def stats_at(first):
    return pl.BlockSpec((1, 2, SLOT), lambda s: (first + s, 0, 0))


def pair_of_all(base):
    return pl.BlockSpec((3, SLOT, PAIR), lambda s: (0, 0, base + s))


def attention_back(count, table, pick, heads, grad_mixed, mixed, stats, base, half, after=()):
    return run(
        "enc_attention_back",
        attn_bwd_kernel(base),
        [count, table, table, pick, heads, grad_mixed, mixed, stats],
        [SCALARS, SCALARS, WHOLE, WHOLE, pair_of_all(base), columns_at(base), columns_at(base), stats_at(base)],
        [narrow(3, SLOT, D), wide(half, 8, 4 * SPAN)],
        [pair_of_all(base), pl.BlockSpec((1, 8, 4 * SPAN), lambda s: (s, 0, 0))],
        after=after,
        grid=(half,),
        scratch=[pltpu.VMEM((H, 3 * SPAN), WIDER)],
        flops=2 * 5 * H * SLOT * SLOT * HD * 4,
    )


def send_out(pairs, sems, first):
    copies = [pltpu.make_async_copy(s, t, sems.at[first + k]) for k, (s, t) in enumerate(pairs)]
    for copy in copies:
        copy.start()
    return copies


def chunk(k):
    return slice(WIDTH * k, WIDTH * k + WIDTH)


def forward_kernel(
    n_ref, ends_ref, table_ref, pick_ref, x_ref, g1_ref, wq_ref, wk_ref, wv_ref,
    g2_ref, g3_ref, dec_table_ref, ans_ref, dg1_ref, dg2_ref,
    wo_any, in_any, out_any, kv_any, dqkv_any, dout_any, dquery_any,
    first_ref, heads_ref, mixed_ref, st_ref, packed_ref, dec_after_ref, lefts_ref, dec_heads_ref, query_ref,
    after_any, second_any, slope_any, hidden_any, final_any, third_any, pairs_any,
    u_ref, wo_ref, in_ref, out_ref, kv_ref, dqkv_ref, dout_ref, dquery_ref, pad_ref,
    after_ref, second_ref, slope_ref, hidden_ref, final_ref, third_ref, pairs_ref,
    sems, dec_sems, out_sems,
):
    step = pl.program_id(0)
    dec_copies = copy_all([(dqkv_any, dqkv_ref), (dout_any, dout_ref), (dquery_any, dquery_ref)], dec_sems)
    pairs = [(wo_any, wo_ref)]
    for k in range(STEPS):
        pairs += [(in_any.at[:, chunk(k)], in_ref.at[k]), (out_any.at[chunk(k)], out_ref.at[k])]
    copies = copy_all(pairs + [(kv_any, kv_ref)], sems)

    @pl.when(step == 0)
    def _():
        begin(dec_copies + copies)

    attn_fwd_kernel(
        n_ref, ends_ref, table_ref, pick_ref, x_ref, g1_ref, wq_ref, wk_ref, wv_ref,
        first_ref, heads_ref, mixed_ref, st_ref, u_ref,
    )

    @pl.when(step == PAIRS - 2)
    def _():
        for copy in dec_copies:
            copy.wait()
        dec_self_part(
            dec_table_ref, ans_ref, dg1_ref, dg2_ref, dec_after_ref, lefts_ref, dec_heads_ref, query_ref,
            dqkv_ref, dout_ref, dquery_ref, pad_ref,
        )

    @pl.when(step == PAIRS - 1)
    def _():
        for copy in copies:
            copy.wait()
        after = x_ref[...].astype(WIDER) + product(mixed_ref[...], wo_ref[...])
        after_ref[...] = after
        second = (after * scale_of(after) * row_of(g2_ref)).astype(LOWER)
        second_ref[...] = second
        inner = product(second, in_ref[0])
        sent = send_out([(after_ref, after_any), (second_ref, second_any)], out_sems, 0)
        total = after
        for k in range(STEPS):
            following = product(second, in_ref[k + 1]) if k + 1 < STEPS else None
            value, slope = silu_like(inner)
            slope_ref[:, chunk(k)] = slope.astype(LOWER)
            hidden = value.astype(LOWER)
            hidden_ref[:, chunk(k)] = hidden
            total = total + product(hidden, out_ref[k])
            inner = following
            if k % 2:
                half = slice(WIDTH * (k - 1), WIDTH * (k + 1))
                sent += send_out(
                    [(slope_ref.at[:, half], slope_any.at[:, half]), (hidden_ref.at[:, half], hidden_any.at[:, half])],
                    out_sems, len(sent),
                )
        final_ref[...] = total
        third = (total * scale_of(total) * row_of(g3_ref)).astype(LOWER)
        third_ref[...] = third
        sent += send_out([(final_ref, final_any), (third_ref, third_any)], out_sems, len(sent))
        for k in range(2):
            half = slice(D * k, D * k + D)
            pairs_ref[:, half] = product(third, kv_ref[:, half]).astype(LOWER)
        sent += send_out([(pairs_ref, pairs_any)], out_sems, len(sent))
        cross_kernel(n_ref, query_ref, pairs_ref, packed_ref)
        for copy in sent:
            copy.wait()


def whole(*shape):
    return pl.BlockSpec(shape, lambda s: (0,) * len(shape))


def forward(count, table, pick, x, gain1, qkv, gain2, gain3, wo, ffn_in, ffn_out, kv, dec, after=()):
    def weights_at(first):
        return pl.BlockSpec((D, PAIR), lambda s: (0, first + s))

    kept = [wide(SLOT, D), narrow(SLOT, D), narrow(SLOT, FF), narrow(SLOT, FF), wide(SLOT, D), narrow(SLOT, D), narrow(SLOT, 2 * D)]
    return run(
        "enc_forward",
        forward_kernel,
        [count, table, table, pick, x, gain1, qkv, qkv, qkv, gain2, gain3, *dec[:4], wo, ffn_in, ffn_out, kv, *dec[4:]],
        [SCALARS, SCALARS, WHOLE, WHOLE, whole(SLOT, D), whole(D), weights_at(0), weights_at(PAIRS), weights_at(2 * PAIRS)]
        + [whole(D), whole(D), SCALARS, whole(ANS, D), whole(D), whole(D)] + [ANY] * 7,
        [narrow(SLOT, D), narrow(3, SLOT, D), narrow(SLOT, D), wide(PAIRS, 2, SLOT), wide(GROUP, D + STAT)]
        + [wide(GROUP, D), narrow(GROUP, 3 * D), narrow(GROUP, 3 * D), narrow(GROUP, D)] + kept,
        [whole(SLOT, D), pair_of_all(0), whole(SLOT, D), stats_at(0), whole(GROUP, D + STAT)]
        + [whole(GROUP, D), whole(GROUP, 3 * D), whole(GROUP, 3 * D), whole(GROUP, D)] + [ANY] * 7,
        after=after,
        grid=(PAIRS,),
        scratch=[
            pltpu.VMEM((H, 3 * SPAN), WIDER),
            pltpu.VMEM((D, D), LOWER),
            pltpu.VMEM((STEPS, D, WIDTH), LOWER),
            pltpu.VMEM((STEPS, WIDTH, D), LOWER),
            pltpu.VMEM((D, 2 * D), LOWER),
            pltpu.VMEM((D, 3 * D), LOWER),
            pltpu.VMEM((D, D), LOWER),
            pltpu.VMEM((D, D), LOWER),
            pltpu.VMEM((GROUP, D), WIDER),
        ]
        + [pltpu.VMEM(out.shape, out.dtype) for out in kept]
        + [pltpu.SemaphoreType.DMA((2 * STEPS + 2,)), pltpu.SemaphoreType.DMA((3,)), pltpu.SemaphoreType.DMA((9,))],
        flops=2 * SLOT * D * (D + 2 * FF + 2 * D),
    )


def ffn_back_kernel(
    branch_ref, g2_ref, gfinal_any, after_any, slope_any, out_any, in_any, wo_any,
    ginner_any, gafter_any, low_any, gmixed_any, gain_ref,
    gfinal_ref, after_ref, slope_ref, out_ref, in_ref, wo_ref, ginner_ref, gafter_ref, low_ref, gmixed_ref,
    sems, out_sems,
):
    pairs = []
    for k in range(STEPS):
        pairs += [(out_any.at[chunk(k)], out_ref.at[k]), (slope_any.at[:, chunk(k)], slope_ref.at[k])]
        pairs += [(in_any.at[:, chunk(k)], in_ref.at[k])]
    copies = copy_all(pairs + [(after_any, after_ref), (gfinal_any, gfinal_ref), (wo_any, wo_ref)], sems)
    begin(copies[:4])
    branch = branch_ref[...]
    copies[0].wait()
    begin(copies[4:7])
    grad = right_product(branch, out_ref[0])
    total = None
    sent = []
    for k in range(STEPS):
        copies[3 * k + 1].wait()
        copies[3 * k + 2].wait()
        copies[3 * k + 3].wait()
        begin(copies[3 * k + 7 : 3 * k + 10])
        following = right_product(branch, out_ref[k + 1]) if k + 1 < STEPS else None
        inner = (grad * slope_ref[k].astype(WIDER)).astype(LOWER)
        ginner_ref[:, chunk(k)] = inner
        term = right_product(inner, in_ref[k])
        total = term if total is None else total + term
        grad = following
        sent += send_out([(ginner_ref.at[:, chunk(k)], ginner_any.at[:, chunk(k)])], out_sems, len(sent))
    copies[3 * STEPS + 1].wait()
    copies[3 * STEPS + 2].wait()
    back, gain = norm_pull(after_ref[...], row_of(g2_ref), total)
    gain_ref[...] = gain
    g_after = gfinal_ref[...] + back
    gafter_ref[...] = g_after
    low = g_after.astype(LOWER)
    low_ref[...] = low
    sent += send_out([(gafter_ref, gafter_any), (low_ref, low_any)], out_sems, len(sent))
    gmixed_ref[...] = right_product(low, wo_ref[...]).astype(LOWER)
    sent += send_out([(gmixed_ref, gmixed_any)], out_sems, len(sent))
    for copy in sent:
        copy.wait()


def ffn_back(branch, ffn_out, slope, ffn_in, after_rows, gain2, g_final, wo, after=()):
    outs = [narrow(SLOT, FF), wide(SLOT, D), narrow(SLOT, D), narrow(SLOT, D)]
    return run(
        "enc_ffn_back",
        ffn_back_kernel,
        [branch, gain2, g_final, after_rows, slope, ffn_out, ffn_in, wo],
        [WHOLE] * 2 + [ANY] * 6,
        outs + [wide(1, D)],
        [ANY] * 4 + [WHOLE],
        after=after,
        scratch=[
            pltpu.VMEM((SLOT, D), WIDER),
            pltpu.VMEM((SLOT, D), WIDER),
            pltpu.VMEM((STEPS, SLOT, WIDTH), LOWER),
            pltpu.VMEM((STEPS, WIDTH, D), LOWER),
            pltpu.VMEM((STEPS, D, WIDTH), LOWER),
            pltpu.VMEM((D, D), LOWER),
        ]
        + [pltpu.VMEM(out.shape, out.dtype) for out in outs]
        + [pltpu.SemaphoreType.DMA((3 * STEPS + 3,)), pltpu.SemaphoreType.DMA((STEPS + 3,))],
        flops=2 * SLOT * D * (D + 2 * FF),
    )


def attention_end(
    count, table, pick, heads, grad_mixed, mixed, stats, begun, diagonal, qkv, x, gain1,
    g_after, gain2, gain3, pick_back, after=(),
):
    base = FIRST
    half = PAIRS - FIRST
    inner = attn_bwd_kernel(base)

    def body(
        n_ref, ends_ref, table_ref, pick_ref, h_ref, g_ref, o_ref, st_ref, begun_any,
        da_ref, x_ref, g1_ref, gain2_ref, gain3_ref, back_ref, qkv_any, gafter_any,
        gh_any, small_ref, gb_ref, grows_any,
        u_ref, gh_ref, gall_ref, w_ref, gafter_ref, grows_ref, sems, out_sems,
    ):
        step = pl.program_id(0)
        old = slice(0, base * PAIR)
        loads = copy_all([(begun_any.at[:, :, old], gall_ref.at[:, :, old]), (qkv_any, w_ref), (gafter_any, gafter_ref)], sems)

        @pl.when(step == 0)
        def _():
            for load in loads:
                load.start()

        inner(n_ref, ends_ref, table_ref, pick_ref, h_ref, g_ref, o_ref, st_ref, gh_ref, gb_ref, u_ref)
        for k in range(half):

            @pl.when(step == k)
            def _():
                place = slice((base + k) * PAIR, (base + k + 1) * PAIR)
                gall_ref[:, :, place] = gh_ref[...]
                sums_ref = gb_ref.at[0]
                small_ref[2 * k : 2 * k + 2] = sums_ref[:2]

        @pl.when(step == half - 1)
        def _():
            new = slice(base * PAIR, D)
            sent = send_out([(gall_ref.at[:, :, new], gh_any.at[:, :, new])], out_sems, 0)
            for load in loads:
                load.wait()
            total = right_product(gall_ref[0], w_ref[:, :D])
            total = total + right_product(gall_ref[1], w_ref[:, D : 2 * D])
            total = total + right_product(gall_ref[2], w_ref[:, 2 * D :])
            back, gain = norm_pull(x_ref[...].astype(WIDER), row_of(g1_ref), total)
            grows_ref[...] = gafter_ref[...] + back
            sent += send_out([(grows_ref, grows_any)], out_sems, 1)
            sums = [da_ref[k, :2] for k in range(base)]
            sums += [small_ref[2 * k : 2 * k + 2] for k in range(half)]
            found = split_product(jnp.concatenate(sums, axis=0), back_ref[...], 2)
            small_ref[...] = jnp.zeros((16, D + 2 * EDGE), WIDER)
            small_ref[0:1, :D] = gain
            small_ref[1:2, :D] = gain2_ref[...]
            small_ref[2:3, :D] = gain3_ref[...]
            small_ref[4:16, :STAT] = found
            for copy in sent:
                copy.wait()

    rows = whole(SLOT, D)
    grads, small, unused, g_rows, token = run(
        "enc_attention_end",
        body,
        [count, table, table, pick, heads, grad_mixed, mixed, stats, begun]
        + [diagonal, x, gain1, gain2, gain3, pick_back, qkv, g_after],
        [SCALARS, SCALARS, WHOLE, WHOLE, pair_of_all(base), columns_at(base), columns_at(base), stats_at(base), ANY]
        + [whole(*diagonal.shape), rows, whole(D), whole(1, D), whole(1, D), whole(4 * SPAN, STAT), ANY, ANY],
        [narrow(3, SLOT, D), wide(16, D + 2 * EDGE), wide(half, 8, 4 * SPAN), wide(SLOT, D)],
        [ANY, whole(16, D + 2 * EDGE), pl.BlockSpec((1, 8, 4 * SPAN), lambda s: (s, 0, 0)), ANY],
        after=after,
        grid=(half,),
        scratch=[
            pltpu.VMEM((H, 3 * SPAN), WIDER),
            pltpu.VMEM((3, SLOT, PAIR), LOWER),
            pltpu.VMEM((3, SLOT, D), LOWER),
            pltpu.VMEM((D, 3 * D), LOWER),
            pltpu.VMEM((SLOT, D), WIDER),
            pltpu.VMEM((SLOT, D), WIDER),
            pltpu.SemaphoreType.DMA((3,)),
            pltpu.SemaphoreType.DMA((2,)),
        ],
        flops=2 * 5 * H * SLOT * SLOT * HD * 4,
        alias={8: 0},
    )
    return g_rows, small, unused, grads, token


def head_lanes(h):
    lanes = lax.broadcasted_iota(jnp.int32, (GROUP, D), 1)
    return (lanes >= h * HD) & (lanes < (h + 1) * HD)


def stack_heads(flat):
    return jnp.concatenate([jnp.where(head_lanes(h), flat, 0.0) for h in range(H)], axis=0)


def merge_heads(stacked):
    total = jnp.zeros((GROUP, D), WIDER)
    for h in range(H):
        total = total + jnp.where(head_lanes(h), stacked[GROUP * h : GROUP * h + GROUP], 0.0)
    return total


def lanes_to_column(stat):
    lanes = lax.broadcasted_iota(jnp.int32, (GROUP, STAT), 1)
    parts = [jnp.sum(jnp.where(lanes == h, stat, 0.0), axis=1, keepdims=True) for h in range(H)]
    return jnp.concatenate(parts, axis=0)


def column_to_lanes(column, first):
    lanes = lax.broadcasted_iota(jnp.int32, (GROUP, STAT), 1)
    total = jnp.zeros((GROUP, STAT), WIDER)
    for h in range(H):
        total = total + jnp.where(lanes == first + h, column[GROUP * h : GROUP * h + GROUP], 0.0)
    return total


def spread_heads(stat):
    rows = lax.broadcasted_iota(jnp.int32, (STAT, D), 0) * HD
    lanes = lax.broadcasted_iota(jnp.int32, (STAT, D), 1)
    spread = jnp.where((lanes >= rows) & (lanes < rows + HD), 1.0, 0.0).astype(LOWER)
    return split_product(stat, spread, 2)


def own_scores(query, keys, table_ref):
    raw = right_product(query, keys)
    rows = lax.broadcasted_iota(jnp.int32, (GROUP, GROUP), 0)
    columns = lax.broadcasted_iota(jnp.int32, (GROUP, GROUP), 1)
    away = rows - columns
    parts = []
    for h in range(H):
        bias = jnp.full((GROUP, GROUP), table_ref[h, 0], WIDER)
        for d in range(1, GROUP):
            bias = jnp.where(away == d, table_ref[h, d], bias)
        part = raw[GROUP * h : GROUP * h + GROUP] + bias
        parts.append(jnp.where(away >= 0, part, MASKED))
    scores = jnp.concatenate(parts, axis=0)
    powers = jnp.exp(scores - jnp.max(scores, axis=1, keepdims=True))
    return powers / jnp.sum(powers, axis=1, keepdims=True)


def padded(ref, pad_ref):
    pad_ref[...] = jnp.zeros((GROUP, D), WIDER)
    pad_ref[:ANS] = ref[...].astype(WIDER)
    return pad_ref[...]


def answer_rows(width):
    return lax.broadcasted_iota(jnp.int32, (GROUP, width), 0) < ANS


def dec_self_part(
    table_ref, x_ref, g1_ref, g2_ref, after_ref, lefts_ref, heads_ref, query_ref, qkv_ref, out_ref, cross_ref, pad_ref
):
    start = padded(x_ref, pad_ref)
    first = (start * scale_of(start) * row_of(g1_ref)).astype(LOWER)
    heads = product(first, qkv_ref[...]).astype(LOWER)
    heads_ref[...] = heads
    query = stack_heads(heads.astype(WIDER)[:, :D] * 0.125).astype(LOWER)
    probs = own_scores(query, heads[:, D : 2 * D], table_ref)
    own = merge_heads(product(probs.astype(LOWER), heads[:, 2 * D :]))
    own = jnp.where(answer_rows(D), own, 0.0).astype(LOWER)
    after = start + product(own, out_ref[...])
    after_ref[...] = after
    second = (after * scale_of(after) * row_of(g2_ref)).astype(LOWER)
    query_ref[...] = product(second, cross_ref[...]).astype(LOWER)
    lefts_ref[:, :D] = first
    lefts_ref[:, D : 2 * D] = own
    lefts_ref[:, 2 * D :] = second


def masked_cross(n_ref, query_ref, pairs_ref):
    query = stack_heads(query_ref[...].astype(WIDER) * 0.125).astype(LOWER)
    raw = right_product(query, pairs_ref[:, :D])
    places = lax.broadcasted_iota(jnp.int32, (STACK, SLOT), 1)
    return query, jnp.where(places < n_ref[0], raw, MASKED)


def cross_kernel(n_ref, query_ref, pairs_ref, packed_ref):
    unused, scores = masked_cross(n_ref, query_ref, pairs_ref)
    top = jnp.max(scores, axis=1, keepdims=True)
    powers = jnp.exp(scores - top)
    total = jnp.sum(powers, axis=1, keepdims=True)
    probs = (powers / total).astype(LOWER)
    packed_ref[:, :D] = merge_heads(product(probs, pairs_ref[:, D:]))
    packed_ref[:, D:] = column_to_lanes(top, 0) + column_to_lanes(total, STAT // 2)


def dec_mid_kernel(
    n_ref, parts_ref, after_ref, cot_ref, g3_ref, lefts_ref, query_ref, e3_ref,
    pairs_any, cross_any, in_any, out_any, kv_any, final_any,
    answer_ref, early_ref, gmid_ref, gain_ref, partial_ref, gain_enc_ref, gpairs_any, gfinal_any, branch_any,
    pairs_ref, cross_ref, in_ref, out_ref, kv_ref, final_ref, gpairs_ref, gfinal_ref, branch_ref, pad_ref,
    sems, out_sems,
):
    held_pairs = ((cross_any, cross_ref), (in_any, in_ref), (out_any, out_ref), (pairs_any, pairs_ref))
    copies = copy_all(held_pairs + ((kv_any, kv_ref), (final_any, final_ref)), sems)
    begin(copies[:2])
    size = parts_ref.shape[0]
    used = lax.broadcasted_iota(jnp.int32, (GROUP, STAT), 1) < H
    tops = [parts_ref[k, :, D:] for k in range(size)]
    totals = [pltpu.roll(stat, STAT // 2, 1) for stat in tops]
    top = tops[0]
    for k in range(1, size):
        top = jnp.maximum(top, tops[k])
    weights = [jnp.where(used, totals[k] * jnp.exp(tops[k] - top), 0.0) for k in range(size)]
    total = weights[0]
    for k in range(1, size):
        total = total + weights[k]
    total = jnp.where(used, total, 1.0)
    mix = jnp.zeros((GROUP, D), WIDER)
    for k in range(size):
        mix = mix + parts_ref[k, :, :D] * spread_heads(weights[k] / total)
    mix_low = mix.astype(LOWER)
    copies[0].wait()
    begin(copies[2:3])
    middle = after_ref[...] + product(mix_low, cross_ref[...])
    third = (middle * scale_of(middle) * row_of(g3_ref)).astype(LOWER)
    copies[1].wait()
    begin(copies[3:])
    inner = product(third, in_ref[...])
    value, slope = silu_like(inner)
    hidden = value.astype(LOWER)
    copies[2].wait()
    answer = (middle + product(hidden, out_ref[...])).astype(LOWER)
    answer_ref[...] = answer[:ANS]
    grad = padded(cot_ref, pad_ref)
    out_low = grad.astype(LOWER)
    g_inner = (right_product(out_low, out_ref[...]) * slope).astype(LOWER)
    back, gain = norm_pull(middle, row_of(g3_ref), right_product(g_inner, in_ref[...]))
    gain_ref[...] = gain
    g_middle = grad + back
    gmid_ref[...] = g_middle
    middle_low = g_middle.astype(LOWER)
    g_mix = right_product(middle_low, cross_ref[...]).astype(LOWER)

    def store(name, rows):
        early_ref[:, AT[name] : AT[name] + rows.shape[1]] = rows

    def kept(rows):
        return jnp.where(answer_rows(rows.shape[1]), rows.astype(WIDER), 0.0).astype(LOWER)

    early_ref[:, : 3 * D] = kept(lefts_ref[...])
    store("mix", kept(mix_low))
    store("third", kept(third))
    store("hidden", kept(hidden))
    store("g_middle", middle_low)
    store("g_inner", g_inner)
    store("g_out", out_low)
    copies[3].wait()
    copies[4].wait()
    copies[5].wait()
    query, scores = masked_cross(n_ref, query_ref, pairs_ref)
    probs = jnp.exp(scores - lanes_to_column(jnp.where(used, top, 0.0))) / lanes_to_column(total)
    grad = stack_heads(g_mix.astype(WIDER))
    weighted = jnp.sum(grad * jnp.concatenate([mix] * H, axis=0), axis=1, keepdims=True)
    grad = grad.astype(LOWER)
    grad_probs = right_product(grad, pairs_ref[:, D:])
    rounded = (probs * (grad_probs - weighted)).astype(LOWER)
    g_keys = left_product(rounded, query).astype(LOWER)
    g_values = left_product(probs.astype(LOWER), grad).astype(LOWER)
    gpairs_ref[:, :D] = g_keys
    gpairs_ref[:, D:] = g_values
    sent = send_out([(gpairs_ref, gpairs_any)], out_sems, 0)
    partial_ref[...] = merge_heads(product(rounded, pairs_ref[:, :D])) * 0.125
    g_third = right_product(g_keys, kv_ref[:, :D]) + right_product(g_values, kv_ref[:, D:])
    back, gain = norm_pull(final_ref[...], row_of(e3_ref), g_third)
    gain_enc_ref[...] = gain
    gfinal_ref[...] = back
    branch_ref[...] = back.astype(LOWER)
    sent += send_out([(gfinal_ref, gfinal_any), (branch_ref, branch_any)], out_sems, 1)
    for copy in sent:
        copy.wait()


def dec_back_kernel(
    table_ref, x_ref, part_ref, got_ref, after_ref, gmid_ref, heads_ref,
    g1_ref, g2_ref, gain3_ref, query_any, out_any, qkv_any,
    late_ref, gstart_ref,
    cross_ref, out_ref, qkv_ref, pad_ref, sems,
):
    copies = copy_all(((query_any, cross_ref), (out_any, out_ref), (qkv_any, qkv_ref)), sems)
    begin(copies[:2])
    g_query = (part_ref[...] + got_ref[...]).astype(LOWER)
    copies[0].wait()
    begin(copies[2:])
    back, gain2 = norm_pull(after_ref[...], row_of(g2_ref), right_product(g_query, cross_ref[...]))
    g_after = gmid_ref[...] + back
    after_low = g_after.astype(LOWER)
    copies[1].wait()
    g_own = stack_heads(right_product(after_low, out_ref[...])).astype(LOWER)
    heads = heads_ref[...]
    query = stack_heads(heads.astype(WIDER)[:, :D] * 0.125).astype(LOWER)
    probs = own_scores(query, heads[:, D : 2 * D], table_ref)
    grad_probs = right_product(g_own, heads[:, 2 * D :])
    rounded = (probs * (grad_probs - jnp.sum(probs * grad_probs, axis=1, keepdims=True))).astype(LOWER)
    g_q = (merge_heads(product(rounded, heads[:, D : 2 * D])) * 0.125).astype(LOWER)
    g_k = left_product(rounded, query).astype(LOWER)
    g_v = left_product(probs.astype(LOWER), g_own).astype(LOWER)
    g_heads = jnp.concatenate([g_q, g_k, g_v], axis=1)
    copies[2].wait()
    start = padded(x_ref, pad_ref)
    back, gain1 = norm_pull(start, row_of(g1_ref), right_product(g_heads, qkv_ref[...]))
    gstart_ref[...] = (g_after + back)[:ANS]
    spread = rounded.astype(WIDER)
    rows = lax.broadcasted_iota(jnp.int32, (GROUP, GROUP), 0)
    columns = lax.broadcasted_iota(jnp.int32, (GROUP, GROUP), 1)
    mirror = jnp.where(rows + columns == GROUP - 1, 1.0, 0.0).astype(LOWER)
    empty = jnp.zeros((GROUP, STAT - GROUP), WIDER)
    tables = []
    for h in range(H):
        part = product(mirror, spread[GROUP * h : GROUP * h + GROUP].astype(LOWER))
        turned = pltpu.roll(jnp.concatenate([part, empty], axis=1), 0, 1, stride=1, stride_axis=0)
        tables.append(jnp.sum(turned, axis=0, keepdims=True))
    small = jnp.concatenate([gain1, gain2, gain3_ref[...]] + tables, axis=1)
    places = lax.broadcasted_iota(jnp.int32, (GROUP, LATE), 0)
    late = jnp.concatenate([g_heads, after_low, g_query], axis=1).astype(WIDER)
    late_ref[...] = jnp.where(places == ANS, small, late).astype(LOWER)


def dec_outer_kernel(size):
    part = D // size

    def body(me_ref, *refs):
        me = me_ref[0]
        small_ref = refs[9]
        there, here = refs[3:9], refs[10:16]
        early_ref, late_ref, sems = refs[16:]
        sent = []
        early_ref[...] = jnp.concatenate([refs[0][me ^ s].astype(WIDER) for s in range(size)], axis=0).astype(LOWER)
        late = [ref[...].astype(WIDER) for ref in refs[1:3]]
        late_ref[...] = jnp.concatenate(late, axis=0).astype(LOWER)
        rows = lax.broadcasted_iota(jnp.int32, (part, D), 0) + me * part
        lanes = lax.broadcasted_iota(jnp.int32, (part, D), 1)
        picked = jnp.where(rows == lanes, 1.0, 0.0).astype(LOWER)
        height = FF // size
        first = pl.multiple_of(AT["hidden"] + me * height, 128)

        def outer(k, name, right):
            left = right_product(picked, early_ref[:, AT[name] : AT[name] + D]).astype(LOWER)
            here[k][...] = product(left, right)
            sent.extend(send_out([(here[k], there[k])], sems, len(sent)))

        outer(4, "third", early_ref[:, AT["g_inner"] : AT["g_inner"] + FF])
        outer(0, "first", late_ref[:, : 3 * D])
        here[5][...] = left_product(early_ref[:, pl.ds(first, height)], early_ref[:, AT["g_out"] : AT["g_out"] + D])
        sent.extend(send_out([(here[5], there[5])], sems, len(sent)))
        outer(1, "own", late_ref[:, AT["g_after"] : AT["g_after"] + D])
        outer(2, "second", late_ref[:, AT["g_query"] : AT["g_query"] + D])
        outer(3, "mix", early_ref[:, AT["g_middle"] : AT["g_middle"] + D])
        total = jnp.zeros((1, LATE), WIDER)
        for part_late in late:
            for k in (0, GROUP):
                total = total + part_late[k + ANS : k + ANS + 1]
        small_ref[...] = total
        for copy in sent:
            copy.wait()

    return body


def held(*shapes):
    return [pltpu.VMEM(shape, LOWER) for shape in shapes] + [
        pltpu.VMEM((GROUP, D), WIDER),
        pltpu.SemaphoreType.DMA((len(shapes),)),
    ]


def dec_mid(count, parts, after_rows, cotangent, gain3, lefts, query, enc_gain3, pairs, cross_out, ffn_in, ffn_out, kv, final, after=()):
    outs = [narrow(SLOT, 2 * D), wide(SLOT, D), narrow(SLOT, D)]
    shapes = [(SLOT, 2 * D), (D, D), (D, FF), (FF, D), (D, 2 * D)]
    return run(
        "dec_mid",
        dec_mid_kernel,
        [count, parts, after_rows, cotangent, gain3, lefts, query, enc_gain3, pairs, cross_out, ffn_in, ffn_out, kv, final],
        [SCALARS] + [WHOLE] * 7 + [ANY] * 6,
        [narrow(ANS, D), narrow(GROUP, EARLY), wide(GROUP, D), wide(1, D), wide(GROUP, D), wide(1, D)] + outs,
        [WHOLE] * 6 + [ANY] * 3,
        after=after,
        scratch=[pltpu.VMEM(shape, LOWER) for shape in shapes]
        + [pltpu.VMEM((SLOT, D), WIDER)]
        + [pltpu.VMEM(out.shape, out.dtype) for out in outs]
        + [pltpu.VMEM((GROUP, D), WIDER), pltpu.SemaphoreType.DMA((6,)), pltpu.SemaphoreType.DMA((3,))],
        flops=4 * 10**9,
    )


def dec_back(table, answers, part, got, after_rows, g_middle, heads, gain1, gain2, g_gain3, query, out, qkv, after=()):
    return run(
        "dec_back",
        dec_back_kernel,
        [table, answers, part, got, after_rows, g_middle, heads, gain1, gain2, g_gain3, query, out, qkv],
        [SCALARS] + [WHOLE] * 9 + [ANY] * 3,
        [narrow(GROUP, LATE), wide(ANS, D)],
        after=after,
        scratch=held((D, D), (D, D), (D, 3 * D)),
        flops=0,
    )


def dec_outer(me, early, late_one, late_two, size, after=()):
    part = D // size
    outs = [wide(part, 3 * D), wide(part, D), wide(part, D), wide(part, D), wide(part, FF), wide(FF // size, D)]
    return run(
        "dec_outer",
        dec_outer_kernel(size),
        [me, early, late_one, late_two],
        [SCALARS, WHOLE, WHOLE, WHOLE],
        outs + [wide(1, LATE)],
        [ANY] * 6 + [WHOLE],
        after=after,
        scratch=[pltpu.VMEM(out.shape, WIDER) for out in outs]
        + [pltpu.VMEM((size * GROUP, EARLY), LOWER), pltpu.VMEM((size * GROUP, LATE), LOWER), pltpu.SemaphoreType.DMA((6,))],
        flops=8 * 10**9,
    )


def stack_late(one, two, after=()):
    def body(one_ref, two_ref, out_ref):
        out_ref[...] = jnp.concatenate([one_ref[...].astype(WIDER), two_ref[...].astype(WIDER)], axis=0).astype(LOWER)

    return run("stack_late", body, [one, two], [WHOLE] * 2, [narrow(2 * GROUP, LATE)], after=after, flops=0)


PLACES = [(0, 0), (0, 1), (1, 0), (1, 1)]


def place_of(me, there):
    return me ^ (4 * there[0] + 2 * there[1])


def turned_rows(me, acts, block):
    lanes = lax.broadcasted_iota(jnp.int32, (block, D), 1)
    rows = lax.broadcasted_iota(jnp.int32, (block, D), 0)
    picked = [jnp.where(lanes - rows == place_of(me, t) * block, 1.0, 0.0).astype(LOWER) for t in PLACES]
    picked = jnp.concatenate(picked, axis=0)
    return jnp.concatenate([right_product(picked, act).astype(LOWER) for act in acts], axis=1)


def target(there, x_refs, y_refs):
    dy, dx = there
    return (x_refs[dx].at[dy], y_refs[dy].at[dx])


def pages_out(pairs, sems, first):
    return send_out([(here.at[k], there.at[k]) for here, there in pairs for k in range(2)], sems, first)


def one_kernel(
    me_ref, t_own, t_par, p_own, p_par, h_own, h_par, b_own, b_par, xk_any, xs_any, yk_any, ys_any,
    xk, xs, yk, ys, t, p, h, b, sems, out_sems,
):
    me = me_ref[0]
    block = FF // 8
    pairs = [(t_own, t.at[0]), (t_par, t.at[1]), (p_own, p.at[:SLOT]), (p_par, p.at[SLOT:])]
    pairs += [(b_own, b.at[:SLOT]), (b_par, b.at[SLOT:])]
    for k, there in enumerate(PLACES):
        lanes = pl.ds(pl.multiple_of(place_of(me, there) * block, 128), block)
        pairs += [(h_own.at[:, lanes], h.at[k, :SLOT]), (h_par.at[:, lanes], h.at[k, SLOT:])]
    copies = copy_all(pairs, sems)
    begin(copies[:4])
    copies[0].wait()
    copies[1].wait()
    begin(copies[4:8])
    height = D // 8
    left = turned_rows(me, (t[0], t[1]), height)
    copies[2].wait()
    copies[3].wait()
    begin(copies[8:])
    for c in range(2):
        grad = product(left, p[:, D * c : D * c + D]).astype(LOWER)
        for k, there in enumerate(PLACES):
            to, unused = target(there, (xk, xs), (yk, ys))
            to[height * c : height * c + height] = grad[height * k : height * k + height]
    for k in range(4, 8):
        copies[k].wait()
    sent = []
    for k, there in enumerate(PLACES):
        grad = left_product(h[k], b[...]).astype(LOWER)
        to_x, to_y = target(there, (xk, xs), (yk, ys))
        to_x[2 * height : 3 * height] = grad[:height]
        to_y[...] = grad[height:]
        out_x, out_y = target(there, (xk_any, xs_any), (yk_any, ys_any))
        if k + 1 < len(PLACES):
            copies[8 + 2 * k].wait()
            copies[9 + 2 * k].wait()
        sent += send_out([(to_x, out_x), (to_y, out_y)], out_sems, len(sent))
    for copy in sent:
        copy.wait()


def two_kernel(
    me_ref, s_own, s_par, i_own, i_par, m_own, m_par, l_own, l_par, xk_any, xs_any, yk_any, ys_any,
    xk, xs, yk, ys, s, i, m, l, sems, out_sems,
):
    me = me_ref[0]
    pairs = [(s_own, s.at[0]), (s_par, s.at[1]), (m_own, m.at[0]), (m_par, m.at[1])]
    pairs += [(l_own, l.at[:SLOT]), (l_par, l.at[SLOT:])]
    for c in range(4):
        lanes = slice(D * c, D * c + D)
        pairs += [(i_own.at[:, lanes], i.at[c, :SLOT]), (i_par.at[:, lanes], i.at[c, SLOT:])]
    copies = copy_all(pairs, sems)
    begin(copies[:6])
    for k in range(4):
        copies[k].wait()
    begin(copies[6:10])
    height = D // 8
    half = height // 2
    left = turned_rows(me, (m[0], m[1]), height)
    turned = turned_rows(me, (s[0], s[1]), height)
    copies[4].wait()
    copies[5].wait()
    begin(copies[10:])
    grad = product(left, l[...]).astype(LOWER)
    for k, there in enumerate(PLACES):
        for to, first in zip(target(there, (xk, xs), (yk, ys)), (0, half)):
            to[2 * height : 2 * height + half] = grad[height * k + first : height * k + first + half]
    sent = []
    for c in range(4):
        if c % 2 == 0:
            for k in range(6 + 2 * c, 10 + 2 * c):
                copies[k].wait()
        grad = product(turned, i[c]).astype(LOWER)
        for k, there in enumerate(PLACES):
            to = target(there, (xk, xs), (yk, ys))[c // 2]
            to[height * (c % 2) : height * (c % 2) + height] = grad[height * k : height * k + height]
        if c % 2:
            done = ((xk, xk_any), (xs, xs_any)) if c == 1 else ((yk, yk_any), (ys, ys_any))
            sent += pages_out(done, out_sems, len(sent))
    for copy in sent:
        copy.wait()


def three_kernel(
    me_ref, f_own, f_par, g_own, g_par, small_ref, got_ref, xk_any, xs_any, yk_any, ys_any,
    xk, xs, yk, ys, f, g, sems, out_sems,
):
    me = me_ref[0]
    small = (small_ref[:, :D] + got_ref[:, :D]).astype(LOWER)
    pairs = [(f_own, f.at[0]), (f_par, f.at[1])]
    for c in range(3):
        pairs += [(g_own.at[c], g.at[c, :SLOT]), (g_par.at[c], g.at[c, SLOT:])]
    copies = copy_all(pairs, sems)
    begin(copies[:4])
    copies[0].wait()
    copies[1].wait()
    begin(copies[4:])
    height = D // 8
    half = D // 2
    left = turned_rows(me, (f[0], f[1]), height)
    for ref in (xk, xs, yk, ys):
        for k in range(2):
            ref[k, height:] = jnp.zeros((16, 3 * half), LOWER)
            if ref is xk or ref is xs:
                ref[k, height:, :D] = small
    copies[2].wait()
    copies[3].wait()
    sent = []
    for c in range(3):
        if c == 1:
            for k in range(4, 8):
                copies[k].wait()
        grad = product(left, g[c]).astype(LOWER)
        for k, there in enumerate(PLACES):
            to_x, to_y = target(there, (xk, xs), (yk, ys))
            block = grad[height * k : height * k + height]
            if c == 0:
                to_x[:height, :D] = block
            elif c == 1:
                to_x[:height, D:] = block[:, :half]
                to_y[:height, :half] = block[:, half:]
            else:
                to_y[:height, half:] = block
        if c:
            done = ((xk, xk_any), (xs, xs_any)) if c == 1 else ((yk, yk_any), (ys, ys_any))
            sent += pages_out(done, out_sems, len(sent))
    for copy in sent:
        copy.wait()


def weight_call(name, body, me, ins, rows, columns, held_shapes, flops, after, extra=()):
    out = narrow(2, rows, columns)
    copies = {"weights_one": 14, "weights_two": 14, "weights_three": 8}[name]
    return run(
        name,
        body,
        [me, *ins, *extra],
        [SCALARS] + [ANY] * len(ins) + [WHOLE] * len(extra),
        [out] * 4,
        [ANY] * 4,
        after=after,
        scratch=[pltpu.VMEM(out.shape, LOWER)] * 4
        + [pltpu.VMEM(shape, LOWER) for shape in held_shapes]
        + [pltpu.SemaphoreType.DMA((copies,)), pltpu.SemaphoreType.DMA((8,))],
        flops=flops,
    )


def weights_one(me, third, g_pairs, hidden, branch, after=()):
    shapes = [(2, SLOT, D), (2 * SLOT, 2 * D), (4, 2 * SLOT, FF // 8), (2 * SLOT, D)]
    ins = (*third, *g_pairs, *hidden, *branch)
    return weight_call("weights_one", one_kernel, me, ins, 3 * D // 8, D, shapes, 4 * 10**9, after)


def weights_two(me, second, g_inner, mixed, low, after=()):
    shapes = [(2, SLOT, D), (4, 2 * SLOT, D), (2, SLOT, D), (2 * SLOT, D)]
    ins = (*second, *g_inner, *mixed, *low)
    return weight_call("weights_two", two_kernel, me, ins, 5 * D // 16, D, shapes, COST[6], after)


def weights_three(me, first, grads, small, after=()):
    shapes = [(2, SLOT, D), (3, 2 * SLOT, D)]
    ins = (*first, *grads)
    return weight_call("weights_three", three_kernel, me, ins, D // 8 + 16, 3 * D // 2, shapes, COST[4], after, small)


def page(array, k):
    return pl.BlockSpec((1,) + array.shape[1:], lambda s: (k, 0, 0))


def add_first(parts, flops=0, after=()):
    count = len(parts)

    def body(*refs):
        for k in range(count):
            refs[2 * count + k][...] = (refs[2 * k][0].astype(WIDER) + refs[2 * k + 1][0].astype(WIDER)).astype(LOWER)

    flat = [a for pair in parts for a in pair]
    outs = [narrow(*keep.shape[1:]) for keep, unused in parts]
    return run("add_first", body, flat, [page(a, 1) for a in flat], outs, after=after, grid=(1,), flops=flops)


def add_second(parts, after=()):
    shapes = [keep.shape[1:] for keep, unused, unused_too in parts]

    def body(*refs):
        first = 0
        for k, (high, across) in enumerate(shapes):
            keep, got, last = refs[3 * k : 3 * k + 3]
            total = keep[0].astype(WIDER) + got[0].astype(WIDER) + last[...].astype(WIDER)
            refs[-1][first : first + high] = total.astype(LOWER)
            first += high

    flat = [a for trio in parts for a in trio]
    specs = [page(a, 0) if a.ndim == 3 else WHOLE for a in flat]
    rows = sum(shape[0] for shape in shapes)
    return run("add_second", body, flat, specs, [narrow(rows, shapes[0][1])], after=after, grid=(1,), flops=0)


def add_pair(one, two, flops=0, after=()):
    def body(one_ref, two_ref, out_ref):
        out_ref[...] = (one_ref[...].astype(WIDER) + two_ref[...].astype(WIDER)).astype(LOWER)

    return run("add_pair", body, [one, two], [WHOLE] * 2, [narrow(*one.shape)], after=after, flops=flops)


def add_last(me, parts, after=()):
    rows, across = parts[0][0].shape[1:]
    quarter = (rows + 16) // 4

    def body(me_ref, *refs):
        total_ref = refs[-1]
        for k in range(2):
            keep, got, last = refs[3 * k : 3 * k + 3]
            total = keep[0].astype(WIDER) + got[0].astype(WIDER) + last[...].astype(WIDER)
            total_ref[:rows, across * k : across * k + across] = total.astype(LOWER)
        total_ref[rows:] = jnp.zeros((16, 2 * across), LOWER)
        for k in range(4):
            first = pl.multiple_of((me_ref[0] ^ k) * quarter, 16)
            refs[6 + k][...] = total_ref[pl.ds(first, quarter), :]

    flat = [a for trio in parts for a in trio]
    specs = [page(a, 0) if a.ndim == 3 else WHOLE for a in flat]
    outs = [narrow(quarter, 2 * across)] * 4
    scratch = [pltpu.VMEM((4 * quarter, 2 * across), LOWER)]
    return run("add_last", body, [me, *flat], [SCALARS] + specs, outs, [WHOLE] * 4, after=after, grid=(1,), scratch=scratch, flops=0)


def add_parts(parts, after=()):
    def body(*refs):
        total = refs[0][...].astype(WIDER)
        for ref in refs[1:4]:
            total = total + ref[...].astype(WIDER)
        refs[4][...] = total.astype(LOWER)

    return run("add_parts", body, parts, [WHOLE] * 4, [narrow(*parts[0].shape)], after=after, flops=0)


def join_parts(me, parts, rows, after=()):
    high, across = parts[0].shape

    def body(me_ref, *refs):
        total_ref = refs[6]
        for k in range(4):
            first = pl.multiple_of((me_ref[0] ^ k) * high, 8)
            total_ref[pl.ds(first, high), :] = refs[k][...].astype(WIDER)
        refs[4][...] = total_ref[:rows]
        refs[5][...] = total_ref[rows : rows + 16, :D]

    scratch = [pltpu.VMEM((4 * high, across), WIDER)]
    outs = [wide(rows, across), wide(16, D)]
    return run("join_parts", body, [me, *parts], [SCALARS] + [WHOLE] * 4, outs, after=after, scratch=scratch, flops=0)


def add_rows(one, two, after=()):
    def body(one_ref, two_ref, out_ref):
        out_ref[...] = one_ref[...] + two_ref[...]

    return run("add_rows", body, [one, two], [WHOLE] * 2, [wide(*one.shape)], after=after, flops=0)


def partner(axis, bit):
    return [(k, k ^ (1 << bit)) for k in range(lax.axis_size(axis))]


def swap(value, axis, bit):
    return lax.ppermute(value, axis, partner(axis, bit))


def all_sum(value, axis):
    for bit in range(lax.axis_size(axis).bit_length() - 1):
        value = value + swap(value, axis, bit)
    return value


def pa_order(turn):
    rest = lax.axis_size("pa").bit_length() - 2
    return [1 + (k + turn) % rest for k in range(rest)]


def both_cores(acts, turn):
    size = lax.axis_size("pa")
    me = lax.axis_index("pa")
    blocks = jnp.transpose(acts).reshape(size, acts.shape[1] // size, acts.shape[0])
    order = pa_order(turn)
    offsets = [
        sum(((k >> (len(order) - 1 - p)) & 1) << bit for p, bit in enumerate(order)) for k in range(size // 2)
    ]
    mine = jnp.concatenate([lax.dynamic_slice_in_dim(blocks, me ^ d, 1) for d in offsets])
    theirs = jnp.concatenate([lax.dynamic_slice_in_dim(blocks, me ^ d ^ 1, 1) for d in offsets])
    return mine, swap(theirs, "pa", 0)


def weight_part(acts, grads, first, last):
    total = None
    for act, grad in zip(acts, grads):
        act = act[first:last]
        term = product(act.reshape(-1, act.shape[2]), grad)
        total = term if total is None else total + term
    height = acts[0].shape[1]
    return total.astype(LOWER).reshape(last - first, height, -1)


def add_up(parts):
    total = parts[0].astype(WIDER)
    for part in parts[1:]:
        total = total + part.astype(WIDER)
    return total.astype(LOWER)


def share_over_pa(acts, grads, turn):
    size = acts[0].shape[0]
    keep = [weight_part(acts, grads, 0, size // 2)]
    send = weight_part(acts, grads, size // 2, size)
    for bit in pa_order(turn):
        keep.append(swap(send, "pa", bit))
        size //= 2
        if size > 1:
            send = add_up([part[size // 2 : size] for part in keep])
            keep = [part[: size // 2] for part in keep]
    return add_up([part[0] for part in keep])


def inward(share):
    return lax.ppermute(share, "pb", [(0, 1), (3, 2)])


def between(share):
    return lax.ppermute(share, "pb", [(1, 2), (2, 1)])


def outward(share):
    me = lax.axis_index("pb")
    got = lax.ppermute(share, "pb", [(1, 0), (2, 3)])
    return jnp.where((me == 1) | (me == 2), share, got).astype(WIDER)


def other_quarters(parts):
    return [lax.ppermute(part, "pb", [(k, k ^ (s + 1)) for k in range(4)]) for s, part in enumerate(parts)]


def total_plain(share):
    return lax.psum(share, "pb").astype(WIDER)


def local(
    passages,
    lengths,
    answers,
    cotangent,
    enc_gain1,
    enc_qkv,
    enc_bias,
    enc_out,
    enc_gain2,
    enc_ffn_in,
    enc_ffn_out,
    enc_gain3,
    cross_kv,
    dec_gain1,
    dec_qkv,
    dec_bias,
    dec_out,
    dec_gain2,
    cross_query,
    cross_out,
    dec_gain3,
    dec_ffn_in,
    dec_ffn_out,
):
    pa_size = lax.axis_size("pa")
    pb_size = lax.axis_size("pb")
    fast = pa_size == 8 and pb_size == 4
    me = lax.axis_index("pa").astype(jnp.int32).reshape(1)
    x = passages.reshape(SLOT, D)
    count = lengths.reshape(1)
    table = jnp.transpose(enc_bias)
    dec_table = jnp.transpose(dec_bias)
    pick = jnp.asarray(PICK, LOWER)
    pick_back = jnp.asarray(PICK_BACK, LOWER)

    def across(value):
        return value, swap(value, "pa", 0)

    first, heads, mixed, stats, packed, dec_after, lefts, dec_heads, query, after, second, slope, hidden, final, third, pairs, token = forward(
        count, table, pick, x, enc_gain1, enc_qkv, enc_gain2, enc_gain3, enc_out, enc_ffn_in, enc_ffn_out, cross_kv,
        (dec_table, answers[0], dec_gain1, dec_gain2, dec_qkv, dec_out, cross_query),
    )
    if fast:
        acts = [across(value) for value in (first, mixed, second, hidden, third)]
    else:
        acts = [both_cores(v, k % 2) for k, v in enumerate((first, mixed, second, hidden, third))]
    gathered = lax.all_gather(packed, "pa")
    answer, early, g_middle, g_gain3, partial, g_enc_gain3, g_pairs, g_final, branch, token = dec_mid(
        count, gathered, dec_after, cotangent[0], dec_gain3, lefts, query, enc_gain3, pairs,
        cross_out, dec_ffn_in, dec_ffn_out, cross_kv, final,
        after=[got for unused, got in acts[:4]],
    )
    early_all = lax.all_gather(early, "pb")
    g_inner, g_after, low, g_mixed, g_enc_gain2, token = ffn_back(
        branch, enc_ffn_out, slope, enc_ffn_in, after, enc_gain2, g_final, enc_out, after=[token]
    )

    def back_of(base, pairs, after):
        return attention_back(count, table, pick, heads, g_mixed, mixed, stats, base, pairs, after=after)

    def dec_end(part, got, token, wait=()):
        return dec_back(
            dec_table, answers[0], part, got, dec_after, g_middle, dec_heads,
            dec_gain1, dec_gain2, g_gain3, cross_query, dec_out, dec_qkv, after=[token, *wait],
        )

    def rows_end(grads, diagonal, token, wait=()):
        return attention_end(
            count, table, pick, heads, g_mixed, mixed, stats, grads, diagonal, enc_qkv, x, enc_gain1,
            g_after, g_enc_gain2, g_enc_gain3, pick_back, after=[token, *wait],
        )

    pb_me = lax.axis_index("pb").astype(jnp.int32).reshape(1)

    def outer_end(token, late_one, late_two):
        *outer, token = dec_outer(pb_me, early_all, late_one, late_two, pb_size, after=[token])
        return outer, token

    if fast:
        partial, token = add_rows(partial, swap(partial, "pa", 0), after=[token])
        got = swap(partial, "pa", 1)
        xk, xs, yk, ys, token = weights_one(me, acts[4], across(g_pairs), acts[3], across(branch), after=[token])
        one = ((xk, swap(xs, "pa", 1)), (yk, swap(ys, "pa", 2)))
        partial, token = add_rows(partial, got, after=[token])
        got = swap(partial, "pa", 2)
        grads, diagonal_a, token = back_of(0, FIRST, [token])
        late, g_start, token = dec_end(partial, got, token)
        late_near = swap(late, "pb", 0)
        send_x, send_y, token = add_first(one, flops=COST[5], after=[token, early_all])
        last = (swap(send_x, "pa", 2), swap(send_y, "pa", 1))
        late, token = stack_late(late, late_near, after=[token])
        late_far = swap(late, "pb", 1)
        xk, xs, yk, ys, token = weights_two(me, acts[2], across(g_inner), acts[1], across(low), after=[token])
        two = ((xk, swap(xs, "pa", 1)), (yk, swap(ys, "pa", 2)))
        share_one, token = add_second([one[0] + last[:1], one[1] + last[1:]], after=[token])
        got_one = inward(share_one)
        g_rows, small, diagonal_a, grads, token = rows_end(grads, diagonal_a, token, [late_far])
        there, got_small = swap(grads, "pa", 0), swap(small, "pa", 0)
        send_x, send_y, token = add_first(two, flops=COST[0], after=[token])
        last = (swap(send_x, "pa", 2), swap(send_y, "pa", 1))
        share_one, token = add_pair(share_one, got_one, flops=COST[1], after=[token])
        got_one = between(share_one)
        xk, xs, yk, ys, token = weights_three(me, acts[0], (grads, there), (small, got_small), after=[token])
        three = ((xk, swap(xs, "pa", 1)), (yk, swap(ys, "pa", 2)))
        share_two, token = add_second([two[0] + last[:1], two[1] + last[1:]], after=[token])
        got_two = inward(share_two)
        share_one, token = add_pair(share_one, got_one, flops=COST[2], after=[token])
        total_one = outward(share_one)
        send_x, send_y, token = add_first(three, after=[token])
        last = (swap(send_x, "pa", 2), swap(send_y, "pa", 1))
        share_two, token = add_pair(share_two, got_two, flops=COST[3], after=[token])
        got_two = between(share_two)
        *quarters, token = add_last(pb_me, [three[0] + last[:1], three[1] + last[1:]], after=[token])
        parts = other_quarters(quarters[1:])
        outer, token = outer_end(token, late, late_far)
        share_two, token = add_pair(share_two, got_two, after=[token])
        total_two = outward(share_two)
        mine, token = add_parts(quarters[:1] + parts, after=[token, total_one])
        total_qkv, small, token = join_parts(pb_me, [mine] + other_quarters([mine] * 3), D // pa_size, after=[token, total_two])
        block = D // pa_size
        total_kv = jnp.concatenate([total_one[:block], total_one[block : 2 * block]], axis=1)
        total_ffn_out = total_one[2 * block :]
        second_part = 2 * block + block // 2
        total_ffn_in = jnp.concatenate(
            [total_two[first : first + block] for first in (0, block, second_part, second_part + block)], axis=1
        )
        total_out = jnp.concatenate([total_two[2 * block : second_part], total_two[second_part + 2 * block :]], axis=0)
    else:
        partial = all_sum(partial, "pa")
        late, g_start, token = dec_end(partial, jnp.zeros_like(partial), token)
        late, token = stack_late(late, swap(late, "pb", 0), after=[token])
        late_far = swap(late, "pb", 1)
        grads, diagonal_a, token = back_of(0, FIRST, [token])
        g_rows, small, diagonal_a, grads, token = rows_end(grads, diagonal_a, token)
        outer, token = outer_end(token, late, late_far)
        small = all_sum(all_sum(small[:, :D], "pa"), "pb")
        g_heads = jnp.concatenate([grads[0], grads[1], grads[2]], axis=1)
        total_kv = total_plain(share_over_pa(acts[4], across(g_pairs), 0))
        total_ffn_out = total_plain(share_over_pa(acts[3], across(branch), 1))
        total_ffn_in = total_plain(share_over_pa(acts[2], across(g_inner), 0))
        total_out = total_plain(share_over_pa(acts[1], across(low), 1))
        total_qkv = total_plain(share_over_pa(acts[0], across(g_heads), 0))

    d_qkv, d_out, d_query, d_cross, d_in, d_ffn, dec_small = outer
    dec_small = dec_small[0]
    dec_bias_rows = dec_small[3 * D :].reshape(H, STAT)[:, GROUP - ANS : GROUP]
    dec_bias_all = jnp.pad(jnp.transpose(dec_bias_rows[:, ::-1]), ((0, BUCKETS - ANS), (0, 0)))

    def own_part(vector, axis):
        height = vector.shape[0] // lax.axis_size(axis)
        return lax.dynamic_slice_in_dim(vector, lax.axis_index(axis) * height, height, axis=0)

    return (
        answer[None],
        g_rows.reshape(1, 1, SLOT, D),
        g_start[None],
        own_part(small[0], "pa"),
        total_qkv,
        jnp.transpose(small[4:16, :BUCKETS]),
        total_out,
        own_part(small[1], "pa"),
        total_ffn_in,
        total_ffn_out,
        own_part(small[2], "pa"),
        total_kv,
        own_part(dec_small[:D], "pb"),
        d_qkv,
        own_part(dec_bias_all, "pb"),
        d_out,
        own_part(dec_small[D : 2 * D], "pb"),
        d_query,
        d_cross,
        own_part(dec_small[2 * D : 3 * D], "pb"),
        d_in,
        d_ffn,
    )


def solution(mesh):
    copied = P()
    in_specs = (
        P("pb", "pa", None, None),
        P("pb", "pa"),
        P("pb", None, None),
        P("pb", None, None),
    ) + (copied,) * 19
    by_pa, by_pa_rows = P("pa"), P("pa", None)
    by_pb, by_pb_rows = P("pb"), P("pb", None)
    out_specs = (
        P("pb", None, None),
        P("pb", "pa", None, None),
        P("pb", None, None),
        by_pa,
        by_pa_rows,
        copied,
        by_pa_rows,
        by_pa,
        by_pa_rows,
        by_pa_rows,
        by_pa,
        by_pa_rows,
        by_pb,
        by_pb_rows,
        by_pb_rows,
        by_pb_rows,
        by_pb,
        by_pb_rows,
        by_pb_rows,
        by_pb,
        by_pb_rows,
        by_pb_rows,
    )
    return jax.shard_map(local, mesh=mesh, in_specs=in_specs, out_specs=out_specs, check_vma=False)
```

```python
import jax
import jax.numpy as jnp
import numpy as np
from jax import lax
from jax.experimental import pallas as pl
from jax.experimental.pallas import tpu as pltpu
from jax.sharding import PartitionSpec as P

D = 768
H = 12
HD = 64
FF = 3072
BUCKETS = 32
ANS = 20
SLOT = 512
PAIR = 2 * HD
PAIRS = H // 2
EDGE = 128
STRIP = 256
SPAN = 256
GROUP = 24
COST = (4 * 10**9, 0, 4 * 10**9, 0, 4 * 10**9, 4 * 10**9, 4 * 10**9)
STACK = H * GROUP
STAT = 128
STEPS = 4
WIDTH = FF // STEPS
FIRST = 4
EPS = 1e-06
MASKED = -1000000000.0
C_GELU = 0.7978845608028654
LOWER = jnp.bfloat16
WIDER = jnp.float32
EARLY = 7 * D + 2 * FF
LATE = 5 * D
AT = {
    "first": 0,
    "own": D,
    "second": 2 * D,
    "mix": 3 * D,
    "third": 4 * D,
    "hidden": 5 * D,
    "g_middle": 5 * D + FF,
    "g_inner": 6 * D + FF,
    "g_out": 6 * D + 2 * FF,
    "g_heads": 0,
    "g_after": 3 * D,
    "g_query": 4 * D,
}


def tile_classes(away):
    rows = [np.clip(EDGE * d - away, -(BUCKETS // 2), BUCKETS // 2 - 1) + BUCKETS // 2 for d in (-1, 0, 1)]
    return np.eye(BUCKETS, dtype=np.float32)[np.concatenate(rows)]


LANES = np.arange(SPAN)
PICK = tile_classes(np.where(LANES < EDGE, LANES, LANES - SPAN)).T
ENDS = np.repeat(np.eye(BUCKETS, dtype=np.float32)[[0, BUCKETS - 1]], EDGE, axis=0)
PICK_BACK = np.pad(np.concatenate([tile_classes(LANES - (EDGE - 1)), ENDS]), ((0, 0), (0, STAT - BUCKETS)))

SCALARS = pl.BlockSpec(memory_space=pltpu.SMEM)
ANY = pl.BlockSpec(memory_space=pl.ANY)
WHOLE = pl.BlockSpec(memory_space=pltpu.VMEM)
TOKEN = (8, 128)


def wide(*shape):
    return jax.ShapeDtypeStruct(shape, WIDER)


def narrow(*shape):
    return jax.ShapeDtypeStruct(shape, LOWER)


def run(name, body, ins, in_specs, outs, out_specs=None, after=(), grid=(), scratch=(), flops=10**9, mib=63, alias=None):
    count, extra, results = len(ins), len(after), len(outs)
    if out_specs is None:
        out_specs = [WHOLE] * results
    zeros = (lambda *s: (0, 0)) if grid else (lambda: (0, 0))

    def wrapped(*refs):
        refs[count + extra + results][...] = jnp.zeros(TOKEN, WIDER)
        body(*refs[:count], *refs[count + extra : count + extra + results], *refs[count + extra + results + 1 :])

    got = pl.pallas_call(
        wrapped,
        grid=grid,
        out_shape=tuple(outs) + (wide(*TOKEN),),
        in_specs=list(in_specs) + [ANY] * extra,
        out_specs=tuple(out_specs) + (pl.BlockSpec(TOKEN, zeros),),
        scratch_shapes=list(scratch),
        input_output_aliases=alias or {},
        compiler_params=pltpu.CompilerParams(vmem_limit_bytes=mib * 2**20),
        cost_estimate=pl.CostEstimate(flops=10 * flops, bytes_accessed=1, transcendentals=0),
        name=name,
    )(*ins, *after)
    return got


def product(left, right):
    return jnp.dot(left, right, preferred_element_type=WIDER)


def left_product(left, right):
    return lax.dot_general(left, right, (((0,), (0,)), ((), ())), preferred_element_type=WIDER)


def right_product(left, right):
    return lax.dot_general(left, right, (((1,), (1,)), ((), ())), preferred_element_type=WIDER)


def split_product(left, right, terms):
    total = None
    for k in range(terms):
        part = left.astype(LOWER)
        left = left - part.astype(WIDER)
        term = product(part, right)
        total = term if total is None else total + term
    return total


def silu_like(inner):
    square = inner * inner
    tanh = jnp.tanh(inner * (C_GELU + (C_GELU * 0.044715) * square))
    half = 0.5 + 0.5 * tanh
    value = inner * half
    slope = half + value * (1.0 - tanh) * (C_GELU + (3.0 * C_GELU * 0.044715) * square)
    return value, slope


def row_of(ref):
    return ref[...].reshape(1, D)


def scale_of(values):
    return lax.rsqrt(jnp.mean(values * values, axis=-1, keepdims=True) + EPS)


def norm_pull(values, gain, grad):
    scale = scale_of(values)
    lifted = grad * gain
    inside = jnp.sum(values * lifted, axis=-1, keepdims=True)
    back = scale * lifted - values * (scale * scale * scale * inside * (1.0 / D))
    return back, jnp.sum(grad * values * scale, axis=0, keepdims=True)


def fetch(pairs, sems):
    copies = [pltpu.make_async_copy(s, t, sems.at[k]) for k, (s, t) in enumerate(pairs)]
    for copy in copies:
        copy.start()
    return copies


def copy_all(pairs, sems):
    return [pltpu.make_async_copy(s, t, sems.at[k]) for k, (s, t) in enumerate(pairs)]


def begin(copies):
    for copy in copies:
        copy.start()


def bias_tiles(u_ref, head):
    tiles = []
    for d in range(3):
        row = u_ref[pl.ds(head, 1), SPAN * d : SPAN * d + SPAN]
        spread = jnp.broadcast_to(row, (EDGE, SPAN))
        tiles.append(pltpu.roll(spread, 0, 1, stride=1, stride_axis=0)[:, :EDGE])
    return tiles


def key_masks(n):
    places = lax.broadcasted_iota(jnp.int32, (EDGE, EDGE), 0)
    return [jnp.where(places + EDGE * j < n, 0.0, MASKED) for j in range(SLOT // EDGE)]


def score_blocks(raw, tiles, masks, low, high, first):
    columns = []
    for c in range(STRIP // EDGE):
        blocks = []
        for j in range(SLOT // EDGE):
            block = raw[EDGE * j : EDGE * j + EDGE, EDGE * c : EDGE * c + EDGE]
            d = j - first - c
            block = block + (tiles[d + 1] if abs(d) <= 1 else (low if d < 0 else high))
            blocks.append(block + masks[j] if j > 0 else block)
        columns.append(blocks)
    return columns


def paved(columns, kind):
    return jnp.concatenate([jnp.concatenate([b.astype(kind) for b in blocks], axis=0) for blocks in columns], axis=1)


def fill_rows(table_ref, pick_ref, u_ref):
    @pl.when(pl.program_id(0) == 0)
    def _():
        u_ref[...] = split_product(table_ref[...], pick_ref[...], 3)


def attn_fwd_kernel(n_ref, ends_ref, table_ref, pick_ref, x_ref, g1_ref, wq_ref, wk_ref, wv_ref, first_ref, heads_ref, o_ref, st_ref, u_ref):
    fill_rows(table_ref, pick_ref, u_ref)
    step = pl.program_id(0)

    @pl.when(step == 0)
    def _():
        rows = x_ref[...].astype(WIDER)
        first_ref[...] = (rows * scale_of(rows) * row_of(g1_ref)).astype(LOWER)

    masks = key_masks(n_ref[0])
    first = first_ref[...]
    for k, w_ref in enumerate((wq_ref, wk_ref, wv_ref)):
        heads_ref[k] = product(first, w_ref[...]).astype(LOWER)
    q_ref, k_ref = heads_ref.at[0], heads_ref.at[1]
    values = jnp.transpose(heads_ref[2])
    ones = jnp.ones((16, SLOT), LOWER)
    mixed = []
    for h in range(2):
        head = 2 * step + h
        low, high = ends_ref[head, 0], ends_ref[head, BUCKETS - 1]
        tiles = bias_tiles(u_ref, head)
        cols = slice(HD * h, HD * h + HD)
        keys = k_ref[:, cols]
        left = jnp.concatenate([values[cols], ones], axis=0)
        strips = []
        for i in range(0, SLOT // EDGE, STRIP // EDGE):
            lanes = slice(EDGE * i, EDGE * i + STRIP)
            raw = right_product(keys, q_ref[lanes, cols] * 0.125)
            tops, powers = [], []
            for blocks in score_blocks(raw, tiles, masks, low, high, i):
                top = jnp.maximum(jnp.maximum(blocks[0], blocks[1]), jnp.maximum(blocks[2], blocks[3]))
                top = jnp.max(top, axis=0, keepdims=True)
                tops.append(top)
                powers.append([jnp.exp(block - top) for block in blocks])
            out = product(left, paved(powers, LOWER))
            total = out[HD : HD + 1]
            st_ref[0, h : h + 1, lanes] = jnp.concatenate(tops, axis=1) + jnp.log(total)
            strips.append(out[:HD] * (1.0 / total))
        mixed.append(jnp.concatenate(strips, axis=1))
    lanes = pl.ds(pl.multiple_of(step * PAIR, PAIR), PAIR)
    o_ref[:, lanes] = jnp.transpose(jnp.concatenate(mixed, axis=0)).astype(LOWER)


def attn_bwd_kernel(base):
    def body(
        n_ref, ends_ref, table_ref, pick_ref, h_ref, g_ref, o_ref, st_ref, gh_ref, gb_ref, u_ref
    ):
        q_ref, k_ref, v_ref = h_ref.at[0], h_ref.at[1], h_ref.at[2]
        fill_rows(table_ref, pick_ref, u_ref)
        step = pl.program_id(0) + base
        masks = key_masks(n_ref[0])
        keys_t = jnp.transpose(k_ref[...])
        rows = lax.broadcasted_iota(jnp.int32, (EDGE, EDGE), 0)
        columns = lax.broadcasted_iota(jnp.int32, (EDGE, EDGE), 1)
        mirror = jnp.where(rows + columns == EDGE - 1, 1.0, 0.0).astype(LOWER)
        rows = lax.broadcasted_iota(jnp.int32, (16, SLOT), 0) * EDGE
        columns = lax.broadcasted_iota(jnp.int32, (16, SLOT), 1)
        places = jnp.where((columns >= rows) & (columns < rows + EDGE), 1.0, 0.0).astype(LOWER)
        rows = lax.broadcasted_iota(jnp.int32, (16, PAIR), 0) * HD
        columns = lax.broadcasted_iota(jnp.int32, (16, PAIR), 1)
        halves = jnp.where((columns >= rows) & (columns < rows + HD), 1.0, 0.0).astype(LOWER)
        met = g_ref[...].astype(WIDER) * o_ref[...].astype(WIDER)
        upper = met.astype(LOWER)
        lower = (met - upper.astype(WIDER)).astype(LOWER)
        weighted = right_product(halves, upper) + right_product(halves, lower)
        grad_queries = []
        gb_ref[0, 2:8, :] = jnp.zeros((6, 4 * SPAN), WIDER)
        for h in range(2):
            head = 2 * step + h
            low, high = ends_ref[head, 0], ends_ref[head, BUCKETS - 1]
            tiles = bias_tiles(u_ref, head)
            cols = slice(HD * h, HD * h + HD)
            keys = k_ref[:, cols]
            values = v_ref[:, cols]
            left = jnp.concatenate([keys_t[cols], places], axis=0)
            grad_keys = jnp.zeros((SLOT, HD), WIDER)
            grad_values = jnp.zeros((SLOT, HD), WIDER)
            strips = []
            sums = {}

            def gather(d, block):
                sums[d] = sums[d] + block if d in sums else block

            for i in range(0, SLOT // EDGE, STRIP // EDGE):
                lanes = slice(EDGE * i, EDGE * i + STRIP)
                query = q_ref[lanes, cols]
                grad = g_ref[lanes, cols]
                raw = right_product(keys, query * 0.125)
                grad_probs = right_product(values, grad)
                probs, changes = [], []
                for c, blocks in enumerate(score_blocks(raw, tiles, masks, low, high, i)):
                    part = slice(EDGE * (i + c), EDGE * (i + c) + EDGE)
                    total = st_ref[0, h : h + 1, part]
                    mean = weighted[h : h + 1, part]
                    probs.append([jnp.exp(block - total) for block in blocks])
                    changes.append([])
                    for j in range(SLOT // EDGE):
                        gap = grad_probs[EDGE * j : EDGE * j + EDGE, EDGE * c : EDGE * c + EDGE] - mean
                        change = probs[c][j] * gap
                        changes[c].append(change)
                        if abs(j - i - c) <= 1:
                            gather(j - i - c, change)
                rounded = paved(changes, LOWER)
                out = product(left, rounded)
                strips.append(out[:HD])
                for c in range(STRIP // EDGE):
                    for j in range(SLOT // EDGE):
                        if abs(j - i - c) > 1:
                            gather(2 if j > i + c else -2, out[HD + j : HD + j + 1, EDGE * c : EDGE * c + EDGE])
                grad_keys += product(rounded, query)
                grad_values += product(paved(probs, LOWER), grad)
            grad_queries.append(jnp.concatenate(strips, axis=1))
            gh_ref[1, :, cols] = (grad_keys * 0.125).astype(LOWER)
            gh_ref[2, :, cols] = grad_values.astype(LOWER)
            empty = jnp.zeros((EDGE, SPAN - EDGE), WIDER)
            band = jnp.concatenate([sums[-1], sums[0], sums[1]], axis=1)
            upper = band.astype(LOWER)
            lower = (band - upper.astype(WIDER)).astype(LOWER)
            mirrored = product(mirror, upper) + product(mirror, lower)
            for d in range(3):
                spread = jnp.concatenate([mirrored[:, EDGE * d : EDGE * d + EDGE], empty], axis=1)
                turned = pltpu.roll(spread, 0, 1, stride=1, stride_axis=0)
                gb_ref[0, h : h + 1, SPAN * d : SPAN * d + SPAN] = jnp.sum(turned, axis=0, keepdims=True)
            for place, d in ((3 * SPAN, -2), (3 * SPAN + EDGE, 2)):
                gb_ref[0, h : h + 1, place : place + EDGE] = sums[d]
        gh_ref[0] = (jnp.transpose(jnp.concatenate(grad_queries, axis=0)) * 0.125).astype(LOWER)

    return body


def columns_at(first):
    return pl.BlockSpec((SLOT, PAIR), lambda s: (0, first + s))


def stats_at(first):
    return pl.BlockSpec((1, 2, SLOT), lambda s: (first + s, 0, 0))


def pair_of_all(base):
    return pl.BlockSpec((3, SLOT, PAIR), lambda s: (0, 0, base + s))


def attention_back(count, table, pick, heads, grad_mixed, mixed, stats, base, half, after=()):
    return run(
        "enc_attention_back",
        attn_bwd_kernel(base),
        [count, table, table, pick, heads, grad_mixed, mixed, stats],
        [SCALARS, SCALARS, WHOLE, WHOLE, pair_of_all(base), columns_at(base), columns_at(base), stats_at(base)],
        [narrow(3, SLOT, D), wide(half, 8, 4 * SPAN)],
        [pair_of_all(base), pl.BlockSpec((1, 8, 4 * SPAN), lambda s: (s, 0, 0))],
        after=after,
        grid=(half,),
        scratch=[pltpu.VMEM((H, 3 * SPAN), WIDER)],
        flops=2 * 5 * H * SLOT * SLOT * HD * 4,
    )


def send_out(pairs, sems, first):
    copies = [pltpu.make_async_copy(s, t, sems.at[first + k]) for k, (s, t) in enumerate(pairs)]
    for copy in copies:
        copy.start()
    return copies


def chunk(k):
    return slice(WIDTH * k, WIDTH * k + WIDTH)


def forward_kernel(
    n_ref, ends_ref, table_ref, pick_ref, x_ref, g1_ref, wq_ref, wk_ref, wv_ref,
    g2_ref, g3_ref, dec_table_ref, ans_ref, dg1_ref, dg2_ref,
    wo_any, in_any, out_any, kv_any, dqkv_any, dout_any, dquery_any,
    first_ref, heads_ref, mixed_ref, st_ref, packed_ref, dec_after_ref, lefts_ref, dec_heads_ref, query_ref,
    after_any, second_any, slope_any, hidden_any, final_any, third_any, pairs_any,
    u_ref, wo_ref, in_ref, out_ref, kv_ref, dqkv_ref, dout_ref, dquery_ref, pad_ref,
    after_ref, second_ref, slope_ref, hidden_ref, final_ref, third_ref, pairs_ref,
    sems, dec_sems, out_sems,
):
    step = pl.program_id(0)
    dec_copies = copy_all([(dqkv_any, dqkv_ref), (dout_any, dout_ref), (dquery_any, dquery_ref)], dec_sems)
    pairs = [(wo_any, wo_ref)]
    for k in range(STEPS):
        pairs += [(in_any.at[:, chunk(k)], in_ref.at[k]), (out_any.at[chunk(k)], out_ref.at[k])]
    copies = copy_all(pairs + [(kv_any, kv_ref)], sems)

    @pl.when(step == 0)
    def _():
        begin(dec_copies + copies)

    attn_fwd_kernel(
        n_ref, ends_ref, table_ref, pick_ref, x_ref, g1_ref, wq_ref, wk_ref, wv_ref,
        first_ref, heads_ref, mixed_ref, st_ref, u_ref,
    )

    @pl.when(step == PAIRS - 2)
    def _():
        for copy in dec_copies:
            copy.wait()
        dec_self_part(
            dec_table_ref, ans_ref, dg1_ref, dg2_ref, dec_after_ref, lefts_ref, dec_heads_ref, query_ref,
            dqkv_ref, dout_ref, dquery_ref, pad_ref,
        )

    @pl.when(step == PAIRS - 1)
    def _():
        for copy in copies:
            copy.wait()
        after = x_ref[...].astype(WIDER) + product(mixed_ref[...], wo_ref[...])
        after_ref[...] = after
        second = (after * scale_of(after) * row_of(g2_ref)).astype(LOWER)
        second_ref[...] = second
        inner = product(second, in_ref[0])
        sent = send_out([(after_ref, after_any), (second_ref, second_any)], out_sems, 0)
        total = after
        for k in range(STEPS):
            following = product(second, in_ref[k + 1]) if k + 1 < STEPS else None
            value, slope = silu_like(inner)
            slope_ref[:, chunk(k)] = slope.astype(LOWER)
            hidden = value.astype(LOWER)
            hidden_ref[:, chunk(k)] = hidden
            total = total + product(hidden, out_ref[k])
            inner = following
            if k % 2:
                half = slice(WIDTH * (k - 1), WIDTH * (k + 1))
                sent += send_out(
                    [(slope_ref.at[:, half], slope_any.at[:, half]), (hidden_ref.at[:, half], hidden_any.at[:, half])],
                    out_sems, len(sent),
                )
        final_ref[...] = total
        third = (total * scale_of(total) * row_of(g3_ref)).astype(LOWER)
        third_ref[...] = third
        sent += send_out([(final_ref, final_any), (third_ref, third_any)], out_sems, len(sent))
        for k in range(2):
            half = slice(D * k, D * k + D)
            pairs_ref[:, half] = product(third, kv_ref[:, half]).astype(LOWER)
        sent += send_out([(pairs_ref, pairs_any)], out_sems, len(sent))
        cross_kernel(n_ref, query_ref, pairs_ref, packed_ref)
        for copy in sent:
            copy.wait()


def whole(*shape):
    return pl.BlockSpec(shape, lambda s: (0,) * len(shape))


def forward(count, table, pick, x, gain1, qkv, gain2, gain3, wo, ffn_in, ffn_out, kv, dec, after=()):
    def weights_at(first):
        return pl.BlockSpec((D, PAIR), lambda s: (0, first + s))

    kept = [wide(SLOT, D), narrow(SLOT, D), narrow(SLOT, FF), narrow(SLOT, FF), wide(SLOT, D), narrow(SLOT, D), narrow(SLOT, 2 * D)]
    return run(
        "enc_forward",
        forward_kernel,
        [count, table, table, pick, x, gain1, qkv, qkv, qkv, gain2, gain3, *dec[:4], wo, ffn_in, ffn_out, kv, *dec[4:]],
        [SCALARS, SCALARS, WHOLE, WHOLE, whole(SLOT, D), whole(D), weights_at(0), weights_at(PAIRS), weights_at(2 * PAIRS)]
        + [whole(D), whole(D), SCALARS, whole(ANS, D), whole(D), whole(D)] + [ANY] * 7,
        [narrow(SLOT, D), narrow(3, SLOT, D), narrow(SLOT, D), wide(PAIRS, 2, SLOT), wide(GROUP, D + STAT)]
        + [wide(GROUP, D), narrow(GROUP, 3 * D), narrow(GROUP, 3 * D), narrow(GROUP, D)] + kept,
        [whole(SLOT, D), pair_of_all(0), whole(SLOT, D), stats_at(0), whole(GROUP, D + STAT)]
        + [whole(GROUP, D), whole(GROUP, 3 * D), whole(GROUP, 3 * D), whole(GROUP, D)] + [ANY] * 7,
        after=after,
        grid=(PAIRS,),
        scratch=[
            pltpu.VMEM((H, 3 * SPAN), WIDER),
            pltpu.VMEM((D, D), LOWER),
            pltpu.VMEM((STEPS, D, WIDTH), LOWER),
            pltpu.VMEM((STEPS, WIDTH, D), LOWER),
            pltpu.VMEM((D, 2 * D), LOWER),
            pltpu.VMEM((D, 3 * D), LOWER),
            pltpu.VMEM((D, D), LOWER),
            pltpu.VMEM((D, D), LOWER),
            pltpu.VMEM((GROUP, D), WIDER),
        ]
        + [pltpu.VMEM(out.shape, out.dtype) for out in kept]
        + [pltpu.SemaphoreType.DMA((2 * STEPS + 2,)), pltpu.SemaphoreType.DMA((3,)), pltpu.SemaphoreType.DMA((9,))],
        flops=2 * SLOT * D * (D + 2 * FF + 2 * D),
    )


def ffn_back_kernel(
    branch_ref, g2_ref, gfinal_any, after_any, slope_any, out_any, in_any, wo_any,
    ginner_any, gafter_any, low_any, gmixed_any, gain_ref,
    gfinal_ref, after_ref, slope_ref, out_ref, in_ref, wo_ref, ginner_ref, gafter_ref, low_ref, gmixed_ref,
    sems, out_sems,
):
    pairs = []
    for k in range(STEPS):
        pairs += [(out_any.at[chunk(k)], out_ref.at[k]), (slope_any.at[:, chunk(k)], slope_ref.at[k])]
        pairs += [(in_any.at[:, chunk(k)], in_ref.at[k])]
    copies = copy_all(pairs + [(after_any, after_ref), (gfinal_any, gfinal_ref), (wo_any, wo_ref)], sems)
    begin(copies[:4])
    branch = branch_ref[...]
    copies[0].wait()
    begin(copies[4:7])
    grad = right_product(branch, out_ref[0])
    total = None
    sent = []
    for k in range(STEPS):
        copies[3 * k + 1].wait()
        copies[3 * k + 2].wait()
        copies[3 * k + 3].wait()
        begin(copies[3 * k + 7 : 3 * k + 10])
        following = right_product(branch, out_ref[k + 1]) if k + 1 < STEPS else None
        inner = (grad * slope_ref[k].astype(WIDER)).astype(LOWER)
        ginner_ref[:, chunk(k)] = inner
        term = right_product(inner, in_ref[k])
        total = term if total is None else total + term
        grad = following
        sent += send_out([(ginner_ref.at[:, chunk(k)], ginner_any.at[:, chunk(k)])], out_sems, len(sent))
    copies[3 * STEPS + 1].wait()
    copies[3 * STEPS + 2].wait()
    back, gain = norm_pull(after_ref[...], row_of(g2_ref), total)
    gain_ref[...] = gain
    g_after = gfinal_ref[...] + back
    gafter_ref[...] = g_after
    low = g_after.astype(LOWER)
    low_ref[...] = low
    sent += send_out([(gafter_ref, gafter_any), (low_ref, low_any)], out_sems, len(sent))
    gmixed_ref[...] = right_product(low, wo_ref[...]).astype(LOWER)
    sent += send_out([(gmixed_ref, gmixed_any)], out_sems, len(sent))
    for copy in sent:
        copy.wait()


def ffn_back(branch, ffn_out, slope, ffn_in, after_rows, gain2, g_final, wo, after=()):
    outs = [narrow(SLOT, FF), wide(SLOT, D), narrow(SLOT, D), narrow(SLOT, D)]
    return run(
        "enc_ffn_back",
        ffn_back_kernel,
        [branch, gain2, g_final, after_rows, slope, ffn_out, ffn_in, wo],
        [WHOLE] * 2 + [ANY] * 6,
        outs + [wide(1, D)],
        [ANY] * 4 + [WHOLE],
        after=after,
        scratch=[
            pltpu.VMEM((SLOT, D), WIDER),
            pltpu.VMEM((SLOT, D), WIDER),
            pltpu.VMEM((STEPS, SLOT, WIDTH), LOWER),
            pltpu.VMEM((STEPS, WIDTH, D), LOWER),
            pltpu.VMEM((STEPS, D, WIDTH), LOWER),
            pltpu.VMEM((D, D), LOWER),
        ]
        + [pltpu.VMEM(out.shape, out.dtype) for out in outs]
        + [pltpu.SemaphoreType.DMA((3 * STEPS + 3,)), pltpu.SemaphoreType.DMA((STEPS + 3,))],
        flops=2 * SLOT * D * (D + 2 * FF),
    )


def attention_end(
    count, table, pick, heads, grad_mixed, mixed, stats, begun, diagonal, qkv, x, gain1,
    g_after, gain2, gain3, pick_back, after=(),
):
    base = FIRST
    half = PAIRS - FIRST
    inner = attn_bwd_kernel(base)

    def body(
        n_ref, ends_ref, table_ref, pick_ref, h_ref, g_ref, o_ref, st_ref, begun_any,
        da_ref, x_ref, g1_ref, gain2_ref, gain3_ref, back_ref, qkv_any, gafter_any,
        gh_any, small_ref, gb_ref, grows_any,
        u_ref, gh_ref, gall_ref, w_ref, gafter_ref, grows_ref, sems, out_sems,
    ):
        step = pl.program_id(0)
        old = slice(0, base * PAIR)
        loads = copy_all([(begun_any.at[:, :, old], gall_ref.at[:, :, old]), (qkv_any, w_ref), (gafter_any, gafter_ref)], sems)

        @pl.when(step == 0)
        def _():
            for load in loads:
                load.start()

        inner(n_ref, ends_ref, table_ref, pick_ref, h_ref, g_ref, o_ref, st_ref, gh_ref, gb_ref, u_ref)
        for k in range(half):

            @pl.when(step == k)
            def _():
                place = slice((base + k) * PAIR, (base + k + 1) * PAIR)
                gall_ref[:, :, place] = gh_ref[...]
                sums_ref = gb_ref.at[0]
                small_ref[2 * k : 2 * k + 2] = sums_ref[:2]

        @pl.when(step == half - 1)
        def _():
            new = slice(base * PAIR, D)
            sent = send_out([(gall_ref.at[:, :, new], gh_any.at[:, :, new])], out_sems, 0)
            for load in loads:
                load.wait()
            total = right_product(gall_ref[0], w_ref[:, :D])
            total = total + right_product(gall_ref[1], w_ref[:, D : 2 * D])
            total = total + right_product(gall_ref[2], w_ref[:, 2 * D :])
            back, gain = norm_pull(x_ref[...].astype(WIDER), row_of(g1_ref), total)
            grows_ref[...] = gafter_ref[...] + back
            sent += send_out([(grows_ref, grows_any)], out_sems, 1)
            sums = [da_ref[k, :2] for k in range(base)]
            sums += [small_ref[2 * k : 2 * k + 2] for k in range(half)]
            found = split_product(jnp.concatenate(sums, axis=0), back_ref[...], 2)
            small_ref[...] = jnp.zeros((16, D + 2 * EDGE), WIDER)
            small_ref[0:1, :D] = gain
            small_ref[1:2, :D] = gain2_ref[...]
            small_ref[2:3, :D] = gain3_ref[...]
            small_ref[4:16, :STAT] = found
            for copy in sent:
                copy.wait()

    rows = whole(SLOT, D)
    grads, small, unused, g_rows, token = run(
        "enc_attention_end",
        body,
        [count, table, table, pick, heads, grad_mixed, mixed, stats, begun]
        + [diagonal, x, gain1, gain2, gain3, pick_back, qkv, g_after],
        [SCALARS, SCALARS, WHOLE, WHOLE, pair_of_all(base), columns_at(base), columns_at(base), stats_at(base), ANY]
        + [whole(*diagonal.shape), rows, whole(D), whole(1, D), whole(1, D), whole(4 * SPAN, STAT), ANY, ANY],
        [narrow(3, SLOT, D), wide(16, D + 2 * EDGE), wide(half, 8, 4 * SPAN), wide(SLOT, D)],
        [ANY, whole(16, D + 2 * EDGE), pl.BlockSpec((1, 8, 4 * SPAN), lambda s: (s, 0, 0)), ANY],
        after=after,
        grid=(half,),
        scratch=[
            pltpu.VMEM((H, 3 * SPAN), WIDER),
            pltpu.VMEM((3, SLOT, PAIR), LOWER),
            pltpu.VMEM((3, SLOT, D), LOWER),
            pltpu.VMEM((D, 3 * D), LOWER),
            pltpu.VMEM((SLOT, D), WIDER),
            pltpu.VMEM((SLOT, D), WIDER),
            pltpu.SemaphoreType.DMA((3,)),
            pltpu.SemaphoreType.DMA((2,)),
        ],
        flops=2 * 5 * H * SLOT * SLOT * HD * 4,
        alias={8: 0},
    )
    return g_rows, small, unused, grads, token


def head_lanes(h):
    lanes = lax.broadcasted_iota(jnp.int32, (GROUP, D), 1)
    return (lanes >= h * HD) & (lanes < (h + 1) * HD)


def stack_heads(flat):
    return jnp.concatenate([jnp.where(head_lanes(h), flat, 0.0) for h in range(H)], axis=0)


def merge_heads(stacked):
    total = jnp.zeros((GROUP, D), WIDER)
    for h in range(H):
        total = total + jnp.where(head_lanes(h), stacked[GROUP * h : GROUP * h + GROUP], 0.0)
    return total


def lanes_to_column(stat):
    lanes = lax.broadcasted_iota(jnp.int32, (GROUP, STAT), 1)
    parts = [jnp.sum(jnp.where(lanes == h, stat, 0.0), axis=1, keepdims=True) for h in range(H)]
    return jnp.concatenate(parts, axis=0)


def column_to_lanes(column, first):
    lanes = lax.broadcasted_iota(jnp.int32, (GROUP, STAT), 1)
    total = jnp.zeros((GROUP, STAT), WIDER)
    for h in range(H):
        total = total + jnp.where(lanes == first + h, column[GROUP * h : GROUP * h + GROUP], 0.0)
    return total


def spread_heads(stat):
    rows = lax.broadcasted_iota(jnp.int32, (STAT, D), 0) * HD
    lanes = lax.broadcasted_iota(jnp.int32, (STAT, D), 1)
    spread = jnp.where((lanes >= rows) & (lanes < rows + HD), 1.0, 0.0).astype(LOWER)
    return split_product(stat, spread, 2)


def own_scores(query, keys, table_ref):
    raw = right_product(query, keys)
    rows = lax.broadcasted_iota(jnp.int32, (GROUP, GROUP), 0)
    columns = lax.broadcasted_iota(jnp.int32, (GROUP, GROUP), 1)
    away = rows - columns
    parts = []
    for h in range(H):
        bias = jnp.full((GROUP, GROUP), table_ref[h, 0], WIDER)
        for d in range(1, GROUP):
            bias = jnp.where(away == d, table_ref[h, d], bias)
        part = raw[GROUP * h : GROUP * h + GROUP] + bias
        parts.append(jnp.where(away >= 0, part, MASKED))
    scores = jnp.concatenate(parts, axis=0)
    powers = jnp.exp(scores - jnp.max(scores, axis=1, keepdims=True))
    return powers / jnp.sum(powers, axis=1, keepdims=True)


def padded(ref, pad_ref):
    pad_ref[...] = jnp.zeros((GROUP, D), WIDER)
    pad_ref[:ANS] = ref[...].astype(WIDER)
    return pad_ref[...]


def answer_rows(width):
    return lax.broadcasted_iota(jnp.int32, (GROUP, width), 0) < ANS


def dec_self_part(
    table_ref, x_ref, g1_ref, g2_ref, after_ref, lefts_ref, heads_ref, query_ref, qkv_ref, out_ref, cross_ref, pad_ref
):
    start = padded(x_ref, pad_ref)
    first = (start * scale_of(start) * row_of(g1_ref)).astype(LOWER)
    heads = product(first, qkv_ref[...]).astype(LOWER)
    heads_ref[...] = heads
    query = stack_heads(heads.astype(WIDER)[:, :D] * 0.125).astype(LOWER)
    probs = own_scores(query, heads[:, D : 2 * D], table_ref)
    own = merge_heads(product(probs.astype(LOWER), heads[:, 2 * D :]))
    own = jnp.where(answer_rows(D), own, 0.0).astype(LOWER)
    after = start + product(own, out_ref[...])
    after_ref[...] = after
    second = (after * scale_of(after) * row_of(g2_ref)).astype(LOWER)
    query_ref[...] = product(second, cross_ref[...]).astype(LOWER)
    lefts_ref[:, :D] = first
    lefts_ref[:, D : 2 * D] = own
    lefts_ref[:, 2 * D :] = second


def masked_cross(n_ref, query_ref, pairs_ref):
    query = stack_heads(query_ref[...].astype(WIDER) * 0.125).astype(LOWER)
    raw = right_product(query, pairs_ref[:, :D])
    places = lax.broadcasted_iota(jnp.int32, (STACK, SLOT), 1)
    return query, jnp.where(places < n_ref[0], raw, MASKED)


def cross_kernel(n_ref, query_ref, pairs_ref, packed_ref):
    unused, scores = masked_cross(n_ref, query_ref, pairs_ref)
    top = jnp.max(scores, axis=1, keepdims=True)
    powers = jnp.exp(scores - top)
    total = jnp.sum(powers, axis=1, keepdims=True)
    probs = (powers / total).astype(LOWER)
    packed_ref[:, :D] = merge_heads(product(probs, pairs_ref[:, D:]))
    packed_ref[:, D:] = column_to_lanes(top, 0) + column_to_lanes(total, STAT // 2)


def dec_mid_kernel(
    n_ref, parts_ref, after_ref, cot_ref, g3_ref, lefts_ref, query_ref, e3_ref,
    pairs_any, cross_any, in_any, out_any, kv_any, final_any,
    answer_ref, early_ref, gmid_ref, gain_ref, partial_ref, gain_enc_ref, gpairs_any, gfinal_any, branch_any,
    pairs_ref, cross_ref, in_ref, out_ref, kv_ref, final_ref, gpairs_ref, gfinal_ref, branch_ref, pad_ref,
    sems, out_sems,
):
    held_pairs = ((cross_any, cross_ref), (in_any, in_ref), (out_any, out_ref), (pairs_any, pairs_ref))
    copies = copy_all(held_pairs + ((kv_any, kv_ref), (final_any, final_ref)), sems)
    begin(copies[:2])
    size = parts_ref.shape[0]
    used = lax.broadcasted_iota(jnp.int32, (GROUP, STAT), 1) < H
    tops = [parts_ref[k, :, D:] for k in range(size)]
    totals = [pltpu.roll(stat, STAT // 2, 1) for stat in tops]
    top = tops[0]
    for k in range(1, size):
        top = jnp.maximum(top, tops[k])
    weights = [jnp.where(used, totals[k] * jnp.exp(tops[k] - top), 0.0) for k in range(size)]
    total = weights[0]
    for k in range(1, size):
        total = total + weights[k]
    total = jnp.where(used, total, 1.0)
    mix = jnp.zeros((GROUP, D), WIDER)
    for k in range(size):
        mix = mix + parts_ref[k, :, :D] * spread_heads(weights[k] / total)
    mix_low = mix.astype(LOWER)
    copies[0].wait()
    begin(copies[2:3])
    middle = after_ref[...] + product(mix_low, cross_ref[...])
    third = (middle * scale_of(middle) * row_of(g3_ref)).astype(LOWER)
    copies[1].wait()
    begin(copies[3:])
    inner = product(third, in_ref[...])
    value, slope = silu_like(inner)
    hidden = value.astype(LOWER)
    copies[2].wait()
    answer = (middle + product(hidden, out_ref[...])).astype(LOWER)
    answer_ref[...] = answer[:ANS]
    grad = padded(cot_ref, pad_ref)
    out_low = grad.astype(LOWER)
    g_inner = (right_product(out_low, out_ref[...]) * slope).astype(LOWER)
    back, gain = norm_pull(middle, row_of(g3_ref), right_product(g_inner, in_ref[...]))
    gain_ref[...] = gain
    g_middle = grad + back
    gmid_ref[...] = g_middle
    middle_low = g_middle.astype(LOWER)
    g_mix = right_product(middle_low, cross_ref[...]).astype(LOWER)

    def store(name, rows):
        early_ref[:, AT[name] : AT[name] + rows.shape[1]] = rows

    def kept(rows):
        return jnp.where(answer_rows(rows.shape[1]), rows.astype(WIDER), 0.0).astype(LOWER)

    early_ref[:, : 3 * D] = kept(lefts_ref[...])
    store("mix", kept(mix_low))
    store("third", kept(third))
    store("hidden", kept(hidden))
    store("g_middle", middle_low)
    store("g_inner", g_inner)
    store("g_out", out_low)
    copies[3].wait()
    copies[4].wait()
    copies[5].wait()
    query, scores = masked_cross(n_ref, query_ref, pairs_ref)
    probs = jnp.exp(scores - lanes_to_column(jnp.where(used, top, 0.0))) / lanes_to_column(total)
    grad = stack_heads(g_mix.astype(WIDER))
    weighted = jnp.sum(grad * jnp.concatenate([mix] * H, axis=0), axis=1, keepdims=True)
    grad = grad.astype(LOWER)
    grad_probs = right_product(grad, pairs_ref[:, D:])
    rounded = (probs * (grad_probs - weighted)).astype(LOWER)
    g_keys = left_product(rounded, query).astype(LOWER)
    g_values = left_product(probs.astype(LOWER), grad).astype(LOWER)
    gpairs_ref[:, :D] = g_keys
    gpairs_ref[:, D:] = g_values
    sent = send_out([(gpairs_ref, gpairs_any)], out_sems, 0)
    partial_ref[...] = merge_heads(product(rounded, pairs_ref[:, :D])) * 0.125
    g_third = right_product(g_keys, kv_ref[:, :D]) + right_product(g_values, kv_ref[:, D:])
    back, gain = norm_pull(final_ref[...], row_of(e3_ref), g_third)
    gain_enc_ref[...] = gain
    gfinal_ref[...] = back
    branch_ref[...] = back.astype(LOWER)
    sent += send_out([(gfinal_ref, gfinal_any), (branch_ref, branch_any)], out_sems, 1)
    for copy in sent:
        copy.wait()


def dec_back_kernel(
    table_ref, x_ref, part_ref, got_ref, after_ref, gmid_ref, heads_ref,
    g1_ref, g2_ref, gain3_ref, query_any, out_any, qkv_any,
    late_ref, gstart_ref,
    cross_ref, out_ref, qkv_ref, pad_ref, sems,
):
    copies = copy_all(((query_any, cross_ref), (out_any, out_ref), (qkv_any, qkv_ref)), sems)
    begin(copies[:2])
    g_query = (part_ref[...] + got_ref[...]).astype(LOWER)
    copies[0].wait()
    begin(copies[2:])
    back, gain2 = norm_pull(after_ref[...], row_of(g2_ref), right_product(g_query, cross_ref[...]))
    g_after = gmid_ref[...] + back
    after_low = g_after.astype(LOWER)
    copies[1].wait()
    g_own = stack_heads(right_product(after_low, out_ref[...])).astype(LOWER)
    heads = heads_ref[...]
    query = stack_heads(heads.astype(WIDER)[:, :D] * 0.125).astype(LOWER)
    probs = own_scores(query, heads[:, D : 2 * D], table_ref)
    grad_probs = right_product(g_own, heads[:, 2 * D :])
    rounded = (probs * (grad_probs - jnp.sum(probs * grad_probs, axis=1, keepdims=True))).astype(LOWER)
    g_q = (merge_heads(product(rounded, heads[:, D : 2 * D])) * 0.125).astype(LOWER)
    g_k = left_product(rounded, query).astype(LOWER)
    g_v = left_product(probs.astype(LOWER), g_own).astype(LOWER)
    g_heads = jnp.concatenate([g_q, g_k, g_v], axis=1)
    copies[2].wait()
    start = padded(x_ref, pad_ref)
    back, gain1 = norm_pull(start, row_of(g1_ref), right_product(g_heads, qkv_ref[...]))
    gstart_ref[...] = (g_after + back)[:ANS]
    spread = rounded.astype(WIDER)
    rows = lax.broadcasted_iota(jnp.int32, (GROUP, GROUP), 0)
    columns = lax.broadcasted_iota(jnp.int32, (GROUP, GROUP), 1)
    mirror = jnp.where(rows + columns == GROUP - 1, 1.0, 0.0).astype(LOWER)
    empty = jnp.zeros((GROUP, STAT - GROUP), WIDER)
    tables = []
    for h in range(H):
        part = product(mirror, spread[GROUP * h : GROUP * h + GROUP].astype(LOWER))
        turned = pltpu.roll(jnp.concatenate([part, empty], axis=1), 0, 1, stride=1, stride_axis=0)
        tables.append(jnp.sum(turned, axis=0, keepdims=True))
    small = jnp.concatenate([gain1, gain2, gain3_ref[...]] + tables, axis=1)
    places = lax.broadcasted_iota(jnp.int32, (GROUP, LATE), 0)
    late = jnp.concatenate([g_heads, after_low, g_query], axis=1).astype(WIDER)
    late_ref[...] = jnp.where(places == ANS, small, late).astype(LOWER)


def dec_outer_kernel(size):
    part = D // size

    def body(me_ref, *refs):
        me = me_ref[0]
        small_ref = refs[9]
        there, here = refs[3:9], refs[10:16]
        early_ref, late_ref, sems = refs[16:]
        sent = []
        early_ref[...] = jnp.concatenate([refs[0][me ^ s].astype(WIDER) for s in range(size)], axis=0).astype(LOWER)
        late = [ref[...].astype(WIDER) for ref in refs[1:3]]
        late_ref[...] = jnp.concatenate(late, axis=0).astype(LOWER)
        rows = lax.broadcasted_iota(jnp.int32, (part, D), 0) + me * part
        lanes = lax.broadcasted_iota(jnp.int32, (part, D), 1)
        picked = jnp.where(rows == lanes, 1.0, 0.0).astype(LOWER)
        height = FF // size
        first = pl.multiple_of(AT["hidden"] + me * height, 128)

        def outer(k, name, right):
            left = right_product(picked, early_ref[:, AT[name] : AT[name] + D]).astype(LOWER)
            here[k][...] = product(left, right)
            sent.extend(send_out([(here[k], there[k])], sems, len(sent)))

        outer(4, "third", early_ref[:, AT["g_inner"] : AT["g_inner"] + FF])
        outer(0, "first", late_ref[:, : 3 * D])
        here[5][...] = left_product(early_ref[:, pl.ds(first, height)], early_ref[:, AT["g_out"] : AT["g_out"] + D])
        sent.extend(send_out([(here[5], there[5])], sems, len(sent)))
        outer(1, "own", late_ref[:, AT["g_after"] : AT["g_after"] + D])
        outer(2, "second", late_ref[:, AT["g_query"] : AT["g_query"] + D])
        outer(3, "mix", early_ref[:, AT["g_middle"] : AT["g_middle"] + D])
        total = jnp.zeros((1, LATE), WIDER)
        for part_late in late:
            for k in (0, GROUP):
                total = total + part_late[k + ANS : k + ANS + 1]
        small_ref[...] = total
        for copy in sent:
            copy.wait()

    return body


def held(*shapes):
    return [pltpu.VMEM(shape, LOWER) for shape in shapes] + [
        pltpu.VMEM((GROUP, D), WIDER),
        pltpu.SemaphoreType.DMA((len(shapes),)),
    ]


def dec_mid(count, parts, after_rows, cotangent, gain3, lefts, query, enc_gain3, pairs, cross_out, ffn_in, ffn_out, kv, final, after=()):
    outs = [narrow(SLOT, 2 * D), wide(SLOT, D), narrow(SLOT, D)]
    shapes = [(SLOT, 2 * D), (D, D), (D, FF), (FF, D), (D, 2 * D)]
    return run(
        "dec_mid",
        dec_mid_kernel,
        [count, parts, after_rows, cotangent, gain3, lefts, query, enc_gain3, pairs, cross_out, ffn_in, ffn_out, kv, final],
        [SCALARS] + [WHOLE] * 7 + [ANY] * 6,
        [narrow(ANS, D), narrow(GROUP, EARLY), wide(GROUP, D), wide(1, D), wide(GROUP, D), wide(1, D)] + outs,
        [WHOLE] * 6 + [ANY] * 3,
        after=after,
        scratch=[pltpu.VMEM(shape, LOWER) for shape in shapes]
        + [pltpu.VMEM((SLOT, D), WIDER)]
        + [pltpu.VMEM(out.shape, out.dtype) for out in outs]
        + [pltpu.VMEM((GROUP, D), WIDER), pltpu.SemaphoreType.DMA((6,)), pltpu.SemaphoreType.DMA((3,))],
        flops=4 * 10**9,
    )


def dec_back(table, answers, part, got, after_rows, g_middle, heads, gain1, gain2, g_gain3, query, out, qkv, after=()):
    return run(
        "dec_back",
        dec_back_kernel,
        [table, answers, part, got, after_rows, g_middle, heads, gain1, gain2, g_gain3, query, out, qkv],
        [SCALARS] + [WHOLE] * 9 + [ANY] * 3,
        [narrow(GROUP, LATE), wide(ANS, D)],
        after=after,
        scratch=held((D, D), (D, D), (D, 3 * D)),
        flops=0,
    )


def dec_outer(me, early, late_one, late_two, size, after=()):
    part = D // size
    outs = [wide(part, 3 * D), wide(part, D), wide(part, D), wide(part, D), wide(part, FF), wide(FF // size, D)]
    return run(
        "dec_outer",
        dec_outer_kernel(size),
        [me, early, late_one, late_two],
        [SCALARS, WHOLE, WHOLE, WHOLE],
        outs + [wide(1, LATE)],
        [ANY] * 6 + [WHOLE],
        after=after,
        scratch=[pltpu.VMEM(out.shape, WIDER) for out in outs]
        + [pltpu.VMEM((size * GROUP, EARLY), LOWER), pltpu.VMEM((size * GROUP, LATE), LOWER), pltpu.SemaphoreType.DMA((6,))],
        flops=8 * 10**9,
    )


def stack_late(one, two, after=()):
    def body(one_ref, two_ref, out_ref):
        out_ref[...] = jnp.concatenate([one_ref[...].astype(WIDER), two_ref[...].astype(WIDER)], axis=0).astype(LOWER)

    return run("stack_late", body, [one, two], [WHOLE] * 2, [narrow(2 * GROUP, LATE)], after=after, flops=0)


PLACES = [(0, 0), (0, 1), (1, 0), (1, 1)]


def place_of(me, there):
    return me ^ (4 * there[0] + 2 * there[1])


def turned_rows(me, acts, block):
    lanes = lax.broadcasted_iota(jnp.int32, (block, D), 1)
    rows = lax.broadcasted_iota(jnp.int32, (block, D), 0)
    picked = [jnp.where(lanes - rows == place_of(me, t) * block, 1.0, 0.0).astype(LOWER) for t in PLACES]
    picked = jnp.concatenate(picked, axis=0)
    return jnp.concatenate([right_product(picked, act).astype(LOWER) for act in acts], axis=1)


def target(there, x_refs, y_refs):
    dy, dx = there
    return (x_refs[dx].at[dy], y_refs[dy].at[dx])


def pages_out(pairs, sems, first):
    return send_out([(here.at[k], there.at[k]) for here, there in pairs for k in range(2)], sems, first)


def one_kernel(
    me_ref, t_own, t_par, p_own, p_par, h_own, h_par, b_own, b_par, xk_any, xs_any, yk_any, ys_any,
    xk, xs, yk, ys, t, p, h, b, sems, out_sems,
):
    me = me_ref[0]
    block = FF // 8
    pairs = [(t_own, t.at[0]), (t_par, t.at[1]), (p_own, p.at[:SLOT]), (p_par, p.at[SLOT:])]
    pairs += [(b_own, b.at[:SLOT]), (b_par, b.at[SLOT:])]
    for k, there in enumerate(PLACES):
        lanes = pl.ds(pl.multiple_of(place_of(me, there) * block, 128), block)
        pairs += [(h_own.at[:, lanes], h.at[k, :SLOT]), (h_par.at[:, lanes], h.at[k, SLOT:])]
    copies = copy_all(pairs, sems)
    begin(copies[:4])
    copies[0].wait()
    copies[1].wait()
    begin(copies[4:8])
    height = D // 8
    left = turned_rows(me, (t[0], t[1]), height)
    copies[2].wait()
    copies[3].wait()
    begin(copies[8:])
    for c in range(2):
        grad = product(left, p[:, D * c : D * c + D]).astype(LOWER)
        for k, there in enumerate(PLACES):
            to, unused = target(there, (xk, xs), (yk, ys))
            to[height * c : height * c + height] = grad[height * k : height * k + height]
    for k in range(4, 8):
        copies[k].wait()
    sent = []
    for k, there in enumerate(PLACES):
        grad = left_product(h[k], b[...]).astype(LOWER)
        to_x, to_y = target(there, (xk, xs), (yk, ys))
        to_x[2 * height : 3 * height] = grad[:height]
        to_y[...] = grad[height:]
        out_x, out_y = target(there, (xk_any, xs_any), (yk_any, ys_any))
        if k + 1 < len(PLACES):
            copies[8 + 2 * k].wait()
            copies[9 + 2 * k].wait()
        sent += send_out([(to_x, out_x), (to_y, out_y)], out_sems, len(sent))
    for copy in sent:
        copy.wait()


def two_kernel(
    me_ref, s_own, s_par, i_own, i_par, m_own, m_par, l_own, l_par, xk_any, xs_any, yk_any, ys_any,
    xk, xs, yk, ys, s, i, m, l, sems, out_sems,
):
    me = me_ref[0]
    pairs = [(s_own, s.at[0]), (s_par, s.at[1]), (m_own, m.at[0]), (m_par, m.at[1])]
    pairs += [(l_own, l.at[:SLOT]), (l_par, l.at[SLOT:])]
    for c in range(4):
        lanes = slice(D * c, D * c + D)
        pairs += [(i_own.at[:, lanes], i.at[c, :SLOT]), (i_par.at[:, lanes], i.at[c, SLOT:])]
    copies = copy_all(pairs, sems)
    begin(copies[:6])
    for k in range(4):
        copies[k].wait()
    begin(copies[6:10])
    height = D // 8
    half = height // 2
    left = turned_rows(me, (m[0], m[1]), height)
    turned = turned_rows(me, (s[0], s[1]), height)
    copies[4].wait()
    copies[5].wait()
    begin(copies[10:])
    grad = product(left, l[...]).astype(LOWER)
    for k, there in enumerate(PLACES):
        for to, first in zip(target(there, (xk, xs), (yk, ys)), (0, half)):
            to[2 * height : 2 * height + half] = grad[height * k + first : height * k + first + half]
    sent = []
    for c in range(4):
        if c % 2 == 0:
            for k in range(6 + 2 * c, 10 + 2 * c):
                copies[k].wait()
        grad = product(turned, i[c]).astype(LOWER)
        for k, there in enumerate(PLACES):
            to = target(there, (xk, xs), (yk, ys))[c // 2]
            to[height * (c % 2) : height * (c % 2) + height] = grad[height * k : height * k + height]
        if c % 2:
            done = ((xk, xk_any), (xs, xs_any)) if c == 1 else ((yk, yk_any), (ys, ys_any))
            sent += pages_out(done, out_sems, len(sent))
    for copy in sent:
        copy.wait()


def three_kernel(
    me_ref, f_own, f_par, g_own, g_par, small_ref, got_ref, xk_any, xs_any, yk_any, ys_any,
    xk, xs, yk, ys, f, g, sems, out_sems,
):
    me = me_ref[0]
    small = (small_ref[:, :D] + got_ref[:, :D]).astype(LOWER)
    pairs = [(f_own, f.at[0]), (f_par, f.at[1])]
    for c in range(3):
        pairs += [(g_own.at[c], g.at[c, :SLOT]), (g_par.at[c], g.at[c, SLOT:])]
    copies = copy_all(pairs, sems)
    begin(copies[:4])
    copies[0].wait()
    copies[1].wait()
    begin(copies[4:])
    height = D // 8
    half = D // 2
    left = turned_rows(me, (f[0], f[1]), height)
    for ref in (xk, xs, yk, ys):
        for k in range(2):
            ref[k, height:] = jnp.zeros((16, 3 * half), LOWER)
            if ref is xk or ref is xs:
                ref[k, height:, :D] = small
    copies[2].wait()
    copies[3].wait()
    sent = []
    for c in range(3):
        if c == 1:
            for k in range(4, 8):
                copies[k].wait()
        grad = product(left, g[c]).astype(LOWER)
        for k, there in enumerate(PLACES):
            to_x, to_y = target(there, (xk, xs), (yk, ys))
            block = grad[height * k : height * k + height]
            if c == 0:
                to_x[:height, :D] = block
            elif c == 1:
                to_x[:height, D:] = block[:, :half]
                to_y[:height, :half] = block[:, half:]
            else:
                to_y[:height, half:] = block
        if c:
            done = ((xk, xk_any), (xs, xs_any)) if c == 1 else ((yk, yk_any), (ys, ys_any))
            sent += pages_out(done, out_sems, len(sent))
    for copy in sent:
        copy.wait()


def weight_call(name, body, me, ins, rows, columns, held_shapes, flops, after, extra=()):
    out = narrow(2, rows, columns)
    copies = {"weights_one": 14, "weights_two": 14, "weights_three": 8}[name]
    return run(
        name,
        body,
        [me, *ins, *extra],
        [SCALARS] + [ANY] * len(ins) + [WHOLE] * len(extra),
        [out] * 4,
        [ANY] * 4,
        after=after,
        scratch=[pltpu.VMEM(out.shape, LOWER)] * 4
        + [pltpu.VMEM(shape, LOWER) for shape in held_shapes]
        + [pltpu.SemaphoreType.DMA((copies,)), pltpu.SemaphoreType.DMA((8,))],
        flops=flops,
    )


def weights_one(me, third, g_pairs, hidden, branch, after=()):
    shapes = [(2, SLOT, D), (2 * SLOT, 2 * D), (4, 2 * SLOT, FF // 8), (2 * SLOT, D)]
    ins = (*third, *g_pairs, *hidden, *branch)
    return weight_call("weights_one", one_kernel, me, ins, 3 * D // 8, D, shapes, 4 * 10**9, after)


def weights_two(me, second, g_inner, mixed, low, after=()):
    shapes = [(2, SLOT, D), (4, 2 * SLOT, D), (2, SLOT, D), (2 * SLOT, D)]
    ins = (*second, *g_inner, *mixed, *low)
    return weight_call("weights_two", two_kernel, me, ins, 5 * D // 16, D, shapes, COST[6], after)


def weights_three(me, first, grads, small, after=()):
    shapes = [(2, SLOT, D), (3, 2 * SLOT, D)]
    ins = (*first, *grads)
    return weight_call("weights_three", three_kernel, me, ins, D // 8 + 16, 3 * D // 2, shapes, COST[4], after, small)


def page(array, k):
    return pl.BlockSpec((1,) + array.shape[1:], lambda s: (k, 0, 0))


def add_first(parts, flops=0, after=()):
    count = len(parts)

    def body(*refs):
        for k in range(count):
            refs[2 * count + k][...] = (refs[2 * k][0].astype(WIDER) + refs[2 * k + 1][0].astype(WIDER)).astype(LOWER)

    flat = [a for pair in parts for a in pair]
    outs = [narrow(*keep.shape[1:]) for keep, unused in parts]
    return run("add_first", body, flat, [page(a, 1) for a in flat], outs, after=after, grid=(1,), flops=flops)


def add_second(parts, after=()):
    shapes = [keep.shape[1:] for keep, unused, unused_too in parts]

    def body(*refs):
        first = 0
        for k, (high, across) in enumerate(shapes):
            keep, got, last = refs[3 * k : 3 * k + 3]
            total = keep[0].astype(WIDER) + got[0].astype(WIDER) + last[...].astype(WIDER)
            refs[-1][first : first + high] = total.astype(LOWER)
            first += high

    flat = [a for trio in parts for a in trio]
    specs = [page(a, 0) if a.ndim == 3 else WHOLE for a in flat]
    rows = sum(shape[0] for shape in shapes)
    return run("add_second", body, flat, specs, [narrow(rows, shapes[0][1])], after=after, grid=(1,), flops=0)


def add_pair(one, two, flops=0, after=()):
    def body(one_ref, two_ref, out_ref):
        out_ref[...] = (one_ref[...].astype(WIDER) + two_ref[...].astype(WIDER)).astype(LOWER)

    return run("add_pair", body, [one, two], [WHOLE] * 2, [narrow(*one.shape)], after=after, flops=flops)


def add_last(me, parts, after=()):
    rows, across = parts[0][0].shape[1:]
    quarter = (rows + 16) // 4

    def body(me_ref, *refs):
        total_ref = refs[-1]
        for k in range(2):
            keep, got, last = refs[3 * k : 3 * k + 3]
            total = keep[0].astype(WIDER) + got[0].astype(WIDER) + last[...].astype(WIDER)
            total_ref[:rows, across * k : across * k + across] = total.astype(LOWER)
        total_ref[rows:] = jnp.zeros((16, 2 * across), LOWER)
        for k in range(4):
            first = pl.multiple_of((me_ref[0] ^ k) * quarter, 16)
            refs[6 + k][...] = total_ref[pl.ds(first, quarter), :]

    flat = [a for trio in parts for a in trio]
    specs = [page(a, 0) if a.ndim == 3 else WHOLE for a in flat]
    outs = [narrow(quarter, 2 * across)] * 4
    scratch = [pltpu.VMEM((4 * quarter, 2 * across), LOWER)]
    return run("add_last", body, [me, *flat], [SCALARS] + specs, outs, [WHOLE] * 4, after=after, grid=(1,), scratch=scratch, flops=0)


def add_parts(parts, after=()):
    def body(*refs):
        total = refs[0][...].astype(WIDER)
        for ref in refs[1:4]:
            total = total + ref[...].astype(WIDER)
        refs[4][...] = total.astype(LOWER)

    return run("add_parts", body, parts, [WHOLE] * 4, [narrow(*parts[0].shape)], after=after, flops=0)


def join_parts(me, parts, rows, after=()):
    high, across = parts[0].shape

    def body(me_ref, *refs):
        total_ref = refs[6]
        for k in range(4):
            first = pl.multiple_of((me_ref[0] ^ k) * high, 8)
            total_ref[pl.ds(first, high), :] = refs[k][...].astype(WIDER)
        refs[4][...] = total_ref[:rows]
        refs[5][...] = total_ref[rows : rows + 16, :D]

    scratch = [pltpu.VMEM((4 * high, across), WIDER)]
    outs = [wide(rows, across), wide(16, D)]
    return run("join_parts", body, [me, *parts], [SCALARS] + [WHOLE] * 4, outs, after=after, scratch=scratch, flops=0)


def join_two(me, share, got, after=()):
    rows, across = share.shape
    block = rows // 5

    def body(me_ref, share_ref, got_ref, in_ref, out_ref):
        here = me_ref[0]
        inner = (here == 1) | (here == 2)
        total = jnp.where(inner, share_ref[...].astype(WIDER), got_ref[...].astype(WIDER))
        for c in range(4):
            first = block * c + (block // 2) * (c // 2)
            in_ref[:, across * c : across * c + across] = total[first : first + block]
        half = block // 2
        out_ref[:half] = total[2 * block : 2 * block + half]
        out_ref[half:] = total[4 * block + half :]

    outs = [wide(block, 4 * across), wide(block, across)]
    return run("join_two", body, [me, share, got], [SCALARS, WHOLE, WHOLE], outs, after=after, flops=0)


def add_rows(one, two, after=()):
    def body(one_ref, two_ref, out_ref):
        out_ref[...] = one_ref[...] + two_ref[...]

    return run("add_rows", body, [one, two], [WHOLE] * 2, [wide(*one.shape)], after=after, flops=0)


def partner(axis, bit):
    return [(k, k ^ (1 << bit)) for k in range(lax.axis_size(axis))]


def swap(value, axis, bit):
    return lax.ppermute(value, axis, partner(axis, bit))


def all_sum(value, axis):
    for bit in range(lax.axis_size(axis).bit_length() - 1):
        value = value + swap(value, axis, bit)
    return value


def pa_order(turn):
    rest = lax.axis_size("pa").bit_length() - 2
    return [1 + (k + turn) % rest for k in range(rest)]


def both_cores(acts, turn):
    size = lax.axis_size("pa")
    me = lax.axis_index("pa")
    blocks = jnp.transpose(acts).reshape(size, acts.shape[1] // size, acts.shape[0])
    order = pa_order(turn)
    offsets = [
        sum(((k >> (len(order) - 1 - p)) & 1) << bit for p, bit in enumerate(order)) for k in range(size // 2)
    ]
    mine = jnp.concatenate([lax.dynamic_slice_in_dim(blocks, me ^ d, 1) for d in offsets])
    theirs = jnp.concatenate([lax.dynamic_slice_in_dim(blocks, me ^ d ^ 1, 1) for d in offsets])
    return mine, swap(theirs, "pa", 0)


def weight_part(acts, grads, first, last):
    total = None
    for act, grad in zip(acts, grads):
        act = act[first:last]
        term = product(act.reshape(-1, act.shape[2]), grad)
        total = term if total is None else total + term
    height = acts[0].shape[1]
    return total.astype(LOWER).reshape(last - first, height, -1)


def add_up(parts):
    total = parts[0].astype(WIDER)
    for part in parts[1:]:
        total = total + part.astype(WIDER)
    return total.astype(LOWER)


def share_over_pa(acts, grads, turn):
    size = acts[0].shape[0]
    keep = [weight_part(acts, grads, 0, size // 2)]
    send = weight_part(acts, grads, size // 2, size)
    for bit in pa_order(turn):
        keep.append(swap(send, "pa", bit))
        size //= 2
        if size > 1:
            send = add_up([part[size // 2 : size] for part in keep])
            keep = [part[: size // 2] for part in keep]
    return add_up([part[0] for part in keep])


def inward(share):
    return lax.ppermute(share, "pb", [(0, 1), (3, 2)])


def between(share):
    return lax.ppermute(share, "pb", [(1, 2), (2, 1)])


def outward(share):
    me = lax.axis_index("pb")
    got = lax.ppermute(share, "pb", [(1, 0), (2, 3)])
    return jnp.where((me == 1) | (me == 2), share, got).astype(WIDER)


def other_quarters(parts):
    return [lax.ppermute(part, "pb", [(k, k ^ (s + 1)) for k in range(4)]) for s, part in enumerate(parts)]


def total_plain(share):
    return lax.psum(share, "pb").astype(WIDER)


def local(
    passages,
    lengths,
    answers,
    cotangent,
    enc_gain1,
    enc_qkv,
    enc_bias,
    enc_out,
    enc_gain2,
    enc_ffn_in,
    enc_ffn_out,
    enc_gain3,
    cross_kv,
    dec_gain1,
    dec_qkv,
    dec_bias,
    dec_out,
    dec_gain2,
    cross_query,
    cross_out,
    dec_gain3,
    dec_ffn_in,
    dec_ffn_out,
):
    pa_size = lax.axis_size("pa")
    pb_size = lax.axis_size("pb")
    fast = pa_size == 8 and pb_size == 4
    me = lax.axis_index("pa").astype(jnp.int32).reshape(1)
    x = passages.reshape(SLOT, D)
    count = lengths.reshape(1)
    table = jnp.transpose(enc_bias)
    dec_table = jnp.transpose(dec_bias)
    pick = jnp.asarray(PICK, LOWER)
    pick_back = jnp.asarray(PICK_BACK, LOWER)

    def across(value):
        return value, swap(value, "pa", 0)

    first, heads, mixed, stats, packed, dec_after, lefts, dec_heads, query, after, second, slope, hidden, final, third, pairs, token = forward(
        count, table, pick, x, enc_gain1, enc_qkv, enc_gain2, enc_gain3, enc_out, enc_ffn_in, enc_ffn_out, cross_kv,
        (dec_table, answers[0], dec_gain1, dec_gain2, dec_qkv, dec_out, cross_query),
    )
    if fast:
        acts = [across(value) for value in (first, mixed, second, hidden, third)]
    else:
        acts = [both_cores(v, k % 2) for k, v in enumerate((first, mixed, second, hidden, third))]
    gathered = lax.all_gather(packed, "pa")
    answer, early, g_middle, g_gain3, partial, g_enc_gain3, g_pairs, g_final, branch, token = dec_mid(
        count, gathered, dec_after, cotangent[0], dec_gain3, lefts, query, enc_gain3, pairs,
        cross_out, dec_ffn_in, dec_ffn_out, cross_kv, final,
        after=[got for unused, got in acts[:4]],
    )
    early_all = lax.all_gather(early, "pb")
    g_inner, g_after, low, g_mixed, g_enc_gain2, token = ffn_back(
        branch, enc_ffn_out, slope, enc_ffn_in, after, enc_gain2, g_final, enc_out, after=[token]
    )

    def back_of(base, pairs, after):
        return attention_back(count, table, pick, heads, g_mixed, mixed, stats, base, pairs, after=after)

    def dec_end(part, got, token, wait=()):
        return dec_back(
            dec_table, answers[0], part, got, dec_after, g_middle, dec_heads,
            dec_gain1, dec_gain2, g_gain3, cross_query, dec_out, dec_qkv, after=[token, *wait],
        )

    def rows_end(grads, diagonal, token, wait=()):
        return attention_end(
            count, table, pick, heads, g_mixed, mixed, stats, grads, diagonal, enc_qkv, x, enc_gain1,
            g_after, g_enc_gain2, g_enc_gain3, pick_back, after=[token, *wait],
        )

    pb_me = lax.axis_index("pb").astype(jnp.int32).reshape(1)

    def outer_end(token, late_one, late_two):
        *outer, token = dec_outer(pb_me, early_all, late_one, late_two, pb_size, after=[token])
        return outer, token

    if fast:
        partial, token = add_rows(partial, swap(partial, "pa", 0), after=[token])
        got = swap(partial, "pa", 1)
        xk, xs, yk, ys, token = weights_one(me, acts[4], across(g_pairs), acts[3], across(branch), after=[token])
        one = ((xk, swap(xs, "pa", 1)), (yk, swap(ys, "pa", 2)))
        partial, token = add_rows(partial, got, after=[token])
        got = swap(partial, "pa", 2)
        grads, diagonal_a, token = back_of(0, FIRST, [token])
        late, g_start, token = dec_end(partial, got, token)
        late_near = swap(late, "pb", 0)
        send_x, send_y, token = add_first(one, flops=COST[5], after=[token, early_all])
        last = (swap(send_x, "pa", 2), swap(send_y, "pa", 1))
        late, token = stack_late(late, late_near, after=[token])
        late_far = swap(late, "pb", 1)
        xk, xs, yk, ys, token = weights_two(me, acts[2], across(g_inner), acts[1], across(low), after=[token])
        two = ((xk, swap(xs, "pa", 1)), (yk, swap(ys, "pa", 2)))
        share_one, token = add_second([one[0] + last[:1], one[1] + last[1:]], after=[token])
        got_one = inward(share_one)
        g_rows, small, diagonal_a, grads, token = rows_end(grads, diagonal_a, token, [late_far])
        there, got_small = swap(grads, "pa", 0), swap(small, "pa", 0)
        send_x, send_y, token = add_first(two, flops=COST[0], after=[token])
        last = (swap(send_x, "pa", 2), swap(send_y, "pa", 1))
        share_one, token = add_pair(share_one, got_one, flops=COST[1], after=[token])
        got_one = between(share_one)
        xk, xs, yk, ys, token = weights_three(me, acts[0], (grads, there), (small, got_small), after=[token])
        three = ((xk, swap(xs, "pa", 1)), (yk, swap(ys, "pa", 2)))
        share_two, token = add_second([two[0] + last[:1], two[1] + last[1:]], after=[token])
        got_two = inward(share_two)
        share_one, token = add_pair(share_one, got_one, flops=COST[2], after=[token])
        total_one = outward(share_one)
        send_x, send_y, token = add_first(three, after=[token])
        last = (swap(send_x, "pa", 2), swap(send_y, "pa", 1))
        share_two, token = add_pair(share_two, got_two, flops=COST[3], after=[token])
        got_two = between(share_two)
        *quarters, token = add_last(pb_me, [three[0] + last[:1], three[1] + last[1:]], after=[token])
        parts = other_quarters(quarters[1:])
        outer, token = outer_end(token, late, late_far)
        share_two, token = add_pair(share_two, got_two, after=[token])
        got_two = lax.ppermute(share_two, "pb", [(1, 0), (2, 3)])
        mine, token = add_parts(quarters[:1] + parts, after=[token, total_one])
        parts = other_quarters([mine] * 3)
        total_ffn_in, total_out, token = join_two(pb_me, share_two, got_two, after=[token])
        total_qkv, small, token = join_parts(pb_me, [mine] + parts, D // pa_size, after=[token])
        block = D // pa_size
        total_kv = jnp.concatenate([total_one[:block], total_one[block : 2 * block]], axis=1)
        total_ffn_out = total_one[2 * block :]
    else:
        partial = all_sum(partial, "pa")
        late, g_start, token = dec_end(partial, jnp.zeros_like(partial), token)
        late, token = stack_late(late, swap(late, "pb", 0), after=[token])
        late_far = swap(late, "pb", 1)
        grads, diagonal_a, token = back_of(0, FIRST, [token])
        g_rows, small, diagonal_a, grads, token = rows_end(grads, diagonal_a, token)
        outer, token = outer_end(token, late, late_far)
        small = all_sum(all_sum(small[:, :D], "pa"), "pb")
        g_heads = jnp.concatenate([grads[0], grads[1], grads[2]], axis=1)
        total_kv = total_plain(share_over_pa(acts[4], across(g_pairs), 0))
        total_ffn_out = total_plain(share_over_pa(acts[3], across(branch), 1))
        total_ffn_in = total_plain(share_over_pa(acts[2], across(g_inner), 0))
        total_out = total_plain(share_over_pa(acts[1], across(low), 1))
        total_qkv = total_plain(share_over_pa(acts[0], across(g_heads), 0))

    d_qkv, d_out, d_query, d_cross, d_in, d_ffn, dec_small = outer
    dec_small = dec_small[0]
    dec_bias_rows = dec_small[3 * D :].reshape(H, STAT)[:, GROUP - ANS : GROUP]
    dec_bias_all = jnp.pad(jnp.transpose(dec_bias_rows[:, ::-1]), ((0, BUCKETS - ANS), (0, 0)))

    def own_part(vector, axis):
        height = vector.shape[0] // lax.axis_size(axis)
        return lax.dynamic_slice_in_dim(vector, lax.axis_index(axis) * height, height, axis=0)

    return (
        answer[None],
        g_rows.reshape(1, 1, SLOT, D),
        g_start[None],
        own_part(small[0], "pa"),
        total_qkv,
        jnp.transpose(small[4:16, :BUCKETS]),
        total_out,
        own_part(small[1], "pa"),
        total_ffn_in,
        total_ffn_out,
        own_part(small[2], "pa"),
        total_kv,
        own_part(dec_small[:D], "pb"),
        d_qkv,
        own_part(dec_bias_all, "pb"),
        d_out,
        own_part(dec_small[D : 2 * D], "pb"),
        d_query,
        d_cross,
        own_part(dec_small[2 * D : 3 * D], "pb"),
        d_in,
        d_ffn,
    )


def solution(mesh):
    copied = P()
    in_specs = (
        P("pb", "pa", None, None),
        P("pb", "pa"),
        P("pb", None, None),
        P("pb", None, None),
    ) + (copied,) * 19
    by_pa, by_pa_rows = P("pa"), P("pa", None)
    by_pb, by_pb_rows = P("pb"), P("pb", None)
    out_specs = (
        P("pb", None, None),
        P("pb", "pa", None, None),
        P("pb", None, None),
        by_pa,
        by_pa_rows,
        copied,
        by_pa_rows,
        by_pa,
        by_pa_rows,
        by_pa_rows,
        by_pa,
        by_pa_rows,
        by_pb,
        by_pb_rows,
        by_pb_rows,
        by_pb_rows,
        by_pb,
        by_pb_rows,
        by_pb_rows,
        by_pb,
        by_pb_rows,
        by_pb_rows,
    )
    return jax.shard_map(local, mesh=mesh, in_specs=in_specs, out_specs=out_specs, check_vma=False)
```
